32 devices in a mesh: section: 2 (over core), row: 16 (over z, y, x).
Axes of the slice: x: 2, y: 2, z: 4, core: 2. Of those that a mesh axis runs over, the one named last changes fastest.
Arguments:
- tokens: bfloat16 [2, 8192, 384], P(None, 'row'), may hold values from -3 to 3
- conditions: bfloat16 [2, 32, 384], P(None, 'row'), may hold values from -2.5 to 2.5
- output_grad: bfloat16 [2, 8192, 384], P(None, 'row'), may hold values from -3 to 3
- layouts: int32 [2, 16], P(None, 'row'), may hold values from 0 to 2
- w_ada: bfloat16 [2, 384, 2304], P('section', 'row'), may hold values from -0.3125 to 0.3125
- b_ada: float32 [2, 2304], P('section'), may hold values from -0.5 to 0.5
- w_query: bfloat16 [2, 384, 384], P('section', 'row'), may hold values from -0.3125 to 0.3125
- w_key: bfloat16 [2, 384, 384], P('section', 'row'), may hold values from -0.3125 to 0.3125
- w_value: bfloat16 [2, 384, 384], P('section', 'row'), may hold values from -0.3125 to 0.3125
- w_gate: bfloat16 [2, 384, 384], P('section', 'row'), may hold values from -0.3125 to 0.3125
- w_out: bfloat16 [2, 384, 384], P('section', 'row'), may hold values from -0.4375 to 0.4375
- w_decay: bfloat16 [2, 384, 6], P('section', 'row'), may hold values from -0.3125 to 0.3125
- b_decay: float32 [2, 6], P('section'), may hold values from -3 to 6
- conv_kernel: float32 [2, 3, 384], P('section'), may hold values from -3 to 3
- w_up: bfloat16 [2, 384, 1536], P('section', 'row'), may hold values from -0.3125 to 0.3125
- b_up: float32 [2, 1536], P('section'), may hold values from -2 to 2
- w_down: bfloat16 [2, 1536, 384], P('section', 'row'), may hold values from -0.15625 to 0.15625
- b_down: float32 [2, 384], P('section'), may hold values from -2 to 2
Outputs:
- activations: bfloat16 [2, 2, 8192, 384], P('section', None, 'row')
- input_grads: float32 [2, 2, 8192, 384], P('section', None, 'row')
- cond_grads: float32 [2, 32, 384], P(None, 'row')
- grad_w_ada: float32 [2, 384, 2304], P('section', 'row')
- grad_b_ada: float32 [2, 2304], P('section')
- grad_w_query: float32 [2, 384, 384], P('section', 'row')
- grad_w_key: float32 [2, 384, 384], P('section', 'row')
- grad_w_value: float32 [2, 384, 384], P('section', 'row')
- grad_w_gate: float32 [2, 384, 384], P('section', 'row')
- grad_w_out: float32 [2, 384, 384], P('section', 'row')
- grad_w_decay: float32 [2, 384, 6], P('section', 'row')
- grad_b_decay: float32 [2, 6], P('section')
- grad_conv_kernel: float32 [2, 3, 384], P('section')
- grad_w_up: float32 [2, 384, 1536], P('section', 'row')
- grad_b_up: float32 [2, 1536], P('section')
- grad_w_down: float32 [2, 1536, 384], P('section', 'row')
- grad_b_down: float32 [2, 384], P('section')
The draws below stay inside these ranges and needn't reach their ends.
Inputs may be any that keep to these rules, and one draw needn't show every extreme that they name: `layouts`: 0: the block of 512 rows holds one item of 16 x 32 patches; k: k items of 16 x 16 patches followed by empty rows.
All inputs are finite; a program needn't handle non-finite values.
Results may differ from the reference program's by a relative error of at most 0.018.
The reference program's roundings to bfloat16 on the way count: a program that leaves them out, or rounds other values in their place, can miss the bound.
Values may be sent and summed in bfloat16 or wider, within the bound.
No kernel may reach another device: no remote copies, remote signals or barrier semaphores. Data moves between devices by JAX's collectives and lax.ppermute only.
A program may use at most 256 MiB of HBM per device.

```python
import jax
import jax.numpy as jnp
from jax import lax

D = 384
HEADS = 6
HEAD_DIM = 64
FF = 1536
GRID_H = 16
WIDE_W = 32
SMALL_W = 16
MICRO = 2
ROWS = 512
SMALL_ROWS = 256
SLOTS = 2
BLOCK = 64
TOKENS = 8192
ITEMS = 32
N_ROW = 16


def place_ends(result, stream_key, low, top_value):
    longest = result.shape.index(max(result.shape))
    spots = []
    for shift in (0, 1):
        where = [jax.random.randint(jax.random.fold_in(stream_key, axis), (), 0, length) for axis, length in enumerate(result.shape)]
        where[longest] = (where[longest] + shift) % result.shape[longest]
        spots.append(tuple(where))
    return result.at[spots[0]].set(low).at[spots[1]].set(top_value)


def level_of(rng, extent, cuts, least, largest):
    loudness = 1.0
    for axis_at, blocks in cuts:
        steps = jax.random.uniform(jax.random.fold_in(jax.random.fold_in(rng, 6), axis_at), (blocks,), jnp.float32, least / len(cuts), largest / len(cuts))
        loudness = loudness * jnp.repeat(jnp.exp(steps), extent[axis_at] // blocks).reshape((-1,) + (1,) * (len(extent) - 1 - axis_at))
    return loudness


def scatter_about(stream_key, dims, deviation, limit, shards=(), kind=jnp.bfloat16):
    drawn = deviation * jax.random.normal(stream_key, dims, jnp.float32)
    if shards:
        drawn = drawn * level_of(stream_key, dims, shards, -0.22, 0.18)
    return jnp.clip(drawn, -limit, limit).astype(kind)


def setup_inputs(seed: int = 0) -> dict:
    keys = jax.random.split(jax.random.key(seed), 19)
    tokens = scatter_about(keys[0], (MICRO, TOKENS, D), 1.0, 3.0, ((1, 16),))
    conditions = scatter_about(keys[1], (MICRO, ITEMS, D), 0.6, 2.5, ((1, 16),))
    output_grad = scatter_about(keys[2], (MICRO, TOKENS, D), 1.0, 3.0, ((1, 16),))
    layouts = place_ends(jax.random.randint(keys[3], (MICRO, N_ROW), 0, SLOTS + 1), jax.random.fold_in(keys[3], 1), 0, SLOTS).astype(jnp.int32)
    w_ada = scatter_about(keys[4], (2, D, 6 * D), D ** -0.5, 0.3125, ((0, 2), (1, 16)))
    b_ada = jnp.clip(jax.random.uniform(keys[5], (2, 6 * D), jnp.float32, -0.5, 0.5) * level_of(keys[5], (2, 6 * D), ((0, 2),), -0.4, 0.0), -0.5, 0.5)
    w_query = scatter_about(keys[6], (2, D, D), D ** -0.5, 0.3125, ((0, 2), (1, 16)))
    w_key = scatter_about(keys[7], (2, D, D), D ** -0.5, 0.3125, ((0, 2), (1, 16)))
    w_value = scatter_about(keys[8], (2, D, D), D ** -0.5, 0.3125, ((0, 2), (1, 16)))
    w_gate = scatter_about(keys[9], (2, D, D), D ** -0.5, 0.3125, ((0, 2), (1, 16)))
    w_out = scatter_about(keys[10], (2, D, D), (D // 2) ** -0.5, 0.4375, ((0, 2), (1, 16)))
    w_decay = scatter_about(keys[11], (2, D, HEADS), D ** -0.5, 0.3125, ((0, 2), (1, 16)))
    b_decay = jnp.clip(-3.0 + 9.0 * jax.random.uniform(keys[12], (2, HEADS), jnp.float32) ** level_of(keys[12], (2, HEADS), ((0, 2),), -0.2, 0.2), -3.0, 6.0)
    conv_kernel = scatter_about(keys[13], (2, 3, D), 0.6, 3.0, ((0, 2),), jnp.float32)
    w_up = scatter_about(keys[14], (2, D, FF), D ** -0.5, 0.3125, ((0, 2), (1, 16)))
    b_up = scatter_about(keys[15], (2, FF), 0.3, 2.0, ((0, 2),), jnp.float32)
    w_down = scatter_about(keys[16], (2, FF, D), FF ** -0.5, 0.15625, ((0, 2), (1, 16)))
    b_down = scatter_about(keys[17], (2, D), 0.3, 2.0, ((0, 2),), jnp.float32)
    return dict(tokens=tokens, conditions=conditions, output_grad=output_grad, layouts=layouts, w_ada=w_ada, b_ada=b_ada, w_query=w_query, w_key=w_key, w_value=w_value, w_gate=w_gate, w_out=w_out, w_decay=w_decay, b_decay=b_decay, conv_kernel=conv_kernel, w_up=w_up, b_up=b_up, w_down=w_down, b_down=b_down)


HIGH = lax.Precision.HIGHEST

@jax.custom_vjp
def low(v):
    return lax.optimization_barrier(v.astype(jnp.bfloat16)).astype(jnp.float32)

@jax.custom_vjp
def low_back(v):
    return v

def low_keep(v):
    return (low(v), None)

def low_pass(kept, grad):
    return (grad,)

def back_keep(v):
    return (v, None)

def back_low(kept, grad):
    return (low(grad),)
low.defvjp(low_keep, low_pass)
low_back.defvjp(back_keep, back_low)

def matmul(left, right):
    return jnp.dot(left, right, precision=HIGH, preferred_element_type=jnp.float32)

def layer_norm(values):
    average = lax.optimization_barrier(jnp.mean(values, axis=-1, keepdims=True))
    centred = values - average
    return centred * lax.rsqrt(lax.optimization_barrier(jnp.mean(centred * centred, axis=-1, keepdims=True)) + 1e-06)

def scan_order(values, is_wide, flipped):
    columns = values.shape[-1]
    wide_form = values.reshape(GRID_H, WIDE_W, columns).swapaxes(0, 1).reshape(ROWS, columns)
    small_form = values.reshape(SLOTS, GRID_H, SMALL_W, columns).swapaxes(1, 2).reshape(ROWS, columns)
    return jnp.where(flipped, jnp.where(is_wide, wide_form, small_form), values)

def raster_order(values, is_wide, flipped):
    columns = values.shape[-1]
    wide_form = values.reshape(WIDE_W, GRID_H, columns).swapaxes(0, 1).reshape(ROWS, columns)
    small_form = values.reshape(SLOTS, SMALL_W, GRID_H, columns).swapaxes(1, 2).reshape(ROWS, columns)
    return jnp.where(flipped, jnp.where(is_wide, wide_form, small_form), values)

def slot_info(layout):
    is_wide = layout == 0
    row_index = jnp.arange(ROWS, dtype=jnp.int32)
    live_rows = jnp.where(is_wide, 1.0, (row_index < layout * SMALL_ROWS).astype(jnp.float32))[:, None]
    slot_index = jnp.where(is_wide, 0, row_index // SMALL_ROWS)
    onehot = (slot_index[:, None] == jnp.arange(SLOTS, dtype=jnp.int32)[None, :]).astype(jnp.float32)
    position = jnp.where(is_wide, row_index, row_index % SMALL_ROWS)
    return (is_wide, live_rows, onehot, position)

def pieces_of(modulation, onehot):
    per_row = jnp.dot(onehot, modulation, precision=HIGH, preferred_element_type=jnp.float32)
    return [per_row[:, number * D:(number + 1) * D] for number in range(6)]

def first_half(stream, modulation, onehot):
    shares = pieces_of(modulation, onehot)
    return layer_norm(stream) * (1.0 + shares[1]) + shares[0]

def second_half(stream, modulation, branch, onehot):
    shares = pieces_of(modulation, onehot)
    middle = stream + shares[2] * branch
    return (middle, layer_norm(middle) * (1.0 + shares[4]) + shares[3])

def activate(up_raw, bias_up):
    return jax.nn.gelu(up_raw + bias_up, approximate=True)

def finish(middle, modulation, down_raw, bias_down, onehot, live_rows):
    shares = pieces_of(modulation, onehot)
    return (middle + shares[5] * (down_raw + bias_down)) * live_rows

def mixer(query_proj, key_proj, value_proj, gate_proj, decay_proj, kernel, decay_bias, position):
    step_one = (position >= 1).astype(jnp.float32)[:, None]
    step_two = (position >= 2).astype(jnp.float32)[:, None]
    width = value_proj.shape[1]
    shifted_one = jnp.concatenate([jnp.zeros((1, width), jnp.float32), value_proj[:-1]], 0) * step_one
    shifted_two = jnp.concatenate([jnp.zeros((2, width), jnp.float32), value_proj[:-2]], 0) * step_two
    convolved = kernel[0] * value_proj + kernel[1] * shifted_one + kernel[2] * shifted_two
    log_decay = jax.nn.log_sigmoid(decay_proj + decay_bias) / 16.0
    block_count = ROWS // BLOCK
    queries = (query_proj * HEAD_DIM ** (-0.5)).reshape(block_count, BLOCK, HEADS, HEAD_DIM)
    keys_all = key_proj.reshape(block_count, BLOCK, HEADS, HEAD_DIM)
    values_all = convolved.reshape(block_count, BLOCK, HEADS, HEAD_DIM)
    cumulative = jnp.cumsum(log_decay.reshape(block_count, BLOCK, HEADS), axis=1)
    causal = jnp.arange(BLOCK)[:, None] >= jnp.arange(BLOCK)[None, :]
    spread = cumulative[:, :, None, :] - cumulative[:, None, :, :]
    factors = jnp.exp(jnp.where(causal[None, :, :, None], spread, -1e+30))
    scores = jnp.einsum('cthd,cshd->ctsh', queries, keys_all, precision=HIGH) * factors
    within = jnp.einsum('ctsh,cshd->cthd', scores, values_all, precision=HIGH)
    final_sum = cumulative[:, -1:, :]
    tails = keys_all * jnp.exp(final_sum - cumulative)[..., None]
    block_states = jnp.einsum('cshd,cshe->chde', tails, values_all, precision=HIGH)
    heads_in = queries * jnp.exp(cumulative)[..., None]
    fading = jnp.exp(final_sum[:, 0, :])
    starts = position.reshape(block_count, BLOCK)[:, 0] == 0

    def advance(carried, inputs):
        query_block, state_block, fade_block, start_block = inputs
        carried = jnp.where(start_block, jnp.zeros_like(carried), carried)
        emitted = jnp.einsum('thd,hde->the', query_block, carried, precision=HIGH)
        return (fade_block[:, None, None] * carried + state_block, emitted)
    initial = jnp.zeros((HEADS, HEAD_DIM, HEAD_DIM), jnp.float32)
    _, across = lax.scan(jax.checkpoint(advance), initial, (heads_in, block_states, fading, starts))
    summed = (within + across).reshape(ROWS, HEADS, HEAD_DIM)
    normed = summed * lax.rsqrt(lax.optimization_barrier(jnp.mean(summed * summed, axis=-1, keepdims=True)) + 1.0)
    return normed.reshape(ROWS, HEADS * HEAD_DIM) * jax.nn.silu(gate_proj)

def block_slot(params, stream, conds, layout, flipped):
    is_wide, live_rows, onehot, position = slot_info(layout)
    lifted = low(jax.nn.silu(conds))
    modulation = low_back(matmul(lifted, params[0])) + params[1]
    inner_one = low(first_half(stream, modulation, onehot))
    ordered = scan_order(inner_one, is_wide, flipped)
    query_proj = low_back(matmul(ordered, params[2]))
    key_proj = low_back(matmul(ordered, params[3]))
    value_proj = low_back(matmul(ordered, params[4]))
    gate_proj = low_back(matmul(ordered, params[5]))
    decay_proj = low_back(matmul(ordered, params[7]))
    mixed = mixer(query_proj, key_proj, value_proj, gate_proj, decay_proj, params[9], params[8], position)
    gated_out = low(raster_order(mixed, is_wide, flipped))
    branch = low_back(matmul(gated_out, params[6]))
    middle, inner_two = second_half(stream, modulation, branch, onehot)
    up_raw = low_back(matmul(low(inner_two), params[10]))
    hidden = low(activate(up_raw, params[11]))
    down_raw = low_back(matmul(hidden, params[12]))
    return finish(middle, modulation, down_raw, params[13], onehot, live_rows)

def forward(tokens_in, conds_in, boundary_probe, params_one, params_two, layout_flat):

    def run_layer(params, flipped, stream_all):

        def single(operands):
            return block_slot(params, operands[0], operands[1], operands[2], flipped)
        return lax.map(jax.checkpoint(single), (stream_all, conds_in, layout_flat))
    first_out = run_layer(params_one, False, tokens_in)
    boundary = low_back(low(first_out)) + boundary_probe
    second_out = run_layer(params_two, True, boundary)
    return (low(first_out), low(second_out))

def reference(tokens, conditions, output_grad, layouts, w_ada, b_ada, w_query, w_key, w_value, w_gate, w_out, w_decay, b_decay, conv_kernel, w_up, b_up, w_down, b_down):
    slot_count = MICRO * N_ROW
    stacked = (w_ada, b_ada, w_query, w_key, w_value, w_gate, w_out, w_decay, b_decay, conv_kernel, w_up, b_up, w_down, b_down)
    params_one = tuple((stacked_param[0].astype(jnp.float32) for stacked_param in stacked))
    params_two = tuple((stacked_param[1].astype(jnp.float32) for stacked_param in stacked))
    tokens_in = tokens.astype(jnp.float32).reshape(slot_count, ROWS, D)
    conds_in = conditions.astype(jnp.float32).reshape(slot_count, SLOTS, D)
    layout_flat = layouts.reshape(slot_count).astype(jnp.int32)
    boundary_probe = jnp.zeros((slot_count, ROWS, D), jnp.float32)

    def whole(tok_in, cond_in, probe_in, first_params, second_params):
        return forward(tok_in, cond_in, probe_in, first_params, second_params, layout_flat)
    primal, pullback = jax.vjp(whole, tokens_in, conds_in, boundary_probe, params_one, params_two)
    cotangent = output_grad.astype(jnp.float32).reshape(slot_count, ROWS, D)
    grad_tokens, grad_conds, grad_probe, grads_one, grads_two = pullback((jnp.zeros_like(cotangent), cotangent))
    activations = jnp.stack([primal[0], primal[1]]).reshape(2, MICRO, N_ROW * ROWS, D).astype(jnp.bfloat16)
    input_grads = jnp.stack([grad_tokens, grad_probe]).reshape(2, MICRO, N_ROW * ROWS, D)
    cond_grads = grad_conds.reshape(MICRO, N_ROW * SLOTS, D)
    weight_grads = [jnp.stack([first_grad, second_grad]) for first_grad, second_grad in zip(grads_one, grads_two)]
    return (activations, input_grads, cond_grads, weight_grads[0], weight_grads[1], weight_grads[2], weight_grads[3], weight_grads[4], weight_grads[5], weight_grads[6], weight_grads[7], weight_grads[8], weight_grads[9], weight_grads[10], weight_grads[11], weight_grads[12], weight_grads[13])
```

```python
import functools

import jax
import jax.numpy as jnp
from jax import lax
from jax.experimental import pallas as pl
from jax.experimental.pallas import tpu as pltpu
from jax.sharding import PartitionSpec as P

D = 384
HEADS = 6
HEAD_DIM = 64
FF = 1536
MICRO = 2
ROWS = 512
HALF = 256
SLOTS = 2
PAIR = 128
PAIRS = D // PAIR
QKVG = 4 * D
LANES = 128
NEG = -1e30
SCALE = HEAD_DIM**-0.5

bf16 = jnp.bfloat16
f32 = jnp.float32


def mm(left, right):
    return jnp.dot(left, right, preferred_element_type=f32)


def mm_t(left, right):
    return lax.dot_general(left, right, (((1,), (1,)), ((), ())), preferred_element_type=f32)


def split(values):
    high = values.astype(bf16)
    return high, (values - high.astype(f32)).astype(bf16)


def split_three(values):
    high, rest = split(values)
    mid = values - high.astype(f32)
    middle, low = split(mid)
    return high, middle, low


def cat_left(values):
    high, low = split(values)
    return jnp.concatenate([high, low, high], axis=1)


def cat_right(values):
    high, low = split(values)
    return jnp.concatenate([high, high, low], axis=1)


def mm_near(left, right_pair, right_high):
    high, low = split(left)
    wide = mm(high, right_pair)
    return wide[:, :PAIR] + wide[:, PAIR:] + mm(low, right_high)


def lane_iota(rows, columns):
    return lax.broadcasted_iota(jnp.int32, (rows, columns), 1)


def row_iota(rows, columns):
    return lax.broadcasted_iota(jnp.int32, (rows, columns), 0)


def order_matrix(start, rows, wide, to_scan):
    t = row_iota(rows, ROWS) + start
    small = (t & 256) + ((t & 15) << 4) + ((t & 255) >> 4)
    if to_scan:
        large = ((t & 15) << 5) + (t >> 4)
    else:
        large = ((t & 31) << 4) + (t >> 5)
    source = jnp.where(wide, large, small)
    return jnp.where(lane_iota(rows, ROWS) == source, 1.0, 0.0).astype(bf16)


def normalise(values):
    centred = values - jnp.mean(values, axis=-1, keepdims=True)
    rate = lax.rsqrt(jnp.mean(centred * centred, axis=-1, keepdims=True) + 1e-06)
    return centred * rate, rate


def normalise_back(normal, rate, grad):
    return rate * (
        grad
        - jnp.mean(grad, axis=-1, keepdims=True)
        - normal * jnp.mean(grad * normal, axis=-1, keepdims=True)
    )


def share(mod_ref, slot, part):
    return mod_ref[pl.ds(slot, 1), part * D : (part + 1) * D]


def sigmoid(values):
    return 1.0 / (1.0 + jnp.exp(-values))


GELU_A = 0.7978845608028654
GELU_B = 0.044715


def gelu_parts(values):
    square = values * values
    tanh = jnp.tanh(GELU_A * values * (1.0 + GELU_B * square))
    return square, tanh


def fill_bias(bias, wide):
    bias[:, :HALF] = jnp.full((HALF, HALF), 0.0, f32) + jnp.where(wide, 0.0, NEG)
    causal = row_iota(HALF, HALF) >= lane_iota(HALF, HALF)
    bias[:, HALF:] = jnp.where(causal, 0.0, NEG)


def decay_factors(cum, cumt, bias, head):
    row = cumt[pl.ds(head, 1), :]
    lanes = lane_iota(1, LANES)
    column = jnp.sum(jnp.where(lanes == head, cum[...], 0.0), axis=1, keepdims=True)
    first = jnp.exp(column[:HALF] - row[:, :HALF] + bias[:, HALF:])
    second = jnp.exp(column[HALF:] - row + bias[...])
    return first, second


def head_norm(values, lanes):
    square = values * values
    low = jnp.sum(jnp.where(lanes < HEAD_DIM, square, 0.0), axis=1, keepdims=True)
    high = jnp.sum(jnp.where(lanes < HEAD_DIM, 0.0, square), axis=1, keepdims=True)
    return jnp.where(lanes < HEAD_DIM, low, high) * (1.0 / HEAD_DIM)


def fill_decay(dp, bd, cum, cumt):
    raw = dp[...] + bd[...]
    log_decay = (jnp.minimum(raw, 0.0) - jnp.log1p(jnp.exp(-jnp.abs(raw)))) * (1.0 / 16.0)
    high, middle, low = split_three(log_decay)
    causal = jnp.where(row_iota(ROWS, ROWS) >= lane_iota(ROWS, ROWS), 1.0, 0.0).astype(bf16)
    cum[...] = mm(causal, high) + mm(causal, middle) + mm(causal, low)
    cumt[...] = jnp.transpose(cum[...])


def columns(index, first=0):
    return pl.ds(pl.multiple_of(index * PAIR + first, PAIR), PAIR)


def attn_forward_kernel(
    flip, sc, x, mod, w, wd, bd, ck, ordered, qkvg, dp, vc, cum, cumt, o, gated, inner, vpad, bias
):
    wide = sc[1] == 0

    def first(i, carry):
        rows = pl.ds(pl.multiple_of(i * HALF, HALF), HALF)
        slot = jnp.where(wide, 0, i)
        normal, _ = normalise(x[rows, :].astype(f32))
        inner[rows, :] = (normal * (1.0 + share(mod, slot, 1)) + share(mod, slot, 0)).astype(bf16)
        return carry

    lax.fori_loop(0, 2, first, 0)

    def project(i, carry):
        start = pl.multiple_of(i * HALF, HALF)
        rows = pl.ds(start, HALF)
        if flip:
            part = mm(order_matrix(start, HALF, wide, True), inner[...]).astype(bf16)
        else:
            part = inner[rows, :]
        ordered[rows, :] = part
        qkvg[rows, :] = mm(part, w[...])
        dp[rows, :] = mm(part, wd[...])
        return carry

    lax.fori_loop(0, 2, project, 0)
    fill_decay(dp, bd, cum, cumt)
    fill_bias(bias, wide)

    vpad[0:8, :] = jnp.zeros((8, D), f32)
    vpad[8 : 8 + ROWS, :] = qkvg[:, 2 * D : 3 * D]
    position = row_iota(ROWS, 1) & jnp.where(wide, ROWS - 1, HALF - 1)
    one = jnp.where(position >= 1, vpad[7 : 7 + ROWS, :], 0.0)
    two = jnp.where(position >= 2, vpad[6 : 6 + ROWS, :], 0.0)
    vc[...] = ck[0:1, :] * vpad[8 : 8 + ROWS, :] + ck[1:2, :] * one + ck[2:3, :] * two

    def pair(p, carry):
        lanes = lane_iota(1, PAIR)
        queries = cat_left(qkvg[:, columns(p)] * SCALE)
        keys = qkvg[:, columns(p, D)]
        value_high, value_low = split(vc[:, columns(p)])
        values = jnp.concatenate([value_high, value_low], axis=1)
        parts = []
        for e in range(2):
            key_cat = cat_right(jnp.where((lanes // HEAD_DIM) == e, keys, 0.0))
            first, second = decay_factors(cum, cumt, bias, 2 * p + e)
            first = first * mm_t(queries[:HALF], key_cat[:HALF])
            second = second * mm_t(queries[HALF:], key_cat)
            parts.append(
                jnp.concatenate(
                    [
                        mm_near(first, values[:HALF], value_high[:HALF]),
                        mm_near(second, values, value_high),
                    ],
                    axis=0,
                )
            )
        total = jnp.where(lanes < HEAD_DIM, parts[0], parts[1])
        o[:, columns(p)] = total
        gate = qkvg[:, columns(p, 3 * D)]
        normed = total * lax.rsqrt(head_norm(total, lanes) + 1.0)
        mixed = (normed * (gate * sigmoid(gate))).astype(bf16)
        if flip:
            inner[:, columns(p)] = mixed
        else:
            gated[:, columns(p)] = mixed
        return carry

    lax.fori_loop(0, PAIRS, pair, 0)
    if flip:

        def back(i, carry):
            start = pl.multiple_of(i * HALF, HALF)
            gated[pl.ds(start, HALF), :] = mm(
                order_matrix(start, HALF, wide, False), inner[...]
            ).astype(bf16)
            return carry

        lax.fori_loop(0, 2, back, 0)


def ffn_forward_kernel(sc, x, mod, gated, wo, wu, bu, wn, bn, out, branch, down):
    wide = sc[1] == 0
    live_rows = jnp.where(wide, ROWS, sc[1] * HALF)

    def tile(i, carry):
        start = pl.multiple_of(i * HALF, HALF)
        rows = pl.ds(start, HALF)
        slot = jnp.where(wide, 0, i)
        grown = mm(gated[rows, :], wo[...])
        branch[rows, :] = grown
        middle = x[rows, :].astype(f32) + share(mod, slot, 2) * grown
        normal, _ = normalise(middle)
        inner = (normal * (1.0 + share(mod, slot, 4)) + share(mod, slot, 3)).astype(bf16)
        up = mm(inner, wu[...]) + bu[...]
        _, tanh = gelu_parts(up)
        hidden = (0.5 * up * (1.0 + tanh)).astype(bf16)
        low = mm(hidden, wn[...])
        down[rows, :] = low
        result = middle + share(mod, slot, 5) * (low + bn[...])
        live = (row_iota(HALF, 1) + start) < live_rows
        out[rows, :] = jnp.where(live, result, 0.0).astype(bf16)
        return carry

    lax.fori_loop(0, 2, tile, 0)


def ffn_backward_kernel(
    sc, x, mod, gated, wo, wu, bu, wn, bn, branch, down, grad,
    mid_grad, branch_low, gwo, gwu, gwn, gmod, gbu, gbn,
    hidden_s, inner_s, up_s, down_s,
):
    wide = sc[1] == 0
    live_rows = jnp.where(wide, ROWS, sc[1] * HALF)
    gmod[...] = jnp.zeros(gmod.shape, f32)
    gbu[...] = jnp.zeros(gbu.shape, f32)
    gbn[...] = jnp.zeros(gbn.shape, f32)

    def tile(i, carry):
        start = pl.multiple_of(i * HALF, HALF)
        rows = pl.ds(start, HALF)
        slot = jnp.where(wide, 0, i)

        def add(part, values):
            where = (pl.ds(slot, 1), slice((part - 2) * D, (part - 1) * D))
            gmod[where] = gmod[where] + jnp.sum(values, axis=0, keepdims=True)

        grown = branch[rows, :]
        middle = x[rows, :].astype(f32) + share(mod, slot, 2) * grown
        normal, rate = normalise(middle)
        inner = (normal * (1.0 + share(mod, slot, 4)) + share(mod, slot, 3)).astype(bf16)
        inner_s[rows, :] = inner
        live = (row_iota(HALF, 1) + start) < live_rows
        above = jnp.where(live, grad[rows, :].astype(f32), 0.0)
        add(5, above * (down[rows, :] + bn[...]))
        grad_down = above * share(mod, slot, 5)
        gbn[...] = gbn[...] + jnp.sum(grad_down, axis=0, keepdims=True)
        down_low = grad_down.astype(bf16)
        down_s[rows, :] = down_low
        up = mm(inner, wu[...]) + bu[...]
        square, tanh = gelu_parts(up)
        half = 0.5 * (1.0 + tanh)
        hidden_s[rows, :] = (up * half).astype(bf16)
        slope = half + 0.5 * up * (1.0 - tanh * tanh) * (
            GELU_A * (1.0 + 3.0 * GELU_B * square)
        )
        grad_up = mm_t(down_low, wn[...]) * slope
        gbu[...] = gbu[...] + jnp.sum(grad_up, axis=0, keepdims=True)
        up_low = grad_up.astype(bf16)
        up_s[rows, :] = up_low
        grad_inner = mm_t(up_low, wu[...])
        add(3, grad_inner)
        add(4, grad_inner * normal)
        grad_middle = above + normalise_back(
            normal, rate, grad_inner * (1.0 + share(mod, slot, 4))
        )
        mid_grad[rows, :] = grad_middle
        add(2, grad_middle * grown)
        branch_low[rows, :] = (grad_middle * share(mod, slot, 2)).astype(bf16)
        return carry

    lax.fori_loop(0, 2, tile, 0)

    inner_t = jnp.transpose(inner_s[...].astype(f32)).astype(bf16)
    gwo[...] = mm(jnp.transpose(gated[...].astype(f32)).astype(bf16), branch_low[...])

    def weights(j, carry):
        part = pl.ds(pl.multiple_of(j * HALF, HALF), HALF)
        hidden_t = jnp.transpose(hidden_s[:, part].astype(f32)).astype(bf16)
        gwn[part, :] = mm(hidden_t, down_s[...])
        gwu[:, part] = mm(inner_t, up_s[:, part])
        return carry

    lax.fori_loop(0, FF // HALF, weights, 0)


def attn_backward_kernel(
    flip,
    sc, x, mod, ordered, qkvg, dp, vc, cum, cumt, o, branch_low, mid_grad, w, wd, wo, bd, ck,
    gx, gw, gwd, gmod, gck, gbd,
    mixed_s, low_s, do_s, dv_s, rows_s, cols_s, bias, perm_s,
):
    wide = sc[1] == 0
    fill_bias(bias, wide)

    def first(i, carry):
        start = pl.multiple_of(i * HALF, HALF)
        rows = pl.ds(start, HALF)
        if flip:
            part = mm(order_matrix(start, HALF, wide, True), branch_low[...]).astype(bf16)
        else:
            part = branch_low[rows, :]
        mixed_s[rows, :] = mm_t(part, wo[...])
        return carry

    lax.fori_loop(0, 2, first, 0)
    rows_s[...] = jnp.zeros(rows_s.shape, f32)
    cols_s[...] = jnp.zeros(cols_s.shape, f32)

    def pair(p, carry):
        lanes = lane_iota(1, PAIR)
        total = o[:, columns(p)]
        gate = qkvg[:, columns(p, 3 * D)]
        above = mixed_s[:, columns(p)]
        rate = lax.rsqrt(head_norm(total, lanes) + 1.0)
        sig = sigmoid(gate)
        grad_gate = above * (total * rate) * (sig * (1.0 + gate * (1.0 - sig)))
        low_s[:, columns(p, 3 * D)] = grad_gate.astype(bf16)
        grad_normed = above * (gate * sig)
        product = grad_normed * total
        inside = jnp.where(
            lanes < HEAD_DIM,
            jnp.sum(jnp.where(lanes < HEAD_DIM, product, 0.0), axis=1, keepdims=True),
            jnp.sum(jnp.where(lanes < HEAD_DIM, 0.0, product), axis=1, keepdims=True),
        ) * (1.0 / HEAD_DIM)
        grad_o = rate * grad_normed - total * (rate * rate * rate) * inside

        queries = qkvg[:, columns(p)] * SCALE
        keys = qkvg[:, columns(p, D)]
        values = vc[:, columns(p)]
        query_cat = cat_left(queries)
        grad_cat = cat_left(grad_o)
        key_high, key_low = split(keys)
        key_pair = jnp.concatenate([key_high, key_low], axis=1)
        query_t = jnp.transpose(queries)
        grad_t = jnp.transpose(grad_o)
        grad_q = []
        grad_k = []
        grad_v = []
        for e in range(2):
            mine = (lanes // HEAD_DIM) == e
            head = 2 * p + e
            key_cat = cat_right(jnp.where(mine, keys, 0.0))
            value_cat = cat_right(jnp.where(mine, values, 0.0))
            first, second = decay_factors(cum, cumt, bias, head)
            raw_first = mm_t(query_cat[:HALF], key_cat[:HALF])
            raw_second = mm_t(query_cat[HALF:], key_cat)
            grad_first = first * mm_t(grad_cat[:HALF], value_cat[:HALF])
            grad_second = second * mm_t(grad_cat[HALF:], value_cat)
            score_first = raw_first * first
            score_second = raw_second * second
            pull_first = grad_first * raw_first
            pull_second = grad_second * raw_second
            here = lanes == head
            rows_s[:HALF, :] = rows_s[:HALF, :] + jnp.where(
                here, jnp.sum(pull_first, axis=1, keepdims=True), 0.0
            )
            rows_s[HALF:, :] = rows_s[HALF:, :] + jnp.where(
                here, jnp.sum(pull_second, axis=1, keepdims=True), 0.0
            )
            low_cols = jnp.sum(pull_second, axis=0, keepdims=True)
            cols_s[pl.ds(head, 1), :HALF] = low_cols[:, :HALF] + jnp.sum(
                pull_first, axis=0, keepdims=True
            )
            cols_s[pl.ds(head, 1), HALF:] = low_cols[:, HALF:]
            grad_q.append(
                jnp.concatenate(
                    [
                        mm_near(grad_first, key_pair[:HALF], key_high[:HALF]),
                        mm_near(grad_second, key_pair, key_high),
                    ],
                    axis=0,
                )
            )

            def turned(source_t, block_first, block_second):
                high, low = split(source_t[e * HEAD_DIM : (e + 1) * HEAD_DIM, :])
                both = jnp.concatenate([high, low], axis=0)
                first_high, first_low = split(block_first)
                second_high, second_low = split(block_second)
                one = mm(both[:, :HALF], first_high)
                one = one[:HEAD_DIM] + one[HEAD_DIM:] + mm(high[:, :HALF], first_low)
                two = mm(both[:, HALF:], second_high)
                two = two[:HEAD_DIM] + two[HEAD_DIM:] + mm(high[:, HALF:], second_low)
                return jnp.concatenate([two[:, :HALF] + one, two[:, HALF:]], axis=1)

            grad_k.append(turned(query_t, grad_first, grad_second))
            grad_v.append(turned(grad_t, score_first, score_second))
        query_grad = jnp.where(lanes < HEAD_DIM, grad_q[0], grad_q[1]) * SCALE
        low_s[:, columns(p)] = query_grad.astype(bf16)
        low_s[:, columns(p, D)] = jnp.transpose(jnp.concatenate(grad_k, axis=0)).astype(bf16)
        dv_s[:ROWS, columns(p)] = jnp.transpose(jnp.concatenate(grad_v, axis=0))
        return carry

    lax.fori_loop(0, PAIRS, pair, 0)

    pulled = rows_s[...] - jnp.transpose(cols_s[...])
    high, middle, low = split_three(pulled)
    upper_first = jnp.concatenate(
        [
            jnp.where(row_iota(HALF, HALF) <= lane_iota(HALF, HALF), 1.0, 0.0),
            jnp.full((HALF, HALF), 0.0, f32) + jnp.where(wide, 1.0, 0.0),
        ],
        axis=1,
    ).astype(bf16)
    upper_second = upper_first[:, :HALF]
    later = jnp.concatenate(
        [
            mm(upper_first, high) + mm(upper_first, middle) + mm(upper_first, low),
            mm(upper_second, high[HALF:]) + mm(upper_second, middle[HALF:])
            + mm(upper_second, low[HALF:]),
        ],
        axis=0,
    )
    grad_dp = later * (1.0 / 16.0) * sigmoid(-(dp[...] + bd[...]))
    gbd[...] = jnp.broadcast_to(jnp.sum(grad_dp, axis=0, keepdims=True), gbd.shape)
    low_s[:, QKVG:] = grad_dp.astype(bf16)

    dv_s[ROWS:, :] = jnp.zeros((8, D), f32)
    position = row_iota(ROWS, 1) & jnp.where(wide, ROWS - 1, HALF - 1)
    last = jnp.where(wide, ROWS - 1, HALF - 1)
    here = dv_s[0:ROWS, :]
    one = jnp.where(position <= last - 1, dv_s[1 : 1 + ROWS, :], 0.0)
    two = jnp.where(position <= last - 2, dv_s[2 : 2 + ROWS, :], 0.0)
    value = qkvg[:, 2 * D : 3 * D]
    low_s[:, 2 * D : 3 * D] = (
        ck[0:1, :] * here + ck[1:2, :] * one + ck[2:3, :] * two
    ).astype(bf16)
    gck[...] = jnp.zeros(gck.shape, f32)
    gck[0:1, :] = jnp.sum(here * value, axis=0, keepdims=True)
    gck[1:2, :] = jnp.sum(one * value, axis=0, keepdims=True)
    gck[2:3, :] = jnp.sum(two * value, axis=0, keepdims=True)

    ordered_t = jnp.transpose(ordered[...].astype(f32)).astype(bf16)

    def weights(j, carry):
        part = pl.ds(pl.multiple_of(j * HALF, HALF), HALF)
        gw[:, part] = mm(ordered_t, low_s[:, part])
        return carry

    lax.fori_loop(0, QKVG // HALF, weights, 0)
    gwd[...] = mm(ordered_t, low_s[:, QKVG:])

    def inner_grad(i, carry):
        rows = pl.ds(pl.multiple_of(i * HALF, HALF), HALF)
        mixed_s[rows, :] = mm_t(low_s[rows, :QKVG], w[...]) + mm_t(low_s[rows, QKVG:], wd[...])
        return carry

    lax.fori_loop(0, 2, inner_grad, 0)
    gmod[...] = jnp.zeros(gmod.shape, f32)
    if flip:
        high, middle, low = split_three(mixed_s[...])
        perm_s[:, :D] = high
        perm_s[:, D : 2 * D] = middle
        perm_s[:, 2 * D :] = low

    def tile(i, carry):
        start = pl.multiple_of(i * HALF, HALF)
        rows = pl.ds(start, HALF)
        slot = jnp.where(wide, 0, i)
        if flip:
            three = mm(order_matrix(start, HALF, wide, False), perm_s[...])
            grad = three[:, :D] + three[:, D : 2 * D] + three[:, 2 * D :]
        else:
            grad = mixed_s[rows, :]
        normal, rate = normalise(x[rows, :].astype(f32))
        where = (pl.ds(slot, 1), slice(0, D))
        gmod[where] = gmod[where] + jnp.sum(grad, axis=0, keepdims=True)
        where = (pl.ds(slot, 1), slice(D, 2 * D))
        gmod[where] = gmod[where] + jnp.sum(grad * normal, axis=0, keepdims=True)
        gx[rows, :] = mid_grad[rows, :] + normalise_back(
            normal, rate, grad * (1.0 + share(mod, slot, 1))
        )
        return carry

    lax.fori_loop(0, 2, tile, 0)


def call(kernel, operands, outs, scratch):
    shapes = [jax.ShapeDtypeStruct(shape, kind) for shape, kind in outs]
    return pl.pallas_call(
        kernel,
        out_shape=shapes,
        in_specs=[pl.BlockSpec(memory_space=pltpu.SMEM)]
        + [pl.BlockSpec(memory_space=pltpu.VMEM)] * (len(operands) - 1),
        out_specs=[pl.BlockSpec(memory_space=pltpu.VMEM)] * len(shapes),
        scratch_shapes=[pltpu.VMEM(shape, kind) for shape, kind in scratch],
        compiler_params=pltpu.CompilerParams(vmem_limit_bytes=48 * 1024 * 1024),
    )(*operands)


def attn_forward(flip, sc, x, mod, w, wd, bd, ck):
    return call(
        functools.partial(attn_forward_kernel, flip),
        (sc, x, mod, w, wd, bd, ck),
        [
            ((ROWS, D), bf16),
            ((ROWS, QKVG), f32),
            ((ROWS, LANES), f32),
            ((ROWS, D), f32),
            ((ROWS, LANES), f32),
            ((LANES, ROWS), f32),
            ((ROWS, D), f32),
            ((ROWS, D), bf16),
        ],
        [((ROWS, D), bf16), ((ROWS + 8, D), f32), ((HALF, ROWS), f32)],
    )


def ffn_forward(sc, x, mod, gated, wo, wu, bu, wn, bn):
    return call(
        ffn_forward_kernel,
        (sc, x, mod, gated, wo, wu, bu, wn, bn),
        [((ROWS, D), bf16), ((ROWS, D), f32), ((ROWS, D), f32)],
        [],
    )


def ffn_backward(sc, x, mod, gated, wo, wu, bu, wn, bn, branch, down, grad):
    return call(
        ffn_backward_kernel,
        (sc, x, mod, gated, wo, wu, bu, wn, bn, branch, down, grad),
        [
            ((ROWS, D), f32),
            ((ROWS, D), bf16),
            ((D, D), f32),
            ((D, FF), f32),
            ((FF, D), f32),
            ((8, 4 * D), f32),
            ((1, FF), f32),
            ((1, D), f32),
        ],
        [((ROWS, FF), bf16), ((ROWS, D), bf16), ((ROWS, FF), bf16), ((ROWS, D), bf16)],
    )


def attn_backward(flip, sc, x, mod, saved, branch_low, mid_grad, w, wd, wo, bd, ck):
    return call(
        functools.partial(attn_backward_kernel, flip),
        (sc, x, mod, *saved, branch_low, mid_grad, w, wd, wo, bd, ck),
        [
            ((ROWS, D), f32),
            ((D, QKVG), f32),
            ((D, LANES), f32),
            ((8, 2 * D), f32),
            ((8, D), f32),
            ((8, LANES), f32),
        ],
        [
            ((ROWS, D), f32),
            ((ROWS, QKVG + LANES), bf16),
            ((ROWS, D), f32),
            ((ROWS + 8, D), f32),
            ((ROWS, LANES), f32),
            ((LANES, ROWS), f32),
            ((HALF, ROWS), f32),
            ((ROWS, 3 * D), bf16),
        ],
    )


def swap(values):
    return lax.ppermute(values, "section", [(0, 1), (1, 0)])


def bits_of(axis):
    size = lax.axis_size(axis)
    return size, size.bit_length() - 1


def partner(values, size, bit):
    return lax.ppermute(values, "row", [(i, i ^ (1 << bit)) for i in range(size)])


def gather_rows(values):
    size, bits = bits_of("row")
    index = lax.axis_index("row")
    held = values.reshape((1,) * bits + values.shape)
    for bit in reversed(range(bits)):
        other = partner(held, size, bit)
        axis = bits - 1 - bit
        held = jnp.where(
            ((index >> bit) & 1) == 0,
            jnp.concatenate([held, other], axis=axis),
            jnp.concatenate([other, held], axis=axis),
        )
    return held.reshape((size,) + values.shape)


def scatter_rows(values):
    size, bits = bits_of("row")
    index = lax.axis_index("row")
    held = values.reshape((2,) * bits + values.shape[1:])
    for bit in range(bits):
        axis = bits - 1 - bit
        mine = (index >> bit) & 1
        sent = lax.dynamic_index_in_dim(held, 1 - mine, axis, keepdims=True).astype(bf16)
        kept = lax.dynamic_index_in_dim(held, mine, axis, keepdims=True)
        held = kept + partner(sent, size, bit).astype(f32)
    return held.reshape(values.shape[1:])


def sum_rows(values):
    size, bits = bits_of("row")
    for bit in range(bits):
        values = values + partner(values, size, bit)
    return values


def on_device(
    tokens, conditions, output_grad, layouts,
    w_ada, b_ada, w_query, w_key, w_value, w_gate, w_out, w_decay, b_decay, conv_kernel,
    w_up, b_up, w_down, b_down,
):
    section = lax.axis_index("section")
    row = lax.axis_index("row")
    is_first = section == 0
    shard = w_query.shape[1]

    decay_wide = jnp.pad(w_decay[0], ((0, 0), (0, LANES - HEADS)))
    attn_shard = jnp.concatenate(
        [w_query[0], w_key[0], w_value[0], w_gate[0], w_out[0], decay_wide, w_ada[0]], axis=1
    )
    ffn_shard = jnp.concatenate([w_up[0]] + [w_down[0][i * shard : (i + 1) * shard] for i in range(4)], axis=1)
    attn_all = gather_rows(attn_shard).reshape(D, -1)
    ffn_all = gather_rows(ffn_shard)
    up_all = ffn_all[:, :, :FF].reshape(D, FF)
    down_all = ffn_all[:, :, FF:].reshape(-1, shard, 4, D).swapaxes(1, 2).reshape(FF, D)

    def both(values):
        other = swap(values)
        return (jnp.where(is_first, values, other), jnp.where(is_first, other, values))

    attn_l = both(attn_all)
    up_l = both(up_all)
    down_l = both(down_all)
    smalls = jnp.concatenate(
        [
            b_ada[0],
            b_up[0],
            b_down[0],
            conv_kernel[0].reshape(-1),
            jnp.pad(b_decay[0], (0, LANES - HEADS)),
        ]
    )
    smalls_l = both(smalls)
    cut = (6 * D, 6 * D + FF, 6 * D + FF + D, 6 * D + FF + 4 * D)

    layer = []
    for l in range(2):
        a = attn_l[l]
        s = smalls_l[l]
        layer.append(
            dict(
                w=a[:, :QKVG],
                wo=a[:, QKVG : QKVG + D],
                wd=a[:, QKVG + D : QKVG + D + LANES],
                ada=a[:, QKVG + D + LANES :],
                wu=up_l[l],
                wn=down_l[l],
                b_ada=s[: cut[0]],
                bu=s[cut[0] : cut[1]][None],
                bn=s[cut[1] : cut[2]][None],
                ck=jnp.pad(s[cut[2] : cut[3]].reshape(3, D), ((0, 5), (0, 0))),
                bd=s[cut[3] :][None],
            )
        )

    stream = lax.dynamic_index_in_dim(tokens, section, 0, keepdims=False)
    grad_rows = lax.dynamic_index_in_dim(output_grad, section, 0, keepdims=False)
    conds = lax.dynamic_index_in_dim(conditions, section, 0, keepdims=False).astype(f32)
    layout = lax.dynamic_index_in_dim(layouts[:, 0], section, 0, keepdims=False)
    sc = jnp.stack([section.astype(jnp.int32), layout])
    lifted = jax.nn.silu(conds).astype(bf16)

    x = stream
    kept = []
    acts = []
    for l in range(2):
        p = layer[l]
        mod = jnp.pad(mm(lifted, p["ada"]) + p["b_ada"], ((0, 6), (0, 0)))
        *saved, gated = attn_forward(l == 1, sc, x, mod, p["w"], p["wd"], p["bd"], p["ck"])
        out, branch, down = ffn_forward(
            sc, x, mod, gated, p["wo"], p["wu"], p["bu"], p["wn"], p["bn"]
        )
        kept.append((x, mod, saved, gated, branch, down))
        acts.append(out)
        x = out

    def assembled(pair):
        mine = jnp.where(is_first, pair[0], pair[1])
        other = swap(jnp.where(is_first, pair[1], pair[0]))
        return jnp.where(is_first, jnp.stack([mine, other]), jnp.stack([other, mine]))

    grad = grad_rows
    in_grads = [None, None]
    grad_mods = [None, None]
    small_grads = [None, None]
    mat_grads = [None, None]
    for l in (1, 0):
        p = layer[l]
        x, mod, saved, gated, branch, down = kept[l]
        mid_grad, branch_low, gwo, gwu, gwn, gmod_b, gbu, gbn = ffn_backward(
            sc, x, mod, gated, p["wo"], p["wu"], p["bu"], p["wn"], p["bn"], branch, down, grad
        )
        gx, gw, gwd, gmod_a, gck, gbd = attn_backward(
            l == 1, sc, x, mod, saved, branch_low, mid_grad,
            p["w"], p["wd"], p["wo"], p["bd"], p["ck"],
        )
        in_grads[l] = gx
        grad = gx.astype(bf16)
        grad_mods[l] = jnp.concatenate([gmod_a[:SLOTS], gmod_b[:SLOTS]], axis=1)
        small_grads[l] = jnp.concatenate([gbu[0], gbn[0], gck[:3].reshape(-1), gbd[0]])
        size = D // shard
        pieces = jnp.concatenate(
            [
                gw.reshape(size, shard, QKVG),
                gwo.reshape(size, shard, D),
                gwd.reshape(size, shard, LANES),
                gwu.reshape(size, shard, FF),
            ]
            + list(jnp.moveaxis(gwn.reshape(size, 4, shard, D), 1, 0)),
            axis=2,
        )
        mat_grads[l] = pieces

    mine = jnp.where(is_first, mat_grads[0], mat_grads[1])
    other = jnp.where(is_first, mat_grads[1], mat_grads[0]).astype(bf16)
    total = scatter_rows(mine + swap(other).astype(f32))
    mine = jnp.where(is_first, small_grads[0], small_grads[1])
    other = jnp.where(is_first, small_grads[1], small_grads[0])
    small_total = sum_rows(mine + swap(other))

    mod_pair = assembled(grad_mods)
    lifted_all = jax.nn.silu(conditions.astype(f32)).astype(bf16)
    sent = jnp.concatenate([mod_pair, lifted_all.astype(f32)], axis=2).reshape(MICRO * SLOTS, -1)
    gathered = gather_rows(sent).reshape(-1, 7 * D)
    grad_mod_all = gathered[:, : 6 * D]
    grad_b_ada = jnp.sum(grad_mod_all, axis=0)
    lifted_rows = lax.dynamic_slice_in_dim(gathered, 6 * D + row * shard, shard, 1).astype(bf16)
    grad_w_ada = lax.dot_general(
        lifted_rows,
        grad_mod_all.astype(bf16),
        (((0,), (0,)), ((), ())),
        preferred_element_type=f32,
    )
    grad_lifted = mm_t(grad_mods[0].astype(bf16), layer[0]["ada"]) + mm_t(
        grad_mods[1].astype(bf16), layer[1]["ada"]
    )
    _, pull_silu = jax.vjp(jax.nn.silu, conds)
    (grad_conds,) = pull_silu(grad_lifted)
    other = swap(grad_conds)
    cond_grads = jnp.where(
        is_first, jnp.stack([grad_conds, other]), jnp.stack([other, grad_conds])
    )

    acts_out = assembled(acts)
    input_out = assembled(in_grads)
    at = QKVG + D + LANES
    down_total = jnp.concatenate(
        [total[:, at + FF + i * D : at + FF + (i + 1) * D] for i in range(4)], axis=0
    )
    s = small_total
    return (
        acts_out[None],
        input_out[None],
        cond_grads,
        grad_w_ada[None],
        grad_b_ada[None],
        total[None, :, :D],
        total[None, :, D : 2 * D],
        total[None, :, 2 * D : 3 * D],
        total[None, :, 3 * D : 4 * D],
        total[None, :, 4 * D : 5 * D],
        total[None, :, 5 * D : 5 * D + HEADS],
        s[None, FF + 4 * D : FF + 4 * D + HEADS],
        s[FF + D : FF + 4 * D].reshape(1, 3, D),
        total[None, :, at : at + FF],
        s[None, :FF],
        down_total[None],
        s[None, FF : FF + D],
    )


def solution(mesh):
    rows = P(None, "row", None)
    mats = P("section", "row", None)
    vector = P("section", None)
    in_specs = (
        rows, rows, rows, P(None, "row"),
        mats, vector, mats, mats, mats, mats, mats, mats, vector, P("section", None, None),
        mats, vector, mats, vector,
    )
    blocks = P("section", None, "row", None)
    out_specs = (
        blocks, blocks, rows,
        mats, vector, mats, mats, mats, mats, mats, mats, vector, P("section", None, None),
        mats, vector, mats, vector,
    )
    return jax.shard_map(
        on_device, mesh=mesh, in_specs=in_specs, out_specs=out_specs, check_vma=False
    )
```

```python
import functools

import jax
import jax.numpy as jnp
from jax import lax
from jax.experimental import pallas as pl
from jax.experimental.pallas import tpu as pltpu
from jax.sharding import PartitionSpec as P

D = 384
HEADS = 6
HEAD_DIM = 64
FF = 1536
MICRO = 2
ROWS = 512
HALF = 256
SLOTS = 2
PAIR = 128
PAIRS = D // PAIR
QKVG = 4 * D
LANES = 128
GROUP = (QKVG + D + LANES) // 2
NEG = -1e30
SCALE = HEAD_DIM**-0.5

bf16 = jnp.bfloat16
f32 = jnp.float32


def mm(left, right):
    return jnp.dot(left, right, preferred_element_type=f32)


def mm_t(left, right):
    return lax.dot_general(left, right, (((1,), (1,)), ((), ())), preferred_element_type=f32)


def split(values):
    high = values.astype(bf16)
    return high, (values - high.astype(f32)).astype(bf16)


def split_three(values):
    high, rest = split(values)
    mid = values - high.astype(f32)
    middle, low = split(mid)
    return high, middle, low


def cat_left(values):
    high, low = split(values)
    return jnp.concatenate([high, low, high], axis=1)


def cat_right(values):
    high, low = split(values)
    return jnp.concatenate([high, high, low], axis=1)


def mm_near(left, right_pair, right_high):
    high, low = split(left)
    wide = mm(high, right_pair)
    return wide[:, :PAIR] + wide[:, PAIR:] + mm(low, right_high)


def lane_iota(rows, columns):
    return lax.broadcasted_iota(jnp.int32, (rows, columns), 1)


def row_iota(rows, columns):
    return lax.broadcasted_iota(jnp.int32, (rows, columns), 0)


def order_matrix(start, rows, wide, to_scan):
    t = row_iota(rows, ROWS) + start
    small = (t & 256) + ((t & 15) << 4) + ((t & 255) >> 4)
    if to_scan:
        large = ((t & 15) << 5) + (t >> 4)
    else:
        large = ((t & 31) << 4) + (t >> 5)
    source = jnp.where(wide, large, small)
    return jnp.where(lane_iota(rows, ROWS) == source, 1.0, 0.0).astype(bf16)


def normalise(values):
    centred = values - jnp.mean(values, axis=-1, keepdims=True)
    rate = lax.rsqrt(jnp.mean(centred * centred, axis=-1, keepdims=True) + 1e-06)
    return centred * rate, rate


def normalise_back(normal, rate, grad):
    return rate * (
        grad
        - jnp.mean(grad, axis=-1, keepdims=True)
        - normal * jnp.mean(grad * normal, axis=-1, keepdims=True)
    )


def share(mod_ref, slot, part):
    return mod_ref[pl.ds(slot, 1), part * D : (part + 1) * D]


def sigmoid(values):
    return 1.0 / (1.0 + jnp.exp(-values))


GELU_A = 0.7978845608028654
GELU_B = 0.044715


def gelu_parts(values):
    square = values * values
    tanh = jnp.tanh(GELU_A * values * (1.0 + GELU_B * square))
    return square, tanh


def fill_bias(bias, wide):
    bias[:, :HALF] = jnp.full((HALF, HALF), 0.0, f32) + jnp.where(wide, 0.0, NEG)
    causal = row_iota(HALF, HALF) >= lane_iota(HALF, HALF)
    bias[:, HALF:] = jnp.where(causal, 0.0, NEG)


def decay_factors(cum, cumt, bias, head):
    row = cumt[pl.ds(head, 1), :]
    lanes = lane_iota(1, LANES)
    column = jnp.sum(jnp.where(lanes == head, cum[...], 0.0), axis=1, keepdims=True)
    first = jnp.exp(column[:HALF] - row[:, :HALF] + bias[:, HALF:])
    second = jnp.exp(column[HALF:] - row + bias[...])
    return first, second


def head_norm(values, lanes):
    square = values * values
    low = jnp.sum(jnp.where(lanes < HEAD_DIM, square, 0.0), axis=1, keepdims=True)
    high = jnp.sum(jnp.where(lanes < HEAD_DIM, 0.0, square), axis=1, keepdims=True)
    return jnp.where(lanes < HEAD_DIM, low, high) * (1.0 / HEAD_DIM)


def fill_decay(dp, bd, cum, cumt):
    raw = dp[...] + bd[...]
    log_decay = (jnp.minimum(raw, 0.0) - jnp.log1p(jnp.exp(-jnp.abs(raw)))) * (1.0 / 16.0)
    high, middle, low = split_three(log_decay)
    causal = jnp.where(row_iota(ROWS, ROWS) >= lane_iota(ROWS, ROWS), 1.0, 0.0).astype(bf16)
    cum[...] = mm(causal, high) + mm(causal, middle) + mm(causal, low)
    cumt[...] = jnp.transpose(cum[...])


def fetch(sc, layer, mine, other, kept, sem):
    @pl.when(sc[0] == layer)
    def _():
        pltpu.make_async_copy(mine, kept, sem).start()

    @pl.when(sc[0] != layer)
    def _():
        pltpu.make_async_copy(other, kept, sem).start()

    return pltpu.make_async_copy(mine, kept, sem)


def columns(index, first=0):
    return pl.ds(pl.multiple_of(index * PAIR + first, PAIR), PAIR)


def attn_forward_kernel(
    layer,
    sc, x, mod, bd, ck, qko_mine, qko_other, vgd_mine, vgd_other,
    ordered, qkvg, dp, vc, cum, cumt, o, gated,
    inner, vpad, bias, w_qk, w_vgd, sems,
):
    flip = layer == 1
    wide = sc[1] == 0
    wait_qk = fetch(
        sc, layer, qko_mine.at[:, : 2 * D], qko_other.at[:, : 2 * D], w_qk, sems.at[0]
    )
    wait_vgd = fetch(sc, layer, vgd_mine, vgd_other, w_vgd, sems.at[1])

    def first(i, carry):
        rows = pl.ds(pl.multiple_of(i * HALF, HALF), HALF)
        slot = jnp.where(wide, 0, i)
        normal, _ = normalise(x[rows, :].astype(f32))
        inner[rows, :] = (normal * (1.0 + share(mod, slot, 1)) + share(mod, slot, 0)).astype(bf16)
        return carry

    lax.fori_loop(0, 2, first, 0)
    wait_qk.wait()
    wait_vgd.wait()

    def project(i, carry):
        start = pl.multiple_of(i * HALF, HALF)
        rows = pl.ds(start, HALF)
        if flip:
            part = mm(order_matrix(start, HALF, wide, True), inner[...]).astype(bf16)
        else:
            part = inner[rows, :]
        ordered[rows, :] = part
        qkvg[rows, : 2 * D] = mm(part, w_qk[...])
        qkvg[rows, 2 * D :] = mm(part, w_vgd[:, : 2 * D])
        dp[rows, :] = mm(part, w_vgd[:, 2 * D :])
        return carry

    lax.fori_loop(0, 2, project, 0)
    fill_decay(dp, bd, cum, cumt)
    fill_bias(bias, wide)

    vpad[0:8, :] = jnp.zeros((8, D), f32)
    vpad[8 : 8 + ROWS, :] = qkvg[:, 2 * D : 3 * D]
    position = row_iota(ROWS, 1) & jnp.where(wide, ROWS - 1, HALF - 1)
    one = jnp.where(position >= 1, vpad[7 : 7 + ROWS, :], 0.0)
    two = jnp.where(position >= 2, vpad[6 : 6 + ROWS, :], 0.0)
    vc[...] = ck[0:1, :] * vpad[8 : 8 + ROWS, :] + ck[1:2, :] * one + ck[2:3, :] * two

    def pair(p, carry):
        lanes = lane_iota(1, PAIR)
        queries = cat_left(qkvg[:, columns(p)] * SCALE)
        keys = qkvg[:, columns(p, D)]
        value_high, value_low = split(vc[:, columns(p)])
        values = jnp.concatenate([value_high, value_low], axis=1)
        parts = []
        for e in range(2):
            key_cat = cat_right(jnp.where((lanes // HEAD_DIM) == e, keys, 0.0))
            first, second = decay_factors(cum, cumt, bias, 2 * p + e)
            first = first * mm_t(queries[:HALF], key_cat[:HALF])
            second = second * mm_t(queries[HALF:], key_cat)
            parts.append(
                jnp.concatenate(
                    [
                        mm_near(first, values[:HALF], value_high[:HALF]),
                        mm_near(second, values, value_high),
                    ],
                    axis=0,
                )
            )
        total = jnp.where(lanes < HEAD_DIM, parts[0], parts[1])
        o[:, columns(p)] = total
        gate = qkvg[:, columns(p, 3 * D)]
        normed = total * lax.rsqrt(head_norm(total, lanes) + 1.0)
        mixed = (normed * (gate * sigmoid(gate))).astype(bf16)
        if flip:
            inner[:, columns(p)] = mixed
        else:
            gated[:, columns(p)] = mixed
        return carry

    lax.fori_loop(0, PAIRS, pair, 0)
    if flip:

        def back(i, carry):
            start = pl.multiple_of(i * HALF, HALF)
            gated[pl.ds(start, HALF), :] = mm(
                order_matrix(start, HALF, wide, False), inner[...]
            ).astype(bf16)
            return carry

        lax.fori_loop(0, 2, back, 0)


def ffn_forward_kernel(
    layer,
    sc, x, mod, gated, bu, bn, qko_mine, qko_other, up_mine, up_other, down_mine, down_other,
    out, branch, down,
    wo, wu, wn, sems,
):
    wide = sc[1] == 0
    waits = [
        fetch(sc, layer, qko_mine.at[:, 2 * D :], qko_other.at[:, 2 * D :], wo, sems.at[0]),
        fetch(sc, layer, up_mine, up_other, wu, sems.at[1]),
        fetch(sc, layer, down_mine, down_other, wn, sems.at[2]),
    ]
    for wait in waits:
        wait.wait()
    live_rows = jnp.where(wide, ROWS, sc[1] * HALF)

    def tile(i, carry):
        start = pl.multiple_of(i * HALF, HALF)
        rows = pl.ds(start, HALF)
        slot = jnp.where(wide, 0, i)
        grown = mm(gated[rows, :], wo[...])
        branch[rows, :] = grown
        middle = x[rows, :].astype(f32) + share(mod, slot, 2) * grown
        normal, _ = normalise(middle)
        inner = (normal * (1.0 + share(mod, slot, 4)) + share(mod, slot, 3)).astype(bf16)
        up = mm(inner, wu[...]) + bu[...]
        _, tanh = gelu_parts(up)
        hidden = (0.5 * up * (1.0 + tanh)).astype(bf16)
        low = mm(hidden, wn[...])
        down[rows, :] = low
        result = middle + share(mod, slot, 5) * (low + bn[...])
        live = (row_iota(HALF, 1) + start) < live_rows
        out[rows, :] = jnp.where(live, result, 0.0).astype(bf16)
        return carry

    lax.fori_loop(0, 2, tile, 0)


def ffn_backward_kernel(
    layer,
    sc, x, mod, gated, bu, bn, branch, down, grad, up_mine, up_other, down_mine, down_other,
    mid_grad, branch_low, gwo, gwu_keep, gwu_send, gwn, gmod, gbu, gbn,
    hidden_s, inner_s, up_s, down_s, wu, wn, sems,
):
    wide = sc[1] == 0
    waits = [
        fetch(sc, layer, up_mine, up_other, wu, sems.at[0]),
        fetch(sc, layer, down_mine, down_other, wn, sems.at[1]),
    ]
    for wait in waits:
        wait.wait()
    live_rows = jnp.where(wide, ROWS, sc[1] * HALF)
    gmod[...] = jnp.zeros(gmod.shape, f32)
    gbu[...] = jnp.zeros(gbu.shape, f32)
    gbn[...] = jnp.zeros(gbn.shape, f32)

    def tile(i, carry):
        start = pl.multiple_of(i * HALF, HALF)
        rows = pl.ds(start, HALF)
        slot = jnp.where(wide, 0, i)

        def add(part, values):
            where = (pl.ds(slot, 1), slice((part - 2) * D, (part - 1) * D))
            gmod[where] = gmod[where] + jnp.sum(values, axis=0, keepdims=True)

        grown = branch[rows, :]
        middle = x[rows, :].astype(f32) + share(mod, slot, 2) * grown
        normal, rate = normalise(middle)
        inner = (normal * (1.0 + share(mod, slot, 4)) + share(mod, slot, 3)).astype(bf16)
        inner_s[rows, :] = inner
        live = (row_iota(HALF, 1) + start) < live_rows
        above = jnp.where(live, grad[rows, :].astype(f32), 0.0)
        add(5, above * (down[rows, :] + bn[...]))
        grad_down = above * share(mod, slot, 5)
        gbn[...] = gbn[...] + jnp.sum(grad_down, axis=0, keepdims=True)
        down_low = grad_down.astype(bf16)
        down_s[rows, :] = down_low
        up = mm(inner, wu[...]) + bu[...]
        square, tanh = gelu_parts(up)
        half = 0.5 * (1.0 + tanh)
        hidden_s[rows, :] = (up * half).astype(bf16)
        slope = half + 0.5 * up * (1.0 - tanh * tanh) * (
            GELU_A * (1.0 + 3.0 * GELU_B * square)
        )
        grad_up = mm_t(down_low, wn[...]) * slope
        gbu[...] = gbu[...] + jnp.sum(grad_up, axis=0, keepdims=True)
        up_low = grad_up.astype(bf16)
        up_s[rows, :] = up_low
        grad_inner = mm_t(up_low, wu[...])
        add(3, grad_inner)
        add(4, grad_inner * normal)
        grad_middle = above + normalise_back(
            normal, rate, grad_inner * (1.0 + share(mod, slot, 4))
        )
        mid_grad[rows, :] = grad_middle
        add(2, grad_middle * grown)
        branch_low[rows, :] = (grad_middle * share(mod, slot, 2)).astype(bf16)
        return carry

    lax.fori_loop(0, 2, tile, 0)

    inner_t = jnp.transpose(inner_s[...].astype(f32)).astype(bf16)
    gwo[...] = mm(jnp.transpose(gated[...].astype(f32)).astype(bf16), branch_low[...])

    def weights(j, carry):
        part = pl.ds(pl.multiple_of(j * HALF, HALF), HALF)
        hidden_t = jnp.transpose(hidden_s[:, part].astype(f32)).astype(bf16)
        gwn[part, :] = mm(hidden_t, down_s[...])
        return carry

    lax.fori_loop(0, FF // HALF, weights, 0)

    def halves(j, carry):
        here = pl.ds(pl.multiple_of(j * HALF, HALF), HALF)
        keep = pl.ds(pl.multiple_of(j * HALF + sc[0] * (FF // 2), HALF), HALF)
        send = pl.ds(pl.multiple_of(j * HALF + (1 - sc[0]) * (FF // 2), HALF), HALF)
        gwu_keep[:, here] = mm(inner_t, up_s[:, keep])
        gwu_send[:, here] = mm(inner_t, up_s[:, send]).astype(bf16)
        return carry

    lax.fori_loop(0, FF // 2 // HALF, halves, 0)


def attn_backward_kernel(
    layer,
    sc, x, mod, ordered, qkvg, dp, vc, cum, cumt, o, branch_low, mid_grad, gwo, bd, ck,
    qko_mine, qko_other, vgd_mine, vgd_other,
    gx, gw_keep, gw_send, gmod, gck, gbd,
    mixed_s, low_s, dv_s, rows_s, cols_s, bias, perm_s, gw, w_qko, w_vgd, sems,
):
    flip = layer == 1
    wide = sc[1] == 0
    wait_qko = fetch(sc, layer, qko_mine, qko_other, w_qko, sems.at[0])
    wait_vgd = fetch(sc, layer, vgd_mine, vgd_other, w_vgd, sems.at[1])
    fill_bias(bias, wide)
    wait_qko.wait()
    wait_vgd.wait()

    def first(i, carry):
        start = pl.multiple_of(i * HALF, HALF)
        rows = pl.ds(start, HALF)
        if flip:
            part = mm(order_matrix(start, HALF, wide, True), branch_low[...]).astype(bf16)
        else:
            part = branch_low[rows, :]
        mixed_s[rows, :] = mm_t(part, w_qko[:, 2 * D :])
        return carry

    lax.fori_loop(0, 2, first, 0)
    rows_s[...] = jnp.zeros(rows_s.shape, f32)
    cols_s[...] = jnp.zeros(cols_s.shape, f32)

    def pair(p, carry):
        lanes = lane_iota(1, PAIR)
        total = o[:, columns(p)]
        gate = qkvg[:, columns(p, 3 * D)]
        above = mixed_s[:, columns(p)]
        rate = lax.rsqrt(head_norm(total, lanes) + 1.0)
        sig = sigmoid(gate)
        grad_gate = above * (total * rate) * (sig * (1.0 + gate * (1.0 - sig)))
        low_s[:, columns(p, 3 * D)] = grad_gate.astype(bf16)
        grad_normed = above * (gate * sig)
        product = grad_normed * total
        inside = jnp.where(
            lanes < HEAD_DIM,
            jnp.sum(jnp.where(lanes < HEAD_DIM, product, 0.0), axis=1, keepdims=True),
            jnp.sum(jnp.where(lanes < HEAD_DIM, 0.0, product), axis=1, keepdims=True),
        ) * (1.0 / HEAD_DIM)
        grad_o = rate * grad_normed - total * (rate * rate * rate) * inside

        queries = qkvg[:, columns(p)] * SCALE
        keys = qkvg[:, columns(p, D)]
        values = vc[:, columns(p)]
        query_cat = cat_left(queries)
        grad_cat = cat_left(grad_o)
        key_high, key_low = split(keys)
        key_pair = jnp.concatenate([key_high, key_low], axis=1)
        query_t = jnp.transpose(queries)
        grad_t = jnp.transpose(grad_o)
        grad_q = []
        grad_k = []
        grad_v = []
        for e in range(2):
            mine = (lanes // HEAD_DIM) == e
            head = 2 * p + e
            key_cat = cat_right(jnp.where(mine, keys, 0.0))
            value_cat = cat_right(jnp.where(mine, values, 0.0))
            first, second = decay_factors(cum, cumt, bias, head)
            raw_first = mm_t(query_cat[:HALF], key_cat[:HALF])
            raw_second = mm_t(query_cat[HALF:], key_cat)
            grad_first = first * mm_t(grad_cat[:HALF], value_cat[:HALF])
            grad_second = second * mm_t(grad_cat[HALF:], value_cat)
            score_first = raw_first * first
            score_second = raw_second * second
            pull_first = grad_first * raw_first
            pull_second = grad_second * raw_second
            here = lanes == head
            rows_s[:HALF, :] = rows_s[:HALF, :] + jnp.where(
                here, jnp.sum(pull_first, axis=1, keepdims=True), 0.0
            )
            rows_s[HALF:, :] = rows_s[HALF:, :] + jnp.where(
                here, jnp.sum(pull_second, axis=1, keepdims=True), 0.0
            )
            low_cols = jnp.sum(pull_second, axis=0, keepdims=True)
            cols_s[pl.ds(head, 1), :HALF] = low_cols[:, :HALF] + jnp.sum(
                pull_first, axis=0, keepdims=True
            )
            cols_s[pl.ds(head, 1), HALF:] = low_cols[:, HALF:]
            grad_q.append(
                jnp.concatenate(
                    [
                        mm_near(grad_first, key_pair[:HALF], key_high[:HALF]),
                        mm_near(grad_second, key_pair, key_high),
                    ],
                    axis=0,
                )
            )

            def turned(source_t, block_first, block_second):
                high, low = split(source_t[e * HEAD_DIM : (e + 1) * HEAD_DIM, :])
                both = jnp.concatenate([high, low], axis=0)
                first_high, first_low = split(block_first)
                second_high, second_low = split(block_second)
                one = mm(both[:, :HALF], first_high)
                one = one[:HEAD_DIM] + one[HEAD_DIM:] + mm(high[:, :HALF], first_low)
                two = mm(both[:, HALF:], second_high)
                two = two[:HEAD_DIM] + two[HEAD_DIM:] + mm(high[:, HALF:], second_low)
                return jnp.concatenate([two[:, :HALF] + one, two[:, HALF:]], axis=1)

            grad_k.append(turned(query_t, grad_first, grad_second))
            grad_v.append(turned(grad_t, score_first, score_second))
        query_grad = jnp.where(lanes < HEAD_DIM, grad_q[0], grad_q[1]) * SCALE
        low_s[:, columns(p)] = query_grad.astype(bf16)
        low_s[:, columns(p, D)] = jnp.transpose(jnp.concatenate(grad_k, axis=0)).astype(bf16)
        dv_s[:ROWS, columns(p)] = jnp.transpose(jnp.concatenate(grad_v, axis=0))
        return carry

    lax.fori_loop(0, PAIRS, pair, 0)

    pulled = rows_s[...] - jnp.transpose(cols_s[...])
    high, middle, low = split_three(pulled)
    upper_first = jnp.concatenate(
        [
            jnp.where(row_iota(HALF, HALF) <= lane_iota(HALF, HALF), 1.0, 0.0),
            jnp.full((HALF, HALF), 0.0, f32) + jnp.where(wide, 1.0, 0.0),
        ],
        axis=1,
    ).astype(bf16)
    upper_second = upper_first[:, :HALF]
    later = jnp.concatenate(
        [
            mm(upper_first, high) + mm(upper_first, middle) + mm(upper_first, low),
            mm(upper_second, high[HALF:]) + mm(upper_second, middle[HALF:])
            + mm(upper_second, low[HALF:]),
        ],
        axis=0,
    )
    grad_dp = later * (1.0 / 16.0) * sigmoid(-(dp[...] + bd[...]))
    gbd[...] = jnp.broadcast_to(jnp.sum(grad_dp, axis=0, keepdims=True), gbd.shape)
    low_s[:, QKVG:] = grad_dp.astype(bf16)

    dv_s[ROWS:, :] = jnp.zeros((8, D), f32)
    position = row_iota(ROWS, 1) & jnp.where(wide, ROWS - 1, HALF - 1)
    last = jnp.where(wide, ROWS - 1, HALF - 1)
    here = dv_s[0:ROWS, :]
    one = jnp.where(position <= last - 1, dv_s[1 : 1 + ROWS, :], 0.0)
    two = jnp.where(position <= last - 2, dv_s[2 : 2 + ROWS, :], 0.0)
    value = qkvg[:, 2 * D : 3 * D]
    low_s[:, 2 * D : 3 * D] = (
        ck[0:1, :] * here + ck[1:2, :] * one + ck[2:3, :] * two
    ).astype(bf16)
    gck[...] = jnp.zeros(gck.shape, f32)
    gck[0:1, :] = jnp.sum(here * value, axis=0, keepdims=True)
    gck[1:2, :] = jnp.sum(one * value, axis=0, keepdims=True)
    gck[2:3, :] = jnp.sum(two * value, axis=0, keepdims=True)

    ordered_t = jnp.transpose(ordered[...].astype(f32)).astype(bf16)

    def weights(j, carry):
        part = pl.ds(pl.multiple_of(j * HALF, HALF), HALF)
        gw[:, part] = mm(ordered_t, low_s[:, part])
        return carry

    lax.fori_loop(0, QKVG // HALF, weights, 0)
    gw[:, QKVG : QKVG + D] = gwo[...]
    gw[:, QKVG + D :] = mm(ordered_t, low_s[:, QKVG:])

    def halves(j, carry):
        here = pl.ds(pl.multiple_of(j * HALF, HALF), HALF)
        gw_keep[:, here] = gw[:, pl.ds(pl.multiple_of(j * HALF + sc[0] * GROUP, HALF), HALF)]
        send = gw[:, pl.ds(pl.multiple_of(j * HALF + (1 - sc[0]) * GROUP, HALF), HALF)]
        gw_send[:, here] = send.astype(bf16)
        return carry

    lax.fori_loop(0, GROUP // HALF, halves, 0)

    def inner_grad(i, carry):
        rows = pl.ds(pl.multiple_of(i * HALF, HALF), HALF)
        mixed_s[rows, :] = mm_t(low_s[rows, : 2 * D], w_qko[:, : 2 * D]) + mm_t(
            low_s[rows, 2 * D :], w_vgd[...]
        )
        return carry

    lax.fori_loop(0, 2, inner_grad, 0)
    gmod[...] = jnp.zeros(gmod.shape, f32)
    if flip:
        high, middle, low = split_three(mixed_s[...])
        perm_s[:, :D] = high
        perm_s[:, D : 2 * D] = middle
        perm_s[:, 2 * D :] = low

    def tile(i, carry):
        start = pl.multiple_of(i * HALF, HALF)
        rows = pl.ds(start, HALF)
        slot = jnp.where(wide, 0, i)
        if flip:
            three = mm(order_matrix(start, HALF, wide, False), perm_s[...])
            grad = three[:, :D] + three[:, D : 2 * D] + three[:, 2 * D :]
        else:
            grad = mixed_s[rows, :]
        normal, rate = normalise(x[rows, :].astype(f32))
        where = (pl.ds(slot, 1), slice(0, D))
        gmod[where] = gmod[where] + jnp.sum(grad, axis=0, keepdims=True)
        where = (pl.ds(slot, 1), slice(D, 2 * D))
        gmod[where] = gmod[where] + jnp.sum(grad * normal, axis=0, keepdims=True)
        gx[rows, :] = mid_grad[rows, :] + normalise_back(
            normal, rate, grad * (1.0 + share(mod, slot, 1))
        )
        return carry

    lax.fori_loop(0, 2, tile, 0)


ANY = pl.BlockSpec(memory_space=pl.ANY)
VMEM = pl.BlockSpec(memory_space=pltpu.VMEM)


def call(kernel, operands, weights, outs, scratch, flops):
    shapes = [jax.ShapeDtypeStruct(shape, kind) for shape, kind in outs]
    buffers = [pltpu.VMEM(shape, kind) for shape, kind in scratch]
    if weights:
        buffers.append(pltpu.SemaphoreType.DMA((3,)))
    return pl.pallas_call(
        kernel,
        out_shape=shapes,
        in_specs=[pl.BlockSpec(memory_space=pltpu.SMEM)]
        + [VMEM] * (len(operands) - 1)
        + [ANY] * len(weights),
        out_specs=[VMEM] * len(shapes),
        scratch_shapes=buffers,
        compiler_params=pltpu.CompilerParams(vmem_limit_bytes=48 * 1024 * 1024),
        cost_estimate=pl.CostEstimate(flops=flops, bytes_accessed=8 << 20, transcendentals=0),
    )(*operands, *weights)


def attn_forward(layer, sc, x, mod, bd, ck, qko, vgd):
    return call(
        functools.partial(attn_forward_kernel, layer),
        (sc, x, mod, bd, ck),
        (*qko, *vgd),
        [
            ((ROWS, D), bf16),
            ((ROWS, QKVG), f32),
            ((ROWS, LANES), f32),
            ((ROWS, D), f32),
            ((ROWS, LANES), f32),
            ((LANES, ROWS), f32),
            ((ROWS, D), f32),
            ((ROWS, D), bf16),
        ],
        [
            ((ROWS, D), bf16),
            ((ROWS + 8, D), f32),
            ((HALF, ROWS), f32),
            ((D, 2 * D), bf16),
            ((D, 2 * D + LANES), bf16),
        ],
        8 * 10**9,
    )


def ffn_forward(layer, sc, x, mod, gated, bu, bn, qko, up, down):
    return call(
        functools.partial(ffn_forward_kernel, layer),
        (sc, x, mod, gated, bu, bn),
        (*qko, *up, *down),
        [((ROWS, D), bf16), ((ROWS, D), f32), ((ROWS, D), f32)],
        [((D, D), bf16), ((D, FF), bf16), ((FF, D), bf16)],
        5 * 10**9,
    )


def ffn_backward(layer, sc, x, mod, gated, bu, bn, branch, down_raw, grad, up, down):
    return call(
        functools.partial(ffn_backward_kernel, layer),
        (sc, x, mod, gated, bu, bn, branch, down_raw, grad),
        (*up, *down),
        [
            ((ROWS, D), f32),
            ((ROWS, D), bf16),
            ((D, D), f32),
            ((D, FF // 2), f32),
            ((D, FF // 2), bf16),
            ((FF, D), f32),
            ((8, 4 * D), f32),
            ((1, FF), f32),
            ((1, D), f32),
        ],
        [
            ((ROWS, FF), bf16),
            ((ROWS, D), bf16),
            ((ROWS, FF), bf16),
            ((ROWS, D), bf16),
            ((D, FF), bf16),
            ((FF, D), bf16),
        ],
        12 * 10**9,
    )


def attn_backward(layer, sc, x, mod, saved, branch_low, mid_grad, gwo, bd, ck, qko, vgd):
    return call(
        functools.partial(attn_backward_kernel, layer),
        (sc, x, mod, *saved, branch_low, mid_grad, gwo, bd, ck),
        (*qko, *vgd),
        [
            ((ROWS, D), f32),
            ((D, GROUP), f32),
            ((D, GROUP), bf16),
            ((8, 2 * D), f32),
            ((8, D), f32),
            ((8, LANES), f32),
        ],
        [
            ((ROWS, D), f32),
            ((ROWS, QKVG + LANES), bf16),
            ((ROWS + 8, D), f32),
            ((ROWS, LANES), f32),
            ((LANES, ROWS), f32),
            ((HALF, ROWS), f32),
            ((ROWS, 3 * D), bf16),
            ((D, 2 * GROUP), f32),
            ((D, 3 * D), bf16),
            ((D, 2 * D + LANES), bf16),
        ],
        18 * 10**9,
    )


def pack_kernel(*refs):
    packed = refs[-1]
    at = 0
    for ref in refs[:-1]:
        width = ref.shape[1]
        if width % LANES:
            packed[:, at:] = jnp.zeros((packed.shape[0], packed.shape[1] - at), packed.dtype)
        packed[:, at : at + width] = ref[...]
        at += width


def pack(*arrays):
    total = sum(-(-array.shape[1] // LANES) * LANES for array in arrays)
    return pl.pallas_call(
        pack_kernel,
        out_shape=jax.ShapeDtypeStruct((arrays[0].shape[0], total), arrays[0].dtype),
        in_specs=[VMEM] * len(arrays),
        out_specs=VMEM,
    )(*arrays)


def swap(values):
    return lax.ppermute(values, "section", [(0, 1), (1, 0)])


def row_bits():
    bits = lax.axis_size("row").bit_length() - 1
    third = bits // 3
    return (
        tuple(range(third)),
        tuple(range(third, 2 * third)),
        tuple(range(2 * third, bits)),
    )


def partner(values, bit):
    size = lax.axis_size("row")
    return lax.ppermute(values, "row", [(i, i ^ (1 << bit)) for i in range(size)])


def double(held, bit):
    bits = lax.axis_size("row").bit_length() - 1
    same = ((lax.axis_index("row") >> bit) & 1) == 0
    other = partner(held, bit)
    axis = bits - 1 - bit
    return jnp.where(
        same,
        jnp.concatenate([held, other], axis=axis),
        jnp.concatenate([other, held], axis=axis),
    )


def gather_pair(first, second):
    along_x, along_y, along_z = row_bits()
    bits = lax.axis_size("row").bit_length() - 1
    first = first.reshape((1,) * bits + first.shape)
    second = second.reshape((1,) * bits + second.shape)
    for bit in reversed(along_z):
        first, second = double(first, bit), double(second, bit)
    for bit in along_x + along_y:
        first = double(first, bit)
    for bit in along_y + along_x:
        second = double(second, bit)
    return first.reshape((-1,) + first.shape[bits:]), second.reshape((-1,) + second.shape[bits:])


def exchange(values):
    return lax.all_to_all(values, "row", 0, 0, tiled=True)


def gather_small(values):
    return exchange(jnp.broadcast_to(values[None], (lax.axis_size("row"),) + values.shape))


def scatter_rows(values):
    return jnp.sum(exchange(values).astype(f32), axis=0)


def on_device(
    tokens, conditions, output_grad, layouts,
    w_ada, b_ada, w_query, w_key, w_value, w_gate, w_out, w_decay, b_decay, conv_kernel,
    w_up, b_up, w_down, b_down,
):
    section = lax.axis_index("section")
    row = lax.axis_index("row")
    devices = lax.axis_size("row")
    is_first = section == 0
    shard = w_query.shape[1]
    def pick(pair):
        return jnp.where(is_first, pair[0], pair[1])

    def pick_other(pair):
        return jnp.where(is_first, pair[1], pair[0])

    lifted_own = jax.nn.silu(conditions.astype(f32)).astype(bf16)
    lifted_parts = lifted_own.reshape(MICRO * SLOTS, devices, shard).swapaxes(0, 1)
    lifted_cut = exchange(lifted_parts).reshape(devices * MICRO * SLOTS, shard)
    terms = mm(lifted_cut, w_ada[0]).reshape(devices, MICRO * SLOTS, 6 * D)
    mod_rows = scatter_rows(terms) + b_ada[0]
    mod_rows = mod_rows.reshape(MICRO, SLOTS, 6 * D)
    mod_mine = lax.dynamic_index_in_dim(mod_rows, section, 0, keepdims=False)
    mod_other = swap(lax.dynamic_index_in_dim(mod_rows, 1 - section, 0, keepdims=False))
    mods = [pick((mod_mine, mod_other)), pick_other((mod_mine, mod_other))]

    def both(values):
        return values, swap(values)

    qko_all, vgd_all = gather_pair(
        pack(w_query[0], w_key[0], w_out[0]), pack(w_value[0], w_gate[0], w_decay[0])
    )
    qko = both(qko_all.reshape(D, 3 * D))
    vgd = both(vgd_all.reshape(D, 2 * D + LANES))
    up_all, down_all = gather_pair(w_up[0], w_down[0])
    up = both(up_all.reshape(D, FF))
    down = both(down_all.reshape(FF, D))
    smalls = jnp.concatenate(
        [
            b_up[0],
            b_down[0],
            conv_kernel[0].reshape(-1),
            jnp.pad(b_decay[0], (0, LANES - HEADS)),
        ]
    )
    smalls_both = both(smalls)
    cut = (FF, FF + D, FF + 4 * D)

    stream = lax.dynamic_index_in_dim(tokens, section, 0, keepdims=False)
    grad = lax.dynamic_index_in_dim(output_grad, section, 0, keepdims=False)
    layout = lax.dynamic_index_in_dim(layouts[:, 0], section, 0, keepdims=False)
    sc = jnp.stack([section.astype(jnp.int32), layout])

    x = stream
    kept = []
    acts = []
    for l in range(2):
        s = pick(smalls_both) if l == 0 else pick_other(smalls_both)
        bu = s[: cut[0]][None]
        bn = s[cut[0] : cut[1]][None]
        ck = jnp.pad(s[cut[1] : cut[2]].reshape(3, D), ((0, 5), (0, 0)))
        bd = s[cut[2] :][None]
        mod = jnp.pad(mods[l], ((0, 6), (0, 0)))
        *saved, gated = attn_forward(l, sc, x, mod, bd, ck, qko, vgd)
        out, branch, down_raw = ffn_forward(l, sc, x, mod, gated, bu, bn, qko, up, down)
        kept.append((x, mod, saved, gated, branch, down_raw, bu, bn, ck, bd))
        acts.append(out)
        x = out

    late, _ = lax.optimization_barrier((w_ada[0], acts[0]))
    ada_all = lax.all_gather(late, "row", axis=0, tiled=True)

    in_grads = [None, None]
    grad_mods = [None, None]
    small_grads = [None, None]
    sums = [None, None]
    for l in (1, 0):
        x, mod, saved, gated, branch, down_raw, bu, bn, ck, bd = kept[l]
        mid_grad, branch_low, gwo, gwu_keep, gwu_send, gwn, gmod_b, gbu, gbn = ffn_backward(
            l, sc, x, mod, gated, bu, bn, branch, down_raw, grad, up, down
        )
        gx, gw_keep, gw_send, gmod_a, gck, gbd = attn_backward(
            l, sc, x, mod, saved, branch_low, mid_grad, gwo, bd, ck, qko, vgd
        )
        in_grads[l] = gx
        grad = gx.astype(bf16)
        grad_mods[l] = jnp.concatenate([gmod_a[:SLOTS], gmod_b[:SLOTS]], axis=1)
        small_grads[l] = jnp.concatenate(
            [jnp.sum(grad_mods[l], axis=0), gbu[0], gbn[0], gck[:3].reshape(-1), gbd[0]]
        )
        up_half = gwu_keep + swap(gwu_send).astype(f32)
        down_pair = gwn.reshape(devices, 2, FF // devices // 2, D)
        down_half = lax.dynamic_index_in_dim(down_pair, section, 1, keepdims=False) + swap(
            lax.dynamic_index_in_dim(down_pair, 1 - section, 1, keepdims=False).astype(bf16)
        ).astype(f32)
        attn_half = gw_keep + swap(gw_send).astype(f32)
        sums[l] = (
            scatter_rows(attn_half.reshape(devices, shard, GROUP).astype(bf16)),
            scatter_rows(up_half.reshape(devices, shard, FF // 2).astype(bf16)),
            scatter_rows(down_half.astype(bf16)),
        )

    def halves(number, axis):
        mine = pick((sums[0][number], sums[1][number]))
        other = swap(pick_other((sums[0][number], sums[1][number])))
        return [pick((mine, other)), pick_other((mine, other))]

    attn_total = jnp.concatenate(halves(0, 1), axis=1)
    up_total = jnp.concatenate(halves(1, 1), axis=1)
    down_total = jnp.concatenate(halves(2, 0), axis=0)

    small_total = jnp.sum(
        gather_small(pick(small_grads) + swap(pick_other(small_grads))), axis=0
    )

    mod_own = pick(grad_mods).astype(bf16)
    mod_swapped = swap(pick_other(grad_mods).astype(bf16))
    mod_low = jnp.concatenate(
        [pick((mod_own, mod_swapped)), pick_other((mod_own, mod_swapped))], axis=0
    )
    mod_all = gather_small(mod_low).reshape(-1, 6 * D)
    grad_w_ada = lax.dot_general(
        lifted_cut, mod_all, (((0,), (0,)), ((), ())), preferred_element_type=f32
    )
    grad_lifted = mm_t(mod_low, ada_all)
    grad_lifted = (grad_lifted + swap(grad_lifted)).reshape(MICRO, SLOTS, D)
    _, pull_silu = jax.vjp(jax.nn.silu, conditions.astype(f32))
    (cond_grads,) = pull_silu(grad_lifted)

    def assembled(pair):
        mine = pick(pair)
        other = swap(pick_other(pair))
        return jnp.stack([pick((mine, other)), pick_other((mine, other))])

    s = small_total
    first = 6 * D
    return (
        assembled(acts)[None],
        assembled(in_grads)[None],
        cond_grads,
        grad_w_ada[None],
        s[None, :first],
        attn_total[None, :, :D],
        attn_total[None, :, D : 2 * D],
        attn_total[None, :, 2 * D : 3 * D],
        attn_total[None, :, 3 * D : 4 * D],
        attn_total[None, :, 4 * D : 5 * D],
        attn_total[None, :, 5 * D : 5 * D + HEADS],
        s[None, first + FF + 4 * D : first + FF + 4 * D + HEADS],
        s[first + FF + D : first + FF + 4 * D].reshape(1, 3, D),
        up_total[None],
        s[None, first : first + FF],
        down_total[None],
        s[None, first + FF : first + FF + D],
    )


def solution(mesh):
    rows = P(None, "row", None)
    mats = P("section", "row", None)
    vector = P("section", None)
    in_specs = (
        rows, rows, rows, P(None, "row"),
        mats, vector, mats, mats, mats, mats, mats, mats, vector, P("section", None, None),
        mats, vector, mats, vector,
    )
    blocks = P("section", None, "row", None)
    out_specs = (
        blocks, blocks, rows,
        mats, vector, mats, mats, mats, mats, mats, mats, vector, P("section", None, None),
        mats, vector, mats, vector,
    )
    return jax.shard_map(
        on_device, mesh=mesh, in_specs=in_specs, out_specs=out_specs, check_vma=False
    )
```

```python
import functools

import jax
import jax.numpy as jnp
from jax import lax
from jax.experimental import pallas as pl
from jax.experimental.pallas import tpu as pltpu
from jax.sharding import PartitionSpec as P

D = 384
HEADS = 6
HEAD_DIM = 64
FF = 1536
MICRO = 2
ROWS = 512
HALF = 256
SLOTS = 2
PAIR = 128
PAIRS = D // PAIR
QKVG = 4 * D
LANES = 128
GROUP = (QKVG + D + LANES) // 2
NEG = -1e30
SCALE = HEAD_DIM**-0.5

bf16 = jnp.bfloat16
f32 = jnp.float32


def mm(left, right):
    return jnp.dot(left, right, preferred_element_type=f32)


def mm_t(left, right):
    return lax.dot_general(left, right, (((1,), (1,)), ((), ())), preferred_element_type=f32)


def split(values):
    high = values.astype(bf16)
    return high, (values - high.astype(f32)).astype(bf16)


def split_three(values):
    high, rest = split(values)
    mid = values - high.astype(f32)
    middle, low = split(mid)
    return high, middle, low


def cat_left(values):
    high, low = split(values)
    return jnp.concatenate([high, low, high], axis=1)


def cat_right(values):
    high, low = split(values)
    return jnp.concatenate([high, high, low], axis=1)


def mm_near(left, right_pair, right_high):
    high, low = split(left)
    wide = mm(high, right_pair)
    return wide[:, :PAIR] + wide[:, PAIR:] + mm(low, right_high)


def lane_iota(rows, columns):
    return lax.broadcasted_iota(jnp.int32, (rows, columns), 1)


def row_iota(rows, columns):
    return lax.broadcasted_iota(jnp.int32, (rows, columns), 0)


def order_matrix(start, rows, wide, to_scan):
    t = row_iota(rows, ROWS) + start
    small = (t & 256) + ((t & 15) << 4) + ((t & 255) >> 4)
    if to_scan:
        large = ((t & 15) << 5) + (t >> 4)
    else:
        large = ((t & 31) << 4) + (t >> 5)
    source = jnp.where(wide, large, small)
    return jnp.where(lane_iota(rows, ROWS) == source, 1.0, 0.0).astype(bf16)


def normalise(values):
    centred = values - jnp.mean(values, axis=-1, keepdims=True)
    rate = lax.rsqrt(jnp.mean(centred * centred, axis=-1, keepdims=True) + 1e-06)
    return centred * rate, rate


def normalise_back(normal, rate, grad):
    return rate * (
        grad
        - jnp.mean(grad, axis=-1, keepdims=True)
        - normal * jnp.mean(grad * normal, axis=-1, keepdims=True)
    )


class Common:
    def __init__(self, layer, refs):
        self.layouts, self.mod_mine, self.mod_other, small_mine, small_other, self.stream = refs
        self.section = lax.axis_index("section")
        self.own = self.section == layer
        self.layout = self.layouts[self.section, 0]
        self.wide = self.layout == 0
        self.live_rows = jnp.where(self.wide, ROWS, self.layout * HALF)
        small = jnp.where(self.own, small_mine[...], small_other[...])
        self.bu = small[0:1, :]
        self.bn = small[1:2, :D]
        self.ck = [small[2 + tap : 3 + tap, :D] for tap in range(3)]
        self.bd = small[5:6, :LANES]

    def slot(self, half):
        return jnp.where(self.wide, 0, half)

    def share(self, slot, part):
        row = pl.ds(2 * self.section + slot, 1)
        columns = slice(part * D, (part + 1) * D)
        return jnp.where(self.own, self.mod_mine[row, columns], self.mod_other[row, columns])

    def fetch_micro(self, array, kept, sem):
        source = array.at[self.section if array.shape[0] == MICRO else 0]
        copy = pltpu.make_async_copy(source, kept, sem)
        copy.start()
        return copy

    def fetch(self, mine, other, kept, sem):
        @pl.when(self.own)
        def _():
            pltpu.make_async_copy(mine, kept, sem).start()

        @pl.when(jnp.logical_not(self.own))
        def _():
            pltpu.make_async_copy(other, kept, sem).start()

        return pltpu.make_async_copy(mine, kept, sem)


def high_low(values):
    high, low = split(values)
    return high.astype(f32), low.astype(f32)


def sigmoid(values):
    return 1.0 / (1.0 + jnp.exp(-values))


GELU_A = 0.7978845608028654
GELU_B = 0.044715


def gelu_parts(values):
    square = values * values
    tanh = jnp.tanh(GELU_A * values * (1.0 + GELU_B * square))
    return square, tanh


def fill_bias(bias, wide):
    bias[:, :HALF] = jnp.full((HALF, HALF), 0.0, f32) + jnp.where(wide, 0.0, NEG)
    causal = row_iota(HALF, HALF) >= lane_iota(HALF, HALF)
    bias[:, HALF:] = jnp.where(causal, 0.0, NEG)


def decay_factors(cum, cumt, bias, head):
    row = cumt[pl.ds(head, 1), :]
    lanes = lane_iota(1, LANES)
    column = jnp.sum(jnp.where(lanes == head, cum[...], 0.0), axis=1, keepdims=True)
    first = jnp.exp(column[:HALF] - row[:, :HALF] + bias[:, HALF:])
    second = jnp.exp(column[HALF:] - row + bias[...])
    return first, second


def head_norm(values, lanes):
    square = values * values
    low = jnp.sum(jnp.where(lanes < HEAD_DIM, square, 0.0), axis=1, keepdims=True)
    high = jnp.sum(jnp.where(lanes < HEAD_DIM, 0.0, square), axis=1, keepdims=True)
    return jnp.where(lanes < HEAD_DIM, low, high) * (1.0 / HEAD_DIM)


def fill_decay(dp, bd, cum, cumt):
    raw = dp[...] + bd
    log_decay = (jnp.minimum(raw, 0.0) - jnp.log1p(jnp.exp(-jnp.abs(raw)))) * (1.0 / 16.0)
    high, middle, low = split_three(log_decay)
    causal = jnp.where(row_iota(ROWS, ROWS) >= lane_iota(ROWS, ROWS), 1.0, 0.0).astype(bf16)
    cum[...] = mm(causal, high) + mm(causal, middle) + mm(causal, low)
    cumt[...] = jnp.transpose(cum[...])


def columns(index, first=0):
    return pl.ds(pl.multiple_of(index * PAIR + first, PAIR), PAIR)


def attn_forward_kernel(
    layer,
    c0, c1, c2, c3, c4, c5, qko_mine, qko_other, vgd_mine, vgd_other,
    ordered, qkvg, dp, vc, cum, cumt, o, gated,
    x, inner, vpad, bias, w_qk, w_vgd, sems,
):
    flip = layer == 1
    c = Common(layer, (c0, c1, c2, c3, c4, c5))
    wide = c.wide
    wait_x = c.fetch_micro(c.stream, x, sems.at[0])
    wait_qk = c.fetch(qko_mine.at[:, : 2 * D], qko_other.at[:, : 2 * D], w_qk, sems.at[1])
    wait_vgd = c.fetch(vgd_mine, vgd_other, w_vgd, sems.at[2])
    wait_x.wait()

    def first(i, carry):
        rows = pl.ds(pl.multiple_of(i * HALF, HALF), HALF)
        slot = c.slot(i)
        normal, _ = normalise(x[rows, :].astype(f32))
        inner[rows, :] = (normal * (1.0 + c.share(slot, 1)) + c.share(slot, 0)).astype(bf16)
        return carry

    lax.fori_loop(0, 2, first, 0)
    wait_qk.wait()
    wait_vgd.wait()

    def project(i, carry):
        start = pl.multiple_of(i * HALF, HALF)
        rows = pl.ds(start, HALF)
        if flip:
            part = mm(order_matrix(start, HALF, wide, True), inner[...]).astype(bf16)
        else:
            part = inner[rows, :]
        ordered[rows, :] = part
        qkvg[rows, : 2 * D] = mm(part, w_qk[...])
        qkvg[rows, 2 * D :] = mm(part, w_vgd[:, : 2 * D])
        dp[rows, :] = mm(part, w_vgd[:, 2 * D :])
        return carry

    lax.fori_loop(0, 2, project, 0)
    fill_decay(dp, c.bd, cum, cumt)
    fill_bias(bias, wide)

    vpad[0:8, :] = jnp.zeros((8, D), f32)
    vpad[8 : 8 + ROWS, :] = qkvg[:, 2 * D : 3 * D]
    position = row_iota(ROWS, 1) & jnp.where(wide, ROWS - 1, HALF - 1)
    one = jnp.where(position >= 1, vpad[7 : 7 + ROWS, :], 0.0)
    two = jnp.where(position >= 2, vpad[6 : 6 + ROWS, :], 0.0)
    vc[...] = c.ck[0] * vpad[8 : 8 + ROWS, :] + c.ck[1] * one + c.ck[2] * two

    def pair(p, carry):
        lanes = lane_iota(1, PAIR)
        queries = cat_left(qkvg[:, columns(p)] * SCALE)
        keys = qkvg[:, columns(p, D)]
        value_high, value_low = split(vc[:, columns(p)])
        values = jnp.concatenate([value_high, value_low], axis=1)
        parts = []
        for e in range(2):
            key_cat = cat_right(jnp.where((lanes // HEAD_DIM) == e, keys, 0.0))
            first, second = decay_factors(cum, cumt, bias, 2 * p + e)
            first = first * mm_t(queries[:HALF], key_cat[:HALF])
            second = second * mm_t(queries[HALF:], key_cat)
            parts.append(
                jnp.concatenate(
                    [
                        mm_near(first, values[:HALF], value_high[:HALF]),
                        mm_near(second, values, value_high),
                    ],
                    axis=0,
                )
            )
        total = jnp.where(lanes < HEAD_DIM, parts[0], parts[1])
        o[:, columns(p)] = total
        gate = qkvg[:, columns(p, 3 * D)]
        normed = total * lax.rsqrt(head_norm(total, lanes) + 1.0)
        mixed = (normed * (gate * sigmoid(gate))).astype(bf16)
        if flip:
            inner[:, columns(p)] = mixed
        else:
            gated[:, columns(p)] = mixed
        return carry

    lax.fori_loop(0, PAIRS, pair, 0)
    if flip:

        def back(i, carry):
            start = pl.multiple_of(i * HALF, HALF)
            gated[pl.ds(start, HALF), :] = mm(
                order_matrix(start, HALF, wide, False), inner[...]
            ).astype(bf16)
            return carry

        lax.fori_loop(0, 2, back, 0)


def ffn_forward_kernel(
    layer,
    c0, c1, c2, c3, c4, gated, c5, qko_mine, qko_other, up_mine, up_other, down_mine, down_other,
    out, branch, down,
    x, wo, wu, wn, sems,
):
    c = Common(layer, (c0, c1, c2, c3, c4, c5))
    waits = [
        c.fetch_micro(c.stream, x, sems.at[0]),
        c.fetch(qko_mine.at[:, 2 * D :], qko_other.at[:, 2 * D :], wo, sems.at[1]),
        c.fetch(up_mine, up_other, wu, sems.at[2]),
        c.fetch(down_mine, down_other, wn, sems.at[3]),
    ]
    for wait in waits:
        wait.wait()

    def tile(i, carry):
        start = pl.multiple_of(i * HALF, HALF)
        rows = pl.ds(start, HALF)
        slot = c.slot(i)
        grown = mm(gated[rows, :], wo[...])
        branch[rows, :] = grown
        middle = x[rows, :].astype(f32) + c.share(slot, 2) * grown
        normal, _ = normalise(middle)
        inner = (normal * (1.0 + c.share(slot, 4)) + c.share(slot, 3)).astype(bf16)
        up = mm(inner, wu[...]) + c.bu
        _, tanh = gelu_parts(up)
        hidden = (0.5 * up * (1.0 + tanh)).astype(bf16)
        low = mm(hidden, wn[...])
        down[rows, :] = low
        result = middle + c.share(slot, 5) * (low + c.bn)
        live = (row_iota(HALF, 1) + start) < c.live_rows
        out[rows, :] = jnp.where(live, result, 0.0).astype(bf16)
        return carry

    lax.fori_loop(0, 2, tile, 0)


def ffn_backward_kernel(
    layer,
    c0, c1, c2, c3, c4, gated, branch, down,
    c5, above_in, up_mine, up_other, down_mine, down_other,
    mid_grad, branch_low, gwo, gwu_keep, gwu_send, gwn, small,
    x, grad, hidden_s, inner_s, up_s, down_s, gmod, gbu, gbn, wu, wn, sems,
):
    c = Common(layer, (c0, c1, c2, c3, c4, c5))
    waits = [
        c.fetch_micro(c.stream, x, sems.at[0]),
        c.fetch_micro(above_in, grad, sems.at[1]),
        c.fetch(up_mine, up_other, wu, sems.at[2]),
        c.fetch(down_mine, down_other, wn, sems.at[3]),
    ]
    gmod[...] = jnp.zeros(gmod.shape, f32)
    gbu[...] = jnp.zeros(gbu.shape, f32)
    gbn[...] = jnp.zeros(gbn.shape, f32)
    for wait in waits:
        wait.wait()

    def tile(i, carry):
        start = pl.multiple_of(i * HALF, HALF)
        rows = pl.ds(start, HALF)
        slot = c.slot(i)

        def add(part, values):
            where = (pl.ds(slot, 1), slice((part - 2) * D, (part - 1) * D))
            gmod[where] = gmod[where] + jnp.sum(values, axis=0, keepdims=True)

        grown = branch[rows, :]
        middle = x[rows, :].astype(f32) + c.share(slot, 2) * grown
        normal, rate = normalise(middle)
        inner = (normal * (1.0 + c.share(slot, 4)) + c.share(slot, 3)).astype(bf16)
        inner_s[rows, :] = inner
        live = (row_iota(HALF, 1) + start) < c.live_rows
        above = jnp.where(live, grad[rows, :].astype(f32), 0.0)
        add(5, above * (down[rows, :] + c.bn))
        grad_down = above * c.share(slot, 5)
        gbn[...] = gbn[...] + jnp.sum(grad_down, axis=0, keepdims=True)
        down_low = grad_down.astype(bf16)
        down_s[rows, :] = down_low
        up = mm(inner, wu[...]) + c.bu
        square, tanh = gelu_parts(up)
        half = 0.5 * (1.0 + tanh)
        hidden_s[rows, :] = (up * half).astype(bf16)
        slope = half + 0.5 * up * (1.0 - tanh * tanh) * (
            GELU_A * (1.0 + 3.0 * GELU_B * square)
        )
        grad_up = mm_t(down_low, wn[...]) * slope
        gbu[...] = gbu[...] + jnp.sum(grad_up, axis=0, keepdims=True)
        up_low = grad_up.astype(bf16)
        up_s[rows, :] = up_low
        grad_inner = mm_t(up_low, wu[...])
        add(3, grad_inner)
        add(4, grad_inner * normal)
        grad_middle = above + normalise_back(
            normal, rate, grad_inner * (1.0 + c.share(slot, 4))
        )
        mid_grad[rows, :] = grad_middle
        add(2, grad_middle * grown)
        branch_low[rows, :] = (grad_middle * c.share(slot, 2)).astype(bf16)
        return carry

    lax.fori_loop(0, 2, tile, 0)

    inner_t = jnp.transpose(inner_s[...].astype(f32)).astype(bf16)
    gwo[...] = mm(jnp.transpose(gated[...].astype(f32)).astype(bf16), branch_low[...])

    def weights(j, carry):
        part = pl.ds(pl.multiple_of(j * HALF, HALF), HALF)
        hidden_t = jnp.transpose(hidden_s[:, part].astype(f32)).astype(bf16)
        gwn[part, :] = mm(hidden_t, down_s[...])
        return carry

    lax.fori_loop(0, FF // HALF, weights, 0)

    def halves(j, carry):
        here = pl.ds(pl.multiple_of(j * HALF, HALF), HALF)
        keep = pl.ds(pl.multiple_of(j * HALF + c.section * (FF // 2), HALF), HALF)
        send = pl.ds(pl.multiple_of(j * HALF + (1 - c.section) * (FF // 2), HALF), HALF)
        gwu_keep[:, here] = mm(inner_t, up_s[:, keep])
        gwu_send[:, here] = mm(inner_t, up_s[:, send]).astype(bf16)
        return carry

    lax.fori_loop(0, FF // 2 // HALF, halves, 0)

    total = high_low(gmod[0:1, :] + gmod[1:2, :])
    short = high_low(jnp.concatenate([gbn[...], jnp.zeros((1, FF - D), f32)], axis=1))
    small[...] = jnp.concatenate(
        [gmod[0:SLOTS, :], *total, *high_low(gbu[...]), *short], axis=0
    ).astype(bf16)


def attn_backward_kernel(
    layer,
    c0, c1, c2, c3, c4, ordered, qkvg, dp, vc, cum, cumt, o, branch_low, mid_grad, gwo,
    c5, qko_mine, qko_other, vgd_mine, vgd_other,
    gx, gx_low, gw_keep, gw_send, small,
    x, mixed_s, low_s, dv_s, rows_s, cols_s, bias, perm_s, gmod, gw, w_qko, w_vgd, sems,
):
    flip = layer == 1
    c = Common(layer, (c0, c1, c2, c3, c4, c5))
    wide = c.wide
    wait_x = c.fetch_micro(c.stream, x, sems.at[0])
    wait_qko = c.fetch(qko_mine, qko_other, w_qko, sems.at[1])
    wait_vgd = c.fetch(vgd_mine, vgd_other, w_vgd, sems.at[2])
    fill_bias(bias, wide)
    wait_x.wait()
    wait_qko.wait()
    wait_vgd.wait()

    def first(i, carry):
        start = pl.multiple_of(i * HALF, HALF)
        rows = pl.ds(start, HALF)
        if flip:
            part = mm(order_matrix(start, HALF, wide, True), branch_low[...]).astype(bf16)
        else:
            part = branch_low[rows, :]
        mixed_s[rows, :] = mm_t(part, w_qko[:, 2 * D :])
        return carry

    lax.fori_loop(0, 2, first, 0)
    rows_s[...] = jnp.zeros(rows_s.shape, f32)
    cols_s[...] = jnp.zeros(cols_s.shape, f32)

    def pair(p, carry):
        lanes = lane_iota(1, PAIR)
        total = o[:, columns(p)]
        gate = qkvg[:, columns(p, 3 * D)]
        above = mixed_s[:, columns(p)]
        rate = lax.rsqrt(head_norm(total, lanes) + 1.0)
        sig = sigmoid(gate)
        grad_gate = above * (total * rate) * (sig * (1.0 + gate * (1.0 - sig)))
        low_s[:, columns(p, 3 * D)] = grad_gate.astype(bf16)
        grad_normed = above * (gate * sig)
        product = grad_normed * total
        inside = jnp.where(
            lanes < HEAD_DIM,
            jnp.sum(jnp.where(lanes < HEAD_DIM, product, 0.0), axis=1, keepdims=True),
            jnp.sum(jnp.where(lanes < HEAD_DIM, 0.0, product), axis=1, keepdims=True),
        ) * (1.0 / HEAD_DIM)
        grad_o = rate * grad_normed - total * (rate * rate * rate) * inside

        queries = qkvg[:, columns(p)] * SCALE
        keys = qkvg[:, columns(p, D)]
        values = vc[:, columns(p)]
        query_cat = cat_left(queries)
        grad_cat = cat_left(grad_o)
        key_high, key_low = split(keys)
        key_pair = jnp.concatenate([key_high, key_low], axis=1)
        query_t = jnp.transpose(queries)
        grad_t = jnp.transpose(grad_o)
        grad_q = []
        grad_k = []
        grad_v = []
        for e in range(2):
            mine = (lanes // HEAD_DIM) == e
            head = 2 * p + e
            key_cat = cat_right(jnp.where(mine, keys, 0.0))
            value_cat = cat_right(jnp.where(mine, values, 0.0))
            first, second = decay_factors(cum, cumt, bias, head)
            raw_first = mm_t(query_cat[:HALF], key_cat[:HALF])
            raw_second = mm_t(query_cat[HALF:], key_cat)
            grad_first = first * mm_t(grad_cat[:HALF], value_cat[:HALF])
            grad_second = second * mm_t(grad_cat[HALF:], value_cat)
            score_first = raw_first * first
            score_second = raw_second * second
            pull_first = grad_first * raw_first
            pull_second = grad_second * raw_second
            here = lanes == head
            rows_s[:HALF, :] = rows_s[:HALF, :] + jnp.where(
                here, jnp.sum(pull_first, axis=1, keepdims=True), 0.0
            )
            rows_s[HALF:, :] = rows_s[HALF:, :] + jnp.where(
                here, jnp.sum(pull_second, axis=1, keepdims=True), 0.0
            )
            low_cols = jnp.sum(pull_second, axis=0, keepdims=True)
            cols_s[pl.ds(head, 1), :HALF] = low_cols[:, :HALF] + jnp.sum(
                pull_first, axis=0, keepdims=True
            )
            cols_s[pl.ds(head, 1), HALF:] = low_cols[:, HALF:]
            grad_q.append(
                jnp.concatenate(
                    [
                        mm_near(grad_first, key_pair[:HALF], key_high[:HALF]),
                        mm_near(grad_second, key_pair, key_high),
                    ],
                    axis=0,
                )
            )

            def turned(source_t, block_first, block_second):
                high, low = split(source_t[e * HEAD_DIM : (e + 1) * HEAD_DIM, :])
                both = jnp.concatenate([high, low], axis=0)
                first_high, first_low = split(block_first)
                second_high, second_low = split(block_second)
                one = mm(both[:, :HALF], first_high)
                one = one[:HEAD_DIM] + one[HEAD_DIM:] + mm(high[:, :HALF], first_low)
                two = mm(both[:, HALF:], second_high)
                two = two[:HEAD_DIM] + two[HEAD_DIM:] + mm(high[:, HALF:], second_low)
                return jnp.concatenate([two[:, :HALF] + one, two[:, HALF:]], axis=1)

            grad_k.append(turned(query_t, grad_first, grad_second))
            grad_v.append(turned(grad_t, score_first, score_second))
        query_grad = jnp.where(lanes < HEAD_DIM, grad_q[0], grad_q[1]) * SCALE
        low_s[:, columns(p)] = query_grad.astype(bf16)
        low_s[:, columns(p, D)] = jnp.transpose(jnp.concatenate(grad_k, axis=0)).astype(bf16)
        dv_s[:ROWS, columns(p)] = jnp.transpose(jnp.concatenate(grad_v, axis=0))
        return carry

    lax.fori_loop(0, PAIRS, pair, 0)

    pulled = rows_s[...] - jnp.transpose(cols_s[...])
    high, middle, low = split_three(pulled)
    upper_first = jnp.concatenate(
        [
            jnp.where(row_iota(HALF, HALF) <= lane_iota(HALF, HALF), 1.0, 0.0),
            jnp.full((HALF, HALF), 0.0, f32) + jnp.where(wide, 1.0, 0.0),
        ],
        axis=1,
    ).astype(bf16)
    upper_second = upper_first[:, :HALF]
    later = jnp.concatenate(
        [
            mm(upper_first, high) + mm(upper_first, middle) + mm(upper_first, low),
            mm(upper_second, high[HALF:]) + mm(upper_second, middle[HALF:])
            + mm(upper_second, low[HALF:]),
        ],
        axis=0,
    )
    grad_dp = later * (1.0 / 16.0) * sigmoid(-(dp[...] + c.bd))
    grad_bd = jnp.sum(grad_dp, axis=0, keepdims=True)
    low_s[:, QKVG:] = grad_dp.astype(bf16)

    dv_s[ROWS:, :] = jnp.zeros((8, D), f32)
    position = row_iota(ROWS, 1) & jnp.where(wide, ROWS - 1, HALF - 1)
    last = jnp.where(wide, ROWS - 1, HALF - 1)
    here = dv_s[0:ROWS, :]
    one = jnp.where(position <= last - 1, dv_s[1 : 1 + ROWS, :], 0.0)
    two = jnp.where(position <= last - 2, dv_s[2 : 2 + ROWS, :], 0.0)
    value = qkvg[:, 2 * D : 3 * D]
    low_s[:, 2 * D : 3 * D] = (c.ck[0] * here + c.ck[1] * one + c.ck[2] * two).astype(bf16)
    grad_ck = [jnp.sum(rows * value, axis=0, keepdims=True) for rows in (here, one, two)]

    ordered_t = jnp.transpose(ordered[...].astype(f32)).astype(bf16)

    def weights(j, carry):
        part = pl.ds(pl.multiple_of(j * HALF, HALF), HALF)
        gw[:, part] = mm(ordered_t, low_s[:, part])
        return carry

    lax.fori_loop(0, QKVG // HALF, weights, 0)
    gw[:, QKVG : QKVG + D] = gwo[...]
    gw[:, QKVG + D :] = mm(ordered_t, low_s[:, QKVG:])

    def halves(j, carry):
        here = pl.ds(pl.multiple_of(j * HALF, HALF), HALF)
        gw_keep[:, here] = gw[:, pl.ds(pl.multiple_of(j * HALF + c.section * GROUP, HALF), HALF)]
        send = gw[:, pl.ds(pl.multiple_of(j * HALF + (1 - c.section) * GROUP, HALF), HALF)]
        gw_send[:, here] = send.astype(bf16)
        return carry

    lax.fori_loop(0, GROUP // HALF, halves, 0)

    def inner_grad(i, carry):
        rows = pl.ds(pl.multiple_of(i * HALF, HALF), HALF)
        mixed_s[rows, :] = mm_t(low_s[rows, : 2 * D], w_qko[:, : 2 * D]) + mm_t(
            low_s[rows, 2 * D :], w_vgd[...]
        )
        return carry

    lax.fori_loop(0, 2, inner_grad, 0)
    gmod[...] = jnp.zeros(gmod.shape, f32)
    if flip:
        high, middle, low = split_three(mixed_s[...])
        perm_s[:, :D] = high
        perm_s[:, D : 2 * D] = middle
        perm_s[:, 2 * D :] = low

    def tile(i, carry):
        start = pl.multiple_of(i * HALF, HALF)
        rows = pl.ds(start, HALF)
        slot = c.slot(i)
        if flip:
            three = mm(order_matrix(start, HALF, wide, False), perm_s[...])
            grad = three[:, :D] + three[:, D : 2 * D] + three[:, 2 * D :]
        else:
            grad = mixed_s[rows, :]
        normal, rate = normalise(x[rows, :].astype(f32))
        where = (pl.ds(slot, 1), slice(0, D))
        gmod[where] = gmod[where] + jnp.sum(grad, axis=0, keepdims=True)
        where = (pl.ds(slot, 1), slice(D, 2 * D))
        gmod[where] = gmod[where] + jnp.sum(grad * normal, axis=0, keepdims=True)
        total = mid_grad[rows, :] + normalise_back(normal, rate, grad * (1.0 + c.share(slot, 1)))
        gx[rows, :] = total
        gx_low[rows, :] = total.astype(bf16)
        return carry

    lax.fori_loop(0, 2, tile, 0)

    total = high_low(gmod[0:1, :] + gmod[1:2, :])
    taps = high_low(jnp.concatenate(grad_ck[:2], axis=1))
    rest = high_low(
        jnp.concatenate([grad_ck[2], grad_bd, jnp.zeros((1, D - LANES), f32)], axis=1)
    )
    small[...] = jnp.concatenate(
        [gmod[0:SLOTS, :], *total, taps[0], rest[0], taps[1], rest[1]], axis=0
    ).astype(bf16)


ANY = pl.BlockSpec(memory_space=pl.ANY)
VMEM = pl.BlockSpec(memory_space=pltpu.VMEM)


def call(kernel, common, operands, weights, outs, scratch, flops):
    *common, stream = common
    shapes = [jax.ShapeDtypeStruct(shape, kind) for shape, kind in outs]
    return pl.pallas_call(
        kernel,
        out_shape=shapes,
        in_specs=[pl.BlockSpec(memory_space=pltpu.SMEM)]
        + [VMEM] * (len(common) - 1 + len(operands))
        + [ANY] * (1 + len(weights)),
        out_specs=[VMEM] * len(shapes),
        scratch_shapes=[pltpu.VMEM(shape, kind) for shape, kind in scratch]
        + [pltpu.SemaphoreType.DMA((4,))],
        compiler_params=pltpu.CompilerParams(vmem_limit_bytes=36 * 1024 * 1024),
        cost_estimate=pl.CostEstimate(flops=flops, bytes_accessed=8 << 20, transcendentals=0),
    )(*common, *operands, stream, *weights)


def attn_forward(layer, common, qko, vgd):
    return call(
        functools.partial(attn_forward_kernel, layer),
        common,
        (),
        (*qko, *vgd),
        [
            ((ROWS, D), bf16),
            ((ROWS, QKVG), f32),
            ((ROWS, LANES), f32),
            ((ROWS, D), f32),
            ((ROWS, LANES), f32),
            ((LANES, ROWS), f32),
            ((ROWS, D), f32),
            ((ROWS, D), bf16),
        ],
        [
            ((ROWS, D), bf16),
            ((ROWS, D), bf16),
            ((ROWS + 8, D), f32),
            ((HALF, ROWS), f32),
            ((D, 2 * D), bf16),
            ((D, 2 * D + LANES), bf16),
        ],
        8 * 10**9,
    )


def ffn_forward(layer, common, gated, qko, up, down):
    return call(
        functools.partial(ffn_forward_kernel, layer),
        common,
        (gated,),
        (*qko, *up, *down),
        [((ROWS, D), bf16), ((ROWS, D), f32), ((ROWS, D), f32)],
        [((ROWS, D), bf16), ((D, D), bf16), ((D, FF), bf16), ((FF, D), bf16)],
        5 * 10**9,
    )


def ffn_backward(layer, common, gated, branch, down_raw, grad, up, down):
    return call(
        functools.partial(ffn_backward_kernel, layer),
        common,
        (gated, branch, down_raw),
        (grad, *up, *down),
        [
            ((ROWS, D), f32),
            ((ROWS, D), bf16),
            ((D, D), f32),
            ((D, FF // 2), f32),
            ((D, FF // 2), bf16),
            ((FF, D), f32),
            ((8, 4 * D), bf16),
        ],
        [
            ((ROWS, D), bf16),
            ((ROWS, D), bf16),
            ((ROWS, FF), bf16),
            ((ROWS, D), bf16),
            ((ROWS, FF), bf16),
            ((ROWS, D), bf16),
            ((8, 4 * D), f32),
            ((1, FF), f32),
            ((1, D), f32),
            ((D, FF), bf16),
            ((FF, D), bf16),
        ],
        12 * 10**9,
    )


def attn_backward(layer, common, saved, branch_low, mid_grad, gwo, qko, vgd):
    return call(
        functools.partial(attn_backward_kernel, layer),
        common,
        (*saved, branch_low, mid_grad, gwo),
        (*qko, *vgd),
        [
            ((ROWS, D), f32),
            ((ROWS, D), bf16),
            ((D, GROUP), f32),
            ((D, GROUP), bf16),
            ((8, 2 * D), bf16),
        ],
        [
            ((ROWS, D), bf16),
            ((ROWS, D), f32),
            ((ROWS, QKVG + LANES), bf16),
            ((ROWS + 8, D), f32),
            ((ROWS, LANES), f32),
            ((LANES, ROWS), f32),
            ((HALF, ROWS), f32),
            ((ROWS, 3 * D), bf16),
            ((8, 2 * D), f32),
            ((D, 2 * GROUP), f32),
            ((D, 3 * D), bf16),
            ((D, 2 * D + LANES), bf16),
        ],
        18 * 10**9,
    )


def small_kernel(b_up, b_down, taps, b_decay, packed):
    packed[...] = jnp.zeros(packed.shape, f32)
    packed[0:1, :] = b_up[...]
    packed[1:2, :D] = b_down[...]
    packed[2:5, :D] = taps[0]
    packed[5:6, :HEADS] = b_decay[...]


def pack_small(b_up, b_down, taps, b_decay):
    return pl.pallas_call(
        small_kernel,
        out_shape=jax.ShapeDtypeStruct((8, FF), f32),
        in_specs=[VMEM] * 4,
        out_specs=VMEM,
    )(b_up, b_down, taps, b_decay)


def pack_kernel(*refs):
    packed = refs[-1]
    at = 0
    for ref in refs[:-1]:
        width = ref.shape[1]
        if width % LANES:
            packed[:, at:] = jnp.zeros((packed.shape[0], packed.shape[1] - at), packed.dtype)
        packed[:, at : at + width] = ref[...]
        at += width


def pack(*arrays):
    total = sum(-(-array.shape[1] // LANES) * LANES for array in arrays)
    return pl.pallas_call(
        pack_kernel,
        out_shape=jax.ShapeDtypeStruct((arrays[0].shape[0], total), arrays[0].dtype),
        in_specs=[VMEM] * len(arrays),
        out_specs=VMEM,
    )(*arrays)


def swap(values):
    return lax.ppermute(values, "section", [(0, 1), (1, 0)])


def row_bits():
    bits = lax.axis_size("row").bit_length() - 1
    third = bits // 3
    return (
        tuple(range(third)),
        tuple(range(third, 2 * third)),
        tuple(range(2 * third, bits)),
    )


def partner(values, bit):
    size = lax.axis_size("row")
    return lax.ppermute(values, "row", [(i, i ^ (1 << bit)) for i in range(size)])


def double(held, bit):
    bits = lax.axis_size("row").bit_length() - 1
    same = ((lax.axis_index("row") >> bit) & 1) == 0
    other = partner(held, bit)
    axis = bits - 1 - bit
    return jnp.where(
        same,
        jnp.concatenate([held, other], axis=axis),
        jnp.concatenate([other, held], axis=axis),
    )


def gather_pair(first, second):
    along_x, along_y, along_z = row_bits()
    bits = lax.axis_size("row").bit_length() - 1
    first = first.reshape((1,) * bits + first.shape)
    second = second.reshape((1,) * bits + second.shape)
    for bit in reversed(along_z):
        first, second = double(first, bit), double(second, bit)
    for bit in along_x + along_y:
        first = double(first, bit)
    for bit in along_y + along_x:
        second = double(second, bit)
    return first.reshape((-1,) + first.shape[bits:]), second.reshape((-1,) + second.shape[bits:])


def exchange(values):
    return lax.all_to_all(values, "row", 0, 0, tiled=True)


def gather_small(values):
    return exchange(jnp.broadcast_to(values[None], (lax.axis_size("row"),) + values.shape))


def scatter_rows(values):
    return jnp.sum(exchange(values).astype(f32), axis=0)


def on_device(
    tokens, conditions, output_grad, layouts,
    w_ada, b_ada, w_query, w_key, w_value, w_gate, w_out, w_decay, b_decay, conv_kernel,
    w_up, b_up, w_down, b_down,
):
    section = lax.axis_index("section")
    devices = lax.axis_size("row")
    is_first = section == 0
    shard = w_query.shape[1]
    def pick(pair):
        return jnp.where(is_first, pair[0], pair[1])

    def pick_other(pair):
        return jnp.where(is_first, pair[1], pair[0])

    def both(values):
        return values, swap(values)

    qko_shard = pack(w_query[0], w_key[0], w_out[0])
    vgd_shard = pack(w_value[0], w_gate[0], w_decay[0])
    qko_shard, vgd_shard, conditions = lax.optimization_barrier(
        (qko_shard, vgd_shard, conditions)
    )
    qko_all, vgd_all = gather_pair(qko_shard, vgd_shard)
    qko = both(qko_all.reshape(D, 3 * D))
    vgd = both(vgd_all.reshape(D, 2 * D + LANES))
    up_all, down_all = gather_pair(w_up[0], w_down[0])
    up = both(up_all.reshape(D, FF))
    down = both(down_all.reshape(FF, D))

    lifted_own = jax.nn.silu(conditions.astype(f32)).astype(bf16)
    lifted_parts = lifted_own.reshape(MICRO * SLOTS, devices, shard).swapaxes(0, 1)
    lifted_cut = exchange(lifted_parts)
    terms = mm(lifted_cut.reshape(devices * MICRO * SLOTS, shard), w_ada[0])
    mods = both(scatter_rows(terms.reshape(devices, MICRO * SLOTS, 6 * D)) + b_ada[0])

    smalls = both(pack_small(b_up, b_down, conv_kernel, b_decay))

    x = tokens
    kept = []
    acts = []
    for l in range(2):
        common = (layouts, *mods, *smalls, x)
        *saved, gated = attn_forward(l, common, qko, vgd)
        out, branch, down_raw = ffn_forward(l, common, gated, qko, up, down)
        kept.append((common, saved, gated, branch, down_raw))
        acts.append(out)
        x = out[None]

    late, _ = lax.optimization_barrier((w_ada[0], acts[0]))
    ada_all = lax.all_gather(late, "row", axis=0, tiled=True)

    def ffn_terms(gwu_keep, gwu_send, gwn, small):
        up_half = gwu_keep + swap(gwu_send).astype(f32)
        pair = gwn.reshape(devices, 2, FF // devices // 2, D)
        down_half = lax.dynamic_index_in_dim(pair, section, 1, keepdims=False) + swap(
            lax.dynamic_index_in_dim(pair, 1 - section, 1, keepdims=False).astype(bf16)
        ).astype(f32)
        return jnp.concatenate(
            [
                up_half.reshape(devices, shard, FF // 2).astype(bf16),
                down_half[:, :shard].astype(bf16),
                down_half[:, shard:].astype(bf16),
                jnp.broadcast_to(small.reshape(1, shard, -1), (devices, shard, small.size // shard)),
            ],
            axis=2,
        )

    def attn_terms(gw_keep, gw_send, small):
        half = gw_keep + swap(gw_send).astype(f32)
        return jnp.concatenate(
            [
                half.reshape(devices, shard, GROUP).astype(bf16),
                jnp.broadcast_to(small.reshape(1, shard, -1), (devices, shard, small.size // shard)),
            ],
            axis=2,
        )

    def ffn_step(l, grad, *wait):
        common, saved, gated, branch, down_raw = kept[l]
        grad, *done = lax.optimization_barrier((grad, *wait))
        mid_grad, branch_low, gwo, *terms, small = ffn_backward(
            l, common, gated, branch, down_raw, grad, up, down
        )
        return (branch_low, mid_grad, gwo), ffn_terms(*terms, small), small, done

    def attn_step(l, carried, *wait):
        common, saved, gated, branch, down_raw = kept[l]
        carried, *done = lax.optimization_barrier((carried, *wait))
        gx, gx_low, *terms, small = attn_backward(l, common, saved, *carried, qko, vgd)
        return gx, gx_low, attn_terms(*terms, small), small, done

    carried, ffn_two, ffn_small_two, _ = ffn_step(1, output_grad)
    gx_two, gx_low, attn_two, attn_small_two, (ffn_two,) = attn_step(1, carried, ffn_two)
    ffn_two = exchange(ffn_two)
    carried, ffn_one, ffn_small_one, (attn_two, ffn_two) = ffn_step(
        0, gx_low[None], attn_two, ffn_two
    )
    attn_two = exchange(attn_two)
    gx_one, _, attn_one, attn_small_one, (ffn_one, attn_two, ada_all) = attn_step(
        0, carried, ffn_one, attn_two, ada_all
    )
    ffn_one = exchange(ffn_one)
    attn_one = exchange(attn_one)

    lifted_mine = lax.dynamic_slice_in_dim(lifted_cut, section * SLOTS, SLOTS, 1)
    lifted_mine = lifted_mine.reshape(devices * SLOTS, shard)

    def summed(ffn_all, attn_all):
        ffn_sum = jnp.sum(ffn_all[:, :, :FF].astype(f32), axis=0)
        attn_sum = jnp.sum(attn_all[:, :, :GROUP].astype(f32), axis=0)
        ffn_small = ffn_all[:, :, FF:].reshape(devices, 8, 4 * D)
        attn_small = attn_all[:, :, GROUP:].reshape(devices, 8, 2 * D)
        mod_low = jnp.concatenate([attn_small[:, :SLOTS], ffn_small[:, :SLOTS]], axis=2)
        ada = lax.dot_general(
            lifted_mine,
            mod_low.reshape(devices * SLOTS, 6 * D),
            (((0,), (0,)), ((), ())),
            preferred_element_type=f32,
        )
        ffn_small = jnp.sum(ffn_small[:, SLOTS:].astype(f32), axis=0)
        attn_small = jnp.sum(attn_small[:, SLOTS:].astype(f32), axis=0)
        return attn_sum, ffn_sum, ada, ffn_small, attn_small

    sums = (summed(ffn_one, attn_one), summed(ffn_two, attn_two))
    mine = [pick(pair) for pair in zip(*sums)]
    other = [swap(pick_other(pair)) for pair in zip(*sums)]

    def halves(number):
        return pick((mine[number], other[number])), pick_other((mine[number], other[number]))

    attn_total = jnp.concatenate(halves(0), axis=1)
    ffn_halves = halves(1)
    up_total = jnp.concatenate([half[:, : FF // 2] for half in ffn_halves], axis=1)
    down_total = jnp.concatenate(
        [half[:, at : at + D] for half in ffn_halves for at in (FF // 2, FF // 2 + D)], axis=0
    )
    grad_w_ada = mine[2] + other[2]
    ffn_small = mine[3] + other[3]
    ffn_small = ffn_small[0::2] + ffn_small[1::2]
    attn_small = mine[4] + other[4]
    grad_b_ada = jnp.concatenate([attn_small[0] + attn_small[1], ffn_small[0]])
    taps = attn_small[2:4] + attn_small[4:6]
    grad_conv = jnp.concatenate([taps[0], taps[1, :D]]).reshape(3, D)

    mod_low = [
        jnp.concatenate([attn[:SLOTS], ffn[:SLOTS]], axis=1)
        for attn, ffn in ((attn_small_one, ffn_small_one), (attn_small_two, ffn_small_two))
    ]
    mod_own = pick(mod_low)
    mod_other = swap(pick_other(mod_low))
    mod_both = jnp.concatenate([pick((mod_own, mod_other)), pick_other((mod_own, mod_other))])
    grad_lifted = mm_t(mod_both, ada_all)
    grad_lifted = (grad_lifted + swap(grad_lifted)).reshape(MICRO, SLOTS, D)
    _, pull_silu = jax.vjp(jax.nn.silu, conditions.astype(f32))
    (cond_grads,) = pull_silu(grad_lifted)

    def assembled(pair):
        mine = pick(pair)
        other = swap(pick_other(pair))
        return jnp.stack([pick((mine, other)), pick_other((mine, other))])

    return (
        assembled(acts)[None],
        assembled((gx_one, gx_two))[None],
        cond_grads,
        grad_w_ada[None],
        grad_b_ada[None],
        attn_total[None, :, :D],
        attn_total[None, :, D : 2 * D],
        attn_total[None, :, 2 * D : 3 * D],
        attn_total[None, :, 3 * D : 4 * D],
        attn_total[None, :, 4 * D : 5 * D],
        attn_total[None, :, 5 * D : 5 * D + HEADS],
        taps[None, 1, D : D + HEADS],
        grad_conv[None],
        up_total[None],
        ffn_small[1:2],
        down_total[None],
        ffn_small[2:3, :D],
    )


def solution(mesh):
    rows = P(None, "row", None)
    mats = P("section", "row", None)
    vector = P("section", None)
    in_specs = (
        rows, rows, rows, P(None, "row"),
        mats, vector, mats, mats, mats, mats, mats, mats, vector, P("section", None, None),
        mats, vector, mats, vector,
    )
    blocks = P("section", None, "row", None)
    out_specs = (
        blocks, blocks, rows,
        mats, vector, mats, mats, mats, mats, mats, mats, vector, P("section", None, None),
        mats, vector, mats, vector,
    )
    return jax.shard_map(
        on_device, mesh=mesh, in_specs=in_specs, out_specs=out_specs, check_vma=False
    )
```

```python
import functools

import jax
import jax.numpy as jnp
from jax import lax
from jax.experimental import pallas as pl
from jax.experimental.pallas import tpu as pltpu
from jax.sharding import PartitionSpec as P

D = 384
HEADS = 6
HEAD_DIM = 64
FF = 1536
MICRO = 2
ROWS = 512
HALF = 256
SLOTS = 2
PAIR = 128
PAIRS = D // PAIR
QKVG = 4 * D
LANES = 128
GROUP = (QKVG + D + LANES) // 2
NEG = -1e30
SCALE = HEAD_DIM**-0.5

bf16 = jnp.bfloat16
f32 = jnp.float32


def mm(left, right):
    return jnp.dot(left, right, preferred_element_type=f32)


def mm_t(left, right):
    return lax.dot_general(left, right, (((1,), (1,)), ((), ())), preferred_element_type=f32)


def split(values):
    high = values.astype(bf16)
    return high, (values - high.astype(f32)).astype(bf16)


def split_three(values):
    high, rest = split(values)
    mid = values - high.astype(f32)
    middle, low = split(mid)
    return high, middle, low


def cat_left(values):
    high, low = split(values)
    return jnp.concatenate([high, low, high], axis=1)


def cat_right(values):
    high, low = split(values)
    return jnp.concatenate([high, high, low], axis=1)


def mm_near(left, right_pair, right_high):
    high, low = split(left)
    wide = mm(high, right_pair)
    return wide[:, :PAIR] + wide[:, PAIR:] + mm(low, right_high)


def lane_iota(rows, columns):
    return lax.broadcasted_iota(jnp.int32, (rows, columns), 1)


def row_iota(rows, columns):
    return lax.broadcasted_iota(jnp.int32, (rows, columns), 0)


def order_matrix(start, rows, wide, to_scan):
    t = row_iota(rows, ROWS) + start
    small = (t & 256) + ((t & 15) << 4) + ((t & 255) >> 4)
    if to_scan:
        large = ((t & 15) << 5) + (t >> 4)
    else:
        large = ((t & 31) << 4) + (t >> 5)
    source = jnp.where(wide, large, small)
    return jnp.where(lane_iota(rows, ROWS) == source, 1.0, 0.0).astype(bf16)


def normalise(values):
    centred = values - jnp.mean(values, axis=-1, keepdims=True)
    rate = lax.rsqrt(jnp.mean(centred * centred, axis=-1, keepdims=True) + 1e-06)
    return centred * rate, rate


def normalise_back(normal, rate, grad):
    return rate * (
        grad
        - jnp.mean(grad, axis=-1, keepdims=True)
        - normal * jnp.mean(grad * normal, axis=-1, keepdims=True)
    )


class In:
    def __init__(self, copy, kept):
        self.copy = copy
        self.kept = kept

    def __call__(self):
        if self.copy is not None:
            self.copy.wait()
            self.copy = None
        return self.kept


class Kernel:
    def __init__(self, layer, layouts):
        self.layer = layer
        self.section = lax.axis_index("section")
        self.own = self.section == layer
        self.layout = layouts[self.section, 0]
        self.wide = self.layout == 0
        self.live_rows = jnp.where(self.wide, ROWS, self.layout * HALF)
        self.pushed = {}

    def load(self, kind, refs, kept, sem):
        if kind == "own":
            mine, other = refs

            @pl.when(self.own)
            def _():
                pltpu.make_async_copy(mine, kept, sem).start()

            @pl.when(jnp.logical_not(self.own))
            def _():
                pltpu.make_async_copy(other, kept, sem).start()

            return In(pltpu.make_async_copy(mine, kept, sem), kept)
        (source,) = refs
        if kind == "micro":
            source = source.at[self.section if source.shape[0] == MICRO else 0]
        copy = pltpu.make_async_copy(source, kept, sem)
        copy.start()
        return In(copy, kept)

    def push(self, name):
        kept, target, sem = self.results[name]
        copy = pltpu.make_async_copy(kept, target, sem)
        copy.start()
        self.pushed[name] = copy

    def finish(self):
        for name in self.results:
            if name not in self.pushed:
                self.push(name)
        for copy in self.pushed.values():
            copy.wait()

    def slot(self, half):
        return jnp.where(self.wide, 0, half)

    def share(self, slot, part):
        row = pl.ds(2 * self.section + slot, 1)
        return self.mods()[row, part * D : (part + 1) * D]

    def bu(self):
        return self.small()[0:1, :]

    def bn(self):
        return self.small()[1:2, :D]

    def ck(self, tap):
        return self.small()[2 + tap : 3 + tap, :D]

    def bd(self):
        return self.small()[5:6, :LANES]


def sigmoid(values):
    return 1.0 / (1.0 + jnp.exp(-values))


GELU_A = 0.7978845608028654
GELU_B = 0.044715


def gelu_parts(values):
    square = values * values
    tanh = jnp.tanh(GELU_A * values * (1.0 + GELU_B * square))
    return square, tanh


def fill_bias(bias, wide):
    bias[:, :HALF] = jnp.full((HALF, HALF), 0.0, f32) + jnp.where(wide, 0.0, NEG)
    causal = row_iota(HALF, HALF) >= lane_iota(HALF, HALF)
    bias[:, HALF:] = jnp.where(causal, 0.0, NEG)


def decay_factors(cum, cumt, bias, head):
    row = cumt[pl.ds(head, 1), :]
    lanes = lane_iota(1, LANES)
    column = jnp.sum(jnp.where(lanes == head, cum[...], 0.0), axis=1, keepdims=True)
    first = jnp.exp(column[:HALF] - row[:, :HALF] + bias[:, HALF:])
    second = jnp.exp(column[HALF:] - row + bias[...])
    return first, second


def head_norm(values, lanes):
    square = values * values
    low = jnp.sum(jnp.where(lanes < HEAD_DIM, square, 0.0), axis=1, keepdims=True)
    high = jnp.sum(jnp.where(lanes < HEAD_DIM, 0.0, square), axis=1, keepdims=True)
    return jnp.where(lanes < HEAD_DIM, low, high) * (1.0 / HEAD_DIM)


def fill_decay(dp, bd, cum, cumt):
    raw = dp[...] + bd
    log_decay = (jnp.minimum(raw, 0.0) - jnp.log1p(jnp.exp(-jnp.abs(raw)))) * (1.0 / 16.0)
    high, middle, low = split_three(log_decay)
    causal = jnp.where(row_iota(ROWS, ROWS) >= lane_iota(ROWS, ROWS), 1.0, 0.0).astype(bf16)
    cum[...] = mm(causal, high) + mm(causal, middle) + mm(causal, low)
    cumt[...] = jnp.transpose(cum[...])


def columns(index, first=0):
    return pl.ds(pl.multiple_of(index * PAIR + first, PAIR), PAIR)


def attn_forward_body(k):
    flip = k.layer == 1
    wide = k.wide
    x = k.x()
    k.mods()

    def first(i, carry):
        rows = pl.ds(pl.multiple_of(i * HALF, HALF), HALF)
        slot = k.slot(i)
        normal, _ = normalise(x[rows, :].astype(f32))
        k.inner[rows, :] = (normal * (1.0 + k.share(slot, 1)) + k.share(slot, 0)).astype(bf16)
        return carry

    lax.fori_loop(0, 2, first, 0)
    w_qk = k.w_qk()
    w_vgd = k.w_vgd()

    def project(i, carry):
        start = pl.multiple_of(i * HALF, HALF)
        rows = pl.ds(start, HALF)
        if flip:
            part = mm(order_matrix(start, HALF, wide, True), k.inner[...]).astype(bf16)
        else:
            part = k.inner[rows, :]
        k.ordered[rows, :] = part
        k.qkvg[rows, : 2 * D] = mm(part, w_qk[...])
        k.qkvg[rows, 2 * D :] = mm(part, w_vgd[:, : 2 * D])
        k.dp[rows, :] = mm(part, w_vgd[:, 2 * D :])
        return carry

    lax.fori_loop(0, 2, project, 0)
    k.small()
    for name in ("ordered", "qkvg", "dp"):
        k.push(name)
    fill_decay(k.dp, k.bd(), k.cum, k.cumt)
    fill_bias(k.bias, wide)

    vpad = k.vpad
    vpad[0:8, :] = jnp.zeros((8, D), f32)
    vpad[8 : 8 + ROWS, :] = k.qkvg[:, 2 * D : 3 * D]
    position = row_iota(ROWS, 1) & jnp.where(wide, ROWS - 1, HALF - 1)
    one = jnp.where(position >= 1, vpad[7 : 7 + ROWS, :], 0.0)
    two = jnp.where(position >= 2, vpad[6 : 6 + ROWS, :], 0.0)
    k.vc[...] = k.ck(0) * vpad[8 : 8 + ROWS, :] + k.ck(1) * one + k.ck(2) * two
    for name in ("cum", "cumt", "vc"):
        k.push(name)

    def pair(p, carry):
        lanes = lane_iota(1, PAIR)
        queries = cat_left(k.qkvg[:, columns(p)] * SCALE)
        keys = k.qkvg[:, columns(p, D)]
        value_high, value_low = split(k.vc[:, columns(p)])
        values = jnp.concatenate([value_high, value_low], axis=1)
        parts = []
        for e in range(2):
            key_cat = cat_right(jnp.where((lanes // HEAD_DIM) == e, keys, 0.0))
            first, second = decay_factors(k.cum, k.cumt, k.bias, 2 * p + e)
            first = first * mm_t(queries[:HALF], key_cat[:HALF])
            second = second * mm_t(queries[HALF:], key_cat)
            parts.append(
                jnp.concatenate(
                    [
                        mm_near(first, values[:HALF], value_high[:HALF]),
                        mm_near(second, values, value_high),
                    ],
                    axis=0,
                )
            )
        total = jnp.where(lanes < HEAD_DIM, parts[0], parts[1])
        k.o[:, columns(p)] = total
        gate = k.qkvg[:, columns(p, 3 * D)]
        normed = total * lax.rsqrt(head_norm(total, lanes) + 1.0)
        mixed = (normed * (gate * sigmoid(gate))).astype(bf16)
        if flip:
            k.inner[:, columns(p)] = mixed
        else:
            k.gated[:, columns(p)] = mixed
        return carry

    lax.fori_loop(0, PAIRS, pair, 0)
    k.push("o")
    if flip:

        def back(i, carry):
            start = pl.multiple_of(i * HALF, HALF)
            k.gated[pl.ds(start, HALF), :] = mm(
                order_matrix(start, HALF, wide, False), k.inner[...]
            ).astype(bf16)
            return carry

        lax.fori_loop(0, 2, back, 0)


def ffn_forward_body(k):
    gated, x, wo = k.gated(), k.x(), k.wo()
    k.mods(), k.small()
    wu, wn = k.wu(), k.wn()

    def tile(i, carry):
        start = pl.multiple_of(i * HALF, HALF)
        rows = pl.ds(start, HALF)
        slot = k.slot(i)
        grown = mm(gated[rows, :], wo[...])
        k.branch[rows, :] = grown
        middle = x[rows, :].astype(f32) + k.share(slot, 2) * grown
        normal, _ = normalise(middle)
        inner = (normal * (1.0 + k.share(slot, 4)) + k.share(slot, 3)).astype(bf16)
        up = mm(inner, wu[...]) + k.bu()
        _, tanh = gelu_parts(up)
        hidden = (0.5 * up * (1.0 + tanh)).astype(bf16)
        low = mm(hidden, wn[...])
        k.down[rows, :] = low
        result = middle + k.share(slot, 5) * (low + k.bn())
        live = (row_iota(HALF, 1) + start) < k.live_rows
        k.out[rows, :] = jnp.where(live, result, 0.0).astype(bf16)
        return carry

    lax.fori_loop(0, 2, tile, 0)


def ffn_backward_body(k):
    gmod, gbu, gbn = k.gmod, k.gbu, k.gbn
    gmod[...] = jnp.zeros(gmod.shape, f32)
    gbu[...] = jnp.zeros(gbu.shape, f32)
    gbn[...] = jnp.zeros(gbn.shape, f32)
    k.mods(), k.small()
    x, grad, branch, down = k.x(), k.grad(), k.branch(), k.down()
    wu, wn = k.wu(), k.wn()

    def tile(i, carry):
        start = pl.multiple_of(i * HALF, HALF)
        rows = pl.ds(start, HALF)
        slot = k.slot(i)

        def add(part, values):
            where = (pl.ds(slot, 1), slice((part - 2) * D, (part - 1) * D))
            gmod[where] = gmod[where] + jnp.sum(values, axis=0, keepdims=True)

        grown = branch[rows, :]
        middle = x[rows, :].astype(f32) + k.share(slot, 2) * grown
        normal, rate = normalise(middle)
        inner = (normal * (1.0 + k.share(slot, 4)) + k.share(slot, 3)).astype(bf16)
        k.inner_s[rows, :] = inner
        live = (row_iota(HALF, 1) + start) < k.live_rows
        above = jnp.where(live, grad[rows, :].astype(f32), 0.0)
        add(5, above * (down[rows, :] + k.bn()))
        grad_down = above * k.share(slot, 5)
        gbn[...] = gbn[...] + jnp.sum(grad_down, axis=0, keepdims=True)
        down_low = grad_down.astype(bf16)
        k.down_s[rows, :] = down_low
        up = mm(inner, wu[...]) + k.bu()
        square, tanh = gelu_parts(up)
        half = 0.5 * (1.0 + tanh)
        k.hidden_s[rows, :] = (up * half).astype(bf16)
        slope = half + 0.5 * up * (1.0 - tanh * tanh) * (
            GELU_A * (1.0 + 3.0 * GELU_B * square)
        )
        grad_up = mm_t(down_low, wn[...]) * slope
        gbu[...] = gbu[...] + jnp.sum(grad_up, axis=0, keepdims=True)
        up_low = grad_up.astype(bf16)
        k.up_s[rows, :] = up_low
        grad_inner = mm_t(up_low, wu[...])
        add(3, grad_inner)
        add(4, grad_inner * normal)
        grad_middle = above + normalise_back(
            normal, rate, grad_inner * (1.0 + k.share(slot, 4))
        )
        k.mid_grad[rows, :] = grad_middle
        add(2, grad_middle * grown)
        k.branch_low[rows, :] = (grad_middle * k.share(slot, 2)).astype(bf16)
        return carry

    lax.fori_loop(0, 2, tile, 0)
    k.push("mid_grad")
    k.push("branch_low")

    def weights(j, carry):
        part = pl.ds(pl.multiple_of(j * HALF, HALF), HALF)
        hidden_t = jnp.transpose(k.hidden_s[:, part].astype(f32)).astype(bf16)
        k.gwn[part, :] = mm(hidden_t, k.down_s[...])
        return carry

    lax.fori_loop(0, FF // HALF, weights, 0)
    k.push("gwn")
    inner_t = jnp.transpose(k.inner_s[...].astype(f32)).astype(bf16)

    def halves(j, carry):
        here = pl.ds(pl.multiple_of(j * HALF, HALF), HALF)
        keep = pl.ds(pl.multiple_of(j * HALF + k.section * (FF // 2), HALF), HALF)
        send = pl.ds(pl.multiple_of(j * HALF + (1 - k.section) * (FF // 2), HALF), HALF)
        k.gwu_keep[:, here] = mm(inner_t, k.up_s[:, keep])
        k.gwu_send[:, here] = mm(inner_t, k.up_s[:, send]).astype(bf16)
        return carry

    lax.fori_loop(0, FF // 2 // HALF, halves, 0)
    k.push("gwu_keep")
    k.push("gwu_send")
    gated = k.gated()
    k.gwo[...] = mm(jnp.transpose(gated[...].astype(f32)).astype(bf16), k.branch_low[...])

    short = jnp.concatenate([gbn[...], jnp.zeros((1, FF - D), f32)], axis=1)
    k.sums[...] = jnp.concatenate(
        [gmod[0:SLOTS, :], gbu[...], short, jnp.zeros((4, FF), f32)], axis=0
    )


def mixer_backward_body(k):
    flip = k.layer == 1
    wide = k.wide
    mixed_s, low, dv_s, rows_s, cols_s = k.mixed_s, k.low, k.dv_s, k.rows_s, k.cols_s
    fill_bias(k.bias, wide)
    branch_low, wo = k.branch_low(), k.wo()

    def first(i, carry):
        start = pl.multiple_of(i * HALF, HALF)
        rows = pl.ds(start, HALF)
        if flip:
            part = mm(order_matrix(start, HALF, wide, True), branch_low[...]).astype(bf16)
        else:
            part = branch_low[rows, :]
        mixed_s[rows, :] = mm_t(part, wo[...])
        return carry

    lax.fori_loop(0, 2, first, 0)
    rows_s[...] = jnp.zeros(rows_s.shape, f32)
    cols_s[...] = jnp.zeros(cols_s.shape, f32)
    qkvg, vc, cum, cumt, o = k.qkvg(), k.vc(), k.cum(), k.cumt(), k.o()
    k.small()

    def pair(p, carry):
        lanes = lane_iota(1, PAIR)
        total = o[:, columns(p)]
        gate = qkvg[:, columns(p, 3 * D)]
        above = mixed_s[:, columns(p)]
        rate = lax.rsqrt(head_norm(total, lanes) + 1.0)
        sig = sigmoid(gate)
        grad_gate = above * (total * rate) * (sig * (1.0 + gate * (1.0 - sig)))
        low[:, columns(p, 3 * D)] = grad_gate.astype(bf16)
        grad_normed = above * (gate * sig)
        product = grad_normed * total
        inside = jnp.where(
            lanes < HEAD_DIM,
            jnp.sum(jnp.where(lanes < HEAD_DIM, product, 0.0), axis=1, keepdims=True),
            jnp.sum(jnp.where(lanes < HEAD_DIM, 0.0, product), axis=1, keepdims=True),
        ) * (1.0 / HEAD_DIM)
        grad_o = rate * grad_normed - total * (rate * rate * rate) * inside

        queries = qkvg[:, columns(p)] * SCALE
        keys = qkvg[:, columns(p, D)]
        values = vc[:, columns(p)]
        query_cat = cat_left(queries)
        grad_cat = cat_left(grad_o)
        key_high, key_low = split(keys)
        key_pair = jnp.concatenate([key_high, key_low], axis=1)
        query_t = jnp.transpose(queries)
        grad_t = jnp.transpose(grad_o)
        grad_q = []
        grad_k = []
        grad_v = []
        for e in range(2):
            mine = (lanes // HEAD_DIM) == e
            head = 2 * p + e
            key_cat = cat_right(jnp.where(mine, keys, 0.0))
            value_cat = cat_right(jnp.where(mine, values, 0.0))
            first, second = decay_factors(cum, cumt, k.bias, head)
            raw_first = mm_t(query_cat[:HALF], key_cat[:HALF])
            raw_second = mm_t(query_cat[HALF:], key_cat)
            grad_first = first * mm_t(grad_cat[:HALF], value_cat[:HALF])
            grad_second = second * mm_t(grad_cat[HALF:], value_cat)
            score_first = raw_first * first
            score_second = raw_second * second
            pull_first = grad_first * raw_first
            pull_second = grad_second * raw_second
            here = lanes == head
            rows_s[:HALF, :] = rows_s[:HALF, :] + jnp.where(
                here, jnp.sum(pull_first, axis=1, keepdims=True), 0.0
            )
            rows_s[HALF:, :] = rows_s[HALF:, :] + jnp.where(
                here, jnp.sum(pull_second, axis=1, keepdims=True), 0.0
            )
            low_cols = jnp.sum(pull_second, axis=0, keepdims=True)
            cols_s[pl.ds(head, 1), :HALF] = low_cols[:, :HALF] + jnp.sum(
                pull_first, axis=0, keepdims=True
            )
            cols_s[pl.ds(head, 1), HALF:] = low_cols[:, HALF:]
            grad_q.append(
                jnp.concatenate(
                    [
                        mm_near(grad_first, key_pair[:HALF], key_high[:HALF]),
                        mm_near(grad_second, key_pair, key_high),
                    ],
                    axis=0,
                )
            )

            def turned(source_t, block_first, block_second):
                high, low = split(source_t[e * HEAD_DIM : (e + 1) * HEAD_DIM, :])
                both = jnp.concatenate([high, low], axis=0)
                first_high, first_low = split(block_first)
                second_high, second_low = split(block_second)
                one = mm(both[:, :HALF], first_high)
                one = one[:HEAD_DIM] + one[HEAD_DIM:] + mm(high[:, :HALF], first_low)
                two = mm(both[:, HALF:], second_high)
                two = two[:HEAD_DIM] + two[HEAD_DIM:] + mm(high[:, HALF:], second_low)
                return jnp.concatenate([two[:, :HALF] + one, two[:, HALF:]], axis=1)

            grad_k.append(turned(query_t, grad_first, grad_second))
            grad_v.append(turned(grad_t, score_first, score_second))
        query_grad = jnp.where(lanes < HEAD_DIM, grad_q[0], grad_q[1]) * SCALE
        low[:, columns(p)] = query_grad.astype(bf16)
        low[:, columns(p, D)] = jnp.transpose(jnp.concatenate(grad_k, axis=0)).astype(bf16)
        dv_s[:ROWS, columns(p)] = jnp.transpose(jnp.concatenate(grad_v, axis=0))
        return carry

    lax.fori_loop(0, PAIRS, pair, 0)

    pulled = rows_s[...] - jnp.transpose(cols_s[...])
    high, middle, rest = split_three(pulled)
    upper_first = jnp.concatenate(
        [
            jnp.where(row_iota(HALF, HALF) <= lane_iota(HALF, HALF), 1.0, 0.0),
            jnp.full((HALF, HALF), 0.0, f32) + jnp.where(wide, 1.0, 0.0),
        ],
        axis=1,
    ).astype(bf16)
    upper_second = upper_first[:, :HALF]
    later = jnp.concatenate(
        [
            mm(upper_first, high) + mm(upper_first, middle) + mm(upper_first, rest),
            mm(upper_second, high[HALF:]) + mm(upper_second, middle[HALF:])
            + mm(upper_second, rest[HALF:]),
        ],
        axis=0,
    )
    grad_dp = later * (1.0 / 16.0) * sigmoid(-(k.dp()[...] + k.bd()))
    grad_bd = jnp.sum(grad_dp, axis=0, keepdims=True)
    low[:, QKVG:] = grad_dp.astype(bf16)

    dv_s[ROWS:, :] = jnp.zeros((8, D), f32)
    position = row_iota(ROWS, 1) & jnp.where(wide, ROWS - 1, HALF - 1)
    last = jnp.where(wide, ROWS - 1, HALF - 1)
    here = dv_s[0:ROWS, :]
    one = jnp.where(position <= last - 1, dv_s[1 : 1 + ROWS, :], 0.0)
    two = jnp.where(position <= last - 2, dv_s[2 : 2 + ROWS, :], 0.0)
    value = qkvg[:, 2 * D : 3 * D]
    low[:, 2 * D : 3 * D] = (k.ck(0) * here + k.ck(1) * one + k.ck(2) * two).astype(bf16)
    k.push("low")

    taps = [jnp.sum(rows * value, axis=0, keepdims=True) for rows in (here, one, two)]
    rest = jnp.concatenate([grad_bd, jnp.zeros((1, D - LANES), f32)], axis=1)
    k.sums[...] = jnp.concatenate([*taps, rest, jnp.zeros((4, D), f32)], axis=0)

    ordered_t = jnp.transpose(k.ordered()[...].astype(f32)).astype(bf16)
    gwo = k.gwo()
    gw = k.gw

    def weights(j, carry):
        part = pl.ds(pl.multiple_of(j * HALF, HALF), HALF)
        gw[:, part] = mm(ordered_t, low[:, part])
        return carry

    lax.fori_loop(0, QKVG // HALF, weights, 0)
    gw[:, QKVG : QKVG + D] = gwo[...]
    gw[:, QKVG + D :] = mm(ordered_t, low[:, QKVG:])

    def halves(j, carry):
        here = pl.ds(pl.multiple_of(j * HALF, HALF), HALF)
        keep = pl.ds(pl.multiple_of(j * HALF + k.section * GROUP, HALF), HALF)
        send = pl.ds(pl.multiple_of(j * HALF + (1 - k.section) * GROUP, HALF), HALF)
        k.gw_keep[:, here] = gw[:, keep]
        k.gw_send[:, here] = gw[:, send].astype(bf16)
        return carry

    lax.fori_loop(0, GROUP // HALF, halves, 0)


def input_backward_body(k):
    flip = k.layer == 1
    wide = k.wide
    gmod, mixed_s, perm_s = k.gmod, k.mixed_s, k.perm_s
    gmod[...] = jnp.zeros(gmod.shape, f32)
    low, w_qk, w_vgd = k.low(), k.w_qk(), k.w_vgd()

    def inner_grad(i, carry):
        rows = pl.ds(pl.multiple_of(i * HALF, HALF), HALF)
        mixed_s[rows, :] = mm_t(low[rows, : 2 * D], w_qk[...]) + mm_t(
            low[rows, 2 * D :], w_vgd[...]
        )
        return carry

    lax.fori_loop(0, 2, inner_grad, 0)
    if flip:
        high, middle, rest = split_three(mixed_s[...])
        perm_s[:, :D] = high
        perm_s[:, D : 2 * D] = middle
        perm_s[:, 2 * D :] = rest
    x, mid_grad = k.x(), k.mid_grad()
    k.mods()

    def tile(i, carry):
        start = pl.multiple_of(i * HALF, HALF)
        rows = pl.ds(start, HALF)
        slot = k.slot(i)
        if flip:
            three = mm(order_matrix(start, HALF, wide, False), perm_s[...])
            grad = three[:, :D] + three[:, D : 2 * D] + three[:, 2 * D :]
        else:
            grad = mixed_s[rows, :]
        normal, rate = normalise(x[rows, :].astype(f32))
        where = (pl.ds(slot, 1), slice(0, D))
        gmod[where] = gmod[where] + jnp.sum(grad, axis=0, keepdims=True)
        where = (pl.ds(slot, 1), slice(D, 2 * D))
        gmod[where] = gmod[where] + jnp.sum(grad * normal, axis=0, keepdims=True)
        total = mid_grad[rows, :] + normalise_back(normal, rate, grad * (1.0 + k.share(slot, 1)))
        k.gx[rows, :] = total
        k.gx_low[rows, :] = total.astype(bf16)
        return carry

    lax.fori_loop(0, 2, tile, 0)
    k.sums[...] = gmod[...]


ANY = pl.BlockSpec(memory_space=pl.ANY)
VMEM = pl.BlockSpec(memory_space=pltpu.VMEM)
HBM = pl.BlockSpec(memory_space=pltpu.HBM)


def call(body, layer, layouts, ins, outs, scratch, flops):
    arrays = []
    counts = []
    kept = []
    for kind, given, part in ins.values():
        given = given if kind == "own" else (given,)
        arrays.extend(given)
        counts.append(len(given))
        rows, wide = given[0].shape[-2:]
        start, stop = part or (0, wide)
        kept.append(pltpu.VMEM((rows, stop - start), given[0].dtype))

    def kernel(*refs):
        refs = list(refs)
        take = lambda count: [refs.pop(0) for _ in range(count)]
        (layouts_ref,) = take(1)
        sources = [take(count) for count in counts]
        targets = take(len(outs))
        buffers = take(len(ins))
        results = take(len(outs))
        rest = take(len(scratch))
        in_sems, out_sems = refs
        k = Kernel(layer, layouts_ref)
        for number, (name, (kind, _, part)) in enumerate(ins.items()):
            given = sources[number]
            if part is not None:
                given = [ref.at[:, part[0] : part[1]] for ref in given]
            setattr(k, name, k.load(kind, given, buffers[number], in_sems.at[number]))
        k.results = {}
        for number, name in enumerate(outs):
            setattr(k, name, results[number])
            k.results[name] = (results[number], targets[number], out_sems.at[number])
        for name, ref in zip(scratch, rest):
            setattr(k, name, ref)
        body(k)
        k.finish()

    return pl.pallas_call(
        kernel,
        out_shape=[jax.ShapeDtypeStruct(shape, kind) for shape, kind, _ in outs.values()],
        in_specs=[pl.BlockSpec(memory_space=pltpu.SMEM)] + [HBM] * len(arrays),
        out_specs=[HBM if for_kernel else ANY for _, _, for_kernel in outs.values()],
        scratch_shapes=kept
        + [pltpu.VMEM(shape, kind) for shape, kind, _ in outs.values()]
        + [pltpu.VMEM(shape, kind) for shape, kind in scratch.values()]
        + [pltpu.SemaphoreType.DMA((len(ins),)), pltpu.SemaphoreType.DMA((len(outs),))],
        compiler_params=pltpu.CompilerParams(vmem_limit_bytes=40 * 1024 * 1024),
        cost_estimate=pl.CostEstimate(flops=flops, bytes_accessed=4 << 20, transcendentals=0),
    )(layouts, *arrays)


def own(pair, part=None):
    return ("own", pair, part)


def plain(array):
    return ("plain", array, None)


def micro(array):
    return ("micro", array, None)


def attn_forward(layer, layouts, x, mods, small, qko, vgd):
    return call(
        attn_forward_body,
        layer,
        layouts,
        dict(
            x=micro(x),
            mods=own(mods),
            w_qk=own(qko, (0, 2 * D)),
            w_vgd=own(vgd),
            small=own(small),
        ),
        dict(
            ordered=((ROWS, D), bf16, True),
            qkvg=((ROWS, QKVG), f32, True),
            dp=((ROWS, LANES), f32, True),
            vc=((ROWS, D), f32, True),
            cum=((ROWS, LANES), f32, True),
            cumt=((LANES, ROWS), f32, True),
            o=((ROWS, D), f32, True),
            gated=((ROWS, D), bf16, True),
        ),
        dict(
            inner=((ROWS, D), bf16),
            vpad=((ROWS + 8, D), f32),
            bias=((HALF, ROWS), f32),
        ),
        8 * 10**9,
    )


def ffn_forward(layer, layouts, x, mods, small, gated, qko, up, down):
    return call(
        ffn_forward_body,
        layer,
        layouts,
        dict(
            gated=plain(gated),
            x=micro(x),
            wo=own(qko, (2 * D, 3 * D)),
            mods=own(mods),
            small=own(small),
            wu=own(up),
            wn=own(down),
        ),
        dict(
            out=((ROWS, D), bf16, True),
            branch=((ROWS, D), f32, True),
            down=((ROWS, D), f32, True),
        ),
        {},
        5 * 10**9,
    )


def ffn_backward(layer, layouts, x, mods, small, gated, branch, down_raw, grad, up, down):
    return call(
        ffn_backward_body,
        layer,
        layouts,
        dict(
            mods=own(mods),
            small=own(small),
            x=micro(x),
            grad=micro(grad),
            branch=plain(branch),
            down=plain(down_raw),
            wu=own(up),
            wn=own(down),
            gated=plain(gated),
        ),
        dict(
            mid_grad=((ROWS, D), f32, True),
            branch_low=((ROWS, D), bf16, True),
            gwo=((D, D), f32, True),
            gwu_keep=((D, FF // 2), f32, False),
            gwu_send=((D, FF // 2), bf16, False),
            gwn=((FF, D), f32, False),
            sums=((8, FF), f32, False),
        ),
        dict(
            hidden_s=((ROWS, FF), bf16),
            inner_s=((ROWS, D), bf16),
            up_s=((ROWS, FF), bf16),
            down_s=((ROWS, D), bf16),
            gmod=((8, FF), f32),
            gbu=((1, FF), f32),
            gbn=((1, D), f32),
        ),
        12 * 10**9,
    )


def mixer_backward(layer, layouts, small, saved, branch_low, gwo, qko):
    ordered, qkvg, dp, vc, cum, cumt, o = saved
    return call(
        mixer_backward_body,
        layer,
        layouts,
        dict(
            branch_low=plain(branch_low),
            wo=own(qko, (2 * D, 3 * D)),
            qkvg=plain(qkvg),
            vc=plain(vc),
            cum=plain(cum),
            cumt=plain(cumt),
            o=plain(o),
            small=own(small),
            dp=plain(dp),
            ordered=plain(ordered),
            gwo=plain(gwo),
        ),
        dict(
            low=((ROWS, QKVG + LANES), bf16, True),
            gw_keep=((D, GROUP), f32, False),
            gw_send=((D, GROUP), bf16, False),
            sums=((8, D), f32, False),
        ),
        dict(
            mixed_s=((ROWS, D), f32),
            dv_s=((ROWS + 8, D), f32),
            rows_s=((ROWS, LANES), f32),
            cols_s=((LANES, ROWS), f32),
            bias=((HALF, ROWS), f32),
            gw=((D, 2 * GROUP), f32),
        ),
        15 * 10**9,
    )


def input_backward(layer, layouts, x, mods, low, mid_grad, qko, vgd):
    return call(
        input_backward_body,
        layer,
        layouts,
        dict(
            low=plain(low),
            w_qk=own(qko, (0, 2 * D)),
            w_vgd=own(vgd),
            x=micro(x),
            mid_grad=plain(mid_grad),
            mods=own(mods),
        ),
        dict(
            gx=((ROWS, D), f32, False),
            gx_low=((ROWS, D), bf16, True),
            sums=((8, 2 * D), f32, False),
        ),
        dict(
            mixed_s=((ROWS, D), f32),
            perm_s=((ROWS, 3 * D), bf16),
            gmod=((8, 2 * D), f32),
        ),
        4 * 10**9,
    )


def small_kernel(b_up, b_down, taps, b_decay, packed):
    packed[...] = jnp.zeros(packed.shape, f32)
    packed[0:1, :] = b_up[...]
    packed[1:2, :D] = b_down[...]
    packed[2:5, :D] = taps[0]
    packed[5:6, :HEADS] = b_decay[...]


def pack_small(b_up, b_down, taps, b_decay):
    return pl.pallas_call(
        small_kernel,
        out_shape=jax.ShapeDtypeStruct((8, FF), f32),
        in_specs=[VMEM] * 4,
        out_specs=VMEM,
    )(b_up, b_down, taps, b_decay)


def pack_kernel(*refs):
    packed = refs[-1]
    at = 0
    for ref in refs[:-1]:
        width = ref.shape[1]
        if width % LANES:
            packed[:, at:] = jnp.zeros((packed.shape[0], packed.shape[1] - at), packed.dtype)
        packed[:, at : at + width] = ref[...]
        at += width


def pack(*arrays):
    total = sum(-(-array.shape[1] // LANES) * LANES for array in arrays)
    return pl.pallas_call(
        pack_kernel,
        out_shape=jax.ShapeDtypeStruct((arrays[0].shape[0], total), arrays[0].dtype),
        in_specs=[VMEM] * len(arrays),
        out_specs=VMEM,
    )(*arrays)


def swap(values):
    return lax.ppermute(values, "section", [(0, 1), (1, 0)])


def row_bits():
    bits = lax.axis_size("row").bit_length() - 1
    third = bits // 3
    return (
        tuple(range(third)),
        tuple(range(third, 2 * third)),
        tuple(range(2 * third, bits)),
    )


def partner(values, bit):
    size = lax.axis_size("row")
    return lax.ppermute(values, "row", [(i, i ^ (1 << bit)) for i in range(size)])


def axis_of(bit):
    return lax.axis_size("row").bit_length() - 2 - bit


def bit_of(bit):
    return (lax.axis_index("row") >> bit) & 1


def single(values):
    return values.reshape((1,) * (lax.axis_size("row").bit_length() - 1) + values.shape)


def join(held, other, bit):
    return jnp.where(
        bit_of(bit) == 0,
        jnp.concatenate([held, other], axis=axis_of(bit)),
        jnp.concatenate([other, held], axis=axis_of(bit)),
    )


def flat(held):
    return held.reshape(-1, held.shape[-1])


def by_bits(values):
    bits = lax.axis_size("row").bit_length() - 1
    return values.reshape((2,) * bits + values.shape[1:])


def cut(held, bit):
    axis = axis_of(bit)
    mine = bit_of(bit)
    sent = lax.dynamic_index_in_dim(held, 1 - mine, axis, keepdims=True)
    kept = lax.dynamic_index_in_dim(held, mine, axis, keepdims=True)
    return sent, kept


def lock(*arrays):
    return lax.optimization_barrier(arrays)


class Scatter:
    def __init__(self, values):
        self.held = by_bits(values)
        self.kept = None

    def ready(self, bit):
        sent, self.kept = cut(self.held, bit)
        return sent.astype(bf16)

    def take(self, other):
        self.held = self.kept + other.astype(f32)

    def result(self):
        return self.held.reshape(self.held.shape[-2:])


class Gather:
    def __init__(self, values):
        self.held = single(values)

    def ready(self, bit):
        self.bit = bit
        return self.held

    def take(self, other):
        self.held = join(self.held, other, self.bit)


class Total:
    def __init__(self, values):
        self.held = values

    def ready(self, bit):
        return self.held

    def take(self, other):
        self.held = self.held + other


def begin(chains, bit):
    return [chain.ready(bit) for chain in chains]


def send(arrays, bit):
    return [partner(array, bit) for array in arrays]


def end(chains, arrays):
    for chain, array in zip(chains, arrays):
        chain.take(array)


def on_device(
    tokens, conditions, output_grad, layouts,
    w_ada, b_ada, w_query, w_key, w_value, w_gate, w_out, w_decay, b_decay, conv_kernel,
    w_up, b_up, w_down, b_down,
):
    section = lax.axis_index("section")
    devices = lax.axis_size("row")
    is_first = section == 0
    shard = w_query.shape[1]
    along_x, along_y, along_z = row_bits()
    plane = along_x + along_y
    every = plane + along_z

    def pick(pair):
        return jnp.where(is_first, pair[0], pair[1])

    def pick_other(pair):
        return jnp.where(is_first, pair[1], pair[0])

    def both(values):
        return values, swap(values)

    qko = Gather(pack(w_query[0], w_key[0], w_out[0]))
    vgd = Gather(pack(w_value[0], w_gate[0], w_decay[0]))
    up = Gather(w_up[0])
    down = Gather(w_down[0])
    lifted = Gather(
        jax.nn.silu(conditions.astype(f32)).astype(bf16).reshape(MICRO * SLOTS, D)
    )
    chains = [qko, vgd, up, down, lifted]
    bit = along_z[-1]
    sent = lock(*begin(chains, bit))
    others = send(sent, bit)
    lifted.take(others[4])
    for bit in tuple(reversed(along_z))[1:] + plane:
        end([lifted], send(begin([lifted], bit), bit))
    lifted_parts = lifted.held.reshape(devices, MICRO * SLOTS, D)
    *others, lifted_parts = lock(*others[:4], lifted_parts)
    chains = chains[:4]
    end(chains, others)
    row = lax.axis_index("row")
    lifted_cut = lax.dynamic_slice_in_dim(lifted_parts, row * shard, shard, 2)
    terms = mm(lifted_cut.reshape(devices * MICRO * SLOTS, shard), w_ada[0])
    held = by_bits(terms.reshape(devices, MICRO * SLOTS, 6 * D))
    for bit in tuple(reversed(along_z))[1:]:
        sent = begin(chains, bit)
        others = send(sent, bit)
        if bit == along_z[0]:
            for low_bit in plane:
                gone, stays = cut(held, low_bit)
                held = stays + partner(gone, low_bit)
        *others, held = lock(*others, held)
        end(chains, others)
    for step, (bit_a, bit_b) in enumerate(zip(plane, along_y + along_x)):
        group_a, group_b = [qko, up], [vgd, down]
        if step == len(along_x):
            for high_bit in along_z:
                gone, stays = cut(held, high_bit)
                held = stays + partner(gone, high_bit)
            mods = both(held.reshape(MICRO * SLOTS, 6 * D) + b_ada[0])
        if step < len(plane) - 1:
            others_a = send(begin(group_a, bit_a), bit_a)
            others_b = send(begin(group_b, bit_b), bit_b)
            others = lock(*others_a, *others_b)
            end(group_a + group_b, others)
        else:
            first = [send(begin([qko], bit_a), bit_a), send(begin([vgd], bit_b), bit_b)]
            second = [send(begin([up], bit_a), bit_a), send(begin([down], bit_b), bit_b)]
            end([qko, vgd], first[0] + first[1])
            end([up, down], second[0] + second[1])
    qko, vgd, up, down = [both(flat(chain.held)) for chain in (qko, vgd, up, down)]
    smalls = both(pack_small(b_up, b_down, conv_kernel, b_decay))

    x = tokens
    kept = []
    acts = []
    for l in range(2):
        *saved, gated = attn_forward(l, layouts, x, mods, smalls, qko, vgd)
        out, branch, down_raw = ffn_forward(l, layouts, x, mods, smalls, gated, qko, up, down)
        kept.append((x, saved, gated, branch, down_raw))
        acts.append(out)
        x = out[None]

    late, _ = lock(w_ada[0], up[0])
    ada_all = lax.all_gather(late, "row", axis=0, tiled=True)

    def ffn_step(l, grad):
        x, saved, gated, branch, down_raw = kept[l]
        mid_grad, branch_low, gwo, keep, sent, gwn, sums = ffn_backward(
            l, layouts, x, mods, smalls, gated, branch, down_raw, grad, up, down
        )
        pair = gwn.reshape(devices, 2, FF // devices // 2, D)
        down_keep = lax.dynamic_index_in_dim(pair, section, 1, keepdims=False)
        down_send = lax.dynamic_index_in_dim(pair, 1 - section, 1, keepdims=False).astype(bf16)
        return (branch_low, gwo), mid_grad, (sent, down_send), (keep, down_keep), sums

    def mixer_step(l, carried):
        return mixer_backward(l, layouts, smalls, kept[l][1], *carried, qko)

    def input_step(l, low, mid_grad):
        return input_backward(l, layouts, kept[l][0], mods, low, mid_grad, qko, vgd)

    def ffn_chains(keep, others):
        up_half = keep[0] + others[0].astype(f32)
        down_half = keep[1] + others[1].astype(f32)
        return [Scatter(up_half.reshape(devices, shard, FF // 2)), Scatter(down_half)]

    def attn_chain(keep, other):
        return [Scatter((keep + other.astype(f32)).reshape(devices, shard, GROUP))]

    def mod_chains(ffn_sums, input_sums, mixer_sums):
        grad_mod = jnp.concatenate([input_sums[:SLOTS], ffn_sums[:SLOTS]], axis=1)
        low = grad_mod.astype(bf16)
        return low, [Gather(low), Total(ffn_sums), Total(input_sums), Total(mixer_sums)]

    x_bits, y_bits, z_bits = along_x, along_y, along_z
    carried, mid_grad, f2_send, f2_keep, f2_sums = ffn_step(1, output_grad)
    acts_send = pick_other(acts)
    *carried, acts_send, s0, s1 = lock(*carried, acts_send, *f2_send)
    f2_other = [swap(s0), swap(s1)]
    acts_other = swap(acts_send)
    low, a2_keep, a2_send, m2_sums = mixer_step(1, carried)
    low, acts_other, *f2_other = lock(low, acts_other, *f2_other)
    f2 = ffn_chains(f2_keep, f2_other)

    def steps(chains, bits):
        for bit in bits[:-1]:
            end(chains, send(begin(chains, bit), bit))
        return begin(chains, bits[-1])

    f2_sent = steps(f2, x_bits)
    low, a2_send, *f2_sent = lock(low, a2_send, *f2_sent)
    f2_other = send(f2_sent, x_bits[-1])
    a2_other = swap(a2_send)
    gx_two, grad, i2_sums = input_step(1, low, mid_grad)
    grad, a2_other = lock(grad, a2_other)
    a2 = attn_chain(a2_keep, a2_other)
    mod_low_two, mod2 = mod_chains(f2_sums, i2_sums, m2_sums)
    a2_sent = steps(a2 + mod2, x_bits)
    grad, *a2_sent = lock(grad, *a2_sent)
    a2_other = send(a2_sent, x_bits[-1])

    carried, mid_grad, f1_send, f1_keep, f1_sums = ffn_step(0, grad[None])
    locked = lock(*carried, *f1_send, *f2_other, *a2_other)
    carried, f1_send, locked = locked[:2], locked[2:4], locked[4:]
    f1_other = [swap(array) for array in f1_send]
    two = f2 + a2 + mod2
    end(two, locked)
    two_sent = steps(two, y_bits)
    f1 = ffn_chains(f1_keep, f1_other)
    f1_sent = steps(f1, x_bits)
    locked = lock(*carried, *two_sent, *f1_sent)
    carried, two_sent, f1_sent = locked[:2], locked[2 : 2 + len(two)], locked[2 + len(two) :]
    two_other = send(two_sent, y_bits[-1])
    f1_other = send(f1_sent, x_bits[-1])
    low, a1_keep, a1_send, m1_sums = mixer_step(0, carried)
    low, ada_all, *locked = lock(low, ada_all, *two_other, *f1_other)
    end(two + f1, locked)
    two_sent = steps(two, z_bits)
    f1_sent = steps(f1, y_bits)
    low, a1_send, *locked = lock(low, a1_send, *two_sent, *f1_sent)
    a1_other = swap(a1_send)
    two_other = send(locked[: len(two)], z_bits[-1])
    f1_other = send(locked[len(two) :], y_bits[-1])
    gx_one, _, i1_sums = input_step(0, low, mid_grad)
    gx_send = pick_other((gx_one, gx_two))
    a1_other, i1_sums, gx_send, *locked = lock(
        a1_other, i1_sums, gx_send, *two_other, *f1_other
    )
    end(two + f1, locked)
    mod_low_one, mod1 = mod_chains(f1_sums, i1_sums, m1_sums)
    one = attn_chain(a1_keep, a1_other) + mod1
    gx_other = swap(gx_send)
    mod_other = swap(pick_other((mod_low_one, mod_low_two)))
    for bit in plane + z_bits:
        sent = begin(one, bit)
        chains = list(one)
        if bit == x_bits[-1]:
            for z_bit in z_bits[:-1]:
                end(f1, send(begin(f1, z_bit), z_bit))
            f1_sent = begin(f1, z_bits[-1])
            f1_other = send(f1_sent, z_bits[-1])
        others = send(sent, bit)
        if bit == x_bits[-1]:
            others = lock(*others, *f1_other)
            end(f1, others[len(one) :])
            others = others[: len(one)]
        end(one, others)

    lifted_mine = lax.dynamic_slice_in_dim(lifted_cut, section * SLOTS, SLOTS, 1)
    lifted_mine = lifted_mine.reshape(devices * SLOTS, shard)

    def summed(ffn, attn, mod):
        ada = lax.dot_general(
            lifted_mine,
            flat(mod[0].held),
            (((0,), (0,)), ((), ())),
            preferred_element_type=f32,
        )
        totals = [chain.held for chain in mod[1:]]
        return [attn.result(), ffn[0].result(), ffn[1].result(), ada, *totals]

    sums = (summed(f1, one[0], mod1), summed(f2, a2[0], mod2))
    mine = [pick(pair) for pair in zip(*sums)]
    other = [swap(pick_other(pair)) for pair in zip(*sums)]

    def halves(number, axis):
        mine_half, other_half = mine[number], other[number]
        return jnp.concatenate(
            [pick((mine_half, other_half)), pick_other((mine_half, other_half))], axis=axis
        )

    attn_total = halves(0, 1)
    up_total = halves(1, 1)
    down_total = halves(2, 0)
    grad_w_ada = mine[3] + other[3]
    ffn_sums = mine[4] + other[4]
    input_sums = mine[5] + other[5]
    mixer_sums = mine[6] + other[6]
    grad_b_ada = jnp.concatenate(
        [input_sums[0] + input_sums[1], ffn_sums[0] + ffn_sums[1]]
    )

    mod_own = pick((mod_low_one, mod_low_two))
    mod_both = jnp.concatenate([pick((mod_own, mod_other)), pick_other((mod_own, mod_other))])
    grad_lifted = mm_t(mod_both, ada_all)
    grad_lifted = (grad_lifted + swap(grad_lifted)).reshape(MICRO, SLOTS, D)
    _, pull_silu = jax.vjp(jax.nn.silu, conditions.astype(f32))
    (cond_grads,) = pull_silu(grad_lifted)

    def assembled(pair, other):
        mine = pick(pair)
        return jnp.stack([pick((mine, other)), pick_other((mine, other))])

    return (
        assembled(acts, acts_other)[None],
        assembled((gx_one, gx_two), gx_other)[None],
        cond_grads,
        grad_w_ada[None],
        grad_b_ada[None],
        attn_total[None, :, :D],
        attn_total[None, :, D : 2 * D],
        attn_total[None, :, 2 * D : 3 * D],
        attn_total[None, :, 3 * D : 4 * D],
        attn_total[None, :, 4 * D : 5 * D],
        attn_total[None, :, 5 * D : 5 * D + HEADS],
        mixer_sums[3:4, :HEADS],
        mixer_sums[None, :3],
        up_total[None],
        ffn_sums[2:3],
        down_total[None],
        ffn_sums[3:4, :D],
    )


def solution(mesh):
    rows = P(None, "row", None)
    mats = P("section", "row", None)
    vector = P("section", None)
    in_specs = (
        rows, rows, rows, P(None, "row"),
        mats, vector, mats, mats, mats, mats, mats, mats, vector, P("section", None, None),
        mats, vector, mats, vector,
    )
    blocks = P("section", None, "row", None)
    out_specs = (
        blocks, blocks, rows,
        mats, vector, mats, mats, mats, mats, mats, mats, vector, P("section", None, None),
        mats, vector, mats, vector,
    )
    return jax.shard_map(
        on_device, mesh=mesh, in_specs=in_specs, out_specs=out_specs, check_vma=False
    )
```

```python
import functools

import jax
import jax.numpy as jnp
from jax import lax
from jax.experimental import pallas as pl
from jax.experimental.pallas import tpu as pltpu
from jax.sharding import PartitionSpec as P

D = 384
HEADS = 6
HEAD_DIM = 64
FF = 1536
MICRO = 2
ROWS = 512
HALF = 256
SLOTS = 2
PAIR = 128
PAIRS = D // PAIR
QKVG = 4 * D
LANES = 128
GROUP = (QKVG + D + LANES) // 2
NEG = -1e30
SCALE = HEAD_DIM**-0.5

bf16 = jnp.bfloat16
f32 = jnp.float32


def mm(left, right):
    return jnp.dot(left, right, preferred_element_type=f32)


def mm_t(left, right):
    return lax.dot_general(left, right, (((1,), (1,)), ((), ())), preferred_element_type=f32)


def split(values):
    high = values.astype(bf16)
    return high, (values - high.astype(f32)).astype(bf16)


def split_three(values):
    high, rest = split(values)
    mid = values - high.astype(f32)
    middle, low = split(mid)
    return high, middle, low


def cat_left(values):
    high, low = split(values)
    return jnp.concatenate([high, low, high], axis=1)


def cat_right(values):
    high, low = split(values)
    return jnp.concatenate([high, high, low], axis=1)


def mm_near(left, right_pair, right_high):
    high, low = split(left)
    wide = mm(high, right_pair)
    return wide[:, :PAIR] + wide[:, PAIR:] + mm(low, right_high)


def lane_iota(rows, columns):
    return lax.broadcasted_iota(jnp.int32, (rows, columns), 1)


def row_iota(rows, columns):
    return lax.broadcasted_iota(jnp.int32, (rows, columns), 0)


def order_matrix(start, rows, wide, to_scan):
    t = row_iota(rows, ROWS) + start
    small = (t & 256) + ((t & 15) << 4) + ((t & 255) >> 4)
    if to_scan:
        large = ((t & 15) << 5) + (t >> 4)
    else:
        large = ((t & 31) << 4) + (t >> 5)
    source = jnp.where(wide, large, small)
    return jnp.where(lane_iota(rows, ROWS) == source, 1.0, 0.0).astype(bf16)


def normalise(values):
    centred = values - jnp.mean(values, axis=-1, keepdims=True)
    rate = lax.rsqrt(jnp.mean(centred * centred, axis=-1, keepdims=True) + 1e-06)
    return centred * rate, rate


def normalise_back(normal, rate, grad):
    return rate * (
        grad
        - jnp.mean(grad, axis=-1, keepdims=True)
        - normal * jnp.mean(grad * normal, axis=-1, keepdims=True)
    )


class In:
    def __init__(self, copy, kept):
        self.copy = copy
        self.kept = kept

    def __call__(self):
        if self.copy is not None:
            self.copy.wait()
            self.copy = None
        return self.kept


class Kernel:
    def __init__(self, layer, layouts):
        self.layer = layer
        self.section = lax.axis_index("section")
        self.own = self.section == layer
        self.layout = layouts[self.section, 0]
        self.wide = self.layout == 0
        self.live_rows = jnp.where(self.wide, ROWS, self.layout * HALF)
        self.pushed = {}

    def load(self, kind, refs, kept, sem):
        if kind == "own":
            mine, other = refs

            @pl.when(self.own)
            def _():
                pltpu.make_async_copy(mine, kept, sem).start()

            @pl.when(jnp.logical_not(self.own))
            def _():
                pltpu.make_async_copy(other, kept, sem).start()

            return In(pltpu.make_async_copy(mine, kept, sem), kept)
        (source,) = refs
        if kind == "micro":
            source = source.at[self.section if source.shape[0] == MICRO else 0]
        copy = pltpu.make_async_copy(source, kept, sem)
        copy.start()
        return In(copy, kept)

    def push(self, name):
        kept, target, sem = self.results[name]
        copy = pltpu.make_async_copy(kept, target, sem)
        copy.start()
        self.pushed[name] = copy

    def finish(self):
        for name in self.results:
            if name not in self.pushed:
                self.push(name)
        for copy in self.pushed.values():
            copy.wait()

    def slot(self, half):
        return jnp.where(self.wide, 0, half)

    def share(self, slot, part):
        row = pl.ds(2 * self.section + slot, 1)
        return self.mods()[row, part * D : (part + 1) * D]

    def bu(self):
        return self.small()[0:1, :]

    def bn(self):
        return self.small()[1:2, :D]

    def ck(self, tap):
        return self.small()[2 + tap : 3 + tap, :D]

    def bd(self):
        return self.small()[5:6, :LANES]


def sigmoid(values):
    return 1.0 / (1.0 + jnp.exp(-values))


GELU_A = 0.7978845608028654
GELU_B = 0.044715


def gelu_parts(values):
    square = values * values
    tanh = jnp.tanh(GELU_A * values * (1.0 + GELU_B * square))
    return square, tanh


def fill_bias(bias, wide):
    bias[:, :HALF] = jnp.full((HALF, HALF), 0.0, f32) + jnp.where(wide, 0.0, NEG)
    causal = row_iota(HALF, HALF) >= lane_iota(HALF, HALF)
    bias[:, HALF:] = jnp.where(causal, 0.0, NEG)


def decay_factors(cum, cumt, bias, head):
    row = cumt[pl.ds(head, 1), :]
    lanes = lane_iota(1, LANES)
    column = jnp.sum(jnp.where(lanes == head, cum[...], 0.0), axis=1, keepdims=True)
    first = jnp.exp(column[:HALF] - row[:, :HALF] + bias[:, HALF:])
    second = jnp.exp(column[HALF:] - row + bias[...])
    return first, second


def head_norm(values, lanes):
    square = values * values
    low = jnp.sum(jnp.where(lanes < HEAD_DIM, square, 0.0), axis=1, keepdims=True)
    high = jnp.sum(jnp.where(lanes < HEAD_DIM, 0.0, square), axis=1, keepdims=True)
    return jnp.where(lanes < HEAD_DIM, low, high) * (1.0 / HEAD_DIM)


def fill_decay(dp, bd, cum, cumt):
    raw = dp[...] + bd
    log_decay = (jnp.minimum(raw, 0.0) - jnp.log1p(jnp.exp(-jnp.abs(raw)))) * (1.0 / 16.0)
    high, middle, low = split_three(log_decay)
    causal = jnp.where(row_iota(ROWS, ROWS) >= lane_iota(ROWS, ROWS), 1.0, 0.0).astype(bf16)
    cum[...] = mm(causal, high) + mm(causal, middle) + mm(causal, low)
    cumt[...] = jnp.transpose(cum[...])


def columns(index, first=0):
    return pl.ds(pl.multiple_of(index * PAIR + first, PAIR), PAIR)


def attn_forward_body(k):
    flip = k.layer == 1
    wide = k.wide
    x = k.x()
    k.mods()

    def first(i, carry):
        rows = pl.ds(pl.multiple_of(i * HALF, HALF), HALF)
        slot = k.slot(i)
        normal, _ = normalise(x[rows, :].astype(f32))
        k.inner[rows, :] = (normal * (1.0 + k.share(slot, 1)) + k.share(slot, 0)).astype(bf16)
        return carry

    lax.fori_loop(0, 2, first, 0)
    w_qk = k.w_qk()
    w_vgd = k.w_vgd()

    def project(i, carry):
        start = pl.multiple_of(i * HALF, HALF)
        rows = pl.ds(start, HALF)
        if flip:
            part = mm(order_matrix(start, HALF, wide, True), k.inner[...]).astype(bf16)
        else:
            part = k.inner[rows, :]
        k.ordered[rows, :] = part
        k.qkvg[rows, : 2 * D] = mm(part, w_qk[...])
        k.qkvg[rows, 2 * D :] = mm(part, w_vgd[:, : 2 * D])
        k.dp[rows, :] = mm(part, w_vgd[:, 2 * D :])
        return carry

    lax.fori_loop(0, 2, project, 0)
    k.small()
    for name in ("ordered", "qkvg", "dp"):
        k.push(name)
    fill_decay(k.dp, k.bd(), k.cum, k.cumt)
    fill_bias(k.bias, wide)

    vpad = k.vpad
    vpad[0:8, :] = jnp.zeros((8, D), f32)
    vpad[8 : 8 + ROWS, :] = k.qkvg[:, 2 * D : 3 * D]
    position = row_iota(ROWS, 1) & jnp.where(wide, ROWS - 1, HALF - 1)
    one = jnp.where(position >= 1, vpad[7 : 7 + ROWS, :], 0.0)
    two = jnp.where(position >= 2, vpad[6 : 6 + ROWS, :], 0.0)
    k.vc[...] = k.ck(0) * vpad[8 : 8 + ROWS, :] + k.ck(1) * one + k.ck(2) * two
    for name in ("cum", "cumt", "vc"):
        k.push(name)

    def pair(p, carry):
        lanes = lane_iota(1, PAIR)
        queries = cat_left(k.qkvg[:, columns(p)] * SCALE)
        keys = k.qkvg[:, columns(p, D)]
        value_high, value_low = split(k.vc[:, columns(p)])
        values = jnp.concatenate([value_high, value_low], axis=1)
        parts = []
        for e in range(2):
            key_cat = cat_right(jnp.where((lanes // HEAD_DIM) == e, keys, 0.0))
            first, second = decay_factors(k.cum, k.cumt, k.bias, 2 * p + e)
            first = first * mm_t(queries[:HALF], key_cat[:HALF])
            second = second * mm_t(queries[HALF:], key_cat)
            parts.append(
                jnp.concatenate(
                    [
                        mm_near(first, values[:HALF], value_high[:HALF]),
                        mm_near(second, values, value_high),
                    ],
                    axis=0,
                )
            )
        total = jnp.where(lanes < HEAD_DIM, parts[0], parts[1])
        k.o[:, columns(p)] = total
        gate = k.qkvg[:, columns(p, 3 * D)]
        normed = total * lax.rsqrt(head_norm(total, lanes) + 1.0)
        mixed = (normed * (gate * sigmoid(gate))).astype(bf16)
        if flip:
            k.inner[:, columns(p)] = mixed
        else:
            k.gated[:, columns(p)] = mixed
        return carry

    lax.fori_loop(0, PAIRS, pair, 0)
    k.push("o")
    if flip:

        def back(i, carry):
            start = pl.multiple_of(i * HALF, HALF)
            k.gated[pl.ds(start, HALF), :] = mm(
                order_matrix(start, HALF, wide, False), k.inner[...]
            ).astype(bf16)
            return carry

        lax.fori_loop(0, 2, back, 0)


def ffn_forward_body(k):
    gated, x, wo = k.gated(), k.x(), k.wo()
    k.mods(), k.small()
    wu, wn = k.wu(), k.wn()

    def tile(i, carry):
        start = pl.multiple_of(i * HALF, HALF)
        rows = pl.ds(start, HALF)
        slot = k.slot(i)
        grown = mm(gated[rows, :], wo[...])
        k.branch[rows, :] = grown
        middle = x[rows, :].astype(f32) + k.share(slot, 2) * grown
        normal, _ = normalise(middle)
        inner = (normal * (1.0 + k.share(slot, 4)) + k.share(slot, 3)).astype(bf16)
        up = mm(inner, wu[...]) + k.bu()
        _, tanh = gelu_parts(up)
        hidden = (0.5 * up * (1.0 + tanh)).astype(bf16)
        low = mm(hidden, wn[...])
        k.down[rows, :] = low
        result = middle + k.share(slot, 5) * (low + k.bn())
        live = (row_iota(HALF, 1) + start) < k.live_rows
        k.out[rows, :] = jnp.where(live, result, 0.0).astype(bf16)
        return carry

    lax.fori_loop(0, 2, tile, 0)


def ffn_backward_body(k):
    gmod, gbu, gbn = k.gmod, k.gbu, k.gbn
    gmod[...] = jnp.zeros(gmod.shape, f32)
    gbu[...] = jnp.zeros(gbu.shape, f32)
    gbn[...] = jnp.zeros(gbn.shape, f32)
    k.mods(), k.small()
    x, grad, branch, down = k.x(), k.grad(), k.branch(), k.down()
    wu, wn = k.wu(), k.wn()

    def tile(i, carry):
        start = pl.multiple_of(i * HALF, HALF)
        rows = pl.ds(start, HALF)
        slot = k.slot(i)

        def add(part, values):
            where = (pl.ds(slot, 1), slice((part - 2) * D, (part - 1) * D))
            gmod[where] = gmod[where] + jnp.sum(values, axis=0, keepdims=True)

        grown = branch[rows, :]
        middle = x[rows, :].astype(f32) + k.share(slot, 2) * grown
        normal, rate = normalise(middle)
        inner = (normal * (1.0 + k.share(slot, 4)) + k.share(slot, 3)).astype(bf16)
        k.inner_s[rows, :] = inner
        live = (row_iota(HALF, 1) + start) < k.live_rows
        above = jnp.where(live, grad[rows, :].astype(f32), 0.0)
        add(5, above * (down[rows, :] + k.bn()))
        grad_down = above * k.share(slot, 5)
        gbn[...] = gbn[...] + jnp.sum(grad_down, axis=0, keepdims=True)
        down_low = grad_down.astype(bf16)
        k.down_s[rows, :] = down_low
        up = mm(inner, wu[...]) + k.bu()
        square, tanh = gelu_parts(up)
        half = 0.5 * (1.0 + tanh)
        k.hidden_s[rows, :] = (up * half).astype(bf16)
        slope = half + 0.5 * up * (1.0 - tanh * tanh) * (
            GELU_A * (1.0 + 3.0 * GELU_B * square)
        )
        grad_up = mm_t(down_low, wn[...]) * slope
        gbu[...] = gbu[...] + jnp.sum(grad_up, axis=0, keepdims=True)
        up_low = grad_up.astype(bf16)
        k.up_s[rows, :] = up_low
        grad_inner = mm_t(up_low, wu[...])
        add(3, grad_inner)
        add(4, grad_inner * normal)
        grad_middle = above + normalise_back(
            normal, rate, grad_inner * (1.0 + k.share(slot, 4))
        )
        k.mid_grad[rows, :] = grad_middle
        add(2, grad_middle * grown)
        k.branch_low[rows, :] = (grad_middle * k.share(slot, 2)).astype(bf16)
        return carry

    lax.fori_loop(0, 2, tile, 0)
    k.push("mid_grad")
    k.push("branch_low")

    def weights(j, carry):
        part = pl.ds(pl.multiple_of(j * HALF, HALF), HALF)
        hidden_t = jnp.transpose(k.hidden_s[:, part].astype(f32)).astype(bf16)
        k.gwn[part, :] = mm(hidden_t, k.down_s[...])
        return carry

    lax.fori_loop(0, FF // HALF, weights, 0)
    k.push("gwn")
    inner_t = jnp.transpose(k.inner_s[...].astype(f32)).astype(bf16)

    def halves(j, carry):
        here = pl.ds(pl.multiple_of(j * HALF, HALF), HALF)
        keep = pl.ds(pl.multiple_of(j * HALF + k.section * (FF // 2), HALF), HALF)
        send = pl.ds(pl.multiple_of(j * HALF + (1 - k.section) * (FF // 2), HALF), HALF)
        k.gwu_keep[:, here] = mm(inner_t, k.up_s[:, keep])
        k.gwu_send[:, here] = mm(inner_t, k.up_s[:, send]).astype(bf16)
        return carry

    lax.fori_loop(0, FF // 2 // HALF, halves, 0)
    k.push("gwu_keep")
    k.push("gwu_send")
    gated = k.gated()
    k.gwo[...] = mm(jnp.transpose(gated[...].astype(f32)).astype(bf16), k.branch_low[...])

    short = jnp.concatenate([gbn[...], jnp.zeros((1, FF - D), f32)], axis=1)
    k.sums[...] = jnp.concatenate(
        [gmod[0:SLOTS, :], gbu[...], short, jnp.zeros((4, FF), f32)], axis=0
    )


def mixer_backward_body(k):
    flip = k.layer == 1
    wide = k.wide
    mixed_s, low, dv_s, rows_s, cols_s = k.mixed_s, k.low, k.dv_s, k.rows_s, k.cols_s
    fill_bias(k.bias, wide)
    branch_low, wo = k.branch_low(), k.wo()

    def first(i, carry):
        start = pl.multiple_of(i * HALF, HALF)
        rows = pl.ds(start, HALF)
        if flip:
            part = mm(order_matrix(start, HALF, wide, True), branch_low[...]).astype(bf16)
        else:
            part = branch_low[rows, :]
        mixed_s[rows, :] = mm_t(part, wo[...])
        return carry

    lax.fori_loop(0, 2, first, 0)
    rows_s[...] = jnp.zeros(rows_s.shape, f32)
    cols_s[...] = jnp.zeros(cols_s.shape, f32)
    qkvg, vc, cum, cumt, o = k.qkvg(), k.vc(), k.cum(), k.cumt(), k.o()
    k.small()

    def pair(p, carry):
        lanes = lane_iota(1, PAIR)
        total = o[:, columns(p)]
        gate = qkvg[:, columns(p, 3 * D)]
        above = mixed_s[:, columns(p)]
        rate = lax.rsqrt(head_norm(total, lanes) + 1.0)
        sig = sigmoid(gate)
        grad_gate = above * (total * rate) * (sig * (1.0 + gate * (1.0 - sig)))
        low[:, columns(p, 3 * D)] = grad_gate.astype(bf16)
        grad_normed = above * (gate * sig)
        product = grad_normed * total
        inside = jnp.where(
            lanes < HEAD_DIM,
            jnp.sum(jnp.where(lanes < HEAD_DIM, product, 0.0), axis=1, keepdims=True),
            jnp.sum(jnp.where(lanes < HEAD_DIM, 0.0, product), axis=1, keepdims=True),
        ) * (1.0 / HEAD_DIM)
        grad_o = rate * grad_normed - total * (rate * rate * rate) * inside

        queries = qkvg[:, columns(p)] * SCALE
        keys = qkvg[:, columns(p, D)]
        values = vc[:, columns(p)]
        query_cat = cat_left(queries)
        grad_cat = cat_left(grad_o)
        key_high, key_low = split(keys)
        key_pair = jnp.concatenate([key_high, key_low], axis=1)
        query_t = jnp.transpose(queries)
        grad_t = jnp.transpose(grad_o)
        grad_q = []
        grad_k = []
        grad_v = []
        for e in range(2):
            mine = (lanes // HEAD_DIM) == e
            head = 2 * p + e
            key_cat = cat_right(jnp.where(mine, keys, 0.0))
            value_cat = cat_right(jnp.where(mine, values, 0.0))
            first, second = decay_factors(cum, cumt, k.bias, head)
            raw_first = mm_t(query_cat[:HALF], key_cat[:HALF])
            raw_second = mm_t(query_cat[HALF:], key_cat)
            grad_first = first * mm_t(grad_cat[:HALF], value_cat[:HALF])
            grad_second = second * mm_t(grad_cat[HALF:], value_cat)
            score_first = raw_first * first
            score_second = raw_second * second
            pull_first = grad_first * raw_first
            pull_second = grad_second * raw_second
            here = lanes == head
            rows_s[:HALF, :] = rows_s[:HALF, :] + jnp.where(
                here, jnp.sum(pull_first, axis=1, keepdims=True), 0.0
            )
            rows_s[HALF:, :] = rows_s[HALF:, :] + jnp.where(
                here, jnp.sum(pull_second, axis=1, keepdims=True), 0.0
            )
            low_cols = jnp.sum(pull_second, axis=0, keepdims=True)
            cols_s[pl.ds(head, 1), :HALF] = low_cols[:, :HALF] + jnp.sum(
                pull_first, axis=0, keepdims=True
            )
            cols_s[pl.ds(head, 1), HALF:] = low_cols[:, HALF:]
            grad_q.append(
                jnp.concatenate(
                    [
                        mm_near(grad_first, key_pair[:HALF], key_high[:HALF]),
                        mm_near(grad_second, key_pair, key_high),
                    ],
                    axis=0,
                )
            )

            def turned(source_t, block_first, block_second):
                high, low = split(source_t[e * HEAD_DIM : (e + 1) * HEAD_DIM, :])
                both = jnp.concatenate([high, low], axis=0)
                first_high, first_low = split(block_first)
                second_high, second_low = split(block_second)
                one = mm(both[:, :HALF], first_high)
                one = one[:HEAD_DIM] + one[HEAD_DIM:] + mm(high[:, :HALF], first_low)
                two = mm(both[:, HALF:], second_high)
                two = two[:HEAD_DIM] + two[HEAD_DIM:] + mm(high[:, HALF:], second_low)
                return jnp.concatenate([two[:, :HALF] + one, two[:, HALF:]], axis=1)

            grad_k.append(turned(query_t, grad_first, grad_second))
            grad_v.append(turned(grad_t, score_first, score_second))
        query_grad = jnp.where(lanes < HEAD_DIM, grad_q[0], grad_q[1]) * SCALE
        low[:, columns(p)] = query_grad.astype(bf16)
        low[:, columns(p, D)] = jnp.transpose(jnp.concatenate(grad_k, axis=0)).astype(bf16)
        dv_s[:ROWS, columns(p)] = jnp.transpose(jnp.concatenate(grad_v, axis=0))
        return carry

    lax.fori_loop(0, PAIRS, pair, 0)

    pulled = rows_s[...] - jnp.transpose(cols_s[...])
    high, middle, rest = split_three(pulled)
    upper_first = jnp.concatenate(
        [
            jnp.where(row_iota(HALF, HALF) <= lane_iota(HALF, HALF), 1.0, 0.0),
            jnp.full((HALF, HALF), 0.0, f32) + jnp.where(wide, 1.0, 0.0),
        ],
        axis=1,
    ).astype(bf16)
    upper_second = upper_first[:, :HALF]
    later = jnp.concatenate(
        [
            mm(upper_first, high) + mm(upper_first, middle) + mm(upper_first, rest),
            mm(upper_second, high[HALF:]) + mm(upper_second, middle[HALF:])
            + mm(upper_second, rest[HALF:]),
        ],
        axis=0,
    )
    grad_dp = later * (1.0 / 16.0) * sigmoid(-(k.dp()[...] + k.bd()))
    grad_bd = jnp.sum(grad_dp, axis=0, keepdims=True)
    low[:, QKVG:] = grad_dp.astype(bf16)

    dv_s[ROWS:, :] = jnp.zeros((8, D), f32)
    position = row_iota(ROWS, 1) & jnp.where(wide, ROWS - 1, HALF - 1)
    last = jnp.where(wide, ROWS - 1, HALF - 1)
    here = dv_s[0:ROWS, :]
    one = jnp.where(position <= last - 1, dv_s[1 : 1 + ROWS, :], 0.0)
    two = jnp.where(position <= last - 2, dv_s[2 : 2 + ROWS, :], 0.0)
    value = qkvg[:, 2 * D : 3 * D]
    low[:, 2 * D : 3 * D] = (k.ck(0) * here + k.ck(1) * one + k.ck(2) * two).astype(bf16)
    k.push("low")

    taps = [jnp.sum(rows * value, axis=0, keepdims=True) for rows in (here, one, two)]
    rest = jnp.concatenate([grad_bd, jnp.zeros((1, D - LANES), f32)], axis=1)
    k.sums[...] = jnp.concatenate([*taps, rest, jnp.zeros((4, D), f32)], axis=0)

    ordered_t = jnp.transpose(k.ordered()[...].astype(f32)).astype(bf16)
    gwo = k.gwo()
    gw = k.gw

    def weights(j, carry):
        part = pl.ds(pl.multiple_of(j * HALF, HALF), HALF)
        gw[:, part] = mm(ordered_t, low[:, part])
        return carry

    lax.fori_loop(0, QKVG // HALF, weights, 0)
    gw[:, QKVG : QKVG + D] = gwo[...]
    gw[:, QKVG + D :] = mm(ordered_t, low[:, QKVG:])

    def halves(j, carry):
        here = pl.ds(pl.multiple_of(j * HALF, HALF), HALF)
        keep = pl.ds(pl.multiple_of(j * HALF + k.section * GROUP, HALF), HALF)
        send = pl.ds(pl.multiple_of(j * HALF + (1 - k.section) * GROUP, HALF), HALF)
        k.gw_keep[:, here] = gw[:, keep]
        k.gw_send[:, here] = gw[:, send].astype(bf16)
        return carry

    lax.fori_loop(0, GROUP // HALF, halves, 0)


def input_backward_body(k):
    flip = k.layer == 1
    wide = k.wide
    gmod, mixed_s, perm_s = k.gmod, k.mixed_s, k.perm_s
    gmod[...] = jnp.zeros(gmod.shape, f32)
    low, w_qk, w_vgd = k.low(), k.w_qk(), k.w_vgd()

    def inner_grad(i, carry):
        rows = pl.ds(pl.multiple_of(i * HALF, HALF), HALF)
        mixed_s[rows, :] = mm_t(low[rows, : 2 * D], w_qk[...]) + mm_t(
            low[rows, 2 * D :], w_vgd[...]
        )
        return carry

    lax.fori_loop(0, 2, inner_grad, 0)
    if flip:
        high, middle, rest = split_three(mixed_s[...])
        perm_s[:, :D] = high
        perm_s[:, D : 2 * D] = middle
        perm_s[:, 2 * D :] = rest
    x, mid_grad = k.x(), k.mid_grad()
    k.mods()

    def tile(i, carry):
        start = pl.multiple_of(i * HALF, HALF)
        rows = pl.ds(start, HALF)
        slot = k.slot(i)
        if flip:
            three = mm(order_matrix(start, HALF, wide, False), perm_s[...])
            grad = three[:, :D] + three[:, D : 2 * D] + three[:, 2 * D :]
        else:
            grad = mixed_s[rows, :]
        normal, rate = normalise(x[rows, :].astype(f32))
        where = (pl.ds(slot, 1), slice(0, D))
        gmod[where] = gmod[where] + jnp.sum(grad, axis=0, keepdims=True)
        where = (pl.ds(slot, 1), slice(D, 2 * D))
        gmod[where] = gmod[where] + jnp.sum(grad * normal, axis=0, keepdims=True)
        total = mid_grad[rows, :] + normalise_back(normal, rate, grad * (1.0 + k.share(slot, 1)))
        k.gx[rows, :] = total
        k.gx_low[rows, :] = total.astype(bf16)
        return carry

    lax.fori_loop(0, 2, tile, 0)
    k.push("gx_low")
    k.push("gx")
    ffn, mixer = k.ffn_sums(), k.mixer_sums()
    k.mod_low[...] = jnp.concatenate([gmod[...], ffn[...]], axis=1).astype(bf16)
    half = 2 * D
    rest = ffn[0:1, :] + ffn[1:2, :]
    k.sums[...] = jnp.concatenate(
        [
            gmod[0:1, :] + gmod[1:2, :],
            rest[:, :half],
            rest[:, half:],
            ffn[2:3, :half],
            ffn[2:3, half:],
            jnp.concatenate([ffn[3:4, :D], mixer[0:1, :]], axis=1),
            jnp.concatenate([mixer[1:2, :], mixer[2:3, :]], axis=1),
            jnp.concatenate([mixer[3:4, :], jnp.zeros((1, D), f32)], axis=1),
        ],
        axis=0,
    )


ANY = pl.BlockSpec(memory_space=pl.ANY)
VMEM = pl.BlockSpec(memory_space=pltpu.VMEM)
HBM = pl.BlockSpec(memory_space=pltpu.HBM)


def call(body, layer, layouts, ins, outs, scratch, flops):
    arrays = []
    counts = []
    kept = []
    places = []
    for kind, given, part in ins.values():
        places.extend([ANY] * 2 if kind == "own" else [HBM])
        given = given if kind == "own" else (given,)
        arrays.extend(given)
        counts.append(len(given))
        rows, wide = given[0].shape[-2:]
        start, stop = part or (0, wide)
        kept.append(pltpu.VMEM((rows, stop - start), given[0].dtype))

    def kernel(*refs):
        refs = list(refs)
        take = lambda count: [refs.pop(0) for _ in range(count)]
        (layouts_ref,) = take(1)
        sources = [take(count) for count in counts]
        targets = take(len(outs))
        buffers = take(len(ins))
        results = take(len(outs))
        rest = take(len(scratch))
        in_sems, out_sems = refs
        k = Kernel(layer, layouts_ref)
        for number, (name, (kind, _, part)) in enumerate(ins.items()):
            given = sources[number]
            if part is not None:
                given = [ref.at[:, part[0] : part[1]] for ref in given]
            setattr(k, name, k.load(kind, given, buffers[number], in_sems.at[number]))
        k.results = {}
        for number, name in enumerate(outs):
            setattr(k, name, results[number])
            k.results[name] = (results[number], targets[number], out_sems.at[number])
        for name, ref in zip(scratch, rest):
            setattr(k, name, ref)
        body(k)
        k.finish()

    return pl.pallas_call(
        kernel,
        out_shape=[jax.ShapeDtypeStruct(shape, kind) for shape, kind, _ in outs.values()],
        in_specs=[pl.BlockSpec(memory_space=pltpu.SMEM)] + places,
        out_specs=[HBM if for_kernel else ANY for _, _, for_kernel in outs.values()],
        scratch_shapes=kept
        + [pltpu.VMEM(shape, kind) for shape, kind, _ in outs.values()]
        + [pltpu.VMEM(shape, kind) for shape, kind in scratch.values()]
        + [pltpu.SemaphoreType.DMA((len(ins),)), pltpu.SemaphoreType.DMA((len(outs),))],
        compiler_params=pltpu.CompilerParams(vmem_limit_bytes=56 * 1024 * 1024),
        cost_estimate=pl.CostEstimate(flops=flops, bytes_accessed=4 << 20, transcendentals=0),
    )(layouts, *arrays)


def own(pair, part=None):
    return ("own", pair, part)


def plain(array):
    return ("plain", array, None)


def micro(array):
    return ("micro", array, None)


AT_UP = (0, FF)
AT_QK = (FF, FF + 2 * D)
AT_OUT = (FF + 2 * D, FF + 3 * D)


def attn_forward(layer, layouts, x, mods, small, packed, vgd):
    return call(
        attn_forward_body,
        layer,
        layouts,
        dict(
            x=micro(x),
            mods=own(mods),
            w_qk=own(packed, AT_QK),
            w_vgd=own(vgd),
            small=own(small),
        ),
        dict(
            ordered=((ROWS, D), bf16, True),
            qkvg=((ROWS, QKVG), f32, True),
            dp=((ROWS, LANES), f32, True),
            vc=((ROWS, D), f32, True),
            cum=((ROWS, LANES), f32, True),
            cumt=((LANES, ROWS), f32, True),
            o=((ROWS, D), f32, True),
            gated=((ROWS, D), bf16, True),
        ),
        dict(
            inner=((ROWS, D), bf16),
            vpad=((ROWS + 8, D), f32),
            bias=((HALF, ROWS), f32),
        ),
        8 * 10**9,
    )


def ffn_forward(layer, layouts, x, mods, small, gated, packed, down):
    return call(
        ffn_forward_body,
        layer,
        layouts,
        dict(
            gated=plain(gated),
            x=micro(x),
            wo=own(packed, AT_OUT),
            mods=own(mods),
            small=own(small),
            wu=own(packed, AT_UP),
            wn=own(down),
        ),
        dict(
            out=((ROWS, D), bf16, True),
            branch=((ROWS, D), f32, True),
            down=((ROWS, D), f32, True),
        ),
        {},
        5 * 10**9,
    )


def ffn_backward(layer, layouts, x, mods, small, gated, branch, down_raw, grad, packed, down):
    return call(
        ffn_backward_body,
        layer,
        layouts,
        dict(
            mods=own(mods),
            small=own(small),
            x=micro(x),
            grad=micro(grad),
            branch=plain(branch),
            down=plain(down_raw),
            wu=own(packed, AT_UP),
            wn=own(down),
            gated=plain(gated),
        ),
        dict(
            mid_grad=((ROWS, D), f32, True),
            branch_low=((ROWS, D), bf16, True),
            gwo=((D, D), f32, True),
            gwu_keep=((D, FF // 2), f32, False),
            gwu_send=((D, FF // 2), bf16, False),
            gwn=((FF, D), f32, False),
            sums=((8, FF), f32, True),
        ),
        dict(
            hidden_s=((ROWS, FF), bf16),
            inner_s=((ROWS, D), bf16),
            up_s=((ROWS, FF), bf16),
            down_s=((ROWS, D), bf16),
            gmod=((8, FF), f32),
            gbu=((1, FF), f32),
            gbn=((1, D), f32),
        ),
        12 * 10**9,
    )


def mixer_backward(layer, layouts, small, saved, branch_low, gwo, packed):
    ordered, qkvg, dp, vc, cum, cumt, o = saved
    return call(
        mixer_backward_body,
        layer,
        layouts,
        dict(
            branch_low=plain(branch_low),
            wo=own(packed, AT_OUT),
            qkvg=plain(qkvg),
            vc=plain(vc),
            cum=plain(cum),
            cumt=plain(cumt),
            o=plain(o),
            small=own(small),
            dp=plain(dp),
            ordered=plain(ordered),
            gwo=plain(gwo),
        ),
        dict(
            low=((ROWS, QKVG + LANES), bf16, True),
            gw_keep=((D, GROUP), f32, False),
            gw_send=((D, GROUP), bf16, False),
            sums=((8, D), f32, True),
        ),
        dict(
            mixed_s=((ROWS, D), f32),
            dv_s=((ROWS + 8, D), f32),
            rows_s=((ROWS, LANES), f32),
            cols_s=((LANES, ROWS), f32),
            bias=((HALF, ROWS), f32),
            gw=((D, 2 * GROUP), f32),
        ),
        15 * 10**9,
    )


def input_backward(layer, layouts, x, mods, low, mid_grad, ffn_sums, mixer_sums, packed, vgd):
    return call(
        input_backward_body,
        layer,
        layouts,
        dict(
            low=plain(low),
            w_qk=own(packed, AT_QK),
            w_vgd=own(vgd),
            x=micro(x),
            mid_grad=plain(mid_grad),
            mods=own(mods),
            ffn_sums=plain(ffn_sums),
            mixer_sums=plain(mixer_sums),
        ),
        dict(
            gx=((ROWS, D), f32, False),
            gx_low=((ROWS, D), bf16, True),
            mod_low=((8, 6 * D), bf16, False),
            sums=((8, 2 * D), f32, False),
        ),
        dict(
            mixed_s=((ROWS, D), f32),
            perm_s=((ROWS, 3 * D), bf16),
            gmod=((8, 2 * D), f32),
        ),
        4 * 10**9,
    )


def small_kernel(b_up, b_down, taps, b_decay, packed):
    packed[...] = jnp.zeros(packed.shape, f32)
    packed[0:1, :] = b_up[...]
    packed[1:2, :D] = b_down[...]
    packed[2:5, :D] = taps[0]
    packed[5:6, :HEADS] = b_decay[...]


def pack_small(b_up, b_down, taps, b_decay):
    return pl.pallas_call(
        small_kernel,
        out_shape=jax.ShapeDtypeStruct((8, FF), f32),
        in_specs=[VMEM] * 4,
        out_specs=VMEM,
    )(b_up, b_down, taps, b_decay)


def pack_kernel(*refs):
    packed = refs[-1]
    at = 0
    for ref in refs[:-1]:
        width = ref.shape[1]
        if width % LANES:
            packed[:, at:] = jnp.zeros((packed.shape[0], packed.shape[1] - at), packed.dtype)
        packed[:, at : at + width] = ref[...]
        at += width


def pack(*arrays):
    total = sum(-(-array.shape[1] // LANES) * LANES for array in arrays)
    return pl.pallas_call(
        pack_kernel,
        out_shape=jax.ShapeDtypeStruct((arrays[0].shape[0], total), arrays[0].dtype),
        in_specs=[VMEM] * len(arrays),
        out_specs=VMEM,
    )(*arrays)


def swap(values):
    return lax.ppermute(values, "section", [(0, 1), (1, 0)])


def row_bits():
    bits = lax.axis_size("row").bit_length() - 1
    third = bits // 3
    return (
        tuple(range(third)),
        tuple(range(third, 2 * third)),
        tuple(range(2 * third, bits)),
    )


def partner(values, bit):
    size = lax.axis_size("row")
    return lax.ppermute(values, "row", [(i, i ^ (1 << bit)) for i in range(size)])


def axis_of(bit):
    return lax.axis_size("row").bit_length() - 2 - bit


def bit_of(bit):
    return (lax.axis_index("row") >> bit) & 1


def single(values):
    return values.reshape((1,) * (lax.axis_size("row").bit_length() - 1) + values.shape)


def join(held, other, bit):
    return jnp.where(
        bit_of(bit) == 0,
        jnp.concatenate([held, other], axis=axis_of(bit)),
        jnp.concatenate([other, held], axis=axis_of(bit)),
    )


def flat(held):
    return held.reshape(-1, held.shape[-1])


def by_bits(values):
    bits = lax.axis_size("row").bit_length() - 1
    return values.reshape((2,) * bits + values.shape[1:])


def cut(held, bit):
    axis = axis_of(bit)
    mine = bit_of(bit)
    sent = lax.dynamic_index_in_dim(held, 1 - mine, axis, keepdims=True)
    kept = lax.dynamic_index_in_dim(held, mine, axis, keepdims=True)
    return sent, kept


def lock(*arrays):
    return lax.optimization_barrier(arrays)


class Scatter:
    def __init__(self, values):
        self.held = by_bits(values)
        self.kept = None

    def ready(self, bit):
        sent, self.kept = cut(self.held, bit)
        return sent.astype(bf16)

    def take(self, other):
        self.held = self.kept + other.astype(f32)

    def result(self):
        return self.held.reshape(self.held.shape[-2:])


class Gather:
    def __init__(self, values):
        self.held = single(values)

    def ready(self, bit):
        self.bit = bit
        return self.held

    def take(self, other):
        self.held = join(self.held, other, self.bit)


class Total:
    def __init__(self, values):
        self.held = values

    def ready(self, bit):
        return self.held

    def take(self, other):
        self.held = self.held + other


def begin(chains, bit):
    return [chain.ready(bit) for chain in chains]


def send(arrays, bit):
    return [partner(array, bit) for array in arrays]


def end(chains, arrays):
    for chain, array in zip(chains, arrays):
        chain.take(array)


def on_device(
    tokens, conditions, output_grad, layouts,
    w_ada, b_ada, w_query, w_key, w_value, w_gate, w_out, w_decay, b_decay, conv_kernel,
    w_up, b_up, w_down, b_down,
):
    section = lax.axis_index("section")
    devices = lax.axis_size("row")
    is_first = section == 0
    shard = w_query.shape[1]
    along_x, along_y, along_z = row_bits()
    plane = along_x + along_y
    every = plane + along_z

    def pick(pair):
        return jnp.where(is_first, pair[0], pair[1])

    def pick_other(pair):
        return jnp.where(is_first, pair[1], pair[0])

    def both(values):
        return values, swap(values)

    def groups(run):
        rest = [bit for bit in every if bit not in run]
        numbers = lambda bits: [
            sum(((i >> place) & 1) << bit for place, bit in enumerate(bits))
            for i in range(1 << len(bits))
        ]
        return [[base + step for step in numbers(run)] for base in numbers(rest)]

    ada = lax.all_gather(w_ada[0], "row", axis_index_groups=groups(along_z), tiled=True)
    ada = lax.all_gather(ada, "row", axis_index_groups=groups(plane), tiled=True)
    height, width = 1 << len(along_z), 1 << len(plane)

    group_a = [Gather(pack(w_up[0], w_query[0], w_key[0], w_out[0]))]
    group_b = [Gather(pack(w_value[0], w_gate[0], w_decay[0])), Gather(w_down[0])]
    chains = group_a + group_b
    for bit in reversed(along_z):
        end(chains, lock(*send(begin(chains, bit), bit)))
    for bit_a, bit_b in zip(plane, along_y + along_x):
        others_a = send(begin(group_a, bit_a), bit_a)
        others_b = send(begin(group_b, bit_b), bit_b)
        others = lock(*others_a, *others_b)
        end(chains, others)
    packed, vgd, down = [both(flat(chain.held)) for chain in chains]

    lifted_own = jax.nn.silu(conditions.astype(f32)).astype(bf16).reshape(MICRO * SLOTS, D)
    lifted_cut = lifted_own.reshape(MICRO * SLOTS, height, width, shard).swapaxes(1, 2)
    mods = both(mm(lifted_cut.reshape(MICRO * SLOTS, D), ada) + b_ada[0])
    smalls = both(pack_small(b_up, b_down, conv_kernel, b_decay))

    late, _ = lock(lifted_own, mods[0])
    lifted_rows = Gather(late)
    for bit in reversed(every):
        end([lifted_rows], send(begin([lifted_rows], bit), bit))
    lifted_rows = lax.dynamic_slice_in_dim(
        flat(lifted_rows.held), lax.axis_index("row") * shard, shard, 1
    )

    x = tokens
    kept = []
    acts = []
    for l in range(2):
        *saved, gated = attn_forward(l, layouts, x, mods, smalls, packed, vgd)
        out, branch, down_raw = ffn_forward(l, layouts, x, mods, smalls, gated, packed, down)
        kept.append((x, saved, gated, branch, down_raw))
        acts.append(out)
        x = out[None]

    def ffn_step(l, grad):
        x, saved, gated, branch, down_raw = kept[l]
        mid_grad, branch_low, gwo, keep, sent, gwn, sums = ffn_backward(
            l, layouts, x, mods, smalls, gated, branch, down_raw, grad, packed, down
        )
        pair = gwn.reshape(devices, 2, FF // devices // 2, D)
        down_keep = lax.dynamic_index_in_dim(pair, section, 1, keepdims=False)
        down_send = lax.dynamic_index_in_dim(pair, 1 - section, 1, keepdims=False).astype(bf16)
        return (branch_low, gwo), mid_grad, (sent, down_send), (keep, down_keep), sums

    def mixer_step(l, carried):
        return mixer_backward(l, layouts, smalls, kept[l][1], *carried, packed)

    def input_step(l, low, mid_grad, ffn_sums, mixer_sums):
        return input_backward(
            l, layouts, kept[l][0], mods, low, mid_grad, ffn_sums, mixer_sums, packed, vgd
        )

    def ffn_chains(keep, others):
        up_half = keep[0] + others[0].astype(f32)
        down_half = keep[1] + others[1].astype(f32)
        return [Scatter(up_half.reshape(devices, shard, FF // 2)), Scatter(down_half)]

    def attn_chain(keep, other):
        return [Scatter((keep + other.astype(f32)).reshape(devices, shard, GROUP))]

    def steps(chains, bits):
        for bit in bits[:-1]:
            end(chains, send(begin(chains, bit), bit))
        return begin(chains, bits[-1])

    def divide(arrays, *counts):
        parts = []
        for count in counts:
            parts.append(list(arrays[:count]))
            arrays = arrays[count:]
        return parts

    x_bits, y_bits, z_bits = along_x, along_y, along_z
    carried, mid_grad, f2_send, f2_keep, f2_sums = ffn_step(1, output_grad)
    acts_send = pick_other(acts)
    *carried, acts_send, s0, s1 = lock(*carried, acts_send, *f2_send)
    f2_other = [swap(s0), swap(s1)]
    acts_other = swap(acts_send)
    low, a2_keep, a2_send, m2_sums = mixer_step(1, carried)
    low, acts_other, *f2_other = lock(low, acts_other, *f2_other)
    f2 = ffn_chains(f2_keep, f2_other)
    f2_sent = steps(f2, x_bits)
    low, a2_send, *f2_sent = lock(low, a2_send, *f2_sent)
    f2_other = send(f2_sent, x_bits[-1])
    a2_other = swap(a2_send)
    gx_two, grad, mod_low_two, sums_two = input_step(1, low, mid_grad, f2_sums, m2_sums)
    grad, a2_other, mod_low_two = lock(grad, a2_other, mod_low_two[:SLOTS])
    a2 = attn_chain(a2_keep, a2_other)
    mod2 = [Gather(mod_low_two)]
    a2_sent = steps(a2 + mod2, x_bits)
    grad, *a2_sent = lock(grad, *a2_sent)
    a2_other = send(a2_sent, x_bits[-1])

    carried, mid_grad, f1_send, f1_keep, f1_sums = ffn_step(0, grad[None])
    locked = lock(*carried, *f1_send, *f2_other, *a2_other)
    carried, f1_send, locked = divide(locked, 2, 2, 4)
    f1_other = lock(*[swap(array) for array in f1_send])
    two = f2 + a2 + mod2
    end(two, locked)
    two_sent = steps(two, y_bits)
    f1 = ffn_chains(f1_keep, f1_other)
    f1_sent = steps(f1, x_bits)
    carried, two_sent, f1_sent = divide(lock(*carried, *two_sent, *f1_sent), 2, 4, 2)
    two_other = send(two_sent, y_bits[-1])
    f1_other = send(f1_sent, x_bits[-1])
    low, a1_keep, a1_send, m1_sums = mixer_step(0, carried)
    low, *locked = lock(low, *two_other, *f1_other)
    end(two + f1, locked)
    two_sent = steps(two, z_bits)
    f1_sent = steps(f1, y_bits)
    low, a1_send, *locked = lock(low, a1_send, *two_sent, *f1_sent)
    two_sent, f1_sent = divide(locked, 4, 2)
    a1_other = swap(a1_send)
    two_other = send(two_sent, z_bits[-1])
    f1_other = send(f1_sent, y_bits[-1])
    gx_one, _, mod_low_one, sums_one = input_step(0, low, mid_grad, f1_sums, m1_sums)
    gx_send = pick_other((gx_one, gx_two))
    mod_low_one = mod_low_one[:SLOTS]
    a1_other, mod_low_one, sums_one, gx_send, *locked = lock(
        a1_other, mod_low_one, sums_one, gx_send, *two_other, *f1_other
    )
    end(two + f1, locked)
    mod1 = [Gather(mod_low_one)]
    totals = [Total(jnp.concatenate([sums_one, sums_two], axis=0))]
    one = attn_chain(a1_keep, a1_other) + mod1 + totals
    gx_other = swap(gx_send)
    mod_other = swap(pick_other((mod_low_one, mod_low_two)))
    for bit in plane:
        end(one, lock(*send(begin(one, bit), bit)))
    one = one + f1
    for bit in z_bits:
        end(one, lock(*send(begin(one, bit), bit)))

    lifted_mine = lax.dynamic_index_in_dim(
        lifted_rows.reshape(devices, MICRO, SLOTS, shard), section, 1, keepdims=False
    ).reshape(devices * SLOTS, shard)

    def summed(ffn, attn, mod, total):
        ada_term = lax.dot_general(
            lifted_mine, flat(mod.held), (((0,), (0,)), ((), ())), preferred_element_type=f32
        )
        return [attn.result(), ffn[0].result(), ffn[1].result(), ada_term, total]

    total = totals[0].held
    sums = (
        summed(f1, one[0], mod1[0], total[:8]),
        summed(f2, a2[0], mod2[0], total[8:]),
    )
    mine = [pick(pair) for pair in zip(*sums)]
    other = [swap(pick_other(pair)) for pair in zip(*sums)]

    def halves(number, axis):
        mine_half, other_half = mine[number], other[number]
        return jnp.concatenate(
            [pick((mine_half, other_half)), pick_other((mine_half, other_half))], axis=axis
        )

    attn_total = halves(0, 1)
    up_total = halves(1, 1)
    down_total = halves(2, 0)
    grad_w_ada = mine[3] + other[3]
    small = mine[4] + other[4]

    mod_own = pick((mod_low_one, mod_low_two))
    mod_both = jnp.concatenate([pick((mod_own, mod_other)), pick_other((mod_own, mod_other))])
    grad_lifted = mm_t(mod_both, ada)
    grad_lifted = (grad_lifted + swap(grad_lifted)).reshape(MICRO * SLOTS, width, height, shard)
    grad_lifted = grad_lifted.swapaxes(1, 2).reshape(MICRO, SLOTS, D)
    _, pull_silu = jax.vjp(jax.nn.silu, conditions.astype(f32))
    (cond_grads,) = pull_silu(grad_lifted)

    def assembled(pair, other):
        mine = pick(pair)
        return jnp.stack([pick((mine, other)), pick_other((mine, other))])

    return (
        assembled(acts, acts_other)[None],
        assembled((gx_one, gx_two), gx_other)[None],
        cond_grads,
        grad_w_ada[None],
        small[0:3].reshape(1, 6 * D),
        attn_total[None, :, :D],
        attn_total[None, :, D : 2 * D],
        attn_total[None, :, 2 * D : 3 * D],
        attn_total[None, :, 3 * D : 4 * D],
        attn_total[None, :, 4 * D : 5 * D],
        attn_total[None, :, 5 * D : 5 * D + HEADS],
        small[7:8, :HEADS],
        jnp.concatenate([small[5, D:], small[6]]).reshape(1, 3, D),
        up_total[None],
        small[3:5].reshape(1, FF),
        down_total[None],
        small[5:6, :D],
    )


def solution(mesh):
    rows = P(None, "row", None)
    mats = P("section", "row", None)
    vector = P("section", None)
    in_specs = (
        rows, rows, rows, P(None, "row"),
        mats, vector, mats, mats, mats, mats, mats, mats, vector, P("section", None, None),
        mats, vector, mats, vector,
    )
    blocks = P("section", None, "row", None)
    out_specs = (
        blocks, blocks, rows,
        mats, vector, mats, mats, mats, mats, mats, mats, vector, P("section", None, None),
        mats, vector, mats, vector,
    )
    return jax.shard_map(
        on_device, mesh=mesh, in_specs=in_specs, out_specs=out_specs, check_vma=False
    )
```

```python
import functools

import jax
import jax.numpy as jnp
from jax import lax
from jax.experimental import pallas as pl
from jax.experimental.pallas import tpu as pltpu
from jax.sharding import PartitionSpec as P

D = 384
HEADS = 6
HEAD_DIM = 64
FF = 1536
MICRO = 2
ROWS = 512
HALF = 256
SLOTS = 2
PAIR = 128
PAIRS = D // PAIR
QKVG = 4 * D
LANES = 128
GROUP = (QKVG + D + LANES) // 2
NEG = -1e30
SCALE = HEAD_DIM**-0.5

bf16 = jnp.bfloat16
f32 = jnp.float32


def mm(left, right):
    return jnp.dot(left, right, preferred_element_type=f32)


def mm_t(left, right):
    return lax.dot_general(left, right, (((1,), (1,)), ((), ())), preferred_element_type=f32)


def split(values):
    high = values.astype(bf16)
    return high, (values - high.astype(f32)).astype(bf16)


def split_three(values):
    high, rest = split(values)
    mid = values - high.astype(f32)
    middle, low = split(mid)
    return high, middle, low


def cat_left(values):
    high, low = split(values)
    return jnp.concatenate([high, low, high], axis=1)


def cat_right(values):
    high, low = split(values)
    return jnp.concatenate([high, high, low], axis=1)


def mm_near(left, right_pair, right_high):
    high, low = split(left)
    wide = mm(high, right_pair)
    return wide[:, :PAIR] + wide[:, PAIR:] + mm(low, right_high)


def lane_iota(rows, columns):
    return lax.broadcasted_iota(jnp.int32, (rows, columns), 1)


def row_iota(rows, columns):
    return lax.broadcasted_iota(jnp.int32, (rows, columns), 0)


def order_matrix(start, rows, wide, to_scan):
    t = row_iota(rows, ROWS) + start
    small = (t & 256) + ((t & 15) << 4) + ((t & 255) >> 4)
    if to_scan:
        large = ((t & 15) << 5) + (t >> 4)
    else:
        large = ((t & 31) << 4) + (t >> 5)
    source = jnp.where(wide, large, small)
    return jnp.where(lane_iota(rows, ROWS) == source, 1.0, 0.0).astype(bf16)


def normalise(values):
    centred = values - jnp.mean(values, axis=-1, keepdims=True)
    rate = lax.rsqrt(jnp.mean(centred * centred, axis=-1, keepdims=True) + 1e-06)
    return centred * rate, rate


def normalise_back(normal, rate, grad):
    return rate * (
        grad
        - jnp.mean(grad, axis=-1, keepdims=True)
        - normal * jnp.mean(grad * normal, axis=-1, keepdims=True)
    )


class In:
    def __init__(self, copy, kept):
        self.copy = copy
        self.kept = kept

    def __call__(self):
        if self.copy is not None:
            self.copy.wait()
            self.copy = None
        return self.kept


class Kernel:
    def __init__(self, layer, layouts):
        self.layer = layer
        self.section = lax.axis_index("section")
        self.own = self.section == layer
        self.layout = layouts[self.section, 0]
        self.wide = self.layout == 0
        self.live_rows = jnp.where(self.wide, ROWS, self.layout * HALF)
        self.pushed = {}

    def load(self, kind, refs, kept, sem):
        if kind == "own":
            mine, other = refs

            @pl.when(self.own)
            def _():
                pltpu.make_async_copy(mine, kept, sem).start()

            @pl.when(jnp.logical_not(self.own))
            def _():
                pltpu.make_async_copy(other, kept, sem).start()

            return In(pltpu.make_async_copy(mine, kept, sem), kept)
        (source,) = refs
        if kind == "micro":
            source = source.at[self.section if source.shape[0] == MICRO else 0]
        copy = pltpu.make_async_copy(source, kept, sem)
        copy.start()
        return In(copy, kept)

    def push(self, name):
        kept, target, sem = self.results[name]
        copy = pltpu.make_async_copy(kept, target, sem)
        copy.start()
        self.pushed[name] = copy

    def finish(self):
        for name in self.results:
            if name not in self.pushed:
                self.push(name)
        for copy in self.pushed.values():
            copy.wait()

    def slot(self, half):
        return jnp.where(self.wide, 0, half)

    def share(self, slot, part):
        row = pl.ds(2 * self.section + slot, 1)
        return self.mods()[row, part * D : (part + 1) * D]

    def bu(self):
        return self.small()[0:1, :]

    def bn(self):
        return self.small()[1:2, :D]

    def ck(self, tap):
        return self.small()[2 + tap : 3 + tap, :D]

    def bd(self):
        return self.small()[5:6, :LANES]


def sigmoid(values):
    return 1.0 / (1.0 + jnp.exp(-values))


GELU_A = 0.7978845608028654
GELU_B = 0.044715


def gelu_parts(values):
    square = values * values
    tanh = jnp.tanh(GELU_A * values * (1.0 + GELU_B * square))
    return square, tanh


def fill_bias(bias, wide):
    bias[:, :HALF] = jnp.full((HALF, HALF), 0.0, f32) + jnp.where(wide, 0.0, NEG)
    causal = row_iota(HALF, HALF) >= lane_iota(HALF, HALF)
    bias[:, HALF:] = jnp.where(causal, 0.0, NEG)


def decay_factors(cum, cumt, bias, head):
    row = cumt[pl.ds(head, 1), :]
    lanes = lane_iota(1, LANES)
    column = jnp.sum(jnp.where(lanes == head, cum[...], 0.0), axis=1, keepdims=True)
    first = jnp.exp(column[:HALF] - row[:, :HALF] + bias[:, HALF:])
    second = jnp.exp(column[HALF:] - row + bias[...])
    return first, second


def head_norm(values, lanes):
    square = values * values
    low = jnp.sum(jnp.where(lanes < HEAD_DIM, square, 0.0), axis=1, keepdims=True)
    high = jnp.sum(jnp.where(lanes < HEAD_DIM, 0.0, square), axis=1, keepdims=True)
    return jnp.where(lanes < HEAD_DIM, low, high) * (1.0 / HEAD_DIM)


def fill_decay(dp, bd, cum, cumt):
    raw = dp[...] + bd
    log_decay = (jnp.minimum(raw, 0.0) - jnp.log1p(jnp.exp(-jnp.abs(raw)))) * (1.0 / 16.0)
    high, middle, low = split_three(log_decay)
    causal = jnp.where(row_iota(ROWS, ROWS) >= lane_iota(ROWS, ROWS), 1.0, 0.0).astype(bf16)
    cum[...] = mm(causal, high) + mm(causal, middle) + mm(causal, low)
    cumt[...] = jnp.transpose(cum[...])


def columns(index, first=0):
    return pl.ds(pl.multiple_of(index * PAIR + first, PAIR), PAIR)


def attn_forward_body(k):
    flip = k.layer == 1
    wide = k.wide
    x = k.x()
    k.mods()

    def first(i, carry):
        rows = pl.ds(pl.multiple_of(i * HALF, HALF), HALF)
        slot = k.slot(i)
        normal, _ = normalise(x[rows, :].astype(f32))
        k.inner[rows, :] = (normal * (1.0 + k.share(slot, 1)) + k.share(slot, 0)).astype(bf16)
        return carry

    lax.fori_loop(0, 2, first, 0)
    w_qk = k.w_qk()
    w_vgd = k.w_vgd()

    def project(i, carry):
        start = pl.multiple_of(i * HALF, HALF)
        rows = pl.ds(start, HALF)
        if flip:
            part = mm(order_matrix(start, HALF, wide, True), k.inner[...]).astype(bf16)
        else:
            part = k.inner[rows, :]
        k.ordered[rows, :] = part
        k.qkvg[rows, : 2 * D] = mm(part, w_qk[...])
        k.qkvg[rows, 2 * D :] = mm(part, w_vgd[:, : 2 * D])
        k.dp[rows, :] = mm(part, w_vgd[:, 2 * D :])
        return carry

    lax.fori_loop(0, 2, project, 0)
    k.small()
    for name in ("ordered", "qkvg", "dp"):
        k.push(name)
    fill_decay(k.dp, k.bd(), k.cum, k.cumt)
    fill_bias(k.bias, wide)

    vpad = k.vpad
    vpad[0:8, :] = jnp.zeros((8, D), f32)
    vpad[8 : 8 + ROWS, :] = k.qkvg[:, 2 * D : 3 * D]
    position = row_iota(ROWS, 1) & jnp.where(wide, ROWS - 1, HALF - 1)
    one = jnp.where(position >= 1, vpad[7 : 7 + ROWS, :], 0.0)
    two = jnp.where(position >= 2, vpad[6 : 6 + ROWS, :], 0.0)
    k.vc[...] = k.ck(0) * vpad[8 : 8 + ROWS, :] + k.ck(1) * one + k.ck(2) * two
    for name in ("cum", "cumt", "vc"):
        k.push(name)

    def pair(p, carry):
        lanes = lane_iota(1, PAIR)
        queries = cat_left(k.qkvg[:, columns(p)] * SCALE)
        keys = k.qkvg[:, columns(p, D)]
        value_high, value_low = split(k.vc[:, columns(p)])
        values = jnp.concatenate([value_high, value_low], axis=1)
        parts = []
        for e in range(2):
            key_cat = cat_right(jnp.where((lanes // HEAD_DIM) == e, keys, 0.0))
            first, second = decay_factors(k.cum, k.cumt, k.bias, 2 * p + e)
            first = first * mm_t(queries[:HALF], key_cat[:HALF])
            second = second * mm_t(queries[HALF:], key_cat)
            parts.append(
                jnp.concatenate(
                    [
                        mm_near(first, values[:HALF], value_high[:HALF]),
                        mm_near(second, values, value_high),
                    ],
                    axis=0,
                )
            )
        total = jnp.where(lanes < HEAD_DIM, parts[0], parts[1])
        k.o[:, columns(p)] = total
        gate = k.qkvg[:, columns(p, 3 * D)]
        normed = total * lax.rsqrt(head_norm(total, lanes) + 1.0)
        mixed = (normed * (gate * sigmoid(gate))).astype(bf16)
        if flip:
            k.inner[:, columns(p)] = mixed
        else:
            k.gated[:, columns(p)] = mixed
        return carry

    lax.fori_loop(0, PAIRS, pair, 0)
    k.push("o")
    if flip:

        def back(i, carry):
            start = pl.multiple_of(i * HALF, HALF)
            k.gated[pl.ds(start, HALF), :] = mm(
                order_matrix(start, HALF, wide, False), k.inner[...]
            ).astype(bf16)
            return carry

        lax.fori_loop(0, 2, back, 0)


def ffn_forward_body(k):
    gated, x, wo = k.gated(), k.x(), k.wo()
    k.mods(), k.small()
    wu, wn = k.wu(), k.wn()

    def tile(i, carry):
        start = pl.multiple_of(i * HALF, HALF)
        rows = pl.ds(start, HALF)
        slot = k.slot(i)
        grown = mm(gated[rows, :], wo[...])
        k.branch[rows, :] = grown
        middle = x[rows, :].astype(f32) + k.share(slot, 2) * grown
        normal, _ = normalise(middle)
        inner = (normal * (1.0 + k.share(slot, 4)) + k.share(slot, 3)).astype(bf16)
        up = mm(inner, wu[...]) + k.bu()
        _, tanh = gelu_parts(up)
        hidden = (0.5 * up * (1.0 + tanh)).astype(bf16)
        low = mm(hidden, wn[...])
        k.down[rows, :] = low
        result = middle + k.share(slot, 5) * (low + k.bn())
        live = (row_iota(HALF, 1) + start) < k.live_rows
        k.out[rows, :] = jnp.where(live, result, 0.0).astype(bf16)
        return carry

    lax.fori_loop(0, 2, tile, 0)


def ffn_backward_body(k):
    gmod, gbu, gbn = k.gmod, k.gbu, k.gbn
    gmod[...] = jnp.zeros(gmod.shape, f32)
    gbu[...] = jnp.zeros(gbu.shape, f32)
    gbn[...] = jnp.zeros(gbn.shape, f32)
    k.mods(), k.small()
    x, grad, branch, down = k.x(), k.grad(), k.branch(), k.down()
    wu, wn = k.wu(), k.wn()

    def tile(i, carry):
        start = pl.multiple_of(i * HALF, HALF)
        rows = pl.ds(start, HALF)
        slot = k.slot(i)

        def add(part, values):
            where = (pl.ds(slot, 1), slice((part - 2) * D, (part - 1) * D))
            gmod[where] = gmod[where] + jnp.sum(values, axis=0, keepdims=True)

        grown = branch[rows, :]
        middle = x[rows, :].astype(f32) + k.share(slot, 2) * grown
        normal, rate = normalise(middle)
        inner = (normal * (1.0 + k.share(slot, 4)) + k.share(slot, 3)).astype(bf16)
        k.inner_s[rows, :] = inner
        live = (row_iota(HALF, 1) + start) < k.live_rows
        above = jnp.where(live, grad[rows, :].astype(f32), 0.0)
        add(5, above * (down[rows, :] + k.bn()))
        grad_down = above * k.share(slot, 5)
        gbn[...] = gbn[...] + jnp.sum(grad_down, axis=0, keepdims=True)
        down_low = grad_down.astype(bf16)
        k.down_s[rows, :] = down_low
        up = mm(inner, wu[...]) + k.bu()
        square, tanh = gelu_parts(up)
        half = 0.5 * (1.0 + tanh)
        k.hidden_s[rows, :] = (up * half).astype(bf16)
        slope = half + 0.5 * up * (1.0 - tanh * tanh) * (
            GELU_A * (1.0 + 3.0 * GELU_B * square)
        )
        grad_up = mm_t(down_low, wn[...]) * slope
        gbu[...] = gbu[...] + jnp.sum(grad_up, axis=0, keepdims=True)
        up_low = grad_up.astype(bf16)
        k.up_s[rows, :] = up_low
        grad_inner = mm_t(up_low, wu[...])
        add(3, grad_inner)
        add(4, grad_inner * normal)
        grad_middle = above + normalise_back(
            normal, rate, grad_inner * (1.0 + k.share(slot, 4))
        )
        k.mid_grad[rows, :] = grad_middle
        add(2, grad_middle * grown)
        k.branch_low[rows, :] = (grad_middle * k.share(slot, 2)).astype(bf16)
        return carry

    lax.fori_loop(0, 2, tile, 0)
    k.push("mid_grad")
    k.push("branch_low")

    def weights(j, carry):
        part = pl.ds(pl.multiple_of(j * HALF, HALF), HALF)
        hidden_t = jnp.transpose(k.hidden_s[:, part].astype(f32)).astype(bf16)
        k.gwn[part, :] = mm(hidden_t, k.down_s[...])
        return carry

    lax.fori_loop(0, FF // HALF, weights, 0)
    k.push("gwn")
    inner_t = jnp.transpose(k.inner_s[...].astype(f32)).astype(bf16)

    def halves(j, carry):
        here = pl.ds(pl.multiple_of(j * HALF, HALF), HALF)
        keep = pl.ds(pl.multiple_of(j * HALF + k.section * (FF // 2), HALF), HALF)
        send = pl.ds(pl.multiple_of(j * HALF + (1 - k.section) * (FF // 2), HALF), HALF)
        k.gwu_keep[:, here] = mm(inner_t, k.up_s[:, keep])
        k.gwu_send[:, here] = mm(inner_t, k.up_s[:, send]).astype(bf16)
        return carry

    lax.fori_loop(0, FF // 2 // HALF, halves, 0)
    k.push("gwu_keep")
    k.push("gwu_send")
    gated = k.gated()
    k.gwo[...] = mm(jnp.transpose(gated[...].astype(f32)).astype(bf16), k.branch_low[...])

    short = jnp.concatenate([gbn[...], jnp.zeros((1, FF - D), f32)], axis=1)
    k.sums[...] = jnp.concatenate(
        [gmod[0:SLOTS, :], gbu[...], short, jnp.zeros((4, FF), f32)], axis=0
    )


def mixer_backward_body(k):
    flip = k.layer == 1
    wide = k.wide
    mixed_s, low, dv_s, rows_s, cols_s = k.mixed_s, k.low, k.dv_s, k.rows_s, k.cols_s
    fill_bias(k.bias, wide)
    branch_low, wo = k.branch_low(), k.wo()

    def first(i, carry):
        start = pl.multiple_of(i * HALF, HALF)
        rows = pl.ds(start, HALF)
        if flip:
            part = mm(order_matrix(start, HALF, wide, True), branch_low[...]).astype(bf16)
        else:
            part = branch_low[rows, :]
        mixed_s[rows, :] = mm_t(part, wo[...])
        return carry

    lax.fori_loop(0, 2, first, 0)
    rows_s[...] = jnp.zeros(rows_s.shape, f32)
    cols_s[...] = jnp.zeros(cols_s.shape, f32)
    qkvg, vc, cum, cumt, o = k.qkvg(), k.vc(), k.cum(), k.cumt(), k.o()
    k.small()

    def pair(p, carry):
        lanes = lane_iota(1, PAIR)
        total = o[:, columns(p)]
        gate = qkvg[:, columns(p, 3 * D)]
        above = mixed_s[:, columns(p)]
        rate = lax.rsqrt(head_norm(total, lanes) + 1.0)
        sig = sigmoid(gate)
        grad_gate = above * (total * rate) * (sig * (1.0 + gate * (1.0 - sig)))
        low[:, columns(p, 3 * D)] = grad_gate.astype(bf16)
        grad_normed = above * (gate * sig)
        product = grad_normed * total
        inside = jnp.where(
            lanes < HEAD_DIM,
            jnp.sum(jnp.where(lanes < HEAD_DIM, product, 0.0), axis=1, keepdims=True),
            jnp.sum(jnp.where(lanes < HEAD_DIM, 0.0, product), axis=1, keepdims=True),
        ) * (1.0 / HEAD_DIM)
        grad_o = rate * grad_normed - total * (rate * rate * rate) * inside

        queries = qkvg[:, columns(p)] * SCALE
        keys = qkvg[:, columns(p, D)]
        values = vc[:, columns(p)]
        query_cat = cat_left(queries)
        grad_cat = cat_left(grad_o)
        key_high, key_low = split(keys)
        key_pair = jnp.concatenate([key_high, key_low], axis=1)
        query_t = jnp.transpose(queries)
        grad_t = jnp.transpose(grad_o)
        grad_q = []
        grad_k = []
        grad_v = []
        for e in range(2):
            mine = (lanes // HEAD_DIM) == e
            head = 2 * p + e
            key_cat = cat_right(jnp.where(mine, keys, 0.0))
            value_cat = cat_right(jnp.where(mine, values, 0.0))
            first, second = decay_factors(cum, cumt, k.bias, head)
            raw_first = mm_t(query_cat[:HALF], key_cat[:HALF])
            raw_second = mm_t(query_cat[HALF:], key_cat)
            grad_first = first * mm_t(grad_cat[:HALF], value_cat[:HALF])
            grad_second = second * mm_t(grad_cat[HALF:], value_cat)
            score_first = raw_first * first
            score_second = raw_second * second
            pull_first = grad_first * raw_first
            pull_second = grad_second * raw_second
            here = lanes == head
            rows_s[:HALF, :] = rows_s[:HALF, :] + jnp.where(
                here, jnp.sum(pull_first, axis=1, keepdims=True), 0.0
            )
            rows_s[HALF:, :] = rows_s[HALF:, :] + jnp.where(
                here, jnp.sum(pull_second, axis=1, keepdims=True), 0.0
            )
            low_cols = jnp.sum(pull_second, axis=0, keepdims=True)
            cols_s[pl.ds(head, 1), :HALF] = low_cols[:, :HALF] + jnp.sum(
                pull_first, axis=0, keepdims=True
            )
            cols_s[pl.ds(head, 1), HALF:] = low_cols[:, HALF:]
            grad_q.append(
                jnp.concatenate(
                    [
                        mm_near(grad_first, key_pair[:HALF], key_high[:HALF]),
                        mm_near(grad_second, key_pair, key_high),
                    ],
                    axis=0,
                )
            )

            def turned(source_t, block_first, block_second):
                high, low = split(source_t[e * HEAD_DIM : (e + 1) * HEAD_DIM, :])
                both = jnp.concatenate([high, low], axis=0)
                first_high, first_low = split(block_first)
                second_high, second_low = split(block_second)
                one = mm(both[:, :HALF], first_high)
                one = one[:HEAD_DIM] + one[HEAD_DIM:] + mm(high[:, :HALF], first_low)
                two = mm(both[:, HALF:], second_high)
                two = two[:HEAD_DIM] + two[HEAD_DIM:] + mm(high[:, HALF:], second_low)
                return jnp.concatenate([two[:, :HALF] + one, two[:, HALF:]], axis=1)

            grad_k.append(turned(query_t, grad_first, grad_second))
            grad_v.append(turned(grad_t, score_first, score_second))
        query_grad = jnp.where(lanes < HEAD_DIM, grad_q[0], grad_q[1]) * SCALE
        low[:, columns(p)] = query_grad.astype(bf16)
        low[:, columns(p, D)] = jnp.transpose(jnp.concatenate(grad_k, axis=0)).astype(bf16)
        dv_s[:ROWS, columns(p)] = jnp.transpose(jnp.concatenate(grad_v, axis=0))
        return carry

    lax.fori_loop(0, PAIRS, pair, 0)

    pulled = rows_s[...] - jnp.transpose(cols_s[...])
    high, middle, rest = split_three(pulled)
    upper_first = jnp.concatenate(
        [
            jnp.where(row_iota(HALF, HALF) <= lane_iota(HALF, HALF), 1.0, 0.0),
            jnp.full((HALF, HALF), 0.0, f32) + jnp.where(wide, 1.0, 0.0),
        ],
        axis=1,
    ).astype(bf16)
    upper_second = upper_first[:, :HALF]
    later = jnp.concatenate(
        [
            mm(upper_first, high) + mm(upper_first, middle) + mm(upper_first, rest),
            mm(upper_second, high[HALF:]) + mm(upper_second, middle[HALF:])
            + mm(upper_second, rest[HALF:]),
        ],
        axis=0,
    )
    grad_dp = later * (1.0 / 16.0) * sigmoid(-(k.dp()[...] + k.bd()))
    grad_bd = jnp.sum(grad_dp, axis=0, keepdims=True)
    low[:, QKVG:] = grad_dp.astype(bf16)

    dv_s[ROWS:, :] = jnp.zeros((8, D), f32)
    position = row_iota(ROWS, 1) & jnp.where(wide, ROWS - 1, HALF - 1)
    last = jnp.where(wide, ROWS - 1, HALF - 1)
    here = dv_s[0:ROWS, :]
    one = jnp.where(position <= last - 1, dv_s[1 : 1 + ROWS, :], 0.0)
    two = jnp.where(position <= last - 2, dv_s[2 : 2 + ROWS, :], 0.0)
    value = qkvg[:, 2 * D : 3 * D]
    low[:, 2 * D : 3 * D] = (k.ck(0) * here + k.ck(1) * one + k.ck(2) * two).astype(bf16)
    k.push("low")

    taps = [jnp.sum(rows * value, axis=0, keepdims=True) for rows in (here, one, two)]
    rest = jnp.concatenate([grad_bd, jnp.zeros((1, D - LANES), f32)], axis=1)
    k.sums[...] = jnp.concatenate([*taps, rest, jnp.zeros((4, D), f32)], axis=0)

    ordered_t = jnp.transpose(k.ordered()[...].astype(f32)).astype(bf16)
    gwo = k.gwo()
    gw = k.gw

    def weights(j, carry):
        part = pl.ds(pl.multiple_of(j * HALF, HALF), HALF)
        gw[:, part] = mm(ordered_t, low[:, part])
        return carry

    lax.fori_loop(0, QKVG // HALF, weights, 0)
    gw[:, QKVG : QKVG + D] = gwo[...]
    gw[:, QKVG + D :] = mm(ordered_t, low[:, QKVG:])

    def halves(j, carry):
        here = pl.ds(pl.multiple_of(j * HALF, HALF), HALF)
        keep = pl.ds(pl.multiple_of(j * HALF + k.section * GROUP, HALF), HALF)
        send = pl.ds(pl.multiple_of(j * HALF + (1 - k.section) * GROUP, HALF), HALF)
        k.gw_keep[:, here] = gw[:, keep]
        k.gw_send[:, here] = gw[:, send].astype(bf16)
        return carry

    lax.fori_loop(0, GROUP // HALF, halves, 0)


def input_backward_body(k):
    flip = k.layer == 1
    wide = k.wide
    gmod, mixed_s, perm_s = k.gmod, k.mixed_s, k.perm_s
    gmod[...] = jnp.zeros(gmod.shape, f32)
    low, w_qk, w_vgd = k.low(), k.w_qk(), k.w_vgd()

    def inner_grad(i, carry):
        rows = pl.ds(pl.multiple_of(i * HALF, HALF), HALF)
        mixed_s[rows, :] = mm_t(low[rows, : 2 * D], w_qk[...]) + mm_t(
            low[rows, 2 * D :], w_vgd[...]
        )
        return carry

    lax.fori_loop(0, 2, inner_grad, 0)
    if flip:
        high, middle, rest = split_three(mixed_s[...])
        perm_s[:, :D] = high
        perm_s[:, D : 2 * D] = middle
        perm_s[:, 2 * D :] = rest
    x, mid_grad = k.x(), k.mid_grad()
    k.mods()

    def tile(i, carry):
        start = pl.multiple_of(i * HALF, HALF)
        rows = pl.ds(start, HALF)
        slot = k.slot(i)
        if flip:
            three = mm(order_matrix(start, HALF, wide, False), perm_s[...])
            grad = three[:, :D] + three[:, D : 2 * D] + three[:, 2 * D :]
        else:
            grad = mixed_s[rows, :]
        normal, rate = normalise(x[rows, :].astype(f32))
        where = (pl.ds(slot, 1), slice(0, D))
        gmod[where] = gmod[where] + jnp.sum(grad, axis=0, keepdims=True)
        where = (pl.ds(slot, 1), slice(D, 2 * D))
        gmod[where] = gmod[where] + jnp.sum(grad * normal, axis=0, keepdims=True)
        total = mid_grad[rows, :] + normalise_back(normal, rate, grad * (1.0 + k.share(slot, 1)))
        k.gx[rows, :] = total
        k.gx_low[rows, :] = total.astype(bf16)
        return carry

    lax.fori_loop(0, 2, tile, 0)
    k.push("gx_low")
    k.push("gx")
    ffn, mixer = k.ffn_sums(), k.mixer_sums()
    k.mod_low[...] = jnp.concatenate([gmod[...], ffn[...]], axis=1).astype(bf16)
    half = 2 * D
    rest = ffn[0:1, :] + ffn[1:2, :]
    k.sums[...] = jnp.concatenate(
        [
            gmod[0:1, :] + gmod[1:2, :],
            rest[:, :half],
            rest[:, half:],
            ffn[2:3, :half],
            ffn[2:3, half:],
            jnp.concatenate([ffn[3:4, :D], mixer[0:1, :]], axis=1),
            jnp.concatenate([mixer[1:2, :], mixer[2:3, :]], axis=1),
            jnp.concatenate([mixer[3:4, :], jnp.zeros((1, D), f32)], axis=1),
        ],
        axis=0,
    )


ANY = pl.BlockSpec(memory_space=pl.ANY)
VMEM = pl.BlockSpec(memory_space=pltpu.VMEM)
HBM = pl.BlockSpec(memory_space=pltpu.HBM)


def call(body, layer, layouts, ins, outs, scratch, flops):
    arrays = []
    counts = []
    kept = []
    places = []
    for kind, given, part in ins.values():
        places.extend([ANY] * 2 if kind == "own" else [HBM])
        given = given if kind == "own" else (given,)
        arrays.extend(given)
        counts.append(len(given))
        rows, wide = given[0].shape[-2:]
        start, stop = part or (0, wide)
        kept.append(pltpu.VMEM((rows, stop - start), given[0].dtype))

    def kernel(*refs):
        refs = list(refs)
        take = lambda count: [refs.pop(0) for _ in range(count)]
        (layouts_ref,) = take(1)
        sources = [take(count) for count in counts]
        targets = take(len(outs))
        buffers = take(len(ins))
        results = take(len(outs))
        rest = take(len(scratch))
        in_sems, out_sems = refs
        k = Kernel(layer, layouts_ref)
        for number, (name, (kind, _, part)) in enumerate(ins.items()):
            given = sources[number]
            if part is not None:
                given = [ref.at[:, part[0] : part[1]] for ref in given]
            setattr(k, name, k.load(kind, given, buffers[number], in_sems.at[number]))
        k.results = {}
        for number, name in enumerate(outs):
            setattr(k, name, results[number])
            k.results[name] = (results[number], targets[number], out_sems.at[number])
        for name, ref in zip(scratch, rest):
            setattr(k, name, ref)
        body(k)
        k.finish()

    return pl.pallas_call(
        kernel,
        out_shape=[jax.ShapeDtypeStruct(shape, kind) for shape, kind, _ in outs.values()],
        in_specs=[pl.BlockSpec(memory_space=pltpu.SMEM)] + places,
        out_specs=[HBM if for_kernel else ANY for _, _, for_kernel in outs.values()],
        scratch_shapes=kept
        + [pltpu.VMEM(shape, kind) for shape, kind, _ in outs.values()]
        + [pltpu.VMEM(shape, kind) for shape, kind in scratch.values()]
        + [pltpu.SemaphoreType.DMA((len(ins),)), pltpu.SemaphoreType.DMA((len(outs),))],
        compiler_params=pltpu.CompilerParams(vmem_limit_bytes=44 * 1024 * 1024),
        cost_estimate=pl.CostEstimate(flops=flops, bytes_accessed=4 << 20, transcendentals=0),
    )(layouts, *arrays)


def own(pair, part=None):
    return ("own", pair, part)


def plain(array):
    return ("plain", array, None)


def micro(array):
    return ("micro", array, None)


AT_UP = (0, FF)
AT_QK = (FF, FF + 2 * D)
AT_OUT = (FF + 2 * D, FF + 3 * D)
ADA_CUT = 1024
AT_ADA_A = (FF + 3 * D, FF + 3 * D + ADA_CUT)
AT_LIFTED = FF + 3 * D + ADA_CUT
AT_VGD = (0, 2 * D + LANES)
AT_ADA_B = (2 * D + LANES, 8 * D + LANES - ADA_CUT)


def attn_forward(layer, layouts, x, mods, small, packed, vgd):
    return call(
        attn_forward_body,
        layer,
        layouts,
        dict(
            x=micro(x),
            mods=own(mods),
            w_qk=own(packed, AT_QK),
            w_vgd=own(vgd, AT_VGD),
            small=own(small),
        ),
        dict(
            ordered=((ROWS, D), bf16, True),
            qkvg=((ROWS, QKVG), f32, True),
            dp=((ROWS, LANES), f32, True),
            vc=((ROWS, D), f32, True),
            cum=((ROWS, LANES), f32, True),
            cumt=((LANES, ROWS), f32, True),
            o=((ROWS, D), f32, True),
            gated=((ROWS, D), bf16, True),
        ),
        dict(
            inner=((ROWS, D), bf16),
            vpad=((ROWS + 8, D), f32),
            bias=((HALF, ROWS), f32),
        ),
        8 * 10**9,
    )


def ffn_forward(layer, layouts, x, mods, small, gated, packed, down):
    return call(
        ffn_forward_body,
        layer,
        layouts,
        dict(
            gated=plain(gated),
            x=micro(x),
            wo=own(packed, AT_OUT),
            mods=own(mods),
            small=own(small),
            wu=own(packed, AT_UP),
            wn=own(down),
        ),
        dict(
            out=((ROWS, D), bf16, True),
            branch=((ROWS, D), f32, True),
            down=((ROWS, D), f32, True),
        ),
        {},
        5 * 10**9,
    )


def ffn_backward(layer, layouts, x, mods, small, gated, branch, down_raw, grad, packed, down):
    return call(
        ffn_backward_body,
        layer,
        layouts,
        dict(
            mods=own(mods),
            small=own(small),
            x=micro(x),
            grad=micro(grad),
            branch=plain(branch),
            down=plain(down_raw),
            wu=own(packed, AT_UP),
            wn=own(down),
            gated=plain(gated),
        ),
        dict(
            mid_grad=((ROWS, D), f32, True),
            branch_low=((ROWS, D), bf16, True),
            gwo=((D, D), f32, True),
            gwu_keep=((D, FF // 2), f32, False),
            gwu_send=((D, FF // 2), bf16, False),
            gwn=((FF, D), f32, False),
            sums=((8, FF), f32, True),
        ),
        dict(
            hidden_s=((ROWS, FF), bf16),
            inner_s=((ROWS, D), bf16),
            up_s=((ROWS, FF), bf16),
            down_s=((ROWS, D), bf16),
            gmod=((8, FF), f32),
            gbu=((1, FF), f32),
            gbn=((1, D), f32),
        ),
        12 * 10**9,
    )


def mixer_backward(layer, layouts, small, saved, branch_low, gwo, packed):
    ordered, qkvg, dp, vc, cum, cumt, o = saved
    return call(
        mixer_backward_body,
        layer,
        layouts,
        dict(
            branch_low=plain(branch_low),
            wo=own(packed, AT_OUT),
            qkvg=plain(qkvg),
            vc=plain(vc),
            cum=plain(cum),
            cumt=plain(cumt),
            o=plain(o),
            small=own(small),
            dp=plain(dp),
            ordered=plain(ordered),
            gwo=plain(gwo),
        ),
        dict(
            low=((ROWS, QKVG + LANES), bf16, True),
            gw_keep=((D, GROUP), f32, False),
            gw_send=((D, GROUP), bf16, False),
            sums=((8, D), f32, True),
        ),
        dict(
            mixed_s=((ROWS, D), f32),
            dv_s=((ROWS + 8, D), f32),
            rows_s=((ROWS, LANES), f32),
            cols_s=((LANES, ROWS), f32),
            bias=((HALF, ROWS), f32),
            gw=((D, 2 * GROUP), f32),
        ),
        15 * 10**9,
    )


def input_backward(layer, layouts, x, mods, low, mid_grad, ffn_sums, mixer_sums, packed, vgd):
    return call(
        input_backward_body,
        layer,
        layouts,
        dict(
            low=plain(low),
            w_qk=own(packed, AT_QK),
            w_vgd=own(vgd, AT_VGD),
            x=micro(x),
            mid_grad=plain(mid_grad),
            mods=own(mods),
            ffn_sums=plain(ffn_sums),
            mixer_sums=plain(mixer_sums),
        ),
        dict(
            gx=((ROWS, D), f32, False),
            gx_low=((ROWS, D), bf16, True),
            mod_low=((8, 6 * D), bf16, False),
            sums=((8, 2 * D), f32, False),
        ),
        dict(
            mixed_s=((ROWS, D), f32),
            perm_s=((ROWS, 3 * D), bf16),
            gmod=((8, 2 * D), f32),
        ),
        4 * 10**9,
    )


def small_kernel(b_up, b_down, taps, b_decay, packed):
    packed[...] = jnp.zeros(packed.shape, f32)
    packed[0:1, :] = b_up[...]
    packed[1:2, :D] = b_down[...]
    packed[2:5, :D] = taps[0]
    packed[5:6, :HEADS] = b_decay[...]


def pack_small(b_up, b_down, taps, b_decay):
    return pl.pallas_call(
        small_kernel,
        out_shape=jax.ShapeDtypeStruct((8, FF), f32),
        in_specs=[VMEM] * 4,
        out_specs=VMEM,
    )(b_up, b_down, taps, b_decay)


def padded(width):
    return -(-width // LANES) * LANES


def pack_kernel(groups, *refs):
    sources, packed = list(refs[: sum(groups)]), refs[sum(groups) :]
    for count, target in zip(groups, packed):
        at = 0
        for _ in range(count):
            ref = sources.pop(0)
            width = ref.shape[1]
            if width % LANES:
                zeros = jnp.zeros((target.shape[0], padded(width)), target.dtype)
                target[:, at : at + padded(width)] = zeros
            target[:, at : at + width] = ref[...]
            at += padded(width)


def pack(*groups):
    arrays = [array for group in groups for array in group]
    return pl.pallas_call(
        functools.partial(pack_kernel, [len(group) for group in groups]),
        out_shape=[
            jax.ShapeDtypeStruct(
                (group[0].shape[0], sum(padded(array.shape[1]) for array in group)), bf16
            )
            for group in groups
        ],
        in_specs=[VMEM] * len(arrays),
        out_specs=[VMEM] * len(groups),
    )(*arrays)


def mods_kernel(conditions, bias, packed, vgd, out, ada_a, ada_b, sems):
    copies = [
        pltpu.make_async_copy(packed.at[:, AT_ADA_A[0] : AT_ADA_A[1]], ada_a, sems.at[0]),
        pltpu.make_async_copy(vgd.at[:, AT_ADA_B[0] : AT_ADA_B[1]], ada_b, sems.at[1]),
    ]
    for copy in copies:
        copy.start()
    values = conditions[...].astype(f32)
    lifted = (values * sigmoid(values)).astype(bf16)
    for copy in copies:
        copy.wait()
    out[...] = jnp.concatenate([mm(lifted, ada_a[...]), mm(lifted, ada_b[...])], axis=1) + bias[...]


ADA_SCRATCH = [
    pltpu.VMEM((D, ADA_CUT), bf16),
    pltpu.VMEM((D, 6 * D - ADA_CUT), bf16),
    pltpu.SemaphoreType.DMA((2,)),
]


def modulations(conditions, bias, packed, vgd):
    return pl.pallas_call(
        mods_kernel,
        out_shape=jax.ShapeDtypeStruct((MICRO * SLOTS, 6 * D), f32),
        in_specs=[VMEM, VMEM, ANY, ANY],
        out_specs=VMEM,
        scratch_shapes=ADA_SCRATCH,
        compiler_params=pltpu.CompilerParams(vmem_limit_bytes=16 * 1024 * 1024),
        cost_estimate=pl.CostEstimate(flops=10**9, bytes_accessed=2 << 20, transcendentals=0),
    )(conditions, bias, packed, vgd)


def lifted_kernel(mod_low, packed, vgd, out, ada_a, ada_b, sems):
    copies = [
        pltpu.make_async_copy(packed.at[:, AT_ADA_A[0] : AT_ADA_A[1]], ada_a, sems.at[0]),
        pltpu.make_async_copy(vgd.at[:, AT_ADA_B[0] : AT_ADA_B[1]], ada_b, sems.at[1]),
    ]
    for copy in copies:
        copy.start()
    for copy in copies:
        copy.wait()
    grad = mod_low[...]
    out[...] = mm_t(grad[:, :ADA_CUT], ada_a[...]) + mm_t(grad[:, ADA_CUT:], ada_b[...])


def lifted_grads(mod_low, packed, vgd):
    return pl.pallas_call(
        lifted_kernel,
        out_shape=jax.ShapeDtypeStruct((MICRO * SLOTS, D), f32),
        in_specs=[VMEM, ANY, ANY],
        out_specs=VMEM,
        scratch_shapes=ADA_SCRATCH,
        compiler_params=pltpu.CompilerParams(vmem_limit_bytes=16 * 1024 * 1024),
        cost_estimate=pl.CostEstimate(flops=10**9, bytes_accessed=2 << 20, transcendentals=0),
    )(mod_low, packed, vgd)


def step_kernel(bit, count, *refs):
    mine = (lax.axis_index("row") >> bit) & 1
    kept, came, stays, goes = (refs[i * count : (i + 1) * count] for i in range(4))
    for i in range(count):
        stays[i][...] = kept[i][:, mine] + came[i][:, mine].astype(f32)
        goes[i][...] = (kept[i][:, 1 - mine] + came[i][:, 1 - mine].astype(f32)).astype(bf16)


def step(kept, came, bit):
    count = len(kept)
    paired = lambda array: array.reshape((array.shape[0] // 2, 2) + array.shape[1:])
    kept = [paired(array) for array in kept]
    came = [paired(array) for array in came]
    shapes = [array.shape[:1] + array.shape[2:] for array in kept]
    size = sum(array.size for array in kept)
    out = pl.pallas_call(
        functools.partial(step_kernel, bit, count),
        out_shape=[jax.ShapeDtypeStruct(shape, f32) for shape in shapes]
        + [jax.ShapeDtypeStruct(shape, bf16) for shape in shapes],
        in_specs=[VMEM] * (2 * count),
        out_specs=[VMEM] * (2 * count),
        compiler_params=pltpu.CompilerParams(vmem_limit_bytes=24 * 1024 * 1024),
        cost_estimate=pl.CostEstimate(flops=size, bytes_accessed=8 * size, transcendentals=0),
    )(*kept, *came)
    return list(out[:count]), list(out[count:])


def output_kernel(*refs):
    first = lax.axis_index("section") == 0
    ins, outs = refs[:20], refs[20:]

    def chosen(number):
        one, two, one_came, two_came = (ins[4 * number + i][...] for i in range(4))
        return jnp.where(first, one, two), jnp.where(first, one_came, two_came)

    def halves(number):
        mine, other = chosen(number)
        return jnp.where(first, mine, other), jnp.where(first, other, mine)

    attn = halves(0)
    cut = GROUP - 2 * D
    outs[0][...] = attn[0][:, :D]
    outs[1][...] = attn[0][:, D : 2 * D]
    outs[2][:, :cut] = attn[0][:, 2 * D :]
    outs[2][:, cut:] = attn[1][:, : D - cut]
    outs[3][...] = attn[1][:, D - cut : 2 * D - cut]
    outs[4][...] = attn[1][:, 2 * D - cut : 3 * D - cut]
    outs[5][...] = attn[1][:, 3 * D - cut : 3 * D - cut + HEADS]
    up = halves(1)
    outs[6][:, : FF // 2] = up[0]
    outs[6][:, FF // 2 :] = up[1]
    down = halves(2)
    outs[7][0] = down[0]
    outs[7][1] = down[1]
    mine, other = chosen(3)
    outs[8][...] = mine + other
    mine, other = chosen(4)
    small = mine + other
    half = 2 * D
    for i in range(3):
        outs[9][:, i * half : (i + 1) * half] = small[i : i + 1, :]
    for i in range(2):
        outs[10][:, i * half : (i + 1) * half] = small[3 + i : 4 + i, :]
    outs[11][...] = small[5:6, :D]
    outs[12][0:1, :] = small[5:6, D:]
    outs[12][1:2, :] = small[6:7, :D]
    outs[12][2:3, :] = small[6:7, D:]
    outs[13][...] = small[7:8, :HEADS]


def outputs(quads, shard, down_rows):
    shapes = (
        [(shard, D)] * 5
        + [(shard, HEADS), (shard, FF), (2, down_rows, D), (shard, 6 * D)]
        + [(1, 6 * D), (1, FF), (1, D), (3, D), (1, HEADS)]
    )
    flat_in = [array for quad in quads for array in quad]
    return pl.pallas_call(
        output_kernel,
        out_shape=[jax.ShapeDtypeStruct(shape, f32) for shape in shapes],
        in_specs=[VMEM] * len(flat_in),
        out_specs=[VMEM] * len(shapes),
    )(*flat_in)


def both_kernel(one, two, one_came, two_came, out, sems):
    section = lax.axis_index("section")

    def move(mine, came, layer):
        copies = [
            pltpu.make_async_copy(mine, out.at[layer], sems.at[0]),
            pltpu.make_async_copy(came, out.at[1 - layer], sems.at[1]),
        ]
        for copy in copies:
            copy.start()
        for copy in copies:
            copy.wait()

    @pl.when(section == 0)
    def _():
        move(one, one_came, 0)

    @pl.when(section == 1)
    def _():
        move(two, two_came, 1)


def both_micros(one, two, one_came, two_came):
    return pl.pallas_call(
        both_kernel,
        out_shape=jax.ShapeDtypeStruct((MICRO,) + one.shape, one.dtype),
        in_specs=[ANY] * 4,
        out_specs=ANY,
        scratch_shapes=[pltpu.SemaphoreType.DMA((2,))],
    )(one, two, one_came, two_came)


def swap(values):
    return lax.ppermute(values, "section", [(0, 1), (1, 0)])


def hand(values, source):
    return lax.ppermute(values, "section", [(source, 1 - source)])


def row_bits():
    bits = lax.axis_size("row").bit_length() - 1
    third = bits // 3
    return (
        tuple(range(third)),
        tuple(range(third, 2 * third)),
        tuple(range(2 * third, bits)),
    )


def partner(values, bit):
    size = lax.axis_size("row")
    return lax.ppermute(values, "row", [(i, i ^ (1 << bit)) for i in range(size)])


def axis_of(bit):
    return lax.axis_size("row").bit_length() - 2 - bit


def bit_of(bit):
    return (lax.axis_index("row") >> bit) & 1


def single(values):
    return values.reshape((1,) * (lax.axis_size("row").bit_length() - 1) + values.shape)


def join(held, other, bit):
    return jnp.where(
        bit_of(bit) == 0,
        jnp.concatenate([held, other], axis=axis_of(bit)),
        jnp.concatenate([other, held], axis=axis_of(bit)),
    )


def flat(held):
    return held.reshape(-1, held.shape[-1])


def lock(*arrays):
    return lax.optimization_barrier(arrays)


class Gather:
    def __init__(self, values):
        self.held = single(values)

    def ready(self, bit):
        self.bit = bit
        return self.held

    def take(self, other):
        self.held = join(self.held, other, self.bit)


class Total:
    def __init__(self, values):
        self.held = values

    def ready(self, bit):
        return self.held

    def take(self, other):
        self.held = self.held + other


def begin(chains, bit):
    return [chain.ready(bit) for chain in chains]


def send(arrays, bit):
    return [partner(array, bit) for array in arrays]


def end(chains, arrays):
    for chain, array in zip(chains, arrays):
        chain.take(array)


def on_device(
    tokens, conditions, output_grad, layouts,
    w_ada, b_ada, w_query, w_key, w_value, w_gate, w_out, w_decay, b_decay, conv_kernel,
    w_up, b_up, w_down, b_down,
):
    section = lax.axis_index("section")
    devices = lax.axis_size("row")
    is_first = section == 0
    shard = w_query.shape[1]
    along_x, along_y, along_z = row_bits()
    plane = along_x + along_y

    def both(values):
        return values, swap(values)

    lifted_own = jax.nn.silu(conditions.astype(f32)).astype(bf16)
    group_a, group_b = pack(
        (w_up[0], w_query[0], w_key[0], w_out[0], w_ada[0, :, :ADA_CUT], lifted_own.reshape(shard, -1)),
        (w_value[0], w_gate[0], w_decay[0], w_ada[0, :, ADA_CUT:]),
    )
    group_a = [Gather(group_a)]
    group_b = [Gather(group_b), Gather(w_down[0])]
    chains = group_a + group_b
    for bit in reversed(along_z):
        end(chains, lock(*send(begin(chains, bit), bit)))
    for bit_a, bit_b in zip(plane, along_y + along_x):
        others_a = send(begin(group_a, bit_a), bit_a)
        others_b = send(begin(group_b, bit_b), bit_b)
        others = lock(*others_a, *others_b)
        end(chains, others)
    packed, vgd, down = [both(flat(chain.held)) for chain in chains]

    mods = both(
        modulations(conditions.reshape(MICRO * SLOTS, D), b_ada, packed[0], vgd[0])
    )
    smalls = both(pack_small(b_up, b_down, conv_kernel, b_decay))

    x = tokens
    kept = []
    acts = []
    for l in range(2):
        *saved, gated = attn_forward(l, layouts, x, mods, smalls, packed, vgd)
        out, branch, down_raw = ffn_forward(l, layouts, x, mods, smalls, gated, packed, down)
        kept.append((x, saved, gated, branch, down_raw))
        acts.append(out)
        x = out[None]

    def ffn_step(l, grad):
        x, saved, gated, branch, down_raw = kept[l]
        mid_grad, branch_low, gwo, up_keep, up_send, gwn, sums = ffn_backward(
            l, layouts, x, mods, smalls, gated, branch, down_raw, grad, packed, down
        )
        pair = gwn.reshape(devices, 2, FF // devices // 2, D)
        down_keep = lax.dynamic_index_in_dim(pair, section, 1, keepdims=False)
        down_send = lax.dynamic_index_in_dim(pair, 1 - section, 1, keepdims=False).astype(bf16)
        keep = [up_keep.reshape(devices, shard, FF // 2), down_keep]
        sent = [up_send.reshape(devices, shard, FF // 2), down_send]
        return [branch_low, gwo], mid_grad, keep, sent, sums

    def mixer_step(l, carried):
        low, keep, sent, sums = mixer_backward(l, layouts, smalls, kept[l][1], *carried, packed)
        by_row = lambda array: [array.reshape(devices, shard, GROUP)]
        return low, by_row(keep), by_row(sent), sums

    def input_step(l, low, mid_grad, ffn_sums, mixer_sums):
        return input_backward(
            l, layouts, kept[l][0], mods, low, mid_grad, ffn_sums, mixer_sums, packed, vgd
        )

    def divide(arrays, *counts):
        parts = []
        for count in counts:
            parts.append(list(arrays[:count]))
            arrays = arrays[count:]
        return parts

    def run(keep, came, bits):
        for bit in bits[:-1]:
            keep, sent = step(keep, came, bit)
            came = send(sent, bit)
        return step(keep, came, bits[-1])

    x_bits, y_bits, z_bits = along_x, along_y, along_z
    carried, mid_grad, f2_keep, f2_sent, f2_sums = ffn_step(1, output_grad)
    *carried, s0, s1 = lock(*carried, *f2_sent)
    f2_came = [swap(s0), swap(s1)]
    acts_came = [hand(acts[0], 1), hand(acts[1], 0)]
    low, a2_keep, a2_sent, m2_sums = mixer_step(1, carried)
    low, a2_sent, f2_came, acts_came = divide(lock(low, *a2_sent, *f2_came, *acts_came), 1, 1, 2, 2)
    a2_came = [swap(a2_sent[0])]
    gx_two, grad, mod_low_two, sums_two = input_step(1, low[0], mid_grad, f2_sums, m2_sums)
    grad, gx_two, mod_low_two, *a2_came = lock(grad, gx_two, mod_low_two[:SLOTS], *a2_came)
    two_keep, two_sent = run(f2_keep + a2_keep, f2_came + a2_came, x_bits)
    mod_two = Gather(mod_low_two)
    for bit in x_bits[:-1]:
        end([mod_two], send(begin([mod_two], bit), bit))
    grad, gx_two, *two_sent = lock(grad, gx_two, *two_sent, mod_two.ready(x_bits[-1]))
    two_came = send(two_sent, x_bits[-1])
    gx_two_came = hand(gx_two, 0)

    carried, mid_grad, f1_keep, f1_sent, f1_sums = ffn_step(0, grad[None])
    carried, f1_sent, two_came, (mod_came, gx_two_came) = divide(
        lock(*carried, *f1_sent, *two_came, gx_two_came), 2, 2, 3, 2
    )
    f1_came = [swap(array) for array in f1_sent]
    mod_two.take(mod_came)
    two_keep, two_sent = run(two_keep, two_came, y_bits)
    f1_keep, f1_sent = run(f1_keep, f1_came, x_bits)
    for bit in y_bits[:-1]:
        end([mod_two], send(begin([mod_two], bit), bit))
    two_sent = two_sent + [mod_two.ready(y_bits[-1])]
    carried, two_sent, f1_sent = divide(lock(*carried, *two_sent, *f1_sent), 2, 4, 2)
    two_came = send(two_sent, y_bits[-1])
    f1_came = send(f1_sent, x_bits[-1])
    low, a1_keep, a1_sent, m1_sums = mixer_step(0, carried)
    low, a1_sent, two_came, (mod_came,), f1_came = divide(
        lock(low, *a1_sent, *two_came, *f1_came), 1, 1, 3, 1, 2
    )
    mod_two.take(mod_came)
    two_keep, two_sent = run(two_keep, two_came, z_bits[:1])
    f1_keep, f1_sent = run(f1_keep, f1_came, y_bits)
    two_sent = two_sent + [mod_two.ready(z_bits[0])]
    low, a1_sent, two_sent, f1_sent = divide(lock(*low, *a1_sent, *two_sent, *f1_sent), 1, 1, 4, 2)
    a1_came = [swap(a1_sent[0])]
    two_came = send(two_sent, z_bits[0])
    f1_came = send(f1_sent, y_bits[-1])
    gx_one, _, mod_low_one, sums_one = input_step(0, low[0], mid_grad, f1_sums, m1_sums)
    mod_low_one = mod_low_one[:SLOTS]
    rest = (gx_one, mod_low_one, sums_one)
    rest, a1_came, two_came, (mod_came,), f1_came = divide(
        lock(*rest, *a1_came, *two_came, *f1_came), 3, 1, 3, 1, 2
    )
    gx_one, mod_low_one, sums_one = rest
    mod_two.take(mod_came)

    mod_one = Gather(mod_low_one)
    total = Total(jnp.concatenate([sums_one, sums_two], axis=0))
    one_keep, one_came = a1_keep, a1_came
    z_work = [(two_keep, two_came, z_bits[1:], [mod_two]), (f1_keep, f1_came, z_bits, [])]
    for place, bit in enumerate(plane):
        one_keep, one_sent = step(one_keep, one_came, bit)
        sent = lock(*one_sent, mod_one.ready(bit), total.ready(bit))
        one_came, (mod_came,), (total_came,) = divide(send(sent, bit), 1, 1, 1)
        if place == 0:
            gx_one_came = hand(gx_one, 1)
            mod_came_one, mod_came_two = hand(mod_low_one, 1), hand(mod_low_two, 0)
        mod_one.take(mod_came)
        total.take(total_came)
    two_keep_came = (two_keep, two_came)
    for place, bit in enumerate(z_bits):
        keep = one_keep + f1_keep
        came = one_came + f1_came
        chains = [mod_one, total]
        if place:
            keep, came = keep + two_keep_came[0], came + two_keep_came[1]
            chains = chains + [mod_two]
        keep, sent = step(keep, came, bit)
        ready = [chain.ready(bit) for chain in chains]
        got = list(lock(*send(lock(*sent, *ready), bit)))
        came = got[: len(keep)]
        end(chains, got[len(keep) :])
        one_keep, f1_keep = keep[:1], keep[1:3]
        one_came, f1_came = came[:1], came[1:3]
        if place:
            two_keep_came = (keep[3:], came[3:])
    added = [
        (mine + other.astype(f32)).reshape(mine.shape[-2:]) for mine, other in zip(keep, came)
    ]
    a1, up1, down1, up2, down2, a2 = added

    lifted_rows = packed[0][:, AT_LIFTED : AT_LIFTED + MICRO * SLOTS * D // shard]
    lifted_rows = lifted_rows.reshape(devices, MICRO, SLOTS, devices, shard)
    lifted_mine = lax.dynamic_index_in_dim(lifted_rows, section, 1, keepdims=False)
    lifted_mine = lax.dynamic_index_in_dim(
        lifted_mine, lax.axis_index("row"), 2, keepdims=False
    ).reshape(devices * SLOTS, shard)

    def ada_term(mod):
        return lax.dot_general(
            lifted_mine, flat(mod.held), (((0,), (0,)), ((), ())), preferred_element_type=f32
        )

    ones = [a1, up1, down1, ada_term(mod_one), total.held[:8]]
    twos = [a2, up2, down2, ada_term(mod_two), total.held[8:]]
    sent_one, sent_two = divide(lock(*ones, *twos), 5, 5)
    quads = [
        (mine_one, mine_two, hand(one, 1), hand(two, 0))
        for mine_one, mine_two, one, two in zip(ones, twos, sent_one, sent_two)
    ]
    (
        g_query, g_key, g_value, g_gate, g_out, g_decay, g_up, g_down, g_ada,
        g_b_ada, g_b_up, g_b_down, g_conv, g_b_decay,
    ) = outputs(quads, shard, FF // devices // 2)

    mod_both = jnp.where(
        is_first,
        jnp.concatenate([mod_low_one, mod_came_one]),
        jnp.concatenate([mod_came_two, mod_low_two]),
    )
    grad_lifted = lifted_grads(mod_both, packed[0], vgd[0])
    grad_lifted = (grad_lifted + swap(grad_lifted)).reshape(MICRO, SLOTS, D)
    _, pull_silu = jax.vjp(jax.nn.silu, conditions.astype(f32))
    (cond_grads,) = pull_silu(grad_lifted)

    return (
        both_micros(acts[0], acts[1], *acts_came)[None],
        both_micros(gx_one, gx_two, gx_one_came, gx_two_came)[None],
        cond_grads,
        g_ada[None],
        g_b_ada,
        g_query[None],
        g_key[None],
        g_value[None],
        g_gate[None],
        g_out[None],
        g_decay[None],
        g_b_decay,
        g_conv[None],
        g_up[None],
        g_b_up,
        g_down.reshape(1, FF // devices, D),
        g_b_down,
    )


def solution(mesh):
    rows = P(None, "row", None)
    mats = P("section", "row", None)
    vector = P("section", None)
    in_specs = (
        rows, rows, rows, P(None, "row"),
        mats, vector, mats, mats, mats, mats, mats, mats, vector, P("section", None, None),
        mats, vector, mats, vector,
    )
    blocks = P("section", None, "row", None)
    out_specs = (
        blocks, blocks, rows,
        mats, vector, mats, mats, mats, mats, mats, mats, vector, P("section", None, None),
        mats, vector, mats, vector,
    )
    return jax.shard_map(
        on_device, mesh=mesh, in_specs=in_specs, out_specs=out_specs, check_vma=False
    )
```

```python
import functools

import jax
import jax.numpy as jnp
from jax import lax
from jax.experimental import pallas as pl
from jax.experimental.pallas import tpu as pltpu
from jax.sharding import PartitionSpec as P

D = 384
HEADS = 6
HEAD_DIM = 64
FF = 1536
MICRO = 2
ROWS = 512
HALF = 256
SLOTS = 2
PAIR = 128
PAIRS = D // PAIR
QKVG = 4 * D
LANES = 128
GROUP = (QKVG + D + LANES) // 2
NEG = -1e30
SCALE = HEAD_DIM**-0.5

bf16 = jnp.bfloat16
f32 = jnp.float32


def mm(left, right):
    return jnp.dot(left, right, preferred_element_type=f32)


def mm_t(left, right):
    return lax.dot_general(left, right, (((1,), (1,)), ((), ())), preferred_element_type=f32)


def split(values):
    high = values.astype(bf16)
    return high, (values - high.astype(f32)).astype(bf16)


def split_three(values):
    high, rest = split(values)
    mid = values - high.astype(f32)
    middle, low = split(mid)
    return high, middle, low


def cat_left(values):
    high, low = split(values)
    return jnp.concatenate([high, low, high], axis=1)


def cat_right(values):
    high, low = split(values)
    return jnp.concatenate([high, high, low], axis=1)


def mm_near(left, right_pair, right_high):
    high, low = split(left)
    wide = mm(high, right_pair)
    return wide[:, :PAIR] + wide[:, PAIR:] + mm(low, right_high)


def lane_iota(rows, columns):
    return lax.broadcasted_iota(jnp.int32, (rows, columns), 1)


def row_iota(rows, columns):
    return lax.broadcasted_iota(jnp.int32, (rows, columns), 0)


def order_matrix(start, rows, wide, to_scan):
    t = row_iota(rows, ROWS) + start
    small = (t & 256) + ((t & 15) << 4) + ((t & 255) >> 4)
    if to_scan:
        large = ((t & 15) << 5) + (t >> 4)
    else:
        large = ((t & 31) << 4) + (t >> 5)
    source = jnp.where(wide, large, small)
    return jnp.where(lane_iota(rows, ROWS) == source, 1.0, 0.0).astype(bf16)


def normalise(values):
    centred = values - jnp.mean(values, axis=-1, keepdims=True)
    rate = lax.rsqrt(jnp.mean(centred * centred, axis=-1, keepdims=True) + 1e-06)
    return centred * rate, rate


def normalise_back(normal, rate, grad):
    return rate * (
        grad
        - jnp.mean(grad, axis=-1, keepdims=True)
        - normal * jnp.mean(grad * normal, axis=-1, keepdims=True)
    )


class In:
    def __init__(self, copy, kept):
        self.copy = copy
        self.kept = kept

    def __call__(self):
        if self.copy is not None:
            self.copy.wait()
            self.copy = None
        return self.kept


class Kernel:
    def __init__(self, layer, layouts):
        self.layer = layer
        self.section = lax.axis_index("section")
        self.own = self.section == layer
        self.layout = layouts[self.section, 0]
        self.wide = self.layout == 0
        self.live_rows = jnp.where(self.wide, ROWS, self.layout * HALF)
        self.pushed = {}

    def load(self, kind, refs, kept, sem):
        if kind == "own":
            mine, other = refs

            @pl.when(self.own)
            def _():
                pltpu.make_async_copy(mine, kept, sem).start()

            @pl.when(jnp.logical_not(self.own))
            def _():
                pltpu.make_async_copy(other, kept, sem).start()

            return In(pltpu.make_async_copy(mine, kept, sem), kept)
        (source,) = refs
        if kind == "micro":
            source = source.at[self.section if source.shape[0] == MICRO else 0]
        copy = pltpu.make_async_copy(source, kept, sem)
        copy.start()
        return In(copy, kept)

    def push(self, name):
        kept, target, sem = self.results[name]
        copy = pltpu.make_async_copy(kept, target, sem)
        copy.start()
        self.pushed[name] = copy

    def finish(self):
        for name in self.results:
            if name not in self.pushed:
                self.push(name)
        for copy in self.pushed.values():
            copy.wait()

    def slot(self, half):
        return jnp.where(self.wide, 0, half)

    def share(self, slot, part):
        row = pl.ds(2 * self.section + slot, 1)
        return self.mods()[row, part * D : (part + 1) * D]

    def bu(self):
        return self.small()[0:1, :]

    def bn(self):
        return self.small()[1:2, :D]

    def ck(self, tap):
        return self.small()[2 + tap : 3 + tap, :D]

    def bd(self):
        return self.small()[5:6, :LANES]


def sigmoid(values):
    return 1.0 / (1.0 + jnp.exp(-values))


GELU_A = 0.7978845608028654
GELU_B = 0.044715


def gelu_parts(values):
    square = values * values
    tanh = jnp.tanh(GELU_A * values * (1.0 + GELU_B * square))
    return square, tanh


def fill_bias(bias, wide):
    bias[:, :HALF] = jnp.full((HALF, HALF), 0.0, f32) + jnp.where(wide, 0.0, NEG)
    causal = row_iota(HALF, HALF) >= lane_iota(HALF, HALF)
    bias[:, HALF:] = jnp.where(causal, 0.0, NEG)


def decay_factors(cum, cumt, bias, head):
    row = cumt[pl.ds(head, 1), :]
    lanes = lane_iota(1, LANES)
    column = jnp.sum(jnp.where(lanes == head, cum[...], 0.0), axis=1, keepdims=True)
    first = jnp.exp(column[:HALF] - row[:, :HALF] + bias[:, HALF:])
    second = jnp.exp(column[HALF:] - row + bias[...])
    return first, second


def head_norm(values, lanes):
    square = values * values
    low = jnp.sum(jnp.where(lanes < HEAD_DIM, square, 0.0), axis=1, keepdims=True)
    high = jnp.sum(jnp.where(lanes < HEAD_DIM, 0.0, square), axis=1, keepdims=True)
    return jnp.where(lanes < HEAD_DIM, low, high) * (1.0 / HEAD_DIM)


def fill_decay(dp, bd, cum, cumt):
    raw = dp[...] + bd
    log_decay = (jnp.minimum(raw, 0.0) - jnp.log1p(jnp.exp(-jnp.abs(raw)))) * (1.0 / 16.0)
    high, middle, low = split_three(log_decay)
    causal = jnp.where(row_iota(ROWS, ROWS) >= lane_iota(ROWS, ROWS), 1.0, 0.0).astype(bf16)
    cum[...] = mm(causal, high) + mm(causal, middle) + mm(causal, low)
    cumt[...] = jnp.transpose(cum[...])


def columns(index, first=0):
    return pl.ds(pl.multiple_of(index * PAIR + first, PAIR), PAIR)


def attn_forward_body(k):
    flip = k.layer == 1
    wide = k.wide
    x = k.x()
    k.mods()

    def first(i, carry):
        rows = pl.ds(pl.multiple_of(i * HALF, HALF), HALF)
        slot = k.slot(i)
        normal, _ = normalise(x[rows, :].astype(f32))
        k.inner[rows, :] = (normal * (1.0 + k.share(slot, 1)) + k.share(slot, 0)).astype(bf16)
        return carry

    lax.fori_loop(0, 2, first, 0)
    w_qk = k.w_qk()
    w_vgd = k.w_vgd()

    def project(i, carry):
        start = pl.multiple_of(i * HALF, HALF)
        rows = pl.ds(start, HALF)
        if flip:
            part = mm(order_matrix(start, HALF, wide, True), k.inner[...]).astype(bf16)
        else:
            part = k.inner[rows, :]
        k.ordered[rows, :] = part
        k.qkvg[rows, : 2 * D] = mm(part, w_qk[...])
        k.qkvg[rows, 2 * D :] = mm(part, w_vgd[:, : 2 * D])
        k.dp[rows, :] = mm(part, w_vgd[:, 2 * D :])
        return carry

    lax.fori_loop(0, 2, project, 0)
    k.small()
    for name in ("ordered", "qkvg", "dp"):
        k.push(name)
    fill_decay(k.dp, k.bd(), k.cum, k.cumt)
    fill_bias(k.bias, wide)

    vpad = k.vpad
    vpad[0:8, :] = jnp.zeros((8, D), f32)
    vpad[8 : 8 + ROWS, :] = k.qkvg[:, 2 * D : 3 * D]
    position = row_iota(ROWS, 1) & jnp.where(wide, ROWS - 1, HALF - 1)
    one = jnp.where(position >= 1, vpad[7 : 7 + ROWS, :], 0.0)
    two = jnp.where(position >= 2, vpad[6 : 6 + ROWS, :], 0.0)
    k.vc[...] = k.ck(0) * vpad[8 : 8 + ROWS, :] + k.ck(1) * one + k.ck(2) * two
    for name in ("cum", "cumt", "vc"):
        k.push(name)

    def pair(p, carry):
        lanes = lane_iota(1, PAIR)
        queries = cat_left(k.qkvg[:, columns(p)] * SCALE)
        keys = k.qkvg[:, columns(p, D)]
        value_high, value_low = split(k.vc[:, columns(p)])
        values = jnp.concatenate([value_high, value_low], axis=1)
        parts = []
        for e in range(2):
            key_cat = cat_right(jnp.where((lanes // HEAD_DIM) == e, keys, 0.0))
            first, second = decay_factors(k.cum, k.cumt, k.bias, 2 * p + e)
            first = first * mm_t(queries[:HALF], key_cat[:HALF])
            second = second * mm_t(queries[HALF:], key_cat)
            parts.append(
                jnp.concatenate(
                    [
                        mm_near(first, values[:HALF], value_high[:HALF]),
                        mm_near(second, values, value_high),
                    ],
                    axis=0,
                )
            )
        total = jnp.where(lanes < HEAD_DIM, parts[0], parts[1])
        k.o[:, columns(p)] = total
        gate = k.qkvg[:, columns(p, 3 * D)]
        normed = total * lax.rsqrt(head_norm(total, lanes) + 1.0)
        mixed = (normed * (gate * sigmoid(gate))).astype(bf16)
        if flip:
            k.inner[:, columns(p)] = mixed
        else:
            k.gated[:, columns(p)] = mixed
        return carry

    lax.fori_loop(0, PAIRS, pair, 0)
    k.push("o")
    if flip:

        def back(i, carry):
            start = pl.multiple_of(i * HALF, HALF)
            k.gated[pl.ds(start, HALF), :] = mm(
                order_matrix(start, HALF, wide, False), k.inner[...]
            ).astype(bf16)
            return carry

        lax.fori_loop(0, 2, back, 0)


def ffn_forward_body(k):
    gated, x, wo = k.gated(), k.x(), k.wo()
    k.mods(), k.small()
    wu, wn = k.wu(), k.wn()

    def tile(i, carry):
        start = pl.multiple_of(i * HALF, HALF)
        rows = pl.ds(start, HALF)
        slot = k.slot(i)
        grown = mm(gated[rows, :], wo[...])
        k.branch[rows, :] = grown
        middle = x[rows, :].astype(f32) + k.share(slot, 2) * grown
        normal, _ = normalise(middle)
        inner = (normal * (1.0 + k.share(slot, 4)) + k.share(slot, 3)).astype(bf16)
        up = mm(inner, wu[...]) + k.bu()
        _, tanh = gelu_parts(up)
        hidden = (0.5 * up * (1.0 + tanh)).astype(bf16)
        low = mm(hidden, wn[...])
        k.down[rows, :] = low
        result = middle + k.share(slot, 5) * (low + k.bn())
        live = (row_iota(HALF, 1) + start) < k.live_rows
        k.out[rows, :] = jnp.where(live, result, 0.0).astype(bf16)
        return carry

    lax.fori_loop(0, 2, tile, 0)
    if k.layer == 1:
        k.sent[...] = jnp.where(k.section == 0, k.out[...].astype(f32), x[...].astype(f32)).astype(bf16)


def ffn_backward_body(k):
    gmod, gbu, gbn = k.gmod, k.gbu, k.gbn
    gmod[...] = jnp.zeros(gmod.shape, f32)
    gbu[...] = jnp.zeros(gbu.shape, f32)
    gbn[...] = jnp.zeros(gbn.shape, f32)
    k.mods(), k.small()
    x, grad, branch, down = k.x(), k.grad(), k.branch(), k.down()
    wu, wn = k.wu(), k.wn()

    def tile(i, carry):
        start = pl.multiple_of(i * HALF, HALF)
        rows = pl.ds(start, HALF)
        slot = k.slot(i)

        def add(part, values):
            where = (pl.ds(slot, 1), slice((part - 2) * D, (part - 1) * D))
            gmod[where] = gmod[where] + jnp.sum(values, axis=0, keepdims=True)

        grown = branch[rows, :]
        middle = x[rows, :].astype(f32) + k.share(slot, 2) * grown
        normal, rate = normalise(middle)
        inner = (normal * (1.0 + k.share(slot, 4)) + k.share(slot, 3)).astype(bf16)
        k.inner_s[rows, :] = inner
        live = (row_iota(HALF, 1) + start) < k.live_rows
        above = jnp.where(live, grad[rows, :].astype(f32), 0.0)
        add(5, above * (down[rows, :] + k.bn()))
        grad_down = above * k.share(slot, 5)
        gbn[...] = gbn[...] + jnp.sum(grad_down, axis=0, keepdims=True)
        down_low = grad_down.astype(bf16)
        k.down_s[rows, :] = down_low
        up = mm(inner, wu[...]) + k.bu()
        square, tanh = gelu_parts(up)
        half = 0.5 * (1.0 + tanh)
        k.hidden_s[rows, :] = (up * half).astype(bf16)
        slope = half + 0.5 * up * (1.0 - tanh * tanh) * (
            GELU_A * (1.0 + 3.0 * GELU_B * square)
        )
        grad_up = mm_t(down_low, wn[...]) * slope
        gbu[...] = gbu[...] + jnp.sum(grad_up, axis=0, keepdims=True)
        up_low = grad_up.astype(bf16)
        k.up_s[rows, :] = up_low
        grad_inner = mm_t(up_low, wu[...])
        add(3, grad_inner)
        add(4, grad_inner * normal)
        grad_middle = above + normalise_back(
            normal, rate, grad_inner * (1.0 + k.share(slot, 4))
        )
        k.mid_grad[rows, :] = grad_middle
        add(2, grad_middle * grown)
        k.branch_low[rows, :] = (grad_middle * k.share(slot, 2)).astype(bf16)
        return carry

    lax.fori_loop(0, 2, tile, 0)
    k.push("mid_grad")
    k.push("branch_low")

    def weights(j, carry):
        part = pl.ds(pl.multiple_of(j * HALF, HALF), HALF)
        hidden_t = jnp.transpose(k.hidden_s[:, part].astype(f32)).astype(bf16)
        k.gwn[part, :] = mm(hidden_t, k.down_s[...])
        return carry

    lax.fori_loop(0, FF // HALF, weights, 0)
    inner_t = jnp.transpose(k.inner_s[...].astype(f32)).astype(bf16)
    if k.packed:
        devices, shard, _ = k.keep.shape

        def halves(j, carry):
            for kept, own in ((k.keep, c_section), (k.sent, 1 - c_section)):
                columns = pl.ds(pl.multiple_of(j * HALF + own * (FF // 2), HALF), HALF)
                here = pl.ds(pl.multiple_of(j * HALF, HALF), HALF)
                part = mm(inner_t, k.up_s[:, columns]).reshape(devices, shard, HALF)
                kept[:, :, here] = part.astype(kept.dtype)
            return carry

        c_section = k.section
        lax.fori_loop(0, FF // 2 // HALF, halves, 0)

        def owner(r, carry):
            for kept, own in ((k.keep, c_section), (k.sent, 1 - c_section)):
                for piece in range(2):
                    start = pl.multiple_of((4 * r + 2 * own + piece) * shard, 8)
                    rows = k.gwn[pl.ds(start, shard), :]
                    at = FF // 2 + piece * D
                    kept[r, :, at : at + D] = rows.astype(kept.dtype)
            return carry

        lax.fori_loop(0, devices, owner, 0)
        k.push("keep")
        k.push("sent")
    else:
        k.gwu[...] = mm(inner_t, k.up_s[...])
    gated = k.gated()
    k.gwo[...] = mm(jnp.transpose(gated[...].astype(f32)).astype(bf16), k.branch_low[...])

    short = jnp.concatenate([gbn[...], jnp.zeros((1, FF - D), f32)], axis=1)
    k.sums[...] = jnp.concatenate(
        [gmod[0:SLOTS, :], gbu[...], short, jnp.zeros((4, FF), f32)], axis=0
    )


def mixer_backward_body(k):
    flip = k.layer == 1
    wide = k.wide
    mixed_s, low, dv_s, rows_s, cols_s = k.mixed_s, k.low, k.dv_s, k.rows_s, k.cols_s
    fill_bias(k.bias, wide)
    branch_low, wo = k.branch_low(), k.wo()

    def first(i, carry):
        start = pl.multiple_of(i * HALF, HALF)
        rows = pl.ds(start, HALF)
        if flip:
            part = mm(order_matrix(start, HALF, wide, True), branch_low[...]).astype(bf16)
        else:
            part = branch_low[rows, :]
        mixed_s[rows, :] = mm_t(part, wo[...])
        return carry

    lax.fori_loop(0, 2, first, 0)
    rows_s[...] = jnp.zeros(rows_s.shape, f32)
    cols_s[...] = jnp.zeros(cols_s.shape, f32)
    qkvg, vc, cum, cumt, o = k.qkvg(), k.vc(), k.cum(), k.cumt(), k.o()
    k.small()

    def pair(p, carry):
        lanes = lane_iota(1, PAIR)
        total = o[:, columns(p)]
        gate = qkvg[:, columns(p, 3 * D)]
        above = mixed_s[:, columns(p)]
        rate = lax.rsqrt(head_norm(total, lanes) + 1.0)
        sig = sigmoid(gate)
        grad_gate = above * (total * rate) * (sig * (1.0 + gate * (1.0 - sig)))
        low[:, columns(p, 3 * D)] = grad_gate.astype(bf16)
        grad_normed = above * (gate * sig)
        product = grad_normed * total
        inside = jnp.where(
            lanes < HEAD_DIM,
            jnp.sum(jnp.where(lanes < HEAD_DIM, product, 0.0), axis=1, keepdims=True),
            jnp.sum(jnp.where(lanes < HEAD_DIM, 0.0, product), axis=1, keepdims=True),
        ) * (1.0 / HEAD_DIM)
        grad_o = rate * grad_normed - total * (rate * rate * rate) * inside

        queries = qkvg[:, columns(p)] * SCALE
        keys = qkvg[:, columns(p, D)]
        values = vc[:, columns(p)]
        query_cat = cat_left(queries)
        grad_cat = cat_left(grad_o)
        key_high, key_low = split(keys)
        key_pair = jnp.concatenate([key_high, key_low], axis=1)
        query_t = jnp.transpose(queries)
        grad_t = jnp.transpose(grad_o)
        grad_q = []
        grad_k = []
        grad_v = []
        for e in range(2):
            mine = (lanes // HEAD_DIM) == e
            head = 2 * p + e
            key_cat = cat_right(jnp.where(mine, keys, 0.0))
            value_cat = cat_right(jnp.where(mine, values, 0.0))
            first, second = decay_factors(cum, cumt, k.bias, head)
            raw_first = mm_t(query_cat[:HALF], key_cat[:HALF])
            raw_second = mm_t(query_cat[HALF:], key_cat)
            grad_first = first * mm_t(grad_cat[:HALF], value_cat[:HALF])
            grad_second = second * mm_t(grad_cat[HALF:], value_cat)
            score_first = raw_first * first
            score_second = raw_second * second
            pull_first = grad_first * raw_first
            pull_second = grad_second * raw_second
            here = lanes == head
            rows_s[:HALF, :] = rows_s[:HALF, :] + jnp.where(
                here, jnp.sum(pull_first, axis=1, keepdims=True), 0.0
            )
            rows_s[HALF:, :] = rows_s[HALF:, :] + jnp.where(
                here, jnp.sum(pull_second, axis=1, keepdims=True), 0.0
            )
            low_cols = jnp.sum(pull_second, axis=0, keepdims=True)
            cols_s[pl.ds(head, 1), :HALF] = low_cols[:, :HALF] + jnp.sum(
                pull_first, axis=0, keepdims=True
            )
            cols_s[pl.ds(head, 1), HALF:] = low_cols[:, HALF:]
            grad_q.append(
                jnp.concatenate(
                    [
                        mm_near(grad_first, key_pair[:HALF], key_high[:HALF]),
                        mm_near(grad_second, key_pair, key_high),
                    ],
                    axis=0,
                )
            )

            def turned(source_t, block_first, block_second):
                high, low = split(source_t[e * HEAD_DIM : (e + 1) * HEAD_DIM, :])
                both = jnp.concatenate([high, low], axis=0)
                first_high, first_low = split(block_first)
                second_high, second_low = split(block_second)
                one = mm(both[:, :HALF], first_high)
                one = one[:HEAD_DIM] + one[HEAD_DIM:] + mm(high[:, :HALF], first_low)
                two = mm(both[:, HALF:], second_high)
                two = two[:HEAD_DIM] + two[HEAD_DIM:] + mm(high[:, HALF:], second_low)
                return jnp.concatenate([two[:, :HALF] + one, two[:, HALF:]], axis=1)

            grad_k.append(turned(query_t, grad_first, grad_second))
            grad_v.append(turned(grad_t, score_first, score_second))
        query_grad = jnp.where(lanes < HEAD_DIM, grad_q[0], grad_q[1]) * SCALE
        low[:, columns(p)] = query_grad.astype(bf16)
        low[:, columns(p, D)] = jnp.transpose(jnp.concatenate(grad_k, axis=0)).astype(bf16)
        dv_s[:ROWS, columns(p)] = jnp.transpose(jnp.concatenate(grad_v, axis=0))
        return carry

    lax.fori_loop(0, PAIRS, pair, 0)

    pulled = rows_s[...] - jnp.transpose(cols_s[...])
    high, middle, rest = split_three(pulled)
    upper_first = jnp.concatenate(
        [
            jnp.where(row_iota(HALF, HALF) <= lane_iota(HALF, HALF), 1.0, 0.0),
            jnp.full((HALF, HALF), 0.0, f32) + jnp.where(wide, 1.0, 0.0),
        ],
        axis=1,
    ).astype(bf16)
    upper_second = upper_first[:, :HALF]
    later = jnp.concatenate(
        [
            mm(upper_first, high) + mm(upper_first, middle) + mm(upper_first, rest),
            mm(upper_second, high[HALF:]) + mm(upper_second, middle[HALF:])
            + mm(upper_second, rest[HALF:]),
        ],
        axis=0,
    )
    grad_dp = later * (1.0 / 16.0) * sigmoid(-(k.dp()[...] + k.bd()))
    grad_bd = jnp.sum(grad_dp, axis=0, keepdims=True)
    low[:, QKVG:] = grad_dp.astype(bf16)

    dv_s[ROWS:, :] = jnp.zeros((8, D), f32)
    position = row_iota(ROWS, 1) & jnp.where(wide, ROWS - 1, HALF - 1)
    last = jnp.where(wide, ROWS - 1, HALF - 1)
    here = dv_s[0:ROWS, :]
    one = jnp.where(position <= last - 1, dv_s[1 : 1 + ROWS, :], 0.0)
    two = jnp.where(position <= last - 2, dv_s[2 : 2 + ROWS, :], 0.0)
    value = qkvg[:, 2 * D : 3 * D]
    low[:, 2 * D : 3 * D] = (k.ck(0) * here + k.ck(1) * one + k.ck(2) * two).astype(bf16)
    k.push("low")

    taps = [jnp.sum(rows * value, axis=0, keepdims=True) for rows in (here, one, two)]
    rest = jnp.concatenate([grad_bd, jnp.zeros((1, D - LANES), f32)], axis=1)
    k.sums[...] = jnp.concatenate([*taps, rest, jnp.zeros((4, D), f32)], axis=0)

    ordered_t = jnp.transpose(k.ordered()[...].astype(f32)).astype(bf16)
    gwo = k.gwo()
    gw = k.gw

    def weights(j, carry):
        part = pl.ds(pl.multiple_of(j * HALF, HALF), HALF)
        gw[:, part] = mm(ordered_t, low[:, part])
        return carry

    lax.fori_loop(0, QKVG // HALF, weights, 0)
    gw[:, QKVG : QKVG + D] = gwo[...]
    gw[:, QKVG + D :] = mm(ordered_t, low[:, QKVG:])

    def halves(j, carry):
        here = pl.ds(pl.multiple_of(j * HALF, HALF), HALF)
        keep = pl.ds(pl.multiple_of(j * HALF + k.section * GROUP, HALF), HALF)
        send = pl.ds(pl.multiple_of(j * HALF + (1 - k.section) * GROUP, HALF), HALF)
        k.gw_keep[:, here] = gw[:, keep]
        k.gw_send[:, here] = gw[:, send].astype(bf16)
        return carry

    lax.fori_loop(0, GROUP // HALF, halves, 0)


def input_backward_body(k):
    flip = k.layer == 1
    wide = k.wide
    gmod, mixed_s, perm_s = k.gmod, k.mixed_s, k.perm_s
    gmod[...] = jnp.zeros(gmod.shape, f32)
    low, w_qk, w_vgd = k.low(), k.w_qk(), k.w_vgd()

    def inner_grad(i, carry):
        rows = pl.ds(pl.multiple_of(i * HALF, HALF), HALF)
        mixed_s[rows, :] = mm_t(low[rows, : 2 * D], w_qk[...]) + mm_t(
            low[rows, 2 * D :], w_vgd[...]
        )
        return carry

    lax.fori_loop(0, 2, inner_grad, 0)
    if flip:
        high, middle, rest = split_three(mixed_s[...])
        perm_s[:, :D] = high
        perm_s[:, D : 2 * D] = middle
        perm_s[:, 2 * D :] = rest
    x, mid_grad = k.x(), k.mid_grad()
    k.mods()

    def tile(i, carry):
        start = pl.multiple_of(i * HALF, HALF)
        rows = pl.ds(start, HALF)
        slot = k.slot(i)
        if flip:
            three = mm(order_matrix(start, HALF, wide, False), perm_s[...])
            grad = three[:, :D] + three[:, D : 2 * D] + three[:, 2 * D :]
        else:
            grad = mixed_s[rows, :]
        normal, rate = normalise(x[rows, :].astype(f32))
        where = (pl.ds(slot, 1), slice(0, D))
        gmod[where] = gmod[where] + jnp.sum(grad, axis=0, keepdims=True)
        where = (pl.ds(slot, 1), slice(D, 2 * D))
        gmod[where] = gmod[where] + jnp.sum(grad * normal, axis=0, keepdims=True)
        total = mid_grad[rows, :] + normalise_back(normal, rate, grad * (1.0 + k.share(slot, 1)))
        k.gx[rows, :] = total
        k.gx_low[rows, :] = total.astype(bf16)
        return carry

    lax.fori_loop(0, 2, tile, 0)
    k.push("gx_low")
    k.push("gx")
    ffn, mixer = k.ffn_sums(), k.mixer_sums()
    k.mod_low[...] = jnp.concatenate([gmod[...], ffn[...]], axis=1).astype(bf16)
    if k.layer == 0:
        first = k.section == 0
        k.gx_send[...] = jnp.where(first, k.gx_two()[...], k.gx[...])
        one, two = k.mod_low[...].astype(f32), k.mod_two()[...].astype(f32)
        k.mod_mine[...] = jnp.where(first, one, two).astype(bf16)
        k.mod_send[...] = jnp.where(first, two, one).astype(bf16)
    half = 2 * D
    rest = ffn[0:1, :] + ffn[1:2, :]
    k.sums[...] = jnp.concatenate(
        [
            gmod[0:1, :] + gmod[1:2, :],
            rest[:, :half],
            rest[:, half:],
            ffn[2:3, :half],
            ffn[2:3, half:],
            jnp.concatenate([ffn[3:4, :D], mixer[0:1, :]], axis=1),
            jnp.concatenate([mixer[1:2, :], mixer[2:3, :]], axis=1),
            jnp.concatenate([mixer[3:4, :], jnp.zeros((1, D), f32)], axis=1),
        ],
        axis=0,
    )


ANY = pl.BlockSpec(memory_space=pl.ANY)
VMEM = pl.BlockSpec(memory_space=pltpu.VMEM)
HBM = pl.BlockSpec(memory_space=pltpu.HBM)


def call(body, layer, layouts, ins, outs, scratch, flops, packed=None):
    arrays = []
    counts = []
    kept = []
    places = []
    for kind, given, part in ins.values():
        places.extend([ANY] * 2 if kind == "own" else [HBM])
        given = given if kind == "own" else (given,)
        arrays.extend(given)
        counts.append(len(given))
        rows, wide = given[0].shape[-2:]
        start, stop = part or (0, wide)
        kept.append(pltpu.VMEM((rows, stop - start), given[0].dtype))

    def kernel(*refs):
        refs = list(refs)
        take = lambda count: [refs.pop(0) for _ in range(count)]
        (layouts_ref,) = take(1)
        sources = [take(count) for count in counts]
        targets = take(len(outs))
        buffers = take(len(ins))
        results = take(len(outs))
        rest = take(len(scratch))
        in_sems, out_sems = refs
        k = Kernel(layer, layouts_ref)
        k.packed = packed
        for number, (name, (kind, _, part)) in enumerate(ins.items()):
            given = sources[number]
            if part is not None:
                given = [ref.at[:, part[0] : part[1]] for ref in given]
            setattr(k, name, k.load(kind, given, buffers[number], in_sems.at[number]))
        k.results = {}
        for number, name in enumerate(outs):
            setattr(k, name, results[number])
            k.results[name] = (results[number], targets[number], out_sems.at[number])
        for name, ref in zip(scratch, rest):
            setattr(k, name, ref)
        body(k)
        k.finish()

    return pl.pallas_call(
        kernel,
        out_shape=[jax.ShapeDtypeStruct(shape, kind) for shape, kind, _ in outs.values()],
        in_specs=[pl.BlockSpec(memory_space=pltpu.SMEM)] + places,
        out_specs=[HBM if for_kernel else ANY for _, _, for_kernel in outs.values()],
        scratch_shapes=kept
        + [pltpu.VMEM(shape, kind) for shape, kind, _ in outs.values()]
        + [pltpu.VMEM(shape, kind) for shape, kind in scratch.values()]
        + [pltpu.SemaphoreType.DMA((len(ins),)), pltpu.SemaphoreType.DMA((len(outs),))],
        compiler_params=pltpu.CompilerParams(vmem_limit_bytes=28 * 1024 * 1024),
        cost_estimate=pl.CostEstimate(flops=flops, bytes_accessed=4 << 20, transcendentals=0),
    )(layouts, *arrays)


def own(pair, part=None):
    return ("own", pair, part)


def plain(array):
    return ("plain", array, None)


def micro(array):
    return ("micro", array, None)


ADA_CUT = 9 * LANES
AT_QK = (0, 2 * D)
AT_ADA_A = (2 * D, 2 * D + ADA_CUT)
AT_VGD = (0, 2 * D + LANES)
AT_ADA_B = (2 * D + LANES, 8 * D + LANES - ADA_CUT)
AT_UP = (0, FF)
AT_OUT = (FF, FF + D)


def attn_forward(layer, layouts, x, mods, small, qka, vgda):
    return call(
        attn_forward_body,
        layer,
        layouts,
        dict(
            x=micro(x),
            mods=own(mods),
            w_qk=own(qka, AT_QK),
            w_vgd=own(vgda, AT_VGD),
            small=own(small),
        ),
        dict(
            ordered=((ROWS, D), bf16, True),
            qkvg=((ROWS, QKVG), f32, True),
            dp=((ROWS, LANES), f32, True),
            vc=((ROWS, D), f32, True),
            cum=((ROWS, LANES), f32, True),
            cumt=((LANES, ROWS), f32, True),
            o=((ROWS, D), f32, True),
            gated=((ROWS, D), bf16, True),
        ),
        dict(
            inner=((ROWS, D), bf16),
            vpad=((ROWS + 8, D), f32),
            bias=((HALF, ROWS), f32),
        ),
        8 * 10**9,
    )


def ffn_forward(layer, layouts, x, mods, small, gated, upo, down):
    return call(
        ffn_forward_body,
        layer,
        layouts,
        dict(
            gated=plain(gated),
            x=micro(x),
            wo=own(upo, AT_OUT),
            mods=own(mods),
            small=own(small),
            wu=own(upo, AT_UP),
            wn=own(down),
        ),
        dict(
            out=((ROWS, D), bf16, True),
            branch=((ROWS, D), f32, True),
            down=((ROWS, D), f32, True),
            **({"sent": ((ROWS, D), bf16, False)} if layer == 1 else {}),
        ),
        {},
        5 * 10**9,
    )


def ffn_backward(
    layer, layouts, x, mods, small, gated, branch, down_raw, grad, upo, down, devices
):
    shard = D // devices
    in_kernel = shard % 8 == 0
    if in_kernel:
        sums = dict(
            keep=((devices, shard, FF), f32, False),
            sent=((devices, shard, FF), bf16, False),
        )
    else:
        sums = dict(gwu=((D, FF), f32, False), gwn=((FF, D), f32, False))
    return call(
        ffn_backward_body,
        layer,
        layouts,
        dict(
            mods=own(mods),
            small=own(small),
            x=micro(x),
            grad=micro(grad),
            branch=plain(branch),
            down=plain(down_raw),
            wu=own(upo, AT_UP),
            wn=own(down),
            gated=plain(gated),
        ),
        dict(
            mid_grad=((ROWS, D), f32, True),
            branch_low=((ROWS, D), bf16, True),
            gwo=((D, D), f32, True),
            sums=((8, FF), f32, True),
            **sums,
        ),
        dict(
            **({"gwn": ((FF, D), f32)} if in_kernel else {}),
            hidden_s=((ROWS, FF), bf16),
            inner_s=((ROWS, D), bf16),
            up_s=((ROWS, FF), bf16),
            down_s=((ROWS, D), bf16),
            gmod=((8, FF), f32),
            gbu=((1, FF), f32),
            gbn=((1, D), f32),
        ),
        12 * 10**9,
        packed=in_kernel,
    )


def mixer_backward(layer, layouts, small, saved, branch_low, gwo, upo):
    ordered, qkvg, dp, vc, cum, cumt, o = saved
    return call(
        mixer_backward_body,
        layer,
        layouts,
        dict(
            branch_low=plain(branch_low),
            wo=own(upo, AT_OUT),
            qkvg=plain(qkvg),
            vc=plain(vc),
            cum=plain(cum),
            cumt=plain(cumt),
            o=plain(o),
            small=own(small),
            dp=plain(dp),
            ordered=plain(ordered),
            gwo=plain(gwo),
        ),
        dict(
            low=((ROWS, QKVG + LANES), bf16, True),
            gw_keep=((D, GROUP), f32, False),
            gw_send=((D, GROUP), bf16, False),
            sums=((8, D), f32, True),
        ),
        dict(
            mixed_s=((ROWS, D), f32),
            dv_s=((ROWS + 8, D), f32),
            rows_s=((ROWS, LANES), f32),
            cols_s=((LANES, ROWS), f32),
            bias=((HALF, ROWS), f32),
            gw=((D, 2 * GROUP), f32),
        ),
        15 * 10**9,
    )


def input_backward(
    layer, layouts, x, mods, low, mid_grad, ffn_sums, mixer_sums, qka, vgda, two=None
):
    extra_in, extra_out = {}, {}
    if two is not None:
        extra_in = dict(gx_two=plain(two[0]), mod_two=plain(two[1]))
        extra_out = dict(
            gx_send=((ROWS, D), f32, False),
            mod_mine=((8, 6 * D), bf16, False),
            mod_send=((8, 6 * D), bf16, False),
        )
    return call(
        input_backward_body,
        layer,
        layouts,
        dict(
            low=plain(low),
            w_qk=own(qka, AT_QK),
            w_vgd=own(vgda, AT_VGD),
            x=micro(x),
            mid_grad=plain(mid_grad),
            mods=own(mods),
            ffn_sums=plain(ffn_sums),
            mixer_sums=plain(mixer_sums),
            **extra_in,
        ),
        dict(
            gx=((ROWS, D), f32, True),
            gx_low=((ROWS, D), bf16, True),
            mod_low=((8, 6 * D), bf16, True),
            sums=((8, 2 * D), f32, False),
            **extra_out,
        ),
        dict(
            mixed_s=((ROWS, D), f32),
            perm_s=((ROWS, 3 * D), bf16),
            gmod=((8, 2 * D), f32),
        ),
        4 * 10**9,
    )


def small_kernel(b_up, b_down, taps, b_decay, packed):
    packed[...] = jnp.zeros(packed.shape, f32)
    packed[0:1, :] = b_up[...]
    packed[1:2, :D] = b_down[...]
    packed[2:5, :D] = taps[0]
    packed[5:6, :HEADS] = b_decay[...]


def pack_small(b_up, b_down, taps, b_decay):
    return pl.pallas_call(
        small_kernel,
        out_shape=jax.ShapeDtypeStruct((8, FF), f32),
        in_specs=[VMEM] * 4,
        out_specs=VMEM,
    )(b_up, b_down, taps, b_decay)


def pack_kernel(w_query, w_key, w_value, w_gate, w_out, w_decay, w_ada, w_up, qka, vgda, upo):
    qka[:, :D] = w_query[0]
    qka[:, D : 2 * D] = w_key[0]
    qka[:, 2 * D :] = w_ada[0, :, :ADA_CUT]
    vgda[:, :D] = w_value[0]
    vgda[:, D : 2 * D] = w_gate[0]
    vgda[:, 2 * D : 2 * D + LANES] = jnp.zeros((vgda.shape[0], LANES), bf16)
    vgda[:, 2 * D : 2 * D + HEADS] = w_decay[0]
    vgda[:, 2 * D + LANES :] = w_ada[0, :, ADA_CUT:]
    upo[:, :FF] = w_up[0]
    upo[:, FF:] = w_out[0]


def pack(*weights):
    shard = weights[0].shape[1]
    widths = (2 * D + ADA_CUT, 8 * D + LANES - ADA_CUT, FF + D)
    return pl.pallas_call(
        pack_kernel,
        out_shape=[jax.ShapeDtypeStruct((shard, width), bf16) for width in widths],
        in_specs=[VMEM] * len(weights),
        out_specs=[VMEM] * len(widths),
    )(*weights)


def join_kernel(bits, *refs):
    count = len(bits)
    held, came, out = refs[:count], refs[count : 2 * count], refs[2 * count :]
    for i, bit in enumerate(bits):
        mine = (lax.axis_index("row") >> bit) & 1
        out[i][:, mine] = held[i][...]
        out[i][:, 1 - mine] = came[i][...]


def join(held, came, bits):
    def parts(array, bit):
        axis = axis_of(bit)
        above = 1
        for size in array.shape[:axis]:
            above *= size
        return array.reshape((above, -1) + array.shape[-2:])

    split_held = [parts(array, bit) for array, bit in zip(held, bits)]
    split_came = [parts(array, bit) for array, bit in zip(came, bits)]
    out = pl.pallas_call(
        functools.partial(join_kernel, bits),
        out_shape=[
            jax.ShapeDtypeStruct(array.shape[:1] + (2,) + array.shape[1:], array.dtype)
            for array in split_held
        ],
        in_specs=[VMEM] * (2 * len(held)),
        out_specs=[VMEM] * len(held),
        compiler_params=pltpu.CompilerParams(vmem_limit_bytes=8 * 1024 * 1024),
        cost_estimate=pl.CostEstimate(flops=10**6, bytes_accessed=10**6, transcendentals=0),
    )(*split_held, *split_came)
    joined = []
    for array, result, bit in zip(held, out, bits):
        shape = list(array.shape)
        shape[axis_of(bit)] = 2
        joined.append(result.reshape(shape))
    return joined


def mods_kernel(conditions, bias, packed, vgd, out, ada_a, ada_b, sems):
    copies = [
        pltpu.make_async_copy(packed.at[:, AT_ADA_A[0] : AT_ADA_A[1]], ada_a, sems.at[0]),
        pltpu.make_async_copy(vgd.at[:, AT_ADA_B[0] : AT_ADA_B[1]], ada_b, sems.at[1]),
    ]
    for copy in copies:
        copy.start()
    values = conditions[...].astype(f32)
    lifted = (values * sigmoid(values)).astype(bf16)
    for copy in copies:
        copy.wait()
    out[...] = jnp.concatenate([mm(lifted, ada_a[...]), mm(lifted, ada_b[...])], axis=1) + bias[...]


ADA_SCRATCH = [
    pltpu.VMEM((D, ADA_CUT), bf16),
    pltpu.VMEM((D, 6 * D - ADA_CUT), bf16),
    pltpu.SemaphoreType.DMA((2,)),
]


def modulations(conditions, bias, packed, vgd):
    return pl.pallas_call(
        mods_kernel,
        out_shape=jax.ShapeDtypeStruct((MICRO * SLOTS, 6 * D), f32),
        in_specs=[VMEM, VMEM, ANY, ANY],
        out_specs=VMEM,
        scratch_shapes=ADA_SCRATCH,
        compiler_params=pltpu.CompilerParams(vmem_limit_bytes=16 * 1024 * 1024),
        cost_estimate=pl.CostEstimate(flops=10**9, bytes_accessed=2 << 20, transcendentals=0),
    )(conditions, bias, packed, vgd)


def lifted_kernel(mine, came, packed, vgd, out, ada_a, ada_b, sems):
    copies = [
        pltpu.make_async_copy(packed.at[:, AT_ADA_A[0] : AT_ADA_A[1]], ada_a, sems.at[0]),
        pltpu.make_async_copy(vgd.at[:, AT_ADA_B[0] : AT_ADA_B[1]], ada_b, sems.at[1]),
    ]
    for copy in copies:
        copy.start()
    for copy in copies:
        copy.wait()
    first = lax.axis_index("section") == 0
    pair = mine[0:SLOTS, :].astype(f32), came[0:SLOTS, :].astype(f32)
    grad = jnp.concatenate(
        [jnp.where(first, pair[0], pair[1]), jnp.where(first, pair[1], pair[0])], axis=0
    ).astype(bf16)
    out[...] = mm_t(grad[:, :ADA_CUT], ada_a[...]) + mm_t(grad[:, ADA_CUT:], ada_b[...])


def lifted_grads(mine, came, packed, vgd):
    return pl.pallas_call(
        lifted_kernel,
        out_shape=jax.ShapeDtypeStruct((MICRO * SLOTS, D), f32),
        in_specs=[VMEM, VMEM, ANY, ANY],
        out_specs=VMEM,
        scratch_shapes=ADA_SCRATCH,
        compiler_params=pltpu.CompilerParams(vmem_limit_bytes=16 * 1024 * 1024),
        cost_estimate=pl.CostEstimate(flops=10**9, bytes_accessed=2 << 20, transcendentals=0),
    )(mine, came, packed, vgd)


def step_kernel(bit, widths, counts, misc, *refs):
    mine = (lax.axis_index("row") >> bit) & 1
    count = len(widths)
    kept, refs = refs[:count], refs[count:]
    came, refs = refs[: len(counts)], refs[len(counts) :]
    if misc:
        (held, arrived), refs = refs[:2], refs[2:]
    stays, goes = refs[:count], refs[count]
    places = [(ref, i) for ref, many in zip(came, counts) for i in range(many)]
    at = 0
    for i in range(count):
        ref, place = places[i]
        start = sum(widths[i - place : i])
        columns = slice(start, start + widths[i])
        stays[i][...] = kept[i][:, mine] + ref[:, mine, :, :, columns].astype(f32)
        total = kept[i][:, 1 - mine] + ref[:, 1 - mine, :, :, columns].astype(f32)
        goes[:, :, :, at : at + widths[i]] = total.astype(bf16)
        at += widths[i]
    if misc:
        grow_misc(held, arrived, refs[count + 1])


def grow_misc(held, arrived, out):
    size = held.shape[0] - SUMS
    out[:size, :] = held[:size, :]
    out[size : 2 * size, :] = arrived[:size, :]
    high, low = split(misc_sums(held, arrived))
    out[2 * size : 2 * size + SUMS // 2, :] = high
    out[2 * size + SUMS // 2 :, :] = low


def misc_sums(*refs):
    size = refs[0].shape[0] - SUMS
    parts = [ref[size:, :].astype(f32) for ref in refs]
    return sum(part[: SUMS // 2] + part[SUMS // 2 :] for part in parts)


def step(kept, came, bit, misc=None, below=1):
    blocks, rows = kept[0].shape[0] // 2, kept[0].shape[1]
    above = blocks // below
    paired = lambda array: array.reshape((above, 2, below) + array.shape[1:])
    widths = [array.shape[2] for array in kept]
    size = sum(array.size for array in kept)
    shapes = [jax.ShapeDtypeStruct((above, below, rows, width), f32) for width in widths]
    shapes.append(jax.ShapeDtypeStruct((above, below, rows, sum(widths)), bf16))
    extra = ()
    if misc is not None:
        extra = misc
        shapes.append(jax.ShapeDtypeStruct((2 * misc[0].shape[0] - SUMS, 2 * D), bf16))
    out = pl.pallas_call(
        functools.partial(
            step_kernel, bit, widths, [count for _, count in came], misc is not None
        ),
        out_shape=shapes,
        in_specs=[VMEM] * (len(kept) + len(came) + len(extra)),
        out_specs=[VMEM] * len(shapes),
        compiler_params=pltpu.CompilerParams(vmem_limit_bytes=8 * 1024 * 1024),
        cost_estimate=pl.CostEstimate(flops=size, bytes_accessed=8 * size, transcendentals=0),
    )(*[paired(array) for array in kept], *[paired(array) for array, _ in came], *extra)
    count = len(kept)
    flat_blocks = [array.reshape((blocks,) + array.shape[2:]) for array in out[: count + 1]]
    return (flat_blocks[:count], flat_blocks[count]) + tuple(out[count + 1 :])


SUMS = 32


def misc_rows(conditions, mod_low):
    values = conditions[...].astype(f32)
    values = jnp.where(lax.axis_index("section") == 0, values[:SLOTS], values[SLOTS:])
    lifted = (values * sigmoid(values)).astype(bf16).astype(f32)
    rows = [
        mod_low[slot : slot + 1, i * 2 * D : (i + 1) * 2 * D].astype(f32)
        for slot in range(SLOTS)
        for i in range(3)
    ]
    rows.append(jnp.concatenate([lifted[0:1], lifted[1:2]], axis=1))
    rows.append(jnp.zeros((1, 2 * D), f32))
    return jnp.concatenate(rows, axis=0)


def misc_kernel(conditions, mod_low, *refs):
    out = refs[-1]
    rows = [misc_rows(conditions, mod_low)]
    if len(refs) == 3:
        rows.extend(part.astype(f32) for part in split(jnp.concatenate([refs[0][...], refs[1][...]], axis=0)))
    out[...] = jnp.concatenate(rows, axis=0).astype(bf16)


def pack_misc(conditions, mod_low, *sums):
    return pl.pallas_call(
        misc_kernel,
        out_shape=jax.ShapeDtypeStruct((8 + (SUMS if sums else 0), 2 * D), bf16),
        in_specs=[VMEM] * (2 + len(sums)),
        out_specs=VMEM,
    )(conditions, mod_low, *sums)


def grow_kernel(held, came, out):
    size = held.shape[0]
    out[:size, :] = held[...]
    out[size:, :] = came[...]


def grow(held, bit):
    came = partner(held, bit)
    return pl.pallas_call(
        grow_kernel,
        out_shape=jax.ShapeDtypeStruct((2 * held.shape[0], held.shape[1]), held.dtype),
        in_specs=[VMEM] * 2,
        out_specs=VMEM,
        cost_estimate=pl.CostEstimate(flops=10**5, bytes_accessed=10**5, transcendentals=0),
    )(held, came)


def finish_kernel(widths, counts, *refs):
    count = len(widths)
    kept, refs = refs[:count], refs[count:]
    came, refs = refs[: len(counts)], refs[len(counts) :]
    lifted, mod_two, misc, misc_came, mine, other, small_mine, small_other = refs
    places = [(ref, i) for ref, many in zip(came, counts) for i in range(many)]
    added = []
    for i in range(count):
        ref, place = places[i]
        start = sum(widths[i - place : i])
        added.append(kept[i][0] + ref[0, :, start : start + widths[i]].astype(f32))
    a1, f1, f2, a2 = added
    size = misc.shape[0] - SUMS
    mod_one = jnp.concatenate([misc[:size, :], misc_came[:size, :]], axis=0)

    def ada(rows):
        rows = rows.astype(f32).reshape(-1, 8, 2 * D)
        columns = []
        for i in range(3):
            both = [rows[:, 3 * slot + i, :] for slot in range(SLOTS)]
            columns.append(mm(lifted[...], jnp.concatenate(both, axis=0).astype(bf16)))
        return jnp.concatenate(columns, axis=1)

    first = lax.axis_index("section") == 0
    at = 0
    for one, two in ((a1, a2), (f1, f2), (ada(mod_one), ada(mod_two[...]))):
        columns = slice(at, at + one.shape[1])
        mine[:, columns] = jnp.where(first, one, two)
        other[:, columns] = jnp.where(first, two, one)
        at += one.shape[1]
    total = misc_sums(misc, misc_came)
    one, two = total[0:8, :], total[8:16, :]
    small_mine[...] = jnp.where(first, one, two)
    small_other[...] = jnp.where(first, two, one)


def finish(kept, came, lifted, mod_two, misc, misc_came):
    widths = [array.shape[2] for array in kept]
    shard = kept[0].shape[1]
    wide = GROUP + FF + 6 * D
    arrays = [array for array, _ in came]
    shapes = [(shard, wide)] * 2 + [(8, 2 * D)] * 2
    return pl.pallas_call(
        functools.partial(finish_kernel, widths, [count for _, count in came]),
        out_shape=[jax.ShapeDtypeStruct(shape, f32) for shape in shapes],
        in_specs=[VMEM] * (len(kept) + len(came) + 4),
        out_specs=[VMEM] * 4,
        compiler_params=pltpu.CompilerParams(vmem_limit_bytes=8 * 1024 * 1024),
    )(*kept, *arrays, lifted, mod_two, misc, misc_came)


def output_kernel(mine, other, small_mine, small_other, *outs):
    first = lax.axis_index("section") == 0

    def halves(start, width):
        columns = slice(start, start + width)
        pair = mine[:, columns], other[:, columns]
        return jnp.where(first, pair[0], pair[1]), jnp.where(first, pair[1], pair[0])

    attn = halves(0, GROUP)
    cut = GROUP - 2 * D
    outs[0][...] = attn[0][:, :D]
    outs[1][...] = attn[0][:, D : 2 * D]
    outs[2][:, :cut] = attn[0][:, 2 * D :]
    outs[2][:, cut:] = attn[1][:, : D - cut]
    outs[3][...] = attn[1][:, D - cut : 2 * D - cut]
    outs[4][...] = attn[1][:, 2 * D - cut : 3 * D - cut]
    decay = jnp.transpose(attn[1][:, 3 * D - cut :])
    for head in range(HEADS):
        outs[5][head] = decay[head : head + 1, :]
    up = halves(GROUP, FF // 2)
    outs[6][:, : FF // 2] = up[0]
    outs[6][:, FF // 2 :] = up[1]
    for piece in range(2):
        down = halves(GROUP + FF // 2 + piece * D, D)
        outs[7][piece] = down[0]
        outs[7][2 + piece] = down[1]
    outs[8][...] = mine[:, GROUP + FF :] + other[:, GROUP + FF :]
    small = small_mine[...] + small_other[...]
    half = 2 * D
    for i in range(3):
        outs[9][:, i * half : (i + 1) * half] = small[i : i + 1, :]
    for i in range(2):
        outs[10][:, i * half : (i + 1) * half] = small[3 + i : 4 + i, :]
    outs[11][...] = small[5:6, :D]
    outs[12][0] = small[5:6, D:]
    outs[12][1] = small[6:7, :D]
    outs[12][2] = small[6:7, D:]
    outs[13][...] = small[7:8, :HEADS]


def outputs(mine, other, small_mine, small_other):
    shard = mine.shape[0]
    shapes = (
        [(shard, D)] * 5
        + [(HEADS, 1, shard), (shard, FF), (4, shard, D), (shard, 6 * D)]
        + [(1, 6 * D), (1, FF), (1, D), (3, 1, D), (1, HEADS)]
    )
    return pl.pallas_call(
        output_kernel,
        out_shape=[jax.ShapeDtypeStruct(shape, f32) for shape in shapes],
        in_specs=[VMEM] * 4,
        out_specs=[VMEM] * len(shapes),
    )(mine, other, small_mine, small_other)


def both_kernel(one, two, came, out, kept, sems):
    section = lax.axis_index("section")

    def move(mine, layer):
        arrive = [
            pltpu.make_async_copy(mine, kept.at[layer], sems.at[0]),
            pltpu.make_async_copy(came, kept.at[1 - layer], sems.at[1]),
        ]
        leave = [
            pltpu.make_async_copy(kept.at[layer], out.at[layer], sems.at[2]),
            pltpu.make_async_copy(kept.at[1 - layer], out.at[1 - layer], sems.at[3]),
        ]
        for copy in arrive:
            copy.start()
        for copy, after in zip(arrive, leave):
            copy.wait()
            after.start()
        for copy in leave:
            copy.wait()

    @pl.when(section == 0)
    def _():
        move(one, 0)

    @pl.when(section == 1)
    def _():
        move(two, 1)


def both_micros(one, two, came):
    return pl.pallas_call(
        both_kernel,
        out_shape=jax.ShapeDtypeStruct((MICRO,) + one.shape, one.dtype),
        in_specs=[ANY] * 3,
        out_specs=ANY,
        scratch_shapes=[
            pltpu.VMEM((MICRO,) + one.shape, one.dtype),
            pltpu.SemaphoreType.DMA((4,)),
        ],
    )(one, two, came)


def swap(values):
    return lax.ppermute(values, "section", [(0, 1), (1, 0)])


def row_bits():
    bits = lax.axis_size("row").bit_length() - 1
    third = bits // 3
    return (
        tuple(range(third)),
        tuple(range(third, 2 * third)),
        tuple(range(2 * third, bits)),
    )


def partner(values, bit):
    size = lax.axis_size("row")
    return lax.ppermute(values, "row", [(i, i ^ (1 << bit)) for i in range(size)])


def axis_of(bit):
    return lax.axis_size("row").bit_length() - 2 - bit


def bit_of(bit):
    return (lax.axis_index("row") >> bit) & 1


def single(values):
    return values.reshape((1,) * (lax.axis_size("row").bit_length() - 1) + values.shape)


def gather_pair(first, second, along_x, along_y, along_z):
    held = [single(first), single(second)]
    steps = [(bit, bit) for bit in reversed(along_z)]
    steps += list(zip(along_x + along_y, along_y + along_x))
    for bits in steps:
        came = [partner(array, bit) for array, bit in zip(held, bits)]
        held = join(held, came, bits)
    return [flat(array) for array in held]


def flat(held):
    return held.reshape(-1, held.shape[-1])


def lock(*arrays):
    return lax.optimization_barrier(arrays)


def on_device(
    tokens, conditions, output_grad, layouts,
    w_ada, b_ada, w_query, w_key, w_value, w_gate, w_out, w_decay, b_decay, conv_kernel,
    w_up, b_up, w_down, b_down,
):
    section = lax.axis_index("section")
    devices = lax.axis_size("row")
    shard = w_query.shape[1]
    along_x, along_y, along_z = row_bits()

    def both(values):
        return values, swap(values)

    qka, vgda, upo = pack(w_query, w_key, w_value, w_gate, w_out, w_decay, w_ada, w_up)
    runs = (along_x, along_y, along_z)
    qka, vgda = [both(array) for array in gather_pair(qka, vgda, *runs)]
    upo, down = [both(array) for array in gather_pair(upo, w_down[0], *runs)]

    conds = conditions.reshape(MICRO * SLOTS, D)
    mods = both(modulations(conds, b_ada, qka[0], vgda[0]))
    smalls = both(pack_small(b_up, b_down, conv_kernel, b_decay))

    x = tokens
    kept = []
    acts = []
    for l in range(2):
        *saved, gated = attn_forward(l, layouts, x, mods, smalls, qka, vgda)
        out, branch, down_raw, *acts_sent = ffn_forward(
            l, layouts, x, mods, smalls, gated, upo, down
        )
        kept.append((x, saved, gated, branch, down_raw))
        acts.append(out)
        x = out[None]

    def ffn_step(l, grad):
        x, saved, gated, branch, down_raw = kept[l]
        mid_grad, branch_low, gwo, sums, *terms = ffn_backward(
            l, layouts, x, mods, smalls, gated, branch, down_raw, grad, upo, down, devices
        )
        if terms[0].ndim == 2:
            up_sum = terms[0].reshape(devices, shard, 2, FF // 2)
            down_sum = terms[1].reshape(devices, 2, 2, shard, D)
            terms = []
            for own in (section, 1 - section):
                up_half = lax.dynamic_index_in_dim(up_sum, own, 2, keepdims=False)
                down_half = lax.dynamic_index_in_dim(down_sum, own, 1, keepdims=False)
                terms.append(
                    jnp.concatenate([up_half, down_half[:, 0], down_half[:, 1]], axis=2)
                )
            terms[1] = terms[1].astype(bf16)
        return [branch_low, gwo], mid_grad, terms[0], terms[1], sums

    def mixer_step(l, carried):
        low, keep, sent, sums = mixer_backward(l, layouts, smalls, kept[l][1], *carried, upo)
        by_row = lambda array: array.reshape(devices, shard, GROUP)
        return low, by_row(keep), by_row(sent), sums

    def input_step(l, low, mid_grad, ffn_sums, mixer_sums, two=None):
        return input_backward(
            l, layouts, kept[l][0], mods, low, mid_grad, ffn_sums, mixer_sums, qka, vgda, two
        )

    def run(keep, came, bits, below=1):
        for bit in bits[:-1]:
            keep, sent = step(keep, came, bit, below=below)
            came = [(partner(sent, bit), len(keep))]
        return step(keep, came, bits[-1], below=below)

    def grown(mod, bits):
        for bit in bits:
            mod = grow(mod, bit)
        return mod

    x_bits, y_bits, z_bits = along_x, along_y, along_z
    carried, mid_grad, f2_keep, f2_sent, f2_sums = ffn_step(1, output_grad)
    *carried, f2_sent, acts_sent = lock(*carried, f2_sent, acts_sent[0])
    f2_came = swap(f2_sent)
    acts_came = swap(acts_sent)
    low, a2_keep, a2_sent, m2_sums = mixer_step(1, carried)
    low, a2_sent, f2_came, acts_came = lock(low, a2_sent, f2_came, acts_came)
    a2_came = swap(a2_sent)
    gx_two, grad, mod_low_two, sums_two = input_step(1, low, mid_grad, f2_sums, m2_sums)
    mod_two = pack_misc(conds, mod_low_two)
    grad, mod_two, a2_came = lock(grad, mod_two, a2_came)
    f2_keep, f2_sent = run([f2_keep], [(f2_came, 1)], x_bits)
    a2_keep, a2_sent = run([a2_keep], [(a2_came, 1)], y_bits, 1 << len(x_bits))
    mod_two = grown(mod_two, x_bits[:-1])
    grad, f2_sent, a2_sent, mod_two = lock(grad, f2_sent, a2_sent, mod_two)
    f2_came = partner(f2_sent, x_bits[-1])
    mod_two = grown(mod_two, x_bits[-1:])
    a2_came = partner(a2_sent, y_bits[-1])

    carried, mid_grad, f1_keep, f1_sent, f1_sums = ffn_step(0, grad[None])
    *carried, f1_sent, f2_came, a2_came, mod_two = lock(
        *carried, f1_sent, f2_came, a2_came, mod_two
    )
    f1_came = swap(f1_sent)
    f2_keep, f2_sent = run(f2_keep, [(f2_came, 1)], y_bits)
    a2_keep, a2_sent = run(a2_keep, [(a2_came, 1)], x_bits)
    mod_two = grown(mod_two, y_bits[:-1])
    f1_keep, f1_sent = run([f1_keep], [(f1_came, 1)], x_bits)
    *carried, f2_sent, a2_sent, mod_two, f1_sent = lock(
        *carried, f2_sent, a2_sent, mod_two, f1_sent
    )
    f1_came = partner(f1_sent, x_bits[-1])
    a2_came = partner(a2_sent, x_bits[-1])
    f2_came = partner(f2_sent, y_bits[-1])
    mod_two = grown(mod_two, y_bits[-1:])
    low, a1_keep, a1_sent, m1_sums = mixer_step(0, carried)
    low, a1_sent, f2_came, a2_came, mod_two, f1_came = lock(
        low, a1_sent, f2_came, a2_came, mod_two, f1_came
    )
    two_keep, two_sent = run(f2_keep + a2_keep, [(f2_came, 1), (a2_came, 1)], z_bits[:1])
    f1_keep, f1_sent = run(f1_keep, [(f1_came, 1)], y_bits)
    low, a1_sent, two_sent, mod_two, f1_sent = lock(low, a1_sent, two_sent, mod_two, f1_sent)
    a1_came = swap(a1_sent)
    two_came = partner(two_sent, z_bits[0])
    mod_two = grown(mod_two, z_bits[:1])
    f1_came = partner(f1_sent, y_bits[-1])
    gx_one, _, mod_low_one, sums_one, gx_sent, mod_mine, mod_sent = input_step(
        0, low, mid_grad, f1_sums, m1_sums, (gx_two, mod_low_two)
    )
    misc = pack_misc(conds, mod_low_one, sums_one, sums_two)
    misc, a1_came, two_came, mod_two, f1_came, gx_sent, mod_sent = lock(
        misc, a1_came, two_came, mod_two, f1_came, gx_sent, mod_sent
    )

    keep, came = [a1_keep], [(a1_came, 1)]
    pair = None
    first_z = len(x_bits + y_bits)
    for place, bit in enumerate(x_bits + y_bits + z_bits):
        if place == first_z:
            keep, came = keep + f1_keep, came + [(f1_came, 1)]
        if pair is None:
            keep, sent = step(keep, came, bit)
        else:
            keep, sent, misc = step(keep, came, bit, pair)
        if place == 0:
            two_keep, two_sent = run(two_keep, [(two_came, 2)], z_bits[1:])
            mod_two = grown(mod_two, z_bits[1:-1])
            sent, misc, two_sent, mod_two = lock(sent, misc, two_sent, mod_two)
        else:
            sent, misc = lock(sent, misc)
        came = [(partner(sent, bit), len(keep))]
        pair = (misc, partner(misc, bit))
        if place == 0:
            two_came = partner(two_sent, z_bits[-1])
            mod_two = grown(mod_two, z_bits[-1:])
            gx_came = swap(gx_sent)
            mod_came = swap(mod_sent)
    lifted = mod_two.reshape(devices, 8, SLOTS, D)[:, 6]
    lifted = lax.dynamic_slice_in_dim(lifted, lax.axis_index("row") * shard, shard, 2)
    lifted = lifted.transpose(2, 1, 0).reshape(shard, SLOTS * devices)
    mine, other, small_mine, small_other = finish(
        keep + two_keep, came + [(two_came, 2)], lifted, mod_two, *pair
    )
    came, small_came = swap(other), swap(small_other)
    (
        g_query, g_key, g_value, g_gate, g_out, g_decay, g_up, g_down, g_ada,
        g_b_ada, g_b_up, g_b_down, g_conv, g_b_decay,
    ) = outputs(mine, came, small_mine, small_came)

    grad_lifted = lifted_grads(mod_mine, mod_came, qka[0], vgda[0])
    grad_lifted = (grad_lifted + swap(grad_lifted)).reshape(MICRO, SLOTS, D)
    _, pull_silu = jax.vjp(jax.nn.silu, conditions.astype(f32))
    (cond_grads,) = pull_silu(grad_lifted)

    return (
        both_micros(acts[0], acts[1], acts_came)[None],
        both_micros(gx_one, gx_two, gx_came)[None],
        cond_grads,
        g_ada[None],
        g_b_ada,
        g_query[None],
        g_key[None],
        g_value[None],
        g_gate[None],
        g_out[None],
        g_decay.transpose(1, 2, 0),
        g_b_decay,
        g_conv.transpose(1, 0, 2),
        g_up[None],
        g_b_up,
        g_down.reshape(1, FF // devices, D),
        g_b_down,
    )


def solution(mesh):
    rows = P(None, "row", None)
    mats = P("section", "row", None)
    vector = P("section", None)
    in_specs = (
        rows, rows, rows, P(None, "row"),
        mats, vector, mats, mats, mats, mats, mats, mats, vector, P("section", None, None),
        mats, vector, mats, vector,
    )
    blocks = P("section", None, "row", None)
    out_specs = (
        blocks, blocks, rows,
        mats, vector, mats, mats, mats, mats, mats, mats, vector, P("section", None, None),
        mats, vector, mats, vector,
    )
    return jax.shard_map(
        on_device, mesh=mesh, in_specs=in_specs, out_specs=out_specs, check_vma=False
    )
```

```python
import functools

import jax
import jax.numpy as jnp
from jax import lax
from jax.experimental import pallas as pl
from jax.experimental.pallas import tpu as pltpu
from jax.sharding import PartitionSpec as P

D = 384
HEADS = 6
HEAD_DIM = 64
FF = 1536
MICRO = 2
ROWS = 512
HALF = 256
SLOTS = 2
PAIR = 128
PAIRS = D // PAIR
QKVG = 4 * D
LANES = 128
GROUP = (QKVG + D + LANES) // 2
NEG = -1e30
SCALE = HEAD_DIM**-0.5

bf16 = jnp.bfloat16
f32 = jnp.float32


def mm(left, right):
    return jnp.dot(left, right, preferred_element_type=f32)


def mm_t(left, right):
    return lax.dot_general(left, right, (((1,), (1,)), ((), ())), preferred_element_type=f32)


def split(values):
    high = values.astype(bf16)
    return high, (values - high.astype(f32)).astype(bf16)


def split_three(values):
    high, rest = split(values)
    mid = values - high.astype(f32)
    middle, low = split(mid)
    return high, middle, low


def cat_left(values):
    high, low = split(values)
    return jnp.concatenate([high, low, high], axis=1)


def cat_right(values):
    high, low = split(values)
    return jnp.concatenate([high, high, low], axis=1)


def mm_near(left, right_pair, right_high):
    high, low = split(left)
    wide = mm(high, right_pair)
    return wide[:, :PAIR] + wide[:, PAIR:] + mm(low, right_high)


def lane_iota(rows, columns):
    return lax.broadcasted_iota(jnp.int32, (rows, columns), 1)


def row_iota(rows, columns):
    return lax.broadcasted_iota(jnp.int32, (rows, columns), 0)


def order_matrix(start, rows, wide, to_scan):
    t = row_iota(rows, ROWS) + start
    small = (t & 256) + ((t & 15) << 4) + ((t & 255) >> 4)
    if to_scan:
        large = ((t & 15) << 5) + (t >> 4)
    else:
        large = ((t & 31) << 4) + (t >> 5)
    source = jnp.where(wide, large, small)
    return jnp.where(lane_iota(rows, ROWS) == source, 1.0, 0.0).astype(bf16)


def normalise(values):
    centred = values - jnp.mean(values, axis=-1, keepdims=True)
    rate = lax.rsqrt(jnp.mean(centred * centred, axis=-1, keepdims=True) + 1e-06)
    return centred * rate, rate


def normalise_back(normal, rate, grad):
    return rate * (
        grad
        - jnp.mean(grad, axis=-1, keepdims=True)
        - normal * jnp.mean(grad * normal, axis=-1, keepdims=True)
    )


class In:
    def __init__(self, copy, kept):
        self.copy = copy
        self.kept = kept

    def __call__(self):
        if self.copy is not None:
            self.copy.wait()
            self.copy = None
        return self.kept


class Kernel:
    def __init__(self, layer, layouts):
        self.layer = layer
        self.section = lax.axis_index("section")
        self.own = self.section == layer
        self.layout = layouts[self.section, 0]
        self.wide = self.layout == 0
        self.live_rows = jnp.where(self.wide, ROWS, self.layout * HALF)
        self.pushed = {}

    def load(self, kind, refs, kept, sem):
        if kind == "own":
            mine, other = refs

            @pl.when(self.own)
            def _():
                pltpu.make_async_copy(mine, kept, sem).start()

            @pl.when(jnp.logical_not(self.own))
            def _():
                pltpu.make_async_copy(other, kept, sem).start()

            return In(pltpu.make_async_copy(mine, kept, sem), kept)
        (source,) = refs
        if kind == "micro":
            source = source.at[self.section if source.shape[0] == MICRO else 0]
        copy = pltpu.make_async_copy(source, kept, sem)
        copy.start()
        return In(copy, kept)

    def push(self, name):
        kept, target, sem = self.results[name]
        copy = pltpu.make_async_copy(kept, target, sem)
        copy.start()
        self.pushed[name] = copy

    def finish(self):
        for name in self.results:
            if name not in self.pushed:
                self.push(name)
        for copy in self.pushed.values():
            copy.wait()

    def slot(self, half):
        return jnp.where(self.wide, 0, half)

    def share(self, slot, part):
        row = pl.ds(2 * self.section + slot, 1)
        return self.mods()[row, part * D : (part + 1) * D]

    def bu(self):
        return self.small()[0:1, :]

    def bn(self):
        return self.small()[1:2, :D]

    def ck(self, tap):
        return self.small()[2 + tap : 3 + tap, :D]

    def bd(self):
        return self.small()[5:6, :LANES]


def sigmoid(values):
    return 1.0 / (1.0 + jnp.exp(-values))


GELU_A = 0.7978845608028654
GELU_B = 0.044715


def gelu_parts(values):
    square = values * values
    tanh = jnp.tanh(GELU_A * values * (1.0 + GELU_B * square))
    return square, tanh


def fill_bias(bias, wide):
    bias[:, :HALF] = jnp.full((HALF, HALF), 0.0, f32) + jnp.where(wide, 0.0, NEG)
    causal = row_iota(HALF, HALF) >= lane_iota(HALF, HALF)
    bias[:, HALF:] = jnp.where(causal, 0.0, NEG)


def decay_factors(cum, cumt, bias, head):
    row = cumt[pl.ds(head, 1), :]
    lanes = lane_iota(1, LANES)
    column = jnp.sum(jnp.where(lanes == head, cum[...], 0.0), axis=1, keepdims=True)
    first = jnp.exp(column[:HALF] - row[:, :HALF] + bias[:, HALF:])
    second = jnp.exp(column[HALF:] - row + bias[...])
    return first, second


def head_norm(values, lanes):
    square = values * values
    low = jnp.sum(jnp.where(lanes < HEAD_DIM, square, 0.0), axis=1, keepdims=True)
    high = jnp.sum(jnp.where(lanes < HEAD_DIM, 0.0, square), axis=1, keepdims=True)
    return jnp.where(lanes < HEAD_DIM, low, high) * (1.0 / HEAD_DIM)


def fill_decay(dp, bd, cum, cumt):
    raw = dp[...] + bd
    log_decay = (jnp.minimum(raw, 0.0) - jnp.log1p(jnp.exp(-jnp.abs(raw)))) * (1.0 / 16.0)
    high, middle, low = split_three(log_decay)
    causal = jnp.where(row_iota(ROWS, ROWS) >= lane_iota(ROWS, ROWS), 1.0, 0.0).astype(bf16)
    cum[...] = mm(causal, high) + mm(causal, middle) + mm(causal, low)
    cumt[...] = jnp.transpose(cum[...])


def columns(index, first=0):
    return slice(index * PAIR + first, index * PAIR + first + PAIR)


def attn_forward_body(k):
    flip = k.layer == 1
    wide = k.wide
    x = k.x()
    k.mods()

    def first(i, carry):
        rows = pl.ds(pl.multiple_of(i * HALF, HALF), HALF)
        slot = k.slot(i)
        normal, _ = normalise(x[rows, :].astype(f32))
        k.inner[rows, :] = (normal * (1.0 + k.share(slot, 1)) + k.share(slot, 0)).astype(bf16)
        return carry

    lax.fori_loop(0, 2, first, 0)
    w_qk = k.w_qk()
    w_vgd = k.w_vgd()

    def project(i, carry):
        start = i * HALF
        rows = pl.ds(start, HALF)
        if flip:
            part = mm(order_matrix(start, HALF, wide, True), k.inner[...]).astype(bf16)
        else:
            part = k.inner[rows, :]
        k.ordered[rows, :] = part
        k.qkvg[rows, : 2 * D] = mm(part, w_qk[...])
        k.qkvg[rows, 2 * D :] = mm(part, w_vgd[:, : 2 * D])
        k.dp[rows, :] = mm(part, w_vgd[:, 2 * D :])
        return carry

    lax.fori_loop(0, 2, project, 0)
    k.small()
    for name in ("ordered", "qkvg", "dp"):
        k.push(name)
    fill_decay(k.dp, k.bd(), k.cum, k.cumt)
    fill_bias(k.bias, wide)

    vpad = k.vpad
    vpad[0:8, :] = jnp.zeros((8, D), f32)
    vpad[8 : 8 + ROWS, :] = k.qkvg[:, 2 * D : 3 * D]
    position = row_iota(ROWS, 1) & jnp.where(wide, ROWS - 1, HALF - 1)
    one = jnp.where(position >= 1, vpad[7 : 7 + ROWS, :], 0.0)
    two = jnp.where(position >= 2, vpad[6 : 6 + ROWS, :], 0.0)
    k.vc[...] = k.ck(0) * vpad[8 : 8 + ROWS, :] + k.ck(1) * one + k.ck(2) * two
    for name in ("cum", "cumt", "vc"):
        k.push(name)

    def pair(p, carry):
        lanes = lane_iota(1, PAIR)
        queries = cat_left(k.qkvg[:, columns(p)] * SCALE)
        keys = k.qkvg[:, columns(p, D)]
        value_high, value_low = split(k.vc[:, columns(p)])
        values = jnp.concatenate([value_high, value_low], axis=1)
        parts = []
        for e in range(2):
            key_cat = cat_right(jnp.where((lanes // HEAD_DIM) == e, keys, 0.0))
            first, second = decay_factors(k.cum, k.cumt, k.bias, 2 * p + e)
            first = first * mm_t(queries[:HALF], key_cat[:HALF])
            second = second * mm_t(queries[HALF:], key_cat)
            parts.append(
                jnp.concatenate(
                    [
                        mm_near(first, values[:HALF], value_high[:HALF]),
                        mm_near(second, values, value_high),
                    ],
                    axis=0,
                )
            )
        total = jnp.where(lanes < HEAD_DIM, parts[0], parts[1])
        k.o[:, columns(p)] = total
        gate = k.qkvg[:, columns(p, 3 * D)]
        normed = total * lax.rsqrt(head_norm(total, lanes) + 1.0)
        mixed = (normed * (gate * sigmoid(gate))).astype(bf16)
        if flip:
            k.inner[:, columns(p)] = mixed
        else:
            k.gated[:, columns(p)] = mixed
        return carry

    for p in range(PAIRS):
        pair(p, 0)
    k.push("o")
    if flip:

        def back(i, carry):
            start = i * HALF
            k.gated[pl.ds(start, HALF), :] = mm(
                order_matrix(start, HALF, wide, False), k.inner[...]
            ).astype(bf16)
            return carry

        lax.fori_loop(0, 2, back, 0)


def ffn_forward_body(k):
    gated, x = k.gated(), k.x()
    k.mods(), k.small()

    def tile(i, carry):
        start = i * HALF
        rows = pl.ds(start, HALF)
        slot = k.slot(i)
        grown = mm(gated[rows, :], k.wo()[...])
        k.branch[rows, :] = grown
        middle = x[rows, :].astype(f32) + k.share(slot, 2) * grown
        normal, _ = normalise(middle)
        inner = (normal * (1.0 + k.share(slot, 4)) + k.share(slot, 3)).astype(bf16)
        up = mm(inner, k.wu()[...]) + k.bu()
        _, tanh = gelu_parts(up)
        hidden = (0.5 * up * (1.0 + tanh)).astype(bf16)
        low = mm(hidden, k.wn()[...])
        k.down[rows, :] = low
        result = middle + k.share(slot, 5) * (low + k.bn())
        live = (row_iota(HALF, 1) + start) < k.live_rows
        k.out[rows, :] = jnp.where(live, result, 0.0).astype(bf16)
        return carry

    for i in range(2):
        tile(i, 0)
    if k.layer == 1:
        k.sent[...] = jnp.where(k.section == 0, k.out[...].astype(f32), x[...].astype(f32)).astype(bf16)


def ffn_backward_body(k):
    gmod, gbu, gbn = k.gmod, k.gbu, k.gbn
    gmod[...] = jnp.zeros(gmod.shape, f32)
    gbu[...] = jnp.zeros(gbu.shape, f32)
    gbn[...] = jnp.zeros(gbn.shape, f32)
    k.mods(), k.small()
    x, grad, branch, down = k.x(), k.grad(), k.branch(), k.down()

    def tile(i, carry):
        start = i * HALF
        rows = pl.ds(start, HALF)
        slot = k.slot(i)

        def add(part, values):
            where = (pl.ds(slot, 1), slice((part - 2) * D, (part - 1) * D))
            gmod[where] = gmod[where] + jnp.sum(values, axis=0, keepdims=True)

        grown = branch[rows, :]
        middle = x[rows, :].astype(f32) + k.share(slot, 2) * grown
        normal, rate = normalise(middle)
        inner = (normal * (1.0 + k.share(slot, 4)) + k.share(slot, 3)).astype(bf16)
        k.inner_s[rows, :] = inner
        live = (row_iota(HALF, 1) + start) < k.live_rows
        above = jnp.where(live, grad[rows, :].astype(f32), 0.0)
        add(5, above * (down[rows, :] + k.bn()))
        grad_down = above * k.share(slot, 5)
        gbn[...] = gbn[...] + jnp.sum(grad_down, axis=0, keepdims=True)
        down_low = grad_down.astype(bf16)
        k.down_s[rows, :] = down_low
        up = mm(inner, k.wu()[...]) + k.bu()
        square, tanh = gelu_parts(up)
        half = 0.5 * (1.0 + tanh)
        k.hidden_s[rows, :] = (up * half).astype(bf16)
        slope = half + 0.5 * up * (1.0 - tanh * tanh) * (
            GELU_A * (1.0 + 3.0 * GELU_B * square)
        )
        grad_up = mm_t(down_low, k.wn()[...]) * slope
        gbu[...] = gbu[...] + jnp.sum(grad_up, axis=0, keepdims=True)
        up_low = grad_up.astype(bf16)
        k.up_s[rows, :] = up_low
        grad_inner = mm_t(up_low, k.wu()[...])
        add(3, grad_inner)
        add(4, grad_inner * normal)
        grad_middle = above + normalise_back(
            normal, rate, grad_inner * (1.0 + k.share(slot, 4))
        )
        k.mid_grad[rows, :] = grad_middle
        add(2, grad_middle * grown)
        k.branch_low[rows, :] = (grad_middle * k.share(slot, 2)).astype(bf16)
        return carry

    for i in range(2):
        tile(i, 0)
    k.push("mid_grad")
    k.push("branch_low")

    def weights(j, carry):
        part = pl.ds(pl.multiple_of(j * HALF, HALF), HALF)
        hidden_t = jnp.transpose(k.hidden_s[:, part].astype(f32)).astype(bf16)
        k.gwn[part, :] = mm(hidden_t, k.down_s[...])
        return carry

    lax.fori_loop(0, FF // HALF, weights, 0)
    inner_t = jnp.transpose(k.inner_s[...].astype(f32)).astype(bf16)
    if k.packed:
        devices, shard, _ = k.keep.shape

        def halves(j, carry):
            for kept, own in ((k.keep, c_section), (k.sent, 1 - c_section)):
                columns = pl.ds(pl.multiple_of(j * HALF + own * (FF // 2), HALF), HALF)
                here = pl.ds(pl.multiple_of(j * HALF, HALF), HALF)
                part = mm(inner_t, k.up_s[:, columns]).reshape(devices, shard, HALF)
                kept[:, :, here] = part.astype(kept.dtype)
            return carry

        c_section = k.section
        lax.fori_loop(0, FF // 2 // HALF, halves, 0)

        def owner(r, carry):
            for kept, own in ((k.keep, c_section), (k.sent, 1 - c_section)):
                for piece in range(2):
                    start = pl.multiple_of((4 * r + 2 * own + piece) * shard, 8)
                    rows = k.gwn[pl.ds(start, shard), :]
                    at = FF // 2 + piece * D
                    kept[r, :, at : at + D] = rows.astype(kept.dtype)
            return carry

        lax.fori_loop(0, devices, owner, 0)
        k.push("keep")
        k.push("sent")
    else:
        k.gwu[...] = mm(inner_t, k.up_s[...])
    gated = k.gated()
    k.gwo[...] = mm(jnp.transpose(gated[...].astype(f32)).astype(bf16), k.branch_low[...])

    short = jnp.concatenate([gbn[...], jnp.zeros((1, FF - D), f32)], axis=1)
    k.sums[...] = jnp.concatenate(
        [gmod[0:SLOTS, :], gbu[...], short, jnp.zeros((4, FF), f32)], axis=0
    )


def mixer_backward_body(k):
    flip = k.layer == 1
    wide = k.wide
    mixed_s, low, dv_s, rows_s, cols_s = k.mixed_s, k.low, k.dv_s, k.rows_s, k.cols_s
    fill_bias(k.bias, wide)
    branch_low, wo = k.branch_low(), k.wo()

    def first(i, carry):
        start = i * HALF
        rows = pl.ds(start, HALF)
        if flip:
            part = mm(order_matrix(start, HALF, wide, True), branch_low[...]).astype(bf16)
        else:
            part = branch_low[rows, :]
        mixed_s[rows, :] = mm_t(part, wo[...])
        return carry

    lax.fori_loop(0, 2, first, 0)
    rows_s[...] = jnp.zeros(rows_s.shape, f32)
    cols_s[...] = jnp.zeros(cols_s.shape, f32)
    qkvg, vc, cum, cumt, o = k.qkvg(), k.vc(), k.cum(), k.cumt(), k.o()
    k.small()

    def pair(p, carry):
        lanes = lane_iota(1, PAIR)
        total = o[:, columns(p)]
        gate = qkvg[:, columns(p, 3 * D)]
        above = mixed_s[:, columns(p)]
        rate = lax.rsqrt(head_norm(total, lanes) + 1.0)
        sig = sigmoid(gate)
        grad_gate = above * (total * rate) * (sig * (1.0 + gate * (1.0 - sig)))
        low[:, columns(p, 3 * D)] = grad_gate.astype(bf16)
        grad_normed = above * (gate * sig)
        product = grad_normed * total
        inside = jnp.where(
            lanes < HEAD_DIM,
            jnp.sum(jnp.where(lanes < HEAD_DIM, product, 0.0), axis=1, keepdims=True),
            jnp.sum(jnp.where(lanes < HEAD_DIM, 0.0, product), axis=1, keepdims=True),
        ) * (1.0 / HEAD_DIM)
        grad_o = rate * grad_normed - total * (rate * rate * rate) * inside

        queries = qkvg[:, columns(p)] * SCALE
        keys = qkvg[:, columns(p, D)]
        values = vc[:, columns(p)]
        query_cat = cat_left(queries)
        grad_cat = cat_left(grad_o)
        key_high, key_low = split(keys)
        key_pair = jnp.concatenate([key_high, key_low], axis=1)
        query_t = jnp.transpose(queries)
        grad_t = jnp.transpose(grad_o)
        grad_q = []
        grad_k = []
        grad_v = []
        for e in range(2):
            mine = (lanes // HEAD_DIM) == e
            head = 2 * p + e
            key_cat = cat_right(jnp.where(mine, keys, 0.0))
            value_cat = cat_right(jnp.where(mine, values, 0.0))
            first, second = decay_factors(cum, cumt, k.bias, head)
            raw_first = mm_t(query_cat[:HALF], key_cat[:HALF])
            raw_second = mm_t(query_cat[HALF:], key_cat)
            grad_first = first * mm_t(grad_cat[:HALF], value_cat[:HALF])
            grad_second = second * mm_t(grad_cat[HALF:], value_cat)
            score_first = raw_first * first
            score_second = raw_second * second
            pull_first = grad_first * raw_first
            pull_second = grad_second * raw_second
            here = lanes == head
            rows_s[:HALF, :] = rows_s[:HALF, :] + jnp.where(
                here, jnp.sum(pull_first, axis=1, keepdims=True), 0.0
            )
            rows_s[HALF:, :] = rows_s[HALF:, :] + jnp.where(
                here, jnp.sum(pull_second, axis=1, keepdims=True), 0.0
            )
            low_cols = jnp.sum(pull_second, axis=0, keepdims=True)
            cols_s[pl.ds(head, 1), :HALF] = low_cols[:, :HALF] + jnp.sum(
                pull_first, axis=0, keepdims=True
            )
            cols_s[pl.ds(head, 1), HALF:] = low_cols[:, HALF:]
            grad_q.append(
                jnp.concatenate(
                    [
                        mm_near(grad_first, key_pair[:HALF], key_high[:HALF]),
                        mm_near(grad_second, key_pair, key_high),
                    ],
                    axis=0,
                )
            )

            def turned(source_t, block_first, block_second):
                high, low = split(source_t[e * HEAD_DIM : (e + 1) * HEAD_DIM, :])
                both = jnp.concatenate([high, low], axis=0)
                first_high, first_low = split(block_first)
                second_high, second_low = split(block_second)
                one = mm(both[:, :HALF], first_high)
                one = one[:HEAD_DIM] + one[HEAD_DIM:] + mm(high[:, :HALF], first_low)
                two = mm(both[:, HALF:], second_high)
                two = two[:HEAD_DIM] + two[HEAD_DIM:] + mm(high[:, HALF:], second_low)
                return jnp.concatenate([two[:, :HALF] + one, two[:, HALF:]], axis=1)

            grad_k.append(turned(query_t, grad_first, grad_second))
            grad_v.append(turned(grad_t, score_first, score_second))
        query_grad = jnp.where(lanes < HEAD_DIM, grad_q[0], grad_q[1]) * SCALE
        low[:, columns(p)] = query_grad.astype(bf16)
        low[:, columns(p, D)] = jnp.transpose(jnp.concatenate(grad_k, axis=0)).astype(bf16)
        dv_s[:ROWS, columns(p)] = jnp.transpose(jnp.concatenate(grad_v, axis=0))
        return carry

    for p in range(PAIRS):
        pair(p, 0)

    pulled = rows_s[...] - jnp.transpose(cols_s[...])
    high, middle, rest = split_three(pulled)
    upper_first = jnp.concatenate(
        [
            jnp.where(row_iota(HALF, HALF) <= lane_iota(HALF, HALF), 1.0, 0.0),
            jnp.full((HALF, HALF), 0.0, f32) + jnp.where(wide, 1.0, 0.0),
        ],
        axis=1,
    ).astype(bf16)
    upper_second = upper_first[:, :HALF]
    later = jnp.concatenate(
        [
            mm(upper_first, high) + mm(upper_first, middle) + mm(upper_first, rest),
            mm(upper_second, high[HALF:]) + mm(upper_second, middle[HALF:])
            + mm(upper_second, rest[HALF:]),
        ],
        axis=0,
    )
    grad_dp = later * (1.0 / 16.0) * sigmoid(-(k.dp()[...] + k.bd()))
    grad_bd = jnp.sum(grad_dp, axis=0, keepdims=True)
    low[:, QKVG:] = grad_dp.astype(bf16)

    dv_s[ROWS:, :] = jnp.zeros((8, D), f32)
    position = row_iota(ROWS, 1) & jnp.where(wide, ROWS - 1, HALF - 1)
    last = jnp.where(wide, ROWS - 1, HALF - 1)
    here = dv_s[0:ROWS, :]
    one = jnp.where(position <= last - 1, dv_s[1 : 1 + ROWS, :], 0.0)
    two = jnp.where(position <= last - 2, dv_s[2 : 2 + ROWS, :], 0.0)
    value = qkvg[:, 2 * D : 3 * D]
    low[:, 2 * D : 3 * D] = (k.ck(0) * here + k.ck(1) * one + k.ck(2) * two).astype(bf16)
    k.push("low")

    taps = [jnp.sum(rows * value, axis=0, keepdims=True) for rows in (here, one, two)]
    rest = jnp.concatenate([grad_bd, jnp.zeros((1, D - LANES), f32)], axis=1)
    k.sums[...] = jnp.concatenate([*taps, rest, jnp.zeros((4, D), f32)], axis=0)

    ordered_t = jnp.transpose(k.ordered()[...].astype(f32)).astype(bf16)
    gwo = k.gwo()
    gw = k.gw

    def weights(j, carry):
        part = pl.ds(pl.multiple_of(j * HALF, HALF), HALF)
        gw[:, part] = mm(ordered_t, low[:, part])
        return carry

    lax.fori_loop(0, QKVG // HALF, weights, 0)
    gw[:, QKVG : QKVG + D] = gwo[...]
    gw[:, QKVG + D :] = mm(ordered_t, low[:, QKVG:])

    def halves(j, carry):
        here = pl.ds(pl.multiple_of(j * HALF, HALF), HALF)
        keep = pl.ds(pl.multiple_of(j * HALF + k.section * GROUP, HALF), HALF)
        send = pl.ds(pl.multiple_of(j * HALF + (1 - k.section) * GROUP, HALF), HALF)
        k.gw_keep[:, here] = gw[:, keep]
        k.gw_send[:, here] = gw[:, send].astype(bf16)
        return carry

    lax.fori_loop(0, GROUP // HALF, halves, 0)


def input_backward_body(k):
    flip = k.layer == 1
    wide = k.wide
    gmod, mixed_s, perm_s = k.gmod, k.mixed_s, k.perm_s
    gmod[...] = jnp.zeros(gmod.shape, f32)
    low, w_qk, w_vgd = k.low(), k.w_qk(), k.w_vgd()

    def inner_grad(i, carry):
        rows = pl.ds(pl.multiple_of(i * HALF, HALF), HALF)
        mixed_s[rows, :] = mm_t(low[rows, : 2 * D], w_qk[...]) + mm_t(
            low[rows, 2 * D :], w_vgd[...]
        )
        return carry

    lax.fori_loop(0, 2, inner_grad, 0)
    if flip:
        high, middle, rest = split_three(mixed_s[...])
        perm_s[:, :D] = high
        perm_s[:, D : 2 * D] = middle
        perm_s[:, 2 * D :] = rest
    x, mid_grad = k.x(), k.mid_grad()
    k.mods()

    def tile(i, carry):
        start = i * HALF
        rows = pl.ds(start, HALF)
        slot = k.slot(i)
        if flip:
            three = mm(order_matrix(start, HALF, wide, False), perm_s[...])
            grad = three[:, :D] + three[:, D : 2 * D] + three[:, 2 * D :]
        else:
            grad = mixed_s[rows, :]
        normal, rate = normalise(x[rows, :].astype(f32))
        where = (pl.ds(slot, 1), slice(0, D))
        gmod[where] = gmod[where] + jnp.sum(grad, axis=0, keepdims=True)
        where = (pl.ds(slot, 1), slice(D, 2 * D))
        gmod[where] = gmod[where] + jnp.sum(grad * normal, axis=0, keepdims=True)
        total = mid_grad[rows, :] + normalise_back(normal, rate, grad * (1.0 + k.share(slot, 1)))
        k.gx[rows, :] = total
        k.gx_low[rows, :] = total.astype(bf16)
        return carry

    for i in range(2):
        tile(i, 0)
    k.push("gx_low")
    k.push("gx")
    ffn, mixer = k.ffn_sums(), k.mixer_sums()
    k.mod_low[...] = jnp.concatenate([gmod[...], ffn[...]], axis=1).astype(bf16)
    if k.layer == 0:
        first = k.section == 0
        k.gx_send[...] = jnp.where(first, k.gx_two()[...], k.gx[...])
        one, two = k.mod_low[...].astype(f32), k.mod_two()[...].astype(f32)
        k.mod_mine[...] = jnp.where(first, one, two).astype(bf16)
        k.mod_send[...] = jnp.where(first, two, one).astype(bf16)
    half = 2 * D
    rest = ffn[0:1, :] + ffn[1:2, :]
    k.sums[...] = jnp.concatenate(
        [
            gmod[0:1, :] + gmod[1:2, :],
            rest[:, :half],
            rest[:, half:],
            ffn[2:3, :half],
            ffn[2:3, half:],
            jnp.concatenate([ffn[3:4, :D], mixer[0:1, :]], axis=1),
            jnp.concatenate([mixer[1:2, :], mixer[2:3, :]], axis=1),
            jnp.concatenate([mixer[3:4, :], jnp.zeros((1, D), f32)], axis=1),
        ],
        axis=0,
    )


ANY = pl.BlockSpec(memory_space=pl.ANY)
VMEM = pl.BlockSpec(memory_space=pltpu.VMEM)
HBM = pl.BlockSpec(memory_space=pltpu.HBM)


def call(body, layer, layouts, ins, outs, scratch, flops, packed=None):
    arrays = []
    counts = []
    kept = []
    places = []
    for kind, given, part in ins.values():
        places.extend([ANY] * 2 if kind == "own" else [HBM])
        given = given if kind == "own" else (given,)
        arrays.extend(given)
        counts.append(len(given))
        rows, wide = given[0].shape[-2:]
        start, stop = part or (0, wide)
        kept.append(pltpu.VMEM((rows, stop - start), given[0].dtype))

    def kernel(*refs):
        refs = list(refs)
        take = lambda count: [refs.pop(0) for _ in range(count)]
        (layouts_ref,) = take(1)
        sources = [take(count) for count in counts]
        targets = take(len(outs))
        buffers = take(len(ins))
        results = take(len(outs))
        rest = take(len(scratch))
        in_sems, out_sems = refs
        k = Kernel(layer, layouts_ref)
        k.packed = packed
        for number, (name, (kind, _, part)) in enumerate(ins.items()):
            given = sources[number]
            if part is not None:
                given = [ref.at[:, part[0] : part[1]] for ref in given]
            setattr(k, name, k.load(kind, given, buffers[number], in_sems.at[number]))
        k.results = {}
        for number, name in enumerate(outs):
            setattr(k, name, results[number])
            k.results[name] = (results[number], targets[number], out_sems.at[number])
        for name, ref in zip(scratch, rest):
            setattr(k, name, ref)
        body(k)
        k.finish()

    return pl.pallas_call(
        kernel,
        out_shape=[jax.ShapeDtypeStruct(shape, kind) for shape, kind, _ in outs.values()],
        in_specs=[pl.BlockSpec(memory_space=pltpu.SMEM)] + places,
        out_specs=[HBM if for_kernel else ANY for _, _, for_kernel in outs.values()],
        scratch_shapes=kept
        + [pltpu.VMEM(shape, kind) for shape, kind, _ in outs.values()]
        + [pltpu.VMEM(shape, kind) for shape, kind in scratch.values()]
        + [pltpu.SemaphoreType.DMA((len(ins),)), pltpu.SemaphoreType.DMA((len(outs),))],
        compiler_params=pltpu.CompilerParams(vmem_limit_bytes=28 * 1024 * 1024),
        cost_estimate=pl.CostEstimate(flops=flops, bytes_accessed=4 << 20, transcendentals=0),
    )(layouts, *arrays)


def own(pair, part=None):
    return ("own", pair, part)


def plain(array):
    return ("plain", array, None)


def micro(array):
    return ("micro", array, None)


ADA_CUT = 9 * LANES
AT_QK = (0, 2 * D)
AT_ADA_A = (2 * D, 2 * D + ADA_CUT)
AT_VGD = (0, 2 * D + LANES)
AT_ADA_B = (2 * D + LANES, 8 * D + LANES - ADA_CUT)
AT_UP = (0, FF)
AT_OUT = (FF, FF + D)


def attn_forward(layer, layouts, x, mods, small, qka, vgda):
    return call(
        attn_forward_body,
        layer,
        layouts,
        dict(
            x=micro(x),
            mods=own(mods),
            w_qk=own(qka, AT_QK),
            w_vgd=own(vgda, AT_VGD),
            small=own(small),
        ),
        dict(
            ordered=((ROWS, D), bf16, True),
            qkvg=((ROWS, QKVG), f32, True),
            dp=((ROWS, LANES), f32, True),
            vc=((ROWS, D), f32, True),
            cum=((ROWS, LANES), f32, True),
            cumt=((LANES, ROWS), f32, True),
            o=((ROWS, D), f32, True),
            gated=((ROWS, D), bf16, True),
        ),
        dict(
            inner=((ROWS, D), bf16),
            vpad=((ROWS + 8, D), f32),
            bias=((HALF, ROWS), f32),
        ),
        8 * 10**9,
    )


def ffn_forward(layer, layouts, x, mods, small, gated, upo, down):
    return call(
        ffn_forward_body,
        layer,
        layouts,
        dict(
            gated=plain(gated),
            x=micro(x),
            wo=own(upo, AT_OUT),
            mods=own(mods),
            small=own(small),
            wu=own(upo, AT_UP),
            wn=own(down),
        ),
        dict(
            out=((ROWS, D), bf16, True),
            branch=((ROWS, D), f32, True),
            down=((ROWS, D), f32, True),
            **({"sent": ((ROWS, D), bf16, False)} if layer == 1 else {}),
        ),
        {},
        5 * 10**9,
    )


def ffn_backward(
    layer, layouts, x, mods, small, gated, branch, down_raw, grad, upo, down, devices
):
    shard = D // devices
    in_kernel = shard % 8 == 0
    if in_kernel:
        sums = dict(
            keep=((devices, shard, FF), f32, True),
            sent=((devices, shard, FF), bf16, False),
        )
    else:
        sums = dict(gwu=((D, FF), f32, False), gwn=((FF, D), f32, False))
    return call(
        ffn_backward_body,
        layer,
        layouts,
        dict(
            mods=own(mods),
            small=own(small),
            x=micro(x),
            grad=micro(grad),
            branch=plain(branch),
            down=plain(down_raw),
            wu=own(upo, AT_UP),
            wn=own(down),
            gated=plain(gated),
        ),
        dict(
            mid_grad=((ROWS, D), f32, True),
            branch_low=((ROWS, D), bf16, True),
            gwo=((D, D), f32, True),
            sums=((8, FF), f32, True),
            **sums,
        ),
        dict(
            **({"gwn": ((FF, D), f32)} if in_kernel else {}),
            hidden_s=((ROWS, FF), bf16),
            inner_s=((ROWS, D), bf16),
            up_s=((ROWS, FF), bf16),
            down_s=((ROWS, D), bf16),
            gmod=((8, FF), f32),
            gbu=((1, FF), f32),
            gbn=((1, D), f32),
        ),
        12 * 10**9,
        packed=in_kernel,
    )


def mixer_backward(layer, layouts, small, saved, branch_low, gwo, upo):
    ordered, qkvg, dp, vc, cum, cumt, o = saved
    return call(
        mixer_backward_body,
        layer,
        layouts,
        dict(
            branch_low=plain(branch_low),
            wo=own(upo, AT_OUT),
            qkvg=plain(qkvg),
            vc=plain(vc),
            cum=plain(cum),
            cumt=plain(cumt),
            o=plain(o),
            small=own(small),
            dp=plain(dp),
            ordered=plain(ordered),
            gwo=plain(gwo),
        ),
        dict(
            low=((ROWS, QKVG + LANES), bf16, True),
            gw_keep=((D, GROUP), f32, True),
            gw_send=((D, GROUP), bf16, False),
            sums=((8, D), f32, True),
        ),
        dict(
            mixed_s=((ROWS, D), f32),
            dv_s=((ROWS + 8, D), f32),
            rows_s=((ROWS, LANES), f32),
            cols_s=((LANES, ROWS), f32),
            bias=((HALF, ROWS), f32),
            gw=((D, 2 * GROUP), f32),
        ),
        15 * 10**9,
    )


def input_backward(
    layer, layouts, x, mods, low, mid_grad, ffn_sums, mixer_sums, qka, vgda, two=None
):
    extra_in, extra_out = {}, {}
    if two is not None:
        extra_in = dict(gx_two=plain(two[0]), mod_two=plain(two[1]))
        extra_out = dict(
            gx_send=((ROWS, D), f32, False),
            mod_mine=((8, 6 * D), bf16, False),
            mod_send=((8, 6 * D), bf16, False),
        )
    return call(
        input_backward_body,
        layer,
        layouts,
        dict(
            low=plain(low),
            w_qk=own(qka, AT_QK),
            w_vgd=own(vgda, AT_VGD),
            x=micro(x),
            mid_grad=plain(mid_grad),
            mods=own(mods),
            ffn_sums=plain(ffn_sums),
            mixer_sums=plain(mixer_sums),
            **extra_in,
        ),
        dict(
            gx=((ROWS, D), f32, True),
            gx_low=((ROWS, D), bf16, True),
            mod_low=((8, 6 * D), bf16, True),
            sums=((8, 2 * D), f32, False),
            **extra_out,
        ),
        dict(
            mixed_s=((ROWS, D), f32),
            perm_s=((ROWS, 3 * D), bf16),
            gmod=((8, 2 * D), f32),
        ),
        4 * 10**9,
    )


def small_kernel(b_up, b_down, taps, b_decay, packed):
    packed[...] = jnp.zeros(packed.shape, f32)
    packed[0:1, :] = b_up[...]
    packed[1:2, :D] = b_down[...]
    packed[2:5, :D] = taps[0]
    packed[5:6, :HEADS] = b_decay[...]


def pack_small(b_up, b_down, taps, b_decay):
    return pl.pallas_call(
        small_kernel,
        out_shape=jax.ShapeDtypeStruct((8, FF), f32),
        in_specs=[VMEM] * 4,
        out_specs=VMEM,
    )(b_up, b_down, taps, b_decay)


def pack_kernel(w_query, w_key, w_value, w_gate, w_out, w_decay, w_ada, w_up, qka, vgda, upo):
    qka[:, :D] = w_query[0]
    qka[:, D : 2 * D] = w_key[0]
    qka[:, 2 * D :] = w_ada[0, :, :ADA_CUT]
    vgda[:, :D] = w_value[0]
    vgda[:, D : 2 * D] = w_gate[0]
    place = jnp.where(row_iota(HEADS, LANES) == lane_iota(HEADS, LANES), 1.0, 0.0).astype(bf16)
    turned = lax.dot_general(
        w_decay[0], place, (((0,), (0,)), ((), ())), preferred_element_type=f32
    )
    vgda[:, 2 * D : 2 * D + LANES] = turned.astype(bf16)
    vgda[:, 2 * D + LANES :] = w_ada[0, :, ADA_CUT:]
    upo[:, :FF] = w_up[0]
    upo[:, FF:] = w_out[0]


def pack(*weights):
    shard = weights[0].shape[1]
    widths = (2 * D + ADA_CUT, 8 * D + LANES - ADA_CUT, FF + D)
    return pl.pallas_call(
        pack_kernel,
        out_shape=[jax.ShapeDtypeStruct((shard, width), bf16) for width in widths],
        in_specs=[VMEM] * len(weights),
        out_specs=[VMEM] * len(widths),
    )(*weights)


def join_kernel(bits, *refs):
    count = len(bits)
    held, came, out = refs[:count], refs[count : 2 * count], refs[2 * count :]
    for i, bit in enumerate(bits):
        mine = (lax.axis_index("row") >> bit) & 1
        out[i][:, mine] = held[i][...]
        out[i][:, 1 - mine] = came[i][...]


def join(held, came, bits):
    def parts(array, bit):
        axis = axis_of(bit)
        above = 1
        for size in array.shape[:axis]:
            above *= size
        return array.reshape((above, -1) + array.shape[-2:])

    split_held = [parts(array, bit) for array, bit in zip(held, bits)]
    split_came = [parts(array, bit) for array, bit in zip(came, bits)]
    out = pl.pallas_call(
        functools.partial(join_kernel, bits),
        out_shape=[
            jax.ShapeDtypeStruct(array.shape[:1] + (2,) + array.shape[1:], array.dtype)
            for array in split_held
        ],
        in_specs=[VMEM] * (2 * len(held)),
        out_specs=[VMEM] * len(held),
        compiler_params=pltpu.CompilerParams(vmem_limit_bytes=8 * 1024 * 1024),
        cost_estimate=pl.CostEstimate(flops=10**6, bytes_accessed=10**6, transcendentals=0),
    )(*split_held, *split_came)
    joined = []
    for array, result, bit in zip(held, out, bits):
        shape = list(array.shape)
        shape[axis_of(bit)] = 2
        joined.append(result.reshape(shape))
    return joined


def mods_kernel(conditions, bias, packed, vgd, out, ada_a, ada_b, sems):
    copies = [
        pltpu.make_async_copy(packed.at[:, AT_ADA_A[0] : AT_ADA_A[1]], ada_a, sems.at[0]),
        pltpu.make_async_copy(vgd.at[:, AT_ADA_B[0] : AT_ADA_B[1]], ada_b, sems.at[1]),
    ]
    for copy in copies:
        copy.start()
    values = conditions[...].astype(f32)
    lifted = (values * sigmoid(values)).astype(bf16)
    for copy in copies:
        copy.wait()
    out[...] = jnp.concatenate([mm(lifted, ada_a[...]), mm(lifted, ada_b[...])], axis=1) + bias[...]


ADA_SCRATCH = [
    pltpu.VMEM((D, ADA_CUT), bf16),
    pltpu.VMEM((D, 6 * D - ADA_CUT), bf16),
    pltpu.SemaphoreType.DMA((2,)),
]


def modulations(conditions, bias, packed, vgd):
    return pl.pallas_call(
        mods_kernel,
        out_shape=jax.ShapeDtypeStruct((MICRO * SLOTS, 6 * D), f32),
        in_specs=[VMEM, VMEM, ANY, ANY],
        out_specs=VMEM,
        scratch_shapes=ADA_SCRATCH,
        compiler_params=pltpu.CompilerParams(vmem_limit_bytes=16 * 1024 * 1024),
        cost_estimate=pl.CostEstimate(flops=10**9, bytes_accessed=2 << 20, transcendentals=0),
    )(conditions, bias, packed, vgd)


def lifted_kernel(mine, came, packed, vgd, out, ada_a, ada_b, sems):
    copies = [
        pltpu.make_async_copy(packed.at[:, AT_ADA_A[0] : AT_ADA_A[1]], ada_a, sems.at[0]),
        pltpu.make_async_copy(vgd.at[:, AT_ADA_B[0] : AT_ADA_B[1]], ada_b, sems.at[1]),
    ]
    for copy in copies:
        copy.start()
    for copy in copies:
        copy.wait()
    first = lax.axis_index("section") == 0
    pair = mine[0:SLOTS, :].astype(f32), came[0:SLOTS, :].astype(f32)
    grad = jnp.concatenate(
        [jnp.where(first, pair[0], pair[1]), jnp.where(first, pair[1], pair[0])], axis=0
    ).astype(bf16)
    out[...] = mm_t(grad[:, :ADA_CUT], ada_a[...]) + mm_t(grad[:, ADA_CUT:], ada_b[...])


def lifted_grads(mine, came, packed, vgd):
    return pl.pallas_call(
        lifted_kernel,
        out_shape=jax.ShapeDtypeStruct((MICRO * SLOTS, D), f32),
        in_specs=[VMEM, VMEM, ANY, ANY],
        out_specs=VMEM,
        scratch_shapes=ADA_SCRATCH,
        compiler_params=pltpu.CompilerParams(vmem_limit_bytes=16 * 1024 * 1024),
        cost_estimate=pl.CostEstimate(flops=10**9, bytes_accessed=2 << 20, transcendentals=0),
    )(mine, came, packed, vgd)


def step_kernel(bit, widths, counts, *refs):
    mine = (lax.axis_index("row") >> bit) & 1
    count, many = len(widths), len(counts)
    refs = list(refs)
    take = lambda number: [refs.pop(0) for _ in range(number)]
    sources = take(count + many)
    targets = take(count + 1)
    buffers = take(count + many)
    results = take(count + 1)
    in_sems, out_sems = refs
    arrive = [
        pltpu.make_async_copy(source, buffer, in_sems.at[i])
        for i, (source, buffer) in enumerate(zip(sources, buffers))
    ]
    leave = [
        pltpu.make_async_copy(result, target, out_sems.at[i])
        for i, (result, target) in enumerate(zip(results, targets))
    ]
    for copy in arrive:
        copy.start()
    kept, came = buffers[:count], buffers[count:]
    places = [(j, i) for j, number in enumerate(counts) for i in range(number)]
    goes = results[count]
    at = 0
    for i in range(count):
        j, place = places[i]
        arrive[i].wait()
        if place == 0:
            arrive[count + j].wait()
        start = sum(widths[i - place : i])
        columns = slice(start, start + widths[i])
        total = kept[i][:, 1 - mine] + came[j][:, 1 - mine, :, :, columns].astype(f32)
        goes[:, :, :, at : at + widths[i]] = total.astype(bf16)
        at += widths[i]
    leave[count].start()
    for i in range(count):
        j, place = places[i]
        start = sum(widths[i - place : i])
        columns = slice(start, start + widths[i])
        results[i][...] = kept[i][:, mine] + came[j][:, mine, :, :, columns].astype(f32)
        leave[i].start()
    for copy in leave:
        copy.wait()


def step(kept, came, bit, below=1):
    blocks, rows = kept[0].shape[0] // 2, kept[0].shape[1]
    above = blocks // below
    paired = lambda array: array.reshape((above, 2, below) + array.shape[1:])
    widths = [array.shape[2] for array in kept]
    size = sum(array.size for array in kept)
    arrays = [paired(array) for array in kept] + [paired(array) for array, _ in came]
    shapes = [((above, below, rows, width), f32) for width in widths]
    shapes.append(((above, below, rows, sum(widths)), bf16))
    out = pl.pallas_call(
        functools.partial(step_kernel, bit, widths, [count for _, count in came]),
        out_shape=[jax.ShapeDtypeStruct(shape, kind) for shape, kind in shapes],
        in_specs=[HBM] * len(kept) + [ANY] * len(came),
        out_specs=[HBM] * len(kept) + [ANY],
        scratch_shapes=[pltpu.VMEM(array.shape, array.dtype) for array in arrays]
        + [pltpu.VMEM(shape, kind) for shape, kind in shapes]
        + [pltpu.SemaphoreType.DMA((len(arrays),)), pltpu.SemaphoreType.DMA((len(shapes),))],
        compiler_params=pltpu.CompilerParams(vmem_limit_bytes=16 * 1024 * 1024),
        cost_estimate=pl.CostEstimate(flops=size, bytes_accessed=8 * size, transcendentals=0),
    )(*arrays)
    count = len(kept)
    flat_blocks = [array.reshape((blocks,) + array.shape[2:]) for array in out]
    return flat_blocks[:count], flat_blocks[count]


def misc_step_kernel(held, arrived, out):
    size = held.shape[0] - SUMS
    out[:size, :] = held[:size, :]
    out[size : 2 * size, :] = arrived[:size, :]
    high, low = split(misc_sums(held, arrived))
    out[2 * size : 2 * size + SUMS // 2, :] = high
    out[2 * size + SUMS // 2 :, :] = low


def misc_step(held, arrived):
    return pl.pallas_call(
        misc_step_kernel,
        out_shape=jax.ShapeDtypeStruct((2 * held.shape[0] - SUMS, 2 * D), bf16),
        in_specs=[VMEM] * 2,
        out_specs=VMEM,
        cost_estimate=pl.CostEstimate(flops=10**5, bytes_accessed=10**5, transcendentals=0),
    )(held, arrived)


def misc_sums(*refs):
    size = refs[0].shape[0] - SUMS
    parts = [ref[size:, :].astype(f32) for ref in refs]
    return sum(part[: SUMS // 2] + part[SUMS // 2 :] for part in parts)


SUMS = 32


def misc_rows(conditions, mod_low):
    values = conditions[...].astype(f32)
    values = jnp.where(lax.axis_index("section") == 0, values[:SLOTS], values[SLOTS:])
    lifted = (values * sigmoid(values)).astype(bf16).astype(f32)
    rows = [
        mod_low[slot : slot + 1, i * 2 * D : (i + 1) * 2 * D].astype(f32)
        for slot in range(SLOTS)
        for i in range(3)
    ]
    rows.append(jnp.concatenate([lifted[0:1], lifted[1:2]], axis=1))
    rows.append(jnp.zeros((1, 2 * D), f32))
    return jnp.concatenate(rows, axis=0)


def misc_kernel(conditions, mod_low, *refs):
    out = refs[-1]
    rows = [misc_rows(conditions, mod_low)]
    if len(refs) == 3:
        rows.extend(part.astype(f32) for part in split(jnp.concatenate([refs[0][...], refs[1][...]], axis=0)))
    out[...] = jnp.concatenate(rows, axis=0).astype(bf16)


def pack_misc(conditions, mod_low, *sums):
    return pl.pallas_call(
        misc_kernel,
        out_shape=jax.ShapeDtypeStruct((8 + (SUMS if sums else 0), 2 * D), bf16),
        in_specs=[VMEM] * (2 + len(sums)),
        out_specs=VMEM,
    )(conditions, mod_low, *sums)


def grow_kernel(held, came, out):
    size = held.shape[0]
    out[:size, :] = held[...]
    out[size:, :] = came[...]


def grow(held, bit):
    came = partner(held, bit)
    return pl.pallas_call(
        grow_kernel,
        out_shape=jax.ShapeDtypeStruct((2 * held.shape[0], held.shape[1]), held.dtype),
        in_specs=[VMEM] * 2,
        out_specs=VMEM,
        cost_estimate=pl.CostEstimate(flops=10**5, bytes_accessed=10**5, transcendentals=0),
    )(held, came)


def finish_kernel(widths, counts, *refs):
    count = len(widths)
    kept, refs = refs[:count], refs[count:]
    came, refs = refs[: len(counts)], refs[len(counts) :]
    lifted, mod_two, misc, misc_came, mine, other, small_mine, small_other = refs
    places = [(ref, i) for ref, many in zip(came, counts) for i in range(many)]
    added = []
    for i in range(count):
        ref, place = places[i]
        start = sum(widths[i - place : i])
        added.append(kept[i][0] + ref[0, :, start : start + widths[i]].astype(f32))
    a1, f1, f2, a2 = added
    size = misc.shape[0] - SUMS
    mod_one = jnp.concatenate([misc[:size, :], misc_came[:size, :]], axis=0)

    def ada(rows):
        rows = rows.astype(f32).reshape(-1, 8, 2 * D)
        columns = []
        for i in range(3):
            both = [rows[:, 3 * slot + i, :] for slot in range(SLOTS)]
            columns.append(mm(lifted[...], jnp.concatenate(both, axis=0).astype(bf16)))
        return jnp.concatenate(columns, axis=1)

    first = lax.axis_index("section") == 0
    at = 0
    for one, two in ((a1, a2), (f1, f2), (ada(mod_one), ada(mod_two[...]))):
        columns = slice(at, at + one.shape[1])
        mine[:, columns] = jnp.where(first, one, two)
        other[:, columns] = jnp.where(first, two, one)
        at += one.shape[1]
    total = misc_sums(misc, misc_came)
    one, two = total[0:8, :], total[8:16, :]
    small_mine[...] = jnp.where(first, one, two)
    small_other[...] = jnp.where(first, two, one)


def finish(kept, came, lifted, mod_two, misc, misc_came):
    widths = [array.shape[2] for array in kept]
    shard = kept[0].shape[1]
    wide = GROUP + FF + 6 * D
    arrays = [array for array, _ in came]
    shapes = [(shard, wide)] * 2 + [(8, 2 * D)] * 2
    return pl.pallas_call(
        functools.partial(finish_kernel, widths, [count for _, count in came]),
        out_shape=[jax.ShapeDtypeStruct(shape, f32) for shape in shapes],
        in_specs=[VMEM] * (len(kept) + len(came) + 4),
        out_specs=[VMEM] * 4,
        compiler_params=pltpu.CompilerParams(vmem_limit_bytes=8 * 1024 * 1024),
    )(*kept, *arrays, lifted, mod_two, misc, misc_came)


def output_kernel(mine, other, small_mine, small_other, *outs):
    first = lax.axis_index("section") == 0

    def halves(start, width):
        columns = slice(start, start + width)
        pair = mine[:, columns], other[:, columns]
        return jnp.where(first, pair[0], pair[1]), jnp.where(first, pair[1], pair[0])

    attn = halves(0, GROUP)
    cut = GROUP - 2 * D
    outs[0][...] = attn[0][:, :D]
    outs[1][...] = attn[0][:, D : 2 * D]
    outs[2][:, :cut] = attn[0][:, 2 * D :]
    outs[2][:, cut:] = attn[1][:, : D - cut]
    outs[3][...] = attn[1][:, D - cut : 2 * D - cut]
    outs[4][...] = attn[1][:, 2 * D - cut : 3 * D - cut]
    decay = jnp.transpose(attn[1][:, 3 * D - cut :])
    for head in range(HEADS):
        outs[5][head] = decay[head : head + 1, :]
    up = halves(GROUP, FF // 2)
    outs[6][:, : FF // 2] = up[0]
    outs[6][:, FF // 2 :] = up[1]
    for piece in range(2):
        down = halves(GROUP + FF // 2 + piece * D, D)
        outs[7][piece] = down[0]
        outs[7][2 + piece] = down[1]
    outs[8][...] = mine[:, GROUP + FF :] + other[:, GROUP + FF :]
    small = small_mine[...] + small_other[...]
    half = 2 * D
    for i in range(3):
        outs[9][:, i * half : (i + 1) * half] = small[i : i + 1, :]
    for i in range(2):
        outs[10][:, i * half : (i + 1) * half] = small[3 + i : 4 + i, :]
    outs[11][...] = small[5:6, :D]
    outs[12][0] = small[5:6, D:]
    outs[12][1] = small[6:7, :D]
    outs[12][2] = small[6:7, D:]
    outs[13][...] = small[7:8, :HEADS]


def outputs(mine, other, small_mine, small_other):
    shard = mine.shape[0]
    shapes = (
        [(shard, D)] * 5
        + [(HEADS, 1, shard), (shard, FF), (4, shard, D), (shard, 6 * D)]
        + [(1, 6 * D), (1, FF), (1, D), (3, 1, D), (1, HEADS)]
    )
    return pl.pallas_call(
        output_kernel,
        out_shape=[jax.ShapeDtypeStruct(shape, f32) for shape in shapes],
        in_specs=[VMEM] * 4,
        out_specs=[VMEM] * len(shapes),
    )(mine, other, small_mine, small_other)


def both_kernel(one, two, came, out, kept, sems):
    section = lax.axis_index("section")

    def move(mine, layer):
        arrive = [
            pltpu.make_async_copy(mine, kept.at[layer], sems.at[0]),
            pltpu.make_async_copy(came, kept.at[1 - layer], sems.at[1]),
        ]
        leave = [
            pltpu.make_async_copy(kept.at[layer], out.at[layer], sems.at[2]),
            pltpu.make_async_copy(kept.at[1 - layer], out.at[1 - layer], sems.at[3]),
        ]
        for copy in arrive:
            copy.start()
        for copy, after in zip(arrive, leave):
            copy.wait()
            after.start()
        for copy in leave:
            copy.wait()

    @pl.when(section == 0)
    def _():
        move(one, 0)

    @pl.when(section == 1)
    def _():
        move(two, 1)


def both_micros(one, two, came):
    return pl.pallas_call(
        both_kernel,
        out_shape=jax.ShapeDtypeStruct((MICRO,) + one.shape, one.dtype),
        in_specs=[ANY] * 3,
        out_specs=ANY,
        scratch_shapes=[
            pltpu.VMEM((MICRO,) + one.shape, one.dtype),
            pltpu.SemaphoreType.DMA((4,)),
        ],
    )(one, two, came)


def swap(values):
    return lax.ppermute(values, "section", [(0, 1), (1, 0)])


def row_bits():
    bits = lax.axis_size("row").bit_length() - 1
    third = bits // 3
    return (
        tuple(range(third)),
        tuple(range(third, 2 * third)),
        tuple(range(2 * third, bits)),
    )


def partner(values, bit):
    size = lax.axis_size("row")
    return lax.ppermute(values, "row", [(i, i ^ (1 << bit)) for i in range(size)])


def axis_of(bit):
    return lax.axis_size("row").bit_length() - 2 - bit


def bit_of(bit):
    return (lax.axis_index("row") >> bit) & 1


def single(values):
    return values.reshape((1,) * (lax.axis_size("row").bit_length() - 1) + values.shape)


def gather_pair(first, second, along_x, along_y, along_z, at_first=None, at_last=None):
    held = [single(first), single(second)]
    steps = [(bit, bit) for bit in reversed(along_z)]
    steps += list(zip(along_x + along_y, along_y + along_x))
    for bits in steps:
        came = [partner(array, bit) for array, bit in zip(held, bits)]
        if at_first is not None and bits is steps[0]:
            *came, at_first = lock(*came, at_first)
        if at_last is not None and bits is steps[-1]:
            *came, at_last = lock(*came, at_last)
        held = join(held, came, bits)
    return [flat(array) for array in held], at_first, at_last


def flat(held):
    return held.reshape(-1, held.shape[-1])


def lock(*arrays):
    return lax.optimization_barrier(arrays)


def on_device(
    tokens, conditions, output_grad, layouts,
    w_ada, b_ada, w_query, w_key, w_value, w_gate, w_out, w_decay, b_decay, conv_kernel,
    w_up, b_up, w_down, b_down,
):
    section = lax.axis_index("section")
    devices = lax.axis_size("row")
    shard = w_query.shape[1]
    along_x, along_y, along_z = row_bits()

    def both(values):
        return values, swap(values)

    qka, vgda, upo = pack(
        w_query, w_key, w_value, w_gate, w_out, w_decay.transpose(0, 2, 1), w_ada, w_up
    )
    runs = (along_x, along_y, along_z)
    small = pack_small(b_up, b_down, conv_kernel, b_decay)
    gathered, small, _ = gather_pair(qka, vgda, *runs, at_first=small)
    qka, vgda = [both(array) for array in gathered]

    conds = conditions.reshape(MICRO * SLOTS, D)
    mods = both(modulations(conds, b_ada, qka[0], vgda[0]))
    smalls = both(small)

    x = tokens
    *saved, gated = attn_forward(0, layouts, x, mods, smalls, qka, vgda)
    gathered, _, gated = gather_pair(upo, w_down[0], *runs, at_last=gated)
    upo, down = [both(array) for array in gathered]
    kept = []
    acts = []
    for l in range(2):
        if l:
            *saved, gated = attn_forward(l, layouts, x, mods, smalls, qka, vgda)
        out, branch, down_raw, *acts_sent = ffn_forward(
            l, layouts, x, mods, smalls, gated, upo, down
        )
        kept.append((x, saved, gated, branch, down_raw))
        acts.append(out)
        x = out[None]

    def ffn_step(l, grad):
        x, saved, gated, branch, down_raw = kept[l]
        mid_grad, branch_low, gwo, sums, *terms = ffn_backward(
            l, layouts, x, mods, smalls, gated, branch, down_raw, grad, upo, down, devices
        )
        if terms[0].ndim == 2:
            up_sum = terms[0].reshape(devices, shard, 2, FF // 2)
            down_sum = terms[1].reshape(devices, 2, 2, shard, D)
            terms = []
            for own in (section, 1 - section):
                up_half = lax.dynamic_index_in_dim(up_sum, own, 2, keepdims=False)
                down_half = lax.dynamic_index_in_dim(down_sum, own, 1, keepdims=False)
                terms.append(
                    jnp.concatenate([up_half, down_half[:, 0], down_half[:, 1]], axis=2)
                )
            terms[1] = terms[1].astype(bf16)
        return [branch_low, gwo], mid_grad, terms[0], terms[1], sums

    def mixer_step(l, carried):
        low, keep, sent, sums = mixer_backward(l, layouts, smalls, kept[l][1], *carried, upo)
        by_row = lambda array: array.reshape(devices, shard, GROUP)
        return low, by_row(keep), by_row(sent), sums

    def input_step(l, low, mid_grad, ffn_sums, mixer_sums, two=None):
        return input_backward(
            l, layouts, kept[l][0], mods, low, mid_grad, ffn_sums, mixer_sums, qka, vgda, two
        )

    def run(keep, came, bits, below=1):
        for bit in bits[:-1]:
            keep, sent = step(keep, came, bit, below=below)
            came = [(partner(sent, bit), len(keep))]
        return step(keep, came, bits[-1], below=below)

    def grown(mod, bits):
        for bit in bits:
            mod = grow(mod, bit)
        return mod

    x_bits, y_bits, z_bits = along_x, along_y, along_z
    carried, mid_grad, f2_keep, f2_sent, f2_sums = ffn_step(1, output_grad)
    *carried, f2_sent, acts_sent = lock(*carried, f2_sent, acts_sent[0])
    f2_came = swap(f2_sent)
    acts_came = swap(acts_sent)
    low, a2_keep, a2_sent, m2_sums = mixer_step(1, carried)
    low, a2_sent, f2_came, acts_came = lock(low, a2_sent, f2_came, acts_came)
    a2_came = swap(a2_sent)
    gx_two, grad, mod_low_two, sums_two = input_step(1, low, mid_grad, f2_sums, m2_sums)
    mod_two = pack_misc(conds, mod_low_two)
    grad, mod_two, a2_came = lock(grad, mod_two, a2_came)
    f2_keep, f2_sent = run([f2_keep], [(f2_came, 1)], x_bits)
    a2_keep, a2_sent = run([a2_keep], [(a2_came, 1)], y_bits, 1 << len(x_bits))
    mod_two = grown(mod_two, x_bits[:-1])
    grad, f2_sent, a2_sent, mod_two = lock(grad, f2_sent, a2_sent, mod_two)
    f2_came = partner(f2_sent, x_bits[-1])
    mod_two = grown(mod_two, x_bits[-1:])
    a2_came = partner(a2_sent, y_bits[-1])

    carried, mid_grad, f1_keep, f1_sent, f1_sums = ffn_step(0, grad[None])
    *carried, f1_sent, f2_came, a2_came, mod_two = lock(
        *carried, f1_sent, f2_came, a2_came, mod_two
    )
    f1_came = swap(f1_sent)
    f2_keep, f2_sent = run(f2_keep, [(f2_came, 1)], y_bits)
    a2_keep, a2_sent = run(a2_keep, [(a2_came, 1)], x_bits)
    mod_two = grown(mod_two, y_bits[:-1])
    f1_keep, f1_sent = run([f1_keep], [(f1_came, 1)], x_bits)
    *carried, f2_sent, a2_sent, mod_two, f1_sent = lock(
        *carried, f2_sent, a2_sent, mod_two, f1_sent
    )
    f1_came = partner(f1_sent, x_bits[-1])
    a2_came = partner(a2_sent, x_bits[-1])
    f2_came = partner(f2_sent, y_bits[-1])
    mod_two = grown(mod_two, y_bits[-1:])
    low, a1_keep, a1_sent, m1_sums = mixer_step(0, carried)
    low, a1_sent, f2_came, a2_came, mod_two, f1_came = lock(
        low, a1_sent, f2_came, a2_came, mod_two, f1_came
    )
    a1_came = swap(a1_sent)
    acts_out = both_micros(acts[0], acts[1], acts_came)
    two_keep, two_sent = run(f2_keep + a2_keep, [(f2_came, 1), (a2_came, 1)], z_bits[:1])
    f1_keep, f1_sent = run(f1_keep, [(f1_came, 1)], y_bits)
    a1_keep, a1_sent = run([a1_keep], [(a1_came, 1)], x_bits)
    low, acts_out, two_sent, mod_two, f1_sent, a1_sent = lock(
        low, acts_out, two_sent, mod_two, f1_sent, a1_sent
    )
    a1_came = partner(a1_sent, x_bits[-1])
    two_came = partner(two_sent, z_bits[0])
    mod_two = grown(mod_two, z_bits[:1])
    f1_came = partner(f1_sent, y_bits[-1])
    gx_one, _, mod_low_one, sums_one, gx_sent, mod_mine, mod_sent = input_step(
        0, low, mid_grad, f1_sums, m1_sums, (gx_two, mod_low_two)
    )
    misc = pack_misc(conds, mod_low_one, sums_one, sums_two)
    misc, a1_came, two_came, mod_two, f1_came, gx_sent, mod_sent = lock(
        misc, a1_came, two_came, mod_two, f1_came, gx_sent, mod_sent
    )

    a1_keep, a1_sent = run(a1_keep, [(a1_came, 1)], y_bits)
    two_keep, two_sent = run(two_keep, [(two_came, 2)], z_bits[1:])
    mod_two = grown(mod_two, z_bits[1:-1])
    a1_sent, misc, two_sent, mod_two = lock(a1_sent, misc, two_sent, mod_two)
    a1_came = partner(a1_sent, y_bits[-1])
    for bit in x_bits + y_bits:
        misc = misc_step(misc, partner(misc, bit))
    two_came = partner(two_sent, z_bits[-1])
    mod_two = grown(mod_two, z_bits[-1:])
    gx_came = swap(gx_sent)
    mod_came = swap(mod_sent)
    gx_out = both_micros(gx_one, gx_two, gx_came)
    grad_lifted = lifted_grads(mod_mine, mod_came, qka[0], vgda[0])
    lifted_came = swap(grad_lifted)
    keep, came = a1_keep + f1_keep, [(a1_came, 1), (f1_came, 1)]
    for bit in z_bits:
        keep, sent = step(keep, came, bit)
        if bit == z_bits[-1]:
            sent, misc, gx_out, grad_lifted, lifted_came, mod_two = lock(
                sent, misc, gx_out, grad_lifted, lifted_came, mod_two
            )
        else:
            sent, misc = lock(sent, misc)
        came = [(partner(sent, bit), len(keep))]
        misc_came = partner(misc, bit)
        if bit != z_bits[-1]:
            misc = misc_step(misc, misc_came)
    pair = (misc, misc_came)
    lifted = mod_two.reshape(devices, 8, SLOTS, D)[:, 6]
    lifted = lax.dynamic_slice_in_dim(lifted, lax.axis_index("row") * shard, shard, 2)
    lifted = lifted.transpose(2, 1, 0).reshape(shard, SLOTS * devices)
    mine, other, small_mine, small_other = finish(
        keep + two_keep, came + [(two_came, 2)], lifted, mod_two, *pair
    )
    came, small_came = swap(other), swap(small_other)
    (
        g_query, g_key, g_value, g_gate, g_out, g_decay, g_up, g_down, g_ada,
        g_b_ada, g_b_up, g_b_down, g_conv, g_b_decay,
    ) = outputs(mine, came, small_mine, small_came)

    grad_lifted = (grad_lifted + lifted_came).reshape(MICRO, SLOTS, D)
    _, pull_silu = jax.vjp(jax.nn.silu, conditions.astype(f32))
    (cond_grads,) = pull_silu(grad_lifted)

    return (
        acts_out[None],
        gx_out[None],
        cond_grads,
        g_ada[None],
        g_b_ada,
        g_query[None],
        g_key[None],
        g_value[None],
        g_gate[None],
        g_out[None],
        g_decay.transpose(1, 2, 0),
        g_b_decay,
        g_conv.transpose(1, 0, 2),
        g_up[None],
        g_b_up,
        g_down.reshape(1, FF // devices, D),
        g_b_down,
    )


def solution(mesh):
    rows = P(None, "row", None)
    mats = P("section", "row", None)
    vector = P("section", None)
    in_specs = (
        rows, rows, rows, P(None, "row"),
        mats, vector, mats, mats, mats, mats, mats, mats, vector, P("section", None, None),
        mats, vector, mats, vector,
    )
    blocks = P("section", None, "row", None)
    out_specs = (
        blocks, blocks, rows,
        mats, vector, mats, mats, mats, mats, mats, mats, vector, P("section", None, None),
        mats, vector, mats, vector,
    )
    return jax.shard_map(
        on_device, mesh=mesh, in_specs=in_specs, out_specs=out_specs, check_vma=False
    )
```

```python
import functools

import jax
import jax.numpy as jnp
from jax import lax
from jax.experimental import pallas as pl
from jax.experimental.pallas import tpu as pltpu
from jax.sharding import PartitionSpec as P

D = 384
HEADS = 6
HEAD_DIM = 64
FF = 1536
MICRO = 2
ROWS = 512
HALF = 256
SLOTS = 2
PAIR = 128
PAIRS = D // PAIR
QKVG = 4 * D
LANES = 128
GROUP = (QKVG + D + LANES) // 2
NEG = -1e30
SCALE = HEAD_DIM**-0.5

bf16 = jnp.bfloat16
f32 = jnp.float32


def mm(left, right):
    return jnp.dot(left, right, preferred_element_type=f32)


def mm_t(left, right):
    return lax.dot_general(left, right, (((1,), (1,)), ((), ())), preferred_element_type=f32)


def split(values):
    high = values.astype(bf16)
    return high, (values - high.astype(f32)).astype(bf16)


def split_three(values):
    high, rest = split(values)
    mid = values - high.astype(f32)
    middle, low = split(mid)
    return high, middle, low


def cat_left(values):
    high, low = split(values)
    return jnp.concatenate([high, low, high], axis=1)


def cat_right(values):
    high, low = split(values)
    return jnp.concatenate([high, high, low], axis=1)


def mm_near(left, right_pair, right_high):
    high, low = split(left)
    wide = mm(high, right_pair)
    return wide[:, :PAIR] + wide[:, PAIR:] + mm(low, right_high)


def lane_iota(rows, columns):
    return lax.broadcasted_iota(jnp.int32, (rows, columns), 1)


def row_iota(rows, columns):
    return lax.broadcasted_iota(jnp.int32, (rows, columns), 0)


def order_matrix(start, rows, wide, to_scan):
    t = row_iota(rows, ROWS) + start
    small = (t & 256) + ((t & 15) << 4) + ((t & 255) >> 4)
    if to_scan:
        large = ((t & 15) << 5) + (t >> 4)
    else:
        large = ((t & 31) << 4) + (t >> 5)
    source = jnp.where(wide, large, small)
    return jnp.where(lane_iota(rows, ROWS) == source, 1.0, 0.0).astype(bf16)


def normalise(values):
    centred = values - jnp.mean(values, axis=-1, keepdims=True)
    rate = lax.rsqrt(jnp.mean(centred * centred, axis=-1, keepdims=True) + 1e-06)
    return centred * rate, rate


def normalise_back(normal, rate, grad):
    return rate * (
        grad
        - jnp.mean(grad, axis=-1, keepdims=True)
        - normal * jnp.mean(grad * normal, axis=-1, keepdims=True)
    )


class In:
    def __init__(self, copy, kept):
        self.copy = copy
        self.kept = kept

    def __call__(self):
        if self.copy is not None:
            self.copy.wait()
            self.copy = None
        return self.kept


class Kernel:
    def __init__(self, layer, layouts):
        self.layer = layer
        self.section = lax.axis_index("section")
        self.own = self.section == layer
        self.layout = layouts[self.section, 0]
        self.wide = self.layout == 0
        self.live_rows = jnp.where(self.wide, ROWS, self.layout * HALF)
        self.pushed = {}

    def load(self, kind, refs, kept, sem):
        if kind == "own":
            mine, other = refs

            @pl.when(self.own)
            def _():
                pltpu.make_async_copy(mine, kept, sem).start()

            @pl.when(jnp.logical_not(self.own))
            def _():
                pltpu.make_async_copy(other, kept, sem).start()

            return In(pltpu.make_async_copy(mine, kept, sem), kept)
        (source,) = refs
        if kind == "micro":
            source = source.at[self.section if source.shape[0] == MICRO else 0]
        copy = pltpu.make_async_copy(source, kept, sem)
        copy.start()
        return In(copy, kept)

    def push(self, name):
        kept, target, sem = self.results[name]
        copy = pltpu.make_async_copy(kept, target, sem)
        copy.start()
        self.pushed[name] = copy

    def finish(self):
        for name in self.results:
            if name not in self.pushed:
                self.push(name)
        for copy in self.pushed.values():
            copy.wait()

    def slot(self, half):
        return jnp.where(self.wide, 0, half)

    def share(self, slot, part):
        row = pl.ds(2 * self.section + slot, 1)
        return self.mods()[row, part * D : (part + 1) * D]

    def bu(self):
        return self.small()[0:1, :]

    def bn(self):
        return self.small()[1:2, :D]

    def ck(self, tap):
        return self.small()[2 + tap : 3 + tap, :D]

    def bd(self):
        return self.small()[5:6, :LANES]


def sigmoid(values):
    return 1.0 / (1.0 + jnp.exp(-values))


GELU_A = 0.7978845608028654
GELU_B = 0.044715


def gelu_parts(values):
    square = values * values
    tanh = jnp.tanh(GELU_A * values * (1.0 + GELU_B * square))
    return square, tanh


def fill_bias(bias, wide):
    bias[:, :HALF] = jnp.full((HALF, HALF), 0.0, f32) + jnp.where(wide, 0.0, NEG)
    causal = row_iota(HALF, HALF) >= lane_iota(HALF, HALF)
    bias[:, HALF:] = jnp.where(causal, 0.0, NEG)


def decay_factors(cum, cumt, bias, head):
    row = cumt[pl.ds(head, 1), :]
    lanes = lane_iota(1, LANES)
    column = jnp.sum(jnp.where(lanes == head, cum[...], 0.0), axis=1, keepdims=True)
    first = jnp.exp(column[:HALF] - row[:, :HALF] + bias[:, HALF:])
    second = jnp.exp(column[HALF:] - row + bias[...])
    return first, second


def head_norm(values, lanes):
    square = values * values
    low = jnp.sum(jnp.where(lanes < HEAD_DIM, square, 0.0), axis=1, keepdims=True)
    high = jnp.sum(jnp.where(lanes < HEAD_DIM, 0.0, square), axis=1, keepdims=True)
    return jnp.where(lanes < HEAD_DIM, low, high) * (1.0 / HEAD_DIM)


def fill_decay(dp, bd, cum, cumt):
    raw = dp[...] + bd
    log_decay = (jnp.minimum(raw, 0.0) - jnp.log1p(jnp.exp(-jnp.abs(raw)))) * (1.0 / 16.0)
    high, middle, low = split_three(log_decay)
    causal = jnp.where(row_iota(ROWS, ROWS) >= lane_iota(ROWS, ROWS), 1.0, 0.0).astype(bf16)
    cum[...] = mm(causal, high) + mm(causal, middle) + mm(causal, low)
    cumt[...] = jnp.transpose(cum[...])


def columns(index, first=0):
    return slice(index * PAIR + first, index * PAIR + first + PAIR)


def attn_forward_body(k):
    flip = k.layer == 1
    wide = k.wide
    x = k.x()
    k.mods()

    def first(i, carry):
        rows = pl.ds(pl.multiple_of(i * HALF, HALF), HALF)
        slot = k.slot(i)
        normal, _ = normalise(x[rows, :].astype(f32))
        k.inner[rows, :] = (normal * (1.0 + k.share(slot, 1)) + k.share(slot, 0)).astype(bf16)
        return carry

    lax.fori_loop(0, 2, first, 0)
    w_qk = k.w_qk()
    w_vgd = k.w_vgd()

    def project(i, carry):
        start = i * HALF
        rows = pl.ds(start, HALF)
        if flip:
            part = mm(order_matrix(start, HALF, wide, True), k.inner[...]).astype(bf16)
        else:
            part = k.inner[rows, :]
        k.ordered[rows, :] = part
        k.qkvg[rows, : 2 * D] = mm(part, w_qk[...])
        k.qkvg[rows, 2 * D :] = mm(part, w_vgd[:, : 2 * D])
        k.dp[rows, :] = mm(part, w_vgd[:, 2 * D :])
        return carry

    lax.fori_loop(0, 2, project, 0)
    k.small()
    for name in ("ordered", "qkvg", "dp"):
        k.push(name)
    fill_decay(k.dp, k.bd(), k.cum, k.cumt)
    fill_bias(k.bias, wide)

    vpad = k.vpad
    vpad[0:8, :] = jnp.zeros((8, D), f32)
    vpad[8 : 8 + ROWS, :] = k.qkvg[:, 2 * D : 3 * D]
    position = row_iota(ROWS, 1) & jnp.where(wide, ROWS - 1, HALF - 1)
    one = jnp.where(position >= 1, vpad[7 : 7 + ROWS, :], 0.0)
    two = jnp.where(position >= 2, vpad[6 : 6 + ROWS, :], 0.0)
    k.vc[...] = k.ck(0) * vpad[8 : 8 + ROWS, :] + k.ck(1) * one + k.ck(2) * two
    for name in ("cum", "cumt", "vc"):
        k.push(name)

    def pair(p, carry):
        lanes = lane_iota(1, PAIR)
        queries = cat_left(k.qkvg[:, columns(p)] * SCALE)
        keys = k.qkvg[:, columns(p, D)]
        value_high, value_low = split(k.vc[:, columns(p)])
        values = jnp.concatenate([value_high, value_low], axis=1)
        parts = []
        for e in range(2):
            key_cat = cat_right(jnp.where((lanes // HEAD_DIM) == e, keys, 0.0))
            first, second = decay_factors(k.cum, k.cumt, k.bias, 2 * p + e)
            first = first * mm_t(queries[:HALF], key_cat[:HALF])
            second = second * mm_t(queries[HALF:], key_cat)
            parts.append(
                jnp.concatenate(
                    [
                        mm_near(first, values[:HALF], value_high[:HALF]),
                        mm_near(second, values, value_high),
                    ],
                    axis=0,
                )
            )
        total = jnp.where(lanes < HEAD_DIM, parts[0], parts[1])
        k.o[:, columns(p)] = total
        gate = k.qkvg[:, columns(p, 3 * D)]
        normed = total * lax.rsqrt(head_norm(total, lanes) + 1.0)
        mixed = (normed * (gate * sigmoid(gate))).astype(bf16)
        if flip:
            k.inner[:, columns(p)] = mixed
        else:
            k.gated[:, columns(p)] = mixed
        return carry

    for p in range(PAIRS):
        pair(p, 0)
    k.push("o")
    if flip:

        def back(i, carry):
            start = i * HALF
            k.gated[pl.ds(start, HALF), :] = mm(
                order_matrix(start, HALF, wide, False), k.inner[...]
            ).astype(bf16)
            return carry

        lax.fori_loop(0, 2, back, 0)


def ffn_forward_body(k):
    gated, x = k.gated(), k.x()
    k.mods(), k.small()

    def tile(i, carry):
        start = i * HALF
        rows = pl.ds(start, HALF)
        slot = k.slot(i)
        grown = mm(gated[rows, :], k.wo()[...])
        k.branch[rows, :] = grown
        middle = x[rows, :].astype(f32) + k.share(slot, 2) * grown
        normal, _ = normalise(middle)
        inner = (normal * (1.0 + k.share(slot, 4)) + k.share(slot, 3)).astype(bf16)
        up = mm(inner, k.wu()[...]) + k.bu()
        _, tanh = gelu_parts(up)
        hidden = (0.5 * up * (1.0 + tanh)).astype(bf16)
        low = mm(hidden, k.wn()[...])
        k.down[rows, :] = low
        result = middle + k.share(slot, 5) * (low + k.bn())
        live = (row_iota(HALF, 1) + start) < k.live_rows
        k.out[rows, :] = jnp.where(live, result, 0.0).astype(bf16)
        return carry

    for i in range(2):
        tile(i, 0)
    if k.layer == 1:
        k.sent[...] = jnp.where(k.section == 0, k.out[...].astype(f32), x[...].astype(f32)).astype(bf16)


def ffn_backward_body(k):
    gmod, gbu, gbn = k.gmod, k.gbu, k.gbn
    gmod[...] = jnp.zeros(gmod.shape, f32)
    gbu[...] = jnp.zeros(gbu.shape, f32)
    gbn[...] = jnp.zeros(gbn.shape, f32)
    k.mods(), k.small()
    x, grad, branch, down = k.x(), k.grad(), k.branch(), k.down()

    def tile(i, carry):
        start = i * HALF
        rows = pl.ds(start, HALF)
        slot = k.slot(i)

        def add(part, values):
            where = (pl.ds(slot, 1), slice((part - 2) * D, (part - 1) * D))
            gmod[where] = gmod[where] + jnp.sum(values, axis=0, keepdims=True)

        grown = branch[rows, :]
        middle = x[rows, :].astype(f32) + k.share(slot, 2) * grown
        normal, rate = normalise(middle)
        inner = (normal * (1.0 + k.share(slot, 4)) + k.share(slot, 3)).astype(bf16)
        k.inner_s[rows, :] = inner
        live = (row_iota(HALF, 1) + start) < k.live_rows
        above = jnp.where(live, grad[rows, :].astype(f32), 0.0)
        add(5, above * (down[rows, :] + k.bn()))
        grad_down = above * k.share(slot, 5)
        gbn[...] = gbn[...] + jnp.sum(grad_down, axis=0, keepdims=True)
        down_low = grad_down.astype(bf16)
        k.down_s[rows, :] = down_low
        up = mm(inner, k.wu()[...]) + k.bu()
        square, tanh = gelu_parts(up)
        half = 0.5 * (1.0 + tanh)
        k.hidden_s[rows, :] = (up * half).astype(bf16)
        slope = half + 0.5 * up * (1.0 - tanh * tanh) * (
            GELU_A * (1.0 + 3.0 * GELU_B * square)
        )
        grad_up = mm_t(down_low, k.wn()[...]) * slope
        gbu[...] = gbu[...] + jnp.sum(grad_up, axis=0, keepdims=True)
        up_low = grad_up.astype(bf16)
        k.up_s[rows, :] = up_low
        grad_inner = mm_t(up_low, k.wu()[...])
        add(3, grad_inner)
        add(4, grad_inner * normal)
        grad_middle = above + normalise_back(
            normal, rate, grad_inner * (1.0 + k.share(slot, 4))
        )
        k.mid_grad[rows, :] = grad_middle
        add(2, grad_middle * grown)
        k.branch_low[rows, :] = (grad_middle * k.share(slot, 2)).astype(bf16)
        return carry

    for i in range(2):
        tile(i, 0)
    k.push("mid_grad")
    k.push("branch_low")

    def weights(j, carry):
        part = pl.ds(pl.multiple_of(j * HALF, HALF), HALF)
        hidden_t = jnp.transpose(k.hidden_s[:, part].astype(f32)).astype(bf16)
        k.gwn[part, :] = mm(hidden_t, k.down_s[...])
        return carry

    lax.fori_loop(0, FF // HALF, weights, 0)
    inner_t = jnp.transpose(k.inner_s[...].astype(f32)).astype(bf16)
    if k.packed:
        devices, shard, _ = k.keep.shape

        def halves(j, carry):
            for kept, own in ((k.keep, c_section), (k.sent, 1 - c_section)):
                columns = pl.ds(pl.multiple_of(j * HALF + own * (FF // 2), HALF), HALF)
                here = pl.ds(pl.multiple_of(j * HALF, HALF), HALF)
                part = mm(inner_t, k.up_s[:, columns]).reshape(devices, shard, HALF)
                kept[:, :, here] = part.astype(kept.dtype)
            return carry

        c_section = k.section
        lax.fori_loop(0, FF // 2 // HALF, halves, 0)

        def owner(r, carry):
            for kept, own in ((k.keep, c_section), (k.sent, 1 - c_section)):
                for piece in range(2):
                    start = pl.multiple_of((4 * r + 2 * own + piece) * shard, 8)
                    rows = k.gwn[pl.ds(start, shard), :]
                    at = FF // 2 + piece * D
                    kept[r, :, at : at + D] = rows.astype(kept.dtype)
            return carry

        lax.fori_loop(0, devices, owner, 0)
        k.push("keep")
        k.push("sent")
    else:
        k.gwu[...] = mm(inner_t, k.up_s[...])
    gated = k.gated()
    k.gwo[...] = mm(jnp.transpose(gated[...].astype(f32)).astype(bf16), k.branch_low[...])

    short = jnp.concatenate([gbn[...], jnp.zeros((1, FF - D), f32)], axis=1)
    k.sums[...] = jnp.concatenate(
        [gmod[0:SLOTS, :], gbu[...], short, jnp.zeros((4, FF), f32)], axis=0
    )


def mixer_backward_body(k):
    flip = k.layer == 1
    wide = k.wide
    mixed_s, low, dv_s, rows_s, cols_s = k.mixed_s, k.low, k.dv_s, k.rows_s, k.cols_s
    fill_bias(k.bias, wide)
    branch_low, wo = k.branch_low(), k.wo()

    def first(i, carry):
        start = i * HALF
        rows = pl.ds(start, HALF)
        if flip:
            part = mm(order_matrix(start, HALF, wide, True), branch_low[...]).astype(bf16)
        else:
            part = branch_low[rows, :]
        mixed_s[rows, :] = mm_t(part, wo[...])
        return carry

    lax.fori_loop(0, 2, first, 0)
    rows_s[...] = jnp.zeros(rows_s.shape, f32)
    cols_s[...] = jnp.zeros(cols_s.shape, f32)
    qkvg, vc, cum, cumt, o = k.qkvg(), k.vc(), k.cum(), k.cumt(), k.o()
    k.small()

    def pair(p, carry):
        lanes = lane_iota(1, PAIR)
        total = o[:, columns(p)]
        gate = qkvg[:, columns(p, 3 * D)]
        above = mixed_s[:, columns(p)]
        rate = lax.rsqrt(head_norm(total, lanes) + 1.0)
        sig = sigmoid(gate)
        grad_gate = above * (total * rate) * (sig * (1.0 + gate * (1.0 - sig)))
        low[:, columns(p, 3 * D)] = grad_gate.astype(bf16)
        grad_normed = above * (gate * sig)
        product = grad_normed * total
        inside = jnp.where(
            lanes < HEAD_DIM,
            jnp.sum(jnp.where(lanes < HEAD_DIM, product, 0.0), axis=1, keepdims=True),
            jnp.sum(jnp.where(lanes < HEAD_DIM, 0.0, product), axis=1, keepdims=True),
        ) * (1.0 / HEAD_DIM)
        grad_o = rate * grad_normed - total * (rate * rate * rate) * inside

        queries = qkvg[:, columns(p)] * SCALE
        keys = qkvg[:, columns(p, D)]
        values = vc[:, columns(p)]
        query_cat = cat_left(queries)
        grad_cat = cat_left(grad_o)
        key_high, key_low = split(keys)
        key_pair = jnp.concatenate([key_high, key_low], axis=1)
        query_t = jnp.transpose(queries)
        grad_t = jnp.transpose(grad_o)
        grad_q = []
        grad_k = []
        grad_v = []
        for e in range(2):
            mine = (lanes // HEAD_DIM) == e
            head = 2 * p + e
            key_cat = cat_right(jnp.where(mine, keys, 0.0))
            value_cat = cat_right(jnp.where(mine, values, 0.0))
            first, second = decay_factors(cum, cumt, k.bias, head)
            raw_first = mm_t(query_cat[:HALF], key_cat[:HALF])
            raw_second = mm_t(query_cat[HALF:], key_cat)
            grad_first = first * mm_t(grad_cat[:HALF], value_cat[:HALF])
            grad_second = second * mm_t(grad_cat[HALF:], value_cat)
            score_first = raw_first * first
            score_second = raw_second * second
            pull_first = grad_first * raw_first
            pull_second = grad_second * raw_second
            here = lanes == head
            rows_s[:HALF, :] = rows_s[:HALF, :] + jnp.where(
                here, jnp.sum(pull_first, axis=1, keepdims=True), 0.0
            )
            rows_s[HALF:, :] = rows_s[HALF:, :] + jnp.where(
                here, jnp.sum(pull_second, axis=1, keepdims=True), 0.0
            )
            low_cols = jnp.sum(pull_second, axis=0, keepdims=True)
            cols_s[pl.ds(head, 1), :HALF] = low_cols[:, :HALF] + jnp.sum(
                pull_first, axis=0, keepdims=True
            )
            cols_s[pl.ds(head, 1), HALF:] = low_cols[:, HALF:]
            grad_q.append(
                jnp.concatenate(
                    [
                        mm_near(grad_first, key_pair[:HALF], key_high[:HALF]),
                        mm_near(grad_second, key_pair, key_high),
                    ],
                    axis=0,
                )
            )

            def turned(source_t, block_first, block_second):
                high, low = split(source_t[e * HEAD_DIM : (e + 1) * HEAD_DIM, :])
                both = jnp.concatenate([high, low], axis=0)
                first_high, first_low = split(block_first)
                second_high, second_low = split(block_second)
                one = mm(both[:, :HALF], first_high)
                one = one[:HEAD_DIM] + one[HEAD_DIM:] + mm(high[:, :HALF], first_low)
                two = mm(both[:, HALF:], second_high)
                two = two[:HEAD_DIM] + two[HEAD_DIM:] + mm(high[:, HALF:], second_low)
                return jnp.concatenate([two[:, :HALF] + one, two[:, HALF:]], axis=1)

            grad_k.append(turned(query_t, grad_first, grad_second))
            grad_v.append(turned(grad_t, score_first, score_second))
        query_grad = jnp.where(lanes < HEAD_DIM, grad_q[0], grad_q[1]) * SCALE
        low[:, columns(p)] = query_grad.astype(bf16)
        low[:, columns(p, D)] = jnp.transpose(jnp.concatenate(grad_k, axis=0)).astype(bf16)
        dv_s[:ROWS, columns(p)] = jnp.transpose(jnp.concatenate(grad_v, axis=0))
        return carry

    for p in range(PAIRS):
        pair(p, 0)

    pulled = rows_s[...] - jnp.transpose(cols_s[...])
    high, middle, rest = split_three(pulled)
    upper_first = jnp.concatenate(
        [
            jnp.where(row_iota(HALF, HALF) <= lane_iota(HALF, HALF), 1.0, 0.0),
            jnp.full((HALF, HALF), 0.0, f32) + jnp.where(wide, 1.0, 0.0),
        ],
        axis=1,
    ).astype(bf16)
    upper_second = upper_first[:, :HALF]
    later = jnp.concatenate(
        [
            mm(upper_first, high) + mm(upper_first, middle) + mm(upper_first, rest),
            mm(upper_second, high[HALF:]) + mm(upper_second, middle[HALF:])
            + mm(upper_second, rest[HALF:]),
        ],
        axis=0,
    )
    grad_dp = later * (1.0 / 16.0) * sigmoid(-(k.dp()[...] + k.bd()))
    grad_bd = jnp.sum(grad_dp, axis=0, keepdims=True)
    low[:, QKVG:] = grad_dp.astype(bf16)

    dv_s[ROWS:, :] = jnp.zeros((8, D), f32)
    position = row_iota(ROWS, 1) & jnp.where(wide, ROWS - 1, HALF - 1)
    last = jnp.where(wide, ROWS - 1, HALF - 1)
    here = dv_s[0:ROWS, :]
    one = jnp.where(position <= last - 1, dv_s[1 : 1 + ROWS, :], 0.0)
    two = jnp.where(position <= last - 2, dv_s[2 : 2 + ROWS, :], 0.0)
    value = qkvg[:, 2 * D : 3 * D]
    low[:, 2 * D : 3 * D] = (k.ck(0) * here + k.ck(1) * one + k.ck(2) * two).astype(bf16)
    k.push("low")

    taps = [jnp.sum(rows * value, axis=0, keepdims=True) for rows in (here, one, two)]
    rest = jnp.concatenate([grad_bd, jnp.zeros((1, D - LANES), f32)], axis=1)
    k.sums[...] = jnp.concatenate([*taps, rest, jnp.zeros((4, D), f32)], axis=0)

    ordered_t = jnp.transpose(k.ordered()[...].astype(f32)).astype(bf16)
    gwo = k.gwo()
    gw = k.gw

    def weights(j, carry):
        part = pl.ds(pl.multiple_of(j * HALF, HALF), HALF)
        gw[:, part] = mm(ordered_t, low[:, part])
        return carry

    lax.fori_loop(0, QKVG // HALF, weights, 0)
    gw[:, QKVG : QKVG + D] = gwo[...]
    gw[:, QKVG + D :] = mm(ordered_t, low[:, QKVG:])

    def halves(j, carry):
        here = pl.ds(pl.multiple_of(j * HALF, HALF), HALF)
        keep = pl.ds(pl.multiple_of(j * HALF + k.section * GROUP, HALF), HALF)
        send = pl.ds(pl.multiple_of(j * HALF + (1 - k.section) * GROUP, HALF), HALF)
        k.gw_keep[:, here] = gw[:, keep]
        k.gw_send[:, here] = gw[:, send].astype(bf16)
        return carry

    lax.fori_loop(0, GROUP // HALF, halves, 0)


def input_backward_body(k):
    flip = k.layer == 1
    wide = k.wide
    gmod, mixed_s, perm_s = k.gmod, k.mixed_s, k.perm_s
    gmod[...] = jnp.zeros(gmod.shape, f32)
    low, w_qk, w_vgd = k.low(), k.w_qk(), k.w_vgd()

    def inner_grad(i, carry):
        rows = pl.ds(pl.multiple_of(i * HALF, HALF), HALF)
        mixed_s[rows, :] = mm_t(low[rows, : 2 * D], w_qk[...]) + mm_t(
            low[rows, 2 * D :], w_vgd[...]
        )
        return carry

    lax.fori_loop(0, 2, inner_grad, 0)
    if flip:
        high, middle, rest = split_three(mixed_s[...])
        perm_s[:, :D] = high
        perm_s[:, D : 2 * D] = middle
        perm_s[:, 2 * D :] = rest
    x, mid_grad = k.x(), k.mid_grad()
    k.mods()

    def tile(i, carry):
        start = i * HALF
        rows = pl.ds(start, HALF)
        slot = k.slot(i)
        if flip:
            three = mm(order_matrix(start, HALF, wide, False), perm_s[...])
            grad = three[:, :D] + three[:, D : 2 * D] + three[:, 2 * D :]
        else:
            grad = mixed_s[rows, :]
        normal, rate = normalise(x[rows, :].astype(f32))
        where = (pl.ds(slot, 1), slice(0, D))
        gmod[where] = gmod[where] + jnp.sum(grad, axis=0, keepdims=True)
        where = (pl.ds(slot, 1), slice(D, 2 * D))
        gmod[where] = gmod[where] + jnp.sum(grad * normal, axis=0, keepdims=True)
        total = mid_grad[rows, :] + normalise_back(normal, rate, grad * (1.0 + k.share(slot, 1)))
        k.gx[rows, :] = total
        k.gx_low[rows, :] = total.astype(bf16)
        return carry

    for i in range(2):
        tile(i, 0)
    k.push("gx_low")
    k.push("gx")
    ffn, mixer = k.ffn_sums(), k.mixer_sums()
    k.mod_low[...] = jnp.concatenate([gmod[...], ffn[...]], axis=1).astype(bf16)
    if k.layer == 0:
        first = k.section == 0
        k.gx_send[...] = jnp.where(first, k.gx_two()[...], k.gx[...])
        one, two = k.mod_low[...].astype(f32), k.mod_two()[...].astype(f32)
        k.mod_mine[...] = jnp.where(first, one, two).astype(bf16)
        k.mod_send[...] = jnp.where(first, two, one).astype(bf16)
    half = 2 * D
    rest = ffn[0:1, :] + ffn[1:2, :]
    k.sums[...] = jnp.concatenate(
        [
            gmod[0:1, :] + gmod[1:2, :],
            rest[:, :half],
            rest[:, half:],
            ffn[2:3, :half],
            ffn[2:3, half:],
            jnp.concatenate([ffn[3:4, :D], mixer[0:1, :]], axis=1),
            jnp.concatenate([mixer[1:2, :], mixer[2:3, :]], axis=1),
            jnp.concatenate([mixer[3:4, :], jnp.zeros((1, D), f32)], axis=1),
        ],
        axis=0,
    )


ANY = pl.BlockSpec(memory_space=pl.ANY)
VMEM = pl.BlockSpec(memory_space=pltpu.VMEM)
HBM = pl.BlockSpec(memory_space=pltpu.HBM)


def call(body, layer, layouts, ins, outs, scratch, flops, packed=None, after=()):
    arrays = []
    counts = []
    kept = []
    places = []
    for kind, given, part in ins.values():
        places.extend([ANY] * 2 if kind == "own" else [HBM])
        given = given if kind == "own" else (given,)
        arrays.extend(given)
        counts.append(len(given))
        rows, wide = given[0].shape[-2:]
        start, stop = part or (0, wide)
        kept.append(pltpu.VMEM((rows, stop - start), given[0].dtype))

    def kernel(*refs):
        refs = list(refs)
        take = lambda count: [refs.pop(0) for _ in range(count)]
        (layouts_ref,) = take(1)
        sources = [take(count) for count in counts]
        take(len(after))
        targets = take(len(outs))
        buffers = take(len(ins))
        results = take(len(outs))
        rest = take(len(scratch))
        in_sems, out_sems = refs
        k = Kernel(layer, layouts_ref)
        k.packed = packed
        for number, (name, (kind, _, part)) in enumerate(ins.items()):
            given = sources[number]
            if part is not None:
                given = [ref.at[:, part[0] : part[1]] for ref in given]
            setattr(k, name, k.load(kind, given, buffers[number], in_sems.at[number]))
        k.results = {}
        for number, name in enumerate(outs):
            setattr(k, name, results[number])
            k.results[name] = (results[number], targets[number], out_sems.at[number])
        for name, ref in zip(scratch, rest):
            setattr(k, name, ref)
        body(k)
        k.finish()

    return pl.pallas_call(
        kernel,
        out_shape=[jax.ShapeDtypeStruct(shape, kind) for shape, kind, _ in outs.values()],
        in_specs=[pl.BlockSpec(memory_space=pltpu.SMEM)] + places + [ANY] * len(after),
        out_specs=[HBM if for_kernel else ANY for _, _, for_kernel in outs.values()],
        scratch_shapes=kept
        + [pltpu.VMEM(shape, kind) for shape, kind, _ in outs.values()]
        + [pltpu.VMEM(shape, kind) for shape, kind in scratch.values()]
        + [pltpu.SemaphoreType.DMA((len(ins),)), pltpu.SemaphoreType.DMA((len(outs),))],
        compiler_params=pltpu.CompilerParams(vmem_limit_bytes=28 * 1024 * 1024),
        cost_estimate=pl.CostEstimate(flops=flops, bytes_accessed=4 << 20, transcendentals=0),
    )(layouts, *arrays, *after)


def own(pair, part=None):
    return ("own", pair, part)


def plain(array):
    return ("plain", array, None)


def micro(array):
    return ("micro", array, None)


ADA_CUT = 9 * LANES
AT_QK = (0, 2 * D)
AT_ADA_A = (2 * D, 2 * D + ADA_CUT)
AT_VGD = (0, 2 * D + LANES)
AT_ADA_B = (2 * D + LANES, 8 * D + LANES - ADA_CUT)
AT_UP = (0, FF)
AT_OUT = (FF, FF + D)


def attn_forward(layer, layouts, x, mods, small, qka, vgda):
    return call(
        attn_forward_body,
        layer,
        layouts,
        dict(
            x=micro(x),
            mods=own(mods),
            w_qk=own(qka, AT_QK),
            w_vgd=own(vgda, AT_VGD),
            small=own(small),
        ),
        dict(
            ordered=((ROWS, D), bf16, True),
            qkvg=((ROWS, QKVG), f32, True),
            dp=((ROWS, LANES), f32, True),
            vc=((ROWS, D), f32, True),
            cum=((ROWS, LANES), f32, True),
            cumt=((LANES, ROWS), f32, True),
            o=((ROWS, D), f32, True),
            gated=((ROWS, D), bf16, True),
        ),
        dict(
            inner=((ROWS, D), bf16),
            vpad=((ROWS + 8, D), f32),
            bias=((HALF, ROWS), f32),
        ),
        8 * 10**9,
    )


def ffn_forward(layer, layouts, x, mods, small, gated, upo, down):
    return call(
        ffn_forward_body,
        layer,
        layouts,
        dict(
            gated=plain(gated),
            x=micro(x),
            wo=own(upo, AT_OUT),
            mods=own(mods),
            small=own(small),
            wu=own(upo, AT_UP),
            wn=own(down),
        ),
        dict(
            out=((ROWS, D), bf16, True),
            branch=((ROWS, D), f32, True),
            down=((ROWS, D), f32, True),
            **({"sent": ((ROWS, D), bf16, False)} if layer == 1 else {}),
        ),
        {},
        5 * 10**9,
    )


def ffn_backward(
    layer, layouts, x, mods, small, gated, branch, down_raw, grad, upo, down, devices, after=()
):
    shard = D // devices
    in_kernel = shard % 8 == 0
    if in_kernel:
        sums = dict(
            keep=((devices, shard, FF), f32, True),
            sent=((devices, shard, FF), bf16, False),
        )
    else:
        sums = dict(gwu=((D, FF), f32, False), gwn=((FF, D), f32, False))
    return call(
        ffn_backward_body,
        layer,
        layouts,
        dict(
            mods=own(mods),
            small=own(small),
            x=micro(x),
            grad=micro(grad),
            branch=plain(branch),
            down=plain(down_raw),
            wu=own(upo, AT_UP),
            wn=own(down),
            gated=plain(gated),
        ),
        dict(
            mid_grad=((ROWS, D), f32, True),
            branch_low=((ROWS, D), bf16, True),
            gwo=((D, D), f32, True),
            sums=((8, FF), f32, True),
            **sums,
        ),
        dict(
            **({"gwn": ((FF, D), f32)} if in_kernel else {}),
            hidden_s=((ROWS, FF), bf16),
            inner_s=((ROWS, D), bf16),
            up_s=((ROWS, FF), bf16),
            down_s=((ROWS, D), bf16),
            gmod=((8, FF), f32),
            gbu=((1, FF), f32),
            gbn=((1, D), f32),
        ),
        12 * 10**9,
        packed=in_kernel,
        after=after,
    )


def mixer_backward(layer, layouts, small, saved, branch_low, gwo, upo, after=()):
    ordered, qkvg, dp, vc, cum, cumt, o = saved
    return call(
        mixer_backward_body,
        layer,
        layouts,
        dict(
            branch_low=plain(branch_low),
            wo=own(upo, AT_OUT),
            qkvg=plain(qkvg),
            vc=plain(vc),
            cum=plain(cum),
            cumt=plain(cumt),
            o=plain(o),
            small=own(small),
            dp=plain(dp),
            ordered=plain(ordered),
            gwo=plain(gwo),
        ),
        dict(
            low=((ROWS, QKVG + LANES), bf16, True),
            gw_keep=((D, GROUP), f32, True),
            gw_send=((D, GROUP), bf16, False),
            sums=((8, D), f32, True),
        ),
        dict(
            mixed_s=((ROWS, D), f32),
            dv_s=((ROWS + 8, D), f32),
            rows_s=((ROWS, LANES), f32),
            cols_s=((LANES, ROWS), f32),
            bias=((HALF, ROWS), f32),
            gw=((D, 2 * GROUP), f32),
        ),
        15 * 10**9,
        after=after,
    )


def input_backward(
    layer, layouts, x, mods, low, mid_grad, ffn_sums, mixer_sums, qka, vgda, two=None, after=()
):
    extra_in, extra_out = {}, {}
    if two is not None:
        extra_in = dict(gx_two=plain(two[0]), mod_two=plain(two[1]))
        extra_out = dict(
            gx_send=((ROWS, D), f32, False),
            mod_mine=((8, 6 * D), bf16, False),
            mod_send=((8, 6 * D), bf16, False),
        )
    return call(
        input_backward_body,
        layer,
        layouts,
        dict(
            low=plain(low),
            w_qk=own(qka, AT_QK),
            w_vgd=own(vgda, AT_VGD),
            x=micro(x),
            mid_grad=plain(mid_grad),
            mods=own(mods),
            ffn_sums=plain(ffn_sums),
            mixer_sums=plain(mixer_sums),
            **extra_in,
        ),
        dict(
            gx=((ROWS, D), f32, True),
            gx_low=((ROWS, D), bf16, True),
            mod_low=((8, 6 * D), bf16, True),
            sums=((8, 2 * D), f32, False),
            **extra_out,
        ),
        dict(
            mixed_s=((ROWS, D), f32),
            perm_s=((ROWS, 3 * D), bf16),
            gmod=((8, 2 * D), f32),
        ),
        4 * 10**9,
        after=after,
    )


def small_kernel(b_up, b_down, taps, b_decay, packed):
    packed[...] = jnp.zeros(packed.shape, f32)
    packed[0:1, :] = b_up[...]
    packed[1:2, :D] = b_down[...]
    packed[2:5, :D] = taps[0]
    packed[5:6, :HEADS] = b_decay[...]


def pack_small(b_up, b_down, taps, b_decay):
    return pl.pallas_call(
        small_kernel,
        out_shape=jax.ShapeDtypeStruct((8, FF), f32),
        in_specs=[VMEM] * 4,
        out_specs=VMEM,
    )(b_up, b_down, taps, b_decay)


def pack_kernel(w_query, w_key, w_value, w_gate, w_out, w_decay, w_ada, w_up, qka, vgda, upo):
    qka[:, :D] = w_query[0]
    qka[:, D : 2 * D] = w_key[0]
    qka[:, 2 * D :] = w_ada[0, :, :ADA_CUT]
    vgda[:, :D] = w_value[0]
    vgda[:, D : 2 * D] = w_gate[0]
    place = jnp.where(row_iota(HEADS, LANES) == lane_iota(HEADS, LANES), 1.0, 0.0).astype(bf16)
    turned = lax.dot_general(
        w_decay[0], place, (((0,), (0,)), ((), ())), preferred_element_type=f32
    )
    vgda[:, 2 * D : 2 * D + LANES] = turned.astype(bf16)
    vgda[:, 2 * D + LANES :] = w_ada[0, :, ADA_CUT:]
    upo[:, :FF] = w_up[0]
    upo[:, FF:] = w_out[0]


def pack(*weights):
    shard = weights[0].shape[1]
    widths = (2 * D + ADA_CUT, 8 * D + LANES - ADA_CUT, FF + D)
    return pl.pallas_call(
        pack_kernel,
        out_shape=[jax.ShapeDtypeStruct((shard, width), bf16) for width in widths],
        in_specs=[VMEM] * len(weights),
        out_specs=[VMEM] * len(widths),
    )(*weights)


def join_kernel(bits, waits, *refs):
    count = len(bits)
    held, came, out = refs[:count], refs[count : 2 * count], refs[2 * count + waits :]
    for i, bit in enumerate(bits):
        mine = (lax.axis_index("row") >> bit) & 1
        out[i][:, mine] = held[i][...]
        out[i][:, 1 - mine] = came[i][...]


def join(held, came, bits, after=()):
    def parts(array, bit):
        axis = axis_of(bit)
        above = 1
        for size in array.shape[:axis]:
            above *= size
        return array.reshape((above, -1) + array.shape[-2:])

    split_held = [parts(array, bit) for array, bit in zip(held, bits)]
    split_came = [parts(array, bit) for array, bit in zip(came, bits)]
    out = pl.pallas_call(
        functools.partial(join_kernel, bits, len(after)),
        out_shape=[
            jax.ShapeDtypeStruct(array.shape[:1] + (2,) + array.shape[1:], array.dtype)
            for array in split_held
        ],
        in_specs=[VMEM] * (2 * len(held)) + [ANY] * len(after),
        out_specs=[VMEM] * len(held),
        compiler_params=pltpu.CompilerParams(vmem_limit_bytes=8 * 1024 * 1024),
        cost_estimate=pl.CostEstimate(flops=10**6, bytes_accessed=10**6, transcendentals=0),
    )(*split_held, *split_came, *after)
    joined = []
    for array, result, bit in zip(held, out, bits):
        shape = list(array.shape)
        shape[axis_of(bit)] = 2
        joined.append(result.reshape(shape))
    return joined


def mods_kernel(conditions, bias, packed, vgd, out, ada_a, ada_b, sems):
    copies = [
        pltpu.make_async_copy(packed.at[:, AT_ADA_A[0] : AT_ADA_A[1]], ada_a, sems.at[0]),
        pltpu.make_async_copy(vgd.at[:, AT_ADA_B[0] : AT_ADA_B[1]], ada_b, sems.at[1]),
    ]
    for copy in copies:
        copy.start()
    values = conditions[...].astype(f32)
    lifted = (values * sigmoid(values)).astype(bf16)
    for copy in copies:
        copy.wait()
    out[...] = jnp.concatenate([mm(lifted, ada_a[...]), mm(lifted, ada_b[...])], axis=1) + bias[...]


ADA_SCRATCH = [
    pltpu.VMEM((D, ADA_CUT), bf16),
    pltpu.VMEM((D, 6 * D - ADA_CUT), bf16),
    pltpu.SemaphoreType.DMA((2,)),
]


def modulations(conditions, bias, packed, vgd):
    return pl.pallas_call(
        mods_kernel,
        out_shape=jax.ShapeDtypeStruct((MICRO * SLOTS, 6 * D), f32),
        in_specs=[VMEM, VMEM, ANY, ANY],
        out_specs=VMEM,
        scratch_shapes=ADA_SCRATCH,
        compiler_params=pltpu.CompilerParams(vmem_limit_bytes=16 * 1024 * 1024),
        cost_estimate=pl.CostEstimate(flops=10**9, bytes_accessed=2 << 20, transcendentals=0),
    )(conditions, bias, packed, vgd)


def lifted_kernel(mine, came, packed, vgd, out, ada_a, ada_b, sems):
    copies = [
        pltpu.make_async_copy(packed.at[:, AT_ADA_A[0] : AT_ADA_A[1]], ada_a, sems.at[0]),
        pltpu.make_async_copy(vgd.at[:, AT_ADA_B[0] : AT_ADA_B[1]], ada_b, sems.at[1]),
    ]
    for copy in copies:
        copy.start()
    for copy in copies:
        copy.wait()
    first = lax.axis_index("section") == 0
    pair = mine[0:SLOTS, :].astype(f32), came[0:SLOTS, :].astype(f32)
    grad = jnp.concatenate(
        [jnp.where(first, pair[0], pair[1]), jnp.where(first, pair[1], pair[0])], axis=0
    ).astype(bf16)
    out[...] = mm_t(grad[:, :ADA_CUT], ada_a[...]) + mm_t(grad[:, ADA_CUT:], ada_b[...])


def lifted_grads(mine, came, packed, vgd):
    return pl.pallas_call(
        lifted_kernel,
        out_shape=jax.ShapeDtypeStruct((MICRO * SLOTS, D), f32),
        in_specs=[VMEM, VMEM, ANY, ANY],
        out_specs=VMEM,
        scratch_shapes=ADA_SCRATCH,
        compiler_params=pltpu.CompilerParams(vmem_limit_bytes=16 * 1024 * 1024),
        cost_estimate=pl.CostEstimate(flops=10**9, bytes_accessed=2 << 20, transcendentals=0),
    )(mine, came, packed, vgd)


def step_kernel(bit, widths, counts, waits, *refs):
    mine = (lax.axis_index("row") >> bit) & 1
    count, many = len(widths), len(counts)
    refs = list(refs)
    take = lambda number: [refs.pop(0) for _ in range(number)]
    sources = take(count + many)
    take(waits)
    targets = take(count + 1)
    buffers = take(count + many)
    results = take(count + 1)
    in_sems, out_sems = refs
    arrive = [
        pltpu.make_async_copy(source, buffer, in_sems.at[i])
        for i, (source, buffer) in enumerate(zip(sources, buffers))
    ]
    leave = [
        pltpu.make_async_copy(result, target, out_sems.at[i])
        for i, (result, target) in enumerate(zip(results, targets))
    ]
    for copy in arrive:
        copy.start()
    kept, came = buffers[:count], buffers[count:]
    places = [(j, i) for j, number in enumerate(counts) for i in range(number)]
    goes = results[count]
    at = 0
    for i in range(count):
        j, place = places[i]
        arrive[i].wait()
        if place == 0:
            arrive[count + j].wait()
        start = sum(widths[i - place : i])
        columns = slice(start, start + widths[i])
        total = kept[i][:, 1 - mine] + came[j][:, 1 - mine, :, :, columns].astype(f32)
        goes[:, :, :, at : at + widths[i]] = total.astype(bf16)
        at += widths[i]
    leave[count].start()
    for i in range(count):
        j, place = places[i]
        start = sum(widths[i - place : i])
        columns = slice(start, start + widths[i])
        results[i][...] = kept[i][:, mine] + came[j][:, mine, :, :, columns].astype(f32)
        leave[i].start()
    for copy in leave:
        copy.wait()


def step(kept, came, bit, below=1, after=()):
    blocks, rows = kept[0].shape[0] // 2, kept[0].shape[1]
    above = blocks // below
    paired = lambda array: array.reshape((above, 2, below) + array.shape[1:])
    widths = [array.shape[2] for array in kept]
    size = sum(array.size for array in kept)
    arrays = [paired(array) for array in kept] + [paired(array) for array, _ in came]
    shapes = [((above, below, rows, width), f32) for width in widths]
    shapes.append(((above, below, rows, sum(widths)), bf16))
    out = pl.pallas_call(
        functools.partial(step_kernel, bit, widths, [count for _, count in came], len(after)),
        out_shape=[jax.ShapeDtypeStruct(shape, kind) for shape, kind in shapes],
        in_specs=[HBM] * len(kept) + [ANY] * (len(came) + len(after)),
        out_specs=[HBM] * len(kept) + [ANY],
        scratch_shapes=[pltpu.VMEM(array.shape, array.dtype) for array in arrays]
        + [pltpu.VMEM(shape, kind) for shape, kind in shapes]
        + [pltpu.SemaphoreType.DMA((len(arrays),)), pltpu.SemaphoreType.DMA((len(shapes),))],
        compiler_params=pltpu.CompilerParams(vmem_limit_bytes=16 * 1024 * 1024),
        cost_estimate=pl.CostEstimate(flops=size, bytes_accessed=8 * size, transcendentals=0),
    )(*arrays, *after)
    count = len(kept)
    flat_blocks = [array.reshape((blocks,) + array.shape[2:]) for array in out]
    return flat_blocks[:count], flat_blocks[count]


def misc_step_kernel(held, arrived, out):
    size = held.shape[0] - SUMS
    out[:size, :] = held[:size, :]
    out[size : 2 * size, :] = arrived[:size, :]
    high, low = split(misc_sums(held, arrived))
    out[2 * size : 2 * size + SUMS // 2, :] = high
    out[2 * size + SUMS // 2 :, :] = low


def misc_step(held, arrived):
    return pl.pallas_call(
        misc_step_kernel,
        out_shape=jax.ShapeDtypeStruct((2 * held.shape[0] - SUMS, 2 * D), bf16),
        in_specs=[VMEM] * 2,
        out_specs=VMEM,
        cost_estimate=pl.CostEstimate(flops=10**5, bytes_accessed=10**5, transcendentals=0),
    )(held, arrived)


def misc_sums(*refs):
    size = refs[0].shape[0] - SUMS
    parts = [ref[size:, :].astype(f32) for ref in refs]
    return sum(part[: SUMS // 2] + part[SUMS // 2 :] for part in parts)


SUMS = 32


def misc_rows(conditions, mod_low):
    values = conditions[...].astype(f32)
    values = jnp.where(lax.axis_index("section") == 0, values[:SLOTS], values[SLOTS:])
    lifted = (values * sigmoid(values)).astype(bf16).astype(f32)
    rows = [
        mod_low[slot : slot + 1, i * 2 * D : (i + 1) * 2 * D].astype(f32)
        for slot in range(SLOTS)
        for i in range(3)
    ]
    rows.append(jnp.concatenate([lifted[0:1], lifted[1:2]], axis=1))
    rows.append(jnp.zeros((1, 2 * D), f32))
    return jnp.concatenate(rows, axis=0)


def misc_kernel(conditions, mod_low, *refs):
    out = refs[-1]
    rows = [misc_rows(conditions, mod_low)]
    if len(refs) == 3:
        rows.extend(part.astype(f32) for part in split(jnp.concatenate([refs[0][...], refs[1][...]], axis=0)))
    out[...] = jnp.concatenate(rows, axis=0).astype(bf16)


def pack_misc(conditions, mod_low, *sums):
    return pl.pallas_call(
        misc_kernel,
        out_shape=jax.ShapeDtypeStruct((8 + (SUMS if sums else 0), 2 * D), bf16),
        in_specs=[VMEM] * (2 + len(sums)),
        out_specs=VMEM,
    )(conditions, mod_low, *sums)


def grow_kernel(held, came, out):
    size = held.shape[0]
    out[:size, :] = held[...]
    out[size:, :] = came[...]


def grow(held, came):
    return pl.pallas_call(
        grow_kernel,
        out_shape=jax.ShapeDtypeStruct((2 * held.shape[0], held.shape[1]), held.dtype),
        in_specs=[VMEM] * 2,
        out_specs=VMEM,
        cost_estimate=pl.CostEstimate(flops=10**5, bytes_accessed=10**5, transcendentals=0),
    )(held, came)


def finish_kernel(widths, counts, *refs):
    count = len(widths)
    kept, refs = refs[:count], refs[count:]
    came, refs = refs[: len(counts)], refs[len(counts) :]
    lifted, mod_two, misc, misc_came, mine, other, small_mine, small_other = refs
    places = [(ref, i) for ref, many in zip(came, counts) for i in range(many)]
    added = []
    for i in range(count):
        ref, place = places[i]
        start = sum(widths[i - place : i])
        added.append(kept[i][0] + ref[0, :, start : start + widths[i]].astype(f32))
    a1, f1, f2, a2 = added
    size = misc.shape[0] - SUMS
    mod_one = jnp.concatenate([misc[:size, :], misc_came[:size, :]], axis=0)

    def ada(rows):
        rows = rows.astype(f32).reshape(-1, 8, 2 * D)
        columns = []
        for i in range(3):
            both = [rows[:, 3 * slot + i, :] for slot in range(SLOTS)]
            columns.append(mm(lifted[...], jnp.concatenate(both, axis=0).astype(bf16)))
        return jnp.concatenate(columns, axis=1)

    first = lax.axis_index("section") == 0
    at = 0
    for one, two in ((a1, a2), (f1, f2), (ada(mod_one), ada(mod_two[...]))):
        columns = slice(at, at + one.shape[1])
        mine[:, columns] = jnp.where(first, one, two)
        other[:, columns] = jnp.where(first, two, one)
        at += one.shape[1]
    total = misc_sums(misc, misc_came)
    one, two = total[0:8, :], total[8:16, :]
    small_mine[...] = jnp.where(first, one, two)
    small_other[...] = jnp.where(first, two, one)


def finish(kept, came, lifted, mod_two, misc, misc_came):
    widths = [array.shape[2] for array in kept]
    shard = kept[0].shape[1]
    wide = GROUP + FF + 6 * D
    arrays = [array for array, _ in came]
    shapes = [(shard, wide)] * 2 + [(8, 2 * D)] * 2
    return pl.pallas_call(
        functools.partial(finish_kernel, widths, [count for _, count in came]),
        out_shape=[jax.ShapeDtypeStruct(shape, f32) for shape in shapes],
        in_specs=[VMEM] * (len(kept) + len(came) + 4),
        out_specs=[VMEM] * 4,
        compiler_params=pltpu.CompilerParams(vmem_limit_bytes=8 * 1024 * 1024),
    )(*kept, *arrays, lifted, mod_two, misc, misc_came)


def output_kernel(mine, other, small_mine, small_other, *outs):
    first = lax.axis_index("section") == 0

    def halves(start, width):
        columns = slice(start, start + width)
        pair = mine[:, columns], other[:, columns]
        return jnp.where(first, pair[0], pair[1]), jnp.where(first, pair[1], pair[0])

    attn = halves(0, GROUP)
    cut = GROUP - 2 * D
    outs[0][...] = attn[0][:, :D]
    outs[1][...] = attn[0][:, D : 2 * D]
    outs[2][:, :cut] = attn[0][:, 2 * D :]
    outs[2][:, cut:] = attn[1][:, : D - cut]
    outs[3][...] = attn[1][:, D - cut : 2 * D - cut]
    outs[4][...] = attn[1][:, 2 * D - cut : 3 * D - cut]
    decay = jnp.transpose(attn[1][:, 3 * D - cut :])
    for head in range(HEADS):
        outs[5][head] = decay[head : head + 1, :]
    up = halves(GROUP, FF // 2)
    outs[6][:, : FF // 2] = up[0]
    outs[6][:, FF // 2 :] = up[1]
    for piece in range(2):
        down = halves(GROUP + FF // 2 + piece * D, D)
        outs[7][piece] = down[0]
        outs[7][2 + piece] = down[1]
    outs[8][...] = mine[:, GROUP + FF :] + other[:, GROUP + FF :]
    small = small_mine[...] + small_other[...]
    half = 2 * D
    for i in range(3):
        outs[9][:, i * half : (i + 1) * half] = small[i : i + 1, :]
    for i in range(2):
        outs[10][:, i * half : (i + 1) * half] = small[3 + i : 4 + i, :]
    outs[11][...] = small[5:6, :D]
    outs[12][0] = small[5:6, D:]
    outs[12][1] = small[6:7, :D]
    outs[12][2] = small[6:7, D:]
    outs[13][...] = small[7:8, :HEADS]


def outputs(mine, other, small_mine, small_other):
    shard = mine.shape[0]
    shapes = (
        [(shard, D)] * 5
        + [(HEADS, 1, shard), (shard, FF), (4, shard, D), (shard, 6 * D)]
        + [(1, 6 * D), (1, FF), (1, D), (3, 1, D), (1, HEADS)]
    )
    return pl.pallas_call(
        output_kernel,
        out_shape=[jax.ShapeDtypeStruct(shape, f32) for shape in shapes],
        in_specs=[VMEM] * 4,
        out_specs=[VMEM] * len(shapes),
    )(mine, other, small_mine, small_other)


def both_kernel(one, two, came, out, kept, sems):
    section = lax.axis_index("section")

    def move(mine, layer):
        arrive = [
            pltpu.make_async_copy(mine, kept.at[layer], sems.at[0]),
            pltpu.make_async_copy(came, kept.at[1 - layer], sems.at[1]),
        ]
        leave = [
            pltpu.make_async_copy(kept.at[layer], out.at[layer], sems.at[2]),
            pltpu.make_async_copy(kept.at[1 - layer], out.at[1 - layer], sems.at[3]),
        ]
        for copy in arrive:
            copy.start()
        for copy, after in zip(arrive, leave):
            copy.wait()
            after.start()
        for copy in leave:
            copy.wait()

    @pl.when(section == 0)
    def _():
        move(one, 0)

    @pl.when(section == 1)
    def _():
        move(two, 1)


def both_micros(one, two, came):
    return pl.pallas_call(
        both_kernel,
        out_shape=jax.ShapeDtypeStruct((MICRO,) + one.shape, one.dtype),
        in_specs=[ANY] * 3,
        out_specs=ANY,
        scratch_shapes=[
            pltpu.VMEM((MICRO,) + one.shape, one.dtype),
            pltpu.SemaphoreType.DMA((4,)),
        ],
    )(one, two, came)


def swap(values):
    return lax.ppermute(values, "section", [(0, 1), (1, 0)])


def row_bits():
    bits = lax.axis_size("row").bit_length() - 1
    third = bits // 3
    return (
        tuple(range(third)),
        tuple(range(third, 2 * third)),
        tuple(range(2 * third, bits)),
    )


def partner(values, bit):
    size = lax.axis_size("row")
    return lax.ppermute(values, "row", [(i, i ^ (1 << bit)) for i in range(size)])


def axis_of(bit):
    return lax.axis_size("row").bit_length() - 2 - bit


def bit_of(bit):
    return (lax.axis_index("row") >> bit) & 1


def single(values):
    return values.reshape((1,) * (lax.axis_size("row").bit_length() - 1) + values.shape)


def gather_steps(along_x, along_y, along_z):
    steps = [(bit, bit) for bit in reversed(along_z)]
    return steps + list(zip(along_x + along_y, along_y + along_x))


def flat(held):
    return held.reshape(-1, held.shape[-1])


def on_device(
    tokens, conditions, output_grad, layouts,
    w_ada, b_ada, w_query, w_key, w_value, w_gate, w_out, w_decay, b_decay, conv_kernel,
    w_up, b_up, w_down, b_down,
):
    section = lax.axis_index("section")
    devices = lax.axis_size("row")
    shard = w_query.shape[1]
    along_x, along_y, along_z = row_bits()

    def both(values):
        return values, swap(values)

    qka, vgda, upo = pack(
        w_query, w_key, w_value, w_gate, w_out, w_decay.transpose(0, 2, 1), w_ada, w_up
    )
    small = pack_small(b_up, b_down, conv_kernel, b_decay)
    steps = gather_steps(along_x, along_y, along_z)
    lag = len(along_z)
    groups = [[single(qka), single(vgda)], [single(upo), single(w_down[0])]]
    after = (small,)
    for place in range(len(steps) + lag):
        numbers = [g for g in range(2) if 0 <= place - g * lag < len(steps)]
        bits = [bit for g in numbers for bit in steps[place - g * lag]]
        held = [array for g in numbers for array in groups[g]]
        came = [partner(array, bit) for array, bit in zip(held, bits)]
        if place == len(steps) + lag - 1:
            after = (gated,)
        held = join(held, came, bits, after)
        after = ()
        for g in numbers:
            groups[g], held = held[:2], held[2:]
        if place == len(steps) - 1:
            qka, vgda = [both(flat(array)) for array in groups[0]]
            conds = conditions.reshape(MICRO * SLOTS, D)
            mods = both(modulations(conds, b_ada, qka[0], vgda[0]))
            smalls = both(small)
            x = tokens
            *saved, gated = attn_forward(0, layouts, x, mods, smalls, qka, vgda)
    upo, down = [both(flat(array)) for array in groups[1]]
    kept = []
    acts = []
    for l in range(2):
        if l:
            *saved, gated = attn_forward(l, layouts, x, mods, smalls, qka, vgda)
        out, branch, down_raw, *acts_sent = ffn_forward(
            l, layouts, x, mods, smalls, gated, upo, down
        )
        kept.append((x, saved, gated, branch, down_raw))
        acts.append(out)
        x = out[None]

    def ffn_step(l, grad, after=()):
        x, saved, gated, branch, down_raw = kept[l]
        mid_grad, branch_low, gwo, sums, *terms = ffn_backward(
            l, layouts, x, mods, smalls, gated, branch, down_raw, grad, upo, down, devices, after
        )
        if terms[0].ndim == 2:
            up_sum = terms[0].reshape(devices, shard, 2, FF // 2)
            down_sum = terms[1].reshape(devices, 2, 2, shard, D)
            terms = []
            for own in (section, 1 - section):
                up_half = lax.dynamic_index_in_dim(up_sum, own, 2, keepdims=False)
                down_half = lax.dynamic_index_in_dim(down_sum, own, 1, keepdims=False)
                terms.append(
                    jnp.concatenate([up_half, down_half[:, 0], down_half[:, 1]], axis=2)
                )
            terms[1] = terms[1].astype(bf16)
        return [branch_low, gwo], mid_grad, terms[0], terms[1], sums

    def mixer_step(l, carried, after=()):
        low, keep, sent, sums = mixer_backward(
            l, layouts, smalls, kept[l][1], *carried, upo, after
        )
        by_row = lambda array: array.reshape(devices, shard, GROUP)
        return low, by_row(keep), by_row(sent), sums

    def input_step(l, low, mid_grad, ffn_sums, mixer_sums, two=None, after=()):
        x = kept[l][0]
        return input_backward(
            l, layouts, x, mods, low, mid_grad, ffn_sums, mixer_sums, qka, vgda, two, after
        )

    def run(keep, came, bits, below=1, after=()):
        for bit in bits[:-1]:
            keep, sent = step(keep, came, bit, below, after)
            came = [(partner(sent, bit), len(keep))]
        return step(keep, came, bits[-1], below, after)

    def grown(mod, bits):
        for bit in bits:
            mod = grow(mod, partner(mod, bit))
        return mod

    x_bits, y_bits, z_bits = along_x, along_y, along_z
    carried, mid_grad, f2_keep, f2_sent, f2_sums = ffn_step(1, output_grad)
    f2_came = swap(f2_sent)
    acts_came = swap(acts_sent[0])
    low, a2_keep, a2_sent, m2_sums = mixer_step(1, carried)
    a2_came = swap(a2_sent)
    gx_two, grad, mod_low_two, sums_two = input_step(
        1, low, mid_grad, f2_sums, m2_sums, after=(f2_came, acts_came)
    )
    mod_two = pack_misc(conds, mod_low_two)
    f2_keep, f2_sent = run([f2_keep], [(f2_came, 1)], x_bits)
    a2_keep, a2_sent = run([a2_keep], [(a2_came, 1)], y_bits, 1 << len(x_bits))
    mod_two = grown(mod_two, x_bits[:-1])
    after = (f2_sent, a2_sent, mod_two)
    f2_came = partner(f2_sent, x_bits[-1])
    mod_came = partner(mod_two, x_bits[-1])
    a2_came = partner(a2_sent, y_bits[-1])

    carried, mid_grad, f1_keep, f1_sent, f1_sums = ffn_step(0, grad[None], after)
    f1_came = swap(f1_sent)
    mod_two = grow(mod_two, mod_came)
    f2_keep, f2_sent = run(f2_keep, [(f2_came, 1)], y_bits)
    a2_keep, a2_sent = run(a2_keep, [(a2_came, 1)], x_bits)
    mod_two = grown(mod_two, y_bits[:-1])
    f1_keep, f1_sent = run([f1_keep], [(f1_came, 1)], x_bits)
    after = (f1_sent, a2_sent, f2_sent, mod_two)
    f1_came = partner(f1_sent, x_bits[-1])
    a2_came = partner(a2_sent, x_bits[-1])
    f2_came = partner(f2_sent, y_bits[-1])
    mod_came = partner(mod_two, y_bits[-1])
    low, a1_keep, a1_sent, m1_sums = mixer_step(0, carried, after)
    a1_came = swap(a1_sent)
    acts_out = both_micros(acts[0], acts[1], acts_came)
    mod_two = grow(mod_two, mod_came)
    two_keep, two_sent = run(f2_keep + a2_keep, [(f2_came, 1), (a2_came, 1)], z_bits[:1])
    f1_keep, f1_sent = run(f1_keep, [(f1_came, 1)], y_bits)
    a1_keep, a1_sent = run([a1_keep], [(a1_came, 1)], x_bits)
    after = (two_sent, mod_two, f1_sent, a1_sent, acts_out)
    a1_came = partner(a1_sent, x_bits[-1])
    f1_came = partner(f1_sent, y_bits[-1])
    two_came = partner(two_sent, z_bits[0])
    mod_came = partner(mod_two, z_bits[0])
    gx_one, _, mod_low_one, sums_one, gx_sent, mod_mine, mod_sent = input_step(
        0, low, mid_grad, f1_sums, m1_sums, (gx_two, mod_low_two), after
    )

    misc = pack_misc(conds, mod_low_one, sums_one, sums_two)
    a1_keep, a1_sent = run(a1_keep, [(a1_came, 1)], y_bits)
    a1_came = partner(a1_sent, y_bits[-1])
    for bit in x_bits + y_bits:
        misc = misc_step(misc, partner(misc, bit))
    mod_two = grown(grow(mod_two, mod_came), z_bits[1:-1])
    two_keep, two_sent = run(two_keep, [(two_came, 2)], z_bits[1:])
    two_came = partner(two_sent, z_bits[-1])
    mod_two = grow(mod_two, partner(mod_two, z_bits[-1]))
    gx_came = swap(gx_sent)
    mod_came = swap(mod_sent)
    gx_out = both_micros(gx_one, gx_two, gx_came)
    grad_lifted = lifted_grads(mod_mine, mod_came, qka[0], vgda[0])
    lifted_came = swap(grad_lifted)
    keep, came = a1_keep + f1_keep, [(a1_came, 1), (f1_came, 1)]
    for bit in z_bits:
        after = (misc,)
        if bit == z_bits[-1]:
            after = (misc, gx_out, lifted_came, mod_two)
        keep, sent = step(keep, came, bit, after=after)
        came = [(partner(sent, bit), len(keep))]
        misc_came = partner(misc, bit)
        if bit != z_bits[-1]:
            misc = misc_step(misc, misc_came)
    pair = (misc, misc_came)
    lifted = mod_two.reshape(devices, 8, SLOTS, D)[:, 6]
    lifted = lax.dynamic_slice_in_dim(lifted, lax.axis_index("row") * shard, shard, 2)
    lifted = lifted.transpose(2, 1, 0).reshape(shard, SLOTS * devices)
    mine, other, small_mine, small_other = finish(
        keep + two_keep, came + [(two_came, 2)], lifted, mod_two, *pair
    )
    came, small_came = swap(other), swap(small_other)
    (
        g_query, g_key, g_value, g_gate, g_out, g_decay, g_up, g_down, g_ada,
        g_b_ada, g_b_up, g_b_down, g_conv, g_b_decay,
    ) = outputs(mine, came, small_mine, small_came)

    grad_lifted = (grad_lifted + lifted_came).reshape(MICRO, SLOTS, D)
    _, pull_silu = jax.vjp(jax.nn.silu, conditions.astype(f32))
    (cond_grads,) = pull_silu(grad_lifted)

    return (
        acts_out[None],
        gx_out[None],
        cond_grads,
        g_ada[None],
        g_b_ada,
        g_query[None],
        g_key[None],
        g_value[None],
        g_gate[None],
        g_out[None],
        g_decay.transpose(1, 2, 0),
        g_b_decay,
        g_conv.transpose(1, 0, 2),
        g_up[None],
        g_b_up,
        g_down.reshape(1, FF // devices, D),
        g_b_down,
    )


def solution(mesh):
    rows = P(None, "row", None)
    mats = P("section", "row", None)
    vector = P("section", None)
    in_specs = (
        rows, rows, rows, P(None, "row"),
        mats, vector, mats, mats, mats, mats, mats, mats, vector, P("section", None, None),
        mats, vector, mats, vector,
    )
    blocks = P("section", None, "row", None)
    out_specs = (
        blocks, blocks, rows,
        mats, vector, mats, mats, mats, mats, mats, mats, vector, P("section", None, None),
        mats, vector, mats, vector,
    )
    return jax.shard_map(
        on_device, mesh=mesh, in_specs=in_specs, out_specs=out_specs, check_vma=False
    )
```

```python
import functools

import jax
import jax.numpy as jnp
from jax import lax
from jax.experimental import pallas as pl
from jax.experimental.pallas import tpu as pltpu
from jax.sharding import PartitionSpec as P

D = 384
HEADS = 6
HEAD_DIM = 64
FF = 1536
MICRO = 2
ROWS = 512
HALF = 256
SLOTS = 2
PAIR = 128
PAIRS = D // PAIR
QKVG = 4 * D
LANES = 128
GROUP = (QKVG + D + LANES) // 2
NEG = -1e30
SCALE = HEAD_DIM**-0.5

bf16 = jnp.bfloat16
f32 = jnp.float32


def mm(left, right):
    return jnp.dot(left, right, preferred_element_type=f32)


def mm_t(left, right):
    return lax.dot_general(left, right, (((1,), (1,)), ((), ())), preferred_element_type=f32)


def split(values):
    high = values.astype(bf16)
    return high, (values - high.astype(f32)).astype(bf16)


def split_three(values):
    high, rest = split(values)
    mid = values - high.astype(f32)
    middle, low = split(mid)
    return high, middle, low


def cat_left(values):
    high, low = split(values)
    return jnp.concatenate([high, low, high], axis=1)


def cat_right(values):
    high, low = split(values)
    return jnp.concatenate([high, high, low], axis=1)


def mm_near(left, right_pair, right_high):
    high, low = split(left)
    wide = mm(high, right_pair)
    return wide[:, :PAIR] + wide[:, PAIR:] + mm(low, right_high)


def lane_iota(rows, columns):
    return lax.broadcasted_iota(jnp.int32, (rows, columns), 1)


def row_iota(rows, columns):
    return lax.broadcasted_iota(jnp.int32, (rows, columns), 0)


def order_matrix(start, rows, wide, to_scan):
    t = row_iota(rows, ROWS) + start
    small = (t & 256) + ((t & 15) << 4) + ((t & 255) >> 4)
    if to_scan:
        large = ((t & 15) << 5) + (t >> 4)
    else:
        large = ((t & 31) << 4) + (t >> 5)
    source = jnp.where(wide, large, small)
    return jnp.where(lane_iota(rows, ROWS) == source, 1.0, 0.0).astype(bf16)


def normalise(values):
    centred = values - jnp.mean(values, axis=-1, keepdims=True)
    rate = lax.rsqrt(jnp.mean(centred * centred, axis=-1, keepdims=True) + 1e-06)
    return centred * rate, rate


def normalise_back(normal, rate, grad):
    return rate * (
        grad
        - jnp.mean(grad, axis=-1, keepdims=True)
        - normal * jnp.mean(grad * normal, axis=-1, keepdims=True)
    )


class In:
    def __init__(self, copy, kept):
        self.copy = copy
        self.kept = kept

    def __call__(self):
        if self.copy is not None:
            self.copy.wait()
            self.copy = None
        return self.kept


class Kernel:
    def __init__(self, layer, layouts):
        self.layer = layer
        self.section = lax.axis_index("section")
        self.own = self.section == layer
        self.layout = layouts[self.section, 0]
        self.wide = self.layout == 0
        self.live_rows = jnp.where(self.wide, ROWS, self.layout * HALF)
        self.pushed = {}

    def load(self, kind, refs, kept, sem):
        if kind == "own":
            mine, other = refs

            @pl.when(self.own)
            def _():
                pltpu.make_async_copy(mine, kept, sem).start()

            @pl.when(jnp.logical_not(self.own))
            def _():
                pltpu.make_async_copy(other, kept, sem).start()

            return In(pltpu.make_async_copy(mine, kept, sem), kept)
        (source,) = refs
        if kind == "micro":
            source = source.at[self.section if source.shape[0] == MICRO else 0]
        copy = pltpu.make_async_copy(source, kept, sem)
        copy.start()
        return In(copy, kept)

    def push(self, name):
        kept, target, sem = self.results[name]
        copy = pltpu.make_async_copy(kept, target, sem)
        copy.start()
        self.pushed[name] = copy

    def finish(self):
        for name in self.results:
            if name not in self.pushed:
                self.push(name)
        for copy in self.pushed.values():
            copy.wait()

    def slot(self, half):
        return jnp.where(self.wide, 0, half)

    def share(self, slot, part):
        row = pl.ds(2 * self.section + slot, 1)
        return self.mods()[row, part * D : (part + 1) * D]

    def bu(self):
        return self.small()[0:1, :]

    def bn(self):
        return self.small()[1:2, :D]

    def ck(self, tap):
        return self.small()[2 + tap : 3 + tap, :D]

    def bd(self):
        return self.small()[5:6, :LANES]


def sigmoid(values):
    return 1.0 / (1.0 + jnp.exp(-values))


GELU_A = 0.7978845608028654
GELU_B = 0.044715


def gelu_parts(values):
    square = values * values
    tanh = jnp.tanh(GELU_A * values * (1.0 + GELU_B * square))
    return square, tanh


def fill_bias(bias, wide):
    bias[:, :HALF] = jnp.full((HALF, HALF), 0.0, f32) + jnp.where(wide, 0.0, NEG)
    causal = row_iota(HALF, HALF) >= lane_iota(HALF, HALF)
    bias[:, HALF:] = jnp.where(causal, 0.0, NEG)


def decay_factors(cum, cumt, bias, head):
    row = cumt[pl.ds(head, 1), :]
    lanes = lane_iota(1, LANES)
    column = jnp.sum(jnp.where(lanes == head, cum[...], 0.0), axis=1, keepdims=True)
    first = jnp.exp(column[:HALF] - row[:, :HALF] + bias[:, HALF:])
    second = jnp.exp(column[HALF:] - row + bias[...])
    return first, second


def head_norm(values, lanes):
    square = values * values
    low = jnp.sum(jnp.where(lanes < HEAD_DIM, square, 0.0), axis=1, keepdims=True)
    high = jnp.sum(jnp.where(lanes < HEAD_DIM, 0.0, square), axis=1, keepdims=True)
    return jnp.where(lanes < HEAD_DIM, low, high) * (1.0 / HEAD_DIM)


def fill_decay(dp, bd, cum, cumt):
    raw = dp[...] + bd
    log_decay = (jnp.minimum(raw, 0.0) - jnp.log1p(jnp.exp(-jnp.abs(raw)))) * (1.0 / 16.0)
    high, middle, low = split_three(log_decay)
    causal = jnp.where(row_iota(ROWS, ROWS) >= lane_iota(ROWS, ROWS), 1.0, 0.0).astype(bf16)
    cum[...] = mm(causal, high) + mm(causal, middle) + mm(causal, low)
    cumt[...] = jnp.transpose(cum[...])


def columns(index, first=0):
    return slice(index * PAIR + first, index * PAIR + first + PAIR)


def attn_forward_body(k):
    flip = k.layer == 1
    wide = k.wide
    x = k.x()
    k.mods()

    def first(i, carry):
        rows = pl.ds(pl.multiple_of(i * HALF, HALF), HALF)
        slot = k.slot(i)
        normal, _ = normalise(x[rows, :].astype(f32))
        k.inner[rows, :] = (normal * (1.0 + k.share(slot, 1)) + k.share(slot, 0)).astype(bf16)
        return carry

    lax.fori_loop(0, 2, first, 0)
    w_qk = k.w_qk()
    w_vgd = k.w_vgd()

    def project(i, carry):
        start = i * HALF
        rows = pl.ds(start, HALF)
        if flip:
            part = mm(order_matrix(start, HALF, wide, True), k.inner[...]).astype(bf16)
        else:
            part = k.inner[rows, :]
        k.ordered[rows, :] = part
        k.qkvg[rows, : 2 * D] = mm(part, w_qk[...])
        k.qkvg[rows, 2 * D :] = mm(part, w_vgd[:, : 2 * D])
        k.dp[rows, :] = mm(part, w_vgd[:, 2 * D :])
        return carry

    lax.fori_loop(0, 2, project, 0)
    k.small()
    for name in ("ordered", "qkvg", "dp"):
        k.push(name)
    fill_decay(k.dp, k.bd(), k.cum, k.cumt)
    fill_bias(k.bias, wide)

    vpad = k.vpad
    vpad[0:8, :] = jnp.zeros((8, D), f32)
    vpad[8 : 8 + ROWS, :] = k.qkvg[:, 2 * D : 3 * D]
    position = row_iota(ROWS, 1) & jnp.where(wide, ROWS - 1, HALF - 1)
    one = jnp.where(position >= 1, vpad[7 : 7 + ROWS, :], 0.0)
    two = jnp.where(position >= 2, vpad[6 : 6 + ROWS, :], 0.0)
    k.vc[...] = k.ck(0) * vpad[8 : 8 + ROWS, :] + k.ck(1) * one + k.ck(2) * two
    for name in ("cum", "cumt", "vc"):
        k.push(name)

    def pair(p, carry):
        lanes = lane_iota(1, PAIR)
        queries = cat_left(k.qkvg[:, columns(p)] * SCALE)
        keys = k.qkvg[:, columns(p, D)]
        value_high, value_low = split(k.vc[:, columns(p)])
        values = jnp.concatenate([value_high, value_low], axis=1)
        parts = []
        for e in range(2):
            key_cat = cat_right(jnp.where((lanes // HEAD_DIM) == e, keys, 0.0))
            first, second = decay_factors(k.cum, k.cumt, k.bias, 2 * p + e)
            first = first * mm_t(queries[:HALF], key_cat[:HALF])
            second = second * mm_t(queries[HALF:], key_cat)
            parts.append(
                jnp.concatenate(
                    [
                        mm_near(first, values[:HALF], value_high[:HALF]),
                        mm_near(second, values, value_high),
                    ],
                    axis=0,
                )
            )
        total = jnp.where(lanes < HEAD_DIM, parts[0], parts[1])
        k.o[:, columns(p)] = total
        gate = k.qkvg[:, columns(p, 3 * D)]
        normed = total * lax.rsqrt(head_norm(total, lanes) + 1.0)
        mixed = (normed * (gate * sigmoid(gate))).astype(bf16)
        if flip:
            k.inner[:, columns(p)] = mixed
        else:
            k.gated[:, columns(p)] = mixed
        return carry

    for p in range(PAIRS):
        pair(p, 0)
    k.push("o")
    if flip:

        def back(i, carry):
            start = i * HALF
            k.gated[pl.ds(start, HALF), :] = mm(
                order_matrix(start, HALF, wide, False), k.inner[...]
            ).astype(bf16)
            return carry

        lax.fori_loop(0, 2, back, 0)


def ffn_forward_body(k):
    gated, x = k.gated(), k.x()
    k.mods(), k.small()

    def tile(i, carry):
        start = i * HALF
        rows = pl.ds(start, HALF)
        slot = k.slot(i)
        grown = mm(gated[rows, :], k.wo()[...])
        k.branch[rows, :] = grown
        middle = x[rows, :].astype(f32) + k.share(slot, 2) * grown
        normal, _ = normalise(middle)
        inner = (normal * (1.0 + k.share(slot, 4)) + k.share(slot, 3)).astype(bf16)
        up = mm(inner, k.wu()[...]) + k.bu()
        _, tanh = gelu_parts(up)
        hidden = (0.5 * up * (1.0 + tanh)).astype(bf16)
        low = mm(hidden, k.wn()[...])
        k.down[rows, :] = low
        result = middle + k.share(slot, 5) * (low + k.bn())
        live = (row_iota(HALF, 1) + start) < k.live_rows
        k.out[rows, :] = jnp.where(live, result, 0.0).astype(bf16)
        return carry

    for i in range(2):
        tile(i, 0)
    if k.layer == 1:
        k.sent[...] = jnp.where(k.section == 0, k.out[...].astype(f32), x[...].astype(f32)).astype(bf16)


def ffn_backward_body(k):
    gmod, gbu, gbn = k.gmod, k.gbu, k.gbn
    gmod[...] = jnp.zeros(gmod.shape, f32)
    gbu[...] = jnp.zeros(gbu.shape, f32)
    gbn[...] = jnp.zeros(gbn.shape, f32)
    k.mods(), k.small()
    x, grad, branch, down = k.x(), k.grad(), k.branch(), k.down()

    def tile(i, carry):
        start = i * HALF
        rows = pl.ds(start, HALF)
        slot = k.slot(i)

        def add(part, values):
            where = (pl.ds(slot, 1), slice((part - 2) * D, (part - 1) * D))
            gmod[where] = gmod[where] + jnp.sum(values, axis=0, keepdims=True)

        grown = branch[rows, :]
        middle = x[rows, :].astype(f32) + k.share(slot, 2) * grown
        normal, rate = normalise(middle)
        inner = (normal * (1.0 + k.share(slot, 4)) + k.share(slot, 3)).astype(bf16)
        k.inner_s[rows, :] = inner
        live = (row_iota(HALF, 1) + start) < k.live_rows
        above = jnp.where(live, grad[rows, :].astype(f32), 0.0)
        add(5, above * (down[rows, :] + k.bn()))
        grad_down = above * k.share(slot, 5)
        gbn[...] = gbn[...] + jnp.sum(grad_down, axis=0, keepdims=True)
        down_low = grad_down.astype(bf16)
        k.down_s[rows, :] = down_low
        up = mm(inner, k.wu()[...]) + k.bu()
        square, tanh = gelu_parts(up)
        half = 0.5 * (1.0 + tanh)
        k.hidden_s[rows, :] = (up * half).astype(bf16)
        slope = half + 0.5 * up * (1.0 - tanh * tanh) * (
            GELU_A * (1.0 + 3.0 * GELU_B * square)
        )
        grad_up = mm_t(down_low, k.wn()[...]) * slope
        gbu[...] = gbu[...] + jnp.sum(grad_up, axis=0, keepdims=True)
        up_low = grad_up.astype(bf16)
        k.up_s[rows, :] = up_low
        grad_inner = mm_t(up_low, k.wu()[...])
        add(3, grad_inner)
        add(4, grad_inner * normal)
        grad_middle = above + normalise_back(
            normal, rate, grad_inner * (1.0 + k.share(slot, 4))
        )
        k.mid_grad[rows, :] = grad_middle
        add(2, grad_middle * grown)
        k.branch_low[rows, :] = (grad_middle * k.share(slot, 2)).astype(bf16)
        return carry

    for i in range(2):
        tile(i, 0)
    k.push("mid_grad")
    k.push("branch_low")

    def weights(j, carry):
        part = pl.ds(pl.multiple_of(j * HALF, HALF), HALF)
        hidden_t = jnp.transpose(k.hidden_s[:, part].astype(f32)).astype(bf16)
        k.gwn[part, :] = mm(hidden_t, k.down_s[...])
        return carry

    lax.fori_loop(0, FF // HALF, weights, 0)
    inner_t = jnp.transpose(k.inner_s[...].astype(f32)).astype(bf16)
    if k.packed:
        devices, shard, _ = k.keep.shape

        def halves(j, carry):
            for kept, own in ((k.keep, c_section), (k.sent, 1 - c_section)):
                columns = pl.ds(pl.multiple_of(j * HALF + own * (FF // 2), HALF), HALF)
                here = pl.ds(pl.multiple_of(j * HALF, HALF), HALF)
                part = mm(inner_t, k.up_s[:, columns]).reshape(devices, shard, HALF)
                kept[:, :, here] = part.astype(kept.dtype)
            return carry

        c_section = k.section
        lax.fori_loop(0, FF // 2 // HALF, halves, 0)

        def owner(r, carry):
            for kept, own in ((k.keep, c_section), (k.sent, 1 - c_section)):
                for piece in range(2):
                    start = pl.multiple_of((4 * r + 2 * own + piece) * shard, 8)
                    rows = k.gwn[pl.ds(start, shard), :]
                    at = FF // 2 + piece * D
                    kept[r, :, at : at + D] = rows.astype(kept.dtype)
            return carry

        lax.fori_loop(0, devices, owner, 0)
        k.push("keep")
        k.push("sent")
    else:
        k.gwu[...] = mm(inner_t, k.up_s[...])
    gated = k.gated()
    k.gwo[...] = mm(jnp.transpose(gated[...].astype(f32)).astype(bf16), k.branch_low[...])

    short = jnp.concatenate([gbn[...], jnp.zeros((1, FF - D), f32)], axis=1)
    k.sums[...] = jnp.concatenate(
        [gmod[0:SLOTS, :], gbu[...], short, jnp.zeros((4, FF), f32)], axis=0
    )


def mixer_backward_body(k):
    flip = k.layer == 1
    wide = k.wide
    mixed_s, low, dv_s, rows_s, cols_s = k.mixed_s, k.low, k.dv_s, k.rows_s, k.cols_s
    fill_bias(k.bias, wide)
    branch_low, wo = k.branch_low(), k.wo()

    def first(i, carry):
        start = i * HALF
        rows = pl.ds(start, HALF)
        if flip:
            part = mm(order_matrix(start, HALF, wide, True), branch_low[...]).astype(bf16)
        else:
            part = branch_low[rows, :]
        mixed_s[rows, :] = mm_t(part, wo[...])
        return carry

    lax.fori_loop(0, 2, first, 0)
    rows_s[...] = jnp.zeros(rows_s.shape, f32)
    cols_s[...] = jnp.zeros(cols_s.shape, f32)
    qkvg, vc, cum, cumt, o = k.qkvg(), k.vc(), k.cum(), k.cumt(), k.o()
    k.small()

    def pair(p, carry):
        lanes = lane_iota(1, PAIR)
        total = o[:, columns(p)]
        gate = qkvg[:, columns(p, 3 * D)]
        above = mixed_s[:, columns(p)]
        rate = lax.rsqrt(head_norm(total, lanes) + 1.0)
        sig = sigmoid(gate)
        grad_gate = above * (total * rate) * (sig * (1.0 + gate * (1.0 - sig)))
        low[:, columns(p, 3 * D)] = grad_gate.astype(bf16)
        grad_normed = above * (gate * sig)
        product = grad_normed * total
        inside = jnp.where(
            lanes < HEAD_DIM,
            jnp.sum(jnp.where(lanes < HEAD_DIM, product, 0.0), axis=1, keepdims=True),
            jnp.sum(jnp.where(lanes < HEAD_DIM, 0.0, product), axis=1, keepdims=True),
        ) * (1.0 / HEAD_DIM)
        grad_o = rate * grad_normed - total * (rate * rate * rate) * inside

        queries = qkvg[:, columns(p)] * SCALE
        keys = qkvg[:, columns(p, D)]
        values = vc[:, columns(p)]
        query_cat = cat_left(queries)
        grad_cat = cat_left(grad_o)
        key_high, key_low = split(keys)
        key_pair = jnp.concatenate([key_high, key_low], axis=1)
        query_t = jnp.transpose(queries)
        grad_t = jnp.transpose(grad_o)
        grad_q = []
        grad_k = []
        grad_v = []
        for e in range(2):
            mine = (lanes // HEAD_DIM) == e
            head = 2 * p + e
            key_cat = cat_right(jnp.where(mine, keys, 0.0))
            value_cat = cat_right(jnp.where(mine, values, 0.0))
            first, second = decay_factors(cum, cumt, k.bias, head)
            raw_first = mm_t(query_cat[:HALF], key_cat[:HALF])
            raw_second = mm_t(query_cat[HALF:], key_cat)
            grad_first = first * mm_t(grad_cat[:HALF], value_cat[:HALF])
            grad_second = second * mm_t(grad_cat[HALF:], value_cat)
            score_first = raw_first * first
            score_second = raw_second * second
            pull_first = grad_first * raw_first
            pull_second = grad_second * raw_second
            here = lanes == head
            rows_s[:HALF, :] = rows_s[:HALF, :] + jnp.where(
                here, jnp.sum(pull_first, axis=1, keepdims=True), 0.0
            )
            rows_s[HALF:, :] = rows_s[HALF:, :] + jnp.where(
                here, jnp.sum(pull_second, axis=1, keepdims=True), 0.0
            )
            low_cols = jnp.sum(pull_second, axis=0, keepdims=True)
            cols_s[pl.ds(head, 1), :HALF] = low_cols[:, :HALF] + jnp.sum(
                pull_first, axis=0, keepdims=True
            )
            cols_s[pl.ds(head, 1), HALF:] = low_cols[:, HALF:]
            grad_q.append(
                jnp.concatenate(
                    [
                        mm_near(grad_first, key_pair[:HALF], key_high[:HALF]),
                        mm_near(grad_second, key_pair, key_high),
                    ],
                    axis=0,
                )
            )

            def turned(source_t, block_first, block_second):
                high, low = split(source_t[e * HEAD_DIM : (e + 1) * HEAD_DIM, :])
                both = jnp.concatenate([high, low], axis=0)
                first_high, first_low = split(block_first)
                second_high, second_low = split(block_second)
                one = mm(both[:, :HALF], first_high)
                one = one[:HEAD_DIM] + one[HEAD_DIM:] + mm(high[:, :HALF], first_low)
                two = mm(both[:, HALF:], second_high)
                two = two[:HEAD_DIM] + two[HEAD_DIM:] + mm(high[:, HALF:], second_low)
                return jnp.concatenate([two[:, :HALF] + one, two[:, HALF:]], axis=1)

            grad_k.append(turned(query_t, grad_first, grad_second))
            grad_v.append(turned(grad_t, score_first, score_second))
        query_grad = jnp.where(lanes < HEAD_DIM, grad_q[0], grad_q[1]) * SCALE
        low[:, columns(p)] = query_grad.astype(bf16)
        low[:, columns(p, D)] = jnp.transpose(jnp.concatenate(grad_k, axis=0)).astype(bf16)
        dv_s[:ROWS, columns(p)] = jnp.transpose(jnp.concatenate(grad_v, axis=0))
        return carry

    for p in range(PAIRS):
        pair(p, 0)

    pulled = rows_s[...] - jnp.transpose(cols_s[...])
    high, middle, rest = split_three(pulled)
    upper_first = jnp.concatenate(
        [
            jnp.where(row_iota(HALF, HALF) <= lane_iota(HALF, HALF), 1.0, 0.0),
            jnp.full((HALF, HALF), 0.0, f32) + jnp.where(wide, 1.0, 0.0),
        ],
        axis=1,
    ).astype(bf16)
    upper_second = upper_first[:, :HALF]
    later = jnp.concatenate(
        [
            mm(upper_first, high) + mm(upper_first, middle) + mm(upper_first, rest),
            mm(upper_second, high[HALF:]) + mm(upper_second, middle[HALF:])
            + mm(upper_second, rest[HALF:]),
        ],
        axis=0,
    )
    grad_dp = later * (1.0 / 16.0) * sigmoid(-(k.dp()[...] + k.bd()))
    grad_bd = jnp.sum(grad_dp, axis=0, keepdims=True)
    low[:, QKVG:] = grad_dp.astype(bf16)

    dv_s[ROWS:, :] = jnp.zeros((8, D), f32)
    position = row_iota(ROWS, 1) & jnp.where(wide, ROWS - 1, HALF - 1)
    last = jnp.where(wide, ROWS - 1, HALF - 1)
    here = dv_s[0:ROWS, :]
    one = jnp.where(position <= last - 1, dv_s[1 : 1 + ROWS, :], 0.0)
    two = jnp.where(position <= last - 2, dv_s[2 : 2 + ROWS, :], 0.0)
    value = qkvg[:, 2 * D : 3 * D]
    low[:, 2 * D : 3 * D] = (k.ck(0) * here + k.ck(1) * one + k.ck(2) * two).astype(bf16)
    k.push("low")

    taps = [jnp.sum(rows * value, axis=0, keepdims=True) for rows in (here, one, two)]
    rest = jnp.concatenate([grad_bd, jnp.zeros((1, D - LANES), f32)], axis=1)
    k.sums[...] = jnp.concatenate([*taps, rest, jnp.zeros((4, D), f32)], axis=0)

    ordered_t = jnp.transpose(k.ordered()[...].astype(f32)).astype(bf16)
    gwo = k.gwo()
    gw = k.gw

    def weights(j, carry):
        part = pl.ds(pl.multiple_of(j * HALF, HALF), HALF)
        gw[:, part] = mm(ordered_t, low[:, part])
        return carry

    lax.fori_loop(0, QKVG // HALF, weights, 0)
    gw[:, QKVG : QKVG + D] = gwo[...]
    gw[:, QKVG + D :] = mm(ordered_t, low[:, QKVG:])

    def halves(j, carry):
        here = pl.ds(pl.multiple_of(j * HALF, HALF), HALF)
        keep = pl.ds(pl.multiple_of(j * HALF + k.section * GROUP, HALF), HALF)
        send = pl.ds(pl.multiple_of(j * HALF + (1 - k.section) * GROUP, HALF), HALF)
        k.gw_keep[:, here] = gw[:, keep]
        k.gw_send[:, here] = gw[:, send].astype(bf16)
        return carry

    lax.fori_loop(0, GROUP // HALF, halves, 0)


def input_backward_body(k):
    flip = k.layer == 1
    wide = k.wide
    gmod, mixed_s, perm_s = k.gmod, k.mixed_s, k.perm_s
    gmod[...] = jnp.zeros(gmod.shape, f32)
    low, w_qk, w_vgd = k.low(), k.w_qk(), k.w_vgd()

    def inner_grad(i, carry):
        rows = pl.ds(pl.multiple_of(i * HALF, HALF), HALF)
        mixed_s[rows, :] = mm_t(low[rows, : 2 * D], w_qk[...]) + mm_t(
            low[rows, 2 * D :], w_vgd[...]
        )
        return carry

    lax.fori_loop(0, 2, inner_grad, 0)
    if flip:
        high, middle, rest = split_three(mixed_s[...])
        perm_s[:, :D] = high
        perm_s[:, D : 2 * D] = middle
        perm_s[:, 2 * D :] = rest
    x, mid_grad = k.x(), k.mid_grad()
    k.mods()

    def tile(i, carry):
        start = i * HALF
        rows = pl.ds(start, HALF)
        slot = k.slot(i)
        if flip:
            three = mm(order_matrix(start, HALF, wide, False), perm_s[...])
            grad = three[:, :D] + three[:, D : 2 * D] + three[:, 2 * D :]
        else:
            grad = mixed_s[rows, :]
        normal, rate = normalise(x[rows, :].astype(f32))
        where = (pl.ds(slot, 1), slice(0, D))
        gmod[where] = gmod[where] + jnp.sum(grad, axis=0, keepdims=True)
        where = (pl.ds(slot, 1), slice(D, 2 * D))
        gmod[where] = gmod[where] + jnp.sum(grad * normal, axis=0, keepdims=True)
        total = mid_grad[rows, :] + normalise_back(normal, rate, grad * (1.0 + k.share(slot, 1)))
        k.gx[rows, :] = total
        k.gx_low[rows, :] = total.astype(bf16)
        return carry

    for i in range(2):
        tile(i, 0)
    k.push("gx_low")
    k.push("gx")
    ffn, mixer = k.ffn_sums(), k.mixer_sums()
    k.mod_low[...] = jnp.concatenate([gmod[...], ffn[...]], axis=1).astype(bf16)
    if k.layer == 0:
        first = k.section == 0
        k.gx_send[...] = jnp.where(first, k.gx_two()[...], k.gx[...])
        one, two = k.mod_low[...].astype(f32), k.mod_two()[...].astype(f32)
        k.mod_mine[...] = jnp.where(first, one, two).astype(bf16)
        k.mod_send[...] = jnp.where(first, two, one).astype(bf16)
    half = 2 * D
    rest = ffn[0:1, :] + ffn[1:2, :]
    k.sums[...] = jnp.concatenate(
        [
            gmod[0:1, :] + gmod[1:2, :],
            rest[:, :half],
            rest[:, half:],
            ffn[2:3, :half],
            ffn[2:3, half:],
            jnp.concatenate([ffn[3:4, :D], mixer[0:1, :]], axis=1),
            jnp.concatenate([mixer[1:2, :], mixer[2:3, :]], axis=1),
            jnp.concatenate([mixer[3:4, :], jnp.zeros((1, D), f32)], axis=1),
        ],
        axis=0,
    )


ANY = pl.BlockSpec(memory_space=pl.ANY)
VMEM = pl.BlockSpec(memory_space=pltpu.VMEM)
HBM = pl.BlockSpec(memory_space=pltpu.HBM)


def call(body, layer, layouts, ins, outs, scratch, flops, packed=None, after=()):
    arrays = []
    counts = []
    kept = []
    places = []
    for kind, given, part in ins.values():
        places.extend([ANY] * 2 if kind == "own" else [HBM])
        given = given if kind == "own" else (given,)
        arrays.extend(given)
        counts.append(len(given))
        rows, wide = given[0].shape[-2:]
        start, stop = part or (0, wide)
        kept.append(pltpu.VMEM((rows, stop - start), given[0].dtype))

    def kernel(*refs):
        refs = list(refs)
        take = lambda count: [refs.pop(0) for _ in range(count)]
        (layouts_ref,) = take(1)
        sources = [take(count) for count in counts]
        take(len(after))
        targets = take(len(outs))
        buffers = take(len(ins))
        results = take(len(outs))
        rest = take(len(scratch))
        in_sems, out_sems = refs
        k = Kernel(layer, layouts_ref)
        k.packed = packed
        for number, (name, (kind, _, part)) in enumerate(ins.items()):
            given = sources[number]
            if part is not None:
                given = [ref.at[:, part[0] : part[1]] for ref in given]
            setattr(k, name, k.load(kind, given, buffers[number], in_sems.at[number]))
        k.results = {}
        for number, name in enumerate(outs):
            setattr(k, name, results[number])
            k.results[name] = (results[number], targets[number], out_sems.at[number])
        for name, ref in zip(scratch, rest):
            setattr(k, name, ref)
        body(k)
        k.finish()

    return pl.pallas_call(
        kernel,
        out_shape=[jax.ShapeDtypeStruct(shape, kind) for shape, kind, _ in outs.values()],
        in_specs=[pl.BlockSpec(memory_space=pltpu.SMEM)] + places + [ANY] * len(after),
        out_specs=[HBM if for_kernel else ANY for _, _, for_kernel in outs.values()],
        scratch_shapes=kept
        + [pltpu.VMEM(shape, kind) for shape, kind, _ in outs.values()]
        + [pltpu.VMEM(shape, kind) for shape, kind in scratch.values()]
        + [pltpu.SemaphoreType.DMA((len(ins),)), pltpu.SemaphoreType.DMA((len(outs),))],
        compiler_params=pltpu.CompilerParams(vmem_limit_bytes=56 * 1024 * 1024),
        cost_estimate=pl.CostEstimate(flops=flops, bytes_accessed=4 << 20, transcendentals=0),
    )(layouts, *arrays, *after)


def own(pair, part=None):
    return ("own", pair, part)


def plain(array):
    return ("plain", array, None)


def micro(array):
    return ("micro", array, None)


ADA_CUT = 9 * LANES
AT_QK = (0, 2 * D)
AT_ADA_A = (2 * D, 2 * D + ADA_CUT)
AT_VGD = (0, 2 * D + LANES)
AT_ADA_B = (2 * D + LANES, 8 * D + LANES - ADA_CUT)
AT_UP = (0, FF)
AT_OUT = (FF, FF + D)


def attn_forward(layer, layouts, x, mods, small, qka, vgda):
    return call(
        attn_forward_body,
        layer,
        layouts,
        dict(
            x=micro(x),
            mods=own(mods),
            w_qk=own(qka, AT_QK),
            w_vgd=own(vgda, AT_VGD),
            small=own(small),
        ),
        dict(
            ordered=((ROWS, D), bf16, True),
            qkvg=((ROWS, QKVG), f32, True),
            dp=((ROWS, LANES), f32, True),
            vc=((ROWS, D), f32, True),
            cum=((ROWS, LANES), f32, True),
            cumt=((LANES, ROWS), f32, True),
            o=((ROWS, D), f32, True),
            gated=((ROWS, D), bf16, True),
        ),
        dict(
            inner=((ROWS, D), bf16),
            vpad=((ROWS + 8, D), f32),
            bias=((HALF, ROWS), f32),
        ),
        8 * 10**9,
    )


def ffn_forward(layer, layouts, x, mods, small, gated, upo, down):
    return call(
        ffn_forward_body,
        layer,
        layouts,
        dict(
            gated=plain(gated),
            x=micro(x),
            wo=own(upo, AT_OUT),
            mods=own(mods),
            small=own(small),
            wu=own(upo, AT_UP),
            wn=own(down),
        ),
        dict(
            out=((ROWS, D), bf16, True),
            branch=((ROWS, D), f32, True),
            down=((ROWS, D), f32, True),
            **({"sent": ((ROWS, D), bf16, False)} if layer == 1 else {}),
        ),
        {},
        5 * 10**9,
    )


def ffn_backward(
    layer, layouts, x, mods, small, gated, branch, down_raw, grad, upo, down, devices, after=()
):
    shard = D // devices
    in_kernel = shard % 8 == 0
    if in_kernel:
        sums = dict(
            keep=((devices, shard, FF), f32, True),
            sent=((devices, shard, FF), bf16, False),
        )
    else:
        sums = dict(gwu=((D, FF), f32, False), gwn=((FF, D), f32, False))
    return call(
        ffn_backward_body,
        layer,
        layouts,
        dict(
            mods=own(mods),
            small=own(small),
            x=micro(x),
            grad=micro(grad),
            branch=plain(branch),
            down=plain(down_raw),
            wu=own(upo, AT_UP),
            wn=own(down),
            gated=plain(gated),
        ),
        dict(
            mid_grad=((ROWS, D), f32, True),
            branch_low=((ROWS, D), bf16, True),
            gwo=((D, D), f32, True),
            sums=((8, FF), f32, True),
            **sums,
        ),
        dict(
            **({"gwn": ((FF, D), f32)} if in_kernel else {}),
            hidden_s=((ROWS, FF), bf16),
            inner_s=((ROWS, D), bf16),
            up_s=((ROWS, FF), bf16),
            down_s=((ROWS, D), bf16),
            gmod=((8, FF), f32),
            gbu=((1, FF), f32),
            gbn=((1, D), f32),
        ),
        12 * 10**9,
        packed=in_kernel,
        after=after,
    )


def mixer_backward(layer, layouts, small, saved, branch_low, gwo, upo, after=()):
    ordered, qkvg, dp, vc, cum, cumt, o = saved
    return call(
        mixer_backward_body,
        layer,
        layouts,
        dict(
            branch_low=plain(branch_low),
            wo=own(upo, AT_OUT),
            qkvg=plain(qkvg),
            vc=plain(vc),
            cum=plain(cum),
            cumt=plain(cumt),
            o=plain(o),
            small=own(small),
            dp=plain(dp),
            ordered=plain(ordered),
            gwo=plain(gwo),
        ),
        dict(
            low=((ROWS, QKVG + LANES), bf16, True),
            gw_keep=((D, GROUP), f32, True),
            gw_send=((D, GROUP), bf16, False),
            sums=((8, D), f32, True),
        ),
        dict(
            mixed_s=((ROWS, D), f32),
            dv_s=((ROWS + 8, D), f32),
            rows_s=((ROWS, LANES), f32),
            cols_s=((LANES, ROWS), f32),
            bias=((HALF, ROWS), f32),
            gw=((D, 2 * GROUP), f32),
        ),
        15 * 10**9,
        after=after,
    )


def input_backward(
    layer, layouts, x, mods, low, mid_grad, ffn_sums, mixer_sums, qka, vgda, two=None, after=()
):
    extra_in, extra_out = {}, {}
    if two is not None:
        extra_in = dict(gx_two=plain(two[0]), mod_two=plain(two[1]))
        extra_out = dict(
            gx_send=((ROWS, D), f32, False),
            mod_mine=((8, 6 * D), bf16, False),
            mod_send=((8, 6 * D), bf16, False),
        )
    return call(
        input_backward_body,
        layer,
        layouts,
        dict(
            low=plain(low),
            w_qk=own(qka, AT_QK),
            w_vgd=own(vgda, AT_VGD),
            x=micro(x),
            mid_grad=plain(mid_grad),
            mods=own(mods),
            ffn_sums=plain(ffn_sums),
            mixer_sums=plain(mixer_sums),
            **extra_in,
        ),
        dict(
            gx=((ROWS, D), f32, True),
            gx_low=((ROWS, D), bf16, True),
            mod_low=((8, 6 * D), bf16, True),
            sums=((8, 2 * D), f32, False),
            **extra_out,
        ),
        dict(
            mixed_s=((ROWS, D), f32),
            perm_s=((ROWS, 3 * D), bf16),
            gmod=((8, 2 * D), f32),
        ),
        4 * 10**9,
        after=after,
    )


def small_kernel(b_up, b_down, taps, b_decay, packed):
    packed[...] = jnp.zeros(packed.shape, f32)
    packed[0:1, :] = b_up[...]
    packed[1:2, :D] = b_down[...]
    packed[2:5, :D] = taps[0]
    packed[5:6, :HEADS] = b_decay[...]


def pack_small(b_up, b_down, taps, b_decay):
    return pl.pallas_call(
        small_kernel,
        out_shape=jax.ShapeDtypeStruct((8, FF), f32),
        in_specs=[VMEM] * 4,
        out_specs=VMEM,
    )(b_up, b_down, taps, b_decay)


def pack_kernel(w_query, w_key, w_value, w_gate, w_out, w_decay, w_ada, w_up, qka, vgda, upo):
    qka[:, :D] = w_query[0]
    qka[:, D : 2 * D] = w_key[0]
    qka[:, 2 * D :] = w_ada[0, :, :ADA_CUT]
    vgda[:, :D] = w_value[0]
    vgda[:, D : 2 * D] = w_gate[0]
    place = jnp.where(row_iota(HEADS, LANES) == lane_iota(HEADS, LANES), 1.0, 0.0).astype(bf16)
    turned = lax.dot_general(
        w_decay[0], place, (((0,), (0,)), ((), ())), preferred_element_type=f32
    )
    vgda[:, 2 * D : 2 * D + LANES] = turned.astype(bf16)
    vgda[:, 2 * D + LANES :] = w_ada[0, :, ADA_CUT:]
    upo[:, :FF] = w_up[0]
    upo[:, FF:] = w_out[0]


def pack(*weights):
    shard = weights[0].shape[1]
    widths = (2 * D + ADA_CUT, 8 * D + LANES - ADA_CUT, FF + D)
    return pl.pallas_call(
        pack_kernel,
        out_shape=[jax.ShapeDtypeStruct((shard, width), bf16) for width in widths],
        in_specs=[VMEM] * len(weights),
        out_specs=[VMEM] * len(widths),
    )(*weights)


def join_kernel(bits, waits, *refs):
    count = len(bits)
    held, came, out = refs[:count], refs[count : 2 * count], refs[2 * count + waits :]
    for i, bit in enumerate(bits):
        mine = (lax.axis_index("row") >> bit) & 1
        out[i][:, mine] = held[i][...]
        out[i][:, 1 - mine] = came[i][...]


def join(held, came, bits, after=()):
    def parts(array, bit):
        axis = axis_of(bit)
        above = 1
        for size in array.shape[:axis]:
            above *= size
        return array.reshape((above, -1) + array.shape[-2:])

    split_held = [parts(array, bit) for array, bit in zip(held, bits)]
    split_came = [parts(array, bit) for array, bit in zip(came, bits)]
    out = pl.pallas_call(
        functools.partial(join_kernel, bits, len(after)),
        out_shape=[
            jax.ShapeDtypeStruct(array.shape[:1] + (2,) + array.shape[1:], array.dtype)
            for array in split_held
        ],
        in_specs=[VMEM] * (2 * len(held)) + [ANY] * len(after),
        out_specs=[VMEM] * len(held),
        compiler_params=pltpu.CompilerParams(vmem_limit_bytes=8 * 1024 * 1024),
        cost_estimate=pl.CostEstimate(flops=10**6, bytes_accessed=10**6, transcendentals=0),
    )(*split_held, *split_came, *after)
    joined = []
    for array, result, bit in zip(held, out, bits):
        shape = list(array.shape)
        shape[axis_of(bit)] = 2
        joined.append(result.reshape(shape))
    return joined


def mods_kernel(conditions, bias, packed, vgd, out, ada_a, ada_b, sems):
    copies = [
        pltpu.make_async_copy(packed.at[:, AT_ADA_A[0] : AT_ADA_A[1]], ada_a, sems.at[0]),
        pltpu.make_async_copy(vgd.at[:, AT_ADA_B[0] : AT_ADA_B[1]], ada_b, sems.at[1]),
    ]
    for copy in copies:
        copy.start()
    values = conditions[...].astype(f32)
    lifted = (values * sigmoid(values)).astype(bf16)
    for copy in copies:
        copy.wait()
    out[...] = jnp.concatenate([mm(lifted, ada_a[...]), mm(lifted, ada_b[...])], axis=1) + bias[...]


ADA_SCRATCH = [
    pltpu.VMEM((D, ADA_CUT), bf16),
    pltpu.VMEM((D, 6 * D - ADA_CUT), bf16),
    pltpu.SemaphoreType.DMA((2,)),
]


def modulations(conditions, bias, packed, vgd):
    return pl.pallas_call(
        mods_kernel,
        out_shape=jax.ShapeDtypeStruct((MICRO * SLOTS, 6 * D), f32),
        in_specs=[VMEM, VMEM, ANY, ANY],
        out_specs=VMEM,
        scratch_shapes=ADA_SCRATCH,
        compiler_params=pltpu.CompilerParams(vmem_limit_bytes=16 * 1024 * 1024),
        cost_estimate=pl.CostEstimate(flops=10**9, bytes_accessed=2 << 20, transcendentals=0),
    )(conditions, bias, packed, vgd)


def lifted_kernel(mine, came, packed, vgd, out, ada_a, ada_b, sems):
    copies = [
        pltpu.make_async_copy(packed.at[:, AT_ADA_A[0] : AT_ADA_A[1]], ada_a, sems.at[0]),
        pltpu.make_async_copy(vgd.at[:, AT_ADA_B[0] : AT_ADA_B[1]], ada_b, sems.at[1]),
    ]
    for copy in copies:
        copy.start()
    for copy in copies:
        copy.wait()
    first = lax.axis_index("section") == 0
    pair = mine[0:SLOTS, :].astype(f32), came[0:SLOTS, :].astype(f32)
    grad = jnp.concatenate(
        [jnp.where(first, pair[0], pair[1]), jnp.where(first, pair[1], pair[0])], axis=0
    ).astype(bf16)
    out[...] = mm_t(grad[:, :ADA_CUT], ada_a[...]) + mm_t(grad[:, ADA_CUT:], ada_b[...])


def lifted_grads(mine, came, packed, vgd):
    return pl.pallas_call(
        lifted_kernel,
        out_shape=jax.ShapeDtypeStruct((MICRO * SLOTS, D), f32),
        in_specs=[VMEM, VMEM, ANY, ANY],
        out_specs=VMEM,
        scratch_shapes=ADA_SCRATCH,
        compiler_params=pltpu.CompilerParams(vmem_limit_bytes=16 * 1024 * 1024),
        cost_estimate=pl.CostEstimate(flops=10**9, bytes_accessed=2 << 20, transcendentals=0),
    )(mine, came, packed, vgd)


def step_kernel(bit, widths, counts, waits, *refs):
    mine = (lax.axis_index("row") >> bit) & 1
    count, many = len(widths), len(counts)
    refs = list(refs)
    take = lambda number: [refs.pop(0) for _ in range(number)]
    sources = take(count + many)
    take(waits)
    targets = take(count + 1)
    buffers = take(count + many)
    results = take(count + 1)
    in_sems, out_sems = refs
    arrive = [
        pltpu.make_async_copy(source, buffer, in_sems.at[i])
        for i, (source, buffer) in enumerate(zip(sources, buffers))
    ]
    leave = [
        pltpu.make_async_copy(result, target, out_sems.at[i])
        for i, (result, target) in enumerate(zip(results, targets))
    ]
    for copy in arrive:
        copy.start()
    kept, came = buffers[:count], buffers[count:]
    places = [(j, i) for j, number in enumerate(counts) for i in range(number)]
    goes = results[count]
    at = 0
    for i in range(count):
        j, place = places[i]
        arrive[i].wait()
        if place == 0:
            arrive[count + j].wait()
        start = sum(widths[i - place : i])
        columns = slice(start, start + widths[i])
        total = kept[i][:, 1 - mine] + came[j][:, 1 - mine, :, :, columns].astype(f32)
        goes[:, :, :, at : at + widths[i]] = total.astype(bf16)
        at += widths[i]
    leave[count].start()
    for i in range(count):
        j, place = places[i]
        start = sum(widths[i - place : i])
        columns = slice(start, start + widths[i])
        results[i][...] = kept[i][:, mine] + came[j][:, mine, :, :, columns].astype(f32)
        leave[i].start()
    for copy in leave:
        copy.wait()


def step(kept, came, bit, below=1, after=()):
    blocks, rows = kept[0].shape[0] // 2, kept[0].shape[1]
    above = blocks // below
    paired = lambda array: array.reshape((above, 2, below) + array.shape[1:])
    widths = [array.shape[2] for array in kept]
    size = sum(array.size for array in kept)
    arrays = [paired(array) for array in kept] + [paired(array) for array, _ in came]
    shapes = [((above, below, rows, width), f32) for width in widths]
    shapes.append(((above, below, rows, sum(widths)), bf16))
    out = pl.pallas_call(
        functools.partial(step_kernel, bit, widths, [count for _, count in came], len(after)),
        out_shape=[jax.ShapeDtypeStruct(shape, kind) for shape, kind in shapes],
        in_specs=[HBM] * len(kept) + [ANY] * (len(came) + len(after)),
        out_specs=[HBM] * len(kept) + [ANY],
        scratch_shapes=[pltpu.VMEM(array.shape, array.dtype) for array in arrays]
        + [pltpu.VMEM(shape, kind) for shape, kind in shapes]
        + [pltpu.SemaphoreType.DMA((len(arrays),)), pltpu.SemaphoreType.DMA((len(shapes),))],
        compiler_params=pltpu.CompilerParams(vmem_limit_bytes=10 * 1024 * 1024),
        cost_estimate=pl.CostEstimate(flops=size, bytes_accessed=8 * size, transcendentals=0),
    )(*arrays, *after)
    count = len(kept)
    flat_blocks = [array.reshape((blocks,) + array.shape[2:]) for array in out]
    return flat_blocks[:count], flat_blocks[count]


def misc_step_kernel(held, arrived, out):
    size = held.shape[0] - SUMS
    out[:size, :] = held[:size, :]
    out[size : 2 * size, :] = arrived[:size, :]
    high, low = split(misc_sums(held, arrived))
    out[2 * size : 2 * size + SUMS // 2, :] = high
    out[2 * size + SUMS // 2 :, :] = low


def misc_step(held, arrived):
    return pl.pallas_call(
        misc_step_kernel,
        out_shape=jax.ShapeDtypeStruct((2 * held.shape[0] - SUMS, 2 * D), bf16),
        in_specs=[VMEM] * 2,
        out_specs=VMEM,
        cost_estimate=pl.CostEstimate(flops=10**5, bytes_accessed=10**5, transcendentals=0),
    )(held, arrived)


def misc_sums(*refs):
    size = refs[0].shape[0] - SUMS
    parts = [ref[size:, :].astype(f32) for ref in refs]
    return sum(part[: SUMS // 2] + part[SUMS // 2 :] for part in parts)


SUMS = 16


def misc_rows(conditions, mod_low):
    values = conditions[...].astype(f32)
    values = jnp.where(lax.axis_index("section") == 0, values[:SLOTS], values[SLOTS:])
    lifted = (values * sigmoid(values)).astype(bf16).astype(f32)
    rows = [
        mod_low[slot : slot + 1, i * 2 * D : (i + 1) * 2 * D].astype(f32)
        for slot in range(SLOTS)
        for i in range(3)
    ]
    rows.append(jnp.concatenate([lifted[0:1], lifted[1:2]], axis=1))
    rows.append(jnp.zeros((1, 2 * D), f32))
    return jnp.concatenate(rows, axis=0)


def misc_kernel(conditions, mod_low, sums, out):
    rows = [misc_rows(conditions, mod_low), *(part.astype(f32) for part in split(sums[...]))]
    out[...] = jnp.concatenate(rows, axis=0).astype(bf16)


def pack_misc(conditions, mod_low, sums):
    return pl.pallas_call(
        misc_kernel,
        out_shape=jax.ShapeDtypeStruct((8 + SUMS, 2 * D), bf16),
        in_specs=[VMEM] * 3,
        out_specs=VMEM,
    )(conditions, mod_low, sums)


def finish_kernel(widths, counts, *refs):
    count = len(widths)
    kept, refs = refs[:count], refs[count:]
    came, refs = refs[: len(counts)], refs[len(counts) :]
    lifted_one, lifted_two, misc_two, misc, misc_came, mine, other, small_mine, small_other = refs
    places = [(ref, i) for ref, many in zip(came, counts) for i in range(many)]
    added = []
    for i in range(count):
        ref, place = places[i]
        start = sum(widths[i - place : i])
        added.append(kept[i][0] + ref[0, :, start : start + widths[i]].astype(f32))
    a1, f1, f2, a2 = added
    size = misc.shape[0] - SUMS
    mod_one = jnp.concatenate([misc[:size, :], misc_came[:size, :]], axis=0)

    def ada(lifted, rows):
        rows = rows.astype(f32).reshape(-1, 8, 2 * D)
        columns = []
        for i in range(3):
            both = [rows[:, 3 * slot + i, :] for slot in range(SLOTS)]
            columns.append(mm(lifted[...], jnp.concatenate(both, axis=0).astype(bf16)))
        return jnp.concatenate(columns, axis=1)

    first = lax.axis_index("section") == 0
    at = 0
    for one, two in ((a1, a2), (f1, f2), (ada(lifted_one, mod_one), ada(lifted_two, misc_two[: 2 * size, :]))):
        columns = slice(at, at + one.shape[1])
        mine[:, columns] = jnp.where(first, one, two)
        other[:, columns] = jnp.where(first, two, one)
        at += one.shape[1]
    one, two = misc_sums(misc, misc_came), misc_sums(misc_two)
    small_mine[...] = jnp.where(first, one, two)
    small_other[...] = jnp.where(first, two, one)


def finish(kept, came, lifted_one, lifted_two, misc_two, misc, misc_came):
    widths = [array.shape[2] for array in kept]
    shard = kept[0].shape[1]
    wide = GROUP + FF + 6 * D
    arrays = [array for array, _ in came]
    shapes = [(shard, wide)] * 2 + [(8, 2 * D)] * 2
    return pl.pallas_call(
        functools.partial(finish_kernel, widths, [count for _, count in came]),
        out_shape=[jax.ShapeDtypeStruct(shape, f32) for shape in shapes],
        in_specs=[VMEM] * (len(kept) + len(came) + 5),
        out_specs=[VMEM] * 4,
        compiler_params=pltpu.CompilerParams(vmem_limit_bytes=8 * 1024 * 1024),
    )(*kept, *arrays, lifted_one, lifted_two, misc_two, misc, misc_came)


def output_kernel(mine, other, small_mine, small_other, *outs):
    first = lax.axis_index("section") == 0

    def halves(start, width):
        columns = slice(start, start + width)
        pair = mine[:, columns], other[:, columns]
        return jnp.where(first, pair[0], pair[1]), jnp.where(first, pair[1], pair[0])

    attn = halves(0, GROUP)
    cut = GROUP - 2 * D
    outs[0][...] = attn[0][:, :D]
    outs[1][...] = attn[0][:, D : 2 * D]
    outs[2][:, :cut] = attn[0][:, 2 * D :]
    outs[2][:, cut:] = attn[1][:, : D - cut]
    outs[3][...] = attn[1][:, D - cut : 2 * D - cut]
    outs[4][...] = attn[1][:, 2 * D - cut : 3 * D - cut]
    decay = jnp.transpose(attn[1][:, 3 * D - cut :])
    for head in range(HEADS):
        outs[5][head] = decay[head : head + 1, :]
    up = halves(GROUP, FF // 2)
    outs[6][:, : FF // 2] = up[0]
    outs[6][:, FF // 2 :] = up[1]
    for piece in range(2):
        down = halves(GROUP + FF // 2 + piece * D, D)
        outs[7][piece] = down[0]
        outs[7][2 + piece] = down[1]
    outs[8][...] = mine[:, GROUP + FF :] + other[:, GROUP + FF :]
    small = small_mine[...] + small_other[...]
    half = 2 * D
    for i in range(3):
        outs[9][:, i * half : (i + 1) * half] = small[i : i + 1, :]
    for i in range(2):
        outs[10][:, i * half : (i + 1) * half] = small[3 + i : 4 + i, :]
    outs[11][...] = small[5:6, :D]
    outs[12][0] = small[5:6, D:]
    outs[12][1] = small[6:7, :D]
    outs[12][2] = small[6:7, D:]
    outs[13][...] = small[7:8, :HEADS]


def outputs(mine, other, small_mine, small_other):
    shard = mine.shape[0]
    shapes = (
        [(shard, D)] * 5
        + [(HEADS, 1, shard), (shard, FF), (4, shard, D), (shard, 6 * D)]
        + [(1, 6 * D), (1, FF), (1, D), (3, 1, D), (1, HEADS)]
    )
    return pl.pallas_call(
        output_kernel,
        out_shape=[jax.ShapeDtypeStruct(shape, f32) for shape in shapes],
        in_specs=[VMEM] * 4,
        out_specs=[VMEM] * len(shapes),
    )(mine, other, small_mine, small_other)


def both_kernel(one, two, came, out, kept, sems):
    section = lax.axis_index("section")

    def move(mine, layer):
        arrive = [
            pltpu.make_async_copy(mine, kept.at[layer], sems.at[0]),
            pltpu.make_async_copy(came, kept.at[1 - layer], sems.at[1]),
        ]
        leave = [
            pltpu.make_async_copy(kept.at[layer], out.at[layer], sems.at[2]),
            pltpu.make_async_copy(kept.at[1 - layer], out.at[1 - layer], sems.at[3]),
        ]
        for copy in arrive:
            copy.start()
        for copy, after in zip(arrive, leave):
            copy.wait()
            after.start()
        for copy in leave:
            copy.wait()

    @pl.when(section == 0)
    def _():
        move(one, 0)

    @pl.when(section == 1)
    def _():
        move(two, 1)


def both_micros(one, two, came):
    return pl.pallas_call(
        both_kernel,
        out_shape=jax.ShapeDtypeStruct((MICRO,) + one.shape, one.dtype),
        in_specs=[ANY] * 3,
        out_specs=ANY,
        scratch_shapes=[
            pltpu.VMEM((MICRO,) + one.shape, one.dtype),
            pltpu.SemaphoreType.DMA((4,)),
        ],
    )(one, two, came)


def swap(values):
    return lax.ppermute(values, "section", [(0, 1), (1, 0)])


def row_bits():
    bits = lax.axis_size("row").bit_length() - 1
    third = bits // 3
    return (
        tuple(range(third)),
        tuple(range(third, 2 * third)),
        tuple(range(2 * third, bits)),
    )


def partner(values, bit):
    size = lax.axis_size("row")
    return lax.ppermute(values, "row", [(i, i ^ (1 << bit)) for i in range(size)])


def axis_of(bit):
    return lax.axis_size("row").bit_length() - 2 - bit


def bit_of(bit):
    return (lax.axis_index("row") >> bit) & 1


def single(values):
    return values.reshape((1,) * (lax.axis_size("row").bit_length() - 1) + values.shape)


def gather_steps(along_x, along_y, along_z):
    steps = [(bit, bit) for bit in reversed(along_z)]
    return steps + list(zip(along_x + along_y, along_y + along_x))


def flat(held):
    return held.reshape(-1, held.shape[-1])


def lock(*arrays):
    return lax.optimization_barrier(arrays)


def on_device(
    tokens, conditions, output_grad, layouts,
    w_ada, b_ada, w_query, w_key, w_value, w_gate, w_out, w_decay, b_decay, conv_kernel,
    w_up, b_up, w_down, b_down,
):
    section = lax.axis_index("section")
    devices = lax.axis_size("row")
    shard = w_query.shape[1]
    along_x, along_y, along_z = row_bits()

    def both(values):
        return values, swap(values)

    qka, vgda, upo = pack(
        w_query, w_key, w_value, w_gate, w_out, w_decay.transpose(0, 2, 1), w_ada, w_up
    )
    small = pack_small(b_up, b_down, conv_kernel, b_decay)
    steps = gather_steps(along_x, along_y, along_z)
    lag = len(along_z)
    groups = [[single(qka), single(vgda)], [single(upo), single(w_down[0])]]
    after = (small,)
    for place in range(len(steps) + lag):
        numbers = [g for g in range(2) if 0 <= place - g * lag < len(steps)]
        bits = [bit for g in numbers for bit in steps[place - g * lag]]
        held = [array for g in numbers for array in groups[g]]
        came = [partner(array, bit) for array, bit in zip(held, bits)]
        if place == len(steps) + lag - 1:
            after = (gated,)
        held = join(held, came, bits, after)
        after = ()
        for g in numbers:
            groups[g], held = held[:2], held[2:]
        if place == len(steps) - 1:
            qka, vgda = [both(flat(array)) for array in groups[0]]
            conds = conditions.reshape(MICRO * SLOTS, D)
            mods = both(modulations(conds, b_ada, qka[0], vgda[0]))
            smalls = both(small)
            x = tokens
            *saved, gated = attn_forward(0, layouts, x, mods, smalls, qka, vgda)
    upo, down = [both(flat(array)) for array in groups[1]]
    kept = []
    acts = []
    for l in range(2):
        if l:
            *saved, gated = attn_forward(l, layouts, x, mods, smalls, qka, vgda)
        out, branch, down_raw, *acts_sent = ffn_forward(
            l, layouts, x, mods, smalls, gated, upo, down
        )
        kept.append((x, saved, gated, branch, down_raw))
        acts.append(out)
        x = out[None]

    def ffn_step(l, grad, after=()):
        x, saved, gated, branch, down_raw = kept[l]
        mid_grad, branch_low, gwo, sums, *terms = ffn_backward(
            l, layouts, x, mods, smalls, gated, branch, down_raw, grad, upo, down, devices, after
        )
        if terms[0].ndim == 2:
            up_sum = terms[0].reshape(devices, shard, 2, FF // 2)
            down_sum = terms[1].reshape(devices, 2, 2, shard, D)
            terms = []
            for own in (section, 1 - section):
                up_half = lax.dynamic_index_in_dim(up_sum, own, 2, keepdims=False)
                down_half = lax.dynamic_index_in_dim(down_sum, own, 1, keepdims=False)
                terms.append(
                    jnp.concatenate([up_half, down_half[:, 0], down_half[:, 1]], axis=2)
                )
            terms[1] = terms[1].astype(bf16)
        return [branch_low, gwo], mid_grad, terms[0], terms[1], sums

    def mixer_step(l, carried, after=()):
        low, keep, sent, sums = mixer_backward(
            l, layouts, smalls, kept[l][1], *carried, upo, after
        )
        by_row = lambda array: array.reshape(devices, shard, GROUP)
        return low, by_row(keep), by_row(sent), sums

    def input_step(l, low, mid_grad, ffn_sums, mixer_sums, two=None, after=()):
        x = kept[l][0]
        return input_backward(
            l, layouts, x, mods, low, mid_grad, ffn_sums, mixer_sums, qka, vgda, two, after
        )

    def run(keep, came, bits, below=1, after=()):
        for bit in bits[:-1]:
            keep, sent = step(keep, came, bit, below, after)
            came = [(partner(sent, bit), len(keep))]
        return step(keep, came, bits[-1], below, after)

    def grown(mod, bits):
        for bit in bits:
            mod = misc_step(mod, partner(mod, bit))
        return mod

    x_bits, y_bits, z_bits = along_x, along_y, along_z
    carried, mid_grad, f2_keep, f2_sent, f2_sums = ffn_step(1, output_grad)
    *carried, f2_sent, acts_sent = lock(*carried, f2_sent, acts_sent[0])
    f2_came = swap(f2_sent)
    acts_came = swap(acts_sent)
    low, a2_keep, a2_sent, m2_sums = mixer_step(1, carried)
    low, a2_sent, f2_came, acts_came = lock(low, a2_sent, f2_came, acts_came)
    a2_came = swap(a2_sent)
    gx_two, grad, mod_low_two, sums_two = input_step(1, low, mid_grad, f2_sums, m2_sums)
    misc_two = pack_misc(conds, mod_low_two, sums_two)
    grad, misc_two, a2_came = lock(grad, misc_two, a2_came)
    f2_keep, f2_sent = run([f2_keep], [(f2_came, 1)], x_bits)
    a2_keep, a2_sent = run([a2_keep], [(a2_came, 1)], y_bits, 1 << len(x_bits))
    misc_two = grown(misc_two, x_bits[:-1])
    grad, f2_sent, a2_sent, misc_two = lock(grad, f2_sent, a2_sent, misc_two)
    f2_came = partner(f2_sent, x_bits[-1])
    misc_came = partner(misc_two, x_bits[-1])
    a2_came = partner(a2_sent, y_bits[-1])

    carried, mid_grad, f1_keep, f1_sent, f1_sums = ffn_step(0, grad[None])
    *carried, f1_sent, f2_came, a2_came, misc_came = lock(
        *carried, f1_sent, f2_came, a2_came, misc_came
    )
    f1_came = swap(f1_sent)
    misc_two = misc_step(misc_two, misc_came)
    f2_keep, f2_sent = run(f2_keep, [(f2_came, 1)], y_bits)
    a2_keep, a2_sent = run(a2_keep, [(a2_came, 1)], x_bits)
    misc_two = grown(misc_two, y_bits[:-1])
    f1_keep, f1_sent = run([f1_keep], [(f1_came, 1)], x_bits)
    *carried, f2_sent, a2_sent, misc_two, f1_sent = lock(
        *carried, f2_sent, a2_sent, misc_two, f1_sent
    )
    f1_came = partner(f1_sent, x_bits[-1])
    a2_came = partner(a2_sent, x_bits[-1])
    f2_came = partner(f2_sent, y_bits[-1])
    misc_came = partner(misc_two, y_bits[-1])
    low, a1_keep, a1_sent, m1_sums = mixer_step(0, carried)
    low, a1_sent, f2_came, a2_came, misc_came, f1_came = lock(
        low, a1_sent, f2_came, a2_came, misc_came, f1_came
    )
    a1_came = swap(a1_sent)
    misc_two = misc_step(misc_two, misc_came)
    two_keep, two_sent = run(f2_keep + a2_keep, [(f2_came, 1), (a2_came, 1)], z_bits[:1])
    f1_keep, f1_sent = run(f1_keep, [(f1_came, 1)], y_bits)
    a1_keep, a1_sent = run([a1_keep], [(a1_came, 1)], x_bits)
    low, two_sent, misc_two, f1_sent, a1_sent = lock(low, two_sent, misc_two, f1_sent, a1_sent)
    a1_came = partner(a1_sent, x_bits[-1])
    f1_came = partner(f1_sent, y_bits[-1])
    two_came = partner(two_sent, z_bits[0])
    misc_came = partner(misc_two, z_bits[0])
    gx_one, _, mod_low_one, sums_one, gx_sent, mod_mine, mod_sent = input_step(
        0, low, mid_grad, f1_sums, m1_sums, (gx_two, mod_low_two)
    )
    misc = pack_misc(conds, mod_low_one, sums_one)
    misc, a1_came, two_came, misc_came, f1_came, gx_sent, mod_sent = lock(
        misc, a1_came, two_came, misc_came, f1_came, gx_sent, mod_sent
    )

    a1_keep, a1_sent = run(a1_keep, [(a1_came, 1)], y_bits)
    misc_two = grown(misc_step(misc_two, misc_came), z_bits[1:-1])
    two_keep, two_sent = run(two_keep, [(two_came, 2)], z_bits[1:])
    a1_sent, misc, two_sent, misc_two = lock(a1_sent, misc, two_sent, misc_two)
    a1_came = partner(a1_sent, y_bits[-1])
    two_came = partner(two_sent, z_bits[-1])
    misc_two = grown(misc_two, z_bits[-1:])
    misc = grown(misc, tuple(reversed(z_bits))[:-1])
    gx_came = swap(gx_sent)
    mod_came = swap(mod_sent)
    keep, came = a1_keep + f1_keep, [(a1_came, 1), (f1_came, 1)]
    for bit in z_bits[:-1]:
        keep, sent = step(keep, came, bit)
        if bit == z_bits[0]:
            sent, misc, gx_came, mod_came = lock(sent, misc, gx_came, mod_came)
        came = [(partner(sent, bit), len(keep))]
    misc = grown(misc, z_bits[:1])
    gx_out = both_micros(gx_one, gx_two, gx_came)
    acts_out = both_micros(acts[0], acts[1], acts_came)
    grad_lifted = lifted_grads(mod_mine, mod_came, qka[0], vgda[0])
    lifted_came = swap(grad_lifted)
    lifted = misc_two[: 8 * devices].reshape(devices, 8, SLOTS, D)[:, 6]
    lifted = lax.dynamic_slice_in_dim(lifted, lax.axis_index("row") * shard, shard, 2)
    lifted = lifted.transpose(2, 1, 0)
    order_two = x_bits + y_bits + z_bits
    order_one = tuple(reversed(z_bits)) + x_bits + y_bits
    places = [2 + len(order_two) - 1 - order_two.index(bit) for bit in reversed(order_one)]
    lifted_one = lifted.reshape((shard, SLOTS) + (2,) * len(order_two)).transpose(0, 1, *places)
    lifted_one = lifted_one.reshape(shard, SLOTS * devices)
    lifted_two = lifted.reshape(shard, SLOTS * devices)
    keep, sent = step(keep, came, z_bits[-1])
    sent, misc, gx_out, acts_out, lifted_came, lifted_one = lock(
        sent, misc, gx_out, acts_out, lifted_came, lifted_one
    )
    came = [(partner(sent, z_bits[-1]), len(keep))]
    misc = grown(misc, (x_bits + y_bits)[:-1])
    misc_came = partner(misc, y_bits[-1])
    mine, other, small_mine, small_other = finish(
        keep + two_keep, came + [(two_came, 2)], lifted_one, lifted_two, misc_two, misc, misc_came
    )
    came, small_came = swap(other), swap(small_other)
    (
        g_query, g_key, g_value, g_gate, g_out, g_decay, g_up, g_down, g_ada,
        g_b_ada, g_b_up, g_b_down, g_conv, g_b_decay,
    ) = outputs(mine, came, small_mine, small_came)

    grad_lifted = (grad_lifted + lifted_came).reshape(MICRO, SLOTS, D)
    _, pull_silu = jax.vjp(jax.nn.silu, conditions.astype(f32))
    (cond_grads,) = pull_silu(grad_lifted)

    return (
        acts_out[None],
        gx_out[None],
        cond_grads,
        g_ada[None],
        g_b_ada,
        g_query[None],
        g_key[None],
        g_value[None],
        g_gate[None],
        g_out[None],
        g_decay.transpose(1, 2, 0),
        g_b_decay,
        g_conv.transpose(1, 0, 2),
        g_up[None],
        g_b_up,
        g_down.reshape(1, FF // devices, D),
        g_b_down,
    )


def solution(mesh):
    rows = P(None, "row", None)
    mats = P("section", "row", None)
    vector = P("section", None)
    in_specs = (
        rows, rows, rows, P(None, "row"),
        mats, vector, mats, mats, mats, mats, mats, mats, vector, P("section", None, None),
        mats, vector, mats, vector,
    )
    blocks = P("section", None, "row", None)
    out_specs = (
        blocks, blocks, rows,
        mats, vector, mats, mats, mats, mats, mats, mats, vector, P("section", None, None),
        mats, vector, mats, vector,
    )
    return jax.shard_map(
        on_device, mesh=mesh, in_specs=in_specs, out_specs=out_specs, check_vma=False
    )
```

```python
import functools

import jax
import jax.numpy as jnp
from jax import lax
from jax.experimental import pallas as pl
from jax.experimental.pallas import tpu as pltpu
from jax.sharding import PartitionSpec as P

D = 384
HEADS = 6
HEAD_DIM = 64
FF = 1536
MICRO = 2
ROWS = 512
HALF = 256
SLOTS = 2
PAIR = 128
PAIRS = D // PAIR
QKVG = 4 * D
LANES = 128
GROUP = (QKVG + D + LANES) // 2
NEG = -1e30
SCALE = HEAD_DIM**-0.5

bf16 = jnp.bfloat16
f32 = jnp.float32


def mm(left, right):
    return jnp.dot(left, right, preferred_element_type=f32)


def mm_t(left, right):
    return lax.dot_general(left, right, (((1,), (1,)), ((), ())), preferred_element_type=f32)


def split(values):
    high = values.astype(bf16)
    return high, (values - high.astype(f32)).astype(bf16)


def split_three(values):
    high, rest = split(values)
    mid = values - high.astype(f32)
    middle, low = split(mid)
    return high, middle, low


def cat_left(values):
    high, low = split(values)
    return jnp.concatenate([high, low, high], axis=1)


def cat_right(values):
    high, low = split(values)
    return jnp.concatenate([high, high, low], axis=1)


def mm_near(left, right_pair, right_high):
    high, low = split(left)
    wide = mm(high, right_pair)
    return wide[:, :PAIR] + wide[:, PAIR:] + mm(low, right_high)


def lane_iota(rows, columns):
    return lax.broadcasted_iota(jnp.int32, (rows, columns), 1)


def row_iota(rows, columns):
    return lax.broadcasted_iota(jnp.int32, (rows, columns), 0)


def order_matrix(start, rows, wide, to_scan):
    t = row_iota(rows, ROWS) + start
    small = (t & 256) + ((t & 15) << 4) + ((t & 255) >> 4)
    if to_scan:
        large = ((t & 15) << 5) + (t >> 4)
    else:
        large = ((t & 31) << 4) + (t >> 5)
    source = jnp.where(wide, large, small)
    return jnp.where(lane_iota(rows, ROWS) == source, 1.0, 0.0).astype(bf16)


def normalise(values):
    centred = values - jnp.mean(values, axis=-1, keepdims=True)
    rate = lax.rsqrt(jnp.mean(centred * centred, axis=-1, keepdims=True) + 1e-06)
    return centred * rate, rate


def normalise_back(normal, rate, grad):
    return rate * (
        grad
        - jnp.mean(grad, axis=-1, keepdims=True)
        - normal * jnp.mean(grad * normal, axis=-1, keepdims=True)
    )


class In:
    def __init__(self, copy, kept):
        self.copy = copy
        self.kept = kept

    def __call__(self):
        if self.copy is not None:
            self.copy.wait()
            self.copy = None
        return self.kept


class Kernel:
    def __init__(self, layer, layouts):
        self.layer = layer
        self.section = lax.axis_index("section")
        self.own = self.section == layer
        self.layout = layouts[self.section, 0]
        self.wide = self.layout == 0
        self.live_rows = jnp.where(self.wide, ROWS, self.layout * HALF)
        self.pushed = {}

    def load(self, kind, refs, kept, sem):
        if kind == "own":
            mine, other = refs

            @pl.when(self.own)
            def _():
                pltpu.make_async_copy(mine, kept, sem).start()

            @pl.when(jnp.logical_not(self.own))
            def _():
                pltpu.make_async_copy(other, kept, sem).start()

            return In(pltpu.make_async_copy(mine, kept, sem), kept)
        (source,) = refs
        if kind == "micro":
            source = source.at[self.section if source.shape[0] == MICRO else 0]
        copy = pltpu.make_async_copy(source, kept, sem)
        copy.start()
        return In(copy, kept)

    def push(self, name):
        kept, target, sem = self.results[name]
        copy = pltpu.make_async_copy(kept, target, sem)
        copy.start()
        self.pushed[name] = copy

    def finish(self):
        for name in self.results:
            if name not in self.pushed:
                self.push(name)
        for copy in self.pushed.values():
            copy.wait()

    def slot(self, half):
        return jnp.where(self.wide, 0, half)

    def share(self, slot, part):
        row = pl.ds(2 * self.section + slot, 1)
        return self.mods()[row, part * D : (part + 1) * D]

    def bu(self):
        return self.small()[0:1, :]

    def bn(self):
        return self.small()[1:2, :D]

    def ck(self, tap):
        return self.small()[2 + tap : 3 + tap, :D]

    def bd(self):
        return self.small()[5:6, :LANES]


def sigmoid(values):
    return 1.0 / (1.0 + jnp.exp(-values))


GELU_A = 0.7978845608028654
GELU_B = 0.044715


def gelu_parts(values):
    square = values * values
    tanh = jnp.tanh(GELU_A * values * (1.0 + GELU_B * square))
    return square, tanh


def fill_bias(bias, wide):
    bias[:, :HALF] = jnp.full((HALF, HALF), 0.0, f32) + jnp.where(wide, 0.0, NEG)
    causal = row_iota(HALF, HALF) >= lane_iota(HALF, HALF)
    bias[:, HALF:] = jnp.where(causal, 0.0, NEG)


def decay_factors(cum, cumt, bias, head):
    row = cumt[pl.ds(head, 1), :]
    lanes = lane_iota(1, LANES)
    column = jnp.sum(jnp.where(lanes == head, cum[...], 0.0), axis=1, keepdims=True)
    first = jnp.exp(column[:HALF] - row[:, :HALF] + bias[:, HALF:])
    second = jnp.exp(column[HALF:] - row + bias[...])
    return first, second


def head_norm(values, lanes):
    square = values * values
    low = jnp.sum(jnp.where(lanes < HEAD_DIM, square, 0.0), axis=1, keepdims=True)
    high = jnp.sum(jnp.where(lanes < HEAD_DIM, 0.0, square), axis=1, keepdims=True)
    return jnp.where(lanes < HEAD_DIM, low, high) * (1.0 / HEAD_DIM)


def fill_decay(dp, bd, cum, cumt):
    raw = dp[...] + bd
    log_decay = (jnp.minimum(raw, 0.0) - jnp.log1p(jnp.exp(-jnp.abs(raw)))) * (1.0 / 16.0)
    high, middle, low = split_three(log_decay)
    causal = jnp.where(row_iota(ROWS, ROWS) >= lane_iota(ROWS, ROWS), 1.0, 0.0).astype(bf16)
    cum[...] = mm(causal, high) + mm(causal, middle) + mm(causal, low)
    cumt[...] = jnp.transpose(cum[...])


def columns(index, first=0):
    return slice(index * PAIR + first, index * PAIR + first + PAIR)


def attn_forward_body(k):
    flip = k.layer == 1
    wide = k.wide
    x = k.x()
    k.mods()

    def first(i, carry):
        rows = pl.ds(pl.multiple_of(i * HALF, HALF), HALF)
        slot = k.slot(i)
        normal, _ = normalise(x[rows, :].astype(f32))
        k.inner[rows, :] = (normal * (1.0 + k.share(slot, 1)) + k.share(slot, 0)).astype(bf16)
        return carry

    lax.fori_loop(0, 2, first, 0)
    w_qk = k.w_qk()
    w_vgd = k.w_vgd()

    def project(i, carry):
        start = i * HALF
        rows = pl.ds(start, HALF)
        if flip:
            part = mm(order_matrix(start, HALF, wide, True), k.inner[...]).astype(bf16)
        else:
            part = k.inner[rows, :]
        k.ordered[rows, :] = part
        k.qkvg[rows, : 2 * D] = mm(part, w_qk[...])
        k.qkvg[rows, 2 * D :] = mm(part, w_vgd[:, : 2 * D])
        k.dp[rows, :] = mm(part, w_vgd[:, 2 * D :])
        return carry

    lax.fori_loop(0, 2, project, 0)
    k.small()
    for name in ("ordered", "qkvg", "dp"):
        k.push(name)
    fill_decay(k.dp, k.bd(), k.cum, k.cumt)
    fill_bias(k.bias, wide)

    vpad = k.vpad
    vpad[0:8, :] = jnp.zeros((8, D), f32)
    vpad[8 : 8 + ROWS, :] = k.qkvg[:, 2 * D : 3 * D]
    position = row_iota(ROWS, 1) & jnp.where(wide, ROWS - 1, HALF - 1)
    one = jnp.where(position >= 1, vpad[7 : 7 + ROWS, :], 0.0)
    two = jnp.where(position >= 2, vpad[6 : 6 + ROWS, :], 0.0)
    k.vc[...] = k.ck(0) * vpad[8 : 8 + ROWS, :] + k.ck(1) * one + k.ck(2) * two
    for name in ("cum", "cumt", "vc"):
        k.push(name)

    def pair(p, carry):
        lanes = lane_iota(1, PAIR)
        queries = cat_left(k.qkvg[:, columns(p)] * SCALE)
        keys = k.qkvg[:, columns(p, D)]
        value_high, value_low = split(k.vc[:, columns(p)])
        values = jnp.concatenate([value_high, value_low], axis=1)
        parts = []
        for e in range(2):
            key_cat = cat_right(jnp.where((lanes // HEAD_DIM) == e, keys, 0.0))
            first, second = decay_factors(k.cum, k.cumt, k.bias, 2 * p + e)
            first = first * mm_t(queries[:HALF], key_cat[:HALF])
            second = second * mm_t(queries[HALF:], key_cat)
            parts.append(
                jnp.concatenate(
                    [
                        mm_near(first, values[:HALF], value_high[:HALF]),
                        mm_near(second, values, value_high),
                    ],
                    axis=0,
                )
            )
        total = jnp.where(lanes < HEAD_DIM, parts[0], parts[1])
        k.o[:, columns(p)] = total
        gate = k.qkvg[:, columns(p, 3 * D)]
        normed = total * lax.rsqrt(head_norm(total, lanes) + 1.0)
        mixed = (normed * (gate * sigmoid(gate))).astype(bf16)
        if flip:
            k.inner[:, columns(p)] = mixed
        else:
            k.gated[:, columns(p)] = mixed
        return carry

    for p in range(PAIRS):
        pair(p, 0)
    k.push("o")
    if flip:

        def back(i, carry):
            start = i * HALF
            k.gated[pl.ds(start, HALF), :] = mm(
                order_matrix(start, HALF, wide, False), k.inner[...]
            ).astype(bf16)
            return carry

        lax.fori_loop(0, 2, back, 0)


def ffn_forward_body(k):
    gated, x = k.gated(), k.x()
    k.mods(), k.small()

    def tile(i, carry):
        start = i * HALF
        rows = pl.ds(start, HALF)
        slot = k.slot(i)
        grown = mm(gated[rows, :], k.wo()[...])
        k.branch[rows, :] = grown
        middle = x[rows, :].astype(f32) + k.share(slot, 2) * grown
        normal, _ = normalise(middle)
        inner = (normal * (1.0 + k.share(slot, 4)) + k.share(slot, 3)).astype(bf16)
        up = mm(inner, k.wu()[...]) + k.bu()
        _, tanh = gelu_parts(up)
        hidden = (0.5 * up * (1.0 + tanh)).astype(bf16)
        low = mm(hidden, k.wn()[...])
        k.down[rows, :] = low
        result = middle + k.share(slot, 5) * (low + k.bn())
        live = (row_iota(HALF, 1) + start) < k.live_rows
        k.out[rows, :] = jnp.where(live, result, 0.0).astype(bf16)
        return carry

    for i in range(2):
        tile(i, 0)
    if k.layer == 1:
        k.sent[...] = jnp.where(k.section == 0, k.out[...].astype(f32), x[...].astype(f32)).astype(bf16)


def ffn_backward_body(k):
    gmod, gbu, gbn = k.gmod, k.gbu, k.gbn
    gmod[...] = jnp.zeros(gmod.shape, f32)
    gbu[...] = jnp.zeros(gbu.shape, f32)
    gbn[...] = jnp.zeros(gbn.shape, f32)
    k.mods(), k.small()
    x, grad, branch, down = k.x(), k.grad(), k.branch(), k.down()

    def tile(i, carry):
        start = i * HALF
        rows = pl.ds(start, HALF)
        slot = k.slot(i)

        def add(part, values):
            where = (pl.ds(slot, 1), slice((part - 2) * D, (part - 1) * D))
            gmod[where] = gmod[where] + jnp.sum(values, axis=0, keepdims=True)

        grown = branch[rows, :]
        middle = x[rows, :].astype(f32) + k.share(slot, 2) * grown
        normal, rate = normalise(middle)
        inner = (normal * (1.0 + k.share(slot, 4)) + k.share(slot, 3)).astype(bf16)
        k.inner_s[rows, :] = inner
        live = (row_iota(HALF, 1) + start) < k.live_rows
        above = jnp.where(live, grad[rows, :].astype(f32), 0.0)
        add(5, above * (down[rows, :] + k.bn()))
        grad_down = above * k.share(slot, 5)
        gbn[...] = gbn[...] + jnp.sum(grad_down, axis=0, keepdims=True)
        down_low = grad_down.astype(bf16)
        k.down_s[rows, :] = down_low
        up = mm(inner, k.wu()[...]) + k.bu()
        square, tanh = gelu_parts(up)
        half = 0.5 * (1.0 + tanh)
        k.hidden_s[rows, :] = (up * half).astype(bf16)
        slope = half + 0.5 * up * (1.0 - tanh * tanh) * (
            GELU_A * (1.0 + 3.0 * GELU_B * square)
        )
        grad_up = mm_t(down_low, k.wn()[...]) * slope
        gbu[...] = gbu[...] + jnp.sum(grad_up, axis=0, keepdims=True)
        up_low = grad_up.astype(bf16)
        k.up_s[rows, :] = up_low
        grad_inner = mm_t(up_low, k.wu()[...])
        add(3, grad_inner)
        add(4, grad_inner * normal)
        grad_middle = above + normalise_back(
            normal, rate, grad_inner * (1.0 + k.share(slot, 4))
        )
        k.mid_grad[rows, :] = grad_middle
        add(2, grad_middle * grown)
        k.branch_low[rows, :] = (grad_middle * k.share(slot, 2)).astype(bf16)
        return carry

    for i in range(2):
        tile(i, 0)
    k.push("mid_grad")
    k.push("branch_low")

    def weights(j, carry):
        part = pl.ds(pl.multiple_of(j * HALF, HALF), HALF)
        hidden_t = jnp.transpose(k.hidden_s[:, part].astype(f32)).astype(bf16)
        k.gwn[part, :] = mm(hidden_t, k.down_s[...])
        return carry

    lax.fori_loop(0, FF // HALF, weights, 0)
    inner_t = jnp.transpose(k.inner_s[...].astype(f32)).astype(bf16)
    if k.packed:
        devices, shard, _ = k.keep.shape

        def halves(j, carry):
            for kept, own in ((k.keep, c_section), (k.sent, 1 - c_section)):
                columns = pl.ds(pl.multiple_of(j * HALF + own * (FF // 2), HALF), HALF)
                here = pl.ds(pl.multiple_of(j * HALF, HALF), HALF)
                part = mm(inner_t, k.up_s[:, columns]).reshape(devices, shard, HALF)
                kept[:, :, here] = part.astype(kept.dtype)
            return carry

        c_section = k.section
        lax.fori_loop(0, FF // 2 // HALF, halves, 0)

        def owner(r, carry):
            for kept, own in ((k.keep, c_section), (k.sent, 1 - c_section)):
                for piece in range(2):
                    start = pl.multiple_of((4 * r + 2 * own + piece) * shard, 8)
                    rows = k.gwn[pl.ds(start, shard), :]
                    at = FF // 2 + piece * D
                    kept[r, :, at : at + D] = rows.astype(kept.dtype)
            return carry

        lax.fori_loop(0, devices, owner, 0)
        k.push("keep")
        k.push("sent")
    else:
        k.gwu[...] = mm(inner_t, k.up_s[...])
    gated = k.gated()
    k.gwo[...] = mm(jnp.transpose(gated[...].astype(f32)).astype(bf16), k.branch_low[...])

    short = jnp.concatenate([gbn[...], jnp.zeros((1, FF - D), f32)], axis=1)
    k.sums[...] = jnp.concatenate(
        [gmod[0:SLOTS, :], gbu[...], short, jnp.zeros((4, FF), f32)], axis=0
    )


def mixer_backward_body(k):
    flip = k.layer == 1
    wide = k.wide
    mixed_s, low, dv_s, rows_s, cols_s = k.mixed_s, k.low, k.dv_s, k.rows_s, k.cols_s
    fill_bias(k.bias, wide)
    branch_low, wo = k.branch_low(), k.wo()

    def first(i, carry):
        start = i * HALF
        rows = pl.ds(start, HALF)
        if flip:
            part = mm(order_matrix(start, HALF, wide, True), branch_low[...]).astype(bf16)
        else:
            part = branch_low[rows, :]
        mixed_s[rows, :] = mm_t(part, wo[...])
        return carry

    lax.fori_loop(0, 2, first, 0)
    rows_s[...] = jnp.zeros(rows_s.shape, f32)
    cols_s[...] = jnp.zeros(cols_s.shape, f32)
    qkvg, vc, cum, cumt, o = k.qkvg(), k.vc(), k.cum(), k.cumt(), k.o()
    k.small()

    def pair(p, carry):
        lanes = lane_iota(1, PAIR)
        total = o[:, columns(p)]
        gate = qkvg[:, columns(p, 3 * D)]
        above = mixed_s[:, columns(p)]
        rate = lax.rsqrt(head_norm(total, lanes) + 1.0)
        sig = sigmoid(gate)
        grad_gate = above * (total * rate) * (sig * (1.0 + gate * (1.0 - sig)))
        low[:, columns(p, 3 * D)] = grad_gate.astype(bf16)
        grad_normed = above * (gate * sig)
        product = grad_normed * total
        inside = jnp.where(
            lanes < HEAD_DIM,
            jnp.sum(jnp.where(lanes < HEAD_DIM, product, 0.0), axis=1, keepdims=True),
            jnp.sum(jnp.where(lanes < HEAD_DIM, 0.0, product), axis=1, keepdims=True),
        ) * (1.0 / HEAD_DIM)
        grad_o = rate * grad_normed - total * (rate * rate * rate) * inside

        queries = qkvg[:, columns(p)] * SCALE
        keys = qkvg[:, columns(p, D)]
        values = vc[:, columns(p)]
        query_cat = cat_left(queries)
        grad_cat = cat_left(grad_o)
        key_high, key_low = split(keys)
        key_pair = jnp.concatenate([key_high, key_low], axis=1)
        query_t = jnp.transpose(queries)
        grad_t = jnp.transpose(grad_o)
        grad_q = []
        grad_k = []
        grad_v = []
        for e in range(2):
            mine = (lanes // HEAD_DIM) == e
            head = 2 * p + e
            key_cat = cat_right(jnp.where(mine, keys, 0.0))
            value_cat = cat_right(jnp.where(mine, values, 0.0))
            first, second = decay_factors(cum, cumt, k.bias, head)
            raw_first = mm_t(query_cat[:HALF], key_cat[:HALF])
            raw_second = mm_t(query_cat[HALF:], key_cat)
            grad_first = first * mm_t(grad_cat[:HALF], value_cat[:HALF])
            grad_second = second * mm_t(grad_cat[HALF:], value_cat)
            score_first = raw_first * first
            score_second = raw_second * second
            pull_first = grad_first * raw_first
            pull_second = grad_second * raw_second
            here = lanes == head
            rows_s[:HALF, :] = rows_s[:HALF, :] + jnp.where(
                here, jnp.sum(pull_first, axis=1, keepdims=True), 0.0
            )
            rows_s[HALF:, :] = rows_s[HALF:, :] + jnp.where(
                here, jnp.sum(pull_second, axis=1, keepdims=True), 0.0
            )
            low_cols = jnp.sum(pull_second, axis=0, keepdims=True)
            cols_s[pl.ds(head, 1), :HALF] = low_cols[:, :HALF] + jnp.sum(
                pull_first, axis=0, keepdims=True
            )
            cols_s[pl.ds(head, 1), HALF:] = low_cols[:, HALF:]
            grad_q.append(
                jnp.concatenate(
                    [
                        mm_near(grad_first, key_pair[:HALF], key_high[:HALF]),
                        mm_near(grad_second, key_pair, key_high),
                    ],
                    axis=0,
                )
            )

            def turned(source_t, block_first, block_second):
                high, low = split(source_t[e * HEAD_DIM : (e + 1) * HEAD_DIM, :])
                both = jnp.concatenate([high, low], axis=0)
                first_high, first_low = split(block_first)
                second_high, second_low = split(block_second)
                one = mm(both[:, :HALF], first_high)
                one = one[:HEAD_DIM] + one[HEAD_DIM:] + mm(high[:, :HALF], first_low)
                two = mm(both[:, HALF:], second_high)
                two = two[:HEAD_DIM] + two[HEAD_DIM:] + mm(high[:, HALF:], second_low)
                return jnp.concatenate([two[:, :HALF] + one, two[:, HALF:]], axis=1)

            grad_k.append(turned(query_t, grad_first, grad_second))
            grad_v.append(turned(grad_t, score_first, score_second))
        query_grad = jnp.where(lanes < HEAD_DIM, grad_q[0], grad_q[1]) * SCALE
        low[:, columns(p)] = query_grad.astype(bf16)
        low[:, columns(p, D)] = jnp.transpose(jnp.concatenate(grad_k, axis=0)).astype(bf16)
        dv_s[:ROWS, columns(p)] = jnp.transpose(jnp.concatenate(grad_v, axis=0))
        return carry

    for p in range(PAIRS):
        pair(p, 0)

    pulled = rows_s[...] - jnp.transpose(cols_s[...])
    high, middle, rest = split_three(pulled)
    upper_first = jnp.concatenate(
        [
            jnp.where(row_iota(HALF, HALF) <= lane_iota(HALF, HALF), 1.0, 0.0),
            jnp.full((HALF, HALF), 0.0, f32) + jnp.where(wide, 1.0, 0.0),
        ],
        axis=1,
    ).astype(bf16)
    upper_second = upper_first[:, :HALF]
    later = jnp.concatenate(
        [
            mm(upper_first, high) + mm(upper_first, middle) + mm(upper_first, rest),
            mm(upper_second, high[HALF:]) + mm(upper_second, middle[HALF:])
            + mm(upper_second, rest[HALF:]),
        ],
        axis=0,
    )
    grad_dp = later * (1.0 / 16.0) * sigmoid(-(k.dp()[...] + k.bd()))
    grad_bd = jnp.sum(grad_dp, axis=0, keepdims=True)
    low[:, QKVG:] = grad_dp.astype(bf16)

    dv_s[ROWS:, :] = jnp.zeros((8, D), f32)
    position = row_iota(ROWS, 1) & jnp.where(wide, ROWS - 1, HALF - 1)
    last = jnp.where(wide, ROWS - 1, HALF - 1)
    here = dv_s[0:ROWS, :]
    one = jnp.where(position <= last - 1, dv_s[1 : 1 + ROWS, :], 0.0)
    two = jnp.where(position <= last - 2, dv_s[2 : 2 + ROWS, :], 0.0)
    value = qkvg[:, 2 * D : 3 * D]
    low[:, 2 * D : 3 * D] = (k.ck(0) * here + k.ck(1) * one + k.ck(2) * two).astype(bf16)
    k.push("low")

    taps = [jnp.sum(rows * value, axis=0, keepdims=True) for rows in (here, one, two)]
    rest = jnp.concatenate([grad_bd, jnp.zeros((1, D - LANES), f32)], axis=1)
    k.sums[...] = jnp.concatenate([*taps, rest, jnp.zeros((4, D), f32)], axis=0)

    ordered_t = jnp.transpose(k.ordered()[...].astype(f32)).astype(bf16)
    gwo = k.gwo()
    gw = k.gw

    def weights(j, carry):
        part = pl.ds(pl.multiple_of(j * HALF, HALF), HALF)
        gw[:, part] = mm(ordered_t, low[:, part])
        return carry

    lax.fori_loop(0, QKVG // HALF, weights, 0)
    gw[:, QKVG : QKVG + D] = gwo[...]
    gw[:, QKVG + D :] = mm(ordered_t, low[:, QKVG:])

    def halves(j, carry):
        here = pl.ds(pl.multiple_of(j * HALF, HALF), HALF)
        keep = pl.ds(pl.multiple_of(j * HALF + k.section * GROUP, HALF), HALF)
        send = pl.ds(pl.multiple_of(j * HALF + (1 - k.section) * GROUP, HALF), HALF)
        k.gw_keep[:, here] = gw[:, keep]
        k.gw_send[:, here] = gw[:, send].astype(bf16)
        return carry

    lax.fori_loop(0, GROUP // HALF, halves, 0)


def input_backward_body(k):
    flip = k.layer == 1
    wide = k.wide
    gmod, mixed_s, perm_s = k.gmod, k.mixed_s, k.perm_s
    gmod[...] = jnp.zeros(gmod.shape, f32)
    low, w_qk, w_vgd = k.low(), k.w_qk(), k.w_vgd()

    def inner_grad(i, carry):
        rows = pl.ds(pl.multiple_of(i * HALF, HALF), HALF)
        mixed_s[rows, :] = mm_t(low[rows, : 2 * D], w_qk[...]) + mm_t(
            low[rows, 2 * D :], w_vgd[...]
        )
        return carry

    lax.fori_loop(0, 2, inner_grad, 0)
    if flip:
        high, middle, rest = split_three(mixed_s[...])
        perm_s[:, :D] = high
        perm_s[:, D : 2 * D] = middle
        perm_s[:, 2 * D :] = rest
    x, mid_grad = k.x(), k.mid_grad()
    k.mods()

    def tile(i, carry):
        start = i * HALF
        rows = pl.ds(start, HALF)
        slot = k.slot(i)
        if flip:
            three = mm(order_matrix(start, HALF, wide, False), perm_s[...])
            grad = three[:, :D] + three[:, D : 2 * D] + three[:, 2 * D :]
        else:
            grad = mixed_s[rows, :]
        normal, rate = normalise(x[rows, :].astype(f32))
        where = (pl.ds(slot, 1), slice(0, D))
        gmod[where] = gmod[where] + jnp.sum(grad, axis=0, keepdims=True)
        where = (pl.ds(slot, 1), slice(D, 2 * D))
        gmod[where] = gmod[where] + jnp.sum(grad * normal, axis=0, keepdims=True)
        total = mid_grad[rows, :] + normalise_back(normal, rate, grad * (1.0 + k.share(slot, 1)))
        k.gx[rows, :] = total
        k.gx_low[rows, :] = total.astype(bf16)
        return carry

    for i in range(2):
        tile(i, 0)
    k.push("gx_low")
    k.push("gx")
    ffn, mixer = k.ffn_sums(), k.mixer_sums()
    k.mod_low[...] = jnp.concatenate([gmod[...], ffn[...]], axis=1).astype(bf16)
    if k.layer == 0:
        first = k.section == 0
        k.gx_send[...] = jnp.where(first, k.gx_two()[...], k.gx[...])
        one, two = k.mod_low[...].astype(f32), k.mod_two()[...].astype(f32)
        k.mod_mine[...] = jnp.where(first, one, two).astype(bf16)
        k.mod_send[...] = jnp.where(first, two, one).astype(bf16)
    half = 2 * D
    rest = ffn[0:1, :] + ffn[1:2, :]
    k.sums[...] = jnp.concatenate(
        [
            gmod[0:1, :] + gmod[1:2, :],
            rest[:, :half],
            rest[:, half:],
            ffn[2:3, :half],
            ffn[2:3, half:],
            jnp.concatenate([ffn[3:4, :D], mixer[0:1, :]], axis=1),
            jnp.concatenate([mixer[1:2, :], mixer[2:3, :]], axis=1),
            jnp.concatenate([mixer[3:4, :], jnp.zeros((1, D), f32)], axis=1),
        ],
        axis=0,
    )


ANY = pl.BlockSpec(memory_space=pl.ANY)
VMEM = pl.BlockSpec(memory_space=pltpu.VMEM)
HBM = pl.BlockSpec(memory_space=pltpu.HBM)


def call(body, layer, layouts, ins, outs, scratch, flops, packed=None, after=()):
    arrays = []
    counts = []
    kept = []
    places = []
    for kind, given, part in ins.values():
        places.extend([ANY] * 2 if kind == "own" else [HBM])
        given = given if kind == "own" else (given,)
        arrays.extend(given)
        counts.append(len(given))
        rows, wide = given[0].shape[-2:]
        start, stop = part or (0, wide)
        kept.append(pltpu.VMEM((rows, stop - start), given[0].dtype))

    def kernel(*refs):
        refs = list(refs)
        take = lambda count: [refs.pop(0) for _ in range(count)]
        (layouts_ref,) = take(1)
        sources = [take(count) for count in counts]
        take(len(after))
        targets = take(len(outs))
        buffers = take(len(ins))
        results = take(len(outs))
        rest = take(len(scratch))
        in_sems, out_sems = refs
        k = Kernel(layer, layouts_ref)
        k.packed = packed
        for number, (name, (kind, _, part)) in enumerate(ins.items()):
            given = sources[number]
            if part is not None:
                given = [ref.at[:, part[0] : part[1]] for ref in given]
            setattr(k, name, k.load(kind, given, buffers[number], in_sems.at[number]))
        k.results = {}
        for number, name in enumerate(outs):
            setattr(k, name, results[number])
            k.results[name] = (results[number], targets[number], out_sems.at[number])
        for name, ref in zip(scratch, rest):
            setattr(k, name, ref)
        body(k)
        k.finish()

    return pl.pallas_call(
        kernel,
        out_shape=[jax.ShapeDtypeStruct(shape, kind) for shape, kind, _ in outs.values()],
        in_specs=[pl.BlockSpec(memory_space=pltpu.SMEM)] + places + [ANY] * len(after),
        out_specs=[HBM if for_kernel else ANY for _, _, for_kernel in outs.values()],
        scratch_shapes=kept
        + [pltpu.VMEM(shape, kind) for shape, kind, _ in outs.values()]
        + [pltpu.VMEM(shape, kind) for shape, kind in scratch.values()]
        + [pltpu.SemaphoreType.DMA((len(ins),)), pltpu.SemaphoreType.DMA((len(outs),))],
        compiler_params=pltpu.CompilerParams(vmem_limit_bytes=56 * 1024 * 1024),
        cost_estimate=pl.CostEstimate(flops=flops, bytes_accessed=4 << 20, transcendentals=0),
    )(layouts, *arrays, *after)


def own(pair, part=None):
    return ("own", pair, part)


def plain(array):
    return ("plain", array, None)


def micro(array):
    return ("micro", array, None)


AT_UP = (0, FF)
AT_OUT = (FF, FF + D)


def attn_forward(layer, layouts, x, mods, small, qk, vgd):
    return call(
        attn_forward_body,
        layer,
        layouts,
        dict(
            x=micro(x),
            mods=own(mods),
            w_qk=own(qk),
            w_vgd=own(vgd),
            small=own(small),
        ),
        dict(
            ordered=((ROWS, D), bf16, True),
            qkvg=((ROWS, QKVG), f32, True),
            dp=((ROWS, LANES), f32, True),
            vc=((ROWS, D), f32, True),
            cum=((ROWS, LANES), f32, True),
            cumt=((LANES, ROWS), f32, True),
            o=((ROWS, D), f32, True),
            gated=((ROWS, D), bf16, True),
        ),
        dict(
            inner=((ROWS, D), bf16),
            vpad=((ROWS + 8, D), f32),
            bias=((HALF, ROWS), f32),
        ),
        8 * 10**9,
    )


def ffn_forward(layer, layouts, x, mods, small, gated, upo, down):
    return call(
        ffn_forward_body,
        layer,
        layouts,
        dict(
            gated=plain(gated),
            x=micro(x),
            wo=own(upo, AT_OUT),
            mods=own(mods),
            small=own(small),
            wu=own(upo, AT_UP),
            wn=own(down),
        ),
        dict(
            out=((ROWS, D), bf16, True),
            branch=((ROWS, D), f32, True),
            down=((ROWS, D), f32, True),
            **({"sent": ((ROWS, D), bf16, False)} if layer == 1 else {}),
        ),
        {},
        5 * 10**9,
    )


def ffn_backward(
    layer, layouts, x, mods, small, gated, branch, down_raw, grad, upo, down, devices, after=()
):
    shard = D // devices
    in_kernel = shard % 8 == 0
    if in_kernel:
        sums = dict(
            keep=((devices, shard, FF), f32, True),
            sent=((devices, shard, FF), bf16, False),
        )
    else:
        sums = dict(gwu=((D, FF), f32, False), gwn=((FF, D), f32, False))
    return call(
        ffn_backward_body,
        layer,
        layouts,
        dict(
            mods=own(mods),
            small=own(small),
            x=micro(x),
            grad=micro(grad),
            branch=plain(branch),
            down=plain(down_raw),
            wu=own(upo, AT_UP),
            wn=own(down),
            gated=plain(gated),
        ),
        dict(
            mid_grad=((ROWS, D), f32, True),
            branch_low=((ROWS, D), bf16, True),
            gwo=((D, D), f32, True),
            sums=((8, FF), f32, True),
            **sums,
        ),
        dict(
            **({"gwn": ((FF, D), f32)} if in_kernel else {}),
            hidden_s=((ROWS, FF), bf16),
            inner_s=((ROWS, D), bf16),
            up_s=((ROWS, FF), bf16),
            down_s=((ROWS, D), bf16),
            gmod=((8, FF), f32),
            gbu=((1, FF), f32),
            gbn=((1, D), f32),
        ),
        12 * 10**9,
        packed=in_kernel,
        after=after,
    )


def mixer_backward(layer, layouts, small, saved, branch_low, gwo, upo, after=()):
    ordered, qkvg, dp, vc, cum, cumt, o = saved
    return call(
        mixer_backward_body,
        layer,
        layouts,
        dict(
            branch_low=plain(branch_low),
            wo=own(upo, AT_OUT),
            qkvg=plain(qkvg),
            vc=plain(vc),
            cum=plain(cum),
            cumt=plain(cumt),
            o=plain(o),
            small=own(small),
            dp=plain(dp),
            ordered=plain(ordered),
            gwo=plain(gwo),
        ),
        dict(
            low=((ROWS, QKVG + LANES), bf16, True),
            gw_keep=((D, GROUP), f32, True),
            gw_send=((D, GROUP), bf16, False),
            sums=((8, D), f32, True),
        ),
        dict(
            mixed_s=((ROWS, D), f32),
            dv_s=((ROWS + 8, D), f32),
            rows_s=((ROWS, LANES), f32),
            cols_s=((LANES, ROWS), f32),
            bias=((HALF, ROWS), f32),
            gw=((D, 2 * GROUP), f32),
        ),
        15 * 10**9,
        after=after,
    )


def input_backward(
    layer, layouts, x, mods, low, mid_grad, ffn_sums, mixer_sums, qk, vgd, two=None, after=()
):
    extra_in, extra_out = {}, {}
    if two is not None:
        extra_in = dict(gx_two=plain(two[0]), mod_two=plain(two[1]))
        extra_out = dict(
            gx_send=((ROWS, D), f32, False),
            mod_mine=((8, 6 * D), bf16, False),
            mod_send=((8, 6 * D), bf16, False),
        )
    return call(
        input_backward_body,
        layer,
        layouts,
        dict(
            low=plain(low),
            w_qk=own(qk),
            w_vgd=own(vgd),
            x=micro(x),
            mid_grad=plain(mid_grad),
            mods=own(mods),
            ffn_sums=plain(ffn_sums),
            mixer_sums=plain(mixer_sums),
            **extra_in,
        ),
        dict(
            gx=((ROWS, D), f32, True),
            gx_low=((ROWS, D), bf16, True),
            mod_low=((8, 6 * D), bf16, True),
            sums=((8, 2 * D), f32, False),
            **extra_out,
        ),
        dict(
            mixed_s=((ROWS, D), f32),
            perm_s=((ROWS, 3 * D), bf16),
            gmod=((8, 2 * D), f32),
        ),
        4 * 10**9,
        after=after,
    )


def small_kernel(b_up, b_down, taps, b_decay, packed):
    packed[...] = jnp.zeros(packed.shape, f32)
    packed[0:1, :] = b_up[...]
    packed[1:2, :D] = b_down[...]
    packed[2:5, :D] = taps[0]
    packed[5:6, :HEADS] = b_decay[...]


def pack_small(b_up, b_down, taps, b_decay):
    return pl.pallas_call(
        small_kernel,
        out_shape=jax.ShapeDtypeStruct((8, FF), f32),
        in_specs=[VMEM] * 4,
        out_specs=VMEM,
    )(b_up, b_down, taps, b_decay)


def pack_kernel(w_query, w_key, w_value, w_gate, w_out, w_decay, w_up, qk, vgd, upo):
    qk[:, :D] = w_query[0]
    qk[:, D:] = w_key[0]
    vgd[:, :D] = w_value[0]
    vgd[:, D : 2 * D] = w_gate[0]
    place = jnp.where(row_iota(HEADS, LANES) == lane_iota(HEADS, LANES), 1.0, 0.0).astype(bf16)
    turned = lax.dot_general(
        w_decay[0], place, (((0,), (0,)), ((), ())), preferred_element_type=f32
    )
    vgd[:, 2 * D :] = turned.astype(bf16)
    upo[:, :FF] = w_up[0]
    upo[:, FF:] = w_out[0]


def pack(*weights):
    shard = weights[0].shape[1]
    widths = (2 * D, 2 * D + LANES, FF + D)
    return pl.pallas_call(
        pack_kernel,
        out_shape=[jax.ShapeDtypeStruct((shard, width), bf16) for width in widths],
        in_specs=[VMEM] * len(weights),
        out_specs=[VMEM] * len(widths),
    )(*weights)


def join_kernel(bits, waits, *refs):
    count = len(bits)
    held, came, out = refs[:count], refs[count : 2 * count], refs[2 * count + waits :]
    for i, bit in enumerate(bits):
        mine = (lax.axis_index("row") >> bit) & 1
        out[i][:, mine] = held[i][...]
        out[i][:, 1 - mine] = came[i][...]


def join(held, came, bits, after=()):
    def parts(array, bit):
        axis = axis_of(bit)
        above = 1
        for size in array.shape[:axis]:
            above *= size
        return array.reshape((above, -1) + array.shape[-2:])

    split_held = [parts(array, bit) for array, bit in zip(held, bits)]
    split_came = [parts(array, bit) for array, bit in zip(came, bits)]
    out = pl.pallas_call(
        functools.partial(join_kernel, bits, len(after)),
        out_shape=[
            jax.ShapeDtypeStruct(array.shape[:1] + (2,) + array.shape[1:], array.dtype)
            for array in split_held
        ],
        in_specs=[VMEM] * (2 * len(held)) + [ANY] * len(after),
        out_specs=[VMEM] * len(held),
        compiler_params=pltpu.CompilerParams(vmem_limit_bytes=8 * 1024 * 1024),
        cost_estimate=pl.CostEstimate(flops=10**6, bytes_accessed=10**6, transcendentals=0),
    )(*split_held, *split_came, *after)
    joined = []
    for array, result, bit in zip(held, out, bits):
        shape = list(array.shape)
        shape[axis_of(bit)] = 2
        joined.append(result.reshape(shape))
    return joined


def lifted_kernel(mine, came, ada, out, kept, sem):
    copy = pltpu.make_async_copy(ada, kept, sem)
    copy.start()
    first = lax.axis_index("section") == 0
    pair = mine[0:SLOTS, :].astype(f32), came[0:SLOTS, :].astype(f32)
    grad = jnp.concatenate(
        [jnp.where(first, pair[0], pair[1]), jnp.where(first, pair[1], pair[0])], axis=0
    ).astype(bf16)
    copy.wait()
    out[...] = mm_t(grad, kept[...])


def lifted_grads(mine, came, ada):
    return pl.pallas_call(
        lifted_kernel,
        out_shape=jax.ShapeDtypeStruct((MICRO * SLOTS, D), f32),
        in_specs=[VMEM, VMEM, ANY],
        out_specs=VMEM,
        scratch_shapes=[pltpu.VMEM((D, 6 * D), bf16), pltpu.SemaphoreType.DMA],
        compiler_params=pltpu.CompilerParams(vmem_limit_bytes=16 * 1024 * 1024),
        cost_estimate=pl.CostEstimate(flops=10**9, bytes_accessed=2 << 20, transcendentals=0),
    )(mine, came, ada)


def term_kernel(bit, *refs):
    mine = (lax.axis_index("row") >> bit) & 1
    *terms, stays, goes = refs
    stays[...] = sum(ref[:, mine] for ref in terms)
    goes[...] = sum(ref[:, 1 - mine] for ref in terms)


def term_step(bit, *terms):
    blocks = terms[0].shape[0] // 2
    paired = [term.reshape((blocks, 2) + term.shape[1:]) for term in terms]
    shape = jax.ShapeDtypeStruct((blocks,) + terms[0].shape[1:], f32)
    return pl.pallas_call(
        functools.partial(term_kernel, bit),
        out_shape=[shape] * 2,
        in_specs=[VMEM] * len(terms),
        out_specs=[VMEM] * 2,
        compiler_params=pltpu.CompilerParams(vmem_limit_bytes=8 * 1024 * 1024),
        cost_estimate=pl.CostEstimate(flops=10**6, bytes_accessed=10**6, transcendentals=0),
    )(*paired)


def step_kernel(bit, widths, counts, waits, *refs):
    mine = (lax.axis_index("row") >> bit) & 1
    count, many = len(widths), len(counts)
    refs = list(refs)
    take = lambda number: [refs.pop(0) for _ in range(number)]
    sources = take(count + many)
    take(waits)
    targets = take(count + 1)
    buffers = take(count + many)
    results = take(count + 1)
    in_sems, out_sems = refs
    arrive = [
        pltpu.make_async_copy(source, buffer, in_sems.at[i])
        for i, (source, buffer) in enumerate(zip(sources, buffers))
    ]
    leave = [
        pltpu.make_async_copy(result, target, out_sems.at[i])
        for i, (result, target) in enumerate(zip(results, targets))
    ]
    for copy in arrive:
        copy.start()
    kept, came = buffers[:count], buffers[count:]
    places = [(j, i) for j, number in enumerate(counts) for i in range(number)]
    goes = results[count]
    at = 0
    for i in range(count):
        j, place = places[i]
        arrive[i].wait()
        if place == 0:
            arrive[count + j].wait()
        start = sum(widths[i - place : i])
        columns = slice(start, start + widths[i])
        total = kept[i][:, 1 - mine] + came[j][:, 1 - mine, :, :, columns].astype(f32)
        goes[:, :, :, at : at + widths[i]] = total.astype(bf16)
        at += widths[i]
    leave[count].start()
    for i in range(count):
        j, place = places[i]
        start = sum(widths[i - place : i])
        columns = slice(start, start + widths[i])
        results[i][...] = kept[i][:, mine] + came[j][:, mine, :, :, columns].astype(f32)
        leave[i].start()
    for copy in leave:
        copy.wait()


def step(kept, came, bit, below=1, after=()):
    blocks, rows = kept[0].shape[0] // 2, kept[0].shape[1]
    above = blocks // below
    paired = lambda array: array.reshape((above, 2, below) + array.shape[1:])
    widths = [array.shape[2] for array in kept]
    size = sum(array.size for array in kept)
    arrays = [paired(array) for array in kept] + [paired(array) for array, _ in came]
    shapes = [((above, below, rows, width), f32) for width in widths]
    shapes.append(((above, below, rows, sum(widths)), bf16))
    out = pl.pallas_call(
        functools.partial(step_kernel, bit, widths, [count for _, count in came], len(after)),
        out_shape=[jax.ShapeDtypeStruct(shape, kind) for shape, kind in shapes],
        in_specs=[HBM] * len(kept) + [ANY] * (len(came) + len(after)),
        out_specs=[HBM] * len(kept) + [ANY],
        scratch_shapes=[pltpu.VMEM(array.shape, array.dtype) for array in arrays]
        + [pltpu.VMEM(shape, kind) for shape, kind in shapes]
        + [pltpu.SemaphoreType.DMA((len(arrays),)), pltpu.SemaphoreType.DMA((len(shapes),))],
        compiler_params=pltpu.CompilerParams(vmem_limit_bytes=10 * 1024 * 1024),
        cost_estimate=pl.CostEstimate(flops=size, bytes_accessed=8 * size, transcendentals=0),
    )(*arrays, *after)
    count = len(kept)
    flat_blocks = [array.reshape((blocks,) + array.shape[2:]) for array in out]
    return flat_blocks[:count], flat_blocks[count]


def misc_step_kernel(held, arrived, out):
    size = held.shape[0] - SUMS
    out[:size, :] = held[:size, :]
    out[size : 2 * size, :] = arrived[:size, :]
    high, low = split(misc_sums(held, arrived))
    out[2 * size : 2 * size + SUMS // 2, :] = high
    out[2 * size + SUMS // 2 :, :] = low


def misc_step(held, arrived):
    return pl.pallas_call(
        misc_step_kernel,
        out_shape=jax.ShapeDtypeStruct((2 * held.shape[0] - SUMS, 2 * D), bf16),
        in_specs=[VMEM] * 2,
        out_specs=VMEM,
        cost_estimate=pl.CostEstimate(flops=10**5, bytes_accessed=10**5, transcendentals=0),
    )(held, arrived)


def misc_sums(*refs):
    size = refs[0].shape[0] - SUMS
    parts = [ref[size:, :].astype(f32) for ref in refs]
    return sum(part[: SUMS // 2] + part[SUMS // 2 :] for part in parts)


SUMS = 32
OWN = 16


def misc_kernel(mod_one, mod_two, sums_one, sums_two, out):
    rows = []
    for mod in (mod_one, mod_two):
        for slot in range(SLOTS):
            for i in range(3):
                part = mod[slot : slot + 1, i * 2 * D : (i + 1) * 2 * D]
                rows.append(part.astype(f32))
        rows.append(jnp.zeros((OWN // 2 - 3 * SLOTS, 2 * D), f32))
    sums = jnp.concatenate([sums_one[...], sums_two[...]], axis=0)
    rows.extend(part.astype(f32) for part in split(sums))
    out[...] = jnp.concatenate(rows, axis=0).astype(bf16)


def pack_misc(mod_one, mod_two, sums_one, sums_two):
    return pl.pallas_call(
        misc_kernel,
        out_shape=jax.ShapeDtypeStruct((OWN + SUMS, 2 * D), bf16),
        in_specs=[VMEM] * 4,
        out_specs=VMEM,
    )(mod_one, mod_two, sums_one, sums_two)


def finish_kernel(widths, counts, waits, *refs):
    count = len(widths)
    kept, refs = refs[:count], refs[count:]
    came, refs = refs[: len(counts)], refs[len(counts) :]
    lifted, misc, misc_came = refs[:3]
    mine, other, small_mine, small_other = refs[3 + waits :]
    places = [(ref, i) for ref, many in zip(came, counts) for i in range(many)]
    added = []
    for i in range(count):
        ref, place = places[i]
        start = sum(widths[i - place : i])
        added.append(kept[i][0] + ref[0, :, start : start + widths[i]].astype(f32))
    a1, f1, f2, a2 = added
    size = misc.shape[0] - SUMS
    rows = jnp.concatenate([misc[:size, :], misc_came[:size, :]], axis=0)
    rows = rows.astype(f32).reshape(-1, OWN, 2 * D)

    def ada(first):
        columns = []
        for i in range(3):
            both = [rows[:, first + 3 * slot + i, :] for slot in range(SLOTS)]
            columns.append(mm(lifted[...], jnp.concatenate(both, axis=0).astype(bf16)))
        return jnp.concatenate(columns, axis=1)

    first = lax.axis_index("section") == 0
    at = 0
    for one, two in ((a1, a2), (f1, f2), (ada(0), ada(OWN // 2))):
        columns = slice(at, at + one.shape[1])
        mine[:, columns] = jnp.where(first, one, two)
        other[:, columns] = jnp.where(first, two, one)
        at += one.shape[1]
    total = misc_sums(misc, misc_came)
    one, two = total[0:8, :], total[8:16, :]
    small_mine[...] = jnp.where(first, one, two)
    small_other[...] = jnp.where(first, two, one)


def finish(kept, came, lifted, misc, misc_came, after):
    widths = [array.shape[2] for array in kept]
    shard = kept[0].shape[1]
    wide = GROUP + FF + 6 * D
    arrays = [array for array, _ in came]
    shapes = [(shard, wide)] * 2 + [(8, 2 * D)] * 2
    return pl.pallas_call(
        functools.partial(finish_kernel, widths, [count for _, count in came], len(after)),
        out_shape=[jax.ShapeDtypeStruct(shape, f32) for shape in shapes],
        in_specs=[VMEM] * (len(kept) + len(came) + 3) + [ANY] * len(after),
        out_specs=[VMEM] * 4,
        compiler_params=pltpu.CompilerParams(vmem_limit_bytes=8 * 1024 * 1024),
    )(*kept, *arrays, lifted, misc, misc_came, *after)


def output_kernel(mine, other, small_mine, small_other, *outs):
    first = lax.axis_index("section") == 0

    def halves(start, width):
        columns = slice(start, start + width)
        pair = mine[:, columns], other[:, columns]
        return jnp.where(first, pair[0], pair[1]), jnp.where(first, pair[1], pair[0])

    attn = halves(0, GROUP)
    cut = GROUP - 2 * D
    outs[0][...] = attn[0][:, :D]
    outs[1][...] = attn[0][:, D : 2 * D]
    outs[2][:, :cut] = attn[0][:, 2 * D :]
    outs[2][:, cut:] = attn[1][:, : D - cut]
    outs[3][...] = attn[1][:, D - cut : 2 * D - cut]
    outs[4][...] = attn[1][:, 2 * D - cut : 3 * D - cut]
    decay = jnp.transpose(attn[1][:, 3 * D - cut :])
    for head in range(HEADS):
        outs[5][head] = decay[head : head + 1, :]
    up = halves(GROUP, FF // 2)
    outs[6][:, : FF // 2] = up[0]
    outs[6][:, FF // 2 :] = up[1]
    for piece in range(2):
        down = halves(GROUP + FF // 2 + piece * D, D)
        outs[7][piece] = down[0]
        outs[7][2 + piece] = down[1]
    outs[8][...] = mine[:, GROUP + FF :] + other[:, GROUP + FF :]
    small = small_mine[...] + small_other[...]
    half = 2 * D
    for i in range(3):
        outs[9][:, i * half : (i + 1) * half] = small[i : i + 1, :]
    for i in range(2):
        outs[10][:, i * half : (i + 1) * half] = small[3 + i : 4 + i, :]
    outs[11][...] = small[5:6, :D]
    outs[12][0] = small[5:6, D:]
    outs[12][1] = small[6:7, :D]
    outs[12][2] = small[6:7, D:]
    outs[13][...] = small[7:8, :HEADS]


def outputs(mine, other, small_mine, small_other):
    shard = mine.shape[0]
    shapes = (
        [(shard, D)] * 5
        + [(HEADS, 1, shard), (shard, FF), (4, shard, D), (shard, 6 * D)]
        + [(1, 6 * D), (1, FF), (1, D), (3, 1, D), (1, HEADS)]
    )
    return pl.pallas_call(
        output_kernel,
        out_shape=[jax.ShapeDtypeStruct(shape, f32) for shape in shapes],
        in_specs=[VMEM] * 4,
        out_specs=[VMEM] * len(shapes),
    )(mine, other, small_mine, small_other)


def both_kernel(one, two, came, out, kept, sems):
    section = lax.axis_index("section")

    def move(mine, layer):
        arrive = [
            pltpu.make_async_copy(mine, kept.at[layer], sems.at[0]),
            pltpu.make_async_copy(came, kept.at[1 - layer], sems.at[1]),
        ]
        leave = [
            pltpu.make_async_copy(kept.at[layer], out.at[layer], sems.at[2]),
            pltpu.make_async_copy(kept.at[1 - layer], out.at[1 - layer], sems.at[3]),
        ]
        for copy in arrive:
            copy.start()
        for copy, after in zip(arrive, leave):
            copy.wait()
            after.start()
        for copy in leave:
            copy.wait()

    @pl.when(section == 0)
    def _():
        move(one, 0)

    @pl.when(section == 1)
    def _():
        move(two, 1)


def both_micros(one, two, came):
    return pl.pallas_call(
        both_kernel,
        out_shape=jax.ShapeDtypeStruct((MICRO,) + one.shape, one.dtype),
        in_specs=[ANY] * 3,
        out_specs=ANY,
        scratch_shapes=[
            pltpu.VMEM((MICRO,) + one.shape, one.dtype),
            pltpu.SemaphoreType.DMA((4,)),
        ],
    )(one, two, came)


def swap(values):
    return lax.ppermute(values, "section", [(0, 1), (1, 0)])


def row_bits():
    bits = lax.axis_size("row").bit_length() - 1
    third = bits // 3
    return (
        tuple(range(third)),
        tuple(range(third, 2 * third)),
        tuple(range(2 * third, bits)),
    )


def partner(values, bit):
    size = lax.axis_size("row")
    return lax.ppermute(values, "row", [(i, i ^ (1 << bit)) for i in range(size)])


def axis_of(bit):
    return lax.axis_size("row").bit_length() - 2 - bit


def bit_of(bit):
    return (lax.axis_index("row") >> bit) & 1


def single(values):
    return values.reshape((1,) * (lax.axis_size("row").bit_length() - 1) + values.shape)


def gather_steps(along_x, along_y, along_z):
    steps = [(bit, bit) for bit in reversed(along_z)]
    return steps + list(zip(along_x + along_y, along_y + along_x))


def flat(held):
    return held.reshape(-1, held.shape[-1])


def lock(*arrays):
    return lax.optimization_barrier(arrays)


def on_device(
    tokens, conditions, output_grad, layouts,
    w_ada, b_ada, w_query, w_key, w_value, w_gate, w_out, w_decay, b_decay, conv_kernel,
    w_up, b_up, w_down, b_down,
):
    section = lax.axis_index("section")
    devices = lax.axis_size("row")
    shard = w_query.shape[1]
    along_x, along_y, along_z = row_bits()

    def both(values):
        return values, swap(values)

    qk, vgd, upo = pack(
        w_query, w_key, w_value, w_gate, w_out, w_decay.transpose(0, 2, 1), w_up
    )
    small = pack_small(b_up, b_down, conv_kernel, b_decay)
    lifted_own = jax.nn.silu(conditions.astype(f32)).astype(bf16).reshape(MICRO * SLOTS, D)
    lifted_parts = lifted_own.reshape(MICRO * SLOTS, devices, shard).swapaxes(0, 1)
    lifted_cut = lax.all_to_all(lifted_parts, "row", 0, 0, tiled=True)
    product = mm(lifted_cut.reshape(devices * MICRO * SLOTS, shard), w_ada[0])
    terms = (product.reshape(devices, MICRO * SLOTS, 6 * D),)
    term_bits = along_x + along_y + along_z
    steps = gather_steps(along_x, along_y, along_z)
    lag = len(along_z)
    groups = [[single(qk), single(vgd)], [single(upo), single(w_down[0])]]
    for place in range(len(steps) + lag):
        numbers = [g for g in range(2) if 0 <= place - g * lag < len(steps)]
        bits = [bit for g in numbers for bit in steps[place - g * lag]]
        held = [array for g in numbers for array in groups[g]]
        came = [partner(array, bit) for array, bit in zip(held, bits)]
        after = (small,)
        if 0 < place <= len(term_bits):
            stays, goes = term_step(term_bits[place - 1], *terms)
            terms = (stays, partner(goes, term_bits[place - 1]))
            after = (terms[1],)
        if place == len(steps) + lag - 1:
            mods = both(sum(term[0] for term in terms) + b_ada[0])
            smalls = both(small)
            x = tokens
            *saved, gated = attn_forward(0, layouts, x, mods, smalls, qk, vgd)
            after = (gated,)
        held = join(held, came, bits, after)
        for g in numbers:
            groups[g], held = held[:2], held[2:]
        if place == len(steps) - 1:
            qk, vgd = [both(flat(array)) for array in groups[0]]
    upo, down = [both(flat(array)) for array in groups[1]]
    kept = []
    acts = []
    for l in range(2):
        if l:
            *saved, gated = attn_forward(l, layouts, x, mods, smalls, qk, vgd)
        out, branch, down_raw, *acts_sent = ffn_forward(
            l, layouts, x, mods, smalls, gated, upo, down
        )
        kept.append((x, saved, gated, branch, down_raw))
        acts.append(out)
        x = out[None]

    late, _ = lock(w_ada[0], acts[0])
    ada_all = lax.all_gather(late, "row", axis=0, tiled=True)

    def ffn_step(l, grad, after=()):
        x, saved, gated, branch, down_raw = kept[l]
        mid_grad, branch_low, gwo, sums, *terms = ffn_backward(
            l, layouts, x, mods, smalls, gated, branch, down_raw, grad, upo, down, devices, after
        )
        if terms[0].ndim == 2:
            up_sum = terms[0].reshape(devices, shard, 2, FF // 2)
            down_sum = terms[1].reshape(devices, 2, 2, shard, D)
            terms = []
            for own in (section, 1 - section):
                up_half = lax.dynamic_index_in_dim(up_sum, own, 2, keepdims=False)
                down_half = lax.dynamic_index_in_dim(down_sum, own, 1, keepdims=False)
                terms.append(
                    jnp.concatenate([up_half, down_half[:, 0], down_half[:, 1]], axis=2)
                )
            terms[1] = terms[1].astype(bf16)
        return [branch_low, gwo], mid_grad, terms[0], terms[1], sums

    def mixer_step(l, carried, after=()):
        low, keep, sent, sums = mixer_backward(
            l, layouts, smalls, kept[l][1], *carried, upo, after
        )
        by_row = lambda array: array.reshape(devices, shard, GROUP)
        return low, by_row(keep), by_row(sent), sums

    def input_step(l, low, mid_grad, ffn_sums, mixer_sums, two=None, after=()):
        x = kept[l][0]
        return input_backward(
            l, layouts, x, mods, low, mid_grad, ffn_sums, mixer_sums, qk, vgd, two, after
        )

    def run(keep, came, bits, below=1, after=()):
        for bit in bits[:-1]:
            keep, sent = step(keep, came, bit, below, after)
            came = [(partner(sent, bit), len(keep))]
        return step(keep, came, bits[-1], below, after)

    def grown(mod, bits):
        for bit in bits:
            mod = misc_step(mod, partner(mod, bit))
        return mod

    x_bits, y_bits, z_bits = along_x, along_y, along_z
    order = tuple(reversed(z_bits)) + x_bits + y_bits
    lifted = lifted_cut.reshape(devices, MICRO, SLOTS, shard)
    lifted = lax.dynamic_index_in_dim(lifted, section, 1, keepdims=False)
    for bit in order:
        pairs = lifted.reshape(-1, 2, 1 << bit, SLOTS, shard)
        pairs = jnp.where(bit_of(bit) == 0, pairs, jnp.flip(pairs, axis=1))
        lifted = pairs.reshape(devices, SLOTS, shard)
    places = [len(order) - 1 - bit for bit in reversed(order)]
    lifted = lifted.reshape((2,) * len(order) + (SLOTS, shard))
    lifted = lifted.transpose(len(order) + 1, len(order), *places)
    lifted = lifted.reshape(shard, SLOTS * devices)

    carried, mid_grad, f2_keep, f2_sent, f2_sums = ffn_step(1, output_grad)
    *carried, f2_sent, acts_sent, lifted = lock(*carried, f2_sent, acts_sent[0], lifted)
    f2_came = swap(f2_sent)
    acts_came = swap(acts_sent)
    low, a2_keep, a2_sent, m2_sums = mixer_step(1, carried)
    low, a2_sent, f2_came, acts_came = lock(low, a2_sent, f2_came, acts_came)
    a2_came = swap(a2_sent)
    gx_two, grad, mod_low_two, sums_two = input_step(1, low, mid_grad, f2_sums, m2_sums)
    grad, a2_came = lock(grad, a2_came)
    f2_keep, f2_sent = run([f2_keep], [(f2_came, 1)], x_bits)
    a2_keep, a2_sent = run([a2_keep], [(a2_came, 1)], y_bits, 1 << len(x_bits))
    grad, f2_sent, a2_sent = lock(grad, f2_sent, a2_sent)
    f2_came = partner(f2_sent, x_bits[-1])
    a2_came = partner(a2_sent, y_bits[-1])

    carried, mid_grad, f1_keep, f1_sent, f1_sums = ffn_step(0, grad[None])
    *carried, f1_sent, f2_came, a2_came = lock(*carried, f1_sent, f2_came, a2_came)
    f1_came = swap(f1_sent)
    f2_keep, f2_sent = run(f2_keep, [(f2_came, 1)], y_bits)
    a2_keep, a2_sent = run(a2_keep, [(a2_came, 1)], x_bits)
    f1_keep, f1_sent = run([f1_keep], [(f1_came, 1)], x_bits)
    *carried, f2_sent, a2_sent, f1_sent = lock(*carried, f2_sent, a2_sent, f1_sent)
    f1_came = partner(f1_sent, x_bits[-1])
    a2_came = partner(a2_sent, x_bits[-1])
    f2_came = partner(f2_sent, y_bits[-1])
    low, a1_keep, a1_sent, m1_sums = mixer_step(0, carried)
    low, a1_sent, f2_came, a2_came, f1_came, ada_all = lock(
        low, a1_sent, f2_came, a2_came, f1_came, ada_all
    )
    a1_came = swap(a1_sent)
    two_keep, two_sent = run(f2_keep + a2_keep, [(f2_came, 1), (a2_came, 1)], z_bits[:1])
    f1_keep, f1_sent = run(f1_keep, [(f1_came, 1)], y_bits)
    a1_keep, a1_sent = run([a1_keep], [(a1_came, 1)], x_bits)
    low, two_sent, f1_sent, a1_sent = lock(low, two_sent, f1_sent, a1_sent)
    a1_came = partner(a1_sent, x_bits[-1])
    f1_came = partner(f1_sent, y_bits[-1])
    two_came = partner(two_sent, z_bits[0])
    gx_one, _, mod_low_one, sums_one, gx_sent, mod_mine, mod_sent = input_step(
        0, low, mid_grad, f1_sums, m1_sums, (gx_two, mod_low_two)
    )
    misc = pack_misc(mod_low_one, mod_low_two, sums_one, sums_two)
    misc, a1_came, two_came, f1_came, gx_sent, mod_sent = lock(
        misc, a1_came, two_came, f1_came, gx_sent, mod_sent
    )

    a1_keep, a1_sent = run(a1_keep, [(a1_came, 1)], y_bits)
    two_keep, two_sent = run(two_keep, [(two_came, 2)], z_bits[1:])
    a1_sent, misc, two_sent = lock(a1_sent, misc, two_sent)
    a1_came = partner(a1_sent, y_bits[-1])
    two_came = partner(two_sent, z_bits[-1])
    misc = grown(misc, tuple(reversed(z_bits))[:-1])
    gx_came = swap(gx_sent)
    mod_came = swap(mod_sent)
    keep, came = a1_keep + f1_keep, [(a1_came, 1), (f1_came, 1)]
    for bit in z_bits[:-1]:
        keep, sent = step(keep, came, bit)
        if bit == z_bits[0]:
            sent, misc = lock(sent, misc)
        came = [(partner(sent, bit), len(keep))]
    misc = grown(misc, z_bits[:1])
    keep, sent = step(keep, came, z_bits[-1])
    sent, misc, gx_came, mod_came = lock(sent, misc, gx_came, mod_came)
    came = [(partner(sent, z_bits[-1]), len(keep))]
    misc = grown(misc, (x_bits + y_bits)[:-1])
    misc_came = partner(misc, y_bits[-1])
    gx_out = both_micros(gx_one, gx_two, gx_came)
    acts_out = both_micros(acts[0], acts[1], acts_came)
    grad_lifted = lifted_grads(mod_mine, mod_came, ada_all)
    lifted_came = swap(grad_lifted)
    mine, other, small_mine, small_other = finish(
        keep + two_keep,
        came + [(two_came, 2)],
        lifted,
        misc,
        misc_came,
        (gx_out, acts_out, lifted_came),
    )
    came, small_came = swap(other), swap(small_other)
    (
        g_query, g_key, g_value, g_gate, g_out, g_decay, g_up, g_down, g_ada,
        g_b_ada, g_b_up, g_b_down, g_conv, g_b_decay,
    ) = outputs(mine, came, small_mine, small_came)

    grad_lifted = (grad_lifted + lifted_came).reshape(MICRO, SLOTS, D)
    _, pull_silu = jax.vjp(jax.nn.silu, conditions.astype(f32))
    (cond_grads,) = pull_silu(grad_lifted)

    return (
        acts_out[None],
        gx_out[None],
        cond_grads,
        g_ada[None],
        g_b_ada,
        g_query[None],
        g_key[None],
        g_value[None],
        g_gate[None],
        g_out[None],
        g_decay.transpose(1, 2, 0),
        g_b_decay,
        g_conv.transpose(1, 0, 2),
        g_up[None],
        g_b_up,
        g_down.reshape(1, FF // devices, D),
        g_b_down,
    )


def solution(mesh):
    rows = P(None, "row", None)
    mats = P("section", "row", None)
    vector = P("section", None)
    in_specs = (
        rows, rows, rows, P(None, "row"),
        mats, vector, mats, mats, mats, mats, mats, mats, vector, P("section", None, None),
        mats, vector, mats, vector,
    )
    blocks = P("section", None, "row", None)
    out_specs = (
        blocks, blocks, rows,
        mats, vector, mats, mats, mats, mats, mats, mats, vector, P("section", None, None),
        mats, vector, mats, vector,
    )
    return jax.shard_map(
        on_device, mesh=mesh, in_specs=in_specs, out_specs=out_specs, check_vma=False
    )
```

```python
import functools

import jax
import jax.numpy as jnp
from jax import lax
from jax.experimental import pallas as pl
from jax.experimental.pallas import tpu as pltpu
from jax.sharding import PartitionSpec as P

D = 384
HEADS = 6
HEAD_DIM = 64
FF = 1536
MICRO = 2
ROWS = 512
HALF = 256
SLOTS = 2
PAIR = 128
PAIRS = D // PAIR
QKVG = 4 * D
LANES = 128
GROUP = (QKVG + D + LANES) // 2
NEG = -1e30
SCALE = HEAD_DIM**-0.5

bf16 = jnp.bfloat16
f32 = jnp.float32


def mm(left, right):
    return jnp.dot(left, right, preferred_element_type=f32)


def mm_t(left, right):
    return lax.dot_general(left, right, (((1,), (1,)), ((), ())), preferred_element_type=f32)


def split(values):
    high = values.astype(bf16)
    return high, (values - high.astype(f32)).astype(bf16)


def split_three(values):
    high, rest = split(values)
    mid = values - high.astype(f32)
    middle, low = split(mid)
    return high, middle, low


def cat_left(values):
    high, low = split(values)
    return jnp.concatenate([high, low, high], axis=1)


def cat_right(values):
    high, low = split(values)
    return jnp.concatenate([high, high, low], axis=1)


def mm_near(left, right_pair, right_high):
    high, low = split(left)
    wide = mm(high, right_pair)
    return wide[:, :PAIR] + wide[:, PAIR:] + mm(low, right_high)


def lane_iota(rows, columns):
    return lax.broadcasted_iota(jnp.int32, (rows, columns), 1)


def row_iota(rows, columns):
    return lax.broadcasted_iota(jnp.int32, (rows, columns), 0)


def order_matrix(start, rows, wide, to_scan):
    t = row_iota(rows, ROWS) + start
    small = (t & 256) + ((t & 15) << 4) + ((t & 255) >> 4)
    if to_scan:
        large = ((t & 15) << 5) + (t >> 4)
    else:
        large = ((t & 31) << 4) + (t >> 5)
    source = jnp.where(wide, large, small)
    return jnp.where(lane_iota(rows, ROWS) == source, 1.0, 0.0).astype(bf16)


def normalise(values):
    centred = values - jnp.mean(values, axis=-1, keepdims=True)
    rate = lax.rsqrt(jnp.mean(centred * centred, axis=-1, keepdims=True) + 1e-06)
    return centred * rate, rate


def normalise_back(normal, rate, grad):
    return rate * (
        grad
        - jnp.mean(grad, axis=-1, keepdims=True)
        - normal * jnp.mean(grad * normal, axis=-1, keepdims=True)
    )


class In:
    def __init__(self, copy, kept):
        self.copy = copy
        self.kept = kept

    def __call__(self):
        if self.copy is not None:
            self.copy.wait()
            self.copy = None
        return self.kept


class Kernel:
    def __init__(self, layer, layouts):
        self.layer = layer
        self.section = lax.axis_index("section")
        self.own = self.section == layer
        self.layout = layouts[self.section, 0]
        self.wide = self.layout == 0
        self.live_rows = jnp.where(self.wide, ROWS, self.layout * HALF)
        self.pushed = {}

    def load(self, kind, refs, kept, sem):
        if kind == "own":
            mine, other = refs

            @pl.when(self.own)
            def _():
                pltpu.make_async_copy(mine, kept, sem).start()

            @pl.when(jnp.logical_not(self.own))
            def _():
                pltpu.make_async_copy(other, kept, sem).start()

            return In(pltpu.make_async_copy(mine, kept, sem), kept)
        (source,) = refs
        if kind == "micro":
            source = source.at[self.section if source.shape[0] == MICRO else 0]
        copy = pltpu.make_async_copy(source, kept, sem)
        copy.start()
        return In(copy, kept)

    def push(self, name):
        kept, target, sem = self.results[name]
        copy = pltpu.make_async_copy(kept, target, sem)
        copy.start()
        self.pushed[name] = copy

    def finish(self):
        for name in self.results:
            if name not in self.pushed:
                self.push(name)
        for copy in self.pushed.values():
            copy.wait()

    def slot(self, half):
        return jnp.where(self.wide, 0, half)

    def share(self, slot, part):
        row = pl.ds(2 * self.section + slot, 1)
        return self.mods()[row, part * D : (part + 1) * D]

    def bu(self):
        return self.small()[0:1, :]

    def bn(self):
        return self.small()[1:2, :D]

    def ck(self, tap):
        return self.small()[2 + tap : 3 + tap, :D]

    def bd(self):
        return self.small()[5:6, :LANES]


def sigmoid(values):
    return 1.0 / (1.0 + jnp.exp(-values))


GELU_A = 0.7978845608028654
GELU_B = 0.044715


def gelu_parts(values):
    square = values * values
    tanh = jnp.tanh(GELU_A * values * (1.0 + GELU_B * square))
    return square, tanh


def fill_bias(bias, wide):
    bias[:, :HALF] = jnp.full((HALF, HALF), 0.0, f32) + jnp.where(wide, 0.0, NEG)
    causal = row_iota(HALF, HALF) >= lane_iota(HALF, HALF)
    bias[:, HALF:] = jnp.where(causal, 0.0, NEG)


def decay_factors(cum, cumt, bias, head):
    row = cumt[pl.ds(head, 1), :]
    lanes = lane_iota(1, LANES)
    column = jnp.sum(jnp.where(lanes == head, cum[...], 0.0), axis=1, keepdims=True)
    first = jnp.exp(column[:HALF] - row[:, :HALF] + bias[:, HALF:])
    second = jnp.exp(column[HALF:] - row + bias[...])
    return first, second


def head_norm(values, lanes):
    square = values * values
    low = jnp.sum(jnp.where(lanes < HEAD_DIM, square, 0.0), axis=1, keepdims=True)
    high = jnp.sum(jnp.where(lanes < HEAD_DIM, 0.0, square), axis=1, keepdims=True)
    return jnp.where(lanes < HEAD_DIM, low, high) * (1.0 / HEAD_DIM)


def fill_decay(dp, bd, cum, cumt):
    raw = dp[...] + bd
    log_decay = (jnp.minimum(raw, 0.0) - jnp.log1p(jnp.exp(-jnp.abs(raw)))) * (1.0 / 16.0)
    high, middle, low = split_three(log_decay)
    causal = jnp.where(row_iota(ROWS, ROWS) >= lane_iota(ROWS, ROWS), 1.0, 0.0).astype(bf16)
    cum[...] = mm(causal, high) + mm(causal, middle) + mm(causal, low)
    cumt[...] = jnp.transpose(cum[...])


def columns(index, first=0):
    return slice(index * PAIR + first, index * PAIR + first + PAIR)


def attn_forward_body(k):
    flip = k.layer == 1
    wide = k.wide
    x = k.x()
    k.mods()

    def first(i, carry):
        rows = pl.ds(pl.multiple_of(i * HALF, HALF), HALF)
        slot = k.slot(i)
        normal, _ = normalise(x[rows, :].astype(f32))
        k.inner[rows, :] = (normal * (1.0 + k.share(slot, 1)) + k.share(slot, 0)).astype(bf16)
        return carry

    lax.fori_loop(0, 2, first, 0)
    w_qk = k.w_qk()
    w_vgd = k.w_vgd()

    def project(i, carry):
        start = i * HALF
        rows = pl.ds(start, HALF)
        if flip:
            part = mm(order_matrix(start, HALF, wide, True), k.inner[...]).astype(bf16)
        else:
            part = k.inner[rows, :]
        k.ordered[rows, :] = part
        k.qkvg[rows, : 2 * D] = mm(part, w_qk[...])
        k.qkvg[rows, 2 * D :] = mm(part, w_vgd[:, : 2 * D])
        k.dp[rows, :] = mm(part, w_vgd[:, 2 * D :])
        return carry

    lax.fori_loop(0, 2, project, 0)
    k.small()
    for name in ("ordered", "qkvg", "dp"):
        k.push(name)
    fill_decay(k.dp, k.bd(), k.cum, k.cumt)
    fill_bias(k.bias, wide)

    vpad = k.vpad
    vpad[0:8, :] = jnp.zeros((8, D), f32)
    vpad[8 : 8 + ROWS, :] = k.qkvg[:, 2 * D : 3 * D]
    position = row_iota(ROWS, 1) & jnp.where(wide, ROWS - 1, HALF - 1)
    one = jnp.where(position >= 1, vpad[7 : 7 + ROWS, :], 0.0)
    two = jnp.where(position >= 2, vpad[6 : 6 + ROWS, :], 0.0)
    k.vc[...] = k.ck(0) * vpad[8 : 8 + ROWS, :] + k.ck(1) * one + k.ck(2) * two
    for name in ("cum", "cumt", "vc"):
        k.push(name)

    def pair(p, carry):
        lanes = lane_iota(1, PAIR)
        queries = cat_left(k.qkvg[:, columns(p)] * SCALE)
        keys = k.qkvg[:, columns(p, D)]
        value_high, value_low = split(k.vc[:, columns(p)])
        values = jnp.concatenate([value_high, value_low], axis=1)
        parts = []
        for e in range(2):
            key_cat = cat_right(jnp.where((lanes // HEAD_DIM) == e, keys, 0.0))
            first, second = decay_factors(k.cum, k.cumt, k.bias, 2 * p + e)
            first = first * mm_t(queries[:HALF], key_cat[:HALF])
            second = second * mm_t(queries[HALF:], key_cat)
            parts.append(
                jnp.concatenate(
                    [
                        mm_near(first, values[:HALF], value_high[:HALF]),
                        mm_near(second, values, value_high),
                    ],
                    axis=0,
                )
            )
        total = jnp.where(lanes < HEAD_DIM, parts[0], parts[1])
        k.o[:, columns(p)] = total
        gate = k.qkvg[:, columns(p, 3 * D)]
        normed = total * lax.rsqrt(head_norm(total, lanes) + 1.0)
        mixed = (normed * (gate * sigmoid(gate))).astype(bf16)
        if flip:
            k.inner[:, columns(p)] = mixed
        else:
            k.gated[:, columns(p)] = mixed
        return carry

    for p in range(PAIRS):
        pair(p, 0)
    k.push("o")
    if flip:

        def back(i, carry):
            start = i * HALF
            k.gated[pl.ds(start, HALF), :] = mm(
                order_matrix(start, HALF, wide, False), k.inner[...]
            ).astype(bf16)
            return carry

        lax.fori_loop(0, 2, back, 0)


def ffn_forward_body(k):
    gated, x = k.gated(), k.x()
    k.mods(), k.small()

    def tile(i, carry):
        start = i * HALF
        rows = pl.ds(start, HALF)
        slot = k.slot(i)
        grown = mm(gated[rows, :], k.wo()[...])
        k.branch[rows, :] = grown
        middle = x[rows, :].astype(f32) + k.share(slot, 2) * grown
        normal, _ = normalise(middle)
        inner = (normal * (1.0 + k.share(slot, 4)) + k.share(slot, 3)).astype(bf16)
        up = mm(inner, k.wu()[...]) + k.bu()
        _, tanh = gelu_parts(up)
        hidden = (0.5 * up * (1.0 + tanh)).astype(bf16)
        low = mm(hidden, k.wn()[...])
        k.down[rows, :] = low
        result = middle + k.share(slot, 5) * (low + k.bn())
        live = (row_iota(HALF, 1) + start) < k.live_rows
        k.out[rows, :] = jnp.where(live, result, 0.0).astype(bf16)
        return carry

    for i in range(2):
        tile(i, 0)
    if k.layer == 1:
        k.sent[...] = jnp.where(k.section == 0, k.out[...].astype(f32), x[...].astype(f32)).astype(bf16)


def ffn_backward_body(k):
    gmod, gbu, gbn = k.gmod, k.gbu, k.gbn
    gmod[...] = jnp.zeros(gmod.shape, f32)
    gbu[...] = jnp.zeros(gbu.shape, f32)
    gbn[...] = jnp.zeros(gbn.shape, f32)
    k.mods(), k.small()
    x, grad, branch, down = k.x(), k.grad(), k.branch(), k.down()

    def tile(i, carry):
        start = i * HALF
        rows = pl.ds(start, HALF)
        slot = k.slot(i)

        def add(part, values):
            where = (pl.ds(slot, 1), slice((part - 2) * D, (part - 1) * D))
            gmod[where] = gmod[where] + jnp.sum(values, axis=0, keepdims=True)

        grown = branch[rows, :]
        middle = x[rows, :].astype(f32) + k.share(slot, 2) * grown
        normal, rate = normalise(middle)
        inner = (normal * (1.0 + k.share(slot, 4)) + k.share(slot, 3)).astype(bf16)
        k.inner_s[rows, :] = inner
        live = (row_iota(HALF, 1) + start) < k.live_rows
        above = jnp.where(live, grad[rows, :].astype(f32), 0.0)
        add(5, above * (down[rows, :] + k.bn()))
        grad_down = above * k.share(slot, 5)
        gbn[...] = gbn[...] + jnp.sum(grad_down, axis=0, keepdims=True)
        down_low = grad_down.astype(bf16)
        k.down_s[rows, :] = down_low
        up = mm(inner, k.wu()[...]) + k.bu()
        square, tanh = gelu_parts(up)
        half = 0.5 * (1.0 + tanh)
        k.hidden_s[rows, :] = (up * half).astype(bf16)
        slope = half + 0.5 * up * (1.0 - tanh * tanh) * (
            GELU_A * (1.0 + 3.0 * GELU_B * square)
        )
        grad_up = mm_t(down_low, k.wn()[...]) * slope
        gbu[...] = gbu[...] + jnp.sum(grad_up, axis=0, keepdims=True)
        up_low = grad_up.astype(bf16)
        k.up_s[rows, :] = up_low
        grad_inner = mm_t(up_low, k.wu()[...])
        add(3, grad_inner)
        add(4, grad_inner * normal)
        grad_middle = above + normalise_back(
            normal, rate, grad_inner * (1.0 + k.share(slot, 4))
        )
        k.mid_grad[rows, :] = grad_middle
        add(2, grad_middle * grown)
        k.branch_low[rows, :] = (grad_middle * k.share(slot, 2)).astype(bf16)
        return carry

    for i in range(2):
        tile(i, 0)
    k.push("mid_grad")
    k.push("branch_low")

    def weights(j, carry):
        part = pl.ds(pl.multiple_of(j * HALF, HALF), HALF)
        hidden_t = jnp.transpose(k.hidden_s[:, part].astype(f32)).astype(bf16)
        k.gwn[part, :] = mm(hidden_t, k.down_s[...])
        return carry

    lax.fori_loop(0, FF // HALF, weights, 0)
    inner_t = jnp.transpose(k.inner_s[...].astype(f32)).astype(bf16)
    if k.packed:
        devices, shard, _ = k.keep.shape

        def halves(j, carry):
            for kept, own in ((k.keep, c_section), (k.sent, 1 - c_section)):
                columns = pl.ds(pl.multiple_of(j * HALF + own * (FF // 2), HALF), HALF)
                here = pl.ds(pl.multiple_of(j * HALF, HALF), HALF)
                part = mm(inner_t, k.up_s[:, columns]).reshape(devices, shard, HALF)
                kept[:, :, here] = part.astype(kept.dtype)
            return carry

        c_section = k.section
        lax.fori_loop(0, FF // 2 // HALF, halves, 0)

        def owner(r, carry):
            for kept, own in ((k.keep, c_section), (k.sent, 1 - c_section)):
                for piece in range(2):
                    start = pl.multiple_of((4 * r + 2 * own + piece) * shard, 8)
                    rows = k.gwn[pl.ds(start, shard), :]
                    at = FF // 2 + piece * D
                    kept[r, :, at : at + D] = rows.astype(kept.dtype)
            return carry

        lax.fori_loop(0, devices, owner, 0)
        k.push("keep")
        k.push("sent")
    else:
        k.gwu[...] = mm(inner_t, k.up_s[...])
    gated = k.gated()
    k.gwo[...] = mm(jnp.transpose(gated[...].astype(f32)).astype(bf16), k.branch_low[...])

    short = jnp.concatenate([gbn[...], jnp.zeros((1, FF - D), f32)], axis=1)
    k.sums[...] = jnp.concatenate(
        [gmod[0:SLOTS, :], gbu[...], short, jnp.zeros((4, FF), f32)], axis=0
    )


def mixer_backward_body(k):
    flip = k.layer == 1
    wide = k.wide
    mixed_s, low, dv_s, rows_s, cols_s = k.mixed_s, k.low, k.dv_s, k.rows_s, k.cols_s
    fill_bias(k.bias, wide)
    branch_low, wo = k.branch_low(), k.wo()

    def first(i, carry):
        start = i * HALF
        rows = pl.ds(start, HALF)
        if flip:
            part = mm(order_matrix(start, HALF, wide, True), branch_low[...]).astype(bf16)
        else:
            part = branch_low[rows, :]
        mixed_s[rows, :] = mm_t(part, wo[...])
        return carry

    lax.fori_loop(0, 2, first, 0)
    rows_s[...] = jnp.zeros(rows_s.shape, f32)
    cols_s[...] = jnp.zeros(cols_s.shape, f32)
    qkvg, vc, cum, cumt, o = k.qkvg(), k.vc(), k.cum(), k.cumt(), k.o()
    k.small()

    def pair(p, carry):
        lanes = lane_iota(1, PAIR)
        total = o[:, columns(p)]
        gate = qkvg[:, columns(p, 3 * D)]
        above = mixed_s[:, columns(p)]
        rate = lax.rsqrt(head_norm(total, lanes) + 1.0)
        sig = sigmoid(gate)
        grad_gate = above * (total * rate) * (sig * (1.0 + gate * (1.0 - sig)))
        low[:, columns(p, 3 * D)] = grad_gate.astype(bf16)
        grad_normed = above * (gate * sig)
        product = grad_normed * total
        inside = jnp.where(
            lanes < HEAD_DIM,
            jnp.sum(jnp.where(lanes < HEAD_DIM, product, 0.0), axis=1, keepdims=True),
            jnp.sum(jnp.where(lanes < HEAD_DIM, 0.0, product), axis=1, keepdims=True),
        ) * (1.0 / HEAD_DIM)
        grad_o = rate * grad_normed - total * (rate * rate * rate) * inside

        queries = qkvg[:, columns(p)] * SCALE
        keys = qkvg[:, columns(p, D)]
        values = vc[:, columns(p)]
        query_cat = cat_left(queries)
        grad_cat = cat_left(grad_o)
        key_high, key_low = split(keys)
        key_pair = jnp.concatenate([key_high, key_low], axis=1)
        query_t = jnp.transpose(queries)
        grad_t = jnp.transpose(grad_o)
        grad_q = []
        grad_k = []
        grad_v = []
        for e in range(2):
            mine = (lanes // HEAD_DIM) == e
            head = 2 * p + e
            key_cat = cat_right(jnp.where(mine, keys, 0.0))
            value_cat = cat_right(jnp.where(mine, values, 0.0))
            first, second = decay_factors(cum, cumt, k.bias, head)
            raw_first = mm_t(query_cat[:HALF], key_cat[:HALF])
            raw_second = mm_t(query_cat[HALF:], key_cat)
            grad_first = first * mm_t(grad_cat[:HALF], value_cat[:HALF])
            grad_second = second * mm_t(grad_cat[HALF:], value_cat)
            score_first = raw_first * first
            score_second = raw_second * second
            pull_first = grad_first * raw_first
            pull_second = grad_second * raw_second
            here = lanes == head
            rows_s[:HALF, :] = rows_s[:HALF, :] + jnp.where(
                here, jnp.sum(pull_first, axis=1, keepdims=True), 0.0
            )
            rows_s[HALF:, :] = rows_s[HALF:, :] + jnp.where(
                here, jnp.sum(pull_second, axis=1, keepdims=True), 0.0
            )
            low_cols = jnp.sum(pull_second, axis=0, keepdims=True)
            cols_s[pl.ds(head, 1), :HALF] = low_cols[:, :HALF] + jnp.sum(
                pull_first, axis=0, keepdims=True
            )
            cols_s[pl.ds(head, 1), HALF:] = low_cols[:, HALF:]
            grad_q.append(
                jnp.concatenate(
                    [
                        mm_near(grad_first, key_pair[:HALF], key_high[:HALF]),
                        mm_near(grad_second, key_pair, key_high),
                    ],
                    axis=0,
                )
            )

            def turned(source_t, block_first, block_second):
                high, low = split(source_t[e * HEAD_DIM : (e + 1) * HEAD_DIM, :])
                both = jnp.concatenate([high, low], axis=0)
                first_high, first_low = split(block_first)
                second_high, second_low = split(block_second)
                one = mm(both[:, :HALF], first_high)
                one = one[:HEAD_DIM] + one[HEAD_DIM:] + mm(high[:, :HALF], first_low)
                two = mm(both[:, HALF:], second_high)
                two = two[:HEAD_DIM] + two[HEAD_DIM:] + mm(high[:, HALF:], second_low)
                return jnp.concatenate([two[:, :HALF] + one, two[:, HALF:]], axis=1)

            grad_k.append(turned(query_t, grad_first, grad_second))
            grad_v.append(turned(grad_t, score_first, score_second))
        query_grad = jnp.where(lanes < HEAD_DIM, grad_q[0], grad_q[1]) * SCALE
        low[:, columns(p)] = query_grad.astype(bf16)
        low[:, columns(p, D)] = jnp.transpose(jnp.concatenate(grad_k, axis=0)).astype(bf16)
        dv_s[:ROWS, columns(p)] = jnp.transpose(jnp.concatenate(grad_v, axis=0))
        return carry

    for p in range(PAIRS):
        pair(p, 0)

    pulled = rows_s[...] - jnp.transpose(cols_s[...])
    high, middle, rest = split_three(pulled)
    upper_first = jnp.concatenate(
        [
            jnp.where(row_iota(HALF, HALF) <= lane_iota(HALF, HALF), 1.0, 0.0),
            jnp.full((HALF, HALF), 0.0, f32) + jnp.where(wide, 1.0, 0.0),
        ],
        axis=1,
    ).astype(bf16)
    upper_second = upper_first[:, :HALF]
    later = jnp.concatenate(
        [
            mm(upper_first, high) + mm(upper_first, middle) + mm(upper_first, rest),
            mm(upper_second, high[HALF:]) + mm(upper_second, middle[HALF:])
            + mm(upper_second, rest[HALF:]),
        ],
        axis=0,
    )
    grad_dp = later * (1.0 / 16.0) * sigmoid(-(k.dp()[...] + k.bd()))
    grad_bd = jnp.sum(grad_dp, axis=0, keepdims=True)
    low[:, QKVG:] = grad_dp.astype(bf16)

    dv_s[ROWS:, :] = jnp.zeros((8, D), f32)
    position = row_iota(ROWS, 1) & jnp.where(wide, ROWS - 1, HALF - 1)
    last = jnp.where(wide, ROWS - 1, HALF - 1)
    here = dv_s[0:ROWS, :]
    one = jnp.where(position <= last - 1, dv_s[1 : 1 + ROWS, :], 0.0)
    two = jnp.where(position <= last - 2, dv_s[2 : 2 + ROWS, :], 0.0)
    value = qkvg[:, 2 * D : 3 * D]
    low[:, 2 * D : 3 * D] = (k.ck(0) * here + k.ck(1) * one + k.ck(2) * two).astype(bf16)
    k.push("low")

    taps = [jnp.sum(rows * value, axis=0, keepdims=True) for rows in (here, one, two)]
    rest = jnp.concatenate([grad_bd, jnp.zeros((1, D - LANES), f32)], axis=1)
    k.sums[...] = jnp.concatenate([*taps, rest, jnp.zeros((4, D), f32)], axis=0)

    ordered_t = jnp.transpose(k.ordered()[...].astype(f32)).astype(bf16)
    gwo = k.gwo()
    gw = k.gw

    def weights(j, carry):
        part = pl.ds(pl.multiple_of(j * HALF, HALF), HALF)
        gw[:, part] = mm(ordered_t, low[:, part])
        return carry

    lax.fori_loop(0, QKVG // HALF, weights, 0)
    gw[:, QKVG : QKVG + D] = gwo[...]
    gw[:, QKVG + D :] = mm(ordered_t, low[:, QKVG:])

    def halves(j, carry):
        here = pl.ds(pl.multiple_of(j * HALF, HALF), HALF)
        keep = pl.ds(pl.multiple_of(j * HALF + k.section * GROUP, HALF), HALF)
        send = pl.ds(pl.multiple_of(j * HALF + (1 - k.section) * GROUP, HALF), HALF)
        k.gw_keep[:, here] = gw[:, keep]
        k.gw_send[:, here] = gw[:, send].astype(bf16)
        return carry

    lax.fori_loop(0, GROUP // HALF, halves, 0)


def input_backward_body(k):
    flip = k.layer == 1
    wide = k.wide
    gmod, mixed_s, perm_s = k.gmod, k.mixed_s, k.perm_s
    gmod[...] = jnp.zeros(gmod.shape, f32)
    low, w_qk, w_vgd = k.low(), k.w_qk(), k.w_vgd()

    def inner_grad(i, carry):
        rows = pl.ds(pl.multiple_of(i * HALF, HALF), HALF)
        mixed_s[rows, :] = mm_t(low[rows, : 2 * D], w_qk[...]) + mm_t(
            low[rows, 2 * D :], w_vgd[...]
        )
        return carry

    lax.fori_loop(0, 2, inner_grad, 0)
    if flip:
        high, middle, rest = split_three(mixed_s[...])
        perm_s[:, :D] = high
        perm_s[:, D : 2 * D] = middle
        perm_s[:, 2 * D :] = rest
    x, mid_grad = k.x(), k.mid_grad()
    k.mods()

    def tile(i, carry):
        start = i * HALF
        rows = pl.ds(start, HALF)
        slot = k.slot(i)
        if flip:
            three = mm(order_matrix(start, HALF, wide, False), perm_s[...])
            grad = three[:, :D] + three[:, D : 2 * D] + three[:, 2 * D :]
        else:
            grad = mixed_s[rows, :]
        normal, rate = normalise(x[rows, :].astype(f32))
        where = (pl.ds(slot, 1), slice(0, D))
        gmod[where] = gmod[where] + jnp.sum(grad, axis=0, keepdims=True)
        where = (pl.ds(slot, 1), slice(D, 2 * D))
        gmod[where] = gmod[where] + jnp.sum(grad * normal, axis=0, keepdims=True)
        total = mid_grad[rows, :] + normalise_back(normal, rate, grad * (1.0 + k.share(slot, 1)))
        k.gx[rows, :] = total
        k.gx_low[rows, :] = total.astype(bf16)
        return carry

    for i in range(2):
        tile(i, 0)
    k.push("gx_low")
    k.push("gx")
    ffn, mixer = k.ffn_sums(), k.mixer_sums()
    k.mod_low[...] = jnp.concatenate([gmod[...], ffn[...]], axis=1).astype(bf16)
    if k.layer == 0:
        first = k.section == 0
        k.gx_send[...] = jnp.where(first, k.gx_two()[...], k.gx[...])
        one, two = k.mod_low[...].astype(f32), k.mod_two()[...].astype(f32)
        k.mod_mine[...] = jnp.where(first, one, two).astype(bf16)
        k.mod_send[...] = jnp.where(first, two, one).astype(bf16)
    half = 2 * D
    rest = ffn[0:1, :] + ffn[1:2, :]
    k.sums[...] = jnp.concatenate(
        [
            gmod[0:1, :] + gmod[1:2, :],
            rest[:, :half],
            rest[:, half:],
            ffn[2:3, :half],
            ffn[2:3, half:],
            jnp.concatenate([ffn[3:4, :D], mixer[0:1, :]], axis=1),
            jnp.concatenate([mixer[1:2, :], mixer[2:3, :]], axis=1),
            jnp.concatenate([mixer[3:4, :], jnp.zeros((1, D), f32)], axis=1),
        ],
        axis=0,
    )


ANY = pl.BlockSpec(memory_space=pl.ANY)
VMEM = pl.BlockSpec(memory_space=pltpu.VMEM)
HBM = pl.BlockSpec(memory_space=pltpu.HBM)


def call(body, layer, layouts, ins, outs, scratch, flops, packed=None, after=()):
    arrays = []
    counts = []
    kept = []
    places = []
    for kind, given, part in ins.values():
        places.extend([ANY] * 2 if kind == "own" else [HBM])
        given = given if kind == "own" else (given,)
        arrays.extend(given)
        counts.append(len(given))
        rows, wide = given[0].shape[-2:]
        start, stop = part or (0, wide)
        kept.append(pltpu.VMEM((rows, stop - start), given[0].dtype))

    def kernel(*refs):
        refs = list(refs)
        take = lambda count: [refs.pop(0) for _ in range(count)]
        (layouts_ref,) = take(1)
        sources = [take(count) for count in counts]
        take(len(after))
        targets = take(len(outs))
        buffers = take(len(ins))
        results = take(len(outs))
        rest = take(len(scratch))
        in_sems, out_sems = refs
        k = Kernel(layer, layouts_ref)
        k.packed = packed
        for number, (name, (kind, _, part)) in enumerate(ins.items()):
            given = sources[number]
            if part is not None:
                given = [ref.at[:, part[0] : part[1]] for ref in given]
            setattr(k, name, k.load(kind, given, buffers[number], in_sems.at[number]))
        k.results = {}
        for number, name in enumerate(outs):
            setattr(k, name, results[number])
            k.results[name] = (results[number], targets[number], out_sems.at[number])
        for name, ref in zip(scratch, rest):
            setattr(k, name, ref)
        body(k)
        k.finish()

    return pl.pallas_call(
        kernel,
        out_shape=[jax.ShapeDtypeStruct(shape, kind) for shape, kind, _ in outs.values()],
        in_specs=[pl.BlockSpec(memory_space=pltpu.SMEM)] + places + [ANY] * len(after),
        out_specs=[HBM if for_kernel else ANY for _, _, for_kernel in outs.values()],
        scratch_shapes=kept
        + [pltpu.VMEM(shape, kind) for shape, kind, _ in outs.values()]
        + [pltpu.VMEM(shape, kind) for shape, kind in scratch.values()]
        + [pltpu.SemaphoreType.DMA((len(ins),)), pltpu.SemaphoreType.DMA((len(outs),))],
        compiler_params=pltpu.CompilerParams(vmem_limit_bytes=56 * 1024 * 1024),
        cost_estimate=pl.CostEstimate(flops=flops, bytes_accessed=4 << 20, transcendentals=0),
    )(layouts, *arrays, *after)


def own(pair, part=None):
    return ("own", pair, part)


def plain(array):
    return ("plain", array, None)


def micro(array):
    return ("micro", array, None)


AT_UP = (0, FF)
AT_OUT = (FF, FF + D)


def attn_forward(layer, layouts, x, mods, small, qk, vgd):
    return call(
        attn_forward_body,
        layer,
        layouts,
        dict(
            x=micro(x),
            mods=own(mods),
            w_qk=own(qk),
            w_vgd=own(vgd),
            small=own(small),
        ),
        dict(
            ordered=((ROWS, D), bf16, True),
            qkvg=((ROWS, QKVG), f32, True),
            dp=((ROWS, LANES), f32, True),
            vc=((ROWS, D), f32, True),
            cum=((ROWS, LANES), f32, True),
            cumt=((LANES, ROWS), f32, True),
            o=((ROWS, D), f32, True),
            gated=((ROWS, D), bf16, True),
        ),
        dict(
            inner=((ROWS, D), bf16),
            vpad=((ROWS + 8, D), f32),
            bias=((HALF, ROWS), f32),
        ),
        4 * 10**9,
    )


def ffn_forward(layer, layouts, x, mods, small, gated, upo, down):
    return call(
        ffn_forward_body,
        layer,
        layouts,
        dict(
            gated=plain(gated),
            x=micro(x),
            wo=own(upo, AT_OUT),
            mods=own(mods),
            small=own(small),
            wu=own(upo, AT_UP),
            wn=own(down),
        ),
        dict(
            out=((ROWS, D), bf16, True),
            branch=((ROWS, D), f32, True),
            down=((ROWS, D), f32, True),
            **({"sent": ((ROWS, D), bf16, False)} if layer == 1 else {}),
        ),
        {},
        3 * 10**9,
    )


def ffn_backward(
    layer, layouts, x, mods, small, gated, branch, down_raw, grad, upo, down, devices, after=()
):
    shard = D // devices
    in_kernel = shard % 8 == 0
    if in_kernel:
        sums = dict(
            keep=((devices, shard, FF), f32, True),
            sent=((devices, shard, FF), bf16, False),
        )
    else:
        sums = dict(gwu=((D, FF), f32, False), gwn=((FF, D), f32, False))
    return call(
        ffn_backward_body,
        layer,
        layouts,
        dict(
            mods=own(mods),
            small=own(small),
            x=micro(x),
            grad=micro(grad),
            branch=plain(branch),
            down=plain(down_raw),
            wu=own(upo, AT_UP),
            wn=own(down),
            gated=plain(gated),
        ),
        dict(
            mid_grad=((ROWS, D), f32, True),
            branch_low=((ROWS, D), bf16, True),
            gwo=((D, D), f32, True),
            sums=((8, FF), f32, True),
            **sums,
        ),
        dict(
            **({"gwn": ((FF, D), f32)} if in_kernel else {}),
            hidden_s=((ROWS, FF), bf16),
            inner_s=((ROWS, D), bf16),
            up_s=((ROWS, FF), bf16),
            down_s=((ROWS, D), bf16),
            gmod=((8, FF), f32),
            gbu=((1, FF), f32),
            gbn=((1, D), f32),
        ),
        5 * 10**9,
        packed=in_kernel,
        after=after,
    )


def mixer_backward(layer, layouts, small, saved, branch_low, gwo, upo, after=()):
    ordered, qkvg, dp, vc, cum, cumt, o = saved
    return call(
        mixer_backward_body,
        layer,
        layouts,
        dict(
            branch_low=plain(branch_low),
            wo=own(upo, AT_OUT),
            qkvg=plain(qkvg),
            vc=plain(vc),
            cum=plain(cum),
            cumt=plain(cumt),
            o=plain(o),
            small=own(small),
            dp=plain(dp),
            ordered=plain(ordered),
            gwo=plain(gwo),
        ),
        dict(
            low=((ROWS, QKVG + LANES), bf16, True),
            gw_keep=((D, GROUP), f32, True),
            gw_send=((D, GROUP), bf16, False),
            sums=((8, D), f32, True),
        ),
        dict(
            mixed_s=((ROWS, D), f32),
            dv_s=((ROWS + 8, D), f32),
            rows_s=((ROWS, LANES), f32),
            cols_s=((LANES, ROWS), f32),
            bias=((HALF, ROWS), f32),
            gw=((D, 2 * GROUP), f32),
        ),
        7 * 10**9,
        after=after,
    )


def input_backward(
    layer, layouts, x, mods, low, mid_grad, ffn_sums, mixer_sums, qk, vgd, two=None, after=()
):
    extra_in, extra_out = {}, {}
    if two is not None:
        extra_in = dict(gx_two=plain(two[0]), mod_two=plain(two[1]))
        extra_out = dict(
            gx_send=((ROWS, D), f32, False),
            mod_mine=((8, 6 * D), bf16, False),
            mod_send=((8, 6 * D), bf16, False),
        )
    return call(
        input_backward_body,
        layer,
        layouts,
        dict(
            low=plain(low),
            w_qk=own(qk),
            w_vgd=own(vgd),
            x=micro(x),
            mid_grad=plain(mid_grad),
            mods=own(mods),
            ffn_sums=plain(ffn_sums),
            mixer_sums=plain(mixer_sums),
            **extra_in,
        ),
        dict(
            gx=((ROWS, D), f32, True),
            gx_low=((ROWS, D), bf16, True),
            mod_low=((8, 6 * D), bf16, True),
            sums=((8, 2 * D), f32, False),
            **extra_out,
        ),
        dict(
            mixed_s=((ROWS, D), f32),
            perm_s=((ROWS, 3 * D), bf16),
            gmod=((8, 2 * D), f32),
        ),
        2 * 10**9,
        after=after,
    )


def small_kernel(b_up, b_down, taps, b_decay, packed):
    packed[...] = jnp.zeros(packed.shape, f32)
    packed[0:1, :] = b_up[...]
    packed[1:2, :D] = b_down[...]
    packed[2:5, :D] = taps[0]
    packed[5:6, :HEADS] = b_decay[...]


def pack_small(b_up, b_down, taps, b_decay):
    return pl.pallas_call(
        small_kernel,
        out_shape=jax.ShapeDtypeStruct((8, FF), f32),
        in_specs=[VMEM] * 4,
        out_specs=VMEM,
    )(b_up, b_down, taps, b_decay)


def pack_kernel(
    w_query, w_key, w_value, w_gate, w_out, w_decay, w_up, conditions, qk, vgd, upo, lifted
):
    qk[:, :D] = w_query[0]
    qk[:, D:] = w_key[0]
    vgd[:, :D] = w_value[0]
    vgd[:, D : 2 * D] = w_gate[0]
    place = jnp.where(row_iota(HEADS, LANES) == lane_iota(HEADS, LANES), 1.0, 0.0).astype(bf16)
    turned = lax.dot_general(
        w_decay[0], place, (((0,), (0,)), ((), ())), preferred_element_type=f32
    )
    vgd[:, 2 * D :] = turned.astype(bf16)
    upo[:, :FF] = w_up[0]
    upo[:, FF:] = w_out[0]
    values = jnp.concatenate([conditions[m].astype(f32) for m in range(MICRO)], axis=0)
    lifted[0] = (values * sigmoid(values)).astype(bf16)


def pack(*weights):
    shard = weights[0].shape[1]
    widths = (2 * D, 2 * D + LANES, FF + D)
    return pl.pallas_call(
        pack_kernel,
        out_shape=[jax.ShapeDtypeStruct((shard, width), bf16) for width in widths]
        + [jax.ShapeDtypeStruct((1, MICRO * SLOTS, D), bf16)],
        in_specs=[VMEM] * len(weights),
        out_specs=[VMEM] * (len(widths) + 1),
    )(*weights)


def join_kernel(bits, waits, *refs):
    count = len(bits)
    held, came, out = refs[:count], refs[count : 2 * count], refs[2 * count + waits :]
    for i, bit in enumerate(bits):
        mine = (lax.axis_index("row") >> bit) & 1
        out[i][:, mine] = held[i][...]
        out[i][:, 1 - mine] = came[i][...]


def join(held, came, bits, after=()):
    def parts(array, bit):
        axis = axis_of(bit)
        above = 1
        for size in array.shape[:axis]:
            above *= size
        return array.reshape((above, -1) + array.shape[-2:])

    split_held = [parts(array, bit) for array, bit in zip(held, bits)]
    split_came = [parts(array, bit) for array, bit in zip(came, bits)]
    out = pl.pallas_call(
        functools.partial(join_kernel, bits, len(after)),
        out_shape=[
            jax.ShapeDtypeStruct(array.shape[:1] + (2,) + array.shape[1:], array.dtype)
            for array in split_held
        ],
        in_specs=[VMEM] * (2 * len(held)) + [ANY] * len(after),
        out_specs=[VMEM] * len(held),
        compiler_params=pltpu.CompilerParams(vmem_limit_bytes=8 * 1024 * 1024),
        cost_estimate=pl.CostEstimate(flops=10**6, bytes_accessed=10**6, transcendentals=0),
    )(*split_held, *split_came, *after)
    joined = []
    for array, result, bit in zip(held, out, bits):
        shape = list(array.shape)
        shape[axis_of(bit)] = 2
        joined.append(result.reshape(shape))
    return joined


def lifted_kernel(mine, came, ada, out, kept, sem):
    copy = pltpu.make_async_copy(ada, kept, sem)
    copy.start()
    first = lax.axis_index("section") == 0
    pair = mine[0:SLOTS, :].astype(f32), came[0:SLOTS, :].astype(f32)
    grad = jnp.concatenate(
        [jnp.where(first, pair[0], pair[1]), jnp.where(first, pair[1], pair[0])], axis=0
    ).astype(bf16)
    copy.wait()
    out[...] = mm_t(grad, kept[...])


def lifted_grads(mine, came, ada):
    return pl.pallas_call(
        lifted_kernel,
        out_shape=jax.ShapeDtypeStruct((MICRO * SLOTS, D), f32),
        in_specs=[VMEM, VMEM, ANY],
        out_specs=VMEM,
        scratch_shapes=[pltpu.VMEM((D, 6 * D), bf16), pltpu.SemaphoreType.DMA],
        compiler_params=pltpu.CompilerParams(vmem_limit_bytes=16 * 1024 * 1024),
        cost_estimate=pl.CostEstimate(flops=10**9, bytes_accessed=2 << 20, transcendentals=0),
    )(mine, came, ada)


def term_kernel(*refs):
    *terms, stays, goes = refs
    stays[...] = sum(ref[:, 0] for ref in terms)
    goes[...] = sum(ref[:, 1] for ref in terms)


def term_step(below, *terms):
    tail = terms[0].shape[1:]
    above = terms[0].shape[0] // (2 * below)
    shape = jax.ShapeDtypeStruct((above, below) + tail, f32)
    out = pl.pallas_call(
        term_kernel,
        out_shape=[shape] * 2,
        in_specs=[VMEM] * len(terms),
        out_specs=[VMEM] * 2,
        compiler_params=pltpu.CompilerParams(vmem_limit_bytes=8 * 1024 * 1024),
        cost_estimate=pl.CostEstimate(flops=10**6, bytes_accessed=10**6, transcendentals=0),
    )(*[term.reshape((above, 2, below) + tail) for term in terms])
    return [array.reshape((above * below,) + tail) for array in out]


def step_kernel(bit, widths, counts, waits, *refs):
    mine = (lax.axis_index("row") >> bit) & 1
    count, many = len(widths), len(counts)
    refs = list(refs)
    take = lambda number: [refs.pop(0) for _ in range(number)]
    sources = take(count + many)
    take(waits)
    targets = take(count + 1)
    buffers = take(count + many)
    results = take(count + 1)
    in_sems, out_sems = refs
    arrive = [
        pltpu.make_async_copy(source, buffer, in_sems.at[i])
        for i, (source, buffer) in enumerate(zip(sources, buffers))
    ]
    leave = [
        pltpu.make_async_copy(result, target, out_sems.at[i])
        for i, (result, target) in enumerate(zip(results, targets))
    ]
    for copy in arrive:
        copy.start()
    kept, came = buffers[:count], buffers[count:]
    places = [(j, i) for j, number in enumerate(counts) for i in range(number)]
    goes = results[count]
    at = 0
    for i in range(count):
        j, place = places[i]
        arrive[i].wait()
        if place == 0:
            arrive[count + j].wait()
        start = sum(widths[i - place : i])
        columns = slice(start, start + widths[i])
        total = kept[i][:, 1 - mine] + came[j][:, 1 - mine, :, :, columns].astype(f32)
        goes[:, :, :, at : at + widths[i]] = total.astype(bf16)
        at += widths[i]
    leave[count].start()
    for i in range(count):
        j, place = places[i]
        start = sum(widths[i - place : i])
        columns = slice(start, start + widths[i])
        results[i][...] = kept[i][:, mine] + came[j][:, mine, :, :, columns].astype(f32)
        leave[i].start()
    for copy in leave:
        copy.wait()


def step(kept, came, bit, below=1, after=()):
    blocks, rows = kept[0].shape[0] // 2, kept[0].shape[1]
    above = blocks // below
    paired = lambda array: array.reshape((above, 2, below) + array.shape[1:])
    widths = [array.shape[2] for array in kept]
    size = sum(array.size for array in kept)
    arrays = [paired(array) for array in kept] + [paired(array) for array, _ in came]
    shapes = [((above, below, rows, width), f32) for width in widths]
    shapes.append(((above, below, rows, sum(widths)), bf16))
    out = pl.pallas_call(
        functools.partial(step_kernel, bit, widths, [count for _, count in came], len(after)),
        out_shape=[jax.ShapeDtypeStruct(shape, kind) for shape, kind in shapes],
        in_specs=[HBM] * len(kept) + [ANY] * (len(came) + len(after)),
        out_specs=[HBM] * len(kept) + [ANY],
        scratch_shapes=[pltpu.VMEM(array.shape, array.dtype) for array in arrays]
        + [pltpu.VMEM(shape, kind) for shape, kind in shapes]
        + [pltpu.SemaphoreType.DMA((len(arrays),)), pltpu.SemaphoreType.DMA((len(shapes),))],
        compiler_params=pltpu.CompilerParams(vmem_limit_bytes=10 * 1024 * 1024),
        cost_estimate=pl.CostEstimate(flops=size, bytes_accessed=8 * size, transcendentals=0),
    )(*arrays, *after)
    count = len(kept)
    flat_blocks = [array.reshape((blocks,) + array.shape[2:]) for array in out]
    return flat_blocks[:count], flat_blocks[count]


def misc_step_kernel(held, arrived, out):
    size = held.shape[0] - SUMS
    out[:size, :] = held[:size, :]
    out[size : 2 * size, :] = arrived[:size, :]
    high, low = split(misc_sums(held, arrived))
    out[2 * size : 2 * size + SUMS // 2, :] = high
    out[2 * size + SUMS // 2 :, :] = low


def misc_step(held, arrived):
    return pl.pallas_call(
        misc_step_kernel,
        out_shape=jax.ShapeDtypeStruct((2 * held.shape[0] - SUMS, 2 * D), bf16),
        in_specs=[VMEM] * 2,
        out_specs=VMEM,
        cost_estimate=pl.CostEstimate(flops=10**5, bytes_accessed=10**5, transcendentals=0),
    )(held, arrived)


def misc_sums(*refs):
    size = refs[0].shape[0] - SUMS
    parts = [ref[size:, :].astype(f32) for ref in refs]
    return sum(part[: SUMS // 2] + part[SUMS // 2 :] for part in parts)


SUMS = 32
OWN = 16


def misc_kernel(mod_one, mod_two, sums_one, sums_two, out):
    rows = []
    for mod in (mod_one, mod_two):
        for slot in range(SLOTS):
            for i in range(3):
                part = mod[slot : slot + 1, i * 2 * D : (i + 1) * 2 * D]
                rows.append(part.astype(f32))
        rows.append(jnp.zeros((OWN // 2 - 3 * SLOTS, 2 * D), f32))
    sums = jnp.concatenate([sums_one[...], sums_two[...]], axis=0)
    rows.extend(part.astype(f32) for part in split(sums))
    out[...] = jnp.concatenate(rows, axis=0).astype(bf16)


def pack_misc(mod_one, mod_two, sums_one, sums_two):
    return pl.pallas_call(
        misc_kernel,
        out_shape=jax.ShapeDtypeStruct((OWN + SUMS, 2 * D), bf16),
        in_specs=[VMEM] * 4,
        out_specs=VMEM,
    )(mod_one, mod_two, sums_one, sums_two)


def finish_kernel(widths, counts, waits, *refs):
    count = len(widths)
    kept, refs = refs[:count], refs[count:]
    came, refs = refs[: len(counts)], refs[len(counts) :]
    lifted, misc, misc_came = refs[:3]
    mine, other, small_mine, small_other = refs[3 + waits :]
    places = [(ref, i) for ref, many in zip(came, counts) for i in range(many)]
    added = []
    for i in range(count):
        ref, place = places[i]
        start = sum(widths[i - place : i])
        added.append(kept[i][0] + ref[0, :, start : start + widths[i]].astype(f32))
    a1, f1, f2, a2 = added
    size = misc.shape[0] - SUMS
    rows = jnp.concatenate([misc[:size, :], misc_came[:size, :]], axis=0)
    rows = rows.astype(f32).reshape(-1, OWN, 2 * D)

    def ada(first):
        columns = []
        for i in range(3):
            both = [rows[:, first + 3 * slot + i, :] for slot in range(SLOTS)]
            columns.append(mm(lifted[...], jnp.concatenate(both, axis=0).astype(bf16)))
        return jnp.concatenate(columns, axis=1)

    first = lax.axis_index("section") == 0
    at = 0
    for one, two in ((a1, a2), (f1, f2), (ada(0), ada(OWN // 2))):
        columns = slice(at, at + one.shape[1])
        mine[:, columns] = jnp.where(first, one, two)
        other[:, columns] = jnp.where(first, two, one)
        at += one.shape[1]
    total = misc_sums(misc, misc_came)
    one, two = total[0:8, :], total[8:16, :]
    small_mine[...] = jnp.where(first, one, two)
    small_other[...] = jnp.where(first, two, one)


def finish(kept, came, lifted, misc, misc_came, after):
    widths = [array.shape[2] for array in kept]
    shard = kept[0].shape[1]
    wide = GROUP + FF + 6 * D
    arrays = [array for array, _ in came]
    shapes = [(shard, wide)] * 2 + [(8, 2 * D)] * 2
    return pl.pallas_call(
        functools.partial(finish_kernel, widths, [count for _, count in came], len(after)),
        out_shape=[jax.ShapeDtypeStruct(shape, f32) for shape in shapes],
        in_specs=[VMEM] * (len(kept) + len(came) + 3) + [ANY] * len(after),
        out_specs=[VMEM] * 4,
        compiler_params=pltpu.CompilerParams(vmem_limit_bytes=8 * 1024 * 1024),
    )(*kept, *arrays, lifted, misc, misc_came, *after)


def output_kernel(mine, other, small_mine, small_other, *outs):
    first = lax.axis_index("section") == 0

    def halves(start, width):
        columns = slice(start, start + width)
        pair = mine[:, columns], other[:, columns]
        return jnp.where(first, pair[0], pair[1]), jnp.where(first, pair[1], pair[0])

    attn = halves(0, GROUP)
    cut = GROUP - 2 * D
    outs[0][...] = attn[0][:, :D]
    outs[1][...] = attn[0][:, D : 2 * D]
    outs[2][:, :cut] = attn[0][:, 2 * D :]
    outs[2][:, cut:] = attn[1][:, : D - cut]
    outs[3][...] = attn[1][:, D - cut : 2 * D - cut]
    outs[4][...] = attn[1][:, 2 * D - cut : 3 * D - cut]
    decay = jnp.transpose(attn[1][:, 3 * D - cut :])
    for head in range(HEADS):
        outs[5][head] = decay[head : head + 1, :]
    up = halves(GROUP, FF // 2)
    outs[6][:, : FF // 2] = up[0]
    outs[6][:, FF // 2 :] = up[1]
    for piece in range(2):
        down = halves(GROUP + FF // 2 + piece * D, D)
        outs[7][piece] = down[0]
        outs[7][2 + piece] = down[1]
    outs[8][...] = mine[:, GROUP + FF :] + other[:, GROUP + FF :]
    small = small_mine[...] + small_other[...]
    half = 2 * D
    for i in range(3):
        outs[9][:, i * half : (i + 1) * half] = small[i : i + 1, :]
    for i in range(2):
        outs[10][:, i * half : (i + 1) * half] = small[3 + i : 4 + i, :]
    outs[11][...] = small[5:6, :D]
    outs[12][0] = small[5:6, D:]
    outs[12][1] = small[6:7, :D]
    outs[12][2] = small[6:7, D:]
    outs[13][...] = small[7:8, :HEADS]


def outputs(mine, other, small_mine, small_other):
    shard = mine.shape[0]
    shapes = (
        [(shard, D)] * 5
        + [(HEADS, 1, shard), (shard, FF), (4, shard, D), (shard, 6 * D)]
        + [(1, 6 * D), (1, FF), (1, D), (3, 1, D), (1, HEADS)]
    )
    return pl.pallas_call(
        output_kernel,
        out_shape=[jax.ShapeDtypeStruct(shape, f32) for shape in shapes],
        in_specs=[VMEM] * 4,
        out_specs=[VMEM] * len(shapes),
    )(mine, other, small_mine, small_other)


def both_kernel(one, two, came, out, kept, sems):
    section = lax.axis_index("section")

    def move(mine, layer):
        arrive = [
            pltpu.make_async_copy(mine, kept.at[layer], sems.at[0]),
            pltpu.make_async_copy(came, kept.at[1 - layer], sems.at[1]),
        ]
        leave = [
            pltpu.make_async_copy(kept.at[layer], out.at[layer], sems.at[2]),
            pltpu.make_async_copy(kept.at[1 - layer], out.at[1 - layer], sems.at[3]),
        ]
        for copy in arrive:
            copy.start()
        for copy, after in zip(arrive, leave):
            copy.wait()
            after.start()
        for copy in leave:
            copy.wait()

    @pl.when(section == 0)
    def _():
        move(one, 0)

    @pl.when(section == 1)
    def _():
        move(two, 1)


def both_micros(one, two, came):
    return pl.pallas_call(
        both_kernel,
        out_shape=jax.ShapeDtypeStruct((MICRO,) + one.shape, one.dtype),
        in_specs=[ANY] * 3,
        out_specs=ANY,
        scratch_shapes=[
            pltpu.VMEM((MICRO,) + one.shape, one.dtype),
            pltpu.SemaphoreType.DMA((4,)),
        ],
    )(one, two, came)


def swap(values):
    return lax.ppermute(values, "section", [(0, 1), (1, 0)])


def row_bits():
    bits = lax.axis_size("row").bit_length() - 1
    third = bits // 3
    return (
        tuple(range(third)),
        tuple(range(third, 2 * third)),
        tuple(range(2 * third, bits)),
    )


def partner(values, bit):
    size = lax.axis_size("row")
    return lax.ppermute(values, "row", [(i, i ^ (1 << bit)) for i in range(size)])


def axis_of(bit):
    return lax.axis_size("row").bit_length() - 2 - bit


def bit_of(bit):
    return (lax.axis_index("row") >> bit) & 1


def single(values):
    return values.reshape((1,) * (lax.axis_size("row").bit_length() - 1) + values.shape)


def gather_steps(along_x, along_y, along_z):
    steps = [(bit, bit) for bit in reversed(along_z)]
    return steps + list(zip(along_x + along_y, along_y + along_x))


def flat(held):
    return held.reshape(-1, held.shape[-1])


def lock(*arrays):
    return lax.optimization_barrier(arrays)


def on_device(
    tokens, conditions, output_grad, layouts,
    w_ada, b_ada, w_query, w_key, w_value, w_gate, w_out, w_decay, b_decay, conv_kernel,
    w_up, b_up, w_down, b_down,
):
    section = lax.axis_index("section")
    devices = lax.axis_size("row")
    shard = w_query.shape[1]
    along_x, along_y, along_z = row_bits()

    def both(values):
        return values, swap(values)

    qk, vgd, upo, lifted = pack(
        w_query, w_key, w_value, w_gate, w_out, w_decay.transpose(0, 2, 1), w_up, conditions
    )
    small = pack_small(b_up, b_down, conv_kernel, b_decay)
    steps = gather_steps(along_x, along_y, along_z)
    lag = len(along_z)
    order = tuple(reversed(along_z)) + along_x + along_y
    term_bits = along_x + along_y + along_z
    spans = len(steps) + lag - 4
    bounds = [(len(term_bits) * i + spans // 2) // spans for i in range(spans + 1)]
    term_bits = [term_bits[bounds[i] : bounds[i + 1]] for i in range(spans)]
    left = list(order)
    groups = [[single(qk), single(vgd)], [single(upo), single(w_down[0])]]
    for place in range(len(steps) + lag):
        numbers = [g for g in range(2) if 0 <= place - g * lag < len(steps)]
        bits = [bit for g in numbers for bit in steps[place - g * lag]]
        held = [array for g in numbers for array in groups[g]]
        came = [partner(array, bit) for array, bit in zip(held, bits)]
        if place < 2:
            after = (small,)
        elif place == 2:
            for bit in order:
                lifted = jnp.concatenate([lifted, partner(lifted, bit)], axis=0)
            after = (lifted,)
        elif place < 3 + spans:
            if place == 3:
                lifted_cut = lax.dynamic_slice_in_dim(
                    lifted, lax.axis_index("row") * shard, shard, 2
                )
                product = mm(lifted_cut.reshape(devices * MICRO * SLOTS, shard), w_ada[0])
                terms = (product.reshape(devices, MICRO * SLOTS, 6 * D),)
            for bit in term_bits[place - 3]:
                stays, goes = term_step(1 << left.index(bit), *terms)
                left.remove(bit)
                terms = (stays, partner(goes, bit))
            after = (terms[1],)
        else:
            mods = both(sum(term[0] for term in terms) + b_ada[0])
            smalls = both(small)
            x = tokens
            *saved, gated = attn_forward(0, layouts, x, mods, smalls, qk, vgd)
            after = (gated,)
        held = join(held, came, bits, after)
        for g in numbers:
            groups[g], held = held[:2], held[2:]
        if place == len(steps) - 1:
            qk, vgd = [both(flat(array)) for array in groups[0]]
    upo, down = [both(flat(array)) for array in groups[1]]
    kept = []
    acts = []
    for l in range(2):
        if l:
            *saved, gated = attn_forward(l, layouts, x, mods, smalls, qk, vgd)
        out, branch, down_raw, *acts_sent = ffn_forward(
            l, layouts, x, mods, smalls, gated, upo, down
        )
        kept.append((x, saved, gated, branch, down_raw))
        acts.append(out)
        x = out[None]

    late, _ = lock(w_ada[0], acts[0])
    ada_all = lax.all_gather(late, "row", axis=0, tiled=True)

    def ffn_step(l, grad, after=()):
        x, saved, gated, branch, down_raw = kept[l]
        mid_grad, branch_low, gwo, sums, *terms = ffn_backward(
            l, layouts, x, mods, smalls, gated, branch, down_raw, grad, upo, down, devices, after
        )
        if terms[0].ndim == 2:
            up_sum = terms[0].reshape(devices, shard, 2, FF // 2)
            down_sum = terms[1].reshape(devices, 2, 2, shard, D)
            terms = []
            for own in (section, 1 - section):
                up_half = lax.dynamic_index_in_dim(up_sum, own, 2, keepdims=False)
                down_half = lax.dynamic_index_in_dim(down_sum, own, 1, keepdims=False)
                terms.append(
                    jnp.concatenate([up_half, down_half[:, 0], down_half[:, 1]], axis=2)
                )
            terms[1] = terms[1].astype(bf16)
        return [branch_low, gwo], mid_grad, terms[0], terms[1], sums

    def mixer_step(l, carried, after=()):
        low, keep, sent, sums = mixer_backward(
            l, layouts, smalls, kept[l][1], *carried, upo, after
        )
        by_row = lambda array: array.reshape(devices, shard, GROUP)
        return low, by_row(keep), by_row(sent), sums

    def input_step(l, low, mid_grad, ffn_sums, mixer_sums, two=None, after=()):
        x = kept[l][0]
        return input_backward(
            l, layouts, x, mods, low, mid_grad, ffn_sums, mixer_sums, qk, vgd, two, after
        )

    def run(keep, came, bits, below=1, after=()):
        for bit in bits[:-1]:
            keep, sent = step(keep, came, bit, below, after)
            came = [(partner(sent, bit), len(keep))]
        return step(keep, came, bits[-1], below, after)

    def grown(mod, bits):
        for bit in bits:
            mod = misc_step(mod, partner(mod, bit))
        return mod

    x_bits, y_bits, z_bits = along_x, along_y, along_z
    lifted = lifted_cut.reshape(devices, MICRO, SLOTS, shard)
    lifted = lax.dynamic_index_in_dim(lifted, section, 1, keepdims=False)
    lifted = lifted.transpose(2, 1, 0).reshape(shard, SLOTS * devices)

    carried, mid_grad, f2_keep, f2_sent, f2_sums = ffn_step(1, output_grad)
    *carried, f2_sent, acts_sent, lifted = lock(*carried, f2_sent, acts_sent[0], lifted)
    f2_came = swap(f2_sent)
    acts_came = swap(acts_sent)
    low, a2_keep, a2_sent, m2_sums = mixer_step(1, carried)
    low, a2_sent, f2_came, acts_came = lock(low, a2_sent, f2_came, acts_came)
    a2_came = swap(a2_sent)
    gx_two, grad, mod_low_two, sums_two = input_step(1, low, mid_grad, f2_sums, m2_sums)
    grad, a2_came = lock(grad, a2_came)
    f2_keep, f2_sent = run([f2_keep], [(f2_came, 1)], x_bits)
    a2_keep, a2_sent = run([a2_keep], [(a2_came, 1)], y_bits, 1 << len(x_bits))
    grad, f2_sent, a2_sent = lock(grad, f2_sent, a2_sent)
    f2_came = partner(f2_sent, x_bits[-1])
    a2_came = partner(a2_sent, y_bits[-1])

    carried, mid_grad, f1_keep, f1_sent, f1_sums = ffn_step(0, grad[None])
    *carried, f1_sent, f2_came, a2_came = lock(*carried, f1_sent, f2_came, a2_came)
    f1_came = swap(f1_sent)
    f2_keep, f2_sent = run(f2_keep, [(f2_came, 1)], y_bits)
    a2_keep, a2_sent = run(a2_keep, [(a2_came, 1)], x_bits)
    f1_keep, f1_sent = run([f1_keep], [(f1_came, 1)], x_bits)
    *carried, f2_sent, a2_sent, f1_sent = lock(*carried, f2_sent, a2_sent, f1_sent)
    f1_came = partner(f1_sent, x_bits[-1])
    a2_came = partner(a2_sent, x_bits[-1])
    f2_came = partner(f2_sent, y_bits[-1])
    low, a1_keep, a1_sent, m1_sums = mixer_step(0, carried)
    low, a1_sent, f2_came, a2_came, f1_came, ada_all = lock(
        low, a1_sent, f2_came, a2_came, f1_came, ada_all
    )
    a1_came = swap(a1_sent)
    two_keep, two_sent = run(f2_keep + a2_keep, [(f2_came, 1), (a2_came, 1)], z_bits[:1])
    f1_keep, f1_sent = run(f1_keep, [(f1_came, 1)], y_bits)
    a1_keep, a1_sent = run([a1_keep], [(a1_came, 1)], x_bits)
    low, two_sent, f1_sent, a1_sent = lock(low, two_sent, f1_sent, a1_sent)
    a1_came = partner(a1_sent, x_bits[-1])
    f1_came = partner(f1_sent, y_bits[-1])
    two_came = partner(two_sent, z_bits[0])
    gx_one, _, mod_low_one, sums_one, gx_sent, mod_mine, mod_sent = input_step(
        0, low, mid_grad, f1_sums, m1_sums, (gx_two, mod_low_two)
    )
    misc = pack_misc(mod_low_one, mod_low_two, sums_one, sums_two)
    misc, a1_came, two_came, f1_came, gx_sent, mod_sent = lock(
        misc, a1_came, two_came, f1_came, gx_sent, mod_sent
    )

    a1_keep, a1_sent = run(a1_keep, [(a1_came, 1)], y_bits)
    a1_sent, misc = lock(a1_sent, misc)
    a1_came = partner(a1_sent, y_bits[-1])
    misc = grown(misc, tuple(reversed(z_bits))[:-1])
    gx_came = swap(gx_sent)
    mod_came = swap(mod_sent)
    keep, came = a1_keep + f1_keep, [(a1_came, 1), (f1_came, 1)]
    for place, bit in enumerate(z_bits):
        if place == 1:
            keep, came = keep + two_keep, came + [(two_came, 2)]
        keep, sent = step(keep, came, bit)
        if place == len(z_bits) - 1:
            sent, misc, gx_came, mod_came = lock(sent, misc, gx_came, mod_came)
        elif place == 0:
            sent, misc = lock(sent, misc)
        came = [(partner(sent, bit), len(keep))]
        if place == 0:
            misc = grown(misc, z_bits[:1] + (x_bits + y_bits)[:-1])
    misc_came = partner(misc, y_bits[-1])
    gx_out = both_micros(gx_one, gx_two, gx_came)
    acts_out = both_micros(acts[0], acts[1], acts_came)
    grad_lifted = lifted_grads(mod_mine, mod_came, ada_all)
    lifted_came = swap(grad_lifted)
    mine, other, small_mine, small_other = finish(
        keep, came, lifted, misc, misc_came, (gx_out, acts_out, lifted_came)
    )
    came, small_came = swap(other), swap(small_other)
    (
        g_query, g_key, g_value, g_gate, g_out, g_decay, g_up, g_down, g_ada,
        g_b_ada, g_b_up, g_b_down, g_conv, g_b_decay,
    ) = outputs(mine, came, small_mine, small_came)

    grad_lifted = (grad_lifted + lifted_came).reshape(MICRO, SLOTS, D)
    _, pull_silu = jax.vjp(jax.nn.silu, conditions.astype(f32))
    (cond_grads,) = pull_silu(grad_lifted)

    return (
        acts_out[None],
        gx_out[None],
        cond_grads,
        g_ada[None],
        g_b_ada,
        g_query[None],
        g_key[None],
        g_value[None],
        g_gate[None],
        g_out[None],
        g_decay.transpose(1, 2, 0),
        g_b_decay,
        g_conv.transpose(1, 0, 2),
        g_up[None],
        g_b_up,
        g_down.reshape(1, FF // devices, D),
        g_b_down,
    )


def solution(mesh):
    rows = P(None, "row", None)
    mats = P("section", "row", None)
    vector = P("section", None)
    in_specs = (
        rows, rows, rows, P(None, "row"),
        mats, vector, mats, mats, mats, mats, mats, mats, vector, P("section", None, None),
        mats, vector, mats, vector,
    )
    blocks = P("section", None, "row", None)
    out_specs = (
        blocks, blocks, rows,
        mats, vector, mats, mats, mats, mats, mats, mats, vector, P("section", None, None),
        mats, vector, mats, vector,
    )
    return jax.shard_map(
        on_device, mesh=mesh, in_specs=in_specs, out_specs=out_specs, check_vma=False
    )
```

```python
import functools

import jax
import jax.numpy as jnp
from jax import lax
from jax.experimental import pallas as pl
from jax.experimental.pallas import tpu as pltpu
from jax.sharding import PartitionSpec as P

D = 384
HEADS = 6
HEAD_DIM = 64
FF = 1536
MICRO = 2
ROWS = 512
HALF = 256
SLOTS = 2
PAIR = 128
PAIRS = D // PAIR
QKVG = 4 * D
LANES = 128
GROUP = (QKVG + D + LANES) // 2
NEG = -1e30
SCALE = HEAD_DIM**-0.5

bf16 = jnp.bfloat16
f32 = jnp.float32


def mm(left, right):
    return jnp.dot(left, right, preferred_element_type=f32)


def mm_t(left, right):
    return lax.dot_general(left, right, (((1,), (1,)), ((), ())), preferred_element_type=f32)


def split(values):
    high = values.astype(bf16)
    return high, (values - high.astype(f32)).astype(bf16)


def split_three(values):
    high, rest = split(values)
    mid = values - high.astype(f32)
    middle, low = split(mid)
    return high, middle, low


def cat_left(values):
    high, low = split(values)
    return jnp.concatenate([high, low, high], axis=1)


def cat_right(values):
    high, low = split(values)
    return jnp.concatenate([high, high, low], axis=1)


def mm_near(left, right_pair, right_high):
    high, low = split(left)
    wide = mm(high, right_pair)
    return wide[:, :PAIR] + wide[:, PAIR:] + mm(low, right_high)


def lane_iota(rows, columns):
    return lax.broadcasted_iota(jnp.int32, (rows, columns), 1)


def row_iota(rows, columns):
    return lax.broadcasted_iota(jnp.int32, (rows, columns), 0)


def order_matrix(start, rows, wide, to_scan):
    t = row_iota(rows, ROWS) + start
    small = (t & 256) + ((t & 15) << 4) + ((t & 255) >> 4)
    if to_scan:
        large = ((t & 15) << 5) + (t >> 4)
    else:
        large = ((t & 31) << 4) + (t >> 5)
    source = jnp.where(wide, large, small)
    return jnp.where(lane_iota(rows, ROWS) == source, 1.0, 0.0).astype(bf16)


def normalise(values):
    centred = values - jnp.mean(values, axis=-1, keepdims=True)
    rate = lax.rsqrt(jnp.mean(centred * centred, axis=-1, keepdims=True) + 1e-06)
    return centred * rate, rate


def normalise_back(normal, rate, grad):
    return rate * (
        grad
        - jnp.mean(grad, axis=-1, keepdims=True)
        - normal * jnp.mean(grad * normal, axis=-1, keepdims=True)
    )


class In:
    def __init__(self, copy, kept):
        self.copy = copy
        self.kept = kept

    def __call__(self):
        if self.copy is not None:
            self.copy.wait()
            self.copy = None
        return self.kept


class Kernel:
    def __init__(self, layer, layouts):
        self.layer = layer
        self.section = lax.axis_index("section")
        self.own = self.section == layer
        self.layout = layouts[self.section, 0]
        self.wide = self.layout == 0
        self.live_rows = jnp.where(self.wide, ROWS, self.layout * HALF)
        self.pushed = {}

    def load(self, kind, refs, kept, sem):
        if kind == "own":
            mine, other = refs

            @pl.when(self.own)
            def _():
                pltpu.make_async_copy(mine, kept, sem).start()

            @pl.when(jnp.logical_not(self.own))
            def _():
                pltpu.make_async_copy(other, kept, sem).start()

            return In(pltpu.make_async_copy(mine, kept, sem), kept)
        (source,) = refs
        if kind == "micro":
            source = source.at[self.section if source.shape[0] == MICRO else 0]
        copy = pltpu.make_async_copy(source, kept, sem)
        copy.start()
        return In(copy, kept)

    def push(self, name):
        kept, target, sem = self.results[name]
        copy = pltpu.make_async_copy(kept, target, sem)
        copy.start()
        self.pushed[name] = copy

    def finish(self):
        for name in self.results:
            if name not in self.pushed:
                self.push(name)
        for copy in self.pushed.values():
            copy.wait()

    def slot(self, half):
        return jnp.where(self.wide, 0, half)

    def share(self, slot, part):
        row = pl.ds(2 * self.section + slot, 1)
        return self.mods()[row, part * D : (part + 1) * D]

    def bu(self):
        return self.small()[0:1, :]

    def bn(self):
        return self.small()[1:2, :D]

    def ck(self, tap):
        return self.small()[2 + tap : 3 + tap, :D]

    def bd(self):
        return self.small()[5:6, :LANES]


def sigmoid(values):
    return 1.0 / (1.0 + jnp.exp(-values))


GELU_A = 0.7978845608028654
GELU_B = 0.044715


def gelu_parts(values):
    square = values * values
    tanh = jnp.tanh(GELU_A * values * (1.0 + GELU_B * square))
    return square, tanh


def fill_bias(bias, wide):
    bias[:, :HALF] = jnp.full((HALF, HALF), 0.0, f32) + jnp.where(wide, 0.0, NEG)
    causal = row_iota(HALF, HALF) >= lane_iota(HALF, HALF)
    bias[:, HALF:] = jnp.where(causal, 0.0, NEG)


def decay_factors(cum, cumt, bias, head):
    row = cumt[pl.ds(head, 1), :]
    lanes = lane_iota(1, LANES)
    column = jnp.sum(jnp.where(lanes == head, cum[...], 0.0), axis=1, keepdims=True)
    first = jnp.exp(column[:HALF] - row[:, :HALF] + bias[:, HALF:])
    second = jnp.exp(column[HALF:] - row + bias[...])
    return first, second


def head_norm(values, lanes):
    square = values * values
    low = jnp.sum(jnp.where(lanes < HEAD_DIM, square, 0.0), axis=1, keepdims=True)
    high = jnp.sum(jnp.where(lanes < HEAD_DIM, 0.0, square), axis=1, keepdims=True)
    return jnp.where(lanes < HEAD_DIM, low, high) * (1.0 / HEAD_DIM)


def fill_decay(dp, bd, cum, cumt):
    raw = dp[...] + bd
    log_decay = (jnp.minimum(raw, 0.0) - jnp.log1p(jnp.exp(-jnp.abs(raw)))) * (1.0 / 16.0)
    high, middle, low = split_three(log_decay)
    causal = jnp.where(row_iota(ROWS, ROWS) >= lane_iota(ROWS, ROWS), 1.0, 0.0).astype(bf16)
    cum[...] = mm(causal, high) + mm(causal, middle) + mm(causal, low)
    cumt[...] = jnp.transpose(cum[...])


def columns(index, first=0):
    return slice(index * PAIR + first, index * PAIR + first + PAIR)


def attn_forward_body(k):
    flip = k.layer == 1
    wide = k.wide
    x = k.x()
    k.mods()

    def first(i, carry):
        rows = pl.ds(pl.multiple_of(i * HALF, HALF), HALF)
        slot = k.slot(i)
        normal, _ = normalise(x[rows, :].astype(f32))
        k.inner[rows, :] = (normal * (1.0 + k.share(slot, 1)) + k.share(slot, 0)).astype(bf16)
        return carry

    lax.fori_loop(0, 2, first, 0)
    w_qk = k.w_qk()
    w_vgd = k.w_vgd()

    def project(i, carry):
        start = i * HALF
        rows = pl.ds(start, HALF)
        if flip:
            part = mm(order_matrix(start, HALF, wide, True), k.inner[...]).astype(bf16)
        else:
            part = k.inner[rows, :]
        k.ordered[rows, :] = part
        k.qkvg[rows, : 2 * D] = mm(part, w_qk[...])
        k.qkvg[rows, 2 * D :] = mm(part, w_vgd[:, : 2 * D])
        k.dp[rows, :] = mm(part, w_vgd[:, 2 * D :])
        return carry

    lax.fori_loop(0, 2, project, 0)
    k.small()
    for name in ("ordered", "qkvg", "dp"):
        k.push(name)
    fill_decay(k.dp, k.bd(), k.cum, k.cumt)
    fill_bias(k.bias, wide)

    vpad = k.vpad
    vpad[0:8, :] = jnp.zeros((8, D), f32)
    vpad[8 : 8 + ROWS, :] = k.qkvg[:, 2 * D : 3 * D]
    position = row_iota(ROWS, 1) & jnp.where(wide, ROWS - 1, HALF - 1)
    one = jnp.where(position >= 1, vpad[7 : 7 + ROWS, :], 0.0)
    two = jnp.where(position >= 2, vpad[6 : 6 + ROWS, :], 0.0)
    k.vc[...] = k.ck(0) * vpad[8 : 8 + ROWS, :] + k.ck(1) * one + k.ck(2) * two
    for name in ("cum", "cumt", "vc"):
        k.push(name)

    def pair(p, carry):
        lanes = lane_iota(1, PAIR)
        queries = cat_left(k.qkvg[:, columns(p)] * SCALE)
        keys = k.qkvg[:, columns(p, D)]
        value_high, value_low = split(k.vc[:, columns(p)])
        values = jnp.concatenate([value_high, value_low], axis=1)
        parts = []
        for e in range(2):
            key_cat = cat_right(jnp.where((lanes // HEAD_DIM) == e, keys, 0.0))
            first, second = decay_factors(k.cum, k.cumt, k.bias, 2 * p + e)
            first = first * mm_t(queries[:HALF], key_cat[:HALF])
            second = second * mm_t(queries[HALF:], key_cat)
            parts.append(
                jnp.concatenate(
                    [
                        mm_near(first, values[:HALF], value_high[:HALF]),
                        mm_near(second, values, value_high),
                    ],
                    axis=0,
                )
            )
        total = jnp.where(lanes < HEAD_DIM, parts[0], parts[1])
        k.o[:, columns(p)] = total
        gate = k.qkvg[:, columns(p, 3 * D)]
        normed = total * lax.rsqrt(head_norm(total, lanes) + 1.0)
        mixed = (normed * (gate * sigmoid(gate))).astype(bf16)
        if flip:
            k.inner[:, columns(p)] = mixed
        else:
            k.gated[:, columns(p)] = mixed
        return carry

    for p in range(PAIRS):
        pair(p, 0)
    k.push("o")
    if flip:

        def back(i, carry):
            start = i * HALF
            k.gated[pl.ds(start, HALF), :] = mm(
                order_matrix(start, HALF, wide, False), k.inner[...]
            ).astype(bf16)
            return carry

        lax.fori_loop(0, 2, back, 0)


def ffn_forward_body(k):
    gated, x = k.gated(), k.x()
    k.mods(), k.small()

    def tile(i, carry):
        start = i * HALF
        rows = pl.ds(start, HALF)
        slot = k.slot(i)
        grown = mm(gated[rows, :], k.wo()[...])
        k.branch[rows, :] = grown
        middle = x[rows, :].astype(f32) + k.share(slot, 2) * grown
        normal, _ = normalise(middle)
        inner = (normal * (1.0 + k.share(slot, 4)) + k.share(slot, 3)).astype(bf16)
        up = mm(inner, k.wu()[...]) + k.bu()
        _, tanh = gelu_parts(up)
        hidden = (0.5 * up * (1.0 + tanh)).astype(bf16)
        low = mm(hidden, k.wn()[...])
        k.down[rows, :] = low
        result = middle + k.share(slot, 5) * (low + k.bn())
        live = (row_iota(HALF, 1) + start) < k.live_rows
        k.out[rows, :] = jnp.where(live, result, 0.0).astype(bf16)
        return carry

    for i in range(2):
        tile(i, 0)
    if k.layer == 1:
        k.sent[...] = jnp.where(k.section == 0, k.out[...].astype(f32), x[...].astype(f32)).astype(bf16)


def ffn_backward_body(k):
    gmod, gbu, gbn = k.gmod, k.gbu, k.gbn
    gmod[...] = jnp.zeros(gmod.shape, f32)
    gbu[...] = jnp.zeros(gbu.shape, f32)
    gbn[...] = jnp.zeros(gbn.shape, f32)
    k.mods(), k.small()
    x, grad, branch, down = k.x(), k.grad(), k.branch(), k.down()

    def tile(i, carry):
        start = i * HALF
        rows = pl.ds(start, HALF)
        slot = k.slot(i)

        def add(part, values):
            where = (pl.ds(slot, 1), slice((part - 2) * D, (part - 1) * D))
            gmod[where] = gmod[where] + jnp.sum(values, axis=0, keepdims=True)

        grown = branch[rows, :]
        middle = x[rows, :].astype(f32) + k.share(slot, 2) * grown
        normal, rate = normalise(middle)
        inner = (normal * (1.0 + k.share(slot, 4)) + k.share(slot, 3)).astype(bf16)
        k.inner_s[rows, :] = inner
        live = (row_iota(HALF, 1) + start) < k.live_rows
        above = jnp.where(live, grad[rows, :].astype(f32), 0.0)
        add(5, above * (down[rows, :] + k.bn()))
        grad_down = above * k.share(slot, 5)
        gbn[...] = gbn[...] + jnp.sum(grad_down, axis=0, keepdims=True)
        down_low = grad_down.astype(bf16)
        k.down_s[rows, :] = down_low
        up = mm(inner, k.wu()[...]) + k.bu()
        square, tanh = gelu_parts(up)
        half = 0.5 * (1.0 + tanh)
        k.hidden_s[rows, :] = (up * half).astype(bf16)
        slope = half + 0.5 * up * (1.0 - tanh * tanh) * (
            GELU_A * (1.0 + 3.0 * GELU_B * square)
        )
        grad_up = mm_t(down_low, k.wn()[...]) * slope
        gbu[...] = gbu[...] + jnp.sum(grad_up, axis=0, keepdims=True)
        up_low = grad_up.astype(bf16)
        k.up_s[rows, :] = up_low
        grad_inner = mm_t(up_low, k.wu()[...])
        add(3, grad_inner)
        add(4, grad_inner * normal)
        grad_middle = above + normalise_back(
            normal, rate, grad_inner * (1.0 + k.share(slot, 4))
        )
        k.mid_grad[rows, :] = grad_middle
        add(2, grad_middle * grown)
        k.branch_low[rows, :] = (grad_middle * k.share(slot, 2)).astype(bf16)
        return carry

    for i in range(2):
        tile(i, 0)
    k.push("mid_grad")
    k.push("branch_low")

    def weights(j, carry):
        part = pl.ds(pl.multiple_of(j * HALF, HALF), HALF)
        hidden_t = jnp.transpose(k.hidden_s[:, part].astype(f32)).astype(bf16)
        k.gwn[part, :] = mm(hidden_t, k.down_s[...])
        return carry

    lax.fori_loop(0, FF // HALF, weights, 0)
    inner_t = jnp.transpose(k.inner_s[...].astype(f32)).astype(bf16)
    if k.packed:
        devices, shard, _ = k.keep.shape

        def halves(j, carry):
            for kept, own in ((k.keep, c_section), (k.sent, 1 - c_section)):
                columns = pl.ds(pl.multiple_of(j * HALF + own * (FF // 2), HALF), HALF)
                here = pl.ds(pl.multiple_of(j * HALF, HALF), HALF)
                part = mm(inner_t, k.up_s[:, columns]).reshape(devices, shard, HALF)
                kept[:, :, here] = part.astype(kept.dtype)
            return carry

        c_section = k.section
        lax.fori_loop(0, FF // 2 // HALF, halves, 0)

        def owner(r, carry):
            for kept, own in ((k.keep, c_section), (k.sent, 1 - c_section)):
                for piece in range(2):
                    start = pl.multiple_of((4 * r + 2 * own + piece) * shard, 8)
                    rows = k.gwn[pl.ds(start, shard), :]
                    at = FF // 2 + piece * D
                    kept[r, :, at : at + D] = rows.astype(kept.dtype)
            return carry

        lax.fori_loop(0, devices, owner, 0)
        k.push("keep")
        k.push("sent")
    else:
        k.gwu[...] = mm(inner_t, k.up_s[...])
    gated = k.gated()
    k.gwo[...] = mm(jnp.transpose(gated[...].astype(f32)).astype(bf16), k.branch_low[...])

    short = jnp.concatenate([gbn[...], jnp.zeros((1, FF - D), f32)], axis=1)
    k.sums[...] = jnp.concatenate(
        [gmod[0:SLOTS, :], gbu[...], short, jnp.zeros((4, FF), f32)], axis=0
    )


def mixer_backward_body(k):
    flip = k.layer == 1
    wide = k.wide
    mixed_s, low, dv_s, rows_s, cols_s = k.mixed_s, k.low, k.dv_s, k.rows_s, k.cols_s
    fill_bias(k.bias, wide)
    branch_low, wo = k.branch_low(), k.wo()

    def first(i, carry):
        start = i * HALF
        rows = pl.ds(start, HALF)
        if flip:
            part = mm(order_matrix(start, HALF, wide, True), branch_low[...]).astype(bf16)
        else:
            part = branch_low[rows, :]
        mixed_s[rows, :] = mm_t(part, wo[...])
        return carry

    lax.fori_loop(0, 2, first, 0)
    rows_s[...] = jnp.zeros(rows_s.shape, f32)
    cols_s[...] = jnp.zeros(cols_s.shape, f32)
    qkvg, vc, cum, cumt, o = k.qkvg(), k.vc(), k.cum(), k.cumt(), k.o()
    k.small()

    def pair(p, carry):
        lanes = lane_iota(1, PAIR)
        total = o[:, columns(p)]
        gate = qkvg[:, columns(p, 3 * D)]
        above = mixed_s[:, columns(p)]
        rate = lax.rsqrt(head_norm(total, lanes) + 1.0)
        sig = sigmoid(gate)
        grad_gate = above * (total * rate) * (sig * (1.0 + gate * (1.0 - sig)))
        low[:, columns(p, 3 * D)] = grad_gate.astype(bf16)
        grad_normed = above * (gate * sig)
        product = grad_normed * total
        inside = jnp.where(
            lanes < HEAD_DIM,
            jnp.sum(jnp.where(lanes < HEAD_DIM, product, 0.0), axis=1, keepdims=True),
            jnp.sum(jnp.where(lanes < HEAD_DIM, 0.0, product), axis=1, keepdims=True),
        ) * (1.0 / HEAD_DIM)
        grad_o = rate * grad_normed - total * (rate * rate * rate) * inside

        queries = qkvg[:, columns(p)] * SCALE
        keys = qkvg[:, columns(p, D)]
        values = vc[:, columns(p)]
        query_cat = cat_left(queries)
        grad_cat = cat_left(grad_o)
        key_high, key_low = split(keys)
        key_pair = jnp.concatenate([key_high, key_low], axis=1)
        query_t = jnp.transpose(queries)
        grad_t = jnp.transpose(grad_o)
        grad_q = []
        grad_k = []
        grad_v = []
        for e in range(2):
            mine = (lanes // HEAD_DIM) == e
            head = 2 * p + e
            key_cat = cat_right(jnp.where(mine, keys, 0.0))
            value_cat = cat_right(jnp.where(mine, values, 0.0))
            first, second = decay_factors(cum, cumt, k.bias, head)
            raw_first = mm_t(query_cat[:HALF], key_cat[:HALF])
            raw_second = mm_t(query_cat[HALF:], key_cat)
            grad_first = first * mm_t(grad_cat[:HALF], value_cat[:HALF])
            grad_second = second * mm_t(grad_cat[HALF:], value_cat)
            score_first = raw_first * first
            score_second = raw_second * second
            pull_first = grad_first * raw_first
            pull_second = grad_second * raw_second
            here = lanes == head
            rows_s[:HALF, :] = rows_s[:HALF, :] + jnp.where(
                here, jnp.sum(pull_first, axis=1, keepdims=True), 0.0
            )
            rows_s[HALF:, :] = rows_s[HALF:, :] + jnp.where(
                here, jnp.sum(pull_second, axis=1, keepdims=True), 0.0
            )
            low_cols = jnp.sum(pull_second, axis=0, keepdims=True)
            cols_s[pl.ds(head, 1), :HALF] = low_cols[:, :HALF] + jnp.sum(
                pull_first, axis=0, keepdims=True
            )
            cols_s[pl.ds(head, 1), HALF:] = low_cols[:, HALF:]
            grad_q.append(
                jnp.concatenate(
                    [
                        mm_near(grad_first, key_pair[:HALF], key_high[:HALF]),
                        mm_near(grad_second, key_pair, key_high),
                    ],
                    axis=0,
                )
            )

            def turned(source_t, block_first, block_second):
                high, low = split(source_t[e * HEAD_DIM : (e + 1) * HEAD_DIM, :])
                both = jnp.concatenate([high, low], axis=0)
                first_high, first_low = split(block_first)
                second_high, second_low = split(block_second)
                one = mm(both[:, :HALF], first_high)
                one = one[:HEAD_DIM] + one[HEAD_DIM:] + mm(high[:, :HALF], first_low)
                two = mm(both[:, HALF:], second_high)
                two = two[:HEAD_DIM] + two[HEAD_DIM:] + mm(high[:, HALF:], second_low)
                return jnp.concatenate([two[:, :HALF] + one, two[:, HALF:]], axis=1)

            grad_k.append(turned(query_t, grad_first, grad_second))
            grad_v.append(turned(grad_t, score_first, score_second))
        query_grad = jnp.where(lanes < HEAD_DIM, grad_q[0], grad_q[1]) * SCALE
        low[:, columns(p)] = query_grad.astype(bf16)
        low[:, columns(p, D)] = jnp.transpose(jnp.concatenate(grad_k, axis=0)).astype(bf16)
        dv_s[:ROWS, columns(p)] = jnp.transpose(jnp.concatenate(grad_v, axis=0))
        return carry

    for p in range(PAIRS):
        pair(p, 0)

    pulled = rows_s[...] - jnp.transpose(cols_s[...])
    high, middle, rest = split_three(pulled)
    upper_first = jnp.concatenate(
        [
            jnp.where(row_iota(HALF, HALF) <= lane_iota(HALF, HALF), 1.0, 0.0),
            jnp.full((HALF, HALF), 0.0, f32) + jnp.where(wide, 1.0, 0.0),
        ],
        axis=1,
    ).astype(bf16)
    upper_second = upper_first[:, :HALF]
    later = jnp.concatenate(
        [
            mm(upper_first, high) + mm(upper_first, middle) + mm(upper_first, rest),
            mm(upper_second, high[HALF:]) + mm(upper_second, middle[HALF:])
            + mm(upper_second, rest[HALF:]),
        ],
        axis=0,
    )
    grad_dp = later * (1.0 / 16.0) * sigmoid(-(k.dp()[...] + k.bd()))
    grad_bd = jnp.sum(grad_dp, axis=0, keepdims=True)
    low[:, QKVG:] = grad_dp.astype(bf16)

    dv_s[ROWS:, :] = jnp.zeros((8, D), f32)
    position = row_iota(ROWS, 1) & jnp.where(wide, ROWS - 1, HALF - 1)
    last = jnp.where(wide, ROWS - 1, HALF - 1)
    here = dv_s[0:ROWS, :]
    one = jnp.where(position <= last - 1, dv_s[1 : 1 + ROWS, :], 0.0)
    two = jnp.where(position <= last - 2, dv_s[2 : 2 + ROWS, :], 0.0)
    value = qkvg[:, 2 * D : 3 * D]
    low[:, 2 * D : 3 * D] = (k.ck(0) * here + k.ck(1) * one + k.ck(2) * two).astype(bf16)
    k.push("low")

    taps = [jnp.sum(rows * value, axis=0, keepdims=True) for rows in (here, one, two)]
    rest = jnp.concatenate([grad_bd, jnp.zeros((1, D - LANES), f32)], axis=1)
    k.sums[...] = jnp.concatenate([*taps, rest, jnp.zeros((4, D), f32)], axis=0)

    ordered_t = jnp.transpose(k.ordered()[...].astype(f32)).astype(bf16)
    gwo = k.gwo()
    gw = k.gw

    def weights(j, carry):
        part = pl.ds(pl.multiple_of(j * HALF, HALF), HALF)
        gw[:, part] = mm(ordered_t, low[:, part])
        return carry

    lax.fori_loop(0, QKVG // HALF, weights, 0)
    gw[:, QKVG : QKVG + D] = gwo[...]
    gw[:, QKVG + D :] = mm(ordered_t, low[:, QKVG:])

    def halves(j, carry):
        here = pl.ds(pl.multiple_of(j * HALF, HALF), HALF)
        keep = pl.ds(pl.multiple_of(j * HALF + k.section * GROUP, HALF), HALF)
        send = pl.ds(pl.multiple_of(j * HALF + (1 - k.section) * GROUP, HALF), HALF)
        k.gw_keep[:, here] = gw[:, keep]
        k.gw_send[:, here] = gw[:, send].astype(bf16)
        return carry

    lax.fori_loop(0, GROUP // HALF, halves, 0)


def input_backward_body(k):
    flip = k.layer == 1
    wide = k.wide
    gmod, mixed_s, perm_s = k.gmod, k.mixed_s, k.perm_s
    gmod[...] = jnp.zeros(gmod.shape, f32)
    low, w_qk, w_vgd = k.low(), k.w_qk(), k.w_vgd()

    def inner_grad(i, carry):
        rows = pl.ds(pl.multiple_of(i * HALF, HALF), HALF)
        mixed_s[rows, :] = mm_t(low[rows, : 2 * D], w_qk[...]) + mm_t(
            low[rows, 2 * D :], w_vgd[...]
        )
        return carry

    lax.fori_loop(0, 2, inner_grad, 0)
    if flip:
        high, middle, rest = split_three(mixed_s[...])
        perm_s[:, :D] = high
        perm_s[:, D : 2 * D] = middle
        perm_s[:, 2 * D :] = rest
    x, mid_grad = k.x(), k.mid_grad()
    k.mods()

    def tile(i, carry):
        start = i * HALF
        rows = pl.ds(start, HALF)
        slot = k.slot(i)
        if flip:
            three = mm(order_matrix(start, HALF, wide, False), perm_s[...])
            grad = three[:, :D] + three[:, D : 2 * D] + three[:, 2 * D :]
        else:
            grad = mixed_s[rows, :]
        normal, rate = normalise(x[rows, :].astype(f32))
        where = (pl.ds(slot, 1), slice(0, D))
        gmod[where] = gmod[where] + jnp.sum(grad, axis=0, keepdims=True)
        where = (pl.ds(slot, 1), slice(D, 2 * D))
        gmod[where] = gmod[where] + jnp.sum(grad * normal, axis=0, keepdims=True)
        total = mid_grad[rows, :] + normalise_back(normal, rate, grad * (1.0 + k.share(slot, 1)))
        k.gx[rows, :] = total
        k.gx_low[rows, :] = total.astype(bf16)
        return carry

    for i in range(2):
        tile(i, 0)
    k.push("gx_low")
    k.push("gx")
    ffn, mixer = k.ffn_sums(), k.mixer_sums()
    k.mod_low[...] = jnp.concatenate([gmod[...], ffn[...]], axis=1).astype(bf16)
    if k.layer == 0:
        first = k.section == 0
        k.gx_send[...] = jnp.where(first, k.gx_two()[...], k.gx[...])
        one, two = k.mod_low[...].astype(f32), k.mod_two()[...].astype(f32)
        k.mod_mine[...] = jnp.where(first, one, two).astype(bf16)
        k.mod_send[...] = jnp.where(first, two, one).astype(bf16)
    half = 2 * D
    rest = ffn[0:1, :] + ffn[1:2, :]
    k.sums[...] = jnp.concatenate(
        [
            gmod[0:1, :] + gmod[1:2, :],
            rest[:, :half],
            rest[:, half:],
            ffn[2:3, :half],
            ffn[2:3, half:],
            jnp.concatenate([ffn[3:4, :D], mixer[0:1, :]], axis=1),
            jnp.concatenate([mixer[1:2, :], mixer[2:3, :]], axis=1),
            jnp.concatenate([mixer[3:4, :], jnp.zeros((1, D), f32)], axis=1),
        ],
        axis=0,
    )


ANY = pl.BlockSpec(memory_space=pl.ANY)
VMEM = pl.BlockSpec(memory_space=pltpu.VMEM)
HBM = pl.BlockSpec(memory_space=pltpu.HBM)


def call(body, layer, layouts, ins, outs, scratch, flops, packed=None, after=()):
    arrays = []
    counts = []
    kept = []
    places = []
    for kind, given, part in ins.values():
        places.extend([ANY] * 2 if kind == "own" else [HBM])
        given = given if kind == "own" else (given,)
        arrays.extend(given)
        counts.append(len(given))
        rows, wide = given[0].shape[-2:]
        start, stop = part or (0, wide)
        kept.append(pltpu.VMEM((rows, stop - start), given[0].dtype))

    def kernel(*refs):
        refs = list(refs)
        take = lambda count: [refs.pop(0) for _ in range(count)]
        (layouts_ref,) = take(1)
        sources = [take(count) for count in counts]
        take(len(after))
        targets = take(len(outs))
        buffers = take(len(ins))
        results = take(len(outs))
        rest = take(len(scratch))
        in_sems, out_sems = refs
        k = Kernel(layer, layouts_ref)
        k.packed = packed
        for number, (name, (kind, _, part)) in enumerate(ins.items()):
            given = sources[number]
            if part is not None:
                given = [ref.at[:, part[0] : part[1]] for ref in given]
            setattr(k, name, k.load(kind, given, buffers[number], in_sems.at[number]))
        k.results = {}
        for number, name in enumerate(outs):
            setattr(k, name, results[number])
            k.results[name] = (results[number], targets[number], out_sems.at[number])
        for name, ref in zip(scratch, rest):
            setattr(k, name, ref)
        body(k)
        k.finish()

    return pl.pallas_call(
        kernel,
        out_shape=[jax.ShapeDtypeStruct(shape, kind) for shape, kind, _ in outs.values()],
        in_specs=[pl.BlockSpec(memory_space=pltpu.SMEM)] + places + [ANY] * len(after),
        out_specs=[HBM if for_kernel else ANY for _, _, for_kernel in outs.values()],
        scratch_shapes=kept
        + [pltpu.VMEM(shape, kind) for shape, kind, _ in outs.values()]
        + [pltpu.VMEM(shape, kind) for shape, kind in scratch.values()]
        + [pltpu.SemaphoreType.DMA((len(ins),)), pltpu.SemaphoreType.DMA((len(outs),))],
        compiler_params=pltpu.CompilerParams(vmem_limit_bytes=56 * 1024 * 1024),
        cost_estimate=pl.CostEstimate(flops=flops, bytes_accessed=4 << 20, transcendentals=0),
    )(layouts, *arrays, *after)


def own(pair, part=None):
    return ("own", pair, part)


def plain(array):
    return ("plain", array, None)


def micro(array):
    return ("micro", array, None)


AT_UP = (0, FF)
AT_OUT = (FF, FF + D)


def attn_forward(layer, layouts, x, mods, small, qk, vgd):
    return call(
        attn_forward_body,
        layer,
        layouts,
        dict(
            x=micro(x),
            mods=own(mods),
            w_qk=own(qk),
            w_vgd=own(vgd),
            small=own(small),
        ),
        dict(
            ordered=((ROWS, D), bf16, True),
            qkvg=((ROWS, QKVG), f32, True),
            dp=((ROWS, LANES), f32, True),
            vc=((ROWS, D), f32, True),
            cum=((ROWS, LANES), f32, True),
            cumt=((LANES, ROWS), f32, True),
            o=((ROWS, D), f32, True),
            gated=((ROWS, D), bf16, True),
        ),
        dict(
            inner=((ROWS, D), bf16),
            vpad=((ROWS + 8, D), f32),
            bias=((HALF, ROWS), f32),
        ),
        4 * 10**9,
    )


def ffn_forward(layer, layouts, x, mods, small, gated, upo, down):
    return call(
        ffn_forward_body,
        layer,
        layouts,
        dict(
            gated=plain(gated),
            x=micro(x),
            wo=own(upo, AT_OUT),
            mods=own(mods),
            small=own(small),
            wu=own(upo, AT_UP),
            wn=own(down),
        ),
        dict(
            out=((ROWS, D), bf16, True),
            branch=((ROWS, D), f32, True),
            down=((ROWS, D), f32, True),
            **({"sent": ((ROWS, D), bf16, False)} if layer == 1 else {}),
        ),
        {},
        3 * 10**9,
    )


def ffn_backward(
    layer, layouts, x, mods, small, gated, branch, down_raw, grad, upo, down, devices, after=()
):
    shard = D // devices
    in_kernel = shard % 8 == 0
    if in_kernel:
        sums = dict(
            keep=((devices, shard, FF), f32, True),
            sent=((devices, shard, FF), bf16, False),
        )
    else:
        sums = dict(gwu=((D, FF), f32, False), gwn=((FF, D), f32, False))
    return call(
        ffn_backward_body,
        layer,
        layouts,
        dict(
            mods=own(mods),
            small=own(small),
            x=micro(x),
            grad=micro(grad),
            branch=plain(branch),
            down=plain(down_raw),
            wu=own(upo, AT_UP),
            wn=own(down),
            gated=plain(gated),
        ),
        dict(
            mid_grad=((ROWS, D), f32, True),
            branch_low=((ROWS, D), bf16, True),
            gwo=((D, D), f32, True),
            sums=((8, FF), f32, True),
            **sums,
        ),
        dict(
            **({"gwn": ((FF, D), f32)} if in_kernel else {}),
            hidden_s=((ROWS, FF), bf16),
            inner_s=((ROWS, D), bf16),
            up_s=((ROWS, FF), bf16),
            down_s=((ROWS, D), bf16),
            gmod=((8, FF), f32),
            gbu=((1, FF), f32),
            gbn=((1, D), f32),
        ),
        5 * 10**9,
        packed=in_kernel,
        after=after,
    )


def mixer_backward(layer, layouts, small, saved, branch_low, gwo, upo, after=()):
    ordered, qkvg, dp, vc, cum, cumt, o = saved
    return call(
        mixer_backward_body,
        layer,
        layouts,
        dict(
            branch_low=plain(branch_low),
            wo=own(upo, AT_OUT),
            qkvg=plain(qkvg),
            vc=plain(vc),
            cum=plain(cum),
            cumt=plain(cumt),
            o=plain(o),
            small=own(small),
            dp=plain(dp),
            ordered=plain(ordered),
            gwo=plain(gwo),
        ),
        dict(
            low=((ROWS, QKVG + LANES), bf16, True),
            gw_keep=((D, GROUP), f32, True),
            gw_send=((D, GROUP), bf16, False),
            sums=((8, D), f32, True),
        ),
        dict(
            mixed_s=((ROWS, D), f32),
            dv_s=((ROWS + 8, D), f32),
            rows_s=((ROWS, LANES), f32),
            cols_s=((LANES, ROWS), f32),
            bias=((HALF, ROWS), f32),
            gw=((D, 2 * GROUP), f32),
        ),
        7 * 10**9,
        after=after,
    )


def input_backward(
    layer, layouts, x, mods, low, mid_grad, ffn_sums, mixer_sums, qk, vgd, two=None, after=()
):
    extra_in, extra_out = {}, {}
    if two is not None:
        extra_in = dict(gx_two=plain(two[0]), mod_two=plain(two[1]))
        extra_out = dict(
            gx_send=((ROWS, D), f32, False),
            mod_mine=((8, 6 * D), bf16, False),
            mod_send=((8, 6 * D), bf16, False),
        )
    return call(
        input_backward_body,
        layer,
        layouts,
        dict(
            low=plain(low),
            w_qk=own(qk),
            w_vgd=own(vgd),
            x=micro(x),
            mid_grad=plain(mid_grad),
            mods=own(mods),
            ffn_sums=plain(ffn_sums),
            mixer_sums=plain(mixer_sums),
            **extra_in,
        ),
        dict(
            gx=((ROWS, D), f32, True),
            gx_low=((ROWS, D), bf16, True),
            mod_low=((8, 6 * D), bf16, True),
            sums=((8, 2 * D), f32, False),
            **extra_out,
        ),
        dict(
            mixed_s=((ROWS, D), f32),
            perm_s=((ROWS, 3 * D), bf16),
            gmod=((8, 2 * D), f32),
        ),
        2 * 10**9,
        after=after,
    )


def small_kernel(b_up, b_down, taps, b_decay, packed):
    packed[...] = jnp.zeros(packed.shape, f32)
    packed[0:1, :] = b_up[...]
    packed[1:2, :D] = b_down[...]
    packed[2:5, :D] = taps[0]
    packed[5:6, :HEADS] = b_decay[...]


def pack_small(b_up, b_down, taps, b_decay):
    return pl.pallas_call(
        small_kernel,
        out_shape=jax.ShapeDtypeStruct((8, FF), f32),
        in_specs=[VMEM] * 4,
        out_specs=VMEM,
    )(b_up, b_down, taps, b_decay)


def pack_kernel(
    w_query, w_key, w_value, w_gate, w_out, w_decay, w_up, conditions, qk, vgd, upo, lifted
):
    qk[:, :D] = w_query[0]
    qk[:, D:] = w_key[0]
    vgd[:, :D] = w_value[0]
    vgd[:, D : 2 * D] = w_gate[0]
    place = jnp.where(row_iota(HEADS, LANES) == lane_iota(HEADS, LANES), 1.0, 0.0).astype(bf16)
    turned = lax.dot_general(
        w_decay[0], place, (((0,), (0,)), ((), ())), preferred_element_type=f32
    )
    vgd[:, 2 * D :] = turned.astype(bf16)
    upo[:, :FF] = w_up[0]
    upo[:, FF:] = w_out[0]
    values = jnp.concatenate([conditions[m].astype(f32) for m in range(MICRO)], axis=0)
    lifted[0] = (values * sigmoid(values)).astype(bf16)


def pack(*weights):
    shard = weights[0].shape[1]
    widths = (2 * D, 2 * D + LANES, FF + D)
    return pl.pallas_call(
        pack_kernel,
        out_shape=[jax.ShapeDtypeStruct((shard, width), bf16) for width in widths]
        + [jax.ShapeDtypeStruct((1, MICRO * SLOTS, D), bf16)],
        in_specs=[VMEM] * len(weights),
        out_specs=[VMEM] * (len(widths) + 1),
    )(*weights)


def join_kernel(bits, waits, *refs):
    count = len(bits)
    held, came, out = refs[:count], refs[count : 2 * count], refs[2 * count + waits :]
    for i, bit in enumerate(bits):
        mine = (lax.axis_index("row") >> bit) & 1
        out[i][:, mine] = held[i][...]
        out[i][:, 1 - mine] = came[i][...]


def join(held, came, bits, after=()):
    def parts(array, bit):
        axis = axis_of(bit)
        above = 1
        for size in array.shape[:axis]:
            above *= size
        return array.reshape((above, -1) + array.shape[-2:])

    split_held = [parts(array, bit) for array, bit in zip(held, bits)]
    split_came = [parts(array, bit) for array, bit in zip(came, bits)]
    out = pl.pallas_call(
        functools.partial(join_kernel, bits, len(after)),
        out_shape=[
            jax.ShapeDtypeStruct(array.shape[:1] + (2,) + array.shape[1:], array.dtype)
            for array in split_held
        ],
        in_specs=[VMEM] * (2 * len(held)) + [ANY] * len(after),
        out_specs=[VMEM] * len(held),
        compiler_params=pltpu.CompilerParams(vmem_limit_bytes=8 * 1024 * 1024),
        cost_estimate=pl.CostEstimate(flops=10**6, bytes_accessed=10**6, transcendentals=0),
    )(*split_held, *split_came, *after)
    joined = []
    for array, result, bit in zip(held, out, bits):
        shape = list(array.shape)
        shape[axis_of(bit)] = 2
        joined.append(result.reshape(shape))
    return joined


def lifted_kernel(mine, came, ada, out, kept, sem):
    copy = pltpu.make_async_copy(ada, kept, sem)
    copy.start()
    first = lax.axis_index("section") == 0
    pair = mine[0:SLOTS, :].astype(f32), came[0:SLOTS, :].astype(f32)
    grad = jnp.concatenate(
        [jnp.where(first, pair[0], pair[1]), jnp.where(first, pair[1], pair[0])], axis=0
    ).astype(bf16)
    copy.wait()
    out[...] = mm_t(grad, kept[...])


def lifted_grads(mine, came, ada):
    return pl.pallas_call(
        lifted_kernel,
        out_shape=jax.ShapeDtypeStruct((MICRO * SLOTS, D), f32),
        in_specs=[VMEM, VMEM, ANY],
        out_specs=VMEM,
        scratch_shapes=[pltpu.VMEM((D, 6 * D), bf16), pltpu.SemaphoreType.DMA],
        compiler_params=pltpu.CompilerParams(vmem_limit_bytes=16 * 1024 * 1024),
        cost_estimate=pl.CostEstimate(flops=10**9, bytes_accessed=2 << 20, transcendentals=0),
    )(mine, came, ada)


def term_kernel(*refs):
    *terms, stays, goes = refs
    stays[...] = sum(ref[:, 0] for ref in terms)
    goes[...] = sum(ref[:, 1] for ref in terms)


def term_step(below, *terms):
    tail = terms[0].shape[1:]
    above = terms[0].shape[0] // (2 * below)
    shape = jax.ShapeDtypeStruct((above, below) + tail, f32)
    out = pl.pallas_call(
        term_kernel,
        out_shape=[shape] * 2,
        in_specs=[VMEM] * len(terms),
        out_specs=[VMEM] * 2,
        compiler_params=pltpu.CompilerParams(vmem_limit_bytes=8 * 1024 * 1024),
        cost_estimate=pl.CostEstimate(flops=10**6, bytes_accessed=10**6, transcendentals=0),
    )(*[term.reshape((above, 2, below) + tail) for term in terms])
    return [array.reshape((above * below,) + tail) for array in out]


def step_kernel(bit, widths, counts, waits, *refs):
    mine = (lax.axis_index("row") >> bit) & 1
    count, many = len(widths), len(counts)
    refs = list(refs)
    take = lambda number: [refs.pop(0) for _ in range(number)]
    sources = take(count + many)
    take(waits)
    targets = take(count + 1)
    buffers = take(count + many)
    results = take(count + 1)
    in_sems, out_sems = refs
    arrive = [
        pltpu.make_async_copy(source, buffer, in_sems.at[i])
        for i, (source, buffer) in enumerate(zip(sources, buffers))
    ]
    leave = [
        pltpu.make_async_copy(result, target, out_sems.at[i])
        for i, (result, target) in enumerate(zip(results, targets))
    ]
    for copy in arrive:
        copy.start()
    kept, came = buffers[:count], buffers[count:]
    places = [(j, i) for j, number in enumerate(counts) for i in range(number)]
    goes = results[count]
    at = 0
    for i in range(count):
        j, place = places[i]
        arrive[i].wait()
        if place == 0:
            arrive[count + j].wait()
        start = sum(widths[i - place : i])
        columns = slice(start, start + widths[i])
        total = kept[i][:, 1 - mine] + came[j][:, 1 - mine, :, :, columns].astype(f32)
        goes[:, :, :, at : at + widths[i]] = total.astype(bf16)
        at += widths[i]
    leave[count].start()
    for i in range(count):
        j, place = places[i]
        start = sum(widths[i - place : i])
        columns = slice(start, start + widths[i])
        results[i][...] = kept[i][:, mine] + came[j][:, mine, :, :, columns].astype(f32)
        leave[i].start()
    for copy in leave:
        copy.wait()


def step(kept, came, bit, below=1, after=()):
    blocks, rows = kept[0].shape[0] // 2, kept[0].shape[1]
    above = blocks // below
    paired = lambda array: array.reshape((above, 2, below) + array.shape[1:])
    widths = [array.shape[2] for array in kept]
    size = sum(array.size for array in kept)
    arrays = [paired(array) for array in kept] + [paired(array) for array, _ in came]
    shapes = [((above, below, rows, width), f32) for width in widths]
    shapes.append(((above, below, rows, sum(widths)), bf16))
    out = pl.pallas_call(
        functools.partial(step_kernel, bit, widths, [count for _, count in came], len(after)),
        out_shape=[jax.ShapeDtypeStruct(shape, kind) for shape, kind in shapes],
        in_specs=[HBM] * len(kept) + [ANY] * (len(came) + len(after)),
        out_specs=[HBM] * len(kept) + [ANY],
        scratch_shapes=[pltpu.VMEM(array.shape, array.dtype) for array in arrays]
        + [pltpu.VMEM(shape, kind) for shape, kind in shapes]
        + [pltpu.SemaphoreType.DMA((len(arrays),)), pltpu.SemaphoreType.DMA((len(shapes),))],
        compiler_params=pltpu.CompilerParams(vmem_limit_bytes=10 * 1024 * 1024),
        cost_estimate=pl.CostEstimate(flops=size, bytes_accessed=8 * size, transcendentals=0),
    )(*arrays, *after)
    count = len(kept)
    flat_blocks = [array.reshape((blocks,) + array.shape[2:]) for array in out]
    return flat_blocks[:count], flat_blocks[count]


def misc_step_kernel(held, arrived, out):
    size = held.shape[0] - SUMS
    out[:size, :] = held[:size, :]
    out[size : 2 * size, :] = arrived[:size, :]
    high, low = split(misc_sums(held, arrived))
    out[2 * size : 2 * size + SUMS // 2, :] = high
    out[2 * size + SUMS // 2 :, :] = low


def misc_step(held, arrived):
    return pl.pallas_call(
        misc_step_kernel,
        out_shape=jax.ShapeDtypeStruct((2 * held.shape[0] - SUMS, 2 * D), bf16),
        in_specs=[VMEM] * 2,
        out_specs=VMEM,
        cost_estimate=pl.CostEstimate(flops=10**5, bytes_accessed=10**5, transcendentals=0),
    )(held, arrived)


def misc_sums(*refs):
    size = refs[0].shape[0] - SUMS
    parts = [ref[size:, :].astype(f32) for ref in refs]
    return sum(part[: SUMS // 2] + part[SUMS // 2 :] for part in parts)


SUMS = 32
OWN = 16


def misc_kernel(mod_one, mod_two, sums_one, sums_two, out):
    rows = []
    for mod in (mod_one, mod_two):
        for slot in range(SLOTS):
            for i in range(3):
                part = mod[slot : slot + 1, i * 2 * D : (i + 1) * 2 * D]
                rows.append(part.astype(f32))
        rows.append(jnp.zeros((OWN // 2 - 3 * SLOTS, 2 * D), f32))
    sums = jnp.concatenate([sums_one[...], sums_two[...]], axis=0)
    rows.extend(part.astype(f32) for part in split(sums))
    out[...] = jnp.concatenate(rows, axis=0).astype(bf16)


def pack_misc(mod_one, mod_two, sums_one, sums_two):
    return pl.pallas_call(
        misc_kernel,
        out_shape=jax.ShapeDtypeStruct((OWN + SUMS, 2 * D), bf16),
        in_specs=[VMEM] * 4,
        out_specs=VMEM,
    )(mod_one, mod_two, sums_one, sums_two)


def finish_kernel(widths, counts, waits, *refs):
    count = len(widths)
    kept, refs = refs[:count], refs[count:]
    came, refs = refs[: len(counts)], refs[len(counts) :]
    lifted, *parts = refs[:5]
    mine, other, small_mine, small_other = refs[5 + waits :]
    places = [(ref, i) for ref, many in zip(came, counts) for i in range(many)]
    added = []
    for i in range(count):
        ref, place = places[i]
        start = sum(widths[i - place : i])
        added.append(kept[i][0] + ref[0, :, start : start + widths[i]].astype(f32))
    a1, f1, f2, a2 = added
    size = parts[0].shape[0] - SUMS
    rows = jnp.concatenate([part[:size, :] for part in parts], axis=0)
    rows = rows.astype(f32).reshape(-1, OWN, 2 * D)

    def ada(first):
        columns = []
        for i in range(3):
            both = [rows[:, first + 3 * slot + i, :] for slot in range(SLOTS)]
            columns.append(mm(lifted[...], jnp.concatenate(both, axis=0).astype(bf16)))
        return jnp.concatenate(columns, axis=1)

    first = lax.axis_index("section") == 0
    at = 0
    for one, two in ((a1, a2), (f1, f2), (ada(0), ada(OWN // 2))):
        columns = slice(at, at + one.shape[1])
        mine[:, columns] = jnp.where(first, one, two)
        other[:, columns] = jnp.where(first, two, one)
        at += one.shape[1]
    total = misc_sums(*parts)
    one, two = total[0:8, :], total[8:16, :]
    small_mine[...] = jnp.where(first, one, two)
    small_other[...] = jnp.where(first, two, one)


def finish(kept, came, lifted, parts, after):
    widths = [array.shape[2] for array in kept]
    shard = kept[0].shape[1]
    wide = GROUP + FF + 6 * D
    arrays = [array for array, _ in came]
    shapes = [(shard, wide)] * 2 + [(8, 2 * D)] * 2
    return pl.pallas_call(
        functools.partial(finish_kernel, widths, [count for _, count in came], len(after)),
        out_shape=[jax.ShapeDtypeStruct(shape, f32) for shape in shapes],
        in_specs=[VMEM] * (len(kept) + len(came) + 5) + [ANY] * len(after),
        out_specs=[VMEM] * 4,
        compiler_params=pltpu.CompilerParams(vmem_limit_bytes=8 * 1024 * 1024),
    )(*kept, *arrays, lifted, *parts, *after)


def output_kernel(mine, other, small_mine, small_other, *outs):
    first = lax.axis_index("section") == 0

    def halves(start, width):
        columns = slice(start, start + width)
        pair = mine[:, columns], other[:, columns]
        return jnp.where(first, pair[0], pair[1]), jnp.where(first, pair[1], pair[0])

    attn = halves(0, GROUP)
    cut = GROUP - 2 * D
    outs[0][...] = attn[0][:, :D]
    outs[1][...] = attn[0][:, D : 2 * D]
    outs[2][:, :cut] = attn[0][:, 2 * D :]
    outs[2][:, cut:] = attn[1][:, : D - cut]
    outs[3][...] = attn[1][:, D - cut : 2 * D - cut]
    outs[4][...] = attn[1][:, 2 * D - cut : 3 * D - cut]
    decay = jnp.transpose(attn[1][:, 3 * D - cut :])
    for head in range(HEADS):
        outs[5][head] = decay[head : head + 1, :]
    up = halves(GROUP, FF // 2)
    outs[6][:, : FF // 2] = up[0]
    outs[6][:, FF // 2 :] = up[1]
    for piece in range(2):
        down = halves(GROUP + FF // 2 + piece * D, D)
        outs[7][piece] = down[0]
        outs[7][2 + piece] = down[1]
    outs[8][...] = mine[:, GROUP + FF :] + other[:, GROUP + FF :]
    small = small_mine[...] + small_other[...]
    half = 2 * D
    for i in range(3):
        outs[9][:, i * half : (i + 1) * half] = small[i : i + 1, :]
    for i in range(2):
        outs[10][:, i * half : (i + 1) * half] = small[3 + i : 4 + i, :]
    outs[11][...] = small[5:6, :D]
    outs[12][0] = small[5:6, D:]
    outs[12][1] = small[6:7, :D]
    outs[12][2] = small[6:7, D:]
    outs[13][...] = small[7:8, :HEADS]


def outputs(mine, other, small_mine, small_other):
    shard = mine.shape[0]
    shapes = (
        [(shard, D)] * 5
        + [(HEADS, 1, shard), (shard, FF), (4, shard, D), (shard, 6 * D)]
        + [(1, 6 * D), (1, FF), (1, D), (3, 1, D), (1, HEADS)]
    )
    return pl.pallas_call(
        output_kernel,
        out_shape=[jax.ShapeDtypeStruct(shape, f32) for shape in shapes],
        in_specs=[VMEM] * 4,
        out_specs=[VMEM] * len(shapes),
    )(mine, other, small_mine, small_other)


def both_kernel(one, two, came, out, mark, kept, sems):
    section = lax.axis_index("section")
    mark[...] = jnp.zeros(mark.shape, f32)

    def move(mine, layer):
        arrive = [
            pltpu.make_async_copy(mine, kept.at[layer], sems.at[0]),
            pltpu.make_async_copy(came, kept.at[1 - layer], sems.at[1]),
        ]
        leave = [
            pltpu.make_async_copy(kept.at[layer], out.at[layer], sems.at[2]),
            pltpu.make_async_copy(kept.at[1 - layer], out.at[1 - layer], sems.at[3]),
        ]
        for copy in arrive:
            copy.start()
        for copy, after in zip(arrive, leave):
            copy.wait()
            after.start()
        for copy in leave:
            copy.wait()

    @pl.when(section == 0)
    def _():
        move(one, 0)

    @pl.when(section == 1)
    def _():
        move(two, 1)


def both_micros(one, two, came):
    return pl.pallas_call(
        both_kernel,
        out_shape=[
            jax.ShapeDtypeStruct((MICRO,) + one.shape, one.dtype),
            jax.ShapeDtypeStruct((8, LANES), f32),
        ],
        in_specs=[ANY] * 3,
        out_specs=[ANY, VMEM],
        scratch_shapes=[
            pltpu.VMEM((MICRO,) + one.shape, one.dtype),
            pltpu.SemaphoreType.DMA((4,)),
        ],
    )(one, two, came)


def swap(values):
    return lax.ppermute(values, "section", [(0, 1), (1, 0)])


def row_bits():
    bits = lax.axis_size("row").bit_length() - 1
    third = bits // 3
    return (
        tuple(range(third)),
        tuple(range(third, 2 * third)),
        tuple(range(2 * third, bits)),
    )


def across(values, flips):
    size = lax.axis_size("row")
    return lax.ppermute(values, "row", [(i, i ^ flips) for i in range(size)])


def partner(values, bit):
    return across(values, 1 << bit)


def axis_of(bit):
    return lax.axis_size("row").bit_length() - 2 - bit


def bit_of(bit):
    return (lax.axis_index("row") >> bit) & 1


def single(values):
    return values.reshape((1,) * (lax.axis_size("row").bit_length() - 1) + values.shape)


def gather_steps(along_x, along_y, along_z):
    steps = [(bit, bit) for bit in reversed(along_z)]
    return steps + list(zip(along_x + along_y, along_y + along_x))


def flat(held):
    return held.reshape(-1, held.shape[-1])


def lock(*arrays):
    return lax.optimization_barrier(arrays)


def on_device(
    tokens, conditions, output_grad, layouts,
    w_ada, b_ada, w_query, w_key, w_value, w_gate, w_out, w_decay, b_decay, conv_kernel,
    w_up, b_up, w_down, b_down,
):
    section = lax.axis_index("section")
    devices = lax.axis_size("row")
    shard = w_query.shape[1]
    along_x, along_y, along_z = row_bits()

    def both(values):
        return values, swap(values)

    qk, vgd, upo, lifted = pack(
        w_query, w_key, w_value, w_gate, w_out, w_decay.transpose(0, 2, 1), w_up, conditions
    )
    small = pack_small(b_up, b_down, conv_kernel, b_decay)
    steps = gather_steps(along_x, along_y, along_z)
    order = tuple(reversed(along_z)) + along_x[:-1] + along_y[:-1] + along_x[-1:] + along_y[-1:]
    term_bits = along_x + along_y + along_z
    spans = len(steps) - 2
    bounds = [len(term_bits) * i // spans for i in range(spans + 1)]
    term_bits = [term_bits[bounds[i] : bounds[i + 1]] for i in range(spans)]
    left = list(order)
    held = [single(array) for array in (qk, vgd, upo, w_down[0])]
    for place, pair in enumerate(steps):
        bits = pair + pair
        came = [partner(array, bit) for array, bit in zip(held, bits)]
        after = (small,)
        if place == 1:
            for bit in order:
                lifted = jnp.concatenate([lifted, partner(lifted, bit)], axis=0)
            after = (lifted,)
        if place == 2:
            lifted_cut = lax.dynamic_slice_in_dim(
                lifted, lax.axis_index("row") * shard, shard, 2
            )
            product = mm(lifted_cut.reshape(devices * MICRO * SLOTS, shard), w_ada[0])
            terms = (product.reshape(devices, MICRO * SLOTS, 6 * D),)
        if place >= 2:
            for bit in term_bits[place - 2]:
                stays, goes = term_step(1 << left.index(bit), *terms)
                left.remove(bit)
                terms = (stays, partner(goes, bit))
            after = (terms[1],)
        if place < len(steps) - 1:
            held = join(held, came, bits, after)
        else:
            qk, vgd = [both(flat(array)) for array in join(held[:2], came[:2], bits[:2])]
            mods = both(sum(term[0] for term in terms) + b_ada[0])
            smalls = both(small)
            x = tokens
            *saved, gated = attn_forward(0, layouts, x, mods, smalls, qk, vgd)
            held = join(held[2:], came[2:], bits[2:], (gated,))
    upo, down = [both(flat(array)) for array in held]
    kept = []
    acts = []
    for l in range(2):
        if l:
            *saved, gated = attn_forward(l, layouts, x, mods, smalls, qk, vgd)
        out, branch, down_raw, *acts_sent = ffn_forward(
            l, layouts, x, mods, smalls, gated, upo, down
        )
        kept.append((x, saved, gated, branch, down_raw))
        acts.append(out)
        x = out[None]

    late, _ = lock(w_ada[0], acts[0])
    ada_all = lax.all_gather(late, "row", axis=0, tiled=True)

    def ffn_step(l, grad, after=()):
        x, saved, gated, branch, down_raw = kept[l]
        mid_grad, branch_low, gwo, sums, *terms = ffn_backward(
            l, layouts, x, mods, smalls, gated, branch, down_raw, grad, upo, down, devices, after
        )
        if terms[0].ndim == 2:
            up_sum = terms[0].reshape(devices, shard, 2, FF // 2)
            down_sum = terms[1].reshape(devices, 2, 2, shard, D)
            terms = []
            for own in (section, 1 - section):
                up_half = lax.dynamic_index_in_dim(up_sum, own, 2, keepdims=False)
                down_half = lax.dynamic_index_in_dim(down_sum, own, 1, keepdims=False)
                terms.append(
                    jnp.concatenate([up_half, down_half[:, 0], down_half[:, 1]], axis=2)
                )
            terms[1] = terms[1].astype(bf16)
        return [branch_low, gwo], mid_grad, terms[0], terms[1], sums

    def mixer_step(l, carried, after=()):
        low, keep, sent, sums = mixer_backward(
            l, layouts, smalls, kept[l][1], *carried, upo, after
        )
        by_row = lambda array: array.reshape(devices, shard, GROUP)
        return low, by_row(keep), by_row(sent), sums

    def input_step(l, low, mid_grad, ffn_sums, mixer_sums, two=None, after=()):
        x = kept[l][0]
        return input_backward(
            l, layouts, x, mods, low, mid_grad, ffn_sums, mixer_sums, qk, vgd, two, after
        )

    def run(keep, came, bits, below=1, after=()):
        for bit in bits[:-1]:
            keep, sent = step(keep, came, bit, below, after)
            came = [(partner(sent, bit), len(keep))]
        return step(keep, came, bits[-1], below, after)

    def grown(mod, bits):
        for bit in bits:
            mod = misc_step(mod, partner(mod, bit))
        return mod

    x_bits, y_bits, z_bits = along_x, along_y, along_z
    lifted = lifted_cut.reshape(devices, MICRO, SLOTS, shard)
    lifted = lax.dynamic_index_in_dim(lifted, section, 1, keepdims=False)
    lifted = lifted.transpose(2, 1, 0).reshape(shard, SLOTS * devices)

    carried, mid_grad, f2_keep, f2_sent, f2_sums = ffn_step(1, output_grad)
    *carried, f2_sent, acts_sent, lifted = lock(*carried, f2_sent, acts_sent[0], lifted)
    f2_came = swap(f2_sent)
    acts_came = swap(acts_sent)
    low, a2_keep, a2_sent, m2_sums = mixer_step(1, carried)
    low, a2_sent, f2_came, acts_came = lock(low, a2_sent, f2_came, acts_came)
    a2_came = swap(a2_sent)
    gx_two, grad, mod_low_two, sums_two = input_step(1, low, mid_grad, f2_sums, m2_sums)
    grad, a2_came = lock(grad, a2_came)
    f2_keep, f2_sent = run([f2_keep], [(f2_came, 1)], x_bits)
    a2_keep, a2_sent = run([a2_keep], [(a2_came, 1)], y_bits, 1 << len(x_bits))
    grad, f2_sent, a2_sent = lock(grad, f2_sent, a2_sent)
    f2_came = partner(f2_sent, x_bits[-1])
    a2_came = partner(a2_sent, y_bits[-1])

    carried, mid_grad, f1_keep, f1_sent, f1_sums = ffn_step(0, grad[None])
    *carried, f1_sent, f2_came, a2_came = lock(*carried, f1_sent, f2_came, a2_came)
    f1_came = swap(f1_sent)
    f2_keep, f2_sent = run(f2_keep, [(f2_came, 1)], y_bits)
    a2_keep, a2_sent = run(a2_keep, [(a2_came, 1)], x_bits)
    f1_keep, f1_sent = run([f1_keep], [(f1_came, 1)], x_bits)
    *carried, f2_sent, a2_sent, f1_sent = lock(*carried, f2_sent, a2_sent, f1_sent)
    f1_came = partner(f1_sent, x_bits[-1])
    a2_came = partner(a2_sent, x_bits[-1])
    f2_came = partner(f2_sent, y_bits[-1])
    low, a1_keep, a1_sent, m1_sums = mixer_step(0, carried)
    low, a1_sent, f2_came, a2_came, f1_came, ada_all = lock(
        low, a1_sent, f2_came, a2_came, f1_came, ada_all
    )
    a1_came = swap(a1_sent)
    two_keep, two_sent = run(f2_keep + a2_keep, [(f2_came, 1), (a2_came, 1)], z_bits[:1])
    f1_keep, f1_sent = run(f1_keep, [(f1_came, 1)], y_bits)
    a1_keep, a1_sent = run([a1_keep], [(a1_came, 1)], x_bits)
    low, two_sent, f1_sent, a1_sent = lock(low, two_sent, f1_sent, a1_sent)
    a1_came = partner(a1_sent, x_bits[-1])
    f1_came = partner(f1_sent, y_bits[-1])
    two_came = partner(two_sent, z_bits[0])
    gx_one, _, mod_low_one, sums_one, gx_sent, mod_mine, mod_sent = input_step(
        0, low, mid_grad, f1_sums, m1_sums, (gx_two, mod_low_two)
    )
    misc = pack_misc(mod_low_one, mod_low_two, sums_one, sums_two)
    misc, a1_came, two_came, f1_came, gx_sent, mod_sent = lock(
        misc, a1_came, two_came, f1_came, gx_sent, mod_sent
    )

    a1_keep, a1_sent = run(a1_keep, [(a1_came, 1)], y_bits)
    a1_sent, misc = lock(a1_sent, misc)
    a1_came = partner(a1_sent, y_bits[-1])
    misc = grown(misc, tuple(reversed(z_bits))[:-1])
    gx_came = swap(gx_sent)
    mod_came = swap(mod_sent)
    keep, came = a1_keep + f1_keep, [(a1_came, 1), (f1_came, 1)]
    for place, bit in enumerate(z_bits):
        if place == 1:
            keep, came = keep + two_keep, came + [(two_came, 2)]
        keep, sent = step(keep, came, bit)
        if place == len(z_bits) - 1:
            sent, misc, gx_came, mod_came = lock(sent, misc, gx_came, mod_came)
        elif place == 0:
            sent, misc = lock(sent, misc)
        came = [(partner(sent, bit), len(keep))]
        if place == 0:
            misc = grown(misc, z_bits[:1] + x_bits[:-1] + y_bits[:-1])
    last = (1 << x_bits[-1], 1 << y_bits[-1])
    parts = [misc] + [across(misc, flips) for flips in (last[0], last[1], last[0] + last[1])]
    gx_out, gx_mark = both_micros(gx_one, gx_two, gx_came)
    acts_out, acts_mark = both_micros(acts[0], acts[1], acts_came)
    grad_lifted = lifted_grads(mod_mine, mod_came, ada_all)
    lifted_came = swap(grad_lifted)
    mine, other, small_mine, small_other = finish(
        keep, came, lifted, parts, (gx_mark, acts_mark, lifted_came)
    )
    came, small_came = swap(other), swap(small_other)
    (
        g_query, g_key, g_value, g_gate, g_out, g_decay, g_up, g_down, g_ada,
        g_b_ada, g_b_up, g_b_down, g_conv, g_b_decay,
    ) = outputs(mine, came, small_mine, small_came)

    grad_lifted = (grad_lifted + lifted_came).reshape(MICRO, SLOTS, D)
    _, pull_silu = jax.vjp(jax.nn.silu, conditions.astype(f32))
    (cond_grads,) = pull_silu(grad_lifted)

    return (
        acts_out[None],
        gx_out[None],
        cond_grads,
        g_ada[None],
        g_b_ada,
        g_query[None],
        g_key[None],
        g_value[None],
        g_gate[None],
        g_out[None],
        g_decay.transpose(1, 2, 0),
        g_b_decay,
        g_conv.transpose(1, 0, 2),
        g_up[None],
        g_b_up,
        g_down.reshape(1, FF // devices, D),
        g_b_down,
    )


def solution(mesh):
    rows = P(None, "row", None)
    mats = P("section", "row", None)
    vector = P("section", None)
    in_specs = (
        rows, rows, rows, P(None, "row"),
        mats, vector, mats, mats, mats, mats, mats, mats, vector, P("section", None, None),
        mats, vector, mats, vector,
    )
    blocks = P("section", None, "row", None)
    out_specs = (
        blocks, blocks, rows,
        mats, vector, mats, mats, mats, mats, mats, mats, vector, P("section", None, None),
        mats, vector, mats, vector,
    )
    return jax.shard_map(
        on_device, mesh=mesh, in_specs=in_specs, out_specs=out_specs, check_vma=False
    )
```

```python
import functools

import jax
import jax.numpy as jnp
from jax import lax
from jax.experimental import pallas as pl
from jax.experimental.pallas import tpu as pltpu
from jax.sharding import PartitionSpec as P

D = 384
HEADS = 6
HEAD_DIM = 64
FF = 1536
MICRO = 2
ROWS = 512
HALF = 256
SLOTS = 2
PAIR = 128
PAIRS = D // PAIR
QKVG = 4 * D
LANES = 128
GROUP = (QKVG + D + LANES) // 2
NEG = -1e30
SCALE = HEAD_DIM**-0.5

bf16 = jnp.bfloat16
f32 = jnp.float32


def mm(left, right):
    return jnp.dot(left, right, preferred_element_type=f32)


def mm_t(left, right):
    return lax.dot_general(left, right, (((1,), (1,)), ((), ())), preferred_element_type=f32)


def split(values):
    high = values.astype(bf16)
    return high, (values - high.astype(f32)).astype(bf16)


def split_three(values):
    high, rest = split(values)
    mid = values - high.astype(f32)
    middle, low = split(mid)
    return high, middle, low


def cat_left(values):
    high, low = split(values)
    return jnp.concatenate([high, low, high], axis=1)


def cat_right(values):
    high, low = split(values)
    return jnp.concatenate([high, high, low], axis=1)


def mm_near(left, right_pair, right_high):
    high, low = split(left)
    wide = mm(high, right_pair)
    return wide[:, :PAIR] + wide[:, PAIR:] + mm(low, right_high)


def lane_iota(rows, columns):
    return lax.broadcasted_iota(jnp.int32, (rows, columns), 1)


def row_iota(rows, columns):
    return lax.broadcasted_iota(jnp.int32, (rows, columns), 0)


def order_matrix(start, rows, wide, to_scan):
    t = row_iota(rows, ROWS) + start
    small = (t & 256) + ((t & 15) << 4) + ((t & 255) >> 4)
    if to_scan:
        large = ((t & 15) << 5) + (t >> 4)
    else:
        large = ((t & 31) << 4) + (t >> 5)
    source = jnp.where(wide, large, small)
    return jnp.where(lane_iota(rows, ROWS) == source, 1.0, 0.0).astype(bf16)


def normalise(values):
    centred = values - jnp.mean(values, axis=-1, keepdims=True)
    rate = lax.rsqrt(jnp.mean(centred * centred, axis=-1, keepdims=True) + 1e-06)
    return centred * rate, rate


def normalise_back(normal, rate, grad):
    return rate * (
        grad
        - jnp.mean(grad, axis=-1, keepdims=True)
        - normal * jnp.mean(grad * normal, axis=-1, keepdims=True)
    )


class In:
    def __init__(self, copy, kept):
        self.copy = copy
        self.kept = kept

    def __call__(self):
        if self.copy is not None:
            self.copy.wait()
            self.copy = None
        return self.kept


class Kernel:
    def __init__(self, layer, layouts):
        self.layer = layer
        self.section = lax.axis_index("section")
        self.own = self.section == layer
        self.layout = layouts[self.section, 0]
        self.wide = self.layout == 0
        self.live_rows = jnp.where(self.wide, ROWS, self.layout * HALF)
        self.pushed = {}

    def load(self, kind, refs, kept, sem):
        if kind == "own":
            mine, other = refs

            @pl.when(self.own)
            def _():
                pltpu.make_async_copy(mine, kept, sem).start()

            @pl.when(jnp.logical_not(self.own))
            def _():
                pltpu.make_async_copy(other, kept, sem).start()

            return In(pltpu.make_async_copy(mine, kept, sem), kept)
        (source,) = refs
        if kind == "micro":
            source = source.at[self.section if source.shape[0] == MICRO else 0]
        copy = pltpu.make_async_copy(source, kept, sem)
        copy.start()
        return In(copy, kept)

    def push(self, name):
        kept, target, sem = self.results[name]
        copy = pltpu.make_async_copy(kept, target, sem)
        copy.start()
        self.pushed[name] = copy

    def finish(self):
        for name in self.results:
            if name not in self.pushed:
                self.push(name)
        for copy in self.pushed.values():
            copy.wait()

    def slot(self, half):
        return jnp.where(self.wide, 0, half)

    def share(self, slot, part):
        row = pl.ds(2 * self.section + slot, 1)
        return self.mods()[row, part * D : (part + 1) * D]

    def bu(self):
        return self.small()[0:1, :]

    def bn(self):
        return self.small()[1:2, :D]

    def ck(self, tap):
        return self.small()[2 + tap : 3 + tap, :D]

    def bd(self):
        return self.small()[5:6, :LANES]


def sigmoid(values):
    return 1.0 / (1.0 + jnp.exp(-values))


GELU_A = 0.7978845608028654
GELU_B = 0.044715


def gelu_parts(values):
    square = values * values
    tanh = jnp.tanh(GELU_A * values * (1.0 + GELU_B * square))
    return square, tanh


def fill_bias(bias, wide):
    bias[:, :HALF] = jnp.full((HALF, HALF), 0.0, f32) + jnp.where(wide, 0.0, NEG)
    causal = row_iota(HALF, HALF) >= lane_iota(HALF, HALF)
    bias[:, HALF:] = jnp.where(causal, 0.0, NEG)


def decay_factors(cum, cumt, bias, head):
    row = cumt[pl.ds(head, 1), :]
    lanes = lane_iota(1, LANES)
    column = jnp.sum(jnp.where(lanes == head, cum[...], 0.0), axis=1, keepdims=True)
    first = jnp.exp(column[:HALF] - row[:, :HALF] + bias[:, HALF:])
    second = jnp.exp(column[HALF:] - row + bias[...])
    return first, second


def head_norm(values, lanes):
    square = values * values
    low = jnp.sum(jnp.where(lanes < HEAD_DIM, square, 0.0), axis=1, keepdims=True)
    high = jnp.sum(jnp.where(lanes < HEAD_DIM, 0.0, square), axis=1, keepdims=True)
    return jnp.where(lanes < HEAD_DIM, low, high) * (1.0 / HEAD_DIM)


def fill_decay(dp, bd, cum, cumt):
    raw = dp[...] + bd
    log_decay = (jnp.minimum(raw, 0.0) - jnp.log1p(jnp.exp(-jnp.abs(raw)))) * (1.0 / 16.0)
    high, middle, low = split_three(log_decay)
    causal = jnp.where(row_iota(ROWS, ROWS) >= lane_iota(ROWS, ROWS), 1.0, 0.0).astype(bf16)
    cum[...] = mm(causal, high) + mm(causal, middle) + mm(causal, low)
    cumt[...] = jnp.transpose(cum[...])


def columns(index, first=0):
    return slice(index * PAIR + first, index * PAIR + first + PAIR)


def attn_forward_body(k):
    flip = k.layer == 1
    wide = k.wide
    x = k.x()
    k.mods()

    def first(i, carry):
        rows = pl.ds(pl.multiple_of(i * HALF, HALF), HALF)
        slot = k.slot(i)
        normal, _ = normalise(x[rows, :].astype(f32))
        k.inner[rows, :] = (normal * (1.0 + k.share(slot, 1)) + k.share(slot, 0)).astype(bf16)
        return carry

    lax.fori_loop(0, 2, first, 0)
    w_qk = k.w_qk()
    w_vgd = k.w_vgd()

    def project(i, carry):
        start = i * HALF
        rows = pl.ds(start, HALF)
        if flip:
            part = mm(order_matrix(start, HALF, wide, True), k.inner[...]).astype(bf16)
        else:
            part = k.inner[rows, :]
        k.ordered[rows, :] = part
        k.qkvg[rows, : 2 * D] = mm(part, w_qk[...])
        k.qkvg[rows, 2 * D :] = mm(part, w_vgd[:, : 2 * D])
        k.dp[rows, :] = mm(part, w_vgd[:, 2 * D :])
        return carry

    lax.fori_loop(0, 2, project, 0)
    k.small()
    for name in ("ordered", "qkvg", "dp"):
        k.push(name)
    fill_decay(k.dp, k.bd(), k.cum, k.cumt)
    fill_bias(k.bias, wide)

    vpad = k.vpad
    vpad[0:8, :] = jnp.zeros((8, D), f32)
    vpad[8 : 8 + ROWS, :] = k.qkvg[:, 2 * D : 3 * D]
    position = row_iota(ROWS, 1) & jnp.where(wide, ROWS - 1, HALF - 1)
    one = jnp.where(position >= 1, vpad[7 : 7 + ROWS, :], 0.0)
    two = jnp.where(position >= 2, vpad[6 : 6 + ROWS, :], 0.0)
    k.vc[...] = k.ck(0) * vpad[8 : 8 + ROWS, :] + k.ck(1) * one + k.ck(2) * two
    for name in ("cum", "cumt", "vc"):
        k.push(name)

    def pair(p, carry):
        lanes = lane_iota(1, PAIR)
        queries = cat_left(k.qkvg[:, columns(p)] * SCALE)
        keys = k.qkvg[:, columns(p, D)]
        value_high, value_low = split(k.vc[:, columns(p)])
        values = jnp.concatenate([value_high, value_low], axis=1)
        parts = []
        for e in range(2):
            key_cat = cat_right(jnp.where((lanes // HEAD_DIM) == e, keys, 0.0))
            first, second = decay_factors(k.cum, k.cumt, k.bias, 2 * p + e)
            first = first * mm_t(queries[:HALF], key_cat[:HALF])
            second = second * mm_t(queries[HALF:], key_cat)
            parts.append(
                jnp.concatenate(
                    [
                        mm_near(first, values[:HALF], value_high[:HALF]),
                        mm_near(second, values, value_high),
                    ],
                    axis=0,
                )
            )
        total = jnp.where(lanes < HEAD_DIM, parts[0], parts[1])
        k.o[:, columns(p)] = total
        gate = k.qkvg[:, columns(p, 3 * D)]
        normed = total * lax.rsqrt(head_norm(total, lanes) + 1.0)
        mixed = (normed * (gate * sigmoid(gate))).astype(bf16)
        if flip:
            k.inner[:, columns(p)] = mixed
        else:
            k.gated[:, columns(p)] = mixed
        return carry

    for p in range(PAIRS):
        pair(p, 0)
    k.push("o")
    if flip:

        def back(i, carry):
            start = i * HALF
            k.gated[pl.ds(start, HALF), :] = mm(
                order_matrix(start, HALF, wide, False), k.inner[...]
            ).astype(bf16)
            return carry

        lax.fori_loop(0, 2, back, 0)


def ffn_forward_body(k):
    gated, x = k.gated(), k.x()
    k.mods(), k.small()

    def tile(i, carry):
        start = i * HALF
        rows = pl.ds(start, HALF)
        slot = k.slot(i)
        grown = mm(gated[rows, :], k.wo()[...])
        k.branch[rows, :] = grown
        middle = x[rows, :].astype(f32) + k.share(slot, 2) * grown
        normal, _ = normalise(middle)
        inner = (normal * (1.0 + k.share(slot, 4)) + k.share(slot, 3)).astype(bf16)
        up = mm(inner, k.wu()[...]) + k.bu()
        _, tanh = gelu_parts(up)
        hidden = (0.5 * up * (1.0 + tanh)).astype(bf16)
        low = mm(hidden, k.wn()[...])
        k.down[rows, :] = low
        result = middle + k.share(slot, 5) * (low + k.bn())
        live = (row_iota(HALF, 1) + start) < k.live_rows
        k.out[rows, :] = jnp.where(live, result, 0.0).astype(bf16)
        return carry

    for i in range(2):
        tile(i, 0)
    if k.layer == 1:
        k.sent[...] = jnp.where(k.section == 0, k.out[...].astype(f32), x[...].astype(f32)).astype(bf16)


def ffn_backward_body(k):
    gmod, gbu, gbn = k.gmod, k.gbu, k.gbn
    gmod[...] = jnp.zeros(gmod.shape, f32)
    gbu[...] = jnp.zeros(gbu.shape, f32)
    gbn[...] = jnp.zeros(gbn.shape, f32)
    k.mods(), k.small()
    x, grad, branch, down = k.x(), k.grad(), k.branch(), k.down()

    def tile(i, carry):
        start = i * HALF
        rows = pl.ds(start, HALF)
        slot = k.slot(i)

        def add(part, values):
            where = (pl.ds(slot, 1), slice((part - 2) * D, (part - 1) * D))
            gmod[where] = gmod[where] + jnp.sum(values, axis=0, keepdims=True)

        grown = branch[rows, :]
        middle = x[rows, :].astype(f32) + k.share(slot, 2) * grown
        normal, rate = normalise(middle)
        inner = (normal * (1.0 + k.share(slot, 4)) + k.share(slot, 3)).astype(bf16)
        k.inner_s[rows, :] = inner
        live = (row_iota(HALF, 1) + start) < k.live_rows
        above = jnp.where(live, grad[rows, :].astype(f32), 0.0)
        add(5, above * (down[rows, :] + k.bn()))
        grad_down = above * k.share(slot, 5)
        gbn[...] = gbn[...] + jnp.sum(grad_down, axis=0, keepdims=True)
        down_low = grad_down.astype(bf16)
        k.down_s[rows, :] = down_low
        up = mm(inner, k.wu()[...]) + k.bu()
        square, tanh = gelu_parts(up)
        half = 0.5 * (1.0 + tanh)
        k.hidden_s[rows, :] = (up * half).astype(bf16)
        slope = half + 0.5 * up * (1.0 - tanh * tanh) * (
            GELU_A * (1.0 + 3.0 * GELU_B * square)
        )
        grad_up = mm_t(down_low, k.wn()[...]) * slope
        gbu[...] = gbu[...] + jnp.sum(grad_up, axis=0, keepdims=True)
        up_low = grad_up.astype(bf16)
        k.up_s[rows, :] = up_low
        grad_inner = mm_t(up_low, k.wu()[...])
        add(3, grad_inner)
        add(4, grad_inner * normal)
        grad_middle = above + normalise_back(
            normal, rate, grad_inner * (1.0 + k.share(slot, 4))
        )
        k.mid_grad[rows, :] = grad_middle
        add(2, grad_middle * grown)
        k.branch_low[rows, :] = (grad_middle * k.share(slot, 2)).astype(bf16)
        return carry

    for i in range(2):
        tile(i, 0)
    k.push("mid_grad")
    k.push("branch_low")

    def weights(j, carry):
        part = pl.ds(pl.multiple_of(j * HALF, HALF), HALF)
        hidden_t = jnp.transpose(k.hidden_s[:, part].astype(f32)).astype(bf16)
        k.gwn[part, :] = mm(hidden_t, k.down_s[...])
        return carry

    lax.fori_loop(0, FF // HALF, weights, 0)
    inner_t = jnp.transpose(k.inner_s[...].astype(f32)).astype(bf16)
    if k.packed:
        devices, shard, _ = k.keep.shape

        def halves(j, carry):
            for kept, own in ((k.keep, c_section), (k.sent, 1 - c_section)):
                columns = pl.ds(pl.multiple_of(j * HALF + own * (FF // 2), HALF), HALF)
                here = pl.ds(pl.multiple_of(j * HALF, HALF), HALF)
                part = mm(inner_t, k.up_s[:, columns]).reshape(devices, shard, HALF)
                kept[:, :, here] = part.astype(kept.dtype)
            return carry

        c_section = k.section
        lax.fori_loop(0, FF // 2 // HALF, halves, 0)

        def owner(r, carry):
            for kept, own in ((k.keep, c_section), (k.sent, 1 - c_section)):
                for piece in range(2):
                    start = pl.multiple_of((4 * r + 2 * own + piece) * shard, 8)
                    rows = k.gwn[pl.ds(start, shard), :]
                    at = FF // 2 + piece * D
                    kept[r, :, at : at + D] = rows.astype(kept.dtype)
            return carry

        lax.fori_loop(0, devices, owner, 0)
        k.push("keep")
        k.push("sent")
    else:
        k.gwu[...] = mm(inner_t, k.up_s[...])
    gated = k.gated()
    k.gwo[...] = mm(jnp.transpose(gated[...].astype(f32)).astype(bf16), k.branch_low[...])

    short = jnp.concatenate([gbn[...], jnp.zeros((1, FF - D), f32)], axis=1)
    k.sums[...] = jnp.concatenate(
        [gmod[0:SLOTS, :], gbu[...], short, jnp.zeros((4, FF), f32)], axis=0
    )


def mixer_backward_body(k):
    flip = k.layer == 1
    wide = k.wide
    mixed_s, low, dv_s, rows_s, cols_s = k.mixed_s, k.low, k.dv_s, k.rows_s, k.cols_s
    fill_bias(k.bias, wide)
    branch_low, wo = k.branch_low(), k.wo()

    def first(i, carry):
        start = i * HALF
        rows = pl.ds(start, HALF)
        if flip:
            part = mm(order_matrix(start, HALF, wide, True), branch_low[...]).astype(bf16)
        else:
            part = branch_low[rows, :]
        mixed_s[rows, :] = mm_t(part, wo[...])
        return carry

    lax.fori_loop(0, 2, first, 0)
    rows_s[...] = jnp.zeros(rows_s.shape, f32)
    cols_s[...] = jnp.zeros(cols_s.shape, f32)
    qkvg, vc, cum, cumt, o = k.qkvg(), k.vc(), k.cum(), k.cumt(), k.o()
    k.small()

    def pair(p, carry):
        lanes = lane_iota(1, PAIR)
        total = o[:, columns(p)]
        gate = qkvg[:, columns(p, 3 * D)]
        above = mixed_s[:, columns(p)]
        rate = lax.rsqrt(head_norm(total, lanes) + 1.0)
        sig = sigmoid(gate)
        grad_gate = above * (total * rate) * (sig * (1.0 + gate * (1.0 - sig)))
        low[:, columns(p, 3 * D)] = grad_gate.astype(bf16)
        grad_normed = above * (gate * sig)
        product = grad_normed * total
        inside = jnp.where(
            lanes < HEAD_DIM,
            jnp.sum(jnp.where(lanes < HEAD_DIM, product, 0.0), axis=1, keepdims=True),
            jnp.sum(jnp.where(lanes < HEAD_DIM, 0.0, product), axis=1, keepdims=True),
        ) * (1.0 / HEAD_DIM)
        grad_o = rate * grad_normed - total * (rate * rate * rate) * inside

        queries = qkvg[:, columns(p)] * SCALE
        keys = qkvg[:, columns(p, D)]
        values = vc[:, columns(p)]
        query_cat = cat_left(queries)
        grad_cat = cat_left(grad_o)
        key_high, key_low = split(keys)
        key_pair = jnp.concatenate([key_high, key_low], axis=1)
        query_t = jnp.transpose(queries)
        grad_t = jnp.transpose(grad_o)
        grad_q = []
        grad_k = []
        grad_v = []
        for e in range(2):
            mine = (lanes // HEAD_DIM) == e
            head = 2 * p + e
            key_cat = cat_right(jnp.where(mine, keys, 0.0))
            value_cat = cat_right(jnp.where(mine, values, 0.0))
            first, second = decay_factors(cum, cumt, k.bias, head)
            raw_first = mm_t(query_cat[:HALF], key_cat[:HALF])
            raw_second = mm_t(query_cat[HALF:], key_cat)
            grad_first = first * mm_t(grad_cat[:HALF], value_cat[:HALF])
            grad_second = second * mm_t(grad_cat[HALF:], value_cat)
            score_first = raw_first * first
            score_second = raw_second * second
            pull_first = grad_first * raw_first
            pull_second = grad_second * raw_second
            here = lanes == head
            rows_s[:HALF, :] = rows_s[:HALF, :] + jnp.where(
                here, jnp.sum(pull_first, axis=1, keepdims=True), 0.0
            )
            rows_s[HALF:, :] = rows_s[HALF:, :] + jnp.where(
                here, jnp.sum(pull_second, axis=1, keepdims=True), 0.0
            )
            low_cols = jnp.sum(pull_second, axis=0, keepdims=True)
            cols_s[pl.ds(head, 1), :HALF] = low_cols[:, :HALF] + jnp.sum(
                pull_first, axis=0, keepdims=True
            )
            cols_s[pl.ds(head, 1), HALF:] = low_cols[:, HALF:]
            grad_q.append(
                jnp.concatenate(
                    [
                        mm_near(grad_first, key_pair[:HALF], key_high[:HALF]),
                        mm_near(grad_second, key_pair, key_high),
                    ],
                    axis=0,
                )
            )

            def turned(source_t, block_first, block_second):
                high, low = split(source_t[e * HEAD_DIM : (e + 1) * HEAD_DIM, :])
                both = jnp.concatenate([high, low], axis=0)
                first_high, first_low = split(block_first)
                second_high, second_low = split(block_second)
                one = mm(both[:, :HALF], first_high)
                one = one[:HEAD_DIM] + one[HEAD_DIM:] + mm(high[:, :HALF], first_low)
                two = mm(both[:, HALF:], second_high)
                two = two[:HEAD_DIM] + two[HEAD_DIM:] + mm(high[:, HALF:], second_low)
                return jnp.concatenate([two[:, :HALF] + one, two[:, HALF:]], axis=1)

            grad_k.append(turned(query_t, grad_first, grad_second))
            grad_v.append(turned(grad_t, score_first, score_second))
        query_grad = jnp.where(lanes < HEAD_DIM, grad_q[0], grad_q[1]) * SCALE
        low[:, columns(p)] = query_grad.astype(bf16)
        low[:, columns(p, D)] = jnp.transpose(jnp.concatenate(grad_k, axis=0)).astype(bf16)
        dv_s[:ROWS, columns(p)] = jnp.transpose(jnp.concatenate(grad_v, axis=0))
        return carry

    for p in range(PAIRS):
        pair(p, 0)

    pulled = rows_s[...] - jnp.transpose(cols_s[...])
    high, middle, rest = split_three(pulled)
    upper_first = jnp.concatenate(
        [
            jnp.where(row_iota(HALF, HALF) <= lane_iota(HALF, HALF), 1.0, 0.0),
            jnp.full((HALF, HALF), 0.0, f32) + jnp.where(wide, 1.0, 0.0),
        ],
        axis=1,
    ).astype(bf16)
    upper_second = upper_first[:, :HALF]
    later = jnp.concatenate(
        [
            mm(upper_first, high) + mm(upper_first, middle) + mm(upper_first, rest),
            mm(upper_second, high[HALF:]) + mm(upper_second, middle[HALF:])
            + mm(upper_second, rest[HALF:]),
        ],
        axis=0,
    )
    grad_dp = later * (1.0 / 16.0) * sigmoid(-(k.dp()[...] + k.bd()))
    grad_bd = jnp.sum(grad_dp, axis=0, keepdims=True)
    low[:, QKVG:] = grad_dp.astype(bf16)

    dv_s[ROWS:, :] = jnp.zeros((8, D), f32)
    position = row_iota(ROWS, 1) & jnp.where(wide, ROWS - 1, HALF - 1)
    last = jnp.where(wide, ROWS - 1, HALF - 1)
    here = dv_s[0:ROWS, :]
    one = jnp.where(position <= last - 1, dv_s[1 : 1 + ROWS, :], 0.0)
    two = jnp.where(position <= last - 2, dv_s[2 : 2 + ROWS, :], 0.0)
    value = qkvg[:, 2 * D : 3 * D]
    low[:, 2 * D : 3 * D] = (k.ck(0) * here + k.ck(1) * one + k.ck(2) * two).astype(bf16)
    k.push("low")

    taps = [jnp.sum(rows * value, axis=0, keepdims=True) for rows in (here, one, two)]
    rest = jnp.concatenate([grad_bd, jnp.zeros((1, D - LANES), f32)], axis=1)
    k.sums[...] = jnp.concatenate([*taps, rest, jnp.zeros((4, D), f32)], axis=0)

    ordered_t = jnp.transpose(k.ordered()[...].astype(f32)).astype(bf16)
    gwo = k.gwo()
    gw = k.gw

    def weights(j, carry):
        part = pl.ds(pl.multiple_of(j * HALF, HALF), HALF)
        gw[:, part] = mm(ordered_t, low[:, part])
        return carry

    lax.fori_loop(0, QKVG // HALF, weights, 0)
    gw[:, QKVG : QKVG + D] = gwo[...]
    gw[:, QKVG + D :] = mm(ordered_t, low[:, QKVG:])

    def halves(j, carry):
        here = pl.ds(pl.multiple_of(j * HALF, HALF), HALF)
        keep = pl.ds(pl.multiple_of(j * HALF + k.section * GROUP, HALF), HALF)
        send = pl.ds(pl.multiple_of(j * HALF + (1 - k.section) * GROUP, HALF), HALF)
        k.gw_keep[:, here] = gw[:, keep]
        k.gw_send[:, here] = gw[:, send].astype(bf16)
        return carry

    lax.fori_loop(0, GROUP // HALF, halves, 0)


def input_backward_body(k):
    flip = k.layer == 1
    wide = k.wide
    gmod, mixed_s, perm_s = k.gmod, k.mixed_s, k.perm_s
    gmod[...] = jnp.zeros(gmod.shape, f32)
    low, w_qk, w_vgd = k.low(), k.w_qk(), k.w_vgd()

    def inner_grad(i, carry):
        rows = pl.ds(pl.multiple_of(i * HALF, HALF), HALF)
        mixed_s[rows, :] = mm_t(low[rows, : 2 * D], w_qk[...]) + mm_t(
            low[rows, 2 * D :], w_vgd[...]
        )
        return carry

    lax.fori_loop(0, 2, inner_grad, 0)
    if flip:
        high, middle, rest = split_three(mixed_s[...])
        perm_s[:, :D] = high
        perm_s[:, D : 2 * D] = middle
        perm_s[:, 2 * D :] = rest
    x, mid_grad = k.x(), k.mid_grad()
    k.mods()

    def tile(i, carry):
        start = i * HALF
        rows = pl.ds(start, HALF)
        slot = k.slot(i)
        if flip:
            three = mm(order_matrix(start, HALF, wide, False), perm_s[...])
            grad = three[:, :D] + three[:, D : 2 * D] + three[:, 2 * D :]
        else:
            grad = mixed_s[rows, :]
        normal, rate = normalise(x[rows, :].astype(f32))
        where = (pl.ds(slot, 1), slice(0, D))
        gmod[where] = gmod[where] + jnp.sum(grad, axis=0, keepdims=True)
        where = (pl.ds(slot, 1), slice(D, 2 * D))
        gmod[where] = gmod[where] + jnp.sum(grad * normal, axis=0, keepdims=True)
        total = mid_grad[rows, :] + normalise_back(normal, rate, grad * (1.0 + k.share(slot, 1)))
        k.gx[rows, :] = total
        k.gx_low[rows, :] = total.astype(bf16)
        return carry

    for i in range(2):
        tile(i, 0)
    k.push("gx_low")
    k.push("gx")
    ffn, mixer = k.ffn_sums(), k.mixer_sums()
    k.mod_low[...] = jnp.concatenate([gmod[...], ffn[...]], axis=1).astype(bf16)
    if k.layer == 0:
        first = k.section == 0
        k.gx_send[...] = jnp.where(first, k.gx_two()[...], k.gx[...])
        one, two = k.mod_low[...].astype(f32), k.mod_two()[...].astype(f32)
        k.mod_mine[...] = jnp.where(first, one, two).astype(bf16)
        k.mod_send[...] = jnp.where(first, two, one).astype(bf16)
    half = 2 * D
    rest = ffn[0:1, :] + ffn[1:2, :]
    k.sums[...] = jnp.concatenate(
        [
            gmod[0:1, :] + gmod[1:2, :],
            rest[:, :half],
            rest[:, half:],
            ffn[2:3, :half],
            ffn[2:3, half:],
            jnp.concatenate([ffn[3:4, :D], mixer[0:1, :]], axis=1),
            jnp.concatenate([mixer[1:2, :], mixer[2:3, :]], axis=1),
            jnp.concatenate([mixer[3:4, :], jnp.zeros((1, D), f32)], axis=1),
        ],
        axis=0,
    )


ANY = pl.BlockSpec(memory_space=pl.ANY)
VMEM = pl.BlockSpec(memory_space=pltpu.VMEM)
HBM = pl.BlockSpec(memory_space=pltpu.HBM)


def call(body, layer, layouts, ins, outs, scratch, flops, packed=None, after=()):
    arrays = []
    counts = []
    kept = []
    places = []
    for kind, given, part in ins.values():
        places.extend([ANY] * 2 if kind == "own" else [HBM])
        given = given if kind == "own" else (given,)
        arrays.extend(given)
        counts.append(len(given))
        rows, wide = given[0].shape[-2:]
        start, stop = part or (0, wide)
        kept.append(pltpu.VMEM((rows, stop - start), given[0].dtype))

    def kernel(*refs):
        refs = list(refs)
        take = lambda count: [refs.pop(0) for _ in range(count)]
        (layouts_ref,) = take(1)
        sources = [take(count) for count in counts]
        take(len(after))
        targets = take(len(outs))
        buffers = take(len(ins))
        results = take(len(outs))
        rest = take(len(scratch))
        in_sems, out_sems = refs
        k = Kernel(layer, layouts_ref)
        k.packed = packed
        for number, (name, (kind, _, part)) in enumerate(ins.items()):
            given = sources[number]
            if part is not None:
                given = [ref.at[:, part[0] : part[1]] for ref in given]
            setattr(k, name, k.load(kind, given, buffers[number], in_sems.at[number]))
        k.results = {}
        for number, name in enumerate(outs):
            setattr(k, name, results[number])
            k.results[name] = (results[number], targets[number], out_sems.at[number])
        for name, ref in zip(scratch, rest):
            setattr(k, name, ref)
        body(k)
        k.finish()

    return pl.pallas_call(
        kernel,
        out_shape=[jax.ShapeDtypeStruct(shape, kind) for shape, kind, _ in outs.values()],
        in_specs=[pl.BlockSpec(memory_space=pltpu.SMEM)] + places + [ANY] * len(after),
        out_specs=[HBM if for_kernel else ANY for _, _, for_kernel in outs.values()],
        scratch_shapes=kept
        + [pltpu.VMEM(shape, kind) for shape, kind, _ in outs.values()]
        + [pltpu.VMEM(shape, kind) for shape, kind in scratch.values()]
        + [pltpu.SemaphoreType.DMA((len(ins),)), pltpu.SemaphoreType.DMA((len(outs),))],
        compiler_params=pltpu.CompilerParams(vmem_limit_bytes=56 * 1024 * 1024),
        cost_estimate=pl.CostEstimate(flops=flops, bytes_accessed=4 << 20, transcendentals=0),
    )(layouts, *arrays, *after)


def own(pair, part=None):
    return ("own", pair, part)


def plain(array):
    return ("plain", array, None)


def micro(array):
    return ("micro", array, None)


AT_UP = (0, FF)
AT_OUT = (FF, FF + D)


def attn_forward(layer, layouts, x, mods, small, qk, vgd):
    return call(
        attn_forward_body,
        layer,
        layouts,
        dict(
            x=micro(x),
            mods=own(mods),
            w_qk=own(qk),
            w_vgd=own(vgd),
            small=own(small),
        ),
        dict(
            ordered=((ROWS, D), bf16, True),
            qkvg=((ROWS, QKVG), f32, True),
            dp=((ROWS, LANES), f32, True),
            vc=((ROWS, D), f32, True),
            cum=((ROWS, LANES), f32, True),
            cumt=((LANES, ROWS), f32, True),
            o=((ROWS, D), f32, True),
            gated=((ROWS, D), bf16, True),
        ),
        dict(
            inner=((ROWS, D), bf16),
            vpad=((ROWS + 8, D), f32),
            bias=((HALF, ROWS), f32),
        ),
        4 * 10**9,
    )


def ffn_forward(layer, layouts, x, mods, small, gated, upo, down):
    return call(
        ffn_forward_body,
        layer,
        layouts,
        dict(
            gated=plain(gated),
            x=micro(x),
            wo=own(upo, AT_OUT),
            mods=own(mods),
            small=own(small),
            wu=own(upo, AT_UP),
            wn=own(down),
        ),
        dict(
            out=((ROWS, D), bf16, True),
            branch=((ROWS, D), f32, True),
            down=((ROWS, D), f32, True),
            **({"sent": ((ROWS, D), bf16, False)} if layer == 1 else {}),
        ),
        {},
        3 * 10**9,
    )


def ffn_backward(
    layer, layouts, x, mods, small, gated, branch, down_raw, grad, upo, down, devices, after=()
):
    shard = D // devices
    in_kernel = shard % 8 == 0
    if in_kernel:
        sums = dict(
            keep=((devices, shard, FF), f32, True),
            sent=((devices, shard, FF), bf16, False),
        )
    else:
        sums = dict(gwu=((D, FF), f32, False), gwn=((FF, D), f32, False))
    return call(
        ffn_backward_body,
        layer,
        layouts,
        dict(
            mods=own(mods),
            small=own(small),
            x=micro(x),
            grad=micro(grad),
            branch=plain(branch),
            down=plain(down_raw),
            wu=own(upo, AT_UP),
            wn=own(down),
            gated=plain(gated),
        ),
        dict(
            mid_grad=((ROWS, D), f32, True),
            branch_low=((ROWS, D), bf16, True),
            gwo=((D, D), f32, True),
            sums=((8, FF), f32, True),
            **sums,
        ),
        dict(
            **({"gwn": ((FF, D), f32)} if in_kernel else {}),
            hidden_s=((ROWS, FF), bf16),
            inner_s=((ROWS, D), bf16),
            up_s=((ROWS, FF), bf16),
            down_s=((ROWS, D), bf16),
            gmod=((8, FF), f32),
            gbu=((1, FF), f32),
            gbn=((1, D), f32),
        ),
        5 * 10**9,
        packed=in_kernel,
        after=after,
    )


def mixer_backward(layer, layouts, small, saved, branch_low, gwo, upo, after=()):
    ordered, qkvg, dp, vc, cum, cumt, o = saved
    return call(
        mixer_backward_body,
        layer,
        layouts,
        dict(
            branch_low=plain(branch_low),
            wo=own(upo, AT_OUT),
            qkvg=plain(qkvg),
            vc=plain(vc),
            cum=plain(cum),
            cumt=plain(cumt),
            o=plain(o),
            small=own(small),
            dp=plain(dp),
            ordered=plain(ordered),
            gwo=plain(gwo),
        ),
        dict(
            low=((ROWS, QKVG + LANES), bf16, True),
            gw_keep=((D, GROUP), f32, True),
            gw_send=((D, GROUP), bf16, False),
            sums=((8, D), f32, True),
        ),
        dict(
            mixed_s=((ROWS, D), f32),
            dv_s=((ROWS + 8, D), f32),
            rows_s=((ROWS, LANES), f32),
            cols_s=((LANES, ROWS), f32),
            bias=((HALF, ROWS), f32),
            gw=((D, 2 * GROUP), f32),
        ),
        7 * 10**9,
        after=after,
    )


def input_backward(
    layer, layouts, x, mods, low, mid_grad, ffn_sums, mixer_sums, qk, vgd, two=None, after=()
):
    extra_in, extra_out = {}, {}
    if two is not None:
        extra_in = dict(gx_two=plain(two[0]), mod_two=plain(two[1]))
        extra_out = dict(
            gx_send=((ROWS, D), f32, False),
            mod_mine=((8, 6 * D), bf16, False),
            mod_send=((8, 6 * D), bf16, False),
        )
    return call(
        input_backward_body,
        layer,
        layouts,
        dict(
            low=plain(low),
            w_qk=own(qk),
            w_vgd=own(vgd),
            x=micro(x),
            mid_grad=plain(mid_grad),
            mods=own(mods),
            ffn_sums=plain(ffn_sums),
            mixer_sums=plain(mixer_sums),
            **extra_in,
        ),
        dict(
            gx=((ROWS, D), f32, True),
            gx_low=((ROWS, D), bf16, True),
            mod_low=((8, 6 * D), bf16, True),
            sums=((8, 2 * D), f32, False),
            **extra_out,
        ),
        dict(
            mixed_s=((ROWS, D), f32),
            perm_s=((ROWS, 3 * D), bf16),
            gmod=((8, 2 * D), f32),
        ),
        2 * 10**9,
        after=after,
    )


def small_kernel(b_up, b_down, taps, b_decay, packed):
    packed[...] = jnp.zeros(packed.shape, f32)
    packed[0:1, :] = b_up[...]
    packed[1:2, :D] = b_down[...]
    packed[2:5, :D] = taps[0]
    packed[5:6, :HEADS] = b_decay[...]


def pack_small(b_up, b_down, taps, b_decay):
    return pl.pallas_call(
        small_kernel,
        out_shape=jax.ShapeDtypeStruct((8, FF), f32),
        in_specs=[VMEM] * 4,
        out_specs=VMEM,
        compiler_params=pltpu.CompilerParams(vmem_limit_bytes=8 * 1024 * 1024),
    )(b_up, b_down, taps, b_decay)


def pack_kernel(
    w_query, w_key, w_value, w_gate, w_out, w_decay, w_up, w_down, w_ada, conditions,
    qk, vgd, upo, down, ada, lifted,
):
    qk[:, :D] = w_query[0]
    qk[:, D:] = w_key[0]
    vgd[:, :D] = w_value[0]
    vgd[:, D : 2 * D] = w_gate[0]
    place = jnp.where(row_iota(HEADS, LANES) == lane_iota(HEADS, LANES), 1.0, 0.0).astype(bf16)
    turned = lax.dot_general(
        w_decay[0], place, (((0,), (0,)), ((), ())), preferred_element_type=f32
    )
    vgd[:, 2 * D :] = turned.astype(bf16)
    upo[:, :FF] = w_up[0]
    upo[:, FF:] = w_out[0]
    down[...] = w_down[0]
    ada[...] = w_ada[0]
    values = jnp.concatenate([conditions[m].astype(f32) for m in range(MICRO)], axis=0)
    lifted[0] = (values * sigmoid(values)).astype(bf16)


def pack(*weights):
    shard = weights[0].shape[1]
    shapes = [(shard, width) for width in (2 * D, 2 * D + LANES, FF + D)]
    shapes += [weights[7].shape[1:], weights[8].shape[1:], (1, MICRO * SLOTS, D)]
    return pl.pallas_call(
        pack_kernel,
        out_shape=[jax.ShapeDtypeStruct(shape, bf16) for shape in shapes],
        in_specs=[VMEM] * len(weights),
        out_specs=[VMEM] * len(shapes),
        compiler_params=pltpu.CompilerParams(vmem_limit_bytes=8 * 1024 * 1024),
    )(*weights)


def join_kernel(bits, waits, *refs):
    count = len(bits)
    held, came, out = refs[:count], refs[count : 2 * count], refs[2 * count + waits :]
    for i, bit in enumerate(bits):
        mine = (lax.axis_index("row") >> bit) & 1
        out[i][:, mine] = held[i][...]
        out[i][:, 1 - mine] = came[i][...]


def join(held, came, bits, after=()):
    def parts(array, bit):
        axis = axis_of(bit)
        above = 1
        for size in array.shape[:axis]:
            above *= size
        return array.reshape((above, -1) + array.shape[-2:])

    split_held = [parts(array, bit) for array, bit in zip(held, bits)]
    split_came = [parts(array, bit) for array, bit in zip(came, bits)]
    out = pl.pallas_call(
        functools.partial(join_kernel, bits, len(after)),
        out_shape=[
            jax.ShapeDtypeStruct(array.shape[:1] + (2,) + array.shape[1:], array.dtype)
            for array in split_held
        ],
        in_specs=[VMEM] * (2 * len(held)) + [ANY] * len(after),
        out_specs=[VMEM] * len(held),
        compiler_params=pltpu.CompilerParams(vmem_limit_bytes=8 * 1024 * 1024),
        cost_estimate=pl.CostEstimate(flops=10**6, bytes_accessed=10**6, transcendentals=0),
    )(*split_held, *split_came, *after)
    joined = []
    for array, result, bit in zip(held, out, bits):
        shape = list(array.shape)
        shape[axis_of(bit)] = 2
        joined.append(result.reshape(shape))
    return joined


def lifted_kernel(mine, came, ada, out, kept, sem):
    copy = pltpu.make_async_copy(ada, kept, sem)
    copy.start()
    first = lax.axis_index("section") == 0
    pair = mine[0:SLOTS, :].astype(f32), came[0:SLOTS, :].astype(f32)
    grad = jnp.concatenate(
        [jnp.where(first, pair[0], pair[1]), jnp.where(first, pair[1], pair[0])], axis=0
    ).astype(bf16)
    copy.wait()
    out[...] = mm_t(grad, kept[...])


def lifted_grads(mine, came, ada):
    return pl.pallas_call(
        lifted_kernel,
        out_shape=jax.ShapeDtypeStruct((MICRO * SLOTS, D), f32),
        in_specs=[VMEM, VMEM, ANY],
        out_specs=VMEM,
        scratch_shapes=[pltpu.VMEM((D, 6 * D), bf16), pltpu.SemaphoreType.DMA],
        compiler_params=pltpu.CompilerParams(vmem_limit_bytes=16 * 1024 * 1024),
        cost_estimate=pl.CostEstimate(flops=10**9, bytes_accessed=2 << 20, transcendentals=0),
    )(mine, came, ada)


def term_kernel(*refs):
    *terms, stays, goes = refs
    stays[...] = sum(ref[:, 0] for ref in terms)
    goes[...] = sum(ref[:, 1] for ref in terms)


def term_step(below, *terms):
    tail = terms[0].shape[1:]
    above = terms[0].shape[0] // (2 * below)
    shape = jax.ShapeDtypeStruct((above, below) + tail, f32)
    out = pl.pallas_call(
        term_kernel,
        out_shape=[shape] * 2,
        in_specs=[VMEM] * len(terms),
        out_specs=[VMEM] * 2,
        compiler_params=pltpu.CompilerParams(vmem_limit_bytes=8 * 1024 * 1024),
        cost_estimate=pl.CostEstimate(flops=10**6, bytes_accessed=10**6, transcendentals=0),
    )(*[term.reshape((above, 2, below) + tail) for term in terms])
    return [array.reshape((above * below,) + tail) for array in out]


def step_kernel(bit, widths, counts, waits, *refs):
    mine = (lax.axis_index("row") >> bit) & 1
    count, many = len(widths), len(counts)
    refs = list(refs)
    take = lambda number: [refs.pop(0) for _ in range(number)]
    sources = take(count + many)
    take(waits)
    targets = take(count + 1)
    buffers = take(count + many)
    results = take(count + 1)
    in_sems, out_sems = refs
    arrive = [
        pltpu.make_async_copy(source, buffer, in_sems.at[i])
        for i, (source, buffer) in enumerate(zip(sources, buffers))
    ]
    leave = [
        pltpu.make_async_copy(result, target, out_sems.at[i])
        for i, (result, target) in enumerate(zip(results, targets))
    ]
    for copy in arrive:
        copy.start()
    kept, came = buffers[:count], buffers[count:]
    places = [(j, i) for j, number in enumerate(counts) for i in range(number)]
    goes = results[count]
    at = 0
    for i in range(count):
        j, place = places[i]
        arrive[i].wait()
        if place == 0:
            arrive[count + j].wait()
        start = sum(widths[i - place : i])
        columns = slice(start, start + widths[i])
        total = kept[i][:, 1 - mine] + came[j][:, 1 - mine, :, :, columns].astype(f32)
        goes[:, :, :, at : at + widths[i]] = total.astype(bf16)
        at += widths[i]
    leave[count].start()
    for i in range(count):
        j, place = places[i]
        start = sum(widths[i - place : i])
        columns = slice(start, start + widths[i])
        results[i][...] = kept[i][:, mine] + came[j][:, mine, :, :, columns].astype(f32)
        leave[i].start()
    for copy in leave:
        copy.wait()


def step(kept, came, bit, below=1, after=()):
    blocks, rows = kept[0].shape[0] // 2, kept[0].shape[1]
    above = blocks // below
    paired = lambda array: array.reshape((above, 2, below) + array.shape[1:])
    widths = [array.shape[2] for array in kept]
    size = sum(array.size for array in kept)
    arrays = [paired(array) for array in kept] + [paired(array) for array, _ in came]
    shapes = [((above, below, rows, width), f32) for width in widths]
    shapes.append(((above, below, rows, sum(widths)), bf16))
    out = pl.pallas_call(
        functools.partial(step_kernel, bit, widths, [count for _, count in came], len(after)),
        out_shape=[jax.ShapeDtypeStruct(shape, kind) for shape, kind in shapes],
        in_specs=[HBM] * len(kept) + [ANY] * (len(came) + len(after)),
        out_specs=[HBM] * len(kept) + [ANY],
        scratch_shapes=[pltpu.VMEM(array.shape, array.dtype) for array in arrays]
        + [pltpu.VMEM(shape, kind) for shape, kind in shapes]
        + [pltpu.SemaphoreType.DMA((len(arrays),)), pltpu.SemaphoreType.DMA((len(shapes),))],
        compiler_params=pltpu.CompilerParams(vmem_limit_bytes=10 * 1024 * 1024),
        cost_estimate=pl.CostEstimate(flops=size, bytes_accessed=8 * size, transcendentals=0),
    )(*arrays, *after)
    count = len(kept)
    flat_blocks = [array.reshape((blocks,) + array.shape[2:]) for array in out]
    return flat_blocks[:count], flat_blocks[count]


def misc_step_kernel(held, arrived, out):
    size = held.shape[0] - SUMS
    out[:size, :] = held[:size, :]
    out[size : 2 * size, :] = arrived[:size, :]
    high, low = split(misc_sums(held, arrived))
    out[2 * size : 2 * size + SUMS // 2, :] = high
    out[2 * size + SUMS // 2 :, :] = low


def misc_step(held, arrived):
    return pl.pallas_call(
        misc_step_kernel,
        out_shape=jax.ShapeDtypeStruct((2 * held.shape[0] - SUMS, 2 * D), bf16),
        in_specs=[VMEM] * 2,
        out_specs=VMEM,
        compiler_params=pltpu.CompilerParams(vmem_limit_bytes=8 * 1024 * 1024),
        cost_estimate=pl.CostEstimate(flops=10**5, bytes_accessed=10**5, transcendentals=0),
    )(held, arrived)


def misc_sums(*refs):
    size = refs[0].shape[0] - SUMS
    parts = [ref[size:, :].astype(f32) for ref in refs]
    return sum(part[: SUMS // 2] + part[SUMS // 2 :] for part in parts)


SUMS = 32
OWN = 16


def misc_kernel(conditions, mod_one, mod_two, sums_one, sums_two, out):
    values = conditions[...].astype(f32)
    values = jnp.where(lax.axis_index("section") == 0, values[:SLOTS], values[SLOTS:])
    lifted = values * sigmoid(values)
    spare = [jnp.concatenate([lifted[0:1], lifted[1:2]], axis=1), jnp.zeros((1, 2 * D), f32)]
    rows = []
    for mod in (mod_one, mod_two):
        for slot in range(SLOTS):
            for i in range(3):
                part = mod[slot : slot + 1, i * 2 * D : (i + 1) * 2 * D]
                rows.append(part.astype(f32))
        rows.extend(spare)
    sums = jnp.concatenate([sums_one[...], sums_two[...]], axis=0)
    rows.extend(part.astype(f32) for part in split(sums))
    out[...] = jnp.concatenate(rows, axis=0).astype(bf16)


def pack_misc(conditions, mod_one, mod_two, sums_one, sums_two):
    return pl.pallas_call(
        misc_kernel,
        out_shape=jax.ShapeDtypeStruct((OWN + SUMS, 2 * D), bf16),
        in_specs=[VMEM] * 5,
        out_specs=VMEM,
        compiler_params=pltpu.CompilerParams(vmem_limit_bytes=8 * 1024 * 1024),
    )(conditions, mod_one, mod_two, sums_one, sums_two)


def finish_kernel(widths, counts, waits, *refs):
    count = len(widths)
    kept, refs = refs[:count], refs[count:]
    came, refs = refs[: len(counts)], refs[len(counts) :]
    parts = refs[:4]
    mine, other, small_mine, small_other = refs[4 + waits :]
    places = [(ref, i) for ref, many in zip(came, counts) for i in range(many)]
    added = []
    for i in range(count):
        ref, place = places[i]
        start = sum(widths[i - place : i])
        added.append(kept[i][0] + ref[0, :, start : start + widths[i]].astype(f32))
    a1, f1, f2, a2 = added
    size = parts[0].shape[0] - SUMS
    rows = jnp.concatenate([part[:size, :] for part in parts], axis=0)
    rows = rows.astype(f32).reshape(-1, OWN, 2 * D)
    shard = mine.shape[0]
    chosen = lane_iota(shard, D) == row_iota(shard, D) + lax.axis_index("row") * shard
    chosen = jnp.where(chosen, 1.0, 0.0).astype(bf16)
    features = [rows[:, 6, slot * D : (slot + 1) * D].astype(bf16) for slot in range(SLOTS)]
    lifted = jnp.concatenate([mm_t(chosen, part) for part in features], axis=1).astype(bf16)

    def ada(first):
        columns = []
        for i in range(3):
            both = [rows[:, first + 3 * slot + i, :] for slot in range(SLOTS)]
            columns.append(mm(lifted, jnp.concatenate(both, axis=0).astype(bf16)))
        return jnp.concatenate(columns, axis=1)

    first = lax.axis_index("section") == 0
    at = 0
    for one, two in ((a1, a2), (f1, f2), (ada(0), ada(OWN // 2))):
        columns = slice(at, at + one.shape[1])
        mine[:, columns] = jnp.where(first, one, two)
        other[:, columns] = jnp.where(first, two, one)
        at += one.shape[1]
    total = misc_sums(*parts)
    one, two = total[0:8, :], total[8:16, :]
    small_mine[...] = jnp.where(first, one, two)
    small_other[...] = jnp.where(first, two, one)


def finish(kept, came, parts, after):
    widths = [array.shape[2] for array in kept]
    shard = kept[0].shape[1]
    wide = GROUP + FF + 6 * D
    arrays = [array for array, _ in came]
    shapes = [(shard, wide)] * 2 + [(8, 2 * D)] * 2
    return pl.pallas_call(
        functools.partial(finish_kernel, widths, [count for _, count in came], len(after)),
        out_shape=[jax.ShapeDtypeStruct(shape, f32) for shape in shapes],
        in_specs=[VMEM] * (len(kept) + len(came) + 4) + [ANY] * len(after),
        out_specs=[VMEM] * 4,
        compiler_params=pltpu.CompilerParams(vmem_limit_bytes=8 * 1024 * 1024),
    )(*kept, *arrays, *parts, *after)


def output_kernel(mine, other, small_mine, small_other, *outs):
    first = lax.axis_index("section") == 0

    def halves(start, width):
        columns = slice(start, start + width)
        pair = mine[:, columns], other[:, columns]
        return jnp.where(first, pair[0], pair[1]), jnp.where(first, pair[1], pair[0])

    attn = halves(0, GROUP)
    cut = GROUP - 2 * D
    outs[0][...] = attn[0][:, :D]
    outs[1][...] = attn[0][:, D : 2 * D]
    outs[2][:, :cut] = attn[0][:, 2 * D :]
    outs[2][:, cut:] = attn[1][:, : D - cut]
    outs[3][...] = attn[1][:, D - cut : 2 * D - cut]
    outs[4][...] = attn[1][:, 2 * D - cut : 3 * D - cut]
    decay = jnp.transpose(attn[1][:, 3 * D - cut :])
    for head in range(HEADS):
        outs[5][head] = decay[head : head + 1, :]
    up = halves(GROUP, FF // 2)
    outs[6][:, : FF // 2] = up[0]
    outs[6][:, FF // 2 :] = up[1]
    for piece in range(2):
        down = halves(GROUP + FF // 2 + piece * D, D)
        outs[7][piece] = down[0]
        outs[7][2 + piece] = down[1]
    outs[8][...] = mine[:, GROUP + FF :] + other[:, GROUP + FF :]
    small = small_mine[...] + small_other[...]
    half = 2 * D
    for i in range(3):
        outs[9][:, i * half : (i + 1) * half] = small[i : i + 1, :]
    for i in range(2):
        outs[10][:, i * half : (i + 1) * half] = small[3 + i : 4 + i, :]
    outs[11][...] = small[5:6, :D]
    outs[12][0] = small[5:6, D:]
    outs[12][1] = small[6:7, :D]
    outs[12][2] = small[6:7, D:]
    outs[13][...] = small[7:8, :HEADS]


def outputs(mine, other, small_mine, small_other):
    shard = mine.shape[0]
    shapes = (
        [(shard, D)] * 5
        + [(HEADS, 1, shard), (shard, FF), (4, shard, D), (shard, 6 * D)]
        + [(1, 6 * D), (1, FF), (1, D), (3, 1, D), (1, HEADS)]
    )
    return pl.pallas_call(
        output_kernel,
        out_shape=[jax.ShapeDtypeStruct(shape, f32) for shape in shapes],
        in_specs=[VMEM] * 4,
        out_specs=[VMEM] * len(shapes),
        compiler_params=pltpu.CompilerParams(vmem_limit_bytes=8 * 1024 * 1024),
    )(mine, other, small_mine, small_other)


def both_kernel(one, two, came, out, mark, kept, sems):
    section = lax.axis_index("section")
    mark[...] = jnp.zeros(mark.shape, f32)

    def move(mine, layer):
        arrive = [
            pltpu.make_async_copy(mine, kept.at[layer], sems.at[0]),
            pltpu.make_async_copy(came, kept.at[1 - layer], sems.at[1]),
        ]
        leave = [
            pltpu.make_async_copy(kept.at[layer], out.at[layer], sems.at[2]),
            pltpu.make_async_copy(kept.at[1 - layer], out.at[1 - layer], sems.at[3]),
        ]
        for copy in arrive:
            copy.start()
        for copy, after in zip(arrive, leave):
            copy.wait()
            after.start()
        for copy in leave:
            copy.wait()

    @pl.when(section == 0)
    def _():
        move(one, 0)

    @pl.when(section == 1)
    def _():
        move(two, 1)


def both_micros(one, two, came):
    return pl.pallas_call(
        both_kernel,
        out_shape=[
            jax.ShapeDtypeStruct((MICRO,) + one.shape, one.dtype),
            jax.ShapeDtypeStruct((8, LANES), f32),
        ],
        in_specs=[ANY] * 3,
        out_specs=[ANY, VMEM],
        scratch_shapes=[
            pltpu.VMEM((MICRO,) + one.shape, one.dtype),
            pltpu.SemaphoreType.DMA((4,)),
        ],
        compiler_params=pltpu.CompilerParams(vmem_limit_bytes=8 * 1024 * 1024),
    )(one, two, came)


def swap(values):
    return lax.ppermute(values, "section", [(0, 1), (1, 0)])


def row_bits():
    bits = lax.axis_size("row").bit_length() - 1
    third = bits // 3
    return (
        tuple(range(third)),
        tuple(range(third, 2 * third)),
        tuple(range(2 * third, bits)),
    )


def across(values, flips):
    size = lax.axis_size("row")
    return lax.ppermute(values, "row", [(i, i ^ flips) for i in range(size)])


def partner(values, bit):
    return across(values, 1 << bit)


def axis_of(bit):
    return lax.axis_size("row").bit_length() - 2 - bit


def bit_of(bit):
    return (lax.axis_index("row") >> bit) & 1


def single(values):
    return values.reshape((1,) * (lax.axis_size("row").bit_length() - 1) + values.shape)


def gather_steps(along_x, along_y, along_z):
    steps = [(bit, bit) for bit in reversed(along_z)]
    return steps + list(zip(along_x + along_y, along_y + along_x))


def flat(held):
    return held.reshape(-1, held.shape[-1])


def lock(*arrays):
    return lax.optimization_barrier(arrays)


def on_device(
    tokens, conditions, output_grad, layouts,
    w_ada, b_ada, w_query, w_key, w_value, w_gate, w_out, w_decay, b_decay, conv_kernel,
    w_up, b_up, w_down, b_down,
):
    section = lax.axis_index("section")
    devices = lax.axis_size("row")
    shard = w_query.shape[1]
    along_x, along_y, along_z = row_bits()

    def both(values):
        return values, swap(values)

    qk, vgd, upo, down, ada, lifted = pack(
        w_query, w_key, w_value, w_gate, w_out, w_decay.transpose(0, 2, 1), w_up, w_down, w_ada,
        conditions,
    )
    small = pack_small(b_up, b_down, conv_kernel, b_decay)
    conds = conditions.reshape(MICRO * SLOTS, D)
    steps = gather_steps(along_x, along_y, along_z)
    lag = len(along_z)
    plane = along_x + along_y
    bounds = [len(plane) * i // lag for i in range(lag + 1)]
    held = [single(array) for array in (qk, vgd, upo, down)]
    ada = single(ada)
    for place, pair in enumerate(steps):
        bits = pair + pair
        came = [partner(array, bit) for array, bit in zip(held, bits)]
        after = ()
        if place < lag:
            lifted = jnp.concatenate([lifted, partner(lifted, pair[0])], axis=0)
            for bit in plane[bounds[place] : bounds[place + 1]]:
                (ada,) = join([ada], [partner(ada, bit)], (bit,))
            after = (small, lifted, ada)
        if place == lag:
            left = list(reversed(along_z))
            rows = D >> lag
            line = (lax.axis_index("row") >> len(plane)) * rows
            lifted = lax.dynamic_slice_in_dim(lifted, line, rows, 2)
            product = mm(lifted.reshape(-1, rows), flat(ada))
            terms = (product.reshape(1 << lag, MICRO * SLOTS, 6 * D),)
            for bit in along_z:
                stays, goes = term_step(1 << left.index(bit), *terms)
                left.remove(bit)
                terms = (stays, partner(goes, bit))
            after = (terms[1],)
        if place < len(steps) - 1:
            held = join(held, came, bits, after)
        else:
            qk, vgd = [both(flat(array)) for array in join(held[:2], came[:2], bits[:2])]
            mods = both(sum(term[0] for term in terms) + b_ada[0])
            smalls = both(small)
            x = tokens
            *saved, gated = attn_forward(0, layouts, x, mods, smalls, qk, vgd)
            held = join(held[2:], came[2:], bits[2:], (gated,))
    upo, down = [both(flat(array)) for array in held]
    kept = []
    acts = []
    for l in range(2):
        if l:
            *saved, gated = attn_forward(l, layouts, x, mods, smalls, qk, vgd)
        out, branch, down_raw, *acts_sent = ffn_forward(
            l, layouts, x, mods, smalls, gated, upo, down
        )
        kept.append((x, saved, gated, branch, down_raw))
        acts.append(out)
        x = out[None]

    late, _ = lock(w_ada[0], acts[0])
    ada_all = lax.all_gather(late, "row", axis=0, tiled=True)

    def ffn_step(l, grad, after=()):
        x, saved, gated, branch, down_raw = kept[l]
        mid_grad, branch_low, gwo, sums, *terms = ffn_backward(
            l, layouts, x, mods, smalls, gated, branch, down_raw, grad, upo, down, devices, after
        )
        if terms[0].ndim == 2:
            up_sum = terms[0].reshape(devices, shard, 2, FF // 2)
            down_sum = terms[1].reshape(devices, 2, 2, shard, D)
            terms = []
            for own in (section, 1 - section):
                up_half = lax.dynamic_index_in_dim(up_sum, own, 2, keepdims=False)
                down_half = lax.dynamic_index_in_dim(down_sum, own, 1, keepdims=False)
                terms.append(
                    jnp.concatenate([up_half, down_half[:, 0], down_half[:, 1]], axis=2)
                )
            terms[1] = terms[1].astype(bf16)
        return [branch_low, gwo], mid_grad, terms[0], terms[1], sums

    def mixer_step(l, carried, after=()):
        low, keep, sent, sums = mixer_backward(
            l, layouts, smalls, kept[l][1], *carried, upo, after
        )
        by_row = lambda array: array.reshape(devices, shard, GROUP)
        return low, by_row(keep), by_row(sent), sums

    def input_step(l, low, mid_grad, ffn_sums, mixer_sums, two=None, after=()):
        x = kept[l][0]
        return input_backward(
            l, layouts, x, mods, low, mid_grad, ffn_sums, mixer_sums, qk, vgd, two, after
        )

    def run(keep, came, bits, below=1, after=()):
        for bit in bits[:-1]:
            keep, sent = step(keep, came, bit, below, after)
            came = [(partner(sent, bit), len(keep))]
        return step(keep, came, bits[-1], below, after)

    def grown(mod, bits):
        for bit in bits:
            mod = misc_step(mod, partner(mod, bit))
        return mod

    x_bits, y_bits, z_bits = along_x, along_y, along_z
    carried, mid_grad, f2_keep, f2_sent, f2_sums = ffn_step(1, output_grad)
    *carried, f2_sent, acts_sent = lock(*carried, f2_sent, acts_sent[0])
    f2_came = swap(f2_sent)
    acts_came = swap(acts_sent)
    low, a2_keep, a2_sent, m2_sums = mixer_step(1, carried)
    low, a2_sent, f2_came, acts_came = lock(low, a2_sent, f2_came, acts_came)
    a2_came = swap(a2_sent)
    gx_two, grad, mod_low_two, sums_two = input_step(1, low, mid_grad, f2_sums, m2_sums)
    grad, a2_came = lock(grad, a2_came)
    f2_keep, f2_sent = run([f2_keep], [(f2_came, 1)], x_bits)
    a2_keep, a2_sent = run([a2_keep], [(a2_came, 1)], y_bits, 1 << len(x_bits))
    grad, f2_sent, a2_sent = lock(grad, f2_sent, a2_sent)
    f2_came = partner(f2_sent, x_bits[-1])
    a2_came = partner(a2_sent, y_bits[-1])

    carried, mid_grad, f1_keep, f1_sent, f1_sums = ffn_step(0, grad[None])
    *carried, f1_sent, f2_came, a2_came = lock(*carried, f1_sent, f2_came, a2_came)
    f1_came = swap(f1_sent)
    f2_keep, f2_sent = run(f2_keep, [(f2_came, 1)], y_bits)
    a2_keep, a2_sent = run(a2_keep, [(a2_came, 1)], x_bits)
    f1_keep, f1_sent = run([f1_keep], [(f1_came, 1)], x_bits)
    *carried, f2_sent, a2_sent, f1_sent = lock(*carried, f2_sent, a2_sent, f1_sent)
    f1_came = partner(f1_sent, x_bits[-1])
    a2_came = partner(a2_sent, x_bits[-1])
    f2_came = partner(f2_sent, y_bits[-1])
    low, a1_keep, a1_sent, m1_sums = mixer_step(0, carried)
    low, a1_sent, f2_came, a2_came, f1_came, ada_all = lock(
        low, a1_sent, f2_came, a2_came, f1_came, ada_all
    )
    a1_came = swap(a1_sent)
    two_keep, two_sent = run(f2_keep + a2_keep, [(f2_came, 1), (a2_came, 1)], z_bits[:1])
    f1_keep, f1_sent = run(f1_keep, [(f1_came, 1)], y_bits)
    a1_keep, a1_sent = run([a1_keep], [(a1_came, 1)], x_bits)
    low, two_sent, f1_sent, a1_sent = lock(low, two_sent, f1_sent, a1_sent)
    a1_came = partner(a1_sent, x_bits[-1])
    f1_came = partner(f1_sent, y_bits[-1])
    two_came = partner(two_sent, z_bits[0])
    gx_one, _, mod_low_one, sums_one, gx_sent, mod_mine, mod_sent = input_step(
        0, low, mid_grad, f1_sums, m1_sums, (gx_two, mod_low_two)
    )
    misc = pack_misc(conds, mod_low_one, mod_low_two, sums_one, sums_two)
    misc, a1_came, two_came, f1_came, gx_sent, mod_sent = lock(
        misc, a1_came, two_came, f1_came, gx_sent, mod_sent
    )

    a1_keep, a1_sent = run(a1_keep, [(a1_came, 1)], y_bits)
    a1_sent, misc = lock(a1_sent, misc)
    a1_came = partner(a1_sent, y_bits[-1])
    misc = grown(misc, tuple(reversed(z_bits))[:-1])
    gx_came = swap(gx_sent)
    mod_came = swap(mod_sent)
    keep, came = a1_keep + f1_keep, [(a1_came, 1), (f1_came, 1)]
    for place, bit in enumerate(z_bits):
        if place == 1:
            keep, came = keep + two_keep, came + [(two_came, 2)]
        keep, sent = step(keep, came, bit)
        if place == len(z_bits) - 1:
            sent, misc, gx_came, mod_came = lock(sent, misc, gx_came, mod_came)
        elif place == 0:
            sent, misc = lock(sent, misc)
        came = [(partner(sent, bit), len(keep))]
        if place == 0:
            misc = grown(misc, z_bits[:1] + x_bits[:-1] + y_bits[:-1])
    last = (1 << x_bits[-1], 1 << y_bits[-1])
    parts = [misc] + [across(misc, flips) for flips in (last[0], last[1], last[0] + last[1])]
    gx_out, gx_mark = both_micros(gx_one, gx_two, gx_came)
    acts_out, acts_mark = both_micros(acts[0], acts[1], acts_came)
    grad_lifted = lifted_grads(mod_mine, mod_came, ada_all)
    lifted_came = swap(grad_lifted)
    mine, other, small_mine, small_other = finish(
        keep, came, parts, (gx_mark, acts_mark, lifted_came)
    )
    came, small_came = swap(other), swap(small_other)
    (
        g_query, g_key, g_value, g_gate, g_out, g_decay, g_up, g_down, g_ada,
        g_b_ada, g_b_up, g_b_down, g_conv, g_b_decay,
    ) = outputs(mine, came, small_mine, small_came)

    grad_lifted = (grad_lifted + lifted_came).reshape(MICRO, SLOTS, D)
    _, pull_silu = jax.vjp(jax.nn.silu, conditions.astype(f32))
    (cond_grads,) = pull_silu(grad_lifted)

    return (
        acts_out[None],
        gx_out[None],
        cond_grads,
        g_ada[None],
        g_b_ada,
        g_query[None],
        g_key[None],
        g_value[None],
        g_gate[None],
        g_out[None],
        g_decay.transpose(1, 2, 0),
        g_b_decay,
        g_conv.transpose(1, 0, 2),
        g_up[None],
        g_b_up,
        g_down.reshape(1, FF // devices, D),
        g_b_down,
    )


def solution(mesh):
    rows = P(None, "row", None)
    mats = P("section", "row", None)
    vector = P("section", None)
    in_specs = (
        rows, rows, rows, P(None, "row"),
        mats, vector, mats, mats, mats, mats, mats, mats, vector, P("section", None, None),
        mats, vector, mats, vector,
    )
    blocks = P("section", None, "row", None)
    out_specs = (
        blocks, blocks, rows,
        mats, vector, mats, mats, mats, mats, mats, mats, vector, P("section", None, None),
        mats, vector, mats, vector,
    )
    return jax.shard_map(
        on_device, mesh=mesh, in_specs=in_specs, out_specs=out_specs, check_vma=False
    )
```

```python
import functools

import jax
import jax.numpy as jnp
from jax import lax
from jax.experimental import pallas as pl
from jax.experimental.pallas import tpu as pltpu
from jax.sharding import PartitionSpec as P

D = 384
HEADS = 6
HEAD_DIM = 64
FF = 1536
MICRO = 2
ROWS = 512
HALF = 256
SLOTS = 2
PAIR = 128
PAIRS = D // PAIR
QKVG = 4 * D
LANES = 128
GROUP = (QKVG + D + LANES) // 2
NEG = -1e30
SCALE = HEAD_DIM**-0.5

bf16 = jnp.bfloat16
f32 = jnp.float32


def mm(left, right):
    return jnp.dot(left, right, preferred_element_type=f32)


def mm_t(left, right):
    return lax.dot_general(left, right, (((1,), (1,)), ((), ())), preferred_element_type=f32)


def split(values):
    high = values.astype(bf16)
    return high, (values - high.astype(f32)).astype(bf16)


def split_three(values):
    high, rest = split(values)
    mid = values - high.astype(f32)
    middle, low = split(mid)
    return high, middle, low


def cat_left(values):
    high, low = split(values)
    return jnp.concatenate([high, low, high], axis=1)


def cat_right(values):
    high, low = split(values)
    return jnp.concatenate([high, high, low], axis=1)


def mm_near(left, right_pair, right_high):
    high, low = split(left)
    wide = mm(high, right_pair)
    return wide[:, :PAIR] + wide[:, PAIR:] + mm(low, right_high)


def lane_iota(rows, columns):
    return lax.broadcasted_iota(jnp.int32, (rows, columns), 1)


def row_iota(rows, columns):
    return lax.broadcasted_iota(jnp.int32, (rows, columns), 0)


def order_matrix(start, rows, wide, to_scan):
    t = row_iota(rows, ROWS) + start
    small = (t & 256) + ((t & 15) << 4) + ((t & 255) >> 4)
    if to_scan:
        large = ((t & 15) << 5) + (t >> 4)
    else:
        large = ((t & 31) << 4) + (t >> 5)
    source = jnp.where(wide, large, small)
    return jnp.where(lane_iota(rows, ROWS) == source, 1.0, 0.0).astype(bf16)


def normalise(values):
    centred = values - jnp.mean(values, axis=-1, keepdims=True)
    rate = lax.rsqrt(jnp.mean(centred * centred, axis=-1, keepdims=True) + 1e-06)
    return centred * rate, rate


def normalise_back(normal, rate, grad):
    return rate * (
        grad
        - jnp.mean(grad, axis=-1, keepdims=True)
        - normal * jnp.mean(grad * normal, axis=-1, keepdims=True)
    )


class In:
    def __init__(self, copy, kept):
        self.copy = copy
        self.kept = kept

    def __call__(self):
        if self.copy is not None:
            self.copy.wait()
            self.copy = None
        return self.kept


class Kernel:
    def __init__(self, layer, layouts):
        self.layer = layer
        self.section = lax.axis_index("section")
        self.own = self.section == layer
        self.layout = layouts[self.section, 0]
        self.wide = self.layout == 0
        self.live_rows = jnp.where(self.wide, ROWS, self.layout * HALF)
        self.pushed = {}

    def load(self, kind, refs, kept, sem):
        if kind == "own":
            mine, other = refs

            @pl.when(self.own)
            def _():
                pltpu.make_async_copy(mine, kept, sem).start()

            @pl.when(jnp.logical_not(self.own))
            def _():
                pltpu.make_async_copy(other, kept, sem).start()

            return In(pltpu.make_async_copy(mine, kept, sem), kept)
        (source,) = refs
        if kind == "micro":
            source = source.at[self.section if source.shape[0] == MICRO else 0]
        copy = pltpu.make_async_copy(source, kept, sem)
        copy.start()
        return In(copy, kept)

    def push(self, name):
        kept, target, sem = self.results[name]
        copy = pltpu.make_async_copy(kept, target, sem)
        copy.start()
        self.pushed[name] = copy

    def finish(self):
        for name in self.results:
            if name not in self.pushed:
                self.push(name)
        for copy in self.pushed.values():
            copy.wait()

    def slot(self, half):
        return jnp.where(self.wide, 0, half)

    def share(self, slot, part):
        row = pl.ds(2 * self.section + slot, 1)
        return self.mods()[row, part * D : (part + 1) * D]

    def bu(self):
        return self.small()[0:1, :]

    def bn(self):
        return self.small()[1:2, :D]

    def ck(self, tap):
        return self.small()[2 + tap : 3 + tap, :D]

    def bd(self):
        return self.small()[5:6, :LANES]


def sigmoid(values):
    return 1.0 / (1.0 + jnp.exp(-values))


GELU_A = 0.7978845608028654
GELU_B = 0.044715


def gelu_parts(values):
    square = values * values
    tanh = jnp.tanh(GELU_A * values * (1.0 + GELU_B * square))
    return square, tanh


def fill_bias(bias, wide):
    bias[:, :HALF] = jnp.full((HALF, HALF), 0.0, f32) + jnp.where(wide, 0.0, NEG)
    causal = row_iota(HALF, HALF) >= lane_iota(HALF, HALF)
    bias[:, HALF:] = jnp.where(causal, 0.0, NEG)


def decay_factors(cum, cumt, bias, head):
    row = cumt[pl.ds(head, 1), :]
    lanes = lane_iota(1, LANES)
    column = jnp.sum(jnp.where(lanes == head, cum[...], 0.0), axis=1, keepdims=True)
    first = jnp.exp(column[:HALF] - row[:, :HALF] + bias[:, HALF:])
    second = jnp.exp(column[HALF:] - row + bias[...])
    return first, second


def head_norm(values, lanes):
    square = values * values
    low = jnp.sum(jnp.where(lanes < HEAD_DIM, square, 0.0), axis=1, keepdims=True)
    high = jnp.sum(jnp.where(lanes < HEAD_DIM, 0.0, square), axis=1, keepdims=True)
    return jnp.where(lanes < HEAD_DIM, low, high) * (1.0 / HEAD_DIM)


def fill_decay(dp, bd, cum, cumt):
    raw = dp[...] + bd
    log_decay = (jnp.minimum(raw, 0.0) - jnp.log1p(jnp.exp(-jnp.abs(raw)))) * (1.0 / 16.0)
    high, middle, low = split_three(log_decay)
    causal = jnp.where(row_iota(ROWS, ROWS) >= lane_iota(ROWS, ROWS), 1.0, 0.0).astype(bf16)
    cum[...] = mm(causal, high) + mm(causal, middle) + mm(causal, low)
    cumt[...] = jnp.transpose(cum[...])


def columns(index, first=0):
    return slice(index * PAIR + first, index * PAIR + first + PAIR)


def attn_forward_body(k):
    flip = k.layer == 1
    wide = k.wide
    x = k.x()
    k.mods()

    def first(i, carry):
        rows = pl.ds(pl.multiple_of(i * HALF, HALF), HALF)
        slot = k.slot(i)
        normal, _ = normalise(x[rows, :].astype(f32))
        k.inner[rows, :] = (normal * (1.0 + k.share(slot, 1)) + k.share(slot, 0)).astype(bf16)
        return carry

    lax.fori_loop(0, 2, first, 0)
    w_qk = k.w_qk()
    w_vgd = k.w_vgd()

    def project(i, carry):
        start = i * HALF
        rows = pl.ds(start, HALF)
        if flip:
            part = mm(order_matrix(start, HALF, wide, True), k.inner[...]).astype(bf16)
        else:
            part = k.inner[rows, :]
        k.ordered[rows, :] = part
        k.qkvg[rows, : 2 * D] = mm(part, w_qk[...])
        k.qkvg[rows, 2 * D :] = mm(part, w_vgd[:, : 2 * D])
        k.dp[rows, :] = mm(part, w_vgd[:, 2 * D :])
        return carry

    lax.fori_loop(0, 2, project, 0)
    k.small()
    for name in ("ordered", "qkvg", "dp"):
        k.push(name)
    fill_decay(k.dp, k.bd(), k.cum, k.cumt)
    fill_bias(k.bias, wide)

    vpad = k.vpad
    vpad[0:8, :] = jnp.zeros((8, D), f32)
    vpad[8 : 8 + ROWS, :] = k.qkvg[:, 2 * D : 3 * D]
    position = row_iota(ROWS, 1) & jnp.where(wide, ROWS - 1, HALF - 1)
    one = jnp.where(position >= 1, vpad[7 : 7 + ROWS, :], 0.0)
    two = jnp.where(position >= 2, vpad[6 : 6 + ROWS, :], 0.0)
    k.vc[...] = k.ck(0) * vpad[8 : 8 + ROWS, :] + k.ck(1) * one + k.ck(2) * two
    for name in ("cum", "cumt", "vc"):
        k.push(name)

    def pair(p, carry):
        lanes = lane_iota(1, PAIR)
        queries = cat_left(k.qkvg[:, columns(p)] * SCALE)
        keys = k.qkvg[:, columns(p, D)]
        value_high, value_low = split(k.vc[:, columns(p)])
        values = jnp.concatenate([value_high, value_low], axis=1)
        parts = []
        for e in range(2):
            key_cat = cat_right(jnp.where((lanes // HEAD_DIM) == e, keys, 0.0))
            first, second = decay_factors(k.cum, k.cumt, k.bias, 2 * p + e)
            first = first * mm_t(queries[:HALF], key_cat[:HALF])
            second = second * mm_t(queries[HALF:], key_cat)
            parts.append(
                jnp.concatenate(
                    [
                        mm_near(first, values[:HALF], value_high[:HALF]),
                        mm_near(second, values, value_high),
                    ],
                    axis=0,
                )
            )
        total = jnp.where(lanes < HEAD_DIM, parts[0], parts[1])
        k.o[:, columns(p)] = total
        gate = k.qkvg[:, columns(p, 3 * D)]
        normed = total * lax.rsqrt(head_norm(total, lanes) + 1.0)
        mixed = (normed * (gate * sigmoid(gate))).astype(bf16)
        if flip:
            k.inner[:, columns(p)] = mixed
        else:
            k.gated[:, columns(p)] = mixed
        return carry

    for p in range(PAIRS):
        pair(p, 0)
    k.push("o")
    if flip:

        def back(i, carry):
            start = i * HALF
            k.gated[pl.ds(start, HALF), :] = mm(
                order_matrix(start, HALF, wide, False), k.inner[...]
            ).astype(bf16)
            return carry

        lax.fori_loop(0, 2, back, 0)


def ffn_forward_body(k):
    gated, x = k.gated(), k.x()
    k.mods(), k.small()

    def tile(i, carry):
        start = i * HALF
        rows = pl.ds(start, HALF)
        slot = k.slot(i)
        grown = mm(gated[rows, :], k.wo()[...])
        k.branch[rows, :] = grown
        middle = x[rows, :].astype(f32) + k.share(slot, 2) * grown
        normal, _ = normalise(middle)
        inner = (normal * (1.0 + k.share(slot, 4)) + k.share(slot, 3)).astype(bf16)
        up = mm(inner, k.wu()[...]) + k.bu()
        _, tanh = gelu_parts(up)
        hidden = (0.5 * up * (1.0 + tanh)).astype(bf16)
        low = mm(hidden, k.wn()[...])
        k.down[rows, :] = low
        result = middle + k.share(slot, 5) * (low + k.bn())
        live = (row_iota(HALF, 1) + start) < k.live_rows
        k.out[rows, :] = jnp.where(live, result, 0.0).astype(bf16)
        return carry

    for i in range(2):
        tile(i, 0)


def ffn_backward_body(k):
    gmod, gbu, gbn = k.gmod, k.gbu, k.gbn
    gmod[...] = jnp.zeros(gmod.shape, f32)
    gbu[...] = jnp.zeros(gbu.shape, f32)
    gbn[...] = jnp.zeros(gbn.shape, f32)
    both_ways = k.layer == 1
    k.mods(), k.small()
    x, grad = k.x(), k.grad()
    if both_ways:
        gated, wo = k.gated(), k.wo()
    else:
        branch, down = k.branch(), k.down()

    def tile(i, carry):
        start = i * HALF
        rows = pl.ds(start, HALF)
        slot = k.slot(i)

        def add(part, values):
            where = (pl.ds(slot, 1), slice((part - 2) * D, (part - 1) * D))
            gmod[where] = gmod[where] + jnp.sum(values, axis=0, keepdims=True)

        grown = mm(gated[rows, :], wo[...]) if both_ways else branch[rows, :]
        middle = x[rows, :].astype(f32) + k.share(slot, 2) * grown
        normal, rate = normalise(middle)
        inner = (normal * (1.0 + k.share(slot, 4)) + k.share(slot, 3)).astype(bf16)
        k.inner_s[rows, :] = inner
        up = mm(inner, k.wu()[...]) + k.bu()
        square, tanh = gelu_parts(up)
        half = 0.5 * (1.0 + tanh)
        hidden = (up * half).astype(bf16)
        k.hidden_s[rows, :] = hidden
        lower = (mm(hidden, k.wn()[...]) if both_ways else down[rows, :]) + k.bn()
        live = (row_iota(HALF, 1) + start) < k.live_rows
        if both_ways:
            result = middle + k.share(slot, 5) * lower
            k.out[rows, :] = jnp.where(live, result, 0.0).astype(bf16)
        above = jnp.where(live, grad[rows, :].astype(f32), 0.0)
        add(5, above * lower)
        grad_down = above * k.share(slot, 5)
        gbn[...] = gbn[...] + jnp.sum(grad_down, axis=0, keepdims=True)
        down_low = grad_down.astype(bf16)
        k.down_s[rows, :] = down_low
        slope = half + 0.5 * up * (1.0 - tanh * tanh) * (
            GELU_A * (1.0 + 3.0 * GELU_B * square)
        )
        grad_up = mm_t(down_low, k.wn()[...]) * slope
        gbu[...] = gbu[...] + jnp.sum(grad_up, axis=0, keepdims=True)
        up_low = grad_up.astype(bf16)
        k.up_s[rows, :] = up_low
        grad_inner = mm_t(up_low, k.wu()[...])
        add(3, grad_inner)
        add(4, grad_inner * normal)
        grad_middle = above + normalise_back(
            normal, rate, grad_inner * (1.0 + k.share(slot, 4))
        )
        k.mid_grad[rows, :] = grad_middle
        add(2, grad_middle * grown)
        k.branch_low[rows, :] = (grad_middle * k.share(slot, 2)).astype(bf16)
        return carry

    for i in range(2):
        tile(i, 0)
    k.push("mid_grad")
    k.push("branch_low")
    if both_ways:
        own = k.section == 0
        k.sent[...] = jnp.where(own, k.out[...].astype(f32), x[...].astype(f32)).astype(bf16)
        k.push("out")
        k.push("sent")

    def weights(j, carry):
        part = pl.ds(pl.multiple_of(j * HALF, HALF), HALF)
        hidden_t = jnp.transpose(k.hidden_s[:, part].astype(f32)).astype(bf16)
        k.gwn[part, :] = mm(hidden_t, k.down_s[...])
        return carry

    lax.fori_loop(0, FF // HALF, weights, 0)
    inner_t = jnp.transpose(k.inner_s[...].astype(f32)).astype(bf16)
    if k.packed:
        devices, shard, _ = k.keep.shape

        def halves(j, carry):
            for kept, own in ((k.keep, c_section), (k.gone, 1 - c_section)):
                columns = pl.ds(pl.multiple_of(j * HALF + own * (FF // 2), HALF), HALF)
                here = pl.ds(pl.multiple_of(j * HALF, HALF), HALF)
                part = mm(inner_t, k.up_s[:, columns]).reshape(devices, shard, HALF)
                kept[:, :, here] = part.astype(kept.dtype)
            return carry

        c_section = k.section
        lax.fori_loop(0, FF // 2 // HALF, halves, 0)

        def owner(r, carry):
            for kept, own in ((k.keep, c_section), (k.gone, 1 - c_section)):
                for piece in range(2):
                    start = pl.multiple_of((4 * r + 2 * own + piece) * shard, 8)
                    rows = k.gwn[pl.ds(start, shard), :]
                    at = FF // 2 + piece * D
                    kept[r, :, at : at + D] = rows.astype(kept.dtype)
            return carry

        lax.fori_loop(0, devices, owner, 0)
        k.push("keep")
        k.push("gone")
    else:
        k.gwu[...] = mm(inner_t, k.up_s[...])
    gated = k.gated()
    k.gwo[...] = mm(jnp.transpose(gated[...].astype(f32)).astype(bf16), k.branch_low[...])

    short = jnp.concatenate([gbn[...], jnp.zeros((1, FF - D), f32)], axis=1)
    k.sums[...] = jnp.concatenate(
        [gmod[0:SLOTS, :], gbu[...], short, jnp.zeros((4, FF), f32)], axis=0
    )


def mixer_backward_body(k):
    flip = k.layer == 1
    wide = k.wide
    mixed_s, low, dv_s, rows_s, cols_s = k.mixed_s, k.low, k.dv_s, k.rows_s, k.cols_s
    fill_bias(k.bias, wide)
    branch_low, wo = k.branch_low(), k.wo()

    def first(i, carry):
        start = i * HALF
        rows = pl.ds(start, HALF)
        if flip:
            part = mm(order_matrix(start, HALF, wide, True), branch_low[...]).astype(bf16)
        else:
            part = branch_low[rows, :]
        mixed_s[rows, :] = mm_t(part, wo[...])
        return carry

    lax.fori_loop(0, 2, first, 0)
    rows_s[...] = jnp.zeros(rows_s.shape, f32)
    cols_s[...] = jnp.zeros(cols_s.shape, f32)
    qkvg, vc, cum, cumt, o = k.qkvg(), k.vc(), k.cum(), k.cumt(), k.o()
    k.small()

    def pair(p, carry):
        lanes = lane_iota(1, PAIR)
        total = o[:, columns(p)]
        gate = qkvg[:, columns(p, 3 * D)]
        above = mixed_s[:, columns(p)]
        rate = lax.rsqrt(head_norm(total, lanes) + 1.0)
        sig = sigmoid(gate)
        grad_gate = above * (total * rate) * (sig * (1.0 + gate * (1.0 - sig)))
        low[:, columns(p, 3 * D)] = grad_gate.astype(bf16)
        grad_normed = above * (gate * sig)
        product = grad_normed * total
        inside = jnp.where(
            lanes < HEAD_DIM,
            jnp.sum(jnp.where(lanes < HEAD_DIM, product, 0.0), axis=1, keepdims=True),
            jnp.sum(jnp.where(lanes < HEAD_DIM, 0.0, product), axis=1, keepdims=True),
        ) * (1.0 / HEAD_DIM)
        grad_o = rate * grad_normed - total * (rate * rate * rate) * inside

        queries = qkvg[:, columns(p)] * SCALE
        keys = qkvg[:, columns(p, D)]
        values = vc[:, columns(p)]
        query_cat = cat_left(queries)
        grad_cat = cat_left(grad_o)
        key_high, key_low = split(keys)
        key_pair = jnp.concatenate([key_high, key_low], axis=1)
        query_t = jnp.transpose(queries)
        grad_t = jnp.transpose(grad_o)
        grad_q = []
        grad_k = []
        grad_v = []
        for e in range(2):
            mine = (lanes // HEAD_DIM) == e
            head = 2 * p + e
            key_cat = cat_right(jnp.where(mine, keys, 0.0))
            value_cat = cat_right(jnp.where(mine, values, 0.0))
            first, second = decay_factors(cum, cumt, k.bias, head)
            raw_first = mm_t(query_cat[:HALF], key_cat[:HALF])
            raw_second = mm_t(query_cat[HALF:], key_cat)
            grad_first = first * mm_t(grad_cat[:HALF], value_cat[:HALF])
            grad_second = second * mm_t(grad_cat[HALF:], value_cat)
            score_first = raw_first * first
            score_second = raw_second * second
            pull_first = grad_first * raw_first
            pull_second = grad_second * raw_second
            here = lanes == head
            rows_s[:HALF, :] = rows_s[:HALF, :] + jnp.where(
                here, jnp.sum(pull_first, axis=1, keepdims=True), 0.0
            )
            rows_s[HALF:, :] = rows_s[HALF:, :] + jnp.where(
                here, jnp.sum(pull_second, axis=1, keepdims=True), 0.0
            )
            low_cols = jnp.sum(pull_second, axis=0, keepdims=True)
            cols_s[pl.ds(head, 1), :HALF] = low_cols[:, :HALF] + jnp.sum(
                pull_first, axis=0, keepdims=True
            )
            cols_s[pl.ds(head, 1), HALF:] = low_cols[:, HALF:]
            grad_q.append(
                jnp.concatenate(
                    [
                        mm_near(grad_first, key_pair[:HALF], key_high[:HALF]),
                        mm_near(grad_second, key_pair, key_high),
                    ],
                    axis=0,
                )
            )

            def turned(source_t, block_first, block_second):
                high, low = split(source_t[e * HEAD_DIM : (e + 1) * HEAD_DIM, :])
                both = jnp.concatenate([high, low], axis=0)
                first_high, first_low = split(block_first)
                second_high, second_low = split(block_second)
                one = mm(both[:, :HALF], first_high)
                one = one[:HEAD_DIM] + one[HEAD_DIM:] + mm(high[:, :HALF], first_low)
                two = mm(both[:, HALF:], second_high)
                two = two[:HEAD_DIM] + two[HEAD_DIM:] + mm(high[:, HALF:], second_low)
                return jnp.concatenate([two[:, :HALF] + one, two[:, HALF:]], axis=1)

            grad_k.append(turned(query_t, grad_first, grad_second))
            grad_v.append(turned(grad_t, score_first, score_second))
        query_grad = jnp.where(lanes < HEAD_DIM, grad_q[0], grad_q[1]) * SCALE
        low[:, columns(p)] = query_grad.astype(bf16)
        low[:, columns(p, D)] = jnp.transpose(jnp.concatenate(grad_k, axis=0)).astype(bf16)
        dv_s[:ROWS, columns(p)] = jnp.transpose(jnp.concatenate(grad_v, axis=0))
        return carry

    for p in range(PAIRS):
        pair(p, 0)

    pulled = rows_s[...] - jnp.transpose(cols_s[...])
    high, middle, rest = split_three(pulled)
    upper_first = jnp.concatenate(
        [
            jnp.where(row_iota(HALF, HALF) <= lane_iota(HALF, HALF), 1.0, 0.0),
            jnp.full((HALF, HALF), 0.0, f32) + jnp.where(wide, 1.0, 0.0),
        ],
        axis=1,
    ).astype(bf16)
    upper_second = upper_first[:, :HALF]
    later = jnp.concatenate(
        [
            mm(upper_first, high) + mm(upper_first, middle) + mm(upper_first, rest),
            mm(upper_second, high[HALF:]) + mm(upper_second, middle[HALF:])
            + mm(upper_second, rest[HALF:]),
        ],
        axis=0,
    )
    grad_dp = later * (1.0 / 16.0) * sigmoid(-(k.dp()[...] + k.bd()))
    grad_bd = jnp.sum(grad_dp, axis=0, keepdims=True)
    low[:, QKVG:] = grad_dp.astype(bf16)

    dv_s[ROWS:, :] = jnp.zeros((8, D), f32)
    position = row_iota(ROWS, 1) & jnp.where(wide, ROWS - 1, HALF - 1)
    last = jnp.where(wide, ROWS - 1, HALF - 1)
    here = dv_s[0:ROWS, :]
    one = jnp.where(position <= last - 1, dv_s[1 : 1 + ROWS, :], 0.0)
    two = jnp.where(position <= last - 2, dv_s[2 : 2 + ROWS, :], 0.0)
    value = qkvg[:, 2 * D : 3 * D]
    low[:, 2 * D : 3 * D] = (k.ck(0) * here + k.ck(1) * one + k.ck(2) * two).astype(bf16)
    k.push("low")

    taps = [jnp.sum(rows * value, axis=0, keepdims=True) for rows in (here, one, two)]
    rest = jnp.concatenate([grad_bd, jnp.zeros((1, D - LANES), f32)], axis=1)
    k.sums[...] = jnp.concatenate([*taps, rest, jnp.zeros((4, D), f32)], axis=0)

    ordered_t = jnp.transpose(k.ordered()[...].astype(f32)).astype(bf16)
    gwo = k.gwo()
    gw = k.gw

    def weights(j, carry):
        part = pl.ds(pl.multiple_of(j * HALF, HALF), HALF)
        gw[:, part] = mm(ordered_t, low[:, part])
        return carry

    lax.fori_loop(0, QKVG // HALF, weights, 0)
    gw[:, QKVG : QKVG + D] = gwo[...]
    gw[:, QKVG + D :] = mm(ordered_t, low[:, QKVG:])

    def halves(j, carry):
        here = pl.ds(pl.multiple_of(j * HALF, HALF), HALF)
        keep = pl.ds(pl.multiple_of(j * HALF + k.section * GROUP, HALF), HALF)
        send = pl.ds(pl.multiple_of(j * HALF + (1 - k.section) * GROUP, HALF), HALF)
        k.gw_keep[:, here] = gw[:, keep]
        k.gw_send[:, here] = gw[:, send].astype(bf16)
        return carry

    lax.fori_loop(0, GROUP // HALF, halves, 0)


def input_backward_body(k):
    flip = k.layer == 1
    wide = k.wide
    gmod, mixed_s, perm_s = k.gmod, k.mixed_s, k.perm_s
    gmod[...] = jnp.zeros(gmod.shape, f32)
    low, w_qk, w_vgd = k.low(), k.w_qk(), k.w_vgd()

    def inner_grad(i, carry):
        rows = pl.ds(pl.multiple_of(i * HALF, HALF), HALF)
        mixed_s[rows, :] = mm_t(low[rows, : 2 * D], w_qk[...]) + mm_t(
            low[rows, 2 * D :], w_vgd[...]
        )
        return carry

    lax.fori_loop(0, 2, inner_grad, 0)
    if flip:
        high, middle, rest = split_three(mixed_s[...])
        perm_s[:, :D] = high
        perm_s[:, D : 2 * D] = middle
        perm_s[:, 2 * D :] = rest
    x, mid_grad = k.x(), k.mid_grad()
    k.mods()

    def tile(i, carry):
        start = i * HALF
        rows = pl.ds(start, HALF)
        slot = k.slot(i)
        if flip:
            three = mm(order_matrix(start, HALF, wide, False), perm_s[...])
            grad = three[:, :D] + three[:, D : 2 * D] + three[:, 2 * D :]
        else:
            grad = mixed_s[rows, :]
        normal, rate = normalise(x[rows, :].astype(f32))
        where = (pl.ds(slot, 1), slice(0, D))
        gmod[where] = gmod[where] + jnp.sum(grad, axis=0, keepdims=True)
        where = (pl.ds(slot, 1), slice(D, 2 * D))
        gmod[where] = gmod[where] + jnp.sum(grad * normal, axis=0, keepdims=True)
        total = mid_grad[rows, :] + normalise_back(normal, rate, grad * (1.0 + k.share(slot, 1)))
        k.gx[rows, :] = total
        k.gx_low[rows, :] = total.astype(bf16)
        return carry

    for i in range(2):
        tile(i, 0)
    k.push("gx_low")
    k.push("gx")
    ffn, mixer = k.ffn_sums(), k.mixer_sums()
    k.mod_low[...] = jnp.concatenate([gmod[...], ffn[...]], axis=1).astype(bf16)
    if k.layer == 0:
        first = k.section == 0
        k.gx_send[...] = jnp.where(first, k.gx_two()[...], k.gx[...])
        one, two = k.mod_low[...].astype(f32), k.mod_two()[...].astype(f32)
        k.mod_mine[...] = jnp.where(first, one, two).astype(bf16)
        k.mod_send[...] = jnp.where(first, two, one).astype(bf16)
    half = 2 * D
    rest = ffn[0:1, :] + ffn[1:2, :]
    k.sums[...] = jnp.concatenate(
        [
            gmod[0:1, :] + gmod[1:2, :],
            rest[:, :half],
            rest[:, half:],
            ffn[2:3, :half],
            ffn[2:3, half:],
            jnp.concatenate([ffn[3:4, :D], mixer[0:1, :]], axis=1),
            jnp.concatenate([mixer[1:2, :], mixer[2:3, :]], axis=1),
            jnp.concatenate([mixer[3:4, :], jnp.zeros((1, D), f32)], axis=1),
        ],
        axis=0,
    )


ANY = pl.BlockSpec(memory_space=pl.ANY)
VMEM = pl.BlockSpec(memory_space=pltpu.VMEM)
HBM = pl.BlockSpec(memory_space=pltpu.HBM)


def call(body, layer, layouts, ins, outs, scratch, flops, packed=None, after=()):
    arrays = []
    counts = []
    kept = []
    places = []
    for kind, given, part in ins.values():
        places.extend([ANY] * 2 if kind == "own" else [HBM])
        given = given if kind == "own" else (given,)
        arrays.extend(given)
        counts.append(len(given))
        rows, wide = given[0].shape[-2:]
        start, stop = part or (0, wide)
        kept.append(pltpu.VMEM((rows, stop - start), given[0].dtype))

    def kernel(*refs):
        refs = list(refs)
        take = lambda count: [refs.pop(0) for _ in range(count)]
        (layouts_ref,) = take(1)
        sources = [take(count) for count in counts]
        take(len(after))
        targets = take(len(outs))
        buffers = take(len(ins))
        results = take(len(outs))
        rest = take(len(scratch))
        in_sems, out_sems = refs
        k = Kernel(layer, layouts_ref)
        k.packed = packed
        for number, (name, (kind, _, part)) in enumerate(ins.items()):
            given = sources[number]
            if part is not None:
                given = [ref.at[:, part[0] : part[1]] for ref in given]
            setattr(k, name, k.load(kind, given, buffers[number], in_sems.at[number]))
        k.results = {}
        for number, name in enumerate(outs):
            setattr(k, name, results[number])
            k.results[name] = (results[number], targets[number], out_sems.at[number])
        for name, ref in zip(scratch, rest):
            setattr(k, name, ref)
        body(k)
        k.finish()

    return pl.pallas_call(
        kernel,
        out_shape=[jax.ShapeDtypeStruct(shape, kind) for shape, kind, _ in outs.values()],
        in_specs=[pl.BlockSpec(memory_space=pltpu.SMEM)] + places + [ANY] * len(after),
        out_specs=[HBM if for_kernel else ANY for _, _, for_kernel in outs.values()],
        scratch_shapes=kept
        + [pltpu.VMEM(shape, kind) for shape, kind, _ in outs.values()]
        + [pltpu.VMEM(shape, kind) for shape, kind in scratch.values()]
        + [pltpu.SemaphoreType.DMA((len(ins),)), pltpu.SemaphoreType.DMA((len(outs),))],
        compiler_params=pltpu.CompilerParams(vmem_limit_bytes=56 * 1024 * 1024),
        cost_estimate=pl.CostEstimate(flops=flops, bytes_accessed=4 << 20, transcendentals=0),
    )(layouts, *arrays, *after)


def own(pair, part=None):
    return ("own", pair, part)


def plain(array):
    return ("plain", array, None)


def micro(array):
    return ("micro", array, None)


AT_UP = (0, FF)
AT_OUT = (FF, FF + D)


def attn_forward(layer, layouts, x, mods, small, qk, vgd):
    return call(
        attn_forward_body,
        layer,
        layouts,
        dict(
            x=micro(x),
            mods=own(mods),
            w_qk=own(qk),
            w_vgd=own(vgd),
            small=own(small),
        ),
        dict(
            ordered=((ROWS, D), bf16, True),
            qkvg=((ROWS, QKVG), f32, True),
            dp=((ROWS, LANES), f32, True),
            vc=((ROWS, D), f32, True),
            cum=((ROWS, LANES), f32, True),
            cumt=((LANES, ROWS), f32, True),
            o=((ROWS, D), f32, True),
            gated=((ROWS, D), bf16, True),
        ),
        dict(
            inner=((ROWS, D), bf16),
            vpad=((ROWS + 8, D), f32),
            bias=((HALF, ROWS), f32),
        ),
        4 * 10**9,
    )


def ffn_forward(layer, layouts, x, mods, small, gated, upo, down):
    return call(
        ffn_forward_body,
        layer,
        layouts,
        dict(
            gated=plain(gated),
            x=micro(x),
            wo=own(upo, AT_OUT),
            mods=own(mods),
            small=own(small),
            wu=own(upo, AT_UP),
            wn=own(down),
        ),
        dict(
            out=((ROWS, D), bf16, True),
            branch=((ROWS, D), f32, True),
            down=((ROWS, D), f32, True),
        ),
        {},
        3 * 10**9,
    )


def ffn_backward(
    layer, layouts, x, mods, small, gated, branch, down_raw, grad, upo, down, devices, after=()
):
    shard = D // devices
    in_kernel = shard % 8 == 0
    if in_kernel:
        sums = dict(
            keep=((devices, shard, FF), f32, True),
            gone=((devices, shard, FF), bf16, False),
        )
    else:
        sums = dict(gwu=((D, FF), f32, False), gwn=((FF, D), f32, False))
    return call(
        ffn_backward_body,
        layer,
        layouts,
        dict(
            mods=own(mods),
            small=own(small),
            x=micro(x),
            **(
                dict(gated=plain(gated), wo=own(upo, AT_OUT))
                if layer == 1
                else dict(branch=plain(branch), down=plain(down_raw))
            ),
            grad=micro(grad),
            wu=own(upo, AT_UP),
            wn=own(down),
            **(dict(gated=plain(gated)) if layer == 0 else {}),
        ),
        dict(
            **(
                dict(out=((ROWS, D), bf16, True), sent=((ROWS, D), bf16, False))
                if layer == 1
                else {}
            ),
            mid_grad=((ROWS, D), f32, True),
            branch_low=((ROWS, D), bf16, True),
            gwo=((D, D), f32, True),
            sums=((8, FF), f32, True),
            **sums,
        ),
        dict(
            **({"gwn": ((FF, D), f32)} if in_kernel else {}),
            hidden_s=((ROWS, FF), bf16),
            inner_s=((ROWS, D), bf16),
            up_s=((ROWS, FF), bf16),
            down_s=((ROWS, D), bf16),
            gmod=((8, FF), f32),
            gbu=((1, FF), f32),
            gbn=((1, D), f32),
        ),
        5 * 10**9,
        packed=in_kernel,
        after=after,
    )


def mixer_backward(layer, layouts, small, saved, branch_low, gwo, upo, after=()):
    ordered, qkvg, dp, vc, cum, cumt, o = saved
    return call(
        mixer_backward_body,
        layer,
        layouts,
        dict(
            branch_low=plain(branch_low),
            wo=own(upo, AT_OUT),
            qkvg=plain(qkvg),
            vc=plain(vc),
            cum=plain(cum),
            cumt=plain(cumt),
            o=plain(o),
            small=own(small),
            dp=plain(dp),
            ordered=plain(ordered),
            gwo=plain(gwo),
        ),
        dict(
            low=((ROWS, QKVG + LANES), bf16, True),
            gw_keep=((D, GROUP), f32, True),
            gw_send=((D, GROUP), bf16, False),
            sums=((8, D), f32, True),
        ),
        dict(
            mixed_s=((ROWS, D), f32),
            dv_s=((ROWS + 8, D), f32),
            rows_s=((ROWS, LANES), f32),
            cols_s=((LANES, ROWS), f32),
            bias=((HALF, ROWS), f32),
            gw=((D, 2 * GROUP), f32),
        ),
        7 * 10**9,
        after=after,
    )


def input_backward(
    layer, layouts, x, mods, low, mid_grad, ffn_sums, mixer_sums, qk, vgd, two=None, after=()
):
    extra_in, extra_out = {}, {}
    if two is not None:
        extra_in = dict(gx_two=plain(two[0]), mod_two=plain(two[1]))
        extra_out = dict(
            gx_send=((ROWS, D), f32, False),
            mod_mine=((8, 6 * D), bf16, False),
            mod_send=((8, 6 * D), bf16, False),
        )
    return call(
        input_backward_body,
        layer,
        layouts,
        dict(
            low=plain(low),
            w_qk=own(qk),
            w_vgd=own(vgd),
            x=micro(x),
            mid_grad=plain(mid_grad),
            mods=own(mods),
            ffn_sums=plain(ffn_sums),
            mixer_sums=plain(mixer_sums),
            **extra_in,
        ),
        dict(
            gx=((ROWS, D), f32, True),
            gx_low=((ROWS, D), bf16, True),
            mod_low=((8, 6 * D), bf16, True),
            sums=((8, 2 * D), f32, False),
            **extra_out,
        ),
        dict(
            mixed_s=((ROWS, D), f32),
            perm_s=((ROWS, 3 * D), bf16),
            gmod=((8, 2 * D), f32),
        ),
        2 * 10**9,
        after=after,
    )


def small_kernel(b_up, b_down, taps, b_decay, packed):
    packed[...] = jnp.zeros(packed.shape, f32)
    packed[0:1, :] = b_up[...]
    packed[1:2, :D] = b_down[...]
    packed[2:5, :D] = taps[0]
    packed[5:6, :HEADS] = b_decay[...]


def pack_small(b_up, b_down, taps, b_decay):
    return pl.pallas_call(
        small_kernel,
        out_shape=jax.ShapeDtypeStruct((8, FF), f32),
        in_specs=[VMEM] * 4,
        out_specs=VMEM,
        compiler_params=pltpu.CompilerParams(vmem_limit_bytes=8 * 1024 * 1024),
    )(b_up, b_down, taps, b_decay)


def pack_kernel(
    w_query, w_key, w_value, w_gate, w_out, w_decay, w_up, w_down, w_ada, conditions,
    qkuo, vgd, down, ada, lifted,
):
    qkuo[:, :D] = w_query[0]
    qkuo[:, D : 2 * D] = w_key[0]
    vgd[:, :D] = w_value[0]
    vgd[:, D : 2 * D] = w_gate[0]
    place = jnp.where(row_iota(HEADS, LANES) == lane_iota(HEADS, LANES), 1.0, 0.0).astype(bf16)
    turned = lax.dot_general(
        w_decay[0], place, (((0,), (0,)), ((), ())), preferred_element_type=f32
    )
    vgd[:, 2 * D :] = turned.astype(bf16)
    qkuo[:, 2 * D : 2 * D + FF] = w_up[0]
    qkuo[:, 2 * D + FF :] = w_out[0]
    down[...] = w_down[0]
    ada[...] = w_ada[0]
    values = jnp.concatenate([conditions[m].astype(f32) for m in range(MICRO)], axis=0)
    lifted[0] = (values * sigmoid(values)).astype(bf16)


def pack(*weights):
    shard = weights[0].shape[1]
    shapes = [(shard, width) for width in (3 * D + FF, 2 * D + LANES)]
    shapes += [weights[7].shape[1:], weights[8].shape[1:], (1, MICRO * SLOTS, D)]
    return pl.pallas_call(
        pack_kernel,
        out_shape=[jax.ShapeDtypeStruct(shape, bf16) for shape in shapes],
        in_specs=[VMEM] * len(weights),
        out_specs=[VMEM] * len(shapes),
    )(*weights)


def join_kernel(bits, waits, *refs):
    count = len(bits)
    held, came, out = refs[:count], refs[count : 2 * count], refs[2 * count + waits :]
    for i, bit in enumerate(bits):
        mine = (lax.axis_index("row") >> bit) & 1
        out[i][:, mine] = held[i][...]
        out[i][:, 1 - mine] = came[i][...]


def join(held, came, bits, after=()):
    def parts(array, bit):
        axis = axis_of(bit)
        above = 1
        for size in array.shape[:axis]:
            above *= size
        return array.reshape((above, -1) + array.shape[-2:])

    split_held = [parts(array, bit) for array, bit in zip(held, bits)]
    split_came = [parts(array, bit) for array, bit in zip(came, bits)]
    out = pl.pallas_call(
        functools.partial(join_kernel, bits, len(after)),
        out_shape=[
            jax.ShapeDtypeStruct(array.shape[:1] + (2,) + array.shape[1:], array.dtype)
            for array in split_held
        ],
        in_specs=[VMEM] * (2 * len(held)) + [ANY] * len(after),
        out_specs=[VMEM] * len(held),
        compiler_params=pltpu.CompilerParams(vmem_limit_bytes=8 * 1024 * 1024),
        cost_estimate=pl.CostEstimate(flops=10**6, bytes_accessed=10**6, transcendentals=0),
    )(*split_held, *split_came, *after)
    joined = []
    for array, result, bit in zip(held, out, bits):
        shape = list(array.shape)
        shape[axis_of(bit)] = 2
        joined.append(result.reshape(shape))
    return joined


def lifted_kernel(mine, came, ada, out, kept, sem):
    copy = pltpu.make_async_copy(ada, kept, sem)
    copy.start()
    first = lax.axis_index("section") == 0
    pair = mine[0:SLOTS, :].astype(f32), came[0:SLOTS, :].astype(f32)
    grad = jnp.concatenate(
        [jnp.where(first, pair[0], pair[1]), jnp.where(first, pair[1], pair[0])], axis=0
    ).astype(bf16)
    copy.wait()
    out[...] = mm_t(grad, kept[...])


def lifted_grads(mine, came, ada):
    return pl.pallas_call(
        lifted_kernel,
        out_shape=jax.ShapeDtypeStruct((MICRO * SLOTS, D), f32),
        in_specs=[VMEM, VMEM, ANY],
        out_specs=VMEM,
        scratch_shapes=[pltpu.VMEM((D, 6 * D), bf16), pltpu.SemaphoreType.DMA],
        compiler_params=pltpu.CompilerParams(vmem_limit_bytes=16 * 1024 * 1024),
        cost_estimate=pl.CostEstimate(flops=10**9, bytes_accessed=2 << 20, transcendentals=0),
    )(mine, came, ada)


def term_kernel(*refs):
    *terms, stays, goes = refs
    stays[...] = sum(ref[:, 0] for ref in terms)
    goes[...] = sum(ref[:, 1] for ref in terms)


def term_step(below, *terms):
    tail = terms[0].shape[1:]
    above = terms[0].shape[0] // (2 * below)
    shape = jax.ShapeDtypeStruct((above, below) + tail, f32)
    out = pl.pallas_call(
        term_kernel,
        out_shape=[shape] * 2,
        in_specs=[VMEM] * len(terms),
        out_specs=[VMEM] * 2,
        compiler_params=pltpu.CompilerParams(vmem_limit_bytes=8 * 1024 * 1024),
        cost_estimate=pl.CostEstimate(flops=10**6, bytes_accessed=10**6, transcendentals=0),
    )(*[term.reshape((above, 2, below) + tail) for term in terms])
    return [array.reshape((above * below,) + tail) for array in out]


def step_kernel(bit, widths, counts, waits, *refs):
    mine = (lax.axis_index("row") >> bit) & 1
    count, many = len(widths), len(counts)
    refs = list(refs)
    take = lambda number: [refs.pop(0) for _ in range(number)]
    sources = take(count + many)
    take(waits)
    targets = take(count + 1)
    buffers = take(count + many)
    results = take(count + 1)
    in_sems, out_sems = refs
    arrive = [
        pltpu.make_async_copy(source, buffer, in_sems.at[i])
        for i, (source, buffer) in enumerate(zip(sources, buffers))
    ]
    leave = [
        pltpu.make_async_copy(result, target, out_sems.at[i])
        for i, (result, target) in enumerate(zip(results, targets))
    ]
    for copy in arrive:
        copy.start()
    kept, came = buffers[:count], buffers[count:]
    places = [(j, i) for j, number in enumerate(counts) for i in range(number)]
    goes = results[count]
    at = 0
    for i in range(count):
        j, place = places[i]
        arrive[i].wait()
        if place == 0:
            arrive[count + j].wait()
        start = sum(widths[i - place : i])
        columns = slice(start, start + widths[i])
        total = kept[i][:, 1 - mine] + came[j][:, 1 - mine, :, :, columns].astype(f32)
        goes[:, :, :, at : at + widths[i]] = total.astype(bf16)
        at += widths[i]
    leave[count].start()
    for i in range(count):
        j, place = places[i]
        start = sum(widths[i - place : i])
        columns = slice(start, start + widths[i])
        results[i][...] = kept[i][:, mine] + came[j][:, mine, :, :, columns].astype(f32)
        leave[i].start()
    for copy in leave:
        copy.wait()


def step(kept, came, bit, below=1, after=()):
    blocks, rows = kept[0].shape[0] // 2, kept[0].shape[1]
    above = blocks // below
    paired = lambda array: array.reshape((above, 2, below) + array.shape[1:])
    widths = [array.shape[2] for array in kept]
    size = sum(array.size for array in kept)
    arrays = [paired(array) for array in kept] + [paired(array) for array, _ in came]
    shapes = [((above, below, rows, width), f32) for width in widths]
    shapes.append(((above, below, rows, sum(widths)), bf16))
    out = pl.pallas_call(
        functools.partial(step_kernel, bit, widths, [count for _, count in came], len(after)),
        out_shape=[jax.ShapeDtypeStruct(shape, kind) for shape, kind in shapes],
        in_specs=[HBM] * len(kept) + [ANY] * (len(came) + len(after)),
        out_specs=[HBM] * len(kept) + [ANY],
        scratch_shapes=[pltpu.VMEM(array.shape, array.dtype) for array in arrays]
        + [pltpu.VMEM(shape, kind) for shape, kind in shapes]
        + [pltpu.SemaphoreType.DMA((len(arrays),)), pltpu.SemaphoreType.DMA((len(shapes),))],
        compiler_params=pltpu.CompilerParams(vmem_limit_bytes=10 * 1024 * 1024),
        cost_estimate=pl.CostEstimate(flops=size, bytes_accessed=8 * size, transcendentals=0),
    )(*arrays, *after)
    count = len(kept)
    flat_blocks = [array.reshape((blocks,) + array.shape[2:]) for array in out]
    return flat_blocks[:count], flat_blocks[count]


def misc_step_kernel(held, arrived, out):
    size = held.shape[0] - SUMS
    out[:size, :] = held[:size, :]
    out[size : 2 * size, :] = arrived[:size, :]
    high, low = split(misc_sums(held, arrived))
    out[2 * size : 2 * size + SUMS // 2, :] = high
    out[2 * size + SUMS // 2 :, :] = low


def misc_step(held, arrived):
    return pl.pallas_call(
        misc_step_kernel,
        out_shape=jax.ShapeDtypeStruct((2 * held.shape[0] - SUMS, 2 * D), bf16),
        in_specs=[VMEM] * 2,
        out_specs=VMEM,
        compiler_params=pltpu.CompilerParams(vmem_limit_bytes=8 * 1024 * 1024),
        cost_estimate=pl.CostEstimate(flops=10**5, bytes_accessed=10**5, transcendentals=0),
    )(held, arrived)


def misc_sums(*refs):
    size = refs[0].shape[0] - SUMS
    parts = [ref[size:, :].astype(f32) for ref in refs]
    return sum(part[: SUMS // 2] + part[SUMS // 2 :] for part in parts)


SUMS = 32
OWN = 16


def misc_kernel(conditions, mod_one, mod_two, sums_one, sums_two, out):
    values = conditions[...].astype(f32)
    values = jnp.where(lax.axis_index("section") == 0, values[:SLOTS], values[SLOTS:])
    lifted = values * sigmoid(values)
    spare = [jnp.concatenate([lifted[0:1], lifted[1:2]], axis=1), jnp.zeros((1, 2 * D), f32)]
    rows = []
    for mod in (mod_one, mod_two):
        for slot in range(SLOTS):
            for i in range(3):
                part = mod[slot : slot + 1, i * 2 * D : (i + 1) * 2 * D]
                rows.append(part.astype(f32))
        rows.extend(spare)
    sums = jnp.concatenate([sums_one[...], sums_two[...]], axis=0)
    rows.extend(part.astype(f32) for part in split(sums))
    out[...] = jnp.concatenate(rows, axis=0).astype(bf16)


def pack_misc(conditions, mod_one, mod_two, sums_one, sums_two):
    return pl.pallas_call(
        misc_kernel,
        out_shape=jax.ShapeDtypeStruct((OWN + SUMS, 2 * D), bf16),
        in_specs=[VMEM] * 5,
        out_specs=VMEM,
        compiler_params=pltpu.CompilerParams(vmem_limit_bytes=8 * 1024 * 1024),
    )(conditions, mod_one, mod_two, sums_one, sums_two)


def finish_kernel(widths, counts, waits, *refs):
    count = len(widths)
    kept, refs = refs[:count], refs[count:]
    came, refs = refs[: len(counts)], refs[len(counts) :]
    parts = refs[:4]
    mine, other, small_mine, small_other = refs[4 + waits :]
    places = [(ref, i) for ref, many in zip(came, counts) for i in range(many)]
    added = []
    for i in range(count):
        ref, place = places[i]
        start = sum(widths[i - place : i])
        added.append(kept[i][0] + ref[0, :, start : start + widths[i]].astype(f32))
    a1, f1, f2, a2 = added
    size = parts[0].shape[0] - SUMS
    rows = jnp.concatenate([part[:size, :] for part in parts], axis=0)
    rows = rows.astype(f32).reshape(-1, OWN, 2 * D)
    shard = mine.shape[0]
    chosen = lane_iota(shard, D) == row_iota(shard, D) + lax.axis_index("row") * shard
    chosen = jnp.where(chosen, 1.0, 0.0).astype(bf16)
    features = [rows[:, 6, slot * D : (slot + 1) * D].astype(bf16) for slot in range(SLOTS)]
    lifted = jnp.concatenate([mm_t(chosen, part) for part in features], axis=1).astype(bf16)

    def ada(first):
        columns = []
        for i in range(3):
            both = [rows[:, first + 3 * slot + i, :] for slot in range(SLOTS)]
            columns.append(mm(lifted, jnp.concatenate(both, axis=0).astype(bf16)))
        return jnp.concatenate(columns, axis=1)

    first = lax.axis_index("section") == 0
    at = 0
    for one, two in ((a1, a2), (f1, f2), (ada(0), ada(OWN // 2))):
        columns = slice(at, at + one.shape[1])
        mine[:, columns] = jnp.where(first, one, two)
        other[:, columns] = jnp.where(first, two, one)
        at += one.shape[1]
    total = misc_sums(*parts)
    one, two = total[0:8, :], total[8:16, :]
    small_mine[...] = jnp.where(first, one, two)
    small_other[...] = jnp.where(first, two, one)


def finish(kept, came, parts, after):
    widths = [array.shape[2] for array in kept]
    shard = kept[0].shape[1]
    wide = GROUP + FF + 6 * D
    arrays = [array for array, _ in came]
    shapes = [(shard, wide)] * 2 + [(8, 2 * D)] * 2
    return pl.pallas_call(
        functools.partial(finish_kernel, widths, [count for _, count in came], len(after)),
        out_shape=[jax.ShapeDtypeStruct(shape, f32) for shape in shapes],
        in_specs=[VMEM] * (len(kept) + len(came) + 4) + [ANY] * len(after),
        out_specs=[VMEM] * 4,
        compiler_params=pltpu.CompilerParams(vmem_limit_bytes=8 * 1024 * 1024),
    )(*kept, *arrays, *parts, *after)


def output_kernel(mine, other, small_mine, small_other, *outs):
    first = lax.axis_index("section") == 0

    def halves(start, width):
        columns = slice(start, start + width)
        pair = mine[:, columns], other[:, columns]
        return jnp.where(first, pair[0], pair[1]), jnp.where(first, pair[1], pair[0])

    attn = halves(0, GROUP)
    cut = GROUP - 2 * D
    outs[0][...] = attn[0][:, :D]
    outs[1][...] = attn[0][:, D : 2 * D]
    outs[2][:, :cut] = attn[0][:, 2 * D :]
    outs[2][:, cut:] = attn[1][:, : D - cut]
    outs[3][...] = attn[1][:, D - cut : 2 * D - cut]
    outs[4][...] = attn[1][:, 2 * D - cut : 3 * D - cut]
    decay = jnp.transpose(attn[1][:, 3 * D - cut :])
    for head in range(HEADS):
        outs[5][head] = decay[head : head + 1, :]
    up = halves(GROUP, FF // 2)
    outs[6][:, : FF // 2] = up[0]
    outs[6][:, FF // 2 :] = up[1]
    for piece in range(2):
        down = halves(GROUP + FF // 2 + piece * D, D)
        outs[7][piece] = down[0]
        outs[7][2 + piece] = down[1]
    outs[8][...] = mine[:, GROUP + FF :] + other[:, GROUP + FF :]
    small = small_mine[...] + small_other[...]
    half = 2 * D
    for i in range(3):
        outs[9][:, i * half : (i + 1) * half] = small[i : i + 1, :]
    for i in range(2):
        outs[10][:, i * half : (i + 1) * half] = small[3 + i : 4 + i, :]
    outs[11][...] = small[5:6, :D]
    outs[12][0] = small[5:6, D:]
    outs[12][1] = small[6:7, :D]
    outs[12][2] = small[6:7, D:]
    outs[13][...] = small[7:8, :HEADS]


def outputs(mine, other, small_mine, small_other):
    shard = mine.shape[0]
    shapes = (
        [(shard, D)] * 5
        + [(HEADS, 1, shard), (shard, FF), (4, shard, D), (shard, 6 * D)]
        + [(1, 6 * D), (1, FF), (1, D), (3, 1, D), (1, HEADS)]
    )
    return pl.pallas_call(
        output_kernel,
        out_shape=[jax.ShapeDtypeStruct(shape, f32) for shape in shapes],
        in_specs=[VMEM] * 4,
        out_specs=[VMEM] * len(shapes),
        compiler_params=pltpu.CompilerParams(vmem_limit_bytes=8 * 1024 * 1024),
    )(mine, other, small_mine, small_other)


def both_kernel(one, two, came, out, mark, kept, sems):
    section = lax.axis_index("section")
    mark[...] = jnp.zeros(mark.shape, f32)

    def move(mine, layer):
        arrive = [
            pltpu.make_async_copy(mine, kept.at[layer], sems.at[0]),
            pltpu.make_async_copy(came, kept.at[1 - layer], sems.at[1]),
        ]
        leave = [
            pltpu.make_async_copy(kept.at[layer], out.at[layer], sems.at[2]),
            pltpu.make_async_copy(kept.at[1 - layer], out.at[1 - layer], sems.at[3]),
        ]
        for copy in arrive:
            copy.start()
        for copy, after in zip(arrive, leave):
            copy.wait()
            after.start()
        for copy in leave:
            copy.wait()

    @pl.when(section == 0)
    def _():
        move(one, 0)

    @pl.when(section == 1)
    def _():
        move(two, 1)


def both_micros(one, two, came):
    return pl.pallas_call(
        both_kernel,
        out_shape=[
            jax.ShapeDtypeStruct((MICRO,) + one.shape, one.dtype),
            jax.ShapeDtypeStruct((8, LANES), f32),
        ],
        in_specs=[ANY] * 3,
        out_specs=[ANY, VMEM],
        scratch_shapes=[
            pltpu.VMEM((MICRO,) + one.shape, one.dtype),
            pltpu.SemaphoreType.DMA((4,)),
        ],
        compiler_params=pltpu.CompilerParams(vmem_limit_bytes=8 * 1024 * 1024),
    )(one, two, came)


def swap(values):
    return lax.ppermute(values, "section", [(0, 1), (1, 0)])


def row_bits():
    bits = lax.axis_size("row").bit_length() - 1
    third = bits // 3
    return (
        tuple(range(third)),
        tuple(range(third, 2 * third)),
        tuple(range(2 * third, bits)),
    )


def across(values, flips):
    size = lax.axis_size("row")
    return lax.ppermute(values, "row", [(i, i ^ flips) for i in range(size)])


def partner(values, bit):
    return across(values, 1 << bit)


def axis_of(bit):
    return lax.axis_size("row").bit_length() - 2 - bit


def bit_of(bit):
    return (lax.axis_index("row") >> bit) & 1


def single(values):
    return values.reshape((1,) * (lax.axis_size("row").bit_length() - 1) + values.shape)


def gather_steps(along_x, along_y, along_z):
    steps = [(bit, bit) for bit in reversed(along_z)]
    return steps + list(zip(along_x + along_y, along_y + along_x))


def flat(held):
    return held.reshape(-1, held.shape[-1])


def lock(*arrays):
    return lax.optimization_barrier(arrays)


def on_device(
    tokens, conditions, output_grad, layouts,
    w_ada, b_ada, w_query, w_key, w_value, w_gate, w_out, w_decay, b_decay, conv_kernel,
    w_up, b_up, w_down, b_down,
):
    section = lax.axis_index("section")
    devices = lax.axis_size("row")
    shard = w_query.shape[1]
    along_x, along_y, along_z = row_bits()

    def both(values):
        return values, swap(values)

    qkuo, vgd, down, ada, lifted = pack(
        w_query, w_key, w_value, w_gate, w_out, w_decay.transpose(0, 2, 1), w_up, w_down, w_ada,
        conditions,
    )
    small = pack_small(b_up, b_down, conv_kernel, b_decay)
    conds = conditions.reshape(MICRO * SLOTS, D)
    steps = gather_steps(along_x, along_y, along_z)
    lag = len(along_z)
    plane = along_x + along_y
    bounds = [len(plane) * i // lag for i in range(lag + 1)]
    held = [single(array) for array in (qkuo, vgd, down)]
    ada = single(ada)
    for place, pair in enumerate(steps):
        bits = pair + pair[1:]
        if place == len(steps) - 1:
            bits = pair + pair
            held = [held[0][..., : 2 * D], held[1], held[0][..., 2 * D :], held[2]]
        came = [partner(array, bit) for array, bit in zip(held, bits)]
        after = ()
        if place < lag:
            lifted = jnp.concatenate([lifted, partner(lifted, pair[0])], axis=0)
            for bit in plane[bounds[place] : bounds[place + 1]]:
                (ada,) = join([ada], [partner(ada, bit)], (bit,))
            after = (small, lifted, ada)
        if place == lag:
            left = list(reversed(along_z))
            rows = D >> lag
            line = (lax.axis_index("row") >> len(plane)) * rows
            lifted = lax.dynamic_slice_in_dim(lifted, line, rows, 2)
            product = mm(lifted.reshape(-1, rows), flat(ada))
            terms = (product.reshape(1 << lag, MICRO * SLOTS, 6 * D),)
            for bit in along_z:
                stays, goes = term_step(1 << left.index(bit), *terms)
                left.remove(bit)
                terms = (stays, partner(goes, bit))
            after = (terms[1],)
        if place < len(steps) - 1:
            held = join(held, came, bits, after)
        else:
            qk, vgd = [both(flat(array)) for array in join(held[:2], came[:2], bits[:2])]
            mods = both(sum(term[0] for term in terms) + b_ada[0])
            smalls = both(small)
            x = tokens
            *saved, gated = attn_forward(0, layouts, x, mods, smalls, qk, vgd)
            held = join(held[2:], came[2:], bits[2:], (gated,))
    upo, down = [both(flat(array)) for array in held]
    out_one, branch, down_raw = ffn_forward(0, layouts, x, mods, smalls, gated, upo, down)
    kept = [(x, saved, gated, branch, down_raw)]
    x = out_one[None]
    *saved, gated = attn_forward(1, layouts, x, mods, smalls, qk, vgd)
    kept.append((x, saved, gated, None, None))

    late, _ = lock(w_ada[0], out_one)
    ada_all = lax.all_gather(late, "row", axis=0, tiled=True)

    def ffn_step(l, grad, after=()):
        x, saved, gated, branch, down_raw = kept[l]
        results = ffn_backward(
            l, layouts, x, mods, smalls, gated, branch, down_raw, grad, upo, down, devices, after
        )
        acts, (mid_grad, branch_low, gwo, sums, *terms) = results[: 2 * l], results[2 * l :]
        if terms[0].ndim == 2:
            up_sum = terms[0].reshape(devices, shard, 2, FF // 2)
            down_sum = terms[1].reshape(devices, 2, 2, shard, D)
            terms = []
            for own in (section, 1 - section):
                up_half = lax.dynamic_index_in_dim(up_sum, own, 2, keepdims=False)
                down_half = lax.dynamic_index_in_dim(down_sum, own, 1, keepdims=False)
                terms.append(
                    jnp.concatenate([up_half, down_half[:, 0], down_half[:, 1]], axis=2)
                )
            terms[1] = terms[1].astype(bf16)
        return [branch_low, gwo], mid_grad, terms[0], terms[1], sums, *acts

    def mixer_step(l, carried, after=()):
        low, keep, sent, sums = mixer_backward(
            l, layouts, smalls, kept[l][1], *carried, upo, after
        )
        by_row = lambda array: array.reshape(devices, shard, GROUP)
        return low, by_row(keep), by_row(sent), sums

    def input_step(l, low, mid_grad, ffn_sums, mixer_sums, two=None, after=()):
        x = kept[l][0]
        return input_backward(
            l, layouts, x, mods, low, mid_grad, ffn_sums, mixer_sums, qk, vgd, two, after
        )

    def run(keep, came, bits, below=1, after=()):
        for bit in bits[:-1]:
            keep, sent = step(keep, came, bit, below, after)
            came = [(partner(sent, bit), len(keep))]
        return step(keep, came, bits[-1], below, after)

    def grown(mod, bits):
        for bit in bits:
            mod = misc_step(mod, partner(mod, bit))
        return mod

    x_bits, y_bits, z_bits = along_x, along_y, along_z
    carried, mid_grad, f2_keep, f2_sent, f2_sums, out_two, acts_sent = ffn_step(1, output_grad)
    *carried, f2_sent, acts_sent = lock(*carried, f2_sent, acts_sent)
    f2_came = swap(f2_sent)
    acts_came = swap(acts_sent)
    low, a2_keep, a2_sent, m2_sums = mixer_step(1, carried)
    low, a2_sent, f2_came, acts_came = lock(low, a2_sent, f2_came, acts_came)
    a2_came = swap(a2_sent)
    gx_two, grad, mod_low_two, sums_two = input_step(1, low, mid_grad, f2_sums, m2_sums)
    grad, a2_came = lock(grad, a2_came)
    f2_keep, f2_sent = run([f2_keep], [(f2_came, 1)], x_bits)
    a2_keep, a2_sent = run([a2_keep], [(a2_came, 1)], y_bits, 1 << len(x_bits))
    grad, f2_sent, a2_sent = lock(grad, f2_sent, a2_sent)
    f2_came = partner(f2_sent, x_bits[-1])
    a2_came = partner(a2_sent, y_bits[-1])

    carried, mid_grad, f1_keep, f1_sent, f1_sums = ffn_step(0, grad[None])
    *carried, f1_sent, f2_came, a2_came = lock(*carried, f1_sent, f2_came, a2_came)
    f1_came = swap(f1_sent)
    f2_keep, f2_sent = run(f2_keep, [(f2_came, 1)], y_bits)
    a2_keep, a2_sent = run(a2_keep, [(a2_came, 1)], x_bits)
    f1_keep, f1_sent = run([f1_keep], [(f1_came, 1)], x_bits)
    *carried, f2_sent, a2_sent, f1_sent = lock(*carried, f2_sent, a2_sent, f1_sent)
    f1_came = partner(f1_sent, x_bits[-1])
    a2_came = partner(a2_sent, x_bits[-1])
    f2_came = partner(f2_sent, y_bits[-1])
    low, a1_keep, a1_sent, m1_sums = mixer_step(0, carried)
    low, a1_sent, f2_came, a2_came, f1_came, ada_all = lock(
        low, a1_sent, f2_came, a2_came, f1_came, ada_all
    )
    a1_came = swap(a1_sent)
    two_keep, two_sent = run(f2_keep + a2_keep, [(f2_came, 1), (a2_came, 1)], z_bits[:1])
    f1_keep, f1_sent = run(f1_keep, [(f1_came, 1)], y_bits)
    a1_keep, a1_sent = run([a1_keep], [(a1_came, 1)], x_bits)
    low, two_sent, f1_sent, a1_sent = lock(low, two_sent, f1_sent, a1_sent)
    a1_came = partner(a1_sent, x_bits[-1])
    f1_came = partner(f1_sent, y_bits[-1])
    two_came = partner(two_sent, z_bits[0])
    gx_one, _, mod_low_one, sums_one, gx_sent, mod_mine, mod_sent = input_step(
        0, low, mid_grad, f1_sums, m1_sums, (gx_two, mod_low_two)
    )
    misc = pack_misc(conds, mod_low_one, mod_low_two, sums_one, sums_two)
    misc, a1_came, two_came, f1_came, gx_sent, mod_sent = lock(
        misc, a1_came, two_came, f1_came, gx_sent, mod_sent
    )

    a1_keep, a1_sent = run(a1_keep, [(a1_came, 1)], y_bits)
    a1_sent, misc = lock(a1_sent, misc)
    a1_came = partner(a1_sent, y_bits[-1])
    misc = grown(misc, tuple(reversed(z_bits))[:-1])
    gx_came = swap(gx_sent)
    mod_came = swap(mod_sent)
    keep, came = a1_keep + f1_keep, [(a1_came, 1), (f1_came, 1)]
    for place, bit in enumerate(z_bits):
        if place == 1:
            keep, came = keep + two_keep, came + [(two_came, 2)]
        keep, sent = step(keep, came, bit)
        if place == len(z_bits) - 1:
            sent, misc, gx_came, mod_came = lock(sent, misc, gx_came, mod_came)
        elif place == 0:
            sent, misc = lock(sent, misc)
        came = [(partner(sent, bit), len(keep))]
        if place == 0:
            misc = grown(misc, z_bits[:1] + x_bits[:-1] + y_bits[:-1])
    last = (1 << x_bits[-1], 1 << y_bits[-1])
    parts = [misc] + [across(misc, flips) for flips in (last[0], last[1], last[0] + last[1])]
    gx_out, gx_mark = both_micros(gx_one, gx_two, gx_came)
    acts_out, acts_mark = both_micros(out_one, out_two, acts_came)
    grad_lifted = lifted_grads(mod_mine, mod_came, ada_all)
    lifted_came = swap(grad_lifted)
    mine, other, small_mine, small_other = finish(
        keep, came, parts, (gx_mark, acts_mark, lifted_came)
    )
    came, small_came = swap(other), swap(small_other)
    (
        g_query, g_key, g_value, g_gate, g_out, g_decay, g_up, g_down, g_ada,
        g_b_ada, g_b_up, g_b_down, g_conv, g_b_decay,
    ) = outputs(mine, came, small_mine, small_came)

    grad_lifted = (grad_lifted + lifted_came).reshape(MICRO, SLOTS, D)
    _, pull_silu = jax.vjp(jax.nn.silu, conditions.astype(f32))
    (cond_grads,) = pull_silu(grad_lifted)

    return (
        acts_out[None],
        gx_out[None],
        cond_grads,
        g_ada[None],
        g_b_ada,
        g_query[None],
        g_key[None],
        g_value[None],
        g_gate[None],
        g_out[None],
        g_decay.transpose(1, 2, 0),
        g_b_decay,
        g_conv.transpose(1, 0, 2),
        g_up[None],
        g_b_up,
        g_down.reshape(1, FF // devices, D),
        g_b_down,
    )


def solution(mesh):
    rows = P(None, "row", None)
    mats = P("section", "row", None)
    vector = P("section", None)
    in_specs = (
        rows, rows, rows, P(None, "row"),
        mats, vector, mats, mats, mats, mats, mats, mats, vector, P("section", None, None),
        mats, vector, mats, vector,
    )
    blocks = P("section", None, "row", None)
    out_specs = (
        blocks, blocks, rows,
        mats, vector, mats, mats, mats, mats, mats, mats, vector, P("section", None, None),
        mats, vector, mats, vector,
    )
    return jax.shard_map(
        on_device, mesh=mesh, in_specs=in_specs, out_specs=out_specs, check_vma=False
    )
```

```python
import functools

import jax
import jax.numpy as jnp
from jax import lax
from jax.experimental import pallas as pl
from jax.experimental.pallas import tpu as pltpu
from jax.sharding import PartitionSpec as P

D = 384
HEADS = 6
HEAD_DIM = 64
FF = 1536
MICRO = 2
ROWS = 512
HALF = 256
SLOTS = 2
PAIR = 128
PAIRS = D // PAIR
QKVG = 4 * D
LANES = 128
GROUP = (QKVG + D + LANES) // 2
NEG = -1e30
SCALE = HEAD_DIM**-0.5

bf16 = jnp.bfloat16
f32 = jnp.float32


def mm(left, right):
    return jnp.dot(left, right, preferred_element_type=f32)


def mm_t(left, right):
    return lax.dot_general(left, right, (((1,), (1,)), ((), ())), preferred_element_type=f32)


def split(values):
    high = values.astype(bf16)
    return high, (values - high.astype(f32)).astype(bf16)


def split_three(values):
    high, rest = split(values)
    mid = values - high.astype(f32)
    middle, low = split(mid)
    return high, middle, low


def cat_left(values):
    high, low = split(values)
    return jnp.concatenate([high, low, high], axis=1)


def cat_right(values):
    high, low = split(values)
    return jnp.concatenate([high, high, low], axis=1)


def mm_near(left, right_pair, right_high):
    high, low = split(left)
    wide = mm(high, right_pair)
    return wide[:, :PAIR] + wide[:, PAIR:] + mm(low, right_high)


def lane_iota(rows, columns):
    return lax.broadcasted_iota(jnp.int32, (rows, columns), 1)


def row_iota(rows, columns):
    return lax.broadcasted_iota(jnp.int32, (rows, columns), 0)


def order_matrix(start, rows, wide, to_scan):
    t = row_iota(rows, ROWS) + start
    small = (t & 256) + ((t & 15) << 4) + ((t & 255) >> 4)
    if to_scan:
        large = ((t & 15) << 5) + (t >> 4)
    else:
        large = ((t & 31) << 4) + (t >> 5)
    source = jnp.where(wide, large, small)
    return jnp.where(lane_iota(rows, ROWS) == source, 1.0, 0.0).astype(bf16)


def normalise(values):
    centred = values - jnp.mean(values, axis=-1, keepdims=True)
    rate = lax.rsqrt(jnp.mean(centred * centred, axis=-1, keepdims=True) + 1e-06)
    return centred * rate, rate


def normalise_back(normal, rate, grad):
    return rate * (
        grad
        - jnp.mean(grad, axis=-1, keepdims=True)
        - normal * jnp.mean(grad * normal, axis=-1, keepdims=True)
    )


class In:
    def __init__(self, copy, kept):
        self.copy = copy
        self.kept = kept

    def __call__(self):
        if self.copy is not None:
            self.copy.wait()
            self.copy = None
        return self.kept


class Kernel:
    def __init__(self, layer, layouts):
        self.layer = layer
        self.section = lax.axis_index("section")
        self.own = self.section == layer
        self.layout = layouts[self.section, 0]
        self.wide = self.layout == 0
        self.live_rows = jnp.where(self.wide, ROWS, self.layout * HALF)
        self.pushed = {}

    def load(self, kind, refs, kept, sem):
        if kind == "own":
            mine, other = refs

            @pl.when(self.own)
            def _():
                pltpu.make_async_copy(mine, kept, sem).start()

            @pl.when(jnp.logical_not(self.own))
            def _():
                pltpu.make_async_copy(other, kept, sem).start()

            return In(pltpu.make_async_copy(mine, kept, sem), kept)
        (source,) = refs
        if kind == "micro":
            source = source.at[self.section if source.shape[0] == MICRO else 0]
        copy = pltpu.make_async_copy(source, kept, sem)
        copy.start()
        return In(copy, kept)

    def push(self, name):
        if name not in self.results:
            return
        kept, target, sem = self.results[name]
        copy = pltpu.make_async_copy(kept, target, sem)
        copy.start()
        self.pushed[name] = copy

    def finish(self):
        for name in self.results:
            if name not in self.pushed:
                self.push(name)
        for copy in self.pushed.values():
            copy.wait()

    def slot(self, half):
        return jnp.where(self.wide, 0, half)

    def share(self, slot, part):
        row = pl.ds(2 * self.section + slot, 1)
        return self.mods()[row, part * D : (part + 1) * D]

    def bu(self):
        return self.small()[0:1, :]

    def bn(self):
        return self.small()[1:2, :D]

    def ck(self, tap):
        return self.small()[2 + tap : 3 + tap, :D]

    def bd(self):
        return self.small()[5:6, :LANES]


def sigmoid(values):
    return 1.0 / (1.0 + jnp.exp(-values))


GELU_A = 0.7978845608028654
GELU_B = 0.044715


def gelu_parts(values):
    square = values * values
    tanh = jnp.tanh(GELU_A * values * (1.0 + GELU_B * square))
    return square, tanh


def fill_bias(bias, wide):
    bias[:, :HALF] = jnp.full((HALF, HALF), 0.0, f32) + jnp.where(wide, 0.0, NEG)
    causal = row_iota(HALF, HALF) >= lane_iota(HALF, HALF)
    bias[:, HALF:] = jnp.where(causal, 0.0, NEG)


def decay_factors(cum, cumt, bias, head):
    row = cumt[pl.ds(head, 1), :]
    lanes = lane_iota(1, LANES)
    column = jnp.sum(jnp.where(lanes == head, cum[...], 0.0), axis=1, keepdims=True)
    first = jnp.exp(column[:HALF] - row[:, :HALF] + bias[:, HALF:])
    second = jnp.exp(column[HALF:] - row + bias[...])
    return first, second


def head_norm(values, lanes):
    square = values * values
    low = jnp.sum(jnp.where(lanes < HEAD_DIM, square, 0.0), axis=1, keepdims=True)
    high = jnp.sum(jnp.where(lanes < HEAD_DIM, 0.0, square), axis=1, keepdims=True)
    return jnp.where(lanes < HEAD_DIM, low, high) * (1.0 / HEAD_DIM)


def fill_decay(dp, bd, cum, cumt):
    raw = dp[...] + bd
    log_decay = (jnp.minimum(raw, 0.0) - jnp.log1p(jnp.exp(-jnp.abs(raw)))) * (1.0 / 16.0)
    high, middle, low = split_three(log_decay)
    causal = jnp.where(row_iota(ROWS, ROWS) >= lane_iota(ROWS, ROWS), 1.0, 0.0).astype(bf16)
    cum[...] = mm(causal, high) + mm(causal, middle) + mm(causal, low)
    cumt[...] = jnp.transpose(cum[...])


def columns(index, first=0):
    return slice(index * PAIR + first, index * PAIR + first + PAIR)


def attn_forward_body(k):
    flip = k.layer == 1
    wide = k.wide
    x = k.x()
    k.mods()

    def first(i, carry):
        rows = pl.ds(pl.multiple_of(i * HALF, HALF), HALF)
        slot = k.slot(i)
        normal, _ = normalise(x[rows, :].astype(f32))
        k.inner[rows, :] = (normal * (1.0 + k.share(slot, 1)) + k.share(slot, 0)).astype(bf16)
        return carry

    lax.fori_loop(0, 2, first, 0)
    w_qk = k.w_qk()
    w_vgd = k.w_vgd()

    def project(i, carry):
        start = i * HALF
        rows = pl.ds(start, HALF)
        if flip:
            part = mm(order_matrix(start, HALF, wide, True), k.inner[...]).astype(bf16)
        else:
            part = k.inner[rows, :]
        k.ordered[rows, :] = part
        k.qkvg[rows, : 2 * D] = mm(part, w_qk[...])
        k.qkvg[rows, 2 * D :] = mm(part, w_vgd[:, : 2 * D])
        k.dp[rows, :] = mm(part, w_vgd[:, 2 * D :])
        return carry

    lax.fori_loop(0, 2, project, 0)
    k.small()
    for name in ("ordered", "qkvg", "dp"):
        k.push(name)
    fill_decay(k.dp, k.bd(), k.cum, k.cumt)
    fill_bias(k.bias, wide)

    vpad = k.vpad
    vpad[0:8, :] = jnp.zeros((8, D), f32)
    vpad[8 : 8 + ROWS, :] = k.qkvg[:, 2 * D : 3 * D]
    position = row_iota(ROWS, 1) & jnp.where(wide, ROWS - 1, HALF - 1)
    one = jnp.where(position >= 1, vpad[7 : 7 + ROWS, :], 0.0)
    two = jnp.where(position >= 2, vpad[6 : 6 + ROWS, :], 0.0)
    k.vc[...] = k.ck(0) * vpad[8 : 8 + ROWS, :] + k.ck(1) * one + k.ck(2) * two
    for name in ("cum", "cumt", "vc"):
        k.push(name)

    def pair(p, carry):
        lanes = lane_iota(1, PAIR)
        queries = cat_left(k.qkvg[:, columns(p)] * SCALE)
        keys = k.qkvg[:, columns(p, D)]
        value_high, value_low = split(k.vc[:, columns(p)])
        values = jnp.concatenate([value_high, value_low], axis=1)
        parts = []
        for e in range(2):
            key_cat = cat_right(jnp.where((lanes // HEAD_DIM) == e, keys, 0.0))
            first, second = decay_factors(k.cum, k.cumt, k.bias, 2 * p + e)
            first = first * mm_t(queries[:HALF], key_cat[:HALF])
            second = second * mm_t(queries[HALF:], key_cat)
            parts.append(
                jnp.concatenate(
                    [
                        mm_near(first, values[:HALF], value_high[:HALF]),
                        mm_near(second, values, value_high),
                    ],
                    axis=0,
                )
            )
        total = jnp.where(lanes < HEAD_DIM, parts[0], parts[1])
        k.o[:, columns(p)] = total
        gate = k.qkvg[:, columns(p, 3 * D)]
        normed = total * lax.rsqrt(head_norm(total, lanes) + 1.0)
        mixed = (normed * (gate * sigmoid(gate))).astype(bf16)
        if flip:
            k.inner[:, columns(p)] = mixed
        else:
            k.gated[:, columns(p)] = mixed
        return carry

    for p in range(PAIRS):
        pair(p, 0)
    k.push("o")
    if flip:

        def back(i, carry):
            start = i * HALF
            k.gated[pl.ds(start, HALF), :] = mm(
                order_matrix(start, HALF, wide, False), k.inner[...]
            ).astype(bf16)
            return carry

        lax.fori_loop(0, 2, back, 0)


def ffn_forward_body(k):
    gated, x = k.gated(), k.x()
    k.mods(), k.small()

    def tile(i, carry):
        start = i * HALF
        rows = pl.ds(start, HALF)
        slot = k.slot(i)
        grown = mm(gated[rows, :], k.wo()[...])
        k.branch[rows, :] = grown
        middle = x[rows, :].astype(f32) + k.share(slot, 2) * grown
        normal, _ = normalise(middle)
        inner = (normal * (1.0 + k.share(slot, 4)) + k.share(slot, 3)).astype(bf16)
        up = mm(inner, k.wu()[...]) + k.bu()
        _, tanh = gelu_parts(up)
        hidden = (0.5 * up * (1.0 + tanh)).astype(bf16)
        low = mm(hidden, k.wn()[...])
        k.down[rows, :] = low
        result = middle + k.share(slot, 5) * (low + k.bn())
        live = (row_iota(HALF, 1) + start) < k.live_rows
        k.out[rows, :] = jnp.where(live, result, 0.0).astype(bf16)
        return carry

    for i in range(2):
        tile(i, 0)


def ffn_backward_body(k):
    gmod, gbu, gbn = k.gmod, k.gbu, k.gbn
    gmod[...] = jnp.zeros(gmod.shape, f32)
    gbu[...] = jnp.zeros(gbu.shape, f32)
    gbn[...] = jnp.zeros(gbn.shape, f32)
    both_ways = k.layer == 1
    k.mods(), k.small()
    x, grad = k.x(), k.grad()
    if both_ways:
        gated, wo = k.gated(), k.wo()
    else:
        branch, down = k.branch(), k.down()

    def tile(i, carry):
        start = i * HALF
        rows = pl.ds(start, HALF)
        slot = k.slot(i)

        def add(part, values):
            where = (pl.ds(slot, 1), slice((part - 2) * D, (part - 1) * D))
            gmod[where] = gmod[where] + jnp.sum(values, axis=0, keepdims=True)

        grown = mm(gated[rows, :], wo[...]) if both_ways else branch[rows, :]
        middle = x[rows, :].astype(f32) + k.share(slot, 2) * grown
        normal, rate = normalise(middle)
        inner = (normal * (1.0 + k.share(slot, 4)) + k.share(slot, 3)).astype(bf16)
        k.inner_s[rows, :] = inner
        up = mm(inner, k.wu()[...]) + k.bu()
        square, tanh = gelu_parts(up)
        half = 0.5 * (1.0 + tanh)
        hidden = (up * half).astype(bf16)
        k.hidden_s[rows, :] = hidden
        lower = (mm(hidden, k.wn()[...]) if both_ways else down[rows, :]) + k.bn()
        live = (row_iota(HALF, 1) + start) < k.live_rows
        if both_ways:
            result = middle + k.share(slot, 5) * lower
            k.out[rows, :] = jnp.where(live, result, 0.0).astype(bf16)
        above = jnp.where(live, grad[rows, :].astype(f32), 0.0)
        add(5, above * lower)
        grad_down = above * k.share(slot, 5)
        gbn[...] = gbn[...] + jnp.sum(grad_down, axis=0, keepdims=True)
        down_low = grad_down.astype(bf16)
        k.down_s[rows, :] = down_low
        slope = half + 0.5 * up * (1.0 - tanh * tanh) * (
            GELU_A * (1.0 + 3.0 * GELU_B * square)
        )
        grad_up = mm_t(down_low, k.wn()[...]) * slope
        gbu[...] = gbu[...] + jnp.sum(grad_up, axis=0, keepdims=True)
        up_low = grad_up.astype(bf16)
        k.up_s[rows, :] = up_low
        grad_inner = mm_t(up_low, k.wu()[...])
        add(3, grad_inner)
        add(4, grad_inner * normal)
        grad_middle = above + normalise_back(
            normal, rate, grad_inner * (1.0 + k.share(slot, 4))
        )
        k.mid_grad[rows, :] = grad_middle
        add(2, grad_middle * grown)
        k.branch_low[rows, :] = (grad_middle * k.share(slot, 2)).astype(bf16)
        return carry

    for i in range(2):
        tile(i, 0)
    k.push("mid_grad")
    k.push("branch_low")
    if both_ways:
        own = k.section == 0
        k.sent[...] = jnp.where(own, k.out[...].astype(f32), x[...].astype(f32)).astype(bf16)
        k.push("out")
        k.push("sent")

    def weights(j, carry):
        part = pl.ds(pl.multiple_of(j * HALF, HALF), HALF)
        hidden_t = jnp.transpose(k.hidden_s[:, part].astype(f32)).astype(bf16)
        k.gwn[part, :] = mm(hidden_t, k.down_s[...])
        return carry

    lax.fori_loop(0, FF // HALF, weights, 0)
    inner_t = jnp.transpose(k.inner_s[...].astype(f32)).astype(bf16)
    if k.packed:
        devices, shard, _ = k.keep.shape

        def halves(j, carry):
            for kept, own in ((k.keep, c_section), (k.gone, 1 - c_section)):
                columns = pl.ds(pl.multiple_of(j * HALF + own * (FF // 2), HALF), HALF)
                here = pl.ds(pl.multiple_of(j * HALF, HALF), HALF)
                part = mm(inner_t, k.up_s[:, columns]).reshape(devices, shard, HALF)
                kept[:, :, here] = part.astype(kept.dtype)
            return carry

        c_section = k.section
        lax.fori_loop(0, FF // 2 // HALF, halves, 0)

        def owner(r, carry):
            for kept, own in ((k.keep, c_section), (k.gone, 1 - c_section)):
                for piece in range(2):
                    start = pl.multiple_of((4 * r + 2 * own + piece) * shard, 8)
                    rows = k.gwn[pl.ds(start, shard), :]
                    at = FF // 2 + piece * D
                    kept[r, :, at : at + D] = rows.astype(kept.dtype)
            return carry

        lax.fori_loop(0, devices, owner, 0)
        k.push("keep")
        k.push("gone")
    else:
        k.gwu[...] = mm(inner_t, k.up_s[...])
    gated = k.gated()
    k.gwo[...] = mm(jnp.transpose(gated[...].astype(f32)).astype(bf16), k.branch_low[...])

    short = jnp.concatenate([gbn[...], jnp.zeros((1, FF - D), f32)], axis=1)
    k.sums[...] = jnp.concatenate(
        [gmod[0:SLOTS, :], gbu[...], short, jnp.zeros((4, FF), f32)], axis=0
    )


def mixer_backward_body(k):
    flip = k.layer == 1
    wide = k.wide
    mixed_s, low, dv_s, rows_s, cols_s = k.mixed_s, k.low, k.dv_s, k.rows_s, k.cols_s
    fill_bias(k.bias, wide)
    branch_low, wo = k.branch_low(), k.wo()

    def first(i, carry):
        start = i * HALF
        rows = pl.ds(start, HALF)
        if flip:
            part = mm(order_matrix(start, HALF, wide, True), branch_low[...]).astype(bf16)
        else:
            part = branch_low[rows, :]
        mixed_s[rows, :] = mm_t(part, wo[...])
        return carry

    lax.fori_loop(0, 2, first, 0)
    rows_s[...] = jnp.zeros(rows_s.shape, f32)
    cols_s[...] = jnp.zeros(cols_s.shape, f32)
    qkvg, vc, cum, cumt, o = k.qkvg(), k.vc(), k.cum(), k.cumt(), k.o()
    k.small()

    def pair(p, carry):
        lanes = lane_iota(1, PAIR)
        total = o[:, columns(p)]
        gate = qkvg[:, columns(p, 3 * D)]
        above = mixed_s[:, columns(p)]
        rate = lax.rsqrt(head_norm(total, lanes) + 1.0)
        sig = sigmoid(gate)
        grad_gate = above * (total * rate) * (sig * (1.0 + gate * (1.0 - sig)))
        low[:, columns(p, 3 * D)] = grad_gate.astype(bf16)
        grad_normed = above * (gate * sig)
        product = grad_normed * total
        inside = jnp.where(
            lanes < HEAD_DIM,
            jnp.sum(jnp.where(lanes < HEAD_DIM, product, 0.0), axis=1, keepdims=True),
            jnp.sum(jnp.where(lanes < HEAD_DIM, 0.0, product), axis=1, keepdims=True),
        ) * (1.0 / HEAD_DIM)
        grad_o = rate * grad_normed - total * (rate * rate * rate) * inside

        queries = qkvg[:, columns(p)] * SCALE
        keys = qkvg[:, columns(p, D)]
        values = vc[:, columns(p)]
        query_cat = cat_left(queries)
        grad_cat = cat_left(grad_o)
        key_high, key_low = split(keys)
        key_pair = jnp.concatenate([key_high, key_low], axis=1)
        query_t = jnp.transpose(queries)
        grad_t = jnp.transpose(grad_o)
        grad_q = []
        grad_k = []
        grad_v = []
        for e in range(2):
            mine = (lanes // HEAD_DIM) == e
            head = 2 * p + e
            key_cat = cat_right(jnp.where(mine, keys, 0.0))
            value_cat = cat_right(jnp.where(mine, values, 0.0))
            first, second = decay_factors(cum, cumt, k.bias, head)
            raw_first = mm_t(query_cat[:HALF], key_cat[:HALF])
            raw_second = mm_t(query_cat[HALF:], key_cat)
            grad_first = first * mm_t(grad_cat[:HALF], value_cat[:HALF])
            grad_second = second * mm_t(grad_cat[HALF:], value_cat)
            score_first = raw_first * first
            score_second = raw_second * second
            pull_first = grad_first * raw_first
            pull_second = grad_second * raw_second
            here = lanes == head
            rows_s[:HALF, :] = rows_s[:HALF, :] + jnp.where(
                here, jnp.sum(pull_first, axis=1, keepdims=True), 0.0
            )
            rows_s[HALF:, :] = rows_s[HALF:, :] + jnp.where(
                here, jnp.sum(pull_second, axis=1, keepdims=True), 0.0
            )
            low_cols = jnp.sum(pull_second, axis=0, keepdims=True)
            cols_s[pl.ds(head, 1), :HALF] = low_cols[:, :HALF] + jnp.sum(
                pull_first, axis=0, keepdims=True
            )
            cols_s[pl.ds(head, 1), HALF:] = low_cols[:, HALF:]
            grad_q.append(
                jnp.concatenate(
                    [
                        mm_near(grad_first, key_pair[:HALF], key_high[:HALF]),
                        mm_near(grad_second, key_pair, key_high),
                    ],
                    axis=0,
                )
            )

            def turned(source_t, block_first, block_second):
                high, low = split(source_t[e * HEAD_DIM : (e + 1) * HEAD_DIM, :])
                both = jnp.concatenate([high, low], axis=0)
                first_high, first_low = split(block_first)
                second_high, second_low = split(block_second)
                one = mm(both[:, :HALF], first_high)
                one = one[:HEAD_DIM] + one[HEAD_DIM:] + mm(high[:, :HALF], first_low)
                two = mm(both[:, HALF:], second_high)
                two = two[:HEAD_DIM] + two[HEAD_DIM:] + mm(high[:, HALF:], second_low)
                return jnp.concatenate([two[:, :HALF] + one, two[:, HALF:]], axis=1)

            grad_k.append(turned(query_t, grad_first, grad_second))
            grad_v.append(turned(grad_t, score_first, score_second))
        query_grad = jnp.where(lanes < HEAD_DIM, grad_q[0], grad_q[1]) * SCALE
        low[:, columns(p)] = query_grad.astype(bf16)
        low[:, columns(p, D)] = jnp.transpose(jnp.concatenate(grad_k, axis=0)).astype(bf16)
        dv_s[:ROWS, columns(p)] = jnp.transpose(jnp.concatenate(grad_v, axis=0))
        return carry

    for p in range(PAIRS):
        pair(p, 0)

    pulled = rows_s[...] - jnp.transpose(cols_s[...])
    high, middle, rest = split_three(pulled)
    upper_first = jnp.concatenate(
        [
            jnp.where(row_iota(HALF, HALF) <= lane_iota(HALF, HALF), 1.0, 0.0),
            jnp.full((HALF, HALF), 0.0, f32) + jnp.where(wide, 1.0, 0.0),
        ],
        axis=1,
    ).astype(bf16)
    upper_second = upper_first[:, :HALF]
    later = jnp.concatenate(
        [
            mm(upper_first, high) + mm(upper_first, middle) + mm(upper_first, rest),
            mm(upper_second, high[HALF:]) + mm(upper_second, middle[HALF:])
            + mm(upper_second, rest[HALF:]),
        ],
        axis=0,
    )
    grad_dp = later * (1.0 / 16.0) * sigmoid(-(k.dp()[...] + k.bd()))
    grad_bd = jnp.sum(grad_dp, axis=0, keepdims=True)
    low[:, QKVG:] = grad_dp.astype(bf16)

    dv_s[ROWS:, :] = jnp.zeros((8, D), f32)
    position = row_iota(ROWS, 1) & jnp.where(wide, ROWS - 1, HALF - 1)
    last = jnp.where(wide, ROWS - 1, HALF - 1)
    here = dv_s[0:ROWS, :]
    one = jnp.where(position <= last - 1, dv_s[1 : 1 + ROWS, :], 0.0)
    two = jnp.where(position <= last - 2, dv_s[2 : 2 + ROWS, :], 0.0)
    value = qkvg[:, 2 * D : 3 * D]
    low[:, 2 * D : 3 * D] = (k.ck(0) * here + k.ck(1) * one + k.ck(2) * two).astype(bf16)
    k.push("low")

    taps = [jnp.sum(rows * value, axis=0, keepdims=True) for rows in (here, one, two)]
    rest = jnp.concatenate([grad_bd, jnp.zeros((1, D - LANES), f32)], axis=1)
    k.sums[...] = jnp.concatenate([*taps, rest, jnp.zeros((4, D), f32)], axis=0)

    ordered_t = jnp.transpose(k.ordered()[...].astype(f32)).astype(bf16)
    gwo = k.gwo()
    gw = k.gw

    def weights(j, carry):
        part = pl.ds(pl.multiple_of(j * HALF, HALF), HALF)
        gw[:, part] = mm(ordered_t, low[:, part])
        return carry

    lax.fori_loop(0, QKVG // HALF, weights, 0)
    gw[:, QKVG : QKVG + D] = gwo[...]
    gw[:, QKVG + D :] = mm(ordered_t, low[:, QKVG:])

    def halves(j, carry):
        here = pl.ds(pl.multiple_of(j * HALF, HALF), HALF)
        keep = pl.ds(pl.multiple_of(j * HALF + k.section * GROUP, HALF), HALF)
        send = pl.ds(pl.multiple_of(j * HALF + (1 - k.section) * GROUP, HALF), HALF)
        k.gw_keep[:, here] = gw[:, keep]
        k.gw_send[:, here] = gw[:, send].astype(bf16)
        return carry

    lax.fori_loop(0, GROUP // HALF, halves, 0)


def second_layer_body(k):
    attn_forward_body(k)
    for name in ("ordered", "qkvg", "dp", "vc", "cum", "cumt", "o", "gated"):
        setattr(k, name, In(None, getattr(k, name)))
    ffn_backward_body(k)
    for name in ("branch_low", "gwo"):
        setattr(k, name, In(None, getattr(k, name)))
    k.sums = k.mixer_sums
    mixer_backward_body(k)


def input_backward_body(k):
    flip = k.layer == 1
    wide = k.wide
    gmod, mixed_s, perm_s = k.gmod, k.mixed_s, k.perm_s
    gmod[...] = jnp.zeros(gmod.shape, f32)
    low, w_qk, w_vgd = k.low(), k.w_qk(), k.w_vgd()

    def inner_grad(i, carry):
        rows = pl.ds(pl.multiple_of(i * HALF, HALF), HALF)
        mixed_s[rows, :] = mm_t(low[rows, : 2 * D], w_qk[...]) + mm_t(
            low[rows, 2 * D :], w_vgd[...]
        )
        return carry

    lax.fori_loop(0, 2, inner_grad, 0)
    if flip:
        high, middle, rest = split_three(mixed_s[...])
        perm_s[:, :D] = high
        perm_s[:, D : 2 * D] = middle
        perm_s[:, 2 * D :] = rest
    x, mid_grad = k.x(), k.mid_grad()
    k.mods()

    def tile(i, carry):
        start = i * HALF
        rows = pl.ds(start, HALF)
        slot = k.slot(i)
        if flip:
            three = mm(order_matrix(start, HALF, wide, False), perm_s[...])
            grad = three[:, :D] + three[:, D : 2 * D] + three[:, 2 * D :]
        else:
            grad = mixed_s[rows, :]
        normal, rate = normalise(x[rows, :].astype(f32))
        where = (pl.ds(slot, 1), slice(0, D))
        gmod[where] = gmod[where] + jnp.sum(grad, axis=0, keepdims=True)
        where = (pl.ds(slot, 1), slice(D, 2 * D))
        gmod[where] = gmod[where] + jnp.sum(grad * normal, axis=0, keepdims=True)
        total = mid_grad[rows, :] + normalise_back(normal, rate, grad * (1.0 + k.share(slot, 1)))
        k.gx[rows, :] = total
        k.gx_low[rows, :] = total.astype(bf16)
        return carry

    for i in range(2):
        tile(i, 0)
    k.push("gx_low")
    k.push("gx")
    ffn, mixer = k.ffn_sums(), k.mixer_sums()
    k.mod_low[...] = jnp.concatenate([gmod[...], ffn[...]], axis=1).astype(bf16)
    if k.layer == 0:
        first = k.section == 0
        k.gx_send[...] = jnp.where(first, k.gx_two()[...], k.gx[...])
        one, two = k.mod_low[...].astype(f32), k.mod_two()[...].astype(f32)
        k.mod_mine[...] = jnp.where(first, one, two).astype(bf16)
        k.mod_send[...] = jnp.where(first, two, one).astype(bf16)
    half = 2 * D
    rest = ffn[0:1, :] + ffn[1:2, :]
    k.sums[...] = jnp.concatenate(
        [
            gmod[0:1, :] + gmod[1:2, :],
            rest[:, :half],
            rest[:, half:],
            ffn[2:3, :half],
            ffn[2:3, half:],
            jnp.concatenate([ffn[3:4, :D], mixer[0:1, :]], axis=1),
            jnp.concatenate([mixer[1:2, :], mixer[2:3, :]], axis=1),
            jnp.concatenate([mixer[3:4, :], jnp.zeros((1, D), f32)], axis=1),
        ],
        axis=0,
    )


ANY = pl.BlockSpec(memory_space=pl.ANY)
VMEM = pl.BlockSpec(memory_space=pltpu.VMEM)
HBM = pl.BlockSpec(memory_space=pltpu.HBM)


def call(body, layer, layouts, ins, outs, scratch, flops, packed=None, after=()):
    arrays = []
    counts = []
    kept = []
    places = []
    for kind, given, part in ins.values():
        places.extend([ANY] * 2 if kind == "own" else [HBM])
        given = given if kind == "own" else (given,)
        arrays.extend(given)
        counts.append(len(given))
        rows, wide = given[0].shape[-2:]
        start, stop = part or (0, wide)
        kept.append(pltpu.VMEM((rows, stop - start), given[0].dtype))

    def kernel(*refs):
        refs = list(refs)
        take = lambda count: [refs.pop(0) for _ in range(count)]
        (layouts_ref,) = take(1)
        sources = [take(count) for count in counts]
        take(len(after))
        targets = take(len(outs))
        buffers = take(len(ins))
        results = take(len(outs))
        rest = take(len(scratch))
        in_sems, out_sems = refs
        k = Kernel(layer, layouts_ref)
        k.packed = packed
        for number, (name, (kind, _, part)) in enumerate(ins.items()):
            given = sources[number]
            if part is not None:
                given = [ref.at[:, part[0] : part[1]] for ref in given]
            setattr(k, name, k.load(kind, given, buffers[number], in_sems.at[number]))
        k.results = {}
        for number, name in enumerate(outs):
            setattr(k, name, results[number])
            k.results[name] = (results[number], targets[number], out_sems.at[number])
        for name, ref in zip(scratch, rest):
            setattr(k, name, ref)
        body(k)
        k.finish()

    return pl.pallas_call(
        kernel,
        out_shape=[jax.ShapeDtypeStruct(shape, kind) for shape, kind, _ in outs.values()],
        in_specs=[pl.BlockSpec(memory_space=pltpu.SMEM)] + places + [ANY] * len(after),
        out_specs=[HBM if for_kernel else ANY for _, _, for_kernel in outs.values()],
        scratch_shapes=kept
        + [pltpu.VMEM(shape, kind) for shape, kind, _ in outs.values()]
        + [pltpu.VMEM(shape, kind) for shape, kind in scratch.values()]
        + [pltpu.SemaphoreType.DMA((len(ins),)), pltpu.SemaphoreType.DMA((len(outs),))],
        compiler_params=pltpu.CompilerParams(vmem_limit_bytes=56 * 1024 * 1024),
        cost_estimate=pl.CostEstimate(flops=flops, bytes_accessed=4 << 20, transcendentals=0),
    )(layouts, *arrays, *after)


def own(pair, part=None):
    return ("own", pair, part)


def plain(array):
    return ("plain", array, None)


def micro(array):
    return ("micro", array, None)


AT_UP = (0, FF)
AT_OUT = (FF, FF + D)


def attn_forward(layer, layouts, x, mods, small, qk, vgd):
    return call(
        attn_forward_body,
        layer,
        layouts,
        dict(
            x=micro(x),
            mods=own(mods),
            w_qk=own(qk),
            w_vgd=own(vgd),
            small=own(small),
        ),
        dict(
            ordered=((ROWS, D), bf16, True),
            qkvg=((ROWS, QKVG), f32, True),
            dp=((ROWS, LANES), f32, True),
            vc=((ROWS, D), f32, True),
            cum=((ROWS, LANES), f32, True),
            cumt=((LANES, ROWS), f32, True),
            o=((ROWS, D), f32, True),
            gated=((ROWS, D), bf16, True),
        ),
        dict(
            inner=((ROWS, D), bf16),
            vpad=((ROWS + 8, D), f32),
            bias=((HALF, ROWS), f32),
        ),
        4 * 10**9,
    )


def ffn_forward(layer, layouts, x, mods, small, gated, upo, down):
    return call(
        ffn_forward_body,
        layer,
        layouts,
        dict(
            gated=plain(gated),
            x=micro(x),
            wo=own(upo, AT_OUT),
            mods=own(mods),
            small=own(small),
            wu=own(upo, AT_UP),
            wn=own(down),
        ),
        dict(
            out=((ROWS, D), bf16, True),
            branch=((ROWS, D), f32, True),
            down=((ROWS, D), f32, True),
        ),
        {},
        3 * 10**9,
    )


def ffn_backward(
    layer, layouts, x, mods, small, gated, branch, down_raw, grad, upo, down, devices, after=()
):
    shard = D // devices
    in_kernel = shard % 8 == 0
    if in_kernel:
        sums = dict(
            keep=((devices, shard, FF), f32, True),
            gone=((devices, shard, FF), bf16, False),
        )
    else:
        sums = dict(gwu=((D, FF), f32, False), gwn=((FF, D), f32, False))
    return call(
        ffn_backward_body,
        layer,
        layouts,
        dict(
            mods=own(mods),
            small=own(small),
            x=micro(x),
            **(
                dict(gated=plain(gated), wo=own(upo, AT_OUT))
                if layer == 1
                else dict(branch=plain(branch), down=plain(down_raw))
            ),
            grad=micro(grad),
            wu=own(upo, AT_UP),
            wn=own(down),
            **(dict(gated=plain(gated)) if layer == 0 else {}),
        ),
        dict(
            **(
                dict(out=((ROWS, D), bf16, True), sent=((ROWS, D), bf16, False))
                if layer == 1
                else {}
            ),
            mid_grad=((ROWS, D), f32, True),
            branch_low=((ROWS, D), bf16, True),
            gwo=((D, D), f32, True),
            sums=((8, FF), f32, True),
            **sums,
        ),
        dict(
            **({"gwn": ((FF, D), f32)} if in_kernel else {}),
            hidden_s=((ROWS, FF), bf16),
            inner_s=((ROWS, D), bf16),
            up_s=((ROWS, FF), bf16),
            down_s=((ROWS, D), bf16),
            gmod=((8, FF), f32),
            gbu=((1, FF), f32),
            gbn=((1, D), f32),
        ),
        5 * 10**9,
        packed=in_kernel,
        after=after,
    )


def second_layer(layouts, x, mods, small, grad, qk, vgd, upo, down, devices):
    shard = D // devices
    in_kernel = shard % 8 == 0
    if in_kernel:
        sums = dict(
            keep=((devices, shard, FF), f32, True),
            gone=((devices, shard, FF), bf16, False),
        )
    else:
        sums = dict(gwu=((D, FF), f32, False), gwn=((FF, D), f32, False))
    return call(
        second_layer_body,
        1,
        layouts,
        dict(
            x=micro(x),
            mods=own(mods),
            w_qk=own(qk),
            w_vgd=own(vgd),
            small=own(small),
            wo=own(upo, AT_OUT),
            grad=micro(grad),
            wu=own(upo, AT_UP),
            wn=own(down),
        ),
        dict(
            out=((ROWS, D), bf16, True),
            sent=((ROWS, D), bf16, False),
            mid_grad=((ROWS, D), f32, True),
            sums=((8, FF), f32, True),
            low=((ROWS, QKVG + LANES), bf16, True),
            gw_keep=((D, GROUP), f32, True),
            gw_send=((D, GROUP), bf16, False),
            mixer_sums=((8, D), f32, True),
            **sums,
        ),
        dict(
            ordered=((ROWS, D), bf16),
            qkvg=((ROWS, QKVG), f32),
            dp=((ROWS, LANES), f32),
            vc=((ROWS, D), f32),
            cum=((ROWS, LANES), f32),
            cumt=((LANES, ROWS), f32),
            o=((ROWS, D), f32),
            gated=((ROWS, D), bf16),
            inner=((ROWS, D), bf16),
            vpad=((ROWS + 8, D), f32),
            bias=((HALF, ROWS), f32),
            branch_low=((ROWS, D), bf16),
            gwo=((D, D), f32),
            **({"gwn": ((FF, D), f32)} if in_kernel else {}),
            hidden_s=((ROWS, FF), bf16),
            inner_s=((ROWS, D), bf16),
            up_s=((ROWS, FF), bf16),
            down_s=((ROWS, D), bf16),
            gmod=((8, FF), f32),
            gbu=((1, FF), f32),
            gbn=((1, D), f32),
            mixed_s=((ROWS, D), f32),
            dv_s=((ROWS + 8, D), f32),
            rows_s=((ROWS, LANES), f32),
            cols_s=((LANES, ROWS), f32),
            gw=((D, 2 * GROUP), f32),
        ),
        14 * 10**9,
        packed=in_kernel,
    )


def mixer_backward(layer, layouts, small, saved, branch_low, gwo, upo, after=()):
    ordered, qkvg, dp, vc, cum, cumt, o = saved
    return call(
        mixer_backward_body,
        layer,
        layouts,
        dict(
            branch_low=plain(branch_low),
            wo=own(upo, AT_OUT),
            qkvg=plain(qkvg),
            vc=plain(vc),
            cum=plain(cum),
            cumt=plain(cumt),
            o=plain(o),
            small=own(small),
            dp=plain(dp),
            ordered=plain(ordered),
            gwo=plain(gwo),
        ),
        dict(
            low=((ROWS, QKVG + LANES), bf16, True),
            gw_keep=((D, GROUP), f32, True),
            gw_send=((D, GROUP), bf16, False),
            sums=((8, D), f32, True),
        ),
        dict(
            mixed_s=((ROWS, D), f32),
            dv_s=((ROWS + 8, D), f32),
            rows_s=((ROWS, LANES), f32),
            cols_s=((LANES, ROWS), f32),
            bias=((HALF, ROWS), f32),
            gw=((D, 2 * GROUP), f32),
        ),
        7 * 10**9,
        after=after,
    )


def input_backward(
    layer, layouts, x, mods, low, mid_grad, ffn_sums, mixer_sums, qk, vgd, two=None, after=()
):
    extra_in, extra_out = {}, {}
    if two is not None:
        extra_in = dict(gx_two=plain(two[0]), mod_two=plain(two[1]))
        extra_out = dict(
            gx_send=((ROWS, D), f32, False),
            mod_mine=((8, 6 * D), bf16, False),
            mod_send=((8, 6 * D), bf16, False),
        )
    return call(
        input_backward_body,
        layer,
        layouts,
        dict(
            low=plain(low),
            w_qk=own(qk),
            w_vgd=own(vgd),
            x=micro(x),
            mid_grad=plain(mid_grad),
            mods=own(mods),
            ffn_sums=plain(ffn_sums),
            mixer_sums=plain(mixer_sums),
            **extra_in,
        ),
        dict(
            gx=((ROWS, D), f32, True),
            gx_low=((ROWS, D), bf16, True),
            mod_low=((8, 6 * D), bf16, True),
            sums=((8, 2 * D), f32, False),
            **extra_out,
        ),
        dict(
            mixed_s=((ROWS, D), f32),
            perm_s=((ROWS, 3 * D), bf16),
            gmod=((8, 2 * D), f32),
        ),
        2 * 10**9,
        after=after,
    )


def small_kernel(b_up, b_down, taps, b_decay, packed):
    packed[...] = jnp.zeros(packed.shape, f32)
    packed[0:1, :] = b_up[...]
    packed[1:2, :D] = b_down[...]
    packed[2:5, :D] = taps[0]
    packed[5:6, :HEADS] = b_decay[...]


def pack_small(b_up, b_down, taps, b_decay):
    return pl.pallas_call(
        small_kernel,
        out_shape=jax.ShapeDtypeStruct((8, FF), f32),
        in_specs=[VMEM] * 4,
        out_specs=VMEM,
        compiler_params=pltpu.CompilerParams(vmem_limit_bytes=8 * 1024 * 1024),
    )(b_up, b_down, taps, b_decay)


def pack_kernel(
    w_query, w_key, w_value, w_gate, w_out, w_decay, w_up, w_down, w_ada, conditions,
    qkuo, vgd, down, ada, lifted,
):
    qkuo[:, :D] = w_query[0]
    qkuo[:, D : 2 * D] = w_key[0]
    vgd[:, :D] = w_value[0]
    vgd[:, D : 2 * D] = w_gate[0]
    place = jnp.where(row_iota(HEADS, LANES) == lane_iota(HEADS, LANES), 1.0, 0.0).astype(bf16)
    turned = lax.dot_general(
        w_decay[0], place, (((0,), (0,)), ((), ())), preferred_element_type=f32
    )
    vgd[:, 2 * D :] = turned.astype(bf16)
    qkuo[:, 2 * D : 2 * D + FF] = w_up[0]
    qkuo[:, 2 * D + FF :] = w_out[0]
    down[...] = w_down[0]
    ada[...] = w_ada[0]
    values = jnp.concatenate([conditions[m].astype(f32) for m in range(MICRO)], axis=0)
    lifted[0] = (values * sigmoid(values)).astype(bf16)


def pack(*weights):
    shard = weights[0].shape[1]
    shapes = [(shard, width) for width in (3 * D + FF, 2 * D + LANES)]
    shapes += [weights[7].shape[1:], weights[8].shape[1:], (1, MICRO * SLOTS, D)]
    return pl.pallas_call(
        pack_kernel,
        out_shape=[jax.ShapeDtypeStruct(shape, bf16) for shape in shapes],
        in_specs=[VMEM] * len(weights),
        out_specs=[VMEM] * len(shapes),
    )(*weights)


def join_kernel(bits, waits, *refs):
    count = len(bits)
    held, came, out = refs[:count], refs[count : 2 * count], refs[2 * count + waits :]
    for i, bit in enumerate(bits):
        mine = (lax.axis_index("row") >> bit) & 1
        out[i][:, mine] = held[i][...]
        out[i][:, 1 - mine] = came[i][...]


def join(held, came, bits, after=()):
    def parts(array, bit):
        axis = axis_of(bit)
        above = 1
        for size in array.shape[:axis]:
            above *= size
        return array.reshape((above, -1) + array.shape[-2:])

    split_held = [parts(array, bit) for array, bit in zip(held, bits)]
    split_came = [parts(array, bit) for array, bit in zip(came, bits)]
    out = pl.pallas_call(
        functools.partial(join_kernel, bits, len(after)),
        out_shape=[
            jax.ShapeDtypeStruct(array.shape[:1] + (2,) + array.shape[1:], array.dtype)
            for array in split_held
        ],
        in_specs=[VMEM] * (2 * len(held)) + [ANY] * len(after),
        out_specs=[VMEM] * len(held),
        compiler_params=pltpu.CompilerParams(vmem_limit_bytes=8 * 1024 * 1024),
        cost_estimate=pl.CostEstimate(flops=10**6, bytes_accessed=10**6, transcendentals=0),
    )(*split_held, *split_came, *after)
    joined = []
    for array, result, bit in zip(held, out, bits):
        shape = list(array.shape)
        shape[axis_of(bit)] = 2
        joined.append(result.reshape(shape))
    return joined


def lifted_kernel(mine, came, ada, out, kept, sem):
    copy = pltpu.make_async_copy(ada, kept, sem)
    copy.start()
    first = lax.axis_index("section") == 0
    pair = mine[0:SLOTS, :].astype(f32), came[0:SLOTS, :].astype(f32)
    grad = jnp.concatenate(
        [jnp.where(first, pair[0], pair[1]), jnp.where(first, pair[1], pair[0])], axis=0
    ).astype(bf16)
    copy.wait()
    out[...] = mm_t(grad, kept[...])


def lifted_grads(mine, came, ada):
    return pl.pallas_call(
        lifted_kernel,
        out_shape=jax.ShapeDtypeStruct((MICRO * SLOTS, D), f32),
        in_specs=[VMEM, VMEM, ANY],
        out_specs=VMEM,
        scratch_shapes=[pltpu.VMEM((D, 6 * D), bf16), pltpu.SemaphoreType.DMA],
        compiler_params=pltpu.CompilerParams(vmem_limit_bytes=16 * 1024 * 1024),
        cost_estimate=pl.CostEstimate(flops=10**9, bytes_accessed=2 << 20, transcendentals=0),
    )(mine, came, ada)


def term_kernel(*refs):
    *terms, stays, goes = refs
    stays[...] = sum(ref[:, 0] for ref in terms)
    goes[...] = sum(ref[:, 1] for ref in terms)


def term_step(below, *terms):
    tail = terms[0].shape[1:]
    above = terms[0].shape[0] // (2 * below)
    shape = jax.ShapeDtypeStruct((above, below) + tail, f32)
    out = pl.pallas_call(
        term_kernel,
        out_shape=[shape] * 2,
        in_specs=[VMEM] * len(terms),
        out_specs=[VMEM] * 2,
        compiler_params=pltpu.CompilerParams(vmem_limit_bytes=8 * 1024 * 1024),
        cost_estimate=pl.CostEstimate(flops=10**6, bytes_accessed=10**6, transcendentals=0),
    )(*[term.reshape((above, 2, below) + tail) for term in terms])
    return [array.reshape((above * below,) + tail) for array in out]


def step_kernel(bit, widths, counts, waits, *refs):
    mine = (lax.axis_index("row") >> bit) & 1
    count, many = len(widths), len(counts)
    refs = list(refs)
    take = lambda number: [refs.pop(0) for _ in range(number)]
    sources = take(count + many)
    take(waits)
    targets = take(count + 1)
    buffers = take(count + many)
    results = take(count + 1)
    in_sems, out_sems = refs
    arrive = [
        pltpu.make_async_copy(source, buffer, in_sems.at[i])
        for i, (source, buffer) in enumerate(zip(sources, buffers))
    ]
    leave = [
        pltpu.make_async_copy(result, target, out_sems.at[i])
        for i, (result, target) in enumerate(zip(results, targets))
    ]
    for copy in arrive:
        copy.start()
    kept, came = buffers[:count], buffers[count:]
    places = [(j, i) for j, number in enumerate(counts) for i in range(number)]
    goes = results[count]
    at = 0
    for i in range(count):
        j, place = places[i]
        arrive[i].wait()
        if place == 0:
            arrive[count + j].wait()
        start = sum(widths[i - place : i])
        columns = slice(start, start + widths[i])
        total = kept[i][:, 1 - mine] + came[j][:, 1 - mine, :, :, columns].astype(f32)
        goes[:, :, :, at : at + widths[i]] = total.astype(bf16)
        at += widths[i]
    leave[count].start()
    for i in range(count):
        j, place = places[i]
        start = sum(widths[i - place : i])
        columns = slice(start, start + widths[i])
        results[i][...] = kept[i][:, mine] + came[j][:, mine, :, :, columns].astype(f32)
        leave[i].start()
    for copy in leave:
        copy.wait()


def step(kept, came, bit, below=1, after=()):
    blocks, rows = kept[0].shape[0] // 2, kept[0].shape[1]
    above = blocks // below
    paired = lambda array: array.reshape((above, 2, below) + array.shape[1:])
    widths = [array.shape[2] for array in kept]
    size = sum(array.size for array in kept)
    arrays = [paired(array) for array in kept] + [paired(array) for array, _ in came]
    shapes = [((above, below, rows, width), f32) for width in widths]
    shapes.append(((above, below, rows, sum(widths)), bf16))
    out = pl.pallas_call(
        functools.partial(step_kernel, bit, widths, [count for _, count in came], len(after)),
        out_shape=[jax.ShapeDtypeStruct(shape, kind) for shape, kind in shapes],
        in_specs=[HBM] * len(kept) + [ANY] * (len(came) + len(after)),
        out_specs=[HBM] * len(kept) + [ANY],
        scratch_shapes=[pltpu.VMEM(array.shape, array.dtype) for array in arrays]
        + [pltpu.VMEM(shape, kind) for shape, kind in shapes]
        + [pltpu.SemaphoreType.DMA((len(arrays),)), pltpu.SemaphoreType.DMA((len(shapes),))],
        compiler_params=pltpu.CompilerParams(vmem_limit_bytes=10 * 1024 * 1024),
        cost_estimate=pl.CostEstimate(flops=size, bytes_accessed=8 * size, transcendentals=0),
    )(*arrays, *after)
    count = len(kept)
    flat_blocks = [array.reshape((blocks,) + array.shape[2:]) for array in out]
    return flat_blocks[:count], flat_blocks[count]


def misc_step_kernel(held, arrived, out):
    size = held.shape[0] - SUMS
    out[:size, :] = held[:size, :]
    out[size : 2 * size, :] = arrived[:size, :]
    high, low = split(misc_sums(held, arrived))
    out[2 * size : 2 * size + SUMS // 2, :] = high
    out[2 * size + SUMS // 2 :, :] = low


def misc_step(held, arrived):
    return pl.pallas_call(
        misc_step_kernel,
        out_shape=jax.ShapeDtypeStruct((2 * held.shape[0] - SUMS, 2 * D), bf16),
        in_specs=[VMEM] * 2,
        out_specs=VMEM,
        compiler_params=pltpu.CompilerParams(vmem_limit_bytes=8 * 1024 * 1024),
        cost_estimate=pl.CostEstimate(flops=10**5, bytes_accessed=10**5, transcendentals=0),
    )(held, arrived)


def misc_sums(*refs):
    size = refs[0].shape[0] - SUMS
    parts = [ref[size:, :].astype(f32) for ref in refs]
    return sum(part[: SUMS // 2] + part[SUMS // 2 :] for part in parts)


SUMS = 32
OWN = 16


def misc_kernel(conditions, mod_one, mod_two, sums_one, sums_two, out):
    values = conditions[...].astype(f32)
    values = jnp.where(lax.axis_index("section") == 0, values[:SLOTS], values[SLOTS:])
    lifted = values * sigmoid(values)
    spare = [jnp.concatenate([lifted[0:1], lifted[1:2]], axis=1), jnp.zeros((1, 2 * D), f32)]
    rows = []
    for mod in (mod_one, mod_two):
        for slot in range(SLOTS):
            for i in range(3):
                part = mod[slot : slot + 1, i * 2 * D : (i + 1) * 2 * D]
                rows.append(part.astype(f32))
        rows.extend(spare)
    sums = jnp.concatenate([sums_one[...], sums_two[...]], axis=0)
    rows.extend(part.astype(f32) for part in split(sums))
    out[...] = jnp.concatenate(rows, axis=0).astype(bf16)


def pack_misc(conditions, mod_one, mod_two, sums_one, sums_two):
    return pl.pallas_call(
        misc_kernel,
        out_shape=jax.ShapeDtypeStruct((OWN + SUMS, 2 * D), bf16),
        in_specs=[VMEM] * 5,
        out_specs=VMEM,
        compiler_params=pltpu.CompilerParams(vmem_limit_bytes=8 * 1024 * 1024),
    )(conditions, mod_one, mod_two, sums_one, sums_two)


def finish_kernel(widths, counts, waits, *refs):
    count = len(widths)
    kept, refs = refs[:count], refs[count:]
    came, refs = refs[: len(counts)], refs[len(counts) :]
    parts = refs[:4]
    mine, other, small_mine, small_other = refs[4 + waits :]
    places = [(ref, i) for ref, many in zip(came, counts) for i in range(many)]
    added = []
    for i in range(count):
        ref, place = places[i]
        start = sum(widths[i - place : i])
        added.append(kept[i][0] + ref[0, :, start : start + widths[i]].astype(f32))
    a1, f1, f2, a2 = added
    size = parts[0].shape[0] - SUMS
    rows = jnp.concatenate([part[:size, :] for part in parts], axis=0)
    rows = rows.astype(f32).reshape(-1, OWN, 2 * D)
    shard = mine.shape[0]
    chosen = lane_iota(shard, D) == row_iota(shard, D) + lax.axis_index("row") * shard
    chosen = jnp.where(chosen, 1.0, 0.0).astype(bf16)
    features = [rows[:, 6, slot * D : (slot + 1) * D].astype(bf16) for slot in range(SLOTS)]
    lifted = jnp.concatenate([mm_t(chosen, part) for part in features], axis=1).astype(bf16)

    def ada(first):
        columns = []
        for i in range(3):
            both = [rows[:, first + 3 * slot + i, :] for slot in range(SLOTS)]
            columns.append(mm(lifted, jnp.concatenate(both, axis=0).astype(bf16)))
        return jnp.concatenate(columns, axis=1)

    first = lax.axis_index("section") == 0
    at = 0
    for one, two in ((a1, a2), (f1, f2), (ada(0), ada(OWN // 2))):
        columns = slice(at, at + one.shape[1])
        mine[:, columns] = jnp.where(first, one, two)
        other[:, columns] = jnp.where(first, two, one)
        at += one.shape[1]
    total = misc_sums(*parts)
    one, two = total[0:8, :], total[8:16, :]
    small_mine[...] = jnp.where(first, one, two)
    small_other[...] = jnp.where(first, two, one)


def finish(kept, came, parts, after):
    widths = [array.shape[2] for array in kept]
    shard = kept[0].shape[1]
    wide = GROUP + FF + 6 * D
    arrays = [array for array, _ in came]
    shapes = [(shard, wide)] * 2 + [(8, 2 * D)] * 2
    return pl.pallas_call(
        functools.partial(finish_kernel, widths, [count for _, count in came], len(after)),
        out_shape=[jax.ShapeDtypeStruct(shape, f32) for shape in shapes],
        in_specs=[VMEM] * (len(kept) + len(came) + 4) + [ANY] * len(after),
        out_specs=[VMEM] * 4,
        compiler_params=pltpu.CompilerParams(vmem_limit_bytes=8 * 1024 * 1024),
    )(*kept, *arrays, *parts, *after)


def output_kernel(mine, other, small_mine, small_other, *outs):
    first = lax.axis_index("section") == 0

    def halves(start, width):
        columns = slice(start, start + width)
        pair = mine[:, columns], other[:, columns]
        return jnp.where(first, pair[0], pair[1]), jnp.where(first, pair[1], pair[0])

    attn = halves(0, GROUP)
    cut = GROUP - 2 * D
    outs[0][...] = attn[0][:, :D]
    outs[1][...] = attn[0][:, D : 2 * D]
    outs[2][:, :cut] = attn[0][:, 2 * D :]
    outs[2][:, cut:] = attn[1][:, : D - cut]
    outs[3][...] = attn[1][:, D - cut : 2 * D - cut]
    outs[4][...] = attn[1][:, 2 * D - cut : 3 * D - cut]
    decay = jnp.transpose(attn[1][:, 3 * D - cut :])
    for head in range(HEADS):
        outs[5][head] = decay[head : head + 1, :]
    up = halves(GROUP, FF // 2)
    outs[6][:, : FF // 2] = up[0]
    outs[6][:, FF // 2 :] = up[1]
    for piece in range(2):
        down = halves(GROUP + FF // 2 + piece * D, D)
        outs[7][piece] = down[0]
        outs[7][2 + piece] = down[1]
    outs[8][...] = mine[:, GROUP + FF :] + other[:, GROUP + FF :]
    small = small_mine[...] + small_other[...]
    half = 2 * D
    for i in range(3):
        outs[9][:, i * half : (i + 1) * half] = small[i : i + 1, :]
    for i in range(2):
        outs[10][:, i * half : (i + 1) * half] = small[3 + i : 4 + i, :]
    outs[11][...] = small[5:6, :D]
    outs[12][0] = small[5:6, D:]
    outs[12][1] = small[6:7, :D]
    outs[12][2] = small[6:7, D:]
    outs[13][...] = small[7:8, :HEADS]


def outputs(mine, other, small_mine, small_other):
    shard = mine.shape[0]
    shapes = (
        [(shard, D)] * 5
        + [(HEADS, 1, shard), (shard, FF), (4, shard, D), (shard, 6 * D)]
        + [(1, 6 * D), (1, FF), (1, D), (3, 1, D), (1, HEADS)]
    )
    return pl.pallas_call(
        output_kernel,
        out_shape=[jax.ShapeDtypeStruct(shape, f32) for shape in shapes],
        in_specs=[VMEM] * 4,
        out_specs=[VMEM] * len(shapes),
        compiler_params=pltpu.CompilerParams(vmem_limit_bytes=8 * 1024 * 1024),
    )(mine, other, small_mine, small_other)


def both_kernel(one, two, came, out, mark, kept, sems):
    section = lax.axis_index("section")
    mark[...] = jnp.zeros(mark.shape, f32)

    def move(mine, layer):
        arrive = [
            pltpu.make_async_copy(mine, kept.at[layer], sems.at[0]),
            pltpu.make_async_copy(came, kept.at[1 - layer], sems.at[1]),
        ]
        leave = [
            pltpu.make_async_copy(kept.at[layer], out.at[layer], sems.at[2]),
            pltpu.make_async_copy(kept.at[1 - layer], out.at[1 - layer], sems.at[3]),
        ]
        for copy in arrive:
            copy.start()
        for copy, after in zip(arrive, leave):
            copy.wait()
            after.start()
        for copy in leave:
            copy.wait()

    @pl.when(section == 0)
    def _():
        move(one, 0)

    @pl.when(section == 1)
    def _():
        move(two, 1)


def both_micros(one, two, came):
    return pl.pallas_call(
        both_kernel,
        out_shape=[
            jax.ShapeDtypeStruct((MICRO,) + one.shape, one.dtype),
            jax.ShapeDtypeStruct((8, LANES), f32),
        ],
        in_specs=[ANY] * 3,
        out_specs=[ANY, VMEM],
        scratch_shapes=[
            pltpu.VMEM((MICRO,) + one.shape, one.dtype),
            pltpu.SemaphoreType.DMA((4,)),
        ],
        compiler_params=pltpu.CompilerParams(vmem_limit_bytes=8 * 1024 * 1024),
    )(one, two, came)


def swap(values):
    return lax.ppermute(values, "section", [(0, 1), (1, 0)])


def row_bits():
    bits = lax.axis_size("row").bit_length() - 1
    third = bits // 3
    return (
        tuple(range(third)),
        tuple(range(third, 2 * third)),
        tuple(range(2 * third, bits)),
    )


def across(values, flips):
    size = lax.axis_size("row")
    return lax.ppermute(values, "row", [(i, i ^ flips) for i in range(size)])


def partner(values, bit):
    return across(values, 1 << bit)


def axis_of(bit):
    return lax.axis_size("row").bit_length() - 2 - bit


def bit_of(bit):
    return (lax.axis_index("row") >> bit) & 1


def single(values):
    return values.reshape((1,) * (lax.axis_size("row").bit_length() - 1) + values.shape)


def gather_steps(along_x, along_y, along_z):
    steps = [(bit, bit) for bit in reversed(along_z)]
    return steps + list(zip(along_x + along_y, along_y + along_x))


def flat(held):
    return held.reshape(-1, held.shape[-1])


def lock(*arrays):
    return lax.optimization_barrier(arrays)


def on_device(
    tokens, conditions, output_grad, layouts,
    w_ada, b_ada, w_query, w_key, w_value, w_gate, w_out, w_decay, b_decay, conv_kernel,
    w_up, b_up, w_down, b_down,
):
    section = lax.axis_index("section")
    devices = lax.axis_size("row")
    shard = w_query.shape[1]
    along_x, along_y, along_z = row_bits()

    def both(values):
        return values, swap(values)

    qkuo, vgd, down, ada, lifted = pack(
        w_query, w_key, w_value, w_gate, w_out, w_decay.transpose(0, 2, 1), w_up, w_down, w_ada,
        conditions,
    )
    small = pack_small(b_up, b_down, conv_kernel, b_decay)
    conds = conditions.reshape(MICRO * SLOTS, D)
    steps = gather_steps(along_x, along_y, along_z)
    lag = len(along_z)
    plane = along_x + along_y
    bounds = [len(plane) * i // lag for i in range(lag + 1)]
    held = [single(array) for array in (qkuo, vgd, down)]
    ada = single(ada)
    for place, pair in enumerate(steps):
        bits = pair + pair[1:]
        if place == len(steps) - 1:
            bits = pair + pair
            held = [held[0][..., : 2 * D], held[1], held[0][..., 2 * D :], held[2]]
        came = [partner(array, bit) for array, bit in zip(held, bits)]
        after = ()
        if place < lag:
            lifted = jnp.concatenate([lifted, partner(lifted, pair[0])], axis=0)
            for bit in plane[bounds[place] : bounds[place + 1]]:
                (ada,) = join([ada], [partner(ada, bit)], (bit,))
            after = (small, lifted, ada)
        if place == lag:
            left = list(reversed(along_z))
            rows = D >> lag
            line = (lax.axis_index("row") >> len(plane)) * rows
            lifted = lax.dynamic_slice_in_dim(lifted, line, rows, 2)
            product = mm(lifted.reshape(-1, rows), flat(ada))
            terms = (product.reshape(1 << lag, MICRO * SLOTS, 6 * D),)
            for bit in along_z:
                stays, goes = term_step(1 << left.index(bit), *terms)
                left.remove(bit)
                terms = (stays, partner(goes, bit))
            after = (terms[1],)
        if place < len(steps) - 1:
            held = join(held, came, bits, after)
        else:
            qk, vgd = [both(flat(array)) for array in join(held[:2], came[:2], bits[:2])]
            mods = both(sum(term[0] for term in terms) + b_ada[0])
            smalls = both(small)
            x = tokens
            *saved, gated = attn_forward(0, layouts, x, mods, smalls, qk, vgd)
            held = join(held[2:], came[2:], bits[2:], (gated,))
    upo, down = [both(flat(array)) for array in held]
    out_one, branch, down_raw = ffn_forward(0, layouts, x, mods, smalls, gated, upo, down)
    kept = [(x, saved, gated, branch, down_raw)]
    x = out_one[None]
    kept.append((x,))

    late, _ = lock(w_ada[0], out_one)
    ada_all = lax.all_gather(late, "row", axis=0, tiled=True)

    def halved(terms):
        if terms[0].ndim == 2:
            up_sum = terms[0].reshape(devices, shard, 2, FF // 2)
            down_sum = terms[1].reshape(devices, 2, 2, shard, D)
            terms = []
            for own in (section, 1 - section):
                up_half = lax.dynamic_index_in_dim(up_sum, own, 2, keepdims=False)
                down_half = lax.dynamic_index_in_dim(down_sum, own, 1, keepdims=False)
                terms.append(
                    jnp.concatenate([up_half, down_half[:, 0], down_half[:, 1]], axis=2)
                )
            terms[1] = terms[1].astype(bf16)
        return terms

    def by_row(array):
        return array.reshape(devices, shard, GROUP)

    def input_step(l, low, mid_grad, ffn_sums, mixer_sums, two=None, after=()):
        x = kept[l][0]
        return input_backward(
            l, layouts, x, mods, low, mid_grad, ffn_sums, mixer_sums, qk, vgd, two, after
        )

    def run(keep, came, bits, below=1, after=()):
        for bit in bits[:-1]:
            keep, sent = step(keep, came, bit, below, after)
            came = [(partner(sent, bit), len(keep))]
        return step(keep, came, bits[-1], below, after)

    def grown(mod, bits):
        for bit in bits:
            mod = misc_step(mod, partner(mod, bit))
        return mod

    x_bits, y_bits, z_bits = along_x, along_y, along_z
    (
        out_two, acts_sent, mid_grad, f2_sums, low, a2_keep, a2_sent, m2_sums, *terms
    ) = second_layer(
        layouts, x, mods, smalls, output_grad, qk, vgd, upo, down, devices
    )
    f2_keep, f2_sent = halved(terms)
    a2_keep, a2_sent = by_row(a2_keep), by_row(a2_sent)
    low, f2_sent, a2_sent, acts_sent = lock(low, f2_sent, a2_sent, acts_sent)
    f2_came = swap(f2_sent)
    a2_came = swap(a2_sent)
    acts_came = swap(acts_sent)
    gx_two, grad, mod_low_two, sums_two = input_step(1, low, mid_grad, f2_sums, m2_sums)
    grad, f2_came, a2_came, acts_came = lock(grad, f2_came, a2_came, acts_came)
    f2_keep, f2_sent = run([f2_keep], [(f2_came, 1)], x_bits)
    a2_keep, a2_sent = run([a2_keep], [(a2_came, 1)], y_bits, 1 << len(x_bits))
    grad, f2_sent, a2_sent = lock(grad, f2_sent, a2_sent)
    f2_came = partner(f2_sent, x_bits[-1])
    a2_came = partner(a2_sent, y_bits[-1])

    x, saved, gated, branch, down_raw = kept[0]
    mid_grad, branch_low, gwo, f1_sums, *terms = ffn_backward(
        0, layouts, x, mods, smalls, gated, branch, down_raw, grad[None], upo, down, devices
    )
    f1_keep, f1_sent = halved(terms)
    carried = (branch_low, gwo)
    *carried, f1_sent, f2_came, a2_came = lock(*carried, f1_sent, f2_came, a2_came)
    f1_came = swap(f1_sent)
    f2_keep, f2_sent = run(f2_keep, [(f2_came, 1)], y_bits)
    a2_keep, a2_sent = run(a2_keep, [(a2_came, 1)], x_bits)
    f1_keep, f1_sent = run([f1_keep], [(f1_came, 1)], x_bits)
    *carried, f2_sent, a2_sent, f1_sent = lock(*carried, f2_sent, a2_sent, f1_sent)
    f1_came = partner(f1_sent, x_bits[-1])
    a2_came = partner(a2_sent, x_bits[-1])
    f2_came = partner(f2_sent, y_bits[-1])
    low, a1_keep, a1_sent, m1_sums = mixer_backward(0, layouts, smalls, saved, *carried, upo)
    a1_keep, a1_sent = by_row(a1_keep), by_row(a1_sent)
    low, a1_sent, f2_came, a2_came, f1_came, ada_all = lock(
        low, a1_sent, f2_came, a2_came, f1_came, ada_all
    )
    a1_came = swap(a1_sent)
    two_keep, two_sent = run(f2_keep + a2_keep, [(f2_came, 1), (a2_came, 1)], z_bits[:1])
    f1_keep, f1_sent = run(f1_keep, [(f1_came, 1)], y_bits)
    a1_keep, a1_sent = run([a1_keep], [(a1_came, 1)], x_bits)
    low, two_sent, f1_sent, a1_sent = lock(low, two_sent, f1_sent, a1_sent)
    a1_came = partner(a1_sent, x_bits[-1])
    f1_came = partner(f1_sent, y_bits[-1])
    two_came = partner(two_sent, z_bits[0])
    gx_one, _, mod_low_one, sums_one, gx_sent, mod_mine, mod_sent = input_step(
        0, low, mid_grad, f1_sums, m1_sums, (gx_two, mod_low_two)
    )
    misc = pack_misc(conds, mod_low_one, mod_low_two, sums_one, sums_two)
    misc, a1_came, two_came, f1_came, gx_sent, mod_sent = lock(
        misc, a1_came, two_came, f1_came, gx_sent, mod_sent
    )

    a1_keep, a1_sent = run(a1_keep, [(a1_came, 1)], y_bits)
    a1_sent, misc = lock(a1_sent, misc)
    a1_came = partner(a1_sent, y_bits[-1])
    misc = grown(misc, tuple(reversed(z_bits))[:-1])
    gx_came = swap(gx_sent)
    mod_came = swap(mod_sent)
    keep, came = a1_keep + f1_keep, [(a1_came, 1), (f1_came, 1)]
    for place, bit in enumerate(z_bits):
        if place == 1:
            keep, came = keep + two_keep, came + [(two_came, 2)]
        keep, sent = step(keep, came, bit)
        if place == len(z_bits) - 1:
            sent, misc, gx_came, mod_came = lock(sent, misc, gx_came, mod_came)
        elif place == 0:
            sent, misc = lock(sent, misc)
        came = [(partner(sent, bit), len(keep))]
        if place == 0:
            misc = grown(misc, z_bits[:1] + x_bits[:-1] + y_bits[:-1])
    last = (1 << x_bits[-1], 1 << y_bits[-1])
    parts = [misc] + [across(misc, flips) for flips in (last[0], last[1], last[0] + last[1])]
    gx_out, gx_mark = both_micros(gx_one, gx_two, gx_came)
    acts_out, acts_mark = both_micros(out_one, out_two, acts_came)
    grad_lifted = lifted_grads(mod_mine, mod_came, ada_all)
    lifted_came = swap(grad_lifted)
    mine, other, small_mine, small_other = finish(
        keep, came, parts, (gx_mark, acts_mark, lifted_came)
    )
    came, small_came = swap(other), swap(small_other)
    (
        g_query, g_key, g_value, g_gate, g_out, g_decay, g_up, g_down, g_ada,
        g_b_ada, g_b_up, g_b_down, g_conv, g_b_decay,
    ) = outputs(mine, came, small_mine, small_came)

    grad_lifted = (grad_lifted + lifted_came).reshape(MICRO, SLOTS, D)
    _, pull_silu = jax.vjp(jax.nn.silu, conditions.astype(f32))
    (cond_grads,) = pull_silu(grad_lifted)

    return (
        acts_out[None],
        gx_out[None],
        cond_grads,
        g_ada[None],
        g_b_ada,
        g_query[None],
        g_key[None],
        g_value[None],
        g_gate[None],
        g_out[None],
        g_decay.transpose(1, 2, 0),
        g_b_decay,
        g_conv.transpose(1, 0, 2),
        g_up[None],
        g_b_up,
        g_down.reshape(1, FF // devices, D),
        g_b_down,
    )


def solution(mesh):
    rows = P(None, "row", None)
    mats = P("section", "row", None)
    vector = P("section", None)
    in_specs = (
        rows, rows, rows, P(None, "row"),
        mats, vector, mats, mats, mats, mats, mats, mats, vector, P("section", None, None),
        mats, vector, mats, vector,
    )
    blocks = P("section", None, "row", None)
    out_specs = (
        blocks, blocks, rows,
        mats, vector, mats, mats, mats, mats, mats, mats, vector, P("section", None, None),
        mats, vector, mats, vector,
    )
    return jax.shard_map(
        on_device, mesh=mesh, in_specs=in_specs, out_specs=out_specs, check_vma=False
    )
```

```python
import functools

import jax
import jax.numpy as jnp
from jax import lax
from jax.experimental import pallas as pl
from jax.experimental.pallas import tpu as pltpu
from jax.sharding import PartitionSpec as P

D = 384
HEADS = 6
HEAD_DIM = 64
FF = 1536
MICRO = 2
ROWS = 512
HALF = 256
SLOTS = 2
PAIR = 128
PAIRS = D // PAIR
QKVG = 4 * D
LANES = 128
GROUP = (QKVG + D + LANES) // 2
NEG = -1e30
SCALE = HEAD_DIM**-0.5

bf16 = jnp.bfloat16
f32 = jnp.float32


def mm(left, right):
    return jnp.dot(left, right, preferred_element_type=f32)


def mm_t(left, right):
    return lax.dot_general(left, right, (((1,), (1,)), ((), ())), preferred_element_type=f32)


def split(values):
    high = values.astype(bf16)
    return high, (values - high.astype(f32)).astype(bf16)


def split_three(values):
    high, rest = split(values)
    mid = values - high.astype(f32)
    middle, low = split(mid)
    return high, middle, low


def cat_left(values):
    high, low = split(values)
    return jnp.concatenate([high, low, high], axis=1)


def cat_right(values):
    high, low = split(values)
    return jnp.concatenate([high, high, low], axis=1)


def mm_near(left, right_pair, right_high):
    high, low = split(left)
    wide = mm(high, right_pair)
    return wide[:, :PAIR] + wide[:, PAIR:] + mm(low, right_high)


def lane_iota(rows, columns):
    return lax.broadcasted_iota(jnp.int32, (rows, columns), 1)


def row_iota(rows, columns):
    return lax.broadcasted_iota(jnp.int32, (rows, columns), 0)


def order_matrix(start, rows, wide, to_scan):
    t = row_iota(rows, ROWS) + start
    small = (t & 256) + ((t & 15) << 4) + ((t & 255) >> 4)
    if to_scan:
        large = ((t & 15) << 5) + (t >> 4)
    else:
        large = ((t & 31) << 4) + (t >> 5)
    source = jnp.where(wide, large, small)
    return jnp.where(lane_iota(rows, ROWS) == source, 1.0, 0.0).astype(bf16)


def normalise(values):
    centred = values - jnp.mean(values, axis=-1, keepdims=True)
    rate = lax.rsqrt(jnp.mean(centred * centred, axis=-1, keepdims=True) + 1e-06)
    return centred * rate, rate


def normalise_back(normal, rate, grad):
    return rate * (
        grad
        - jnp.mean(grad, axis=-1, keepdims=True)
        - normal * jnp.mean(grad * normal, axis=-1, keepdims=True)
    )


class In:
    def __init__(self, copy, kept):
        self.copy = copy
        self.kept = kept

    def __call__(self):
        if self.copy is not None:
            self.copy.wait()
            self.copy = None
        return self.kept


class Kernel:
    def __init__(self, layer, layouts):
        self.layer = layer
        self.section = lax.axis_index("section")
        self.own = self.section == layer
        self.layout = layouts[self.section, 0]
        self.wide = self.layout == 0
        self.live_rows = jnp.where(self.wide, ROWS, self.layout * HALF)
        self.pushed = {}

    def load(self, kind, refs, kept, sem):
        if kind == "own":
            mine, other = refs

            @pl.when(self.own)
            def _():
                pltpu.make_async_copy(mine, kept, sem).start()

            @pl.when(jnp.logical_not(self.own))
            def _():
                pltpu.make_async_copy(other, kept, sem).start()

            return In(pltpu.make_async_copy(mine, kept, sem), kept)
        (source,) = refs
        if kind == "micro":
            source = source.at[self.section if source.shape[0] == MICRO else 0]
        copy = pltpu.make_async_copy(source, kept, sem)
        copy.start()
        return In(copy, kept)

    def push(self, name):
        if name not in self.results:
            return
        kept, target, sem = self.results[name]
        copy = pltpu.make_async_copy(kept, target, sem)
        copy.start()
        self.pushed[name] = copy

    def finish(self):
        for name in self.results:
            if name not in self.pushed:
                self.push(name)
        for copy in self.pushed.values():
            copy.wait()

    def slot(self, half):
        return jnp.where(self.wide, 0, half)

    def share(self, slot, part):
        row = pl.ds(2 * self.section + slot, 1)
        return self.mods()[row, part * D : (part + 1) * D]

    def bu(self):
        return self.small()[0:1, :]

    def bn(self):
        return self.small()[1:2, :D]

    def ck(self, tap):
        return self.small()[2 + tap : 3 + tap, :D]

    def bd(self):
        return self.small()[5:6, :LANES]


def sigmoid(values):
    return 1.0 / (1.0 + jnp.exp(-values))


GELU_A = 0.7978845608028654
GELU_B = 0.044715


def gelu_parts(values):
    square = values * values
    tanh = jnp.tanh(GELU_A * values * (1.0 + GELU_B * square))
    return square, tanh


def fill_bias(bias, wide):
    bias[:, :HALF] = jnp.full((HALF, HALF), 0.0, f32) + jnp.where(wide, 0.0, NEG)
    causal = row_iota(HALF, HALF) >= lane_iota(HALF, HALF)
    bias[:, HALF:] = jnp.where(causal, 0.0, NEG)


def decay_factors(cum, cumt, bias, head):
    row = cumt[pl.ds(head, 1), :]
    lanes = lane_iota(1, LANES)
    column = jnp.sum(jnp.where(lanes == head, cum[...], 0.0), axis=1, keepdims=True)
    first = jnp.exp(column[:HALF] - row[:, :HALF] + bias[:, HALF:])
    second = jnp.exp(column[HALF:] - row + bias[...])
    return first, second


def head_norm(values, lanes):
    square = values * values
    low = jnp.sum(jnp.where(lanes < HEAD_DIM, square, 0.0), axis=1, keepdims=True)
    high = jnp.sum(jnp.where(lanes < HEAD_DIM, 0.0, square), axis=1, keepdims=True)
    return jnp.where(lanes < HEAD_DIM, low, high) * (1.0 / HEAD_DIM)


def fill_decay(dp, bd, cum, cumt):
    raw = dp[...] + bd
    log_decay = (jnp.minimum(raw, 0.0) - jnp.log1p(jnp.exp(-jnp.abs(raw)))) * (1.0 / 16.0)
    high, middle, low = split_three(log_decay)
    causal = jnp.where(row_iota(ROWS, ROWS) >= lane_iota(ROWS, ROWS), 1.0, 0.0).astype(bf16)
    cum[...] = mm(causal, high) + mm(causal, middle) + mm(causal, low)
    cumt[...] = jnp.transpose(cum[...])


def columns(index, first=0):
    return slice(index * PAIR + first, index * PAIR + first + PAIR)


def attn_forward_body(k):
    flip = k.layer == 1
    wide = k.wide
    x = k.x()
    k.mods()

    def first(i, carry):
        rows = pl.ds(pl.multiple_of(i * HALF, HALF), HALF)
        slot = k.slot(i)
        normal, _ = normalise(x[rows, :].astype(f32))
        k.inner[rows, :] = (normal * (1.0 + k.share(slot, 1)) + k.share(slot, 0)).astype(bf16)
        return carry

    lax.fori_loop(0, 2, first, 0)
    w_qk = k.w_qk()
    w_vgd = k.w_vgd()

    def project(i, carry):
        start = i * HALF
        rows = pl.ds(start, HALF)
        if flip:
            part = mm(order_matrix(start, HALF, wide, True), k.inner[...]).astype(bf16)
        else:
            part = k.inner[rows, :]
        k.ordered[rows, :] = part
        k.qkvg[rows, : 2 * D] = mm(part, w_qk[...])
        k.qkvg[rows, 2 * D :] = mm(part, w_vgd[:, : 2 * D])
        k.dp[rows, :] = mm(part, w_vgd[:, 2 * D :])
        return carry

    lax.fori_loop(0, 2, project, 0)
    k.small()
    for name in ("ordered", "qkvg", "dp"):
        k.push(name)
    fill_decay(k.dp, k.bd(), k.cum, k.cumt)
    fill_bias(k.bias, wide)

    vpad = k.vpad
    vpad[0:8, :] = jnp.zeros((8, D), f32)
    vpad[8 : 8 + ROWS, :] = k.qkvg[:, 2 * D : 3 * D]
    position = row_iota(ROWS, 1) & jnp.where(wide, ROWS - 1, HALF - 1)
    one = jnp.where(position >= 1, vpad[7 : 7 + ROWS, :], 0.0)
    two = jnp.where(position >= 2, vpad[6 : 6 + ROWS, :], 0.0)
    k.vc[...] = k.ck(0) * vpad[8 : 8 + ROWS, :] + k.ck(1) * one + k.ck(2) * two
    for name in ("cum", "cumt", "vc"):
        k.push(name)

    def pair(p, carry):
        lanes = lane_iota(1, PAIR)
        queries = cat_left(k.qkvg[:, columns(p)] * SCALE)
        keys = k.qkvg[:, columns(p, D)]
        value_high, value_low = split(k.vc[:, columns(p)])
        values = jnp.concatenate([value_high, value_low], axis=1)
        parts = []
        for e in range(2):
            key_cat = cat_right(jnp.where((lanes // HEAD_DIM) == e, keys, 0.0))
            first, second = decay_factors(k.cum, k.cumt, k.bias, 2 * p + e)
            first = first * mm_t(queries[:HALF], key_cat[:HALF])
            second = second * mm_t(queries[HALF:], key_cat)
            parts.append(
                jnp.concatenate(
                    [
                        mm_near(first, values[:HALF], value_high[:HALF]),
                        mm_near(second, values, value_high),
                    ],
                    axis=0,
                )
            )
        total = jnp.where(lanes < HEAD_DIM, parts[0], parts[1])
        k.o[:, columns(p)] = total
        gate = k.qkvg[:, columns(p, 3 * D)]
        normed = total * lax.rsqrt(head_norm(total, lanes) + 1.0)
        mixed = (normed * (gate * sigmoid(gate))).astype(bf16)
        if flip:
            k.inner[:, columns(p)] = mixed
        else:
            k.gated[:, columns(p)] = mixed
        return carry

    for p in range(PAIRS):
        pair(p, 0)
    k.push("o")
    if flip:

        def back(i, carry):
            start = i * HALF
            k.gated[pl.ds(start, HALF), :] = mm(
                order_matrix(start, HALF, wide, False), k.inner[...]
            ).astype(bf16)
            return carry

        lax.fori_loop(0, 2, back, 0)


def ffn_forward_body(k):
    gated, x = k.gated(), k.x()
    k.mods(), k.small()

    def tile(i, carry):
        start = i * HALF
        rows = pl.ds(start, HALF)
        slot = k.slot(i)
        grown = mm(gated[rows, :], k.wo()[...])
        k.branch[rows, :] = grown
        middle = x[rows, :].astype(f32) + k.share(slot, 2) * grown
        normal, _ = normalise(middle)
        inner = (normal * (1.0 + k.share(slot, 4)) + k.share(slot, 3)).astype(bf16)
        up = mm(inner, k.wu()[...]) + k.bu()
        _, tanh = gelu_parts(up)
        hidden = (0.5 * up * (1.0 + tanh)).astype(bf16)
        low = mm(hidden, k.wn()[...])
        k.down[rows, :] = low
        result = middle + k.share(slot, 5) * (low + k.bn())
        live = (row_iota(HALF, 1) + start) < k.live_rows
        k.out[rows, :] = jnp.where(live, result, 0.0).astype(bf16)
        return carry

    for i in range(2):
        tile(i, 0)


def ffn_backward_body(k):
    gmod, gbu, gbn = k.gmod, k.gbu, k.gbn
    gmod[...] = jnp.zeros(gmod.shape, f32)
    gbu[...] = jnp.zeros(gbu.shape, f32)
    gbn[...] = jnp.zeros(gbn.shape, f32)
    both_ways = k.layer == 1
    k.mods(), k.small()
    x, grad = k.x(), k.grad()
    if both_ways:
        gated, wo = k.gated(), k.wo()
    else:
        branch, down = k.branch(), k.down()

    def tile(i, carry):
        start = i * HALF
        rows = pl.ds(start, HALF)
        slot = k.slot(i)

        def add(part, values):
            where = (pl.ds(slot, 1), slice((part - 2) * D, (part - 1) * D))
            gmod[where] = gmod[where] + jnp.sum(values, axis=0, keepdims=True)

        grown = mm(gated[rows, :], wo[...]) if both_ways else branch[rows, :]
        middle = x[rows, :].astype(f32) + k.share(slot, 2) * grown
        normal, rate = normalise(middle)
        inner = (normal * (1.0 + k.share(slot, 4)) + k.share(slot, 3)).astype(bf16)
        k.inner_s[rows, :] = inner
        up = mm(inner, k.wu()[...]) + k.bu()
        square, tanh = gelu_parts(up)
        half = 0.5 * (1.0 + tanh)
        hidden = (up * half).astype(bf16)
        k.hidden_s[rows, :] = hidden
        lower = (mm(hidden, k.wn()[...]) if both_ways else down[rows, :]) + k.bn()
        live = (row_iota(HALF, 1) + start) < k.live_rows
        if both_ways:
            result = middle + k.share(slot, 5) * lower
            k.out[rows, :] = jnp.where(live, result, 0.0).astype(bf16)
        above = jnp.where(live, grad[rows, :].astype(f32), 0.0)
        add(5, above * lower)
        grad_down = above * k.share(slot, 5)
        gbn[...] = gbn[...] + jnp.sum(grad_down, axis=0, keepdims=True)
        down_low = grad_down.astype(bf16)
        k.down_s[rows, :] = down_low
        slope = half + 0.5 * up * (1.0 - tanh * tanh) * (
            GELU_A * (1.0 + 3.0 * GELU_B * square)
        )
        grad_up = mm_t(down_low, k.wn()[...]) * slope
        gbu[...] = gbu[...] + jnp.sum(grad_up, axis=0, keepdims=True)
        up_low = grad_up.astype(bf16)
        k.up_s[rows, :] = up_low
        grad_inner = mm_t(up_low, k.wu()[...])
        add(3, grad_inner)
        add(4, grad_inner * normal)
        grad_middle = above + normalise_back(
            normal, rate, grad_inner * (1.0 + k.share(slot, 4))
        )
        k.mid_grad[rows, :] = grad_middle
        add(2, grad_middle * grown)
        k.branch_low[rows, :] = (grad_middle * k.share(slot, 2)).astype(bf16)
        return carry

    for i in range(2):
        tile(i, 0)
    k.push("mid_grad")
    k.push("branch_low")
    if both_ways:
        own = k.section == 0
        k.sent[...] = jnp.where(own, k.out[...].astype(f32), x[...].astype(f32)).astype(bf16)
        k.push("out")
        k.push("sent")

    def weights(j, carry):
        part = pl.ds(pl.multiple_of(j * HALF, HALF), HALF)
        hidden_t = jnp.transpose(k.hidden_s[:, part].astype(f32)).astype(bf16)
        k.gwn[part, :] = mm(hidden_t, k.down_s[...])
        return carry

    lax.fori_loop(0, FF // HALF, weights, 0)
    inner_t = jnp.transpose(k.inner_s[...].astype(f32)).astype(bf16)
    if k.packed:
        devices, shard, _ = k.keep.shape

        def halves(j, carry):
            for kept, own in ((k.keep, c_section), (k.gone, 1 - c_section)):
                columns = pl.ds(pl.multiple_of(j * HALF + own * (FF // 2), HALF), HALF)
                here = pl.ds(pl.multiple_of(j * HALF, HALF), HALF)
                part = mm(inner_t, k.up_s[:, columns]).reshape(devices, shard, HALF)
                kept[:, :, here] = part.astype(kept.dtype)
            return carry

        c_section = k.section
        lax.fori_loop(0, FF // 2 // HALF, halves, 0)

        def owner(r, carry):
            for kept, own in ((k.keep, c_section), (k.gone, 1 - c_section)):
                for piece in range(2):
                    start = pl.multiple_of((4 * r + 2 * own + piece) * shard, 8)
                    rows = k.gwn[pl.ds(start, shard), :]
                    at = FF // 2 + piece * D
                    kept[r, :, at : at + D] = rows.astype(kept.dtype)
            return carry

        lax.fori_loop(0, devices, owner, 0)
        k.push("keep")
        k.push("gone")
    else:
        k.gwu[...] = mm(inner_t, k.up_s[...])
    gated = k.gated()
    k.gwo[...] = mm(jnp.transpose(gated[...].astype(f32)).astype(bf16), k.branch_low[...])

    short = jnp.concatenate([gbn[...], jnp.zeros((1, FF - D), f32)], axis=1)
    k.sums[...] = jnp.concatenate(
        [gmod[0:SLOTS, :], gbu[...], short, jnp.zeros((4, FF), f32)], axis=0
    )


def mixer_backward_body(k):
    flip = k.layer == 1
    wide = k.wide
    mixed_s, low, dv_s, rows_s, cols_s = k.mixed_s, k.low, k.dv_s, k.rows_s, k.cols_s
    fill_bias(k.bias, wide)
    branch_low, wo = k.branch_low(), k.wo()

    def first(i, carry):
        start = i * HALF
        rows = pl.ds(start, HALF)
        if flip:
            part = mm(order_matrix(start, HALF, wide, True), branch_low[...]).astype(bf16)
        else:
            part = branch_low[rows, :]
        mixed_s[rows, :] = mm_t(part, wo[...])
        return carry

    lax.fori_loop(0, 2, first, 0)
    rows_s[...] = jnp.zeros(rows_s.shape, f32)
    cols_s[...] = jnp.zeros(cols_s.shape, f32)
    qkvg, vc, cum, cumt, o = k.qkvg(), k.vc(), k.cum(), k.cumt(), k.o()
    k.small()

    def pair(p, carry):
        lanes = lane_iota(1, PAIR)
        total = o[:, columns(p)]
        gate = qkvg[:, columns(p, 3 * D)]
        above = mixed_s[:, columns(p)]
        rate = lax.rsqrt(head_norm(total, lanes) + 1.0)
        sig = sigmoid(gate)
        grad_gate = above * (total * rate) * (sig * (1.0 + gate * (1.0 - sig)))
        low[:, columns(p, 3 * D)] = grad_gate.astype(bf16)
        grad_normed = above * (gate * sig)
        product = grad_normed * total
        inside = jnp.where(
            lanes < HEAD_DIM,
            jnp.sum(jnp.where(lanes < HEAD_DIM, product, 0.0), axis=1, keepdims=True),
            jnp.sum(jnp.where(lanes < HEAD_DIM, 0.0, product), axis=1, keepdims=True),
        ) * (1.0 / HEAD_DIM)
        grad_o = rate * grad_normed - total * (rate * rate * rate) * inside

        queries = qkvg[:, columns(p)] * SCALE
        keys = qkvg[:, columns(p, D)]
        values = vc[:, columns(p)]
        query_cat = cat_left(queries)
        grad_cat = cat_left(grad_o)
        key_high, key_low = split(keys)
        key_pair = jnp.concatenate([key_high, key_low], axis=1)
        query_t = jnp.transpose(queries)
        grad_t = jnp.transpose(grad_o)
        grad_q = []
        grad_k = []
        grad_v = []
        for e in range(2):
            mine = (lanes // HEAD_DIM) == e
            head = 2 * p + e
            key_cat = cat_right(jnp.where(mine, keys, 0.0))
            value_cat = cat_right(jnp.where(mine, values, 0.0))
            first, second = decay_factors(cum, cumt, k.bias, head)
            raw_first = mm_t(query_cat[:HALF], key_cat[:HALF])
            raw_second = mm_t(query_cat[HALF:], key_cat)
            grad_first = first * mm_t(grad_cat[:HALF], value_cat[:HALF])
            grad_second = second * mm_t(grad_cat[HALF:], value_cat)
            score_first = raw_first * first
            score_second = raw_second * second
            pull_first = grad_first * raw_first
            pull_second = grad_second * raw_second
            here = lanes == head
            rows_s[:HALF, :] = rows_s[:HALF, :] + jnp.where(
                here, jnp.sum(pull_first, axis=1, keepdims=True), 0.0
            )
            rows_s[HALF:, :] = rows_s[HALF:, :] + jnp.where(
                here, jnp.sum(pull_second, axis=1, keepdims=True), 0.0
            )
            low_cols = jnp.sum(pull_second, axis=0, keepdims=True)
            cols_s[pl.ds(head, 1), :HALF] = low_cols[:, :HALF] + jnp.sum(
                pull_first, axis=0, keepdims=True
            )
            cols_s[pl.ds(head, 1), HALF:] = low_cols[:, HALF:]
            grad_q.append(
                jnp.concatenate(
                    [
                        mm_near(grad_first, key_pair[:HALF], key_high[:HALF]),
                        mm_near(grad_second, key_pair, key_high),
                    ],
                    axis=0,
                )
            )

            def turned(source_t, block_first, block_second):
                high, low = split(source_t[e * HEAD_DIM : (e + 1) * HEAD_DIM, :])
                both = jnp.concatenate([high, low], axis=0)
                first_high, first_low = split(block_first)
                second_high, second_low = split(block_second)
                one = mm(both[:, :HALF], first_high)
                one = one[:HEAD_DIM] + one[HEAD_DIM:] + mm(high[:, :HALF], first_low)
                two = mm(both[:, HALF:], second_high)
                two = two[:HEAD_DIM] + two[HEAD_DIM:] + mm(high[:, HALF:], second_low)
                return jnp.concatenate([two[:, :HALF] + one, two[:, HALF:]], axis=1)

            grad_k.append(turned(query_t, grad_first, grad_second))
            grad_v.append(turned(grad_t, score_first, score_second))
        query_grad = jnp.where(lanes < HEAD_DIM, grad_q[0], grad_q[1]) * SCALE
        low[:, columns(p)] = query_grad.astype(bf16)
        low[:, columns(p, D)] = jnp.transpose(jnp.concatenate(grad_k, axis=0)).astype(bf16)
        dv_s[:ROWS, columns(p)] = jnp.transpose(jnp.concatenate(grad_v, axis=0))
        return carry

    for p in range(PAIRS):
        pair(p, 0)

    pulled = rows_s[...] - jnp.transpose(cols_s[...])
    high, middle, rest = split_three(pulled)
    upper_first = jnp.concatenate(
        [
            jnp.where(row_iota(HALF, HALF) <= lane_iota(HALF, HALF), 1.0, 0.0),
            jnp.full((HALF, HALF), 0.0, f32) + jnp.where(wide, 1.0, 0.0),
        ],
        axis=1,
    ).astype(bf16)
    upper_second = upper_first[:, :HALF]
    later = jnp.concatenate(
        [
            mm(upper_first, high) + mm(upper_first, middle) + mm(upper_first, rest),
            mm(upper_second, high[HALF:]) + mm(upper_second, middle[HALF:])
            + mm(upper_second, rest[HALF:]),
        ],
        axis=0,
    )
    grad_dp = later * (1.0 / 16.0) * sigmoid(-(k.dp()[...] + k.bd()))
    grad_bd = jnp.sum(grad_dp, axis=0, keepdims=True)
    low[:, QKVG:] = grad_dp.astype(bf16)

    dv_s[ROWS:, :] = jnp.zeros((8, D), f32)
    position = row_iota(ROWS, 1) & jnp.where(wide, ROWS - 1, HALF - 1)
    last = jnp.where(wide, ROWS - 1, HALF - 1)
    here = dv_s[0:ROWS, :]
    one = jnp.where(position <= last - 1, dv_s[1 : 1 + ROWS, :], 0.0)
    two = jnp.where(position <= last - 2, dv_s[2 : 2 + ROWS, :], 0.0)
    value = qkvg[:, 2 * D : 3 * D]
    low[:, 2 * D : 3 * D] = (k.ck(0) * here + k.ck(1) * one + k.ck(2) * two).astype(bf16)
    k.push("low")

    taps = [jnp.sum(rows * value, axis=0, keepdims=True) for rows in (here, one, two)]
    rest = jnp.concatenate([grad_bd, jnp.zeros((1, D - LANES), f32)], axis=1)
    k.sums[...] = jnp.concatenate([*taps, rest, jnp.zeros((4, D), f32)], axis=0)

    ordered_t = jnp.transpose(k.ordered()[...].astype(f32)).astype(bf16)
    gwo = k.gwo()
    gw = k.gw

    def weights(j, carry):
        part = pl.ds(pl.multiple_of(j * HALF, HALF), HALF)
        gw[:, part] = mm(ordered_t, low[:, part])
        return carry

    lax.fori_loop(0, QKVG // HALF, weights, 0)
    gw[:, QKVG : QKVG + D] = gwo[...]
    gw[:, QKVG + D :] = mm(ordered_t, low[:, QKVG:])

    def halves(j, carry):
        here = pl.ds(pl.multiple_of(j * HALF, HALF), HALF)
        keep = pl.ds(pl.multiple_of(j * HALF + k.section * GROUP, HALF), HALF)
        send = pl.ds(pl.multiple_of(j * HALF + (1 - k.section) * GROUP, HALF), HALF)
        k.gw_keep[:, here] = gw[:, keep]
        k.gw_send[:, here] = gw[:, send].astype(bf16)
        return carry

    lax.fori_loop(0, GROUP // HALF, halves, 0)


def second_layer_body(k):
    attn_forward_body(k)
    for name in ("ordered", "qkvg", "dp", "vc", "cum", "cumt", "o", "gated"):
        setattr(k, name, In(None, getattr(k, name)))
    ffn_backward_body(k)
    for name in ("branch_low", "gwo"):
        setattr(k, name, In(None, getattr(k, name)))
    k.sums = k.mixer_sums
    mixer_backward_body(k)


def input_backward_body(k):
    flip = k.layer == 1
    wide = k.wide
    gmod, mixed_s, perm_s = k.gmod, k.mixed_s, k.perm_s
    gmod[...] = jnp.zeros(gmod.shape, f32)
    low, w_qk, w_vgd = k.low(), k.w_qk(), k.w_vgd()

    def inner_grad(i, carry):
        rows = pl.ds(pl.multiple_of(i * HALF, HALF), HALF)
        mixed_s[rows, :] = mm_t(low[rows, : 2 * D], w_qk[...]) + mm_t(
            low[rows, 2 * D :], w_vgd[...]
        )
        return carry

    lax.fori_loop(0, 2, inner_grad, 0)
    if flip:
        high, middle, rest = split_three(mixed_s[...])
        perm_s[:, :D] = high
        perm_s[:, D : 2 * D] = middle
        perm_s[:, 2 * D :] = rest
    x, mid_grad = k.x(), k.mid_grad()
    k.mods()

    def tile(i, carry):
        start = i * HALF
        rows = pl.ds(start, HALF)
        slot = k.slot(i)
        if flip:
            three = mm(order_matrix(start, HALF, wide, False), perm_s[...])
            grad = three[:, :D] + three[:, D : 2 * D] + three[:, 2 * D :]
        else:
            grad = mixed_s[rows, :]
        normal, rate = normalise(x[rows, :].astype(f32))
        where = (pl.ds(slot, 1), slice(0, D))
        gmod[where] = gmod[where] + jnp.sum(grad, axis=0, keepdims=True)
        where = (pl.ds(slot, 1), slice(D, 2 * D))
        gmod[where] = gmod[where] + jnp.sum(grad * normal, axis=0, keepdims=True)
        total = mid_grad[rows, :] + normalise_back(normal, rate, grad * (1.0 + k.share(slot, 1)))
        k.gx[rows, :] = total
        k.gx_low[rows, :] = total.astype(bf16)
        return carry

    for i in range(2):
        tile(i, 0)
    k.push("gx_low")
    k.push("gx")
    ffn, mixer = k.ffn_sums(), k.mixer_sums()
    k.mod_low[...] = jnp.concatenate([gmod[...], ffn[...]], axis=1).astype(bf16)
    if k.layer == 0:
        first = k.section == 0
        k.gx_send[...] = jnp.where(first, k.gx_two()[...], k.gx[...])
        one, two = k.mod_low[...].astype(f32), k.mod_two()[...].astype(f32)
        k.mod_mine[...] = jnp.where(first, one, two).astype(bf16)
        k.mod_send[...] = jnp.where(first, two, one).astype(bf16)
    half = 2 * D
    rest = ffn[0:1, :] + ffn[1:2, :]
    k.sums[...] = jnp.concatenate(
        [
            gmod[0:1, :] + gmod[1:2, :],
            rest[:, :half],
            rest[:, half:],
            ffn[2:3, :half],
            ffn[2:3, half:],
            jnp.concatenate([ffn[3:4, :D], mixer[0:1, :]], axis=1),
            jnp.concatenate([mixer[1:2, :], mixer[2:3, :]], axis=1),
            jnp.concatenate([mixer[3:4, :], jnp.zeros((1, D), f32)], axis=1),
        ],
        axis=0,
    )


ANY = pl.BlockSpec(memory_space=pl.ANY)
VMEM = pl.BlockSpec(memory_space=pltpu.VMEM)
HBM = pl.BlockSpec(memory_space=pltpu.HBM)


def call(body, layer, layouts, ins, outs, scratch, flops, packed=None, after=()):
    arrays = []
    counts = []
    kept = []
    places = []
    for kind, given, part in ins.values():
        places.extend([ANY] * 2 if kind == "own" else [HBM])
        given = given if kind == "own" else (given,)
        arrays.extend(given)
        counts.append(len(given))
        rows, wide = given[0].shape[-2:]
        start, stop = part or (0, wide)
        kept.append(pltpu.VMEM((rows, stop - start), given[0].dtype))

    def kernel(*refs):
        refs = list(refs)
        take = lambda count: [refs.pop(0) for _ in range(count)]
        (layouts_ref,) = take(1)
        sources = [take(count) for count in counts]
        take(len(after))
        targets = take(len(outs))
        buffers = take(len(ins))
        results = take(len(outs))
        rest = take(len(scratch))
        in_sems, out_sems = refs
        k = Kernel(layer, layouts_ref)
        k.packed = packed
        for number, (name, (kind, _, part)) in enumerate(ins.items()):
            given = sources[number]
            if part is not None:
                given = [ref.at[:, part[0] : part[1]] for ref in given]
            setattr(k, name, k.load(kind, given, buffers[number], in_sems.at[number]))
        k.results = {}
        for number, name in enumerate(outs):
            setattr(k, name, results[number])
            k.results[name] = (results[number], targets[number], out_sems.at[number])
        for name, ref in zip(scratch, rest):
            setattr(k, name, ref)
        body(k)
        k.finish()

    return pl.pallas_call(
        kernel,
        out_shape=[jax.ShapeDtypeStruct(shape, kind) for shape, kind, _ in outs.values()],
        in_specs=[pl.BlockSpec(memory_space=pltpu.SMEM)] + places + [ANY] * len(after),
        out_specs=[HBM if for_kernel else ANY for _, _, for_kernel in outs.values()],
        scratch_shapes=kept
        + [pltpu.VMEM(shape, kind) for shape, kind, _ in outs.values()]
        + [pltpu.VMEM(shape, kind) for shape, kind in scratch.values()]
        + [pltpu.SemaphoreType.DMA((len(ins),)), pltpu.SemaphoreType.DMA((len(outs),))],
        compiler_params=pltpu.CompilerParams(vmem_limit_bytes=56 * 1024 * 1024),
        cost_estimate=pl.CostEstimate(flops=flops, bytes_accessed=4 << 20, transcendentals=0),
    )(layouts, *arrays, *after)


def own(pair, part=None):
    return ("own", pair, part)


def plain(array):
    return ("plain", array, None)


def micro(array):
    return ("micro", array, None)


AT_UP = (0, FF)
AT_OUT = (FF, FF + D)


def attn_forward(layer, layouts, x, mods, small, qk, vgd):
    return call(
        attn_forward_body,
        layer,
        layouts,
        dict(
            x=micro(x),
            mods=own(mods),
            w_qk=own(qk),
            w_vgd=own(vgd),
            small=own(small),
        ),
        dict(
            ordered=((ROWS, D), bf16, True),
            qkvg=((ROWS, QKVG), f32, True),
            dp=((ROWS, LANES), f32, True),
            vc=((ROWS, D), f32, True),
            cum=((ROWS, LANES), f32, True),
            cumt=((LANES, ROWS), f32, True),
            o=((ROWS, D), f32, True),
            gated=((ROWS, D), bf16, True),
        ),
        dict(
            inner=((ROWS, D), bf16),
            vpad=((ROWS + 8, D), f32),
            bias=((HALF, ROWS), f32),
        ),
        4 * 10**9,
    )


def ffn_forward(layer, layouts, x, mods, small, gated, upo, down):
    return call(
        ffn_forward_body,
        layer,
        layouts,
        dict(
            gated=plain(gated),
            x=micro(x),
            wo=own(upo, AT_OUT),
            mods=own(mods),
            small=own(small),
            wu=own(upo, AT_UP),
            wn=own(down),
        ),
        dict(
            out=((ROWS, D), bf16, True),
            branch=((ROWS, D), f32, True),
            down=((ROWS, D), f32, True),
        ),
        {},
        3 * 10**9,
    )


def ffn_backward(
    layer, layouts, x, mods, small, gated, branch, down_raw, grad, upo, down, devices, after=()
):
    shard = D // devices
    in_kernel = shard % 8 == 0
    if in_kernel:
        sums = dict(
            keep=((devices, shard, FF), f32, True),
            gone=((devices, shard, FF), bf16, False),
        )
    else:
        sums = dict(gwu=((D, FF), f32, False), gwn=((FF, D), f32, False))
    return call(
        ffn_backward_body,
        layer,
        layouts,
        dict(
            mods=own(mods),
            small=own(small),
            x=micro(x),
            **(
                dict(gated=plain(gated), wo=own(upo, AT_OUT))
                if layer == 1
                else dict(branch=plain(branch), down=plain(down_raw))
            ),
            grad=micro(grad),
            wu=own(upo, AT_UP),
            wn=own(down),
            **(dict(gated=plain(gated)) if layer == 0 else {}),
        ),
        dict(
            **(
                dict(out=((ROWS, D), bf16, True), sent=((ROWS, D), bf16, False))
                if layer == 1
                else {}
            ),
            mid_grad=((ROWS, D), f32, True),
            branch_low=((ROWS, D), bf16, True),
            gwo=((D, D), f32, True),
            sums=((8, FF), f32, True),
            **sums,
        ),
        dict(
            **({"gwn": ((FF, D), f32)} if in_kernel else {}),
            hidden_s=((ROWS, FF), bf16),
            inner_s=((ROWS, D), bf16),
            up_s=((ROWS, FF), bf16),
            down_s=((ROWS, D), bf16),
            gmod=((8, FF), f32),
            gbu=((1, FF), f32),
            gbn=((1, D), f32),
        ),
        2 * 10**9,
        packed=in_kernel,
        after=after,
    )


def second_layer(layouts, x, mods, small, grad, qk, vgd, upo, down, devices):
    shard = D // devices
    in_kernel = shard % 8 == 0
    if in_kernel:
        sums = dict(
            keep=((devices, shard, FF), f32, True),
            gone=((devices, shard, FF), bf16, False),
        )
    else:
        sums = dict(gwu=((D, FF), f32, False), gwn=((FF, D), f32, False))
    return call(
        second_layer_body,
        1,
        layouts,
        dict(
            x=micro(x),
            mods=own(mods),
            w_qk=own(qk),
            w_vgd=own(vgd),
            small=own(small),
            wo=own(upo, AT_OUT),
            grad=micro(grad),
            wu=own(upo, AT_UP),
            wn=own(down),
        ),
        dict(
            out=((ROWS, D), bf16, True),
            sent=((ROWS, D), bf16, False),
            mid_grad=((ROWS, D), f32, True),
            sums=((8, FF), f32, True),
            low=((ROWS, QKVG + LANES), bf16, True),
            gw_keep=((D, GROUP), f32, True),
            gw_send=((D, GROUP), bf16, False),
            mixer_sums=((8, D), f32, True),
            **sums,
        ),
        dict(
            ordered=((ROWS, D), bf16),
            qkvg=((ROWS, QKVG), f32),
            dp=((ROWS, LANES), f32),
            vc=((ROWS, D), f32),
            cum=((ROWS, LANES), f32),
            cumt=((LANES, ROWS), f32),
            o=((ROWS, D), f32),
            gated=((ROWS, D), bf16),
            inner=((ROWS, D), bf16),
            vpad=((ROWS + 8, D), f32),
            bias=((HALF, ROWS), f32),
            branch_low=((ROWS, D), bf16),
            gwo=((D, D), f32),
            **({"gwn": ((FF, D), f32)} if in_kernel else {}),
            hidden_s=((ROWS, FF), bf16),
            inner_s=((ROWS, D), bf16),
            up_s=((ROWS, FF), bf16),
            down_s=((ROWS, D), bf16),
            gmod=((8, FF), f32),
            gbu=((1, FF), f32),
            gbn=((1, D), f32),
            mixed_s=((ROWS, D), f32),
            dv_s=((ROWS + 8, D), f32),
            rows_s=((ROWS, LANES), f32),
            cols_s=((LANES, ROWS), f32),
            gw=((D, 2 * GROUP), f32),
        ),
        14 * 10**9,
        packed=in_kernel,
    )


def mixer_backward(layer, layouts, small, saved, branch_low, gwo, upo, after=()):
    ordered, qkvg, dp, vc, cum, cumt, o = saved
    return call(
        mixer_backward_body,
        layer,
        layouts,
        dict(
            branch_low=plain(branch_low),
            wo=own(upo, AT_OUT),
            qkvg=plain(qkvg),
            vc=plain(vc),
            cum=plain(cum),
            cumt=plain(cumt),
            o=plain(o),
            small=own(small),
            dp=plain(dp),
            ordered=plain(ordered),
            gwo=plain(gwo),
        ),
        dict(
            low=((ROWS, QKVG + LANES), bf16, True),
            gw_keep=((D, GROUP), f32, True),
            gw_send=((D, GROUP), bf16, False),
            sums=((8, D), f32, True),
        ),
        dict(
            mixed_s=((ROWS, D), f32),
            dv_s=((ROWS + 8, D), f32),
            rows_s=((ROWS, LANES), f32),
            cols_s=((LANES, ROWS), f32),
            bias=((HALF, ROWS), f32),
            gw=((D, 2 * GROUP), f32),
        ),
        3 * 10**9,
        after=after,
    )


def input_backward(
    layer, layouts, x, mods, low, mid_grad, ffn_sums, mixer_sums, qk, vgd, two=None, after=()
):
    extra_in, extra_out = {}, {}
    if two is not None:
        extra_in = dict(gx_two=plain(two[0]), mod_two=plain(two[1]))
        extra_out = dict(
            gx_send=((ROWS, D), f32, False),
            mod_mine=((8, 6 * D), bf16, False),
            mod_send=((8, 6 * D), bf16, False),
        )
    return call(
        input_backward_body,
        layer,
        layouts,
        dict(
            low=plain(low),
            w_qk=own(qk),
            w_vgd=own(vgd),
            x=micro(x),
            mid_grad=plain(mid_grad),
            mods=own(mods),
            ffn_sums=plain(ffn_sums),
            mixer_sums=plain(mixer_sums),
            **extra_in,
        ),
        dict(
            gx=((ROWS, D), f32, True),
            gx_low=((ROWS, D), bf16, True),
            mod_low=((8, 6 * D), bf16, True),
            sums=((8, 2 * D), f32, False),
            **extra_out,
        ),
        dict(
            mixed_s=((ROWS, D), f32),
            perm_s=((ROWS, 3 * D), bf16),
            gmod=((8, 2 * D), f32),
        ),
        1 * 10**9,
        after=after,
    )


def small_kernel(b_up, b_down, taps, b_decay, packed):
    packed[...] = jnp.zeros(packed.shape, f32)
    packed[0:1, :] = b_up[...]
    packed[1:2, :D] = b_down[...]
    packed[2:5, :D] = taps[0]
    packed[5:6, :HEADS] = b_decay[...]


def pack_small(b_up, b_down, taps, b_decay):
    return pl.pallas_call(
        small_kernel,
        out_shape=jax.ShapeDtypeStruct((8, FF), f32),
        in_specs=[VMEM] * 4,
        out_specs=VMEM,
        compiler_params=pltpu.CompilerParams(vmem_limit_bytes=8 * 1024 * 1024),
    )(b_up, b_down, taps, b_decay)


def pack_kernel(
    w_query, w_key, w_value, w_gate, w_out, w_decay, w_up, w_down, w_ada, conditions,
    qkuo, vgd, down, ada, lifted,
):
    qkuo[:, :D] = w_query[0]
    qkuo[:, D : 2 * D] = w_key[0]
    vgd[:, :D] = w_value[0]
    vgd[:, D : 2 * D] = w_gate[0]
    place = jnp.where(row_iota(HEADS, LANES) == lane_iota(HEADS, LANES), 1.0, 0.0).astype(bf16)
    turned = lax.dot_general(
        w_decay[0], place, (((0,), (0,)), ((), ())), preferred_element_type=f32
    )
    vgd[:, 2 * D :] = turned.astype(bf16)
    qkuo[:, 2 * D : 2 * D + FF] = w_up[0]
    qkuo[:, 2 * D + FF :] = w_out[0]
    down[...] = w_down[0]
    ada[...] = w_ada[0]
    values = jnp.concatenate([conditions[m].astype(f32) for m in range(MICRO)], axis=0)
    lifted[0] = (values * sigmoid(values)).astype(bf16)


def pack(*weights):
    shard = weights[0].shape[1]
    shapes = [(shard, width) for width in (3 * D + FF, 2 * D + LANES)]
    shapes += [weights[7].shape[1:], weights[8].shape[1:], (1, MICRO * SLOTS, D)]
    return pl.pallas_call(
        pack_kernel,
        out_shape=[jax.ShapeDtypeStruct(shape, bf16) for shape in shapes],
        in_specs=[VMEM] * len(weights),
        out_specs=[VMEM] * len(shapes),
    )(*weights)


def join_kernel(bits, waits, *refs):
    count = len(bits)
    held, came, out = refs[:count], refs[count : 2 * count], refs[2 * count + waits :]
    for i, bit in enumerate(bits):
        mine = (lax.axis_index("row") >> bit) & 1
        out[i][:, mine] = held[i][...]
        out[i][:, 1 - mine] = came[i][...]


def join(held, came, bits, after=()):
    def parts(array, bit):
        axis = axis_of(bit)
        above = 1
        for size in array.shape[:axis]:
            above *= size
        return array.reshape((above, -1) + array.shape[-2:])

    split_held = [parts(array, bit) for array, bit in zip(held, bits)]
    split_came = [parts(array, bit) for array, bit in zip(came, bits)]
    out = pl.pallas_call(
        functools.partial(join_kernel, bits, len(after)),
        out_shape=[
            jax.ShapeDtypeStruct(array.shape[:1] + (2,) + array.shape[1:], array.dtype)
            for array in split_held
        ],
        in_specs=[VMEM] * (2 * len(held)) + [ANY] * len(after),
        out_specs=[VMEM] * len(held),
        compiler_params=pltpu.CompilerParams(vmem_limit_bytes=8 * 1024 * 1024),
        cost_estimate=pl.CostEstimate(flops=10**6, bytes_accessed=10**6, transcendentals=0),
    )(*split_held, *split_came, *after)
    joined = []
    for array, result, bit in zip(held, out, bits):
        shape = list(array.shape)
        shape[axis_of(bit)] = 2
        joined.append(result.reshape(shape))
    return joined


def lifted_kernel(mine, came, ada, out, kept, sem):
    copy = pltpu.make_async_copy(ada, kept, sem)
    copy.start()
    first = lax.axis_index("section") == 0
    pair = mine[0:SLOTS, :].astype(f32), came[0:SLOTS, :].astype(f32)
    grad = jnp.concatenate(
        [jnp.where(first, pair[0], pair[1]), jnp.where(first, pair[1], pair[0])], axis=0
    ).astype(bf16)
    copy.wait()
    out[...] = mm_t(grad, kept[...])


def lifted_grads(mine, came, ada):
    return pl.pallas_call(
        lifted_kernel,
        out_shape=jax.ShapeDtypeStruct((MICRO * SLOTS, D), f32),
        in_specs=[VMEM, VMEM, ANY],
        out_specs=VMEM,
        scratch_shapes=[pltpu.VMEM((D, 6 * D), bf16), pltpu.SemaphoreType.DMA],
        compiler_params=pltpu.CompilerParams(vmem_limit_bytes=16 * 1024 * 1024),
        cost_estimate=pl.CostEstimate(flops=10**9, bytes_accessed=2 << 20, transcendentals=0),
    )(mine, came, ada)


def term_kernel(*refs):
    *terms, stays, goes = refs
    stays[...] = sum(ref[:, 0] for ref in terms)
    goes[...] = sum(ref[:, 1] for ref in terms)


def term_step(below, *terms):
    tail = terms[0].shape[1:]
    above = terms[0].shape[0] // (2 * below)
    shape = jax.ShapeDtypeStruct((above, below) + tail, f32)
    out = pl.pallas_call(
        term_kernel,
        out_shape=[shape] * 2,
        in_specs=[VMEM] * len(terms),
        out_specs=[VMEM] * 2,
        compiler_params=pltpu.CompilerParams(vmem_limit_bytes=8 * 1024 * 1024),
        cost_estimate=pl.CostEstimate(flops=10**6, bytes_accessed=10**6, transcendentals=0),
    )(*[term.reshape((above, 2, below) + tail) for term in terms])
    return [array.reshape((above * below,) + tail) for array in out]


def step_kernel(bit, widths, counts, waits, *refs):
    mine = (lax.axis_index("row") >> bit) & 1
    count, many = len(widths), len(counts)
    refs = list(refs)
    take = lambda number: [refs.pop(0) for _ in range(number)]
    sources = take(count + many)
    take(waits)
    targets = take(count + 1)
    buffers = take(count + many)
    results = take(count + 1)
    in_sems, out_sems = refs
    arrive = [
        pltpu.make_async_copy(source, buffer, in_sems.at[i])
        for i, (source, buffer) in enumerate(zip(sources, buffers))
    ]
    leave = [
        pltpu.make_async_copy(result, target, out_sems.at[i])
        for i, (result, target) in enumerate(zip(results, targets))
    ]
    for copy in arrive:
        copy.start()
    kept, came = buffers[:count], buffers[count:]
    places = [(j, i) for j, number in enumerate(counts) for i in range(number)]
    goes = results[count]
    at = 0
    for i in range(count):
        j, place = places[i]
        arrive[i].wait()
        if place == 0:
            arrive[count + j].wait()
        start = sum(widths[i - place : i])
        columns = slice(start, start + widths[i])
        total = kept[i][:, 1 - mine] + came[j][:, 1 - mine, :, :, columns].astype(f32)
        goes[:, :, :, at : at + widths[i]] = total.astype(bf16)
        at += widths[i]
    leave[count].start()
    for i in range(count):
        j, place = places[i]
        start = sum(widths[i - place : i])
        columns = slice(start, start + widths[i])
        results[i][...] = kept[i][:, mine] + came[j][:, mine, :, :, columns].astype(f32)
        leave[i].start()
    for copy in leave:
        copy.wait()


def step(kept, came, bit, below=1, after=()):
    blocks, rows = kept[0].shape[0] // 2, kept[0].shape[1]
    above = blocks // below
    paired = lambda array: array.reshape((above, 2, below) + array.shape[1:])
    widths = [array.shape[2] for array in kept]
    arrays = [paired(array) for array in kept] + [paired(array) for array, _ in came]
    shapes = [((above, below, rows, width), f32) for width in widths]
    shapes.append(((above, below, rows, sum(widths)), bf16))
    out = pl.pallas_call(
        functools.partial(step_kernel, bit, widths, [count for _, count in came], len(after)),
        out_shape=[jax.ShapeDtypeStruct(shape, kind) for shape, kind in shapes],
        in_specs=[HBM] * len(kept) + [ANY] * (len(came) + len(after)),
        out_specs=[HBM] * len(kept) + [ANY],
        scratch_shapes=[pltpu.VMEM(array.shape, array.dtype) for array in arrays]
        + [pltpu.VMEM(shape, kind) for shape, kind in shapes]
        + [pltpu.SemaphoreType.DMA((len(arrays),)), pltpu.SemaphoreType.DMA((len(shapes),))],
        compiler_params=pltpu.CompilerParams(vmem_limit_bytes=10 * 1024 * 1024),
        cost_estimate=pl.CostEstimate(flops=10**5, bytes_accessed=10**5, transcendentals=0),
    )(*arrays, *after)
    count = len(kept)
    flat_blocks = [array.reshape((blocks,) + array.shape[2:]) for array in out]
    return flat_blocks[:count], flat_blocks[count]


def misc_step_kernel(held, arrived, out):
    size = held.shape[0] - SUMS
    out[:size, :] = held[:size, :]
    out[size : 2 * size, :] = arrived[:size, :]
    high, low = split(misc_sums(held, arrived))
    out[2 * size : 2 * size + SUMS // 2, :] = high
    out[2 * size + SUMS // 2 :, :] = low


def misc_step(held, arrived):
    return pl.pallas_call(
        misc_step_kernel,
        out_shape=jax.ShapeDtypeStruct((2 * held.shape[0] - SUMS, 2 * D), bf16),
        in_specs=[VMEM] * 2,
        out_specs=VMEM,
        compiler_params=pltpu.CompilerParams(vmem_limit_bytes=8 * 1024 * 1024),
        cost_estimate=pl.CostEstimate(flops=10**5, bytes_accessed=10**5, transcendentals=0),
    )(held, arrived)


def misc_sums(*refs):
    size = refs[0].shape[0] - SUMS
    parts = [ref[size:, :].astype(f32) for ref in refs]
    return sum(part[: SUMS // 2] + part[SUMS // 2 :] for part in parts)


SUMS = 32
OWN = 16


def misc_kernel(conditions, mod_one, mod_two, sums_one, sums_two, out):
    values = conditions[...].astype(f32)
    values = jnp.where(lax.axis_index("section") == 0, values[:SLOTS], values[SLOTS:])
    lifted = values * sigmoid(values)
    spare = [jnp.concatenate([lifted[0:1], lifted[1:2]], axis=1), jnp.zeros((1, 2 * D), f32)]
    rows = []
    for mod in (mod_one, mod_two):
        for slot in range(SLOTS):
            for i in range(3):
                part = mod[slot : slot + 1, i * 2 * D : (i + 1) * 2 * D]
                rows.append(part.astype(f32))
        rows.extend(spare)
    sums = jnp.concatenate([sums_one[...], sums_two[...]], axis=0)
    rows.extend(part.astype(f32) for part in split(sums))
    out[...] = jnp.concatenate(rows, axis=0).astype(bf16)


def pack_misc(conditions, mod_one, mod_two, sums_one, sums_two):
    return pl.pallas_call(
        misc_kernel,
        out_shape=jax.ShapeDtypeStruct((OWN + SUMS, 2 * D), bf16),
        in_specs=[VMEM] * 5,
        out_specs=VMEM,
        compiler_params=pltpu.CompilerParams(vmem_limit_bytes=8 * 1024 * 1024),
    )(conditions, mod_one, mod_two, sums_one, sums_two)


def finish_kernel(widths, counts, waits, *refs):
    count = len(widths)
    kept, refs = refs[:count], refs[count:]
    came, refs = refs[: len(counts)], refs[len(counts) :]
    parts = refs[:4]
    mine, other, small_mine, small_other = refs[4 + waits :]
    places = [(ref, i) for ref, many in zip(came, counts) for i in range(many)]
    added = []
    for i in range(count):
        ref, place = places[i]
        start = sum(widths[i - place : i])
        added.append(kept[i][0] + ref[0, :, start : start + widths[i]].astype(f32))
    a1, f1, f2, a2 = added
    size = parts[0].shape[0] - SUMS
    rows = jnp.concatenate([part[:size, :] for part in parts], axis=0)
    rows = rows.astype(f32).reshape(-1, OWN, 2 * D)
    shard = mine.shape[0]
    chosen = lane_iota(shard, D) == row_iota(shard, D) + lax.axis_index("row") * shard
    chosen = jnp.where(chosen, 1.0, 0.0).astype(bf16)
    features = [rows[:, 6, slot * D : (slot + 1) * D].astype(bf16) for slot in range(SLOTS)]
    lifted = jnp.concatenate([mm_t(chosen, part) for part in features], axis=1).astype(bf16)

    def ada(first):
        columns = []
        for i in range(3):
            both = [rows[:, first + 3 * slot + i, :] for slot in range(SLOTS)]
            columns.append(mm(lifted, jnp.concatenate(both, axis=0).astype(bf16)))
        return jnp.concatenate(columns, axis=1)

    first = lax.axis_index("section") == 0
    at = 0
    for one, two in ((a1, a2), (f1, f2), (ada(0), ada(OWN // 2))):
        columns = slice(at, at + one.shape[1])
        mine[:, columns] = jnp.where(first, one, two)
        other[:, columns] = jnp.where(first, two, one)
        at += one.shape[1]
    total = misc_sums(*parts)
    one, two = total[0:8, :], total[8:16, :]
    small_mine[...] = jnp.where(first, one, two)
    small_other[...] = jnp.where(first, two, one)


def finish(kept, came, parts, after):
    widths = [array.shape[2] for array in kept]
    shard = kept[0].shape[1]
    wide = GROUP + FF + 6 * D
    arrays = [array for array, _ in came]
    shapes = [(shard, wide)] * 2 + [(8, 2 * D)] * 2
    return pl.pallas_call(
        functools.partial(finish_kernel, widths, [count for _, count in came], len(after)),
        out_shape=[jax.ShapeDtypeStruct(shape, f32) for shape in shapes],
        in_specs=[VMEM] * (len(kept) + len(came) + 4) + [ANY] * len(after),
        out_specs=[VMEM] * 4,
        compiler_params=pltpu.CompilerParams(vmem_limit_bytes=8 * 1024 * 1024),
    )(*kept, *arrays, *parts, *after)


def output_kernel(mine, other, small_mine, small_other, *outs):
    first = lax.axis_index("section") == 0

    def halves(start, width):
        columns = slice(start, start + width)
        pair = mine[:, columns], other[:, columns]
        return jnp.where(first, pair[0], pair[1]), jnp.where(first, pair[1], pair[0])

    attn = halves(0, GROUP)
    cut = GROUP - 2 * D
    outs[0][...] = attn[0][:, :D]
    outs[1][...] = attn[0][:, D : 2 * D]
    outs[2][:, :cut] = attn[0][:, 2 * D :]
    outs[2][:, cut:] = attn[1][:, : D - cut]
    outs[3][...] = attn[1][:, D - cut : 2 * D - cut]
    outs[4][...] = attn[1][:, 2 * D - cut : 3 * D - cut]
    decay = jnp.transpose(attn[1][:, 3 * D - cut :])
    for head in range(HEADS):
        outs[5][head] = decay[head : head + 1, :]
    up = halves(GROUP, FF // 2)
    outs[6][:, : FF // 2] = up[0]
    outs[6][:, FF // 2 :] = up[1]
    for piece in range(2):
        down = halves(GROUP + FF // 2 + piece * D, D)
        outs[7][piece] = down[0]
        outs[7][2 + piece] = down[1]
    outs[8][...] = mine[:, GROUP + FF :] + other[:, GROUP + FF :]
    small = small_mine[...] + small_other[...]
    half = 2 * D
    for i in range(3):
        outs[9][:, i * half : (i + 1) * half] = small[i : i + 1, :]
    for i in range(2):
        outs[10][:, i * half : (i + 1) * half] = small[3 + i : 4 + i, :]
    outs[11][...] = small[5:6, :D]
    outs[12][0] = small[5:6, D:]
    outs[12][1] = small[6:7, :D]
    outs[12][2] = small[6:7, D:]
    outs[13][...] = small[7:8, :HEADS]


def outputs(mine, other, small_mine, small_other):
    shard = mine.shape[0]
    shapes = (
        [(shard, D)] * 5
        + [(HEADS, 1, shard), (shard, FF), (4, shard, D), (shard, 6 * D)]
        + [(1, 6 * D), (1, FF), (1, D), (3, 1, D), (1, HEADS)]
    )
    return pl.pallas_call(
        output_kernel,
        out_shape=[jax.ShapeDtypeStruct(shape, f32) for shape in shapes],
        in_specs=[VMEM] * 4,
        out_specs=[VMEM] * len(shapes),
        compiler_params=pltpu.CompilerParams(vmem_limit_bytes=8 * 1024 * 1024),
    )(mine, other, small_mine, small_other)


def both_kernel(one, two, came, out, mark, kept, sems):
    section = lax.axis_index("section")
    mark[...] = jnp.zeros(mark.shape, f32)

    def move(mine, layer):
        arrive = [
            pltpu.make_async_copy(mine, kept.at[layer], sems.at[0]),
            pltpu.make_async_copy(came, kept.at[1 - layer], sems.at[1]),
        ]
        leave = [
            pltpu.make_async_copy(kept.at[layer], out.at[layer], sems.at[2]),
            pltpu.make_async_copy(kept.at[1 - layer], out.at[1 - layer], sems.at[3]),
        ]
        for copy in arrive:
            copy.start()
        for copy, after in zip(arrive, leave):
            copy.wait()
            after.start()
        for copy in leave:
            copy.wait()

    @pl.when(section == 0)
    def _():
        move(one, 0)

    @pl.when(section == 1)
    def _():
        move(two, 1)


def both_micros(one, two, came):
    return pl.pallas_call(
        both_kernel,
        out_shape=[
            jax.ShapeDtypeStruct((MICRO,) + one.shape, one.dtype),
            jax.ShapeDtypeStruct((8, LANES), f32),
        ],
        in_specs=[ANY] * 3,
        out_specs=[ANY, VMEM],
        scratch_shapes=[
            pltpu.VMEM((MICRO,) + one.shape, one.dtype),
            pltpu.SemaphoreType.DMA((4,)),
        ],
        compiler_params=pltpu.CompilerParams(vmem_limit_bytes=8 * 1024 * 1024),
    )(one, two, came)


def swap(values):
    return lax.ppermute(values, "section", [(0, 1), (1, 0)])


def row_bits():
    bits = lax.axis_size("row").bit_length() - 1
    third = bits // 3
    return (
        tuple(range(third)),
        tuple(range(third, 2 * third)),
        tuple(range(2 * third, bits)),
    )


def across(values, flips):
    size = lax.axis_size("row")
    return lax.ppermute(values, "row", [(i, i ^ flips) for i in range(size)])


def partner(values, bit):
    return across(values, 1 << bit)


def axis_of(bit):
    return lax.axis_size("row").bit_length() - 2 - bit


def bit_of(bit):
    return (lax.axis_index("row") >> bit) & 1


def single(values):
    return values.reshape((1,) * (lax.axis_size("row").bit_length() - 1) + values.shape)


def gather_steps(along_x, along_y, along_z):
    steps = [(bit, bit) for bit in reversed(along_z)]
    return steps + list(zip(along_x + along_y, along_y + along_x))


def flat(held):
    return held.reshape(-1, held.shape[-1])


def lock(*arrays):
    return lax.optimization_barrier(arrays)


def on_device(
    tokens, conditions, output_grad, layouts,
    w_ada, b_ada, w_query, w_key, w_value, w_gate, w_out, w_decay, b_decay, conv_kernel,
    w_up, b_up, w_down, b_down,
):
    section = lax.axis_index("section")
    devices = lax.axis_size("row")
    shard = w_query.shape[1]
    along_x, along_y, along_z = row_bits()

    def both(values):
        return values, swap(values)

    qkuo, vgd, down, ada, lifted = pack(
        w_query, w_key, w_value, w_gate, w_out, w_decay.transpose(0, 2, 1), w_up, w_down, w_ada,
        conditions,
    )
    small = pack_small(b_up, b_down, conv_kernel, b_decay)
    conds = conditions.reshape(MICRO * SLOTS, D)
    steps = gather_steps(along_x, along_y, along_z)
    lag = len(along_z)
    plane = along_x + along_y
    bounds = [len(plane) * i // lag for i in range(lag + 1)]
    held = [single(array) for array in (qkuo, vgd, down)]
    ada = single(ada)
    for place, pair in enumerate(steps):
        bits = pair + pair[1:]
        if place == len(steps) - 1:
            bits = pair + pair
            held = [held[0][..., : 2 * D], held[1], held[0][..., 2 * D :], held[2]]
        came = [partner(array, bit) for array, bit in zip(held, bits)]
        after = ()
        if place < lag:
            lifted = jnp.concatenate([lifted, partner(lifted, pair[0])], axis=0)
            for bit in plane[bounds[place] : bounds[place + 1]]:
                (ada,) = join([ada], [partner(ada, bit)], (bit,))
            after = (small, lifted, ada)
        if place == lag:
            left = list(reversed(along_z))
            rows = D >> lag
            line = (lax.axis_index("row") >> len(plane)) * rows
            lifted = lax.dynamic_slice_in_dim(lifted, line, rows, 2)
            product = mm(lifted.reshape(-1, rows), flat(ada))
            terms = (product.reshape(1 << lag, MICRO * SLOTS, 6 * D),)
            for bit in along_z:
                stays, goes = term_step(1 << left.index(bit), *terms)
                left.remove(bit)
                terms = (stays, partner(goes, bit))
            after = (terms[1],)
        if place < len(steps) - 1:
            held = join(held, came, bits, after)
        else:
            qk, vgd = [both(flat(array)) for array in join(held[:2], came[:2], bits[:2])]
            mods = both(sum(term[0] for term in terms) + b_ada[0])
            smalls = both(small)
            x = tokens
            *saved, gated = attn_forward(0, layouts, x, mods, smalls, qk, vgd)
            held = join(held[2:], came[2:], bits[2:], (gated,))
    upo, down = [both(flat(array)) for array in held]
    out_one, branch, down_raw = ffn_forward(0, layouts, x, mods, smalls, gated, upo, down)
    kept = [(x, saved, gated, branch, down_raw)]
    x = out_one[None]
    kept.append((x,))

    late, _ = lock(w_ada[0], out_one)
    ada_all = lax.all_gather(late, "row", axis=0, tiled=True)

    def halved(terms):
        if terms[0].ndim == 2:
            up_sum = terms[0].reshape(devices, shard, 2, FF // 2)
            down_sum = terms[1].reshape(devices, 2, 2, shard, D)
            terms = []
            for own in (section, 1 - section):
                up_half = lax.dynamic_index_in_dim(up_sum, own, 2, keepdims=False)
                down_half = lax.dynamic_index_in_dim(down_sum, own, 1, keepdims=False)
                terms.append(
                    jnp.concatenate([up_half, down_half[:, 0], down_half[:, 1]], axis=2)
                )
            terms[1] = terms[1].astype(bf16)
        return terms

    def by_row(array):
        return array.reshape(devices, shard, GROUP)

    def input_step(l, low, mid_grad, ffn_sums, mixer_sums, two=None, after=()):
        x = kept[l][0]
        return input_backward(
            l, layouts, x, mods, low, mid_grad, ffn_sums, mixer_sums, qk, vgd, two, after
        )

    def run(keep, came, bits, below=1, after=()):
        for bit in bits[:-1]:
            keep, sent = step(keep, came, bit, below, after)
            came = [(partner(sent, bit), len(keep))]
        return step(keep, came, bits[-1], below, after)

    def grown(mod, bits):
        for bit in bits:
            mod = misc_step(mod, partner(mod, bit))
        return mod

    x_bits, y_bits, z_bits = along_x, along_y, along_z
    (
        out_two, acts_sent, mid_grad, f2_sums, low, a2_keep, a2_sent, m2_sums, *terms
    ) = second_layer(
        layouts, x, mods, smalls, output_grad, qk, vgd, upo, down, devices
    )
    f2_keep, f2_sent = halved(terms)
    a2_keep, a2_sent = by_row(a2_keep), by_row(a2_sent)
    low, f2_sent, a2_sent, acts_sent = lock(low, f2_sent, a2_sent, acts_sent)
    f2_came = swap(f2_sent)
    a2_came = swap(a2_sent)
    acts_came = swap(acts_sent)
    gx_two, grad, mod_low_two, sums_two = input_step(1, low, mid_grad, f2_sums, m2_sums)
    grad, f2_came, a2_came, acts_came = lock(grad, f2_came, a2_came, acts_came)
    f2_keep, f2_sent = run([f2_keep], [(f2_came, 1)], x_bits)
    a2_keep, a2_sent = run([a2_keep], [(a2_came, 1)], y_bits, 1 << len(x_bits))
    grad, f2_sent, a2_sent = lock(grad, f2_sent, a2_sent)
    f2_came = partner(f2_sent, x_bits[-1])
    a2_came = partner(a2_sent, y_bits[-1])

    x, saved, gated, branch, down_raw = kept[0]
    mid_grad, branch_low, gwo, f1_sums, *terms = ffn_backward(
        0, layouts, x, mods, smalls, gated, branch, down_raw, grad[None], upo, down, devices
    )
    f1_keep, f1_sent = halved(terms)
    carried = (branch_low, gwo)
    *carried, f1_sent, f2_came, a2_came = lock(*carried, f1_sent, f2_came, a2_came)
    f1_came = swap(f1_sent)
    f2_keep, f2_sent = run(f2_keep, [(f2_came, 1)], y_bits)
    a2_keep, a2_sent = run(a2_keep, [(a2_came, 1)], x_bits)
    f1_keep, f1_sent = run([f1_keep], [(f1_came, 1)], x_bits)
    *carried, f2_sent, a2_sent, f1_sent = lock(*carried, f2_sent, a2_sent, f1_sent)
    f1_came = partner(f1_sent, x_bits[-1])
    a2_came = partner(a2_sent, x_bits[-1])
    f2_came = partner(f2_sent, y_bits[-1])
    low, a1_keep, a1_sent, m1_sums = mixer_backward(0, layouts, smalls, saved, *carried, upo)
    a1_keep, a1_sent = by_row(a1_keep), by_row(a1_sent)
    low, a1_sent, f2_came, a2_came, f1_came, ada_all = lock(
        low, a1_sent, f2_came, a2_came, f1_came, ada_all
    )
    a1_came = swap(a1_sent)
    two_keep, two_sent = run(f2_keep + a2_keep, [(f2_came, 1), (a2_came, 1)], z_bits[:1])
    f1_keep, f1_sent = run(f1_keep, [(f1_came, 1)], y_bits)
    a1_keep, a1_sent = run([a1_keep], [(a1_came, 1)], x_bits)
    low, two_sent, f1_sent, a1_sent = lock(low, two_sent, f1_sent, a1_sent)
    a1_came = partner(a1_sent, x_bits[-1])
    f1_came = partner(f1_sent, y_bits[-1])
    two_came = partner(two_sent, z_bits[0])
    gx_one, _, mod_low_one, sums_one, gx_sent, mod_mine, mod_sent = input_step(
        0, low, mid_grad, f1_sums, m1_sums, (gx_two, mod_low_two)
    )
    misc = pack_misc(conds, mod_low_one, mod_low_two, sums_one, sums_two)
    misc, a1_came, two_came, f1_came, gx_sent, mod_sent = lock(
        misc, a1_came, two_came, f1_came, gx_sent, mod_sent
    )

    a1_keep, a1_sent = run(a1_keep, [(a1_came, 1)], y_bits)
    a1_sent, misc = lock(a1_sent, misc)
    a1_came = partner(a1_sent, y_bits[-1])
    misc = grown(misc, tuple(reversed(z_bits))[:-1])
    gx_came = swap(gx_sent)
    mod_came = swap(mod_sent)
    keep, came = a1_keep + f1_keep, [(a1_came, 1), (f1_came, 1)]
    for place, bit in enumerate(z_bits):
        if place == 1:
            keep, came = keep + two_keep, came + [(two_came, 2)]
        keep, sent = step(keep, came, bit)
        if place == len(z_bits) - 1:
            sent, misc, gx_came, mod_came = lock(sent, misc, gx_came, mod_came)
        elif place == 0:
            sent, misc = lock(sent, misc)
        came = [(partner(sent, bit), len(keep))]
        if place == 0:
            misc = grown(misc, z_bits[:1] + x_bits[:-1] + y_bits[:-1])
    last = (1 << x_bits[-1], 1 << y_bits[-1])
    parts = [misc] + [across(misc, flips) for flips in (last[0], last[1], last[0] + last[1])]
    gx_out, gx_mark = both_micros(gx_one, gx_two, gx_came)
    acts_out, acts_mark = both_micros(out_one, out_two, acts_came)
    grad_lifted = lifted_grads(mod_mine, mod_came, ada_all)
    lifted_came = swap(grad_lifted)
    mine, other, small_mine, small_other = finish(
        keep, came, parts, (gx_mark, acts_mark, lifted_came)
    )
    came, small_came = swap(other), swap(small_other)
    (
        g_query, g_key, g_value, g_gate, g_out, g_decay, g_up, g_down, g_ada,
        g_b_ada, g_b_up, g_b_down, g_conv, g_b_decay,
    ) = outputs(mine, came, small_mine, small_came)

    grad_lifted = (grad_lifted + lifted_came).reshape(MICRO, SLOTS, D)
    _, pull_silu = jax.vjp(jax.nn.silu, conditions.astype(f32))
    (cond_grads,) = pull_silu(grad_lifted)

    return (
        acts_out[None],
        gx_out[None],
        cond_grads,
        g_ada[None],
        g_b_ada,
        g_query[None],
        g_key[None],
        g_value[None],
        g_gate[None],
        g_out[None],
        g_decay.transpose(1, 2, 0),
        g_b_decay,
        g_conv.transpose(1, 0, 2),
        g_up[None],
        g_b_up,
        g_down.reshape(1, FF // devices, D),
        g_b_down,
    )


def solution(mesh):
    rows = P(None, "row", None)
    mats = P("section", "row", None)
    vector = P("section", None)
    in_specs = (
        rows, rows, rows, P(None, "row"),
        mats, vector, mats, mats, mats, mats, mats, mats, vector, P("section", None, None),
        mats, vector, mats, vector,
    )
    blocks = P("section", None, "row", None)
    out_specs = (
        blocks, blocks, rows,
        mats, vector, mats, mats, mats, mats, mats, mats, vector, P("section", None, None),
        mats, vector, mats, vector,
    )
    return jax.shard_map(
        on_device, mesh=mesh, in_specs=in_specs, out_specs=out_specs, check_vma=False
    )
```

```python
import functools

import jax
import jax.numpy as jnp
from jax import lax
from jax.experimental import pallas as pl
from jax.experimental.pallas import tpu as pltpu
from jax.sharding import PartitionSpec as P

D = 384
HEADS = 6
HEAD_DIM = 64
FF = 1536
MICRO = 2
ROWS = 512
HALF = 256
SLOTS = 2
PAIR = 128
PAIRS = D // PAIR
QKVG = 4 * D
LANES = 128
GROUP = (QKVG + D + LANES) // 2
NEG = -1e30
SCALE = HEAD_DIM**-0.5

bf16 = jnp.bfloat16
f32 = jnp.float32


def mm(left, right):
    return jnp.dot(left, right, preferred_element_type=f32)


def mm_t(left, right):
    return lax.dot_general(left, right, (((1,), (1,)), ((), ())), preferred_element_type=f32)


def split(values):
    high = values.astype(bf16)
    return high, (values - high.astype(f32)).astype(bf16)


def split_three(values):
    high, rest = split(values)
    mid = values - high.astype(f32)
    middle, low = split(mid)
    return high, middle, low


def cat_left(values):
    high, low = split(values)
    return jnp.concatenate([high, low, high], axis=1)


def cat_right(values):
    high, low = split(values)
    return jnp.concatenate([high, high, low], axis=1)


def mm_near(left, right_pair, right_high):
    high, low = split(left)
    wide = mm(high, right_pair)
    return wide[:, :PAIR] + wide[:, PAIR:] + mm(low, right_high)


def lane_iota(rows, columns):
    return lax.broadcasted_iota(jnp.int32, (rows, columns), 1)


def row_iota(rows, columns):
    return lax.broadcasted_iota(jnp.int32, (rows, columns), 0)


def order_matrix(start, rows, wide, to_scan):
    t = row_iota(rows, ROWS) + start
    small = (t & 256) + ((t & 15) << 4) + ((t & 255) >> 4)
    if to_scan:
        large = ((t & 15) << 5) + (t >> 4)
    else:
        large = ((t & 31) << 4) + (t >> 5)
    source = jnp.where(wide, large, small)
    return jnp.where(lane_iota(rows, ROWS) == source, 1.0, 0.0).astype(bf16)


def normalise(values):
    centred = values - jnp.mean(values, axis=-1, keepdims=True)
    rate = lax.rsqrt(jnp.mean(centred * centred, axis=-1, keepdims=True) + 1e-06)
    return centred * rate, rate


def normalise_back(normal, rate, grad):
    return rate * (
        grad
        - jnp.mean(grad, axis=-1, keepdims=True)
        - normal * jnp.mean(grad * normal, axis=-1, keepdims=True)
    )


class In:
    def __init__(self, copy, kept):
        self.copy = copy
        self.kept = kept

    def __call__(self):
        if self.copy is not None:
            self.copy.wait()
            self.copy = None
        return self.kept


class Kernel:
    def __init__(self, layer, layouts):
        self.layer = layer
        self.section = lax.axis_index("section")
        self.own = self.section == layer
        self.layout = layouts[self.section, 0]
        self.wide = self.layout == 0
        self.live_rows = jnp.where(self.wide, ROWS, self.layout * HALF)
        self.pushed = {}

    def load(self, kind, refs, kept, sem):
        if kind == "own":
            mine, other = refs

            @pl.when(self.own)
            def _():
                pltpu.make_async_copy(mine, kept, sem).start()

            @pl.when(jnp.logical_not(self.own))
            def _():
                pltpu.make_async_copy(other, kept, sem).start()

            return In(pltpu.make_async_copy(mine, kept, sem), kept)
        (source,) = refs
        if kind == "micro":
            source = source.at[self.section if source.shape[0] == MICRO else 0]
        copy = pltpu.make_async_copy(source, kept, sem)
        copy.start()
        return In(copy, kept)

    def push(self, name):
        if name not in self.results:
            return
        kept, target, sem = self.results[name]
        copy = pltpu.make_async_copy(kept, target, sem)
        copy.start()
        self.pushed[name] = copy

    def finish(self):
        for name in self.results:
            if name not in self.pushed:
                self.push(name)
        for copy in self.pushed.values():
            copy.wait()

    def slot(self, half):
        return jnp.where(self.wide, 0, half)

    def share(self, slot, part):
        row = pl.ds(2 * self.section + slot, 1)
        return self.mods()[row, part * D : (part + 1) * D]

    def bu(self):
        return self.small()[0:1, :]

    def bn(self):
        return self.small()[1:2, :D]

    def ck(self, tap):
        return self.small()[2 + tap : 3 + tap, :D]

    def bd(self):
        return self.small()[5:6, :LANES]


def sigmoid(values):
    return 1.0 / (1.0 + jnp.exp(-values))


GELU_A = 0.7978845608028654
GELU_B = 0.044715


def gelu_parts(values):
    square = values * values
    tanh = jnp.tanh(GELU_A * values * (1.0 + GELU_B * square))
    return square, tanh


def fill_bias(bias, wide):
    bias[:, :HALF] = jnp.full((HALF, HALF), 0.0, f32) + jnp.where(wide, 0.0, NEG)
    causal = row_iota(HALF, HALF) >= lane_iota(HALF, HALF)
    bias[:, HALF:] = jnp.where(causal, 0.0, NEG)


def decay_factors(cum, cumt, bias, head):
    row = cumt[pl.ds(head, 1), :]
    lanes = lane_iota(1, LANES)
    column = jnp.sum(jnp.where(lanes == head, cum[...], 0.0), axis=1, keepdims=True)
    first = jnp.exp(column[:HALF] - row[:, :HALF] + bias[:, HALF:])
    second = jnp.exp(column[HALF:] - row + bias[...])
    return first, second


def head_norm(values, lanes):
    square = values * values
    low = jnp.sum(jnp.where(lanes < HEAD_DIM, square, 0.0), axis=1, keepdims=True)
    high = jnp.sum(jnp.where(lanes < HEAD_DIM, 0.0, square), axis=1, keepdims=True)
    return jnp.where(lanes < HEAD_DIM, low, high) * (1.0 / HEAD_DIM)


def fill_decay(dp, bd, cum, cumt):
    raw = dp[...] + bd
    log_decay = (jnp.minimum(raw, 0.0) - jnp.log1p(jnp.exp(-jnp.abs(raw)))) * (1.0 / 16.0)
    high, middle, low = split_three(log_decay)
    causal = jnp.where(row_iota(ROWS, ROWS) >= lane_iota(ROWS, ROWS), 1.0, 0.0).astype(bf16)
    cum[...] = mm(causal, high) + mm(causal, middle) + mm(causal, low)
    cumt[...] = jnp.transpose(cum[...])


def columns(index, first=0):
    return slice(index * PAIR + first, index * PAIR + first + PAIR)


def attn_forward_body(k):
    flip = k.layer == 1
    wide = k.wide
    x = k.x()
    k.mods()

    def first(i, carry):
        rows = pl.ds(pl.multiple_of(i * HALF, HALF), HALF)
        slot = k.slot(i)
        normal, _ = normalise(x[rows, :].astype(f32))
        k.inner[rows, :] = (normal * (1.0 + k.share(slot, 1)) + k.share(slot, 0)).astype(bf16)
        return carry

    lax.fori_loop(0, 2, first, 0)
    w_qk = k.w_qk()
    w_vgd = k.w_vgd()

    def project(i, carry):
        start = i * HALF
        rows = pl.ds(start, HALF)
        if flip:
            part = mm(order_matrix(start, HALF, wide, True), k.inner[...]).astype(bf16)
        else:
            part = k.inner[rows, :]
        k.ordered[rows, :] = part
        k.qkvg[rows, : 2 * D] = mm(part, w_qk[...])
        k.qkvg[rows, 2 * D :] = mm(part, w_vgd[:, : 2 * D])
        k.dp[rows, :] = mm(part, w_vgd[:, 2 * D :])
        return carry

    lax.fori_loop(0, 2, project, 0)
    k.small()
    for name in ("ordered", "qkvg", "dp"):
        k.push(name)
    fill_decay(k.dp, k.bd(), k.cum, k.cumt)
    fill_bias(k.bias, wide)

    vpad = k.vpad
    vpad[0:8, :] = jnp.zeros((8, D), f32)
    vpad[8 : 8 + ROWS, :] = k.qkvg[:, 2 * D : 3 * D]
    position = row_iota(ROWS, 1) & jnp.where(wide, ROWS - 1, HALF - 1)
    one = jnp.where(position >= 1, vpad[7 : 7 + ROWS, :], 0.0)
    two = jnp.where(position >= 2, vpad[6 : 6 + ROWS, :], 0.0)
    k.vc[...] = k.ck(0) * vpad[8 : 8 + ROWS, :] + k.ck(1) * one + k.ck(2) * two
    for name in ("cum", "cumt", "vc"):
        k.push(name)

    def pair(p, carry):
        lanes = lane_iota(1, PAIR)
        queries = cat_left(k.qkvg[:, columns(p)] * SCALE)
        keys = k.qkvg[:, columns(p, D)]
        value_high, value_low = split(k.vc[:, columns(p)])
        values = jnp.concatenate([value_high, value_low], axis=1)
        parts = []
        for e in range(2):
            key_cat = cat_right(jnp.where((lanes // HEAD_DIM) == e, keys, 0.0))
            first, second = decay_factors(k.cum, k.cumt, k.bias, 2 * p + e)
            first = first * mm_t(queries[:HALF], key_cat[:HALF])
            second = second * mm_t(queries[HALF:], key_cat)
            parts.append(
                jnp.concatenate(
                    [
                        mm_near(first, values[:HALF], value_high[:HALF]),
                        mm_near(second, values, value_high),
                    ],
                    axis=0,
                )
            )
        total = jnp.where(lanes < HEAD_DIM, parts[0], parts[1])
        k.o[:, columns(p)] = total
        gate = k.qkvg[:, columns(p, 3 * D)]
        normed = total * lax.rsqrt(head_norm(total, lanes) + 1.0)
        mixed = (normed * (gate * sigmoid(gate))).astype(bf16)
        if flip:
            k.inner[:, columns(p)] = mixed
        else:
            k.gated[:, columns(p)] = mixed
        return carry

    for p in range(PAIRS):
        pair(p, 0)
    k.push("o")
    if flip:

        def back(i, carry):
            start = i * HALF
            k.gated[pl.ds(start, HALF), :] = mm(
                order_matrix(start, HALF, wide, False), k.inner[...]
            ).astype(bf16)
            return carry

        lax.fori_loop(0, 2, back, 0)


def ffn_forward_body(k):
    gated, x = k.gated(), k.x()
    k.mods(), k.small()

    def tile(i, carry):
        start = i * HALF
        rows = pl.ds(start, HALF)
        slot = k.slot(i)
        grown = mm(gated[rows, :], k.wo()[...])
        k.branch[rows, :] = grown
        middle = x[rows, :].astype(f32) + k.share(slot, 2) * grown
        normal, _ = normalise(middle)
        inner = (normal * (1.0 + k.share(slot, 4)) + k.share(slot, 3)).astype(bf16)
        up = mm(inner, k.wu()[...]) + k.bu()
        _, tanh = gelu_parts(up)
        hidden = (0.5 * up * (1.0 + tanh)).astype(bf16)
        low = mm(hidden, k.wn()[...])
        k.down[rows, :] = low
        result = middle + k.share(slot, 5) * (low + k.bn())
        live = (row_iota(HALF, 1) + start) < k.live_rows
        k.out[rows, :] = jnp.where(live, result, 0.0).astype(bf16)
        return carry

    for i in range(2):
        tile(i, 0)


def ffn_backward_body(k):
    gmod, gbu, gbn = k.gmod, k.gbu, k.gbn
    gmod[...] = jnp.zeros(gmod.shape, f32)
    gbu[...] = jnp.zeros(gbu.shape, f32)
    gbn[...] = jnp.zeros(gbn.shape, f32)
    both_ways = k.layer == 1
    k.mods(), k.small()
    x, grad = k.x(), k.grad()
    if both_ways:
        gated, wo = k.gated(), k.wo()
    else:
        branch, down = k.branch(), k.down()

    def tile(i, carry):
        start = i * HALF
        rows = pl.ds(start, HALF)
        slot = k.slot(i)

        def add(part, values):
            where = (pl.ds(slot, 1), slice((part - 2) * D, (part - 1) * D))
            gmod[where] = gmod[where] + jnp.sum(values, axis=0, keepdims=True)

        grown = mm(gated[rows, :], wo[...]) if both_ways else branch[rows, :]
        middle = x[rows, :].astype(f32) + k.share(slot, 2) * grown
        normal, rate = normalise(middle)
        inner = (normal * (1.0 + k.share(slot, 4)) + k.share(slot, 3)).astype(bf16)
        k.inner_s[rows, :] = inner
        up = mm(inner, k.wu()[...]) + k.bu()
        square, tanh = gelu_parts(up)
        half = 0.5 * (1.0 + tanh)
        hidden = (up * half).astype(bf16)
        k.hidden_s[rows, :] = hidden
        lower = (mm(hidden, k.wn()[...]) if both_ways else down[rows, :]) + k.bn()
        live = (row_iota(HALF, 1) + start) < k.live_rows
        if both_ways:
            result = middle + k.share(slot, 5) * lower
            k.out[rows, :] = jnp.where(live, result, 0.0).astype(bf16)
        above = jnp.where(live, grad[rows, :].astype(f32), 0.0)
        add(5, above * lower)
        grad_down = above * k.share(slot, 5)
        gbn[...] = gbn[...] + jnp.sum(grad_down, axis=0, keepdims=True)
        down_low = grad_down.astype(bf16)
        k.down_s[rows, :] = down_low
        slope = half + 0.5 * up * (1.0 - tanh * tanh) * (
            GELU_A * (1.0 + 3.0 * GELU_B * square)
        )
        grad_up = mm_t(down_low, k.wn()[...]) * slope
        gbu[...] = gbu[...] + jnp.sum(grad_up, axis=0, keepdims=True)
        up_low = grad_up.astype(bf16)
        k.up_s[rows, :] = up_low
        grad_inner = mm_t(up_low, k.wu()[...])
        add(3, grad_inner)
        add(4, grad_inner * normal)
        grad_middle = above + normalise_back(
            normal, rate, grad_inner * (1.0 + k.share(slot, 4))
        )
        k.mid_grad[rows, :] = grad_middle
        add(2, grad_middle * grown)
        k.branch_low[rows, :] = (grad_middle * k.share(slot, 2)).astype(bf16)
        return carry

    for i in range(2):
        tile(i, 0)
    k.push("mid_grad")
    k.push("branch_low")
    if both_ways:
        own = k.section == 0
        k.sent[...] = jnp.where(own, k.out[...].astype(f32), x[...].astype(f32)).astype(bf16)
        k.push("out")
        k.push("sent")

    def weights(j, carry):
        part = pl.ds(pl.multiple_of(j * HALF, HALF), HALF)
        hidden_t = jnp.transpose(k.hidden_s[:, part].astype(f32)).astype(bf16)
        k.gwn[part, :] = mm(hidden_t, k.down_s[...])
        return carry

    lax.fori_loop(0, FF // HALF, weights, 0)
    inner_t = jnp.transpose(k.inner_s[...].astype(f32)).astype(bf16)
    if k.packed:
        devices, shard, _ = k.keep.shape

        def halves(j, carry):
            for kept, own in ((k.keep, c_section), (k.gone, 1 - c_section)):
                columns = pl.ds(pl.multiple_of(j * HALF + own * (FF // 2), HALF), HALF)
                here = pl.ds(pl.multiple_of(j * HALF, HALF), HALF)
                part = mm(inner_t, k.up_s[:, columns]).reshape(devices, shard, HALF)
                kept[:, :, here] = part.astype(kept.dtype)
            return carry

        c_section = k.section
        lax.fori_loop(0, FF // 2 // HALF, halves, 0)

        def owner(r, carry):
            for kept, own in ((k.keep, c_section), (k.gone, 1 - c_section)):
                for piece in range(2):
                    start = pl.multiple_of((4 * r + 2 * own + piece) * shard, 8)
                    rows = k.gwn[pl.ds(start, shard), :]
                    at = FF // 2 + piece * D
                    kept[r, :, at : at + D] = rows.astype(kept.dtype)
            return carry

        lax.fori_loop(0, devices, owner, 0)
        k.push("keep")
        k.push("gone")
    else:
        k.gwu[...] = mm(inner_t, k.up_s[...])
    gated = k.gated()
    k.gwo[...] = mm(jnp.transpose(gated[...].astype(f32)).astype(bf16), k.branch_low[...])

    short = jnp.concatenate([gbn[...], jnp.zeros((1, FF - D), f32)], axis=1)
    k.sums[...] = jnp.concatenate(
        [gmod[0:SLOTS, :], gbu[...], short, jnp.zeros((4, FF), f32)], axis=0
    )


def mixer_backward_body(k):
    flip = k.layer == 1
    wide = k.wide
    mixed_s, low, dv_s, rows_s, cols_s = k.mixed_s, k.low, k.dv_s, k.rows_s, k.cols_s
    fill_bias(k.bias, wide)
    branch_low, wo = k.branch_low(), k.wo()

    def first(i, carry):
        start = i * HALF
        rows = pl.ds(start, HALF)
        if flip:
            part = mm(order_matrix(start, HALF, wide, True), branch_low[...]).astype(bf16)
        else:
            part = branch_low[rows, :]
        mixed_s[rows, :] = mm_t(part, wo[...])
        return carry

    lax.fori_loop(0, 2, first, 0)
    rows_s[...] = jnp.zeros(rows_s.shape, f32)
    cols_s[...] = jnp.zeros(cols_s.shape, f32)
    qkvg, vc, cum, cumt, o = k.qkvg(), k.vc(), k.cum(), k.cumt(), k.o()
    k.small()

    def pair(p, carry):
        lanes = lane_iota(1, PAIR)
        total = o[:, columns(p)]
        gate = qkvg[:, columns(p, 3 * D)]
        above = mixed_s[:, columns(p)]
        rate = lax.rsqrt(head_norm(total, lanes) + 1.0)
        sig = sigmoid(gate)
        grad_gate = above * (total * rate) * (sig * (1.0 + gate * (1.0 - sig)))
        low[:, columns(p, 3 * D)] = grad_gate.astype(bf16)
        grad_normed = above * (gate * sig)
        product = grad_normed * total
        inside = jnp.where(
            lanes < HEAD_DIM,
            jnp.sum(jnp.where(lanes < HEAD_DIM, product, 0.0), axis=1, keepdims=True),
            jnp.sum(jnp.where(lanes < HEAD_DIM, 0.0, product), axis=1, keepdims=True),
        ) * (1.0 / HEAD_DIM)
        grad_o = rate * grad_normed - total * (rate * rate * rate) * inside

        queries = qkvg[:, columns(p)] * SCALE
        keys = qkvg[:, columns(p, D)]
        values = vc[:, columns(p)]
        query_cat = cat_left(queries)
        grad_cat = cat_left(grad_o)
        key_high, key_low = split(keys)
        key_pair = jnp.concatenate([key_high, key_low], axis=1)
        query_t = jnp.transpose(queries)
        grad_t = jnp.transpose(grad_o)
        grad_q = []
        grad_k = []
        grad_v = []
        for e in range(2):
            mine = (lanes // HEAD_DIM) == e
            head = 2 * p + e
            key_cat = cat_right(jnp.where(mine, keys, 0.0))
            value_cat = cat_right(jnp.where(mine, values, 0.0))
            first, second = decay_factors(cum, cumt, k.bias, head)
            raw_first = mm_t(query_cat[:HALF], key_cat[:HALF])
            raw_second = mm_t(query_cat[HALF:], key_cat)
            grad_first = first * mm_t(grad_cat[:HALF], value_cat[:HALF])
            grad_second = second * mm_t(grad_cat[HALF:], value_cat)
            score_first = raw_first * first
            score_second = raw_second * second
            pull_first = grad_first * raw_first
            pull_second = grad_second * raw_second
            here = lanes == head
            rows_s[:HALF, :] = rows_s[:HALF, :] + jnp.where(
                here, jnp.sum(pull_first, axis=1, keepdims=True), 0.0
            )
            rows_s[HALF:, :] = rows_s[HALF:, :] + jnp.where(
                here, jnp.sum(pull_second, axis=1, keepdims=True), 0.0
            )
            low_cols = jnp.sum(pull_second, axis=0, keepdims=True)
            cols_s[pl.ds(head, 1), :HALF] = low_cols[:, :HALF] + jnp.sum(
                pull_first, axis=0, keepdims=True
            )
            cols_s[pl.ds(head, 1), HALF:] = low_cols[:, HALF:]
            grad_q.append(
                jnp.concatenate(
                    [
                        mm_near(grad_first, key_pair[:HALF], key_high[:HALF]),
                        mm_near(grad_second, key_pair, key_high),
                    ],
                    axis=0,
                )
            )

            def turned(source_t, block_first, block_second):
                high, low = split(source_t[e * HEAD_DIM : (e + 1) * HEAD_DIM, :])
                both = jnp.concatenate([high, low], axis=0)
                first_high, first_low = split(block_first)
                second_high, second_low = split(block_second)
                one = mm(both[:, :HALF], first_high)
                one = one[:HEAD_DIM] + one[HEAD_DIM:] + mm(high[:, :HALF], first_low)
                two = mm(both[:, HALF:], second_high)
                two = two[:HEAD_DIM] + two[HEAD_DIM:] + mm(high[:, HALF:], second_low)
                return jnp.concatenate([two[:, :HALF] + one, two[:, HALF:]], axis=1)

            grad_k.append(turned(query_t, grad_first, grad_second))
            grad_v.append(turned(grad_t, score_first, score_second))
        query_grad = jnp.where(lanes < HEAD_DIM, grad_q[0], grad_q[1]) * SCALE
        low[:, columns(p)] = query_grad.astype(bf16)
        low[:, columns(p, D)] = jnp.transpose(jnp.concatenate(grad_k, axis=0)).astype(bf16)
        dv_s[:ROWS, columns(p)] = jnp.transpose(jnp.concatenate(grad_v, axis=0))
        return carry

    for p in range(PAIRS):
        pair(p, 0)

    pulled = rows_s[...] - jnp.transpose(cols_s[...])
    high, middle, rest = split_three(pulled)
    upper_first = jnp.concatenate(
        [
            jnp.where(row_iota(HALF, HALF) <= lane_iota(HALF, HALF), 1.0, 0.0),
            jnp.full((HALF, HALF), 0.0, f32) + jnp.where(wide, 1.0, 0.0),
        ],
        axis=1,
    ).astype(bf16)
    upper_second = upper_first[:, :HALF]
    later = jnp.concatenate(
        [
            mm(upper_first, high) + mm(upper_first, middle) + mm(upper_first, rest),
            mm(upper_second, high[HALF:]) + mm(upper_second, middle[HALF:])
            + mm(upper_second, rest[HALF:]),
        ],
        axis=0,
    )
    grad_dp = later * (1.0 / 16.0) * sigmoid(-(k.dp()[...] + k.bd()))
    grad_bd = jnp.sum(grad_dp, axis=0, keepdims=True)
    low[:, QKVG:] = grad_dp.astype(bf16)

    dv_s[ROWS:, :] = jnp.zeros((8, D), f32)
    position = row_iota(ROWS, 1) & jnp.where(wide, ROWS - 1, HALF - 1)
    last = jnp.where(wide, ROWS - 1, HALF - 1)
    here = dv_s[0:ROWS, :]
    one = jnp.where(position <= last - 1, dv_s[1 : 1 + ROWS, :], 0.0)
    two = jnp.where(position <= last - 2, dv_s[2 : 2 + ROWS, :], 0.0)
    value = qkvg[:, 2 * D : 3 * D]
    low[:, 2 * D : 3 * D] = (k.ck(0) * here + k.ck(1) * one + k.ck(2) * two).astype(bf16)
    k.push("low")

    taps = [jnp.sum(rows * value, axis=0, keepdims=True) for rows in (here, one, two)]
    rest = jnp.concatenate([grad_bd, jnp.zeros((1, D - LANES), f32)], axis=1)
    k.sums[...] = jnp.concatenate([*taps, rest, jnp.zeros((4, D), f32)], axis=0)

    ordered_t = jnp.transpose(k.ordered()[...].astype(f32)).astype(bf16)
    gwo = k.gwo()
    gw = k.gw

    def weights(j, carry):
        part = pl.ds(pl.multiple_of(j * HALF, HALF), HALF)
        gw[:, part] = mm(ordered_t, low[:, part])
        return carry

    lax.fori_loop(0, QKVG // HALF, weights, 0)
    gw[:, QKVG : QKVG + D] = gwo[...]
    gw[:, QKVG + D :] = mm(ordered_t, low[:, QKVG:])

    def halves(j, carry):
        here = pl.ds(pl.multiple_of(j * HALF, HALF), HALF)
        keep = pl.ds(pl.multiple_of(j * HALF + k.section * GROUP, HALF), HALF)
        send = pl.ds(pl.multiple_of(j * HALF + (1 - k.section) * GROUP, HALF), HALF)
        k.gw_keep[:, here] = gw[:, keep]
        k.gw_send[:, here] = gw[:, send].astype(bf16)
        return carry

    lax.fori_loop(0, GROUP // HALF, halves, 0)


def second_layer_body(k):
    attn_forward_body(k)
    for name in ("ordered", "qkvg", "dp", "vc", "cum", "cumt", "o", "gated"):
        setattr(k, name, In(None, getattr(k, name)))
    ffn_backward_body(k)
    for name in ("branch_low", "gwo"):
        setattr(k, name, In(None, getattr(k, name)))
    k.sums = k.mixer_sums
    mixer_backward_body(k)


def input_backward_body(k):
    flip = k.layer == 1
    wide = k.wide
    gmod, mixed_s, perm_s = k.gmod, k.mixed_s, k.perm_s
    gmod[...] = jnp.zeros(gmod.shape, f32)
    low, w_qk, w_vgd = k.low(), k.w_qk(), k.w_vgd()

    def inner_grad(i, carry):
        rows = pl.ds(pl.multiple_of(i * HALF, HALF), HALF)
        mixed_s[rows, :] = mm_t(low[rows, : 2 * D], w_qk[...]) + mm_t(
            low[rows, 2 * D :], w_vgd[...]
        )
        return carry

    lax.fori_loop(0, 2, inner_grad, 0)
    if flip:
        high, middle, rest = split_three(mixed_s[...])
        perm_s[:, :D] = high
        perm_s[:, D : 2 * D] = middle
        perm_s[:, 2 * D :] = rest
    x, mid_grad = k.x(), k.mid_grad()
    k.mods()

    def tile(i, carry):
        start = i * HALF
        rows = pl.ds(start, HALF)
        slot = k.slot(i)
        if flip:
            three = mm(order_matrix(start, HALF, wide, False), perm_s[...])
            grad = three[:, :D] + three[:, D : 2 * D] + three[:, 2 * D :]
        else:
            grad = mixed_s[rows, :]
        normal, rate = normalise(x[rows, :].astype(f32))
        where = (pl.ds(slot, 1), slice(0, D))
        gmod[where] = gmod[where] + jnp.sum(grad, axis=0, keepdims=True)
        where = (pl.ds(slot, 1), slice(D, 2 * D))
        gmod[where] = gmod[where] + jnp.sum(grad * normal, axis=0, keepdims=True)
        total = mid_grad[rows, :] + normalise_back(normal, rate, grad * (1.0 + k.share(slot, 1)))
        k.gx[rows, :] = total
        k.gx_low[rows, :] = total.astype(bf16)
        return carry

    for i in range(2):
        tile(i, 0)
    k.push("gx_low")
    k.push("gx")
    ffn, mixer = k.ffn_sums(), k.mixer_sums()
    k.mod_low[...] = jnp.concatenate([gmod[...], ffn[...]], axis=1).astype(bf16)
    if k.layer == 0:
        first = k.section == 0
        k.gx_send[...] = jnp.where(first, k.gx_two()[...], k.gx[...])
        one, two = k.mod_low[...].astype(f32), k.mod_two()[...].astype(f32)
        k.mod_mine[...] = jnp.where(first, one, two).astype(bf16)
        k.mod_send[...] = jnp.where(first, two, one).astype(bf16)
    half = 2 * D
    rest = ffn[0:1, :] + ffn[1:2, :]
    k.sums[...] = jnp.concatenate(
        [
            gmod[0:1, :] + gmod[1:2, :],
            rest[:, :half],
            rest[:, half:],
            ffn[2:3, :half],
            ffn[2:3, half:],
            jnp.concatenate([ffn[3:4, :D], mixer[0:1, :]], axis=1),
            jnp.concatenate([mixer[1:2, :], mixer[2:3, :]], axis=1),
            jnp.concatenate([mixer[3:4, :], jnp.zeros((1, D), f32)], axis=1),
        ],
        axis=0,
    )


ANY = pl.BlockSpec(memory_space=pl.ANY)
VMEM = pl.BlockSpec(memory_space=pltpu.VMEM)
HBM = pl.BlockSpec(memory_space=pltpu.HBM)


def call(body, layer, layouts, ins, outs, scratch, flops, packed=None, after=()):
    arrays = []
    counts = []
    kept = []
    places = []
    for kind, given, part in ins.values():
        places.extend([ANY] * 2 if kind == "own" else [HBM])
        given = given if kind == "own" else (given,)
        arrays.extend(given)
        counts.append(len(given))
        rows, wide = given[0].shape[-2:]
        start, stop = part or (0, wide)
        kept.append(pltpu.VMEM((rows, stop - start), given[0].dtype))

    def kernel(*refs):
        refs = list(refs)
        take = lambda count: [refs.pop(0) for _ in range(count)]
        (layouts_ref,) = take(1)
        sources = [take(count) for count in counts]
        take(len(after))
        targets = take(len(outs))
        buffers = take(len(ins))
        results = take(len(outs))
        rest = take(len(scratch))
        in_sems, out_sems = refs
        k = Kernel(layer, layouts_ref)
        k.packed = packed
        for number, (name, (kind, _, part)) in enumerate(ins.items()):
            given = sources[number]
            if part is not None:
                given = [ref.at[:, part[0] : part[1]] for ref in given]
            setattr(k, name, k.load(kind, given, buffers[number], in_sems.at[number]))
        k.results = {}
        for number, name in enumerate(outs):
            setattr(k, name, results[number])
            k.results[name] = (results[number], targets[number], out_sems.at[number])
        for name, ref in zip(scratch, rest):
            setattr(k, name, ref)
        body(k)
        k.finish()

    return pl.pallas_call(
        kernel,
        out_shape=[jax.ShapeDtypeStruct(shape, kind) for shape, kind, _ in outs.values()],
        in_specs=[pl.BlockSpec(memory_space=pltpu.SMEM)] + places + [ANY] * len(after),
        out_specs=[HBM if for_kernel else ANY for _, _, for_kernel in outs.values()],
        scratch_shapes=kept
        + [pltpu.VMEM(shape, kind) for shape, kind, _ in outs.values()]
        + [pltpu.VMEM(shape, kind) for shape, kind in scratch.values()]
        + [pltpu.SemaphoreType.DMA((len(ins),)), pltpu.SemaphoreType.DMA((len(outs),))],
        compiler_params=pltpu.CompilerParams(vmem_limit_bytes=56 * 1024 * 1024),
        cost_estimate=pl.CostEstimate(flops=flops, bytes_accessed=4 << 20, transcendentals=0),
    )(layouts, *arrays, *after)


def own(pair, part=None):
    return ("own", pair, part)


def plain(array):
    return ("plain", array, None)


def micro(array):
    return ("micro", array, None)


AT_UP = (0, FF)
AT_OUT = (FF, FF + D)


def attn_forward(layer, layouts, x, mods, small, qk, vgd):
    return call(
        attn_forward_body,
        layer,
        layouts,
        dict(
            x=micro(x),
            mods=own(mods),
            w_qk=own(qk),
            w_vgd=own(vgd),
            small=own(small),
        ),
        dict(
            ordered=((ROWS, D), bf16, True),
            qkvg=((ROWS, QKVG), f32, True),
            dp=((ROWS, LANES), f32, True),
            vc=((ROWS, D), f32, True),
            cum=((ROWS, LANES), f32, True),
            cumt=((LANES, ROWS), f32, True),
            o=((ROWS, D), f32, True),
            gated=((ROWS, D), bf16, True),
        ),
        dict(
            inner=((ROWS, D), bf16),
            vpad=((ROWS + 8, D), f32),
            bias=((HALF, ROWS), f32),
        ),
        4 * 10**9,
    )


def ffn_forward(layer, layouts, x, mods, small, gated, upo, down):
    return call(
        ffn_forward_body,
        layer,
        layouts,
        dict(
            gated=plain(gated),
            x=micro(x),
            wo=own(upo, AT_OUT),
            mods=own(mods),
            small=own(small),
            wu=own(upo, AT_UP),
            wn=own(down),
        ),
        dict(
            out=((ROWS, D), bf16, True),
            branch=((ROWS, D), f32, True),
            down=((ROWS, D), f32, True),
        ),
        {},
        3 * 10**9,
    )


def ffn_backward(
    layer, layouts, x, mods, small, gated, branch, down_raw, grad, upo, down, devices, after=()
):
    shard = D // devices
    in_kernel = shard % 8 == 0
    if in_kernel:
        sums = dict(
            keep=((devices, shard, FF), f32, True),
            gone=((devices, shard, FF), bf16, False),
        )
    else:
        sums = dict(gwu=((D, FF), f32, False), gwn=((FF, D), f32, False))
    return call(
        ffn_backward_body,
        layer,
        layouts,
        dict(
            mods=own(mods),
            small=own(small),
            x=micro(x),
            **(
                dict(gated=plain(gated), wo=own(upo, AT_OUT))
                if layer == 1
                else dict(branch=plain(branch), down=plain(down_raw))
            ),
            grad=micro(grad),
            wu=own(upo, AT_UP),
            wn=own(down),
            **(dict(gated=plain(gated)) if layer == 0 else {}),
        ),
        dict(
            **(
                dict(out=((ROWS, D), bf16, True), sent=((ROWS, D), bf16, False))
                if layer == 1
                else {}
            ),
            mid_grad=((ROWS, D), f32, True),
            branch_low=((ROWS, D), bf16, True),
            gwo=((D, D), f32, True),
            sums=((8, FF), f32, True),
            **sums,
        ),
        dict(
            **({"gwn": ((FF, D), f32)} if in_kernel else {}),
            hidden_s=((ROWS, FF), bf16),
            inner_s=((ROWS, D), bf16),
            up_s=((ROWS, FF), bf16),
            down_s=((ROWS, D), bf16),
            gmod=((8, FF), f32),
            gbu=((1, FF), f32),
            gbn=((1, D), f32),
        ),
        5 * 10**9,
        packed=in_kernel,
        after=after,
    )


def second_layer(layouts, x, mods, small, grad, qk, vgd, upo, down, devices):
    shard = D // devices
    in_kernel = shard % 8 == 0
    if in_kernel:
        sums = dict(
            keep=((devices, shard, FF), f32, True),
            gone=((devices, shard, FF), bf16, False),
        )
    else:
        sums = dict(gwu=((D, FF), f32, False), gwn=((FF, D), f32, False))
    return call(
        second_layer_body,
        1,
        layouts,
        dict(
            x=micro(x),
            mods=own(mods),
            w_qk=own(qk),
            w_vgd=own(vgd),
            small=own(small),
            wo=own(upo, AT_OUT),
            grad=micro(grad),
            wu=own(upo, AT_UP),
            wn=own(down),
        ),
        dict(
            out=((ROWS, D), bf16, True),
            sent=((ROWS, D), bf16, False),
            mid_grad=((ROWS, D), f32, True),
            sums=((8, FF), f32, True),
            low=((ROWS, QKVG + LANES), bf16, True),
            gw_keep=((D, GROUP), f32, True),
            gw_send=((D, GROUP), bf16, False),
            mixer_sums=((8, D), f32, True),
            **sums,
        ),
        dict(
            ordered=((ROWS, D), bf16),
            qkvg=((ROWS, QKVG), f32),
            dp=((ROWS, LANES), f32),
            vc=((ROWS, D), f32),
            cum=((ROWS, LANES), f32),
            cumt=((LANES, ROWS), f32),
            o=((ROWS, D), f32),
            gated=((ROWS, D), bf16),
            inner=((ROWS, D), bf16),
            vpad=((ROWS + 8, D), f32),
            bias=((HALF, ROWS), f32),
            branch_low=((ROWS, D), bf16),
            gwo=((D, D), f32),
            **({"gwn": ((FF, D), f32)} if in_kernel else {}),
            hidden_s=((ROWS, FF), bf16),
            inner_s=((ROWS, D), bf16),
            up_s=((ROWS, FF), bf16),
            down_s=((ROWS, D), bf16),
            gmod=((8, FF), f32),
            gbu=((1, FF), f32),
            gbn=((1, D), f32),
            mixed_s=((ROWS, D), f32),
            dv_s=((ROWS + 8, D), f32),
            rows_s=((ROWS, LANES), f32),
            cols_s=((LANES, ROWS), f32),
            gw=((D, 2 * GROUP), f32),
        ),
        14 * 10**9,
        packed=in_kernel,
    )


def mixer_backward(layer, layouts, small, saved, branch_low, gwo, upo, after=()):
    ordered, qkvg, dp, vc, cum, cumt, o = saved
    return call(
        mixer_backward_body,
        layer,
        layouts,
        dict(
            branch_low=plain(branch_low),
            wo=own(upo, AT_OUT),
            qkvg=plain(qkvg),
            vc=plain(vc),
            cum=plain(cum),
            cumt=plain(cumt),
            o=plain(o),
            small=own(small),
            dp=plain(dp),
            ordered=plain(ordered),
            gwo=plain(gwo),
        ),
        dict(
            low=((ROWS, QKVG + LANES), bf16, True),
            gw_keep=((D, GROUP), f32, True),
            gw_send=((D, GROUP), bf16, False),
            sums=((8, D), f32, True),
        ),
        dict(
            mixed_s=((ROWS, D), f32),
            dv_s=((ROWS + 8, D), f32),
            rows_s=((ROWS, LANES), f32),
            cols_s=((LANES, ROWS), f32),
            bias=((HALF, ROWS), f32),
            gw=((D, 2 * GROUP), f32),
        ),
        7 * 10**9,
        after=after,
    )


def input_backward(
    layer, layouts, x, mods, low, mid_grad, ffn_sums, mixer_sums, qk, vgd, two=None, after=()
):
    extra_in, extra_out = {}, {}
    if two is not None:
        extra_in = dict(gx_two=plain(two[0]), mod_two=plain(two[1]))
        extra_out = dict(
            gx_send=((ROWS, D), f32, False),
            mod_mine=((8, 6 * D), bf16, False),
            mod_send=((8, 6 * D), bf16, False),
        )
    return call(
        input_backward_body,
        layer,
        layouts,
        dict(
            low=plain(low),
            w_qk=own(qk),
            w_vgd=own(vgd),
            x=micro(x),
            mid_grad=plain(mid_grad),
            mods=own(mods),
            ffn_sums=plain(ffn_sums),
            mixer_sums=plain(mixer_sums),
            **extra_in,
        ),
        dict(
            gx=((ROWS, D), f32, True),
            gx_low=((ROWS, D), bf16, True),
            mod_low=((8, 6 * D), bf16, True),
            sums=((8, 2 * D), f32, False),
            **extra_out,
        ),
        dict(
            mixed_s=((ROWS, D), f32),
            perm_s=((ROWS, 3 * D), bf16),
            gmod=((8, 2 * D), f32),
        ),
        2 * 10**9,
        after=after,
    )


def small_kernel(b_up, b_down, taps, b_decay, packed):
    packed[...] = jnp.zeros(packed.shape, f32)
    packed[0:1, :] = b_up[...]
    packed[1:2, :D] = b_down[...]
    packed[2:5, :D] = taps[0]
    packed[5:6, :HEADS] = b_decay[...]


def pack_small(b_up, b_down, taps, b_decay):
    return pl.pallas_call(
        small_kernel,
        out_shape=jax.ShapeDtypeStruct((8, FF), f32),
        in_specs=[VMEM] * 4,
        out_specs=VMEM,
        compiler_params=pltpu.CompilerParams(vmem_limit_bytes=8 * 1024 * 1024),
    )(b_up, b_down, taps, b_decay)


def pack_kernel(
    w_query, w_key, w_value, w_gate, w_out, w_decay, w_up, w_down, w_ada, conditions,
    qkuo, vgd, down, ada, lifted,
):
    qkuo[:, :D] = w_query[0]
    qkuo[:, D : 2 * D] = w_key[0]
    vgd[:, :D] = w_value[0]
    vgd[:, D : 2 * D] = w_gate[0]
    place = jnp.where(row_iota(HEADS, LANES) == lane_iota(HEADS, LANES), 1.0, 0.0).astype(bf16)
    turned = lax.dot_general(
        w_decay[0], place, (((0,), (0,)), ((), ())), preferred_element_type=f32
    )
    vgd[:, 2 * D :] = turned.astype(bf16)
    qkuo[:, 2 * D : 2 * D + FF] = w_up[0]
    qkuo[:, 2 * D + FF :] = w_out[0]
    down[...] = w_down[0]
    ada[...] = w_ada[0]
    values = jnp.concatenate([conditions[m].astype(f32) for m in range(MICRO)], axis=0)
    lifted[0] = (values * sigmoid(values)).astype(bf16)


def pack(*weights):
    shard = weights[0].shape[1]
    shapes = [(shard, width) for width in (3 * D + FF, 2 * D + LANES)]
    shapes += [weights[7].shape[1:], weights[8].shape[1:], (1, MICRO * SLOTS, D)]
    return pl.pallas_call(
        pack_kernel,
        out_shape=[jax.ShapeDtypeStruct(shape, bf16) for shape in shapes],
        in_specs=[VMEM] * len(weights),
        out_specs=[VMEM] * len(shapes),
    )(*weights)


def join_kernel(bits, waits, *refs):
    count = len(bits)
    held, came, out = refs[:count], refs[count : 2 * count], refs[2 * count + waits :]
    for i, bit in enumerate(bits):
        mine = (lax.axis_index("row") >> bit) & 1
        out[i][:, mine] = held[i][...]
        out[i][:, 1 - mine] = came[i][...]


def join(held, came, bits, after=()):
    def parts(array, bit):
        axis = axis_of(bit)
        above = 1
        for size in array.shape[:axis]:
            above *= size
        return array.reshape((above, -1) + array.shape[-2:])

    split_held = [parts(array, bit) for array, bit in zip(held, bits)]
    split_came = [parts(array, bit) for array, bit in zip(came, bits)]
    out = pl.pallas_call(
        functools.partial(join_kernel, bits, len(after)),
        out_shape=[
            jax.ShapeDtypeStruct(array.shape[:1] + (2,) + array.shape[1:], array.dtype)
            for array in split_held
        ],
        in_specs=[VMEM] * (2 * len(held)) + [ANY] * len(after),
        out_specs=[VMEM] * len(held),
        compiler_params=pltpu.CompilerParams(vmem_limit_bytes=8 * 1024 * 1024),
        cost_estimate=pl.CostEstimate(flops=10**6, bytes_accessed=10**6, transcendentals=0),
    )(*split_held, *split_came, *after)
    joined = []
    for array, result, bit in zip(held, out, bits):
        shape = list(array.shape)
        shape[axis_of(bit)] = 2
        joined.append(result.reshape(shape))
    return joined


def lifted_kernel(mine, came, ada, out, kept, sem):
    copy = pltpu.make_async_copy(ada, kept, sem)
    copy.start()
    first = lax.axis_index("section") == 0
    pair = mine[0:SLOTS, :].astype(f32), came[0:SLOTS, :].astype(f32)
    grad = jnp.concatenate(
        [jnp.where(first, pair[0], pair[1]), jnp.where(first, pair[1], pair[0])], axis=0
    ).astype(bf16)
    copy.wait()
    out[...] = mm_t(grad, kept[...])


def lifted_grads(mine, came, ada):
    return pl.pallas_call(
        lifted_kernel,
        out_shape=jax.ShapeDtypeStruct((MICRO * SLOTS, D), f32),
        in_specs=[VMEM, VMEM, ANY],
        out_specs=VMEM,
        scratch_shapes=[pltpu.VMEM((D, 6 * D), bf16), pltpu.SemaphoreType.DMA],
        compiler_params=pltpu.CompilerParams(vmem_limit_bytes=16 * 1024 * 1024),
        cost_estimate=pl.CostEstimate(flops=10**9, bytes_accessed=2 << 20, transcendentals=0),
    )(mine, came, ada)


def term_kernel(*refs):
    *terms, stays, goes = refs
    stays[...] = sum(ref[:, 0] for ref in terms)
    goes[...] = sum(ref[:, 1] for ref in terms)


def term_step(below, *terms):
    tail = terms[0].shape[1:]
    above = terms[0].shape[0] // (2 * below)
    shape = jax.ShapeDtypeStruct((above, below) + tail, f32)
    out = pl.pallas_call(
        term_kernel,
        out_shape=[shape] * 2,
        in_specs=[VMEM] * len(terms),
        out_specs=[VMEM] * 2,
        compiler_params=pltpu.CompilerParams(vmem_limit_bytes=8 * 1024 * 1024),
        cost_estimate=pl.CostEstimate(flops=10**6, bytes_accessed=10**6, transcendentals=0),
    )(*[term.reshape((above, 2, below) + tail) for term in terms])
    return [array.reshape((above * below,) + tail) for array in out]


def step_kernel(bit, widths, counts, waits, *refs):
    mine = (lax.axis_index("row") >> bit) & 1
    count, many = len(widths), len(counts)
    refs = list(refs)
    take = lambda number: [refs.pop(0) for _ in range(number)]
    sources = take(count + many)
    take(waits)
    targets = take(count + 1)
    buffers = take(count + many)
    results = take(count + 1)
    in_sems, out_sems = refs
    arrive = [
        pltpu.make_async_copy(source, buffer, in_sems.at[i])
        for i, (source, buffer) in enumerate(zip(sources, buffers))
    ]
    leave = [
        pltpu.make_async_copy(result, target, out_sems.at[i])
        for i, (result, target) in enumerate(zip(results, targets))
    ]
    for copy in arrive:
        copy.start()
    kept, came = buffers[:count], buffers[count:]
    places = [(j, i) for j, number in enumerate(counts) for i in range(number)]
    goes = results[count]
    at = 0
    for i in range(count):
        j, place = places[i]
        arrive[i].wait()
        if place == 0:
            arrive[count + j].wait()
        start = sum(widths[i - place : i])
        columns = slice(start, start + widths[i])
        total = kept[i][:, 1 - mine] + came[j][:, 1 - mine, :, :, columns].astype(f32)
        goes[:, :, :, at : at + widths[i]] = total.astype(bf16)
        at += widths[i]
    leave[count].start()
    for i in range(count):
        j, place = places[i]
        start = sum(widths[i - place : i])
        columns = slice(start, start + widths[i])
        results[i][...] = kept[i][:, mine] + came[j][:, mine, :, :, columns].astype(f32)
        leave[i].start()
    for copy in leave:
        copy.wait()


def step(kept, came, bit, below=1, after=()):
    blocks, rows = kept[0].shape[0] // 2, kept[0].shape[1]
    above = blocks // below
    paired = lambda array: array.reshape((above, 2, below) + array.shape[1:])
    widths = [array.shape[2] for array in kept]
    size = sum(array.size for array in kept)
    arrays = [paired(array) for array in kept] + [paired(array) for array, _ in came]
    shapes = [((above, below, rows, width), f32) for width in widths]
    shapes.append(((above, below, rows, sum(widths)), bf16))
    out = pl.pallas_call(
        functools.partial(step_kernel, bit, widths, [count for _, count in came], len(after)),
        out_shape=[jax.ShapeDtypeStruct(shape, kind) for shape, kind in shapes],
        in_specs=[HBM] * len(kept) + [ANY] * (len(came) + len(after)),
        out_specs=[HBM] * len(kept) + [ANY],
        scratch_shapes=[pltpu.VMEM(array.shape, array.dtype) for array in arrays]
        + [pltpu.VMEM(shape, kind) for shape, kind in shapes]
        + [pltpu.SemaphoreType.DMA((len(arrays),)), pltpu.SemaphoreType.DMA((len(shapes),))],
        compiler_params=pltpu.CompilerParams(vmem_limit_bytes=10 * 1024 * 1024),
        cost_estimate=pl.CostEstimate(flops=size, bytes_accessed=8 * size, transcendentals=0),
    )(*arrays, *after)
    count = len(kept)
    flat_blocks = [array.reshape((blocks,) + array.shape[2:]) for array in out]
    return flat_blocks[:count], flat_blocks[count]


def misc_step_kernel(held, arrived, out):
    size = held.shape[0] - SUMS
    out[:size, :] = held[:size, :]
    out[size : 2 * size, :] = arrived[:size, :]
    high, low = split(misc_sums(held, arrived))
    out[2 * size : 2 * size + SUMS // 2, :] = high
    out[2 * size + SUMS // 2 :, :] = low


def misc_step(held, arrived):
    return pl.pallas_call(
        misc_step_kernel,
        out_shape=jax.ShapeDtypeStruct((2 * held.shape[0] - SUMS, 2 * D), bf16),
        in_specs=[VMEM] * 2,
        out_specs=VMEM,
        compiler_params=pltpu.CompilerParams(vmem_limit_bytes=8 * 1024 * 1024),
        cost_estimate=pl.CostEstimate(flops=10**5, bytes_accessed=10**5, transcendentals=0),
    )(held, arrived)


def misc_sums(*refs):
    size = refs[0].shape[0] - SUMS
    parts = [ref[size:, :].astype(f32) for ref in refs]
    return sum(part[: SUMS // 2] + part[SUMS // 2 :] for part in parts)


SUMS = 32
OWN = 16


def misc_kernel(conditions, mod_one, mod_two, sums_one, sums_two, out):
    values = conditions[...].astype(f32)
    values = jnp.where(lax.axis_index("section") == 0, values[:SLOTS], values[SLOTS:])
    lifted = values * sigmoid(values)
    spare = [jnp.concatenate([lifted[0:1], lifted[1:2]], axis=1), jnp.zeros((1, 2 * D), f32)]
    rows = []
    for mod in (mod_one, mod_two):
        for slot in range(SLOTS):
            for i in range(3):
                part = mod[slot : slot + 1, i * 2 * D : (i + 1) * 2 * D]
                rows.append(part.astype(f32))
        rows.extend(spare)
    sums = jnp.concatenate([sums_one[...], sums_two[...]], axis=0)
    rows.extend(part.astype(f32) for part in split(sums))
    out[...] = jnp.concatenate(rows, axis=0).astype(bf16)


def pack_misc(conditions, mod_one, mod_two, sums_one, sums_two):
    return pl.pallas_call(
        misc_kernel,
        out_shape=jax.ShapeDtypeStruct((OWN + SUMS, 2 * D), bf16),
        in_specs=[VMEM] * 5,
        out_specs=VMEM,
        compiler_params=pltpu.CompilerParams(vmem_limit_bytes=8 * 1024 * 1024),
    )(conditions, mod_one, mod_two, sums_one, sums_two)


def finish_kernel(widths, counts, waits, *refs):
    count = len(widths)
    kept, refs = refs[:count], refs[count:]
    came, refs = refs[: len(counts)], refs[len(counts) :]
    parts = refs[:4]
    mine, other, small_mine, small_other = refs[4 + waits :]
    places = [(ref, i) for ref, many in zip(came, counts) for i in range(many)]
    added = []
    for i in range(count):
        ref, place = places[i]
        start = sum(widths[i - place : i])
        added.append(kept[i][0] + ref[0, :, start : start + widths[i]].astype(f32))
    a1, f1, f2, a2 = added
    size = parts[0].shape[0] - SUMS
    rows = jnp.concatenate([part[:size, :] for part in parts], axis=0)
    rows = rows.astype(f32).reshape(-1, OWN, 2 * D)
    shard = mine.shape[0]
    chosen = lane_iota(shard, D) == row_iota(shard, D) + lax.axis_index("row") * shard
    chosen = jnp.where(chosen, 1.0, 0.0).astype(bf16)
    features = [rows[:, 6, slot * D : (slot + 1) * D].astype(bf16) for slot in range(SLOTS)]
    lifted = jnp.concatenate([mm_t(chosen, part) for part in features], axis=1).astype(bf16)

    def ada(first):
        columns = []
        for i in range(3):
            both = [rows[:, first + 3 * slot + i, :] for slot in range(SLOTS)]
            columns.append(mm(lifted, jnp.concatenate(both, axis=0).astype(bf16)))
        return jnp.concatenate(columns, axis=1)

    first = lax.axis_index("section") == 0
    at = 0
    for one, two in ((a1, a2), (f1, f2), (ada(0), ada(OWN // 2))):
        columns = slice(at, at + one.shape[1])
        mine[:, columns] = jnp.where(first, one, two)
        other[:, columns] = jnp.where(first, two, one)
        at += one.shape[1]
    total = misc_sums(*parts)
    one, two = total[0:8, :], total[8:16, :]
    small_mine[...] = jnp.where(first, one, two)
    small_other[...] = jnp.where(first, two, one)


def finish(kept, came, parts, after):
    widths = [array.shape[2] for array in kept]
    shard = kept[0].shape[1]
    wide = GROUP + FF + 6 * D
    arrays = [array for array, _ in came]
    shapes = [(shard, wide)] * 2 + [(8, 2 * D)] * 2
    return pl.pallas_call(
        functools.partial(finish_kernel, widths, [count for _, count in came], len(after)),
        out_shape=[jax.ShapeDtypeStruct(shape, f32) for shape in shapes],
        in_specs=[VMEM] * (len(kept) + len(came) + 4) + [ANY] * len(after),
        out_specs=[VMEM] * 4,
        compiler_params=pltpu.CompilerParams(vmem_limit_bytes=8 * 1024 * 1024),
    )(*kept, *arrays, *parts, *after)


def output_kernel(mine, other, small_mine, small_other, *outs):
    first = lax.axis_index("section") == 0

    def halves(start, width):
        columns = slice(start, start + width)
        pair = mine[:, columns], other[:, columns]
        return jnp.where(first, pair[0], pair[1]), jnp.where(first, pair[1], pair[0])

    attn = halves(0, GROUP)
    cut = GROUP - 2 * D
    outs[0][...] = attn[0][:, :D]
    outs[1][...] = attn[0][:, D : 2 * D]
    outs[2][:, :cut] = attn[0][:, 2 * D :]
    outs[2][:, cut:] = attn[1][:, : D - cut]
    outs[3][...] = attn[1][:, D - cut : 2 * D - cut]
    outs[4][...] = attn[1][:, 2 * D - cut : 3 * D - cut]
    decay = jnp.transpose(attn[1][:, 3 * D - cut :])
    for head in range(HEADS):
        outs[5][head] = decay[head : head + 1, :]
    up = halves(GROUP, FF // 2)
    outs[6][:, : FF // 2] = up[0]
    outs[6][:, FF // 2 :] = up[1]
    for piece in range(2):
        down = halves(GROUP + FF // 2 + piece * D, D)
        outs[7][piece] = down[0]
        outs[7][2 + piece] = down[1]
    outs[8][...] = mine[:, GROUP + FF :] + other[:, GROUP + FF :]
    small = small_mine[...] + small_other[...]
    half = 2 * D
    for i in range(3):
        outs[9][:, i * half : (i + 1) * half] = small[i : i + 1, :]
    for i in range(2):
        outs[10][:, i * half : (i + 1) * half] = small[3 + i : 4 + i, :]
    outs[11][...] = small[5:6, :D]
    outs[12][0] = small[5:6, D:]
    outs[12][1] = small[6:7, :D]
    outs[12][2] = small[6:7, D:]
    outs[13][...] = small[7:8, :HEADS]


def outputs(mine, other, small_mine, small_other):
    shard = mine.shape[0]
    shapes = (
        [(shard, D)] * 5
        + [(HEADS, 1, shard), (shard, FF), (4, shard, D), (shard, 6 * D)]
        + [(1, 6 * D), (1, FF), (1, D), (3, 1, D), (1, HEADS)]
    )
    return pl.pallas_call(
        output_kernel,
        out_shape=[jax.ShapeDtypeStruct(shape, f32) for shape in shapes],
        in_specs=[VMEM] * 4,
        out_specs=[VMEM] * len(shapes),
        compiler_params=pltpu.CompilerParams(vmem_limit_bytes=8 * 1024 * 1024),
    )(mine, other, small_mine, small_other)


def both_kernel(one, two, came, out, mark, kept, sems):
    section = lax.axis_index("section")
    mark[...] = jnp.zeros(mark.shape, f32)

    def move(mine, layer):
        arrive = [
            pltpu.make_async_copy(mine, kept.at[layer], sems.at[0]),
            pltpu.make_async_copy(came, kept.at[1 - layer], sems.at[1]),
        ]
        leave = [
            pltpu.make_async_copy(kept.at[layer], out.at[layer], sems.at[2]),
            pltpu.make_async_copy(kept.at[1 - layer], out.at[1 - layer], sems.at[3]),
        ]
        for copy in arrive:
            copy.start()
        for copy, after in zip(arrive, leave):
            copy.wait()
            after.start()
        for copy in leave:
            copy.wait()

    @pl.when(section == 0)
    def _():
        move(one, 0)

    @pl.when(section == 1)
    def _():
        move(two, 1)


def both_micros(one, two, came):
    return pl.pallas_call(
        both_kernel,
        out_shape=[
            jax.ShapeDtypeStruct((MICRO,) + one.shape, one.dtype),
            jax.ShapeDtypeStruct((8, LANES), f32),
        ],
        in_specs=[ANY] * 3,
        out_specs=[ANY, VMEM],
        scratch_shapes=[
            pltpu.VMEM((MICRO,) + one.shape, one.dtype),
            pltpu.SemaphoreType.DMA((4,)),
        ],
        compiler_params=pltpu.CompilerParams(vmem_limit_bytes=8 * 1024 * 1024),
    )(one, two, came)


def swap(values):
    return lax.ppermute(values, "section", [(0, 1), (1, 0)])


def row_bits():
    bits = lax.axis_size("row").bit_length() - 1
    third = bits // 3
    return (
        tuple(range(third)),
        tuple(range(third, 2 * third)),
        tuple(range(2 * third, bits)),
    )


def across(values, flips):
    size = lax.axis_size("row")
    return lax.ppermute(values, "row", [(i, i ^ flips) for i in range(size)])


def partner(values, bit):
    return across(values, 1 << bit)


def axis_of(bit):
    return lax.axis_size("row").bit_length() - 2 - bit


def bit_of(bit):
    return (lax.axis_index("row") >> bit) & 1


def single(values):
    return values.reshape((1,) * (lax.axis_size("row").bit_length() - 1) + values.shape)


def gather_steps(along_x, along_y, along_z):
    steps = [(bit, bit) for bit in reversed(along_z)]
    return steps + list(zip(along_x + along_y, along_y + along_x))


def flat(held):
    return held.reshape(-1, held.shape[-1])


def lock(*arrays):
    return lax.optimization_barrier(arrays)


def on_device(
    tokens, conditions, output_grad, layouts,
    w_ada, b_ada, w_query, w_key, w_value, w_gate, w_out, w_decay, b_decay, conv_kernel,
    w_up, b_up, w_down, b_down,
):
    section = lax.axis_index("section")
    devices = lax.axis_size("row")
    shard = w_query.shape[1]
    along_x, along_y, along_z = row_bits()

    def both(values):
        return values, swap(values)

    qkuo, vgd, down, ada, lifted = pack(
        w_query, w_key, w_value, w_gate, w_out, w_decay.transpose(0, 2, 1), w_up, w_down, w_ada,
        conditions,
    )
    small = pack_small(b_up, b_down, conv_kernel, b_decay)
    conds = conditions.reshape(MICRO * SLOTS, D)
    steps = gather_steps(along_x, along_y, along_z)
    lag = len(along_z)
    plane = along_x + along_y
    bounds = [len(plane) * i // lag for i in range(lag + 1)]
    held = [single(array) for array in (qkuo, vgd, down)]
    ada = single(ada)
    for place, pair in enumerate(steps):
        bits = pair + pair[1:]
        if place == len(steps) - 1:
            bits = pair + pair
            held = [held[0][..., : 2 * D], held[1], held[0][..., 2 * D :], held[2]]
        came = [partner(array, bit) for array, bit in zip(held, bits)]
        after = ()
        if place < lag:
            lifted = jnp.concatenate([lifted, partner(lifted, pair[0])], axis=0)
            for bit in plane[bounds[place] : bounds[place + 1]]:
                (ada,) = join([ada], [partner(ada, bit)], (bit,))
            after = (small, lifted, ada)
        if place == lag:
            left = list(reversed(along_z))
            rows = D >> lag
            line = (lax.axis_index("row") >> len(plane)) * rows
            lifted = lax.dynamic_slice_in_dim(lifted, line, rows, 2)
            product = mm(lifted.reshape(-1, rows), flat(ada))
            terms = (product.reshape(1 << lag, MICRO * SLOTS, 6 * D),)
            for bit in along_z:
                stays, goes = term_step(1 << left.index(bit), *terms)
                left.remove(bit)
                terms = (stays, partner(goes, bit))
            after = (terms[1],)
        if place < len(steps) - 1:
            held = join(held, came, bits, after)
        else:
            qk, vgd = [both(flat(array)) for array in join(held[:2], came[:2], bits[:2])]
            mods = both(sum(term[0] for term in terms) + b_ada[0])
            smalls = both(small)
            x = tokens
            *saved, gated = attn_forward(0, layouts, x, mods, smalls, qk, vgd)
            held = join(held[2:], came[2:], bits[2:], (gated,))
    upo, down = [both(flat(array)) for array in held]
    out_one, branch, down_raw = ffn_forward(0, layouts, x, mods, smalls, gated, upo, down)
    kept = [(x, saved, gated, branch, down_raw)]
    x = out_one[None]
    kept.append((x,))

    late, _ = lock(w_ada[0], out_one)
    ada_all = lax.all_gather(late, "row", axis=0, tiled=True)

    def halved(terms):
        if terms[0].ndim == 2:
            up_sum = terms[0].reshape(devices, shard, 2, FF // 2)
            down_sum = terms[1].reshape(devices, 2, 2, shard, D)
            terms = []
            for own in (section, 1 - section):
                up_half = lax.dynamic_index_in_dim(up_sum, own, 2, keepdims=False)
                down_half = lax.dynamic_index_in_dim(down_sum, own, 1, keepdims=False)
                terms.append(
                    jnp.concatenate([up_half, down_half[:, 0], down_half[:, 1]], axis=2)
                )
            terms[1] = terms[1].astype(bf16)
        return terms

    def by_row(array):
        return array.reshape(devices, shard, GROUP)

    def input_step(l, low, mid_grad, ffn_sums, mixer_sums, two=None, after=()):
        x = kept[l][0]
        return input_backward(
            l, layouts, x, mods, low, mid_grad, ffn_sums, mixer_sums, qk, vgd, two, after
        )

    def run(keep, came, bits, below=1, after=()):
        for bit in bits[:-1]:
            keep, sent = step(keep, came, bit, below, after)
            came = [(partner(sent, bit), len(keep))]
        return step(keep, came, bits[-1], below, after)

    def grown(mod, bits):
        for bit in bits:
            mod = misc_step(mod, partner(mod, bit))
        return mod

    x_bits, y_bits, z_bits = along_x, along_y, along_z
    (
        out_two, acts_sent, mid_grad, f2_sums, low, a2_keep, a2_sent, m2_sums, *terms
    ) = second_layer(
        layouts, x, mods, smalls, output_grad, qk, vgd, upo, down, devices
    )
    f2_keep, f2_sent = halved(terms)
    a2_keep, a2_sent = by_row(a2_keep), by_row(a2_sent)
    low, f2_sent, a2_sent, acts_sent = lock(low, f2_sent, a2_sent, acts_sent)
    f2_came = swap(f2_sent)
    a2_came = swap(a2_sent)
    acts_came = swap(acts_sent)
    gx_two, grad, mod_low_two, sums_two = input_step(1, low, mid_grad, f2_sums, m2_sums)
    grad, f2_came, a2_came, acts_came = lock(grad, f2_came, a2_came, acts_came)
    f2_keep, f2_sent = run([f2_keep], [(f2_came, 1)], x_bits)
    a2_keep, a2_sent = run([a2_keep], [(a2_came, 1)], y_bits, 1 << len(x_bits))
    grad, f2_sent, a2_sent = lock(grad, f2_sent, a2_sent)
    f2_came = partner(f2_sent, x_bits[-1])
    a2_came = partner(a2_sent, y_bits[-1])

    x, saved, gated, branch, down_raw = kept[0]
    mid_grad, branch_low, gwo, f1_sums, *terms = ffn_backward(
        0, layouts, x, mods, smalls, gated, branch, down_raw, grad[None], upo, down, devices
    )
    f1_keep, f1_sent = halved(terms)
    carried = (branch_low, gwo)
    *carried, f1_sent, f2_came, a2_came = lock(*carried, f1_sent, f2_came, a2_came)
    f1_came = swap(f1_sent)
    f2_keep, f2_sent = run(f2_keep, [(f2_came, 1)], y_bits)
    a2_keep, a2_sent = run(a2_keep, [(a2_came, 1)], x_bits)
    f1_keep, f1_sent = run([f1_keep], [(f1_came, 1)], x_bits)
    *carried, f2_sent, a2_sent, f1_sent = lock(*carried, f2_sent, a2_sent, f1_sent)
    f1_came = partner(f1_sent, x_bits[-1])
    a2_came = partner(a2_sent, x_bits[-1])
    f2_came = partner(f2_sent, y_bits[-1])
    low, a1_keep, a1_sent, m1_sums = mixer_backward(0, layouts, smalls, saved, *carried, upo)
    a1_keep, a1_sent = by_row(a1_keep), by_row(a1_sent)
    low, a1_sent, f2_came, a2_came, f1_came = lock(low, a1_sent, f2_came, a2_came, f1_came)
    a1_came = swap(a1_sent)
    two_keep, two_sent = run(f2_keep + a2_keep, [(f2_came, 1), (a2_came, 1)], z_bits[:1])
    f1_keep, f1_sent = run(f1_keep, [(f1_came, 1)], y_bits)
    a1_keep, a1_sent = run([a1_keep], [(a1_came, 1)], x_bits)
    low, two_sent, f1_sent, a1_sent = lock(low, two_sent, f1_sent, a1_sent)
    a1_came = partner(a1_sent, x_bits[-1])
    f1_came = partner(f1_sent, y_bits[-1])
    two_came = partner(two_sent, z_bits[0])
    gx_one, _, mod_low_one, sums_one, gx_sent, mod_mine, mod_sent = input_step(
        0, low, mid_grad, f1_sums, m1_sums, (gx_two, mod_low_two)
    )
    misc = pack_misc(conds, mod_low_one, mod_low_two, sums_one, sums_two)
    misc, a1_came, two_came, f1_came, gx_sent, mod_sent, ada_all = lock(
        misc, a1_came, two_came, f1_came, gx_sent, mod_sent, ada_all
    )

    a1_keep, a1_sent = run(a1_keep, [(a1_came, 1)], y_bits)
    a1_sent, misc = lock(a1_sent, misc)
    a1_came = partner(a1_sent, y_bits[-1])
    misc = grown(misc, tuple(reversed(z_bits))[:-1])
    gx_came = swap(gx_sent)
    mod_came = swap(mod_sent)
    keep, came = a1_keep + f1_keep, [(a1_came, 1), (f1_came, 1)]
    for place, bit in enumerate(z_bits):
        if place == 1:
            keep, came = keep + two_keep, came + [(two_came, 2)]
        keep, sent = step(keep, came, bit)
        if place == len(z_bits) - 1:
            sent, misc, gx_came, mod_came = lock(sent, misc, gx_came, mod_came)
        elif place == 0:
            sent, misc = lock(sent, misc)
        came = [(partner(sent, bit), len(keep))]
        if place == 0:
            misc = grown(misc, z_bits[:1] + x_bits[:-1] + y_bits[:-1])
    last = (1 << x_bits[-1], 1 << y_bits[-1])
    parts = [misc] + [across(misc, flips) for flips in (last[0], last[1], last[0] + last[1])]
    gx_out, gx_mark = both_micros(gx_one, gx_two, gx_came)
    acts_out, acts_mark = both_micros(out_one, out_two, acts_came)
    grad_lifted = lifted_grads(mod_mine, mod_came, ada_all)
    lifted_came = swap(grad_lifted)
    mine, other, small_mine, small_other = finish(
        keep, came, parts, (gx_mark, acts_mark, lifted_came)
    )
    came, small_came = swap(other), swap(small_other)
    (
        g_query, g_key, g_value, g_gate, g_out, g_decay, g_up, g_down, g_ada,
        g_b_ada, g_b_up, g_b_down, g_conv, g_b_decay,
    ) = outputs(mine, came, small_mine, small_came)

    grad_lifted = (grad_lifted + lifted_came).reshape(MICRO, SLOTS, D)
    _, pull_silu = jax.vjp(jax.nn.silu, conditions.astype(f32))
    (cond_grads,) = pull_silu(grad_lifted)

    return (
        acts_out[None],
        gx_out[None],
        cond_grads,
        g_ada[None],
        g_b_ada,
        g_query[None],
        g_key[None],
        g_value[None],
        g_gate[None],
        g_out[None],
        g_decay.transpose(1, 2, 0),
        g_b_decay,
        g_conv.transpose(1, 0, 2),
        g_up[None],
        g_b_up,
        g_down.reshape(1, FF // devices, D),
        g_b_down,
    )


def solution(mesh):
    rows = P(None, "row", None)
    mats = P("section", "row", None)
    vector = P("section", None)
    in_specs = (
        rows, rows, rows, P(None, "row"),
        mats, vector, mats, mats, mats, mats, mats, mats, vector, P("section", None, None),
        mats, vector, mats, vector,
    )
    blocks = P("section", None, "row", None)
    out_specs = (
        blocks, blocks, rows,
        mats, vector, mats, mats, mats, mats, mats, mats, vector, P("section", None, None),
        mats, vector, mats, vector,
    )
    return jax.shard_map(
        on_device, mesh=mesh, in_specs=in_specs, out_specs=out_specs, check_vma=False
    )
```
